32 devices in a mesh: grp: 8 (over y, x, core), blk: 4 (over z).
Axes of the slice: x: 2, y: 2, z: 4, core: 2. Of those that a mesh axis runs over, the one named last changes fastest.
Arguments:
- patches: bfloat16 [4, 3072, 1152], P('blk', 'grp'), may hold values from -6 to 6
- segment_ids: int32 [4, 3072], P('blk'), may hold values from 0 to 3, never falling along the last dimension, each value on 1 to 1024 neighbouring positions
- qkv_weight: bfloat16 [1152, 1728], replicated
- out_weight: bfloat16 [576, 1152], replicated, may hold values from -0.25 to 0.25
- text_embed: bfloat16 [16, 1152], P('blk'), may hold values from -6 to 6
Outputs:
- mixed: bfloat16 [4, 3072, 1152], P('blk', 'grp')
- row_loss: float32 [16], P('blk')
The draws below stay inside these ranges and needn't reach their ends.
Inputs may be any that keep to these rules, and one draw needn't show every extreme that they name: `segment_ids`: within each group ids never fall, every image has 1 to 1024 rows, and some image has exactly 1024.
All inputs are finite; a program needn't handle non-finite values.
Results may differ from the reference program's by a relative error of at most 0.0025.
The reference program's roundings to bfloat16 on the way count: a program that leaves them out, or rounds other values in their place, can miss the bound.
Values may be sent and summed in bfloat16 or wider, within the bound.
No kernel may reach another device: no remote copies, remote signals or barrier semaphores. Data moves between devices by JAX's collectives and lax.ppermute only.
A program may use at most 64 MiB of HBM per device.

```python
import math
import jax
import jax.numpy as jnp
import numpy as np
from jax import lax

D = 1152
HS = 72
HEADS = 8
MAXP = 1024
IMG_GRP = 4
HD = 576
PACK = 3072
GROUPS = 4
IMAGES = 16


def draw_qkv_weight(key, part):
    key = jax.random.fold_in(key, 11)
    matrix = jax.random.normal(key, (D, 3 * HEADS * HS), jnp.float32) * D ** (-0.5)
    return matrix.astype(jnp.bfloat16)


def steps_of(key, extent, pieces, least, largest):
    loudness = 1.0
    for axis_at, shards_of in pieces:
        draws = jax.random.uniform(jax.random.fold_in(jax.random.fold_in(key, 6), axis_at), (shards_of,), jnp.float32, least / len(pieces), largest / len(pieces))
        loudness = loudness * jnp.repeat(jnp.exp(draws), extent[axis_at] // shards_of).reshape((-1,) + (1,) * (len(extent) - 1 - axis_at))
    return loudness


def length_profile(amount, total, bound, lean):
    loads = [(1 << 20) // math.isqrt(rank ** lean) + 1 for rank in range(2, amount + 1)]
    spare, counts = total - bound - (amount - 1), [1] * (amount - 1)
    while spare > 0:
        movable = [i for i in range(amount - 1) if counts[i] < bound]
        whole, left = sum([loads[i] for i in movable]), spare
        for i in movable:
            addition = min(bound - counts[i], max(1, left * loads[i] // whole), spare)
            counts[i] = counts[i] + addition
            spare = spare - addition
    return np.array([bound] + counts)


def uneven(rng, count, total, bound, skew):
    if count == 2:
        one = jax.random.randint(rng, (), max(1, total - bound), min(bound, total - 1) + 1)
        return jnp.stack([one, total - one])
    tallies = jnp.asarray(length_profile(count, total, bound, skew), jnp.int32)
    pairs = (count - 1) // 2
    donor, receiver = tallies[1:1 + 2 * pairs:2], tallies[2:2 + 2 * pairs:2]
    margin = jnp.minimum(donor - 1, bound - receiver)
    passed = jax.random.randint(jax.random.fold_in(rng, 1), (pairs,), 0, 1 << 20) % (margin + 1)
    tallies = tallies.at[1:1 + 2 * pairs:2].set(donor - passed).at[2:2 + 2 * pairs:2].set(receiver + passed)
    return tallies[jax.random.permutation(jax.random.fold_in(rng, 2), count)]


def bell_draw(rng, extent, scale, bound, pieces=(), kind=jnp.bfloat16):
    array = jax.random.normal(rng, extent, jnp.float32) * scale
    if len(pieces) > 0:
        array = steps_of(rng, extent, pieces, -0.22, 0.18) * array
    return jnp.clip(array, min=-bound, max=bound).astype(kind)


def setup_inputs(seed: int = 0) -> dict:
    seeds = jax.random.split(jax.random.key(seed), 6)
    patches = bell_draw(seeds[0], (GROUPS, PACK, D), 1.0, 6.0, ((0, 4), (1, 8)))
    segment_ids = jax.vmap(lambda own: jnp.searchsorted(jnp.cumsum(uneven(own, IMG_GRP, PACK, MAXP, 2)), jnp.arange(PACK), side="right"))(jax.random.split(seeds[1], GROUPS)).reshape((GROUPS, PACK)).astype(jnp.int32)
    qkv_weight = draw_qkv_weight(jax.random.fold_in(seeds[5], 71), 0)
    out_weight = bell_draw(seeds[3], (HD, D), HD ** -0.5, 0.25)
    text_embed = bell_draw(seeds[4], (IMAGES, D), 1.0, 6.0, ((0, 4),))
    return dict(patches=patches, segment_ids=segment_ids, qkv_weight=qkv_weight, out_weight=out_weight, text_embed=text_embed)


logit_scale = 30.0
logit_bias = -5.0

def normalize_rows(rows):
    values = rows.astype(jnp.float32)
    center = values - lax.optimization_barrier(jnp.mean(values, axis=1, keepdims=True))
    spread = lax.optimization_barrier(jnp.mean(center * center, axis=1, keepdims=True))
    return (center * lax.rsqrt(spread + 1e-06)).astype(jnp.bfloat16)

def unit_rows(matrix):
    return matrix * lax.rsqrt(lax.optimization_barrier(jnp.sum(matrix * matrix, axis=1, keepdims=True)) + 1e-06)

def head_terms(query_head, key_head, value_head, query_ids, key_ids):
    scores = lax.dot_general(query_head, key_head, (((1,), (1,)), ((), ())), preferred_element_type=jnp.float32)
    scores = scores * query_head.shape[1] ** (-0.5)
    same = query_ids[:, None] == key_ids[None, :]
    scores = jnp.where(same, scores, -1e+30)
    highest = lax.optimization_barrier(jnp.max(scores, axis=1))
    probs = jnp.where(same, jnp.exp(scores - highest[:, None]), 0.0)
    summed = lax.optimization_barrier(jnp.sum(probs, axis=1))
    weighted = jnp.dot(probs.astype(jnp.bfloat16), value_head, preferred_element_type=jnp.float32)
    return (highest, summed, weighted)

def split_heads(matrix):
    return matrix.reshape(matrix.shape[0], HEADS, -1).transpose(1, 0, 2)

def group_layer(rows, image_ids, qkv_weight, out_weight):
    normed = normalize_rows(rows)
    qkv = jnp.dot(normed, qkv_weight, preferred_element_type=jnp.float32).astype(jnp.bfloat16)
    width = out_weight.shape[0]
    queries = split_heads(qkv[:, :width])
    keys = split_heads(qkv[:, width:2 * width])
    values = split_heads(qkv[:, 2 * width:])

    def one_head(triple):
        highest, summed, weighted = head_terms(triple[0], triple[1], triple[2], image_ids, image_ids)
        return (weighted / summed[:, None]).astype(jnp.bfloat16)
    heads = lax.map(one_head, (queries, keys, values))
    attended = heads.transpose(1, 0, 2).reshape(rows.shape[0], width)
    mixed = rows.astype(jnp.float32) + jnp.dot(attended, out_weight, preferred_element_type=jnp.float32)
    mixed = mixed.astype(jnp.bfloat16)
    onehot = (image_ids[:, None] == jnp.arange(IMG_GRP, dtype=jnp.int32)[None, :]).astype(jnp.bfloat16)
    pooled = lax.dot_general(onehot, mixed, (((0,), (0,)), ((), ())), preferred_element_type=jnp.float32)
    return (mixed, unit_rows(pooled))

def loss_rows(image_vecs, texts, row_start, col_start):
    text_vecs = unit_rows(texts.astype(jnp.float32))
    cosine = jnp.dot(image_vecs, text_vecs.T, precision=lax.Precision.HIGHEST)
    row_index = row_start + jnp.arange(image_vecs.shape[0], dtype=jnp.int32)
    col_index = col_start + jnp.arange(texts.shape[0], dtype=jnp.int32)
    labels = jnp.where(row_index[:, None] == col_index[None, :], 1.0, -1.0)
    return lax.optimization_barrier(jnp.sum(jax.nn.softplus(-labels * (logit_scale * cosine + logit_bias)), axis=1))

def reference(patches, segment_ids, qkv_weight, out_weight, text_embed):

    def per_group(pair):
        return group_layer(pair[0], pair[1], qkv_weight, out_weight)
    mixed, image_vecs = lax.map(per_group, (patches, segment_ids))
    image_vecs = image_vecs.reshape(-1, image_vecs.shape[2])
    row_loss = loss_rows(image_vecs, text_embed, 0, 0)
    return (mixed, row_loss)
```

```python
import functools
import math

import jax
import jax.numpy as jnp
from jax import lax
from jax.experimental import pallas as pl
from jax.experimental.pallas import tpu as pltpu
from jax.sharding import PartitionSpec as P

HEADS = 8
MAXP = 1024
LANES = 128
SPARE = 8
HIDDEN = -1e30

logit_scale = 30.0
logit_bias = -5.0

VMEM_LIMIT = 56 * 1024 * 1024


def rounded_up(value, step):
    return (value + step - 1) // step * step


def split_in_two(total, images):
    row = lax.broadcasted_iota(jnp.int32, total.shape, 0)
    main = total.astype(jnp.bfloat16).astype(jnp.float32)
    return jnp.where(row < images, main, total - main)


def image_rows(ids, images):
    row = lax.broadcasted_iota(jnp.int32, (SPARE, ids.shape[1]), 0)
    return (lax.rem(row, images) == ids).astype(jnp.float32).astype(jnp.bfloat16)


def project_kernel(images, piggy, ids_ref, rows_ref, weight_ref, out_ref, weight, turned, sem):
    fetch = pltpu.make_async_copy(weight_ref, weight, sem)
    fetch.start()
    count, depth = rows_ref.shape
    width = weight.shape[1] // 3
    size = width // HEADS
    rows = rows_ref[...]
    values = rows.astype(jnp.float32)
    center = values - jnp.mean(values, axis=1, keepdims=True)
    spread = jnp.mean(center * center, axis=1, keepdims=True)
    normed = (center * lax.rsqrt(spread + 1e-06)).astype(jnp.bfloat16)
    if piggy:
        own = lax.axis_index("grp") * count
        ids = ids_ref[:, pl.ds(pl.multiple_of(own, LANES), count)]
        sums = jnp.dot(image_rows(ids, images), rows, preferred_element_type=jnp.float32)
        sums = split_in_two(sums, images)
    fetch.wait()
    step = 3 * LANES
    for first in range(0, 3 * width, step):
        last = min(first + step, 3 * width)
        part = jnp.dot(normed, weight[:, first:last], preferred_element_type=jnp.float32)
        turned[first:last, :] = part.T
    for head in range(HEADS):
        query, key, value = (
            turned[at * width + head * size : at * width + (head + 1) * size, :] for at in range(3)
        )
        if piggy:
            spare = jnp.concatenate(
                [
                    sums[:, head * LANES : (head + 1) * LANES],
                    sums[:, HEADS * LANES :],
                    jnp.zeros((SPARE, count - depth + (HEADS - 1) * LANES), jnp.float32),
                ],
                axis=1,
            )
        else:
            spare = jnp.zeros((SPARE, count), jnp.float32)
        block = jnp.concatenate([value, key, spare, query], axis=0)
        out_ref[head] = block.astype(jnp.bfloat16)


def attend_kernel(images, piggy, halo, ids_ref, got_ref, *rest):
    if halo:
        left_ref, right_ref, out_ref, keys, values, queries, attended, starts = rest
    else:
        out_ref, keys, values, queries, attended, starts = rest
    count = got_ref.shape[2]
    padded = attended.shape[0]
    size = padded - SPARE
    total_rows = HEADS * count
    length = ids_ref.shape[1]
    window = min(rounded_up(MAXP + LANES - 1, LANES), length)
    tile = 2 * LANES
    bits = max(1, (images - 1).bit_length())
    ids = ids_ref[...]
    for image in range(images):
        starts[image] = jnp.sum((ids < image).astype(jnp.int32))

    row = lax.broadcasted_iota(jnp.int32, (SPARE, length), 0)
    bit = jnp.bitwise_and(lax.shift_right_logical(jnp.broadcast_to(ids, row.shape), row >> 1), 1)
    odd = jnp.bitwise_and(row, 1)
    used = row < 2 * bits
    outside = jnp.logical_or(ids < 0, ids >= images)
    key_side = jnp.where(odd == 1, bit, 1 - bit).astype(jnp.float32)
    key_side = jnp.where(outside, 1.0, key_side)
    key_side = jnp.where(used, key_side * HIDDEN, 0.0)
    query_side = jnp.where(used, jnp.where(odd == 1, 1 - bit, bit), 0).astype(jnp.float32)

    def with_rows(marks, block):
        return jnp.concatenate([marks, block.astype(jnp.float32)[SPARE:]], axis=0).astype(jnp.bfloat16)

    key_at = size - SPARE
    query_at = 2 * size
    for source in range(HEADS):
        here = slice(halo + source * count, halo + (source + 1) * count)
        there = slice(source * count, (source + 1) * count)
        values[:, here] = got_ref[source, 0:padded]
        keys[0:16, here] = with_rows(key_side[:, here], got_ref[source, key_at : key_at + 16])
        keys[16:padded, here] = got_ref[source, key_at + 16 : key_at + padded]
        queries[0:16, there] = with_rows(query_side[:, here], got_ref[source, query_at : query_at + 16])
        queries[16:padded, there] = got_ref[source, query_at + 16 : query_at + padded]
    if halo:
        for ref, here in ((left_ref, slice(0, halo)), (right_ref, slice(length - halo, length))):
            values[:, here] = ref[0:padded]
            keys[0:16, here] = with_rows(key_side[:, here], ref[key_at : key_at + 16])
            keys[16:padded, here] = ref[key_at + 16 : key_at + padded]

    def one_tile(at, _):
        first = pl.multiple_of(at * tile, tile)
        lowest = jnp.int32(0)
        highest = jnp.int32(0)
        for image in range(1, images):
            lowest += (starts[image] <= halo + first).astype(jnp.int32)
            highest += (starts[image] <= halo + first + tile - 1).astype(jnp.int32)
        query = queries[:, pl.ds(first, tile)]
        labels = ids_ref[:, pl.ds(pl.multiple_of(halo + first, LANES), tile)]

        def one_image(image, _):
            begin = jnp.minimum(starts[image] // LANES * LANES, length - window)
            here = pl.ds(pl.multiple_of(begin, LANES), window)
            scores = lax.dot_general(
                keys[:, here], query, (((0,), (0,)), ((), ())), preferred_element_type=jnp.float32
            )
            top = jnp.max(scores, axis=0, keepdims=True)
            probs = jnp.exp2((scores - top) * (size ** (-0.5) * math.log2(math.e)))
            total = jnp.sum(probs, axis=0, keepdims=True)
            weighted = jnp.dot(
                values[:, here], probs.astype(jnp.bfloat16), preferred_element_type=jnp.float32
            )
            result = weighted / total
            place = (slice(None), pl.ds(first, tile))
            attended[place] = jnp.where(labels == image, result, attended[place])
            return 0

        lax.fori_loop(lowest, highest + 1, one_image, 0)
        return 0

    lax.fori_loop(0, total_rows // tile, one_tile, 0)

    odd_head = lax.rem(lax.axis_index("grp"), 2) == 1
    mine = ids[:, halo : halo + total_rows]

    def placed(block, spare):
        even = jnp.concatenate([block[0:size], spare], axis=0)
        odd = jnp.concatenate([spare, block[0:size]], axis=0)
        return jnp.where(odd_head, odd, even)

    if piggy:
        nothing = jnp.zeros((SPARE, total_rows), jnp.float32)
        flat = placed(attended[...], nothing).astype(jnp.bfloat16)
        pooled = lax.dot_general(
            image_rows(mine, images), flat, (((1,), (1,)), ((), ())), preferred_element_type=jnp.float32
        )
        pooled = split_in_two(pooled, images)
        sums = jnp.zeros((SPARE, 2 * LANES), jnp.float32)
        for source in range(HEADS):
            sums += got_ref[source, query_at : query_at + 16].astype(jnp.float32)[0:SPARE, 0 : 2 * LANES]
        sums = split_in_two(sums + pltpu.roll(sums, images, axis=0), images)
        spare = jnp.concatenate(
            [pooled, jnp.zeros((SPARE, LANES - padded), jnp.float32), sums], axis=1
        )
    else:
        spare = jnp.zeros((SPARE, count), jnp.float32)
    for source in range(HEADS):
        block = placed(attended[:, source * count : (source + 1) * count], spare)
        out_ref[source] = block.astype(jnp.bfloat16)


def joined_heads(got_ref, out_weight_ref, flat, weight):
    padded = got_ref.shape[1]
    size = padded - SPARE
    spares = []
    for head in range(HEADS):
        at = head * padded
        from_row = head * size - (SPARE if head % 2 else 0)
        weight[at : at + padded] = out_weight_ref[from_row : from_row + padded]
        edge = 0 if head % 2 else padded - 16
        rest = slice(16, padded) if head % 2 else slice(0, padded - 16)
        mixed_rows = got_ref[head, edge : edge + 16].astype(jnp.float32)
        nothing = jnp.zeros((SPARE, mixed_rows.shape[1]), jnp.float32)
        if head % 2:
            spares.append(mixed_rows[:SPARE])
            block = jnp.concatenate([nothing, mixed_rows[SPARE:]], axis=0)
        else:
            spares.append(mixed_rows[SPARE:])
            block = jnp.concatenate([mixed_rows[:SPARE], nothing], axis=0)
        flat[at + edge : at + edge + 16] = block.astype(jnp.bfloat16)
        flat[at + rest.start : at + rest.stop] = got_ref[head, rest]
    return spares


def mixed_rows_of(rows_ref, flat, weight):
    added = lax.dot_general(
        flat[...], weight[...], (((0,), (0,)), ((), ())), preferred_element_type=jnp.float32
    )
    return (rows_ref[...].astype(jnp.float32) + added).astype(jnp.bfloat16)


def unit_rows(matrix):
    return matrix * lax.rsqrt(jnp.sum(matrix * matrix, axis=1, keepdims=True) + 1e-06)


def losses(cosine, labels):
    logits = -labels * (logit_scale * cosine + logit_bias)
    return jnp.maximum(logits, 0.0) + jnp.log1p(jnp.exp(-jnp.abs(logits)))


def finish_kernel(images, rows_ref, got_ref, out_weight_ref, text_ref, mixed_ref, loss_ref, flat, weight, pooled_heads):
    padded = got_ref.shape[1]
    spares = joined_heads(got_ref, out_weight_ref, flat, weight)
    for head in range(HEADS):
        pooled_heads[:, head * padded : (head + 1) * padded] = spares[head][:, 0:padded]
    pooled = jnp.dot(
        pooled_heads[...].astype(jnp.bfloat16), weight[...], preferred_element_type=jnp.float32
    )
    patch_sums = [spare[:, LANES : 2 * LANES] for spare in spares] + [spares[0][:, 2 * LANES :]]
    pooled = pooled + jnp.concatenate(patch_sums, axis=1)
    pooled = pooled + pltpu.roll(pooled, images, axis=0)
    image_vecs = unit_rows(pooled)
    text_vecs = unit_rows(text_ref[...].astype(jnp.float32))
    cosine = lax.dot_general(
        text_vecs,
        image_vecs,
        (((1,), (1,)), ((), ())),
        precision=lax.Precision.HIGHEST,
        preferred_element_type=jnp.float32,
    )
    text = lax.broadcasted_iota(jnp.int32, cosine.shape, 0)
    image = lax.broadcasted_iota(jnp.int32, cosine.shape, 1)
    terms = losses(cosine, jnp.where(text == image, 1.0, -1.0))
    loss_ref[...] = jnp.sum(terms, axis=0, keepdims=True)[:, 0:images]
    mixed_ref[...] = mixed_rows_of(rows_ref, flat, weight)


def mix_kernel(rows_ref, got_ref, out_weight_ref, mixed_ref, flat, weight):
    joined_heads(got_ref, out_weight_ref, flat, weight)
    mixed_ref[...] = mixed_rows_of(rows_ref, flat, weight)


def in_vmem(count):
    return [pl.BlockSpec(memory_space=pltpu.VMEM)] * count


def call(kernel, out_shape, scratch, in_specs, flops):
    out_specs = jax.tree.map(lambda _: pl.BlockSpec(memory_space=pltpu.VMEM), out_shape)
    return pl.pallas_call(
        kernel,
        out_shape=out_shape,
        in_specs=in_specs,
        out_specs=out_specs,
        scratch_shapes=scratch,
        compiler_params=pltpu.CompilerParams(vmem_limit_bytes=VMEM_LIMIT),
        cost_estimate=pl.CostEstimate(flops=flops, bytes_accessed=8 << 20, transcendentals=0),
    )


def moved(value, axis, pairs):
    return lax.ppermute(value, axis, pairs)


def all_texts(texts):
    peers = lax.axis_size("blk")
    if peers & (peers - 1):
        shifts = range(1, peers)
        others = [moved(texts, "blk", [(i, (i + by) % peers) for i in range(peers)]) for by in shifts]
        return jnp.concatenate([texts] + others, axis=0)
    by = 1
    while by < peers:
        other = moved(texts, "blk", [(i, i ^ by) for i in range(peers)])
        texts = jnp.concatenate([texts, other], axis=0)
        by *= 2
    return texts


def exchanged(blocks, groups):
    return lax.all_to_all(blocks, "grp", 0, 0, axis_index_groups=groups, tiled=True)


def local(patches, segment_ids, qkv_weight, out_weight, text_embed):
    rows = patches[0]
    count, depth = rows.shape
    width = out_weight.shape[0]
    size = width // HEADS
    padded = size + SPARE
    images = text_embed.shape[0]
    group_size = lax.axis_size("grp")
    parts = group_size // HEADS
    piggy = parts == 1 and 2 * images == SPARE and count >= depth - (HEADS - 2) * LANES
    groups = None if parts == 1 else [list(range(p * HEADS, (p + 1) * HEADS)) for p in range(parts)]
    bf16, f32 = jnp.bfloat16, jnp.float32
    shape = jax.ShapeDtypeStruct

    blocks = call(
        functools.partial(project_kernel, images, piggy),
        shape((HEADS, 3 * size + SPARE, count), bf16),
        [
            pltpu.VMEM((depth, 3 * width), bf16),
            pltpu.VMEM((3 * width, count), f32),
            pltpu.SemaphoreType.DMA,
        ],
        in_vmem(2) + [pl.BlockSpec(memory_space=pl.ANY)],
        2 * count * depth * 3 * width,
    )(segment_ids, rows, qkv_weight)
    got = exchanged(blocks, groups)
    texts = all_texts(text_embed)

    length = HEADS * count
    halo = 0
    operands = [segment_ids, got]
    if parts > 1:
        halo = rounded_up(MAXP - 1, LANES)
        part = lax.axis_index("grp") // HEADS
        whole_ids = jnp.concatenate(
            [
                jnp.full((1, halo), -1, jnp.int32),
                segment_ids,
                jnp.full((1, halo), images, jnp.int32),
            ],
            axis=1,
        )
        near_ids = lax.dynamic_slice_in_dim(whole_ids, part * length, length + 2 * halo, axis=1)
        flat = got[:, : 2 * size].transpose(1, 0, 2).reshape(2 * size, length)
        flat = jnp.concatenate([flat, jnp.zeros((16, length), bf16)], axis=0)
        ahead = [(i, i + HEADS) for i in range(group_size - HEADS)]
        back = [(i + HEADS, i) for i in range(group_size - HEADS)]
        left = moved(flat[:, length - halo :], "grp", ahead)
        right = moved(flat[:, :halo], "grp", back)
        operands = [near_ids, got, left, right]
    reach = length + 2 * halo
    answers = call(
        functools.partial(attend_kernel, images, piggy, halo),
        shape((HEADS, padded, count), bf16),
        [
            pltpu.VMEM((padded, reach), bf16),
            pltpu.VMEM((padded, reach), bf16),
            pltpu.VMEM((padded, length), bf16),
            pltpu.VMEM((padded, length), f32),
            pltpu.SMEM((images,), jnp.int32),
        ],
        in_vmem(len(operands)),
        4 * size * length * MAXP,
    )(*operands)
    back_home = exchanged(answers, groups)

    joined = [pltpu.VMEM((HEADS * padded, count), bf16), pltpu.VMEM((HEADS * padded, depth), bf16)]
    flops = 2 * count * depth * width
    if piggy:
        mixed, row_loss = call(
            functools.partial(finish_kernel, images),
            (shape((count, depth), bf16), shape((1, images), f32)),
            joined + [pltpu.VMEM((SPARE, HEADS * padded), f32)],
            in_vmem(4),
            flops,
        )(rows, back_home, out_weight, texts)
        return (mixed[None], row_loss[0])
    mixed = call(mix_kernel, shape((count, depth), bf16), joined, in_vmem(3), flops)(
        rows, back_home, out_weight
    )
    own_ids = lax.dynamic_slice_in_dim(segment_ids[0], lax.axis_index("grp") * count, count)
    onehot = (own_ids[None, :] == jnp.arange(images, dtype=jnp.int32)[:, None]).astype(bf16)
    pooled = lax.psum(jnp.dot(onehot, mixed, preferred_element_type=f32), "grp")
    text_vecs = unit_rows(texts.astype(f32))
    cosine = jnp.dot(unit_rows(pooled), text_vecs.T, precision=lax.Precision.HIGHEST)
    same = jnp.arange(images)[:, None] == jnp.arange(texts.shape[0])[None, :]
    row_loss = jnp.sum(losses(cosine, jnp.where(same, 1.0, -1.0)), axis=1)
    return (mixed[None], row_loss)


def solution(mesh):
    placed = (P("blk", "grp", None), P("blk", None), P(), P(), P("blk", None))
    return jax.shard_map(
        local,
        mesh=mesh,
        in_specs=placed,
        out_specs=(P("blk", "grp", None), P("blk")),
        check_vma=False,
    )
```

```python
import functools
import math

import jax
import jax.numpy as jnp
from jax import lax
from jax.experimental import pallas as pl
from jax.experimental.pallas import tpu as pltpu
from jax.sharding import PartitionSpec as P

HEADS = 8
MAXP = 1024
LANES = 128
SPARE = 8
HIDDEN = -1e30

logit_scale = 30.0
logit_bias = -5.0

VMEM_LIMIT = 32 * 1024 * 1024


def rounded_up(value, step):
    return (value + step - 1) // step * step


def split_in_two(total, images):
    row = lax.broadcasted_iota(jnp.int32, total.shape, 0)
    main = total.astype(jnp.bfloat16).astype(jnp.float32)
    return jnp.where(row < images, main, total - main)


def image_rows(ids, images):
    row = lax.broadcasted_iota(jnp.int32, (SPARE, ids.shape[1]), 0)
    return (lax.rem(row, images) == ids).astype(jnp.float32).astype(jnp.bfloat16)


def project_kernel(images, piggy, ids_ref, rows_ref, weight_ref, out_ref, weight, turned, sems):
    count, depth = rows_ref.shape
    width = weight.shape[0] // 3
    size = width // HEADS
    pieces = sems.shape[0]
    step = 3 * width // pieces
    cuts = [slice(piece * step, (piece + 1) * step) for piece in range(pieces)]
    fetches = [
        pltpu.make_async_copy(weight_ref.at[cut], weight.at[cut], sems.at[piece])
        for piece, cut in enumerate(cuts)
    ]
    for fetch in fetches:
        fetch.start()
    rows = rows_ref[...]
    values = rows.astype(jnp.float32)
    center = values - jnp.mean(values, axis=1, keepdims=True)
    spread = jnp.mean(center * center, axis=1, keepdims=True)
    normed = (center * lax.rsqrt(spread + 1e-06)).astype(jnp.bfloat16)
    if piggy:
        own = lax.axis_index("grp") * count
        ids = ids_ref[:, pl.ds(pl.multiple_of(own, LANES), count)]
        sums = jnp.dot(image_rows(ids, images), rows, preferred_element_type=jnp.float32)
        sums = split_in_two(sums, images)
    for fetch, cut in zip(fetches, cuts):
        fetch.wait()
        turned[cut, :] = lax.dot_general(
            weight[cut, :], normed, (((1,), (1,)), ((), ())), preferred_element_type=jnp.float32
        )
    for head in range(HEADS):
        query, key, value = (
            turned[at * width + head * size : at * width + (head + 1) * size, :] for at in range(3)
        )
        if piggy:
            spare = jnp.concatenate(
                [
                    sums[:, head * LANES : (head + 1) * LANES],
                    sums[:, HEADS * LANES :],
                    jnp.zeros((SPARE, count - depth + (HEADS - 1) * LANES), jnp.float32),
                ],
                axis=1,
            )
        else:
            spare = jnp.zeros((SPARE, count), jnp.float32)
        block = jnp.concatenate([value, key, spare, query], axis=0)
        out_ref[head] = block.astype(jnp.bfloat16)


def attend_kernel(images, piggy, halo, ids_ref, got_ref, *rest):
    if halo:
        left_ref, right_ref, *rest = rest
    out_ref, keys, values, queries, attended, scores_a, scores_b, tops_a, tops_b, starts = rest
    count = got_ref.shape[2]
    padded = attended.shape[0]
    size = padded - SPARE
    total_rows = HEADS * count
    length = ids_ref.shape[1]
    window = scores_a.shape[0]
    tile = scores_a.shape[1]
    tiles = total_rows // tile
    bits = max(1, (images - 1).bit_length())
    ids = ids_ref[...]
    for image in range(images):
        starts[image] = jnp.sum((ids < image).astype(jnp.int32))

    row = lax.broadcasted_iota(jnp.int32, (SPARE, length), 0)
    bit = jnp.bitwise_and(lax.shift_right_logical(jnp.broadcast_to(ids, row.shape), row >> 1), 1)
    odd = jnp.bitwise_and(row, 1)
    used = row < 2 * bits
    outside = jnp.logical_or(ids < 0, ids >= images)
    key_side = jnp.where(odd == 1, bit, 1 - bit).astype(jnp.float32)
    key_side = jnp.where(outside, 1.0, key_side)
    key_side = jnp.where(used, key_side * HIDDEN, 0.0)
    query_side = jnp.where(used, jnp.where(odd == 1, 1 - bit, bit), 0).astype(jnp.float32)

    def with_rows(marks, block):
        return jnp.concatenate([marks, block.astype(jnp.float32)[SPARE:]], axis=0).astype(jnp.bfloat16)

    key_at = size - SPARE
    query_at = 2 * size
    blank = jnp.zeros((LANES - padded, count), jnp.float32)

    def turned_keys(here, block):
        marked = jnp.concatenate([key_side[:, here], block.astype(jnp.float32)[SPARE:]], axis=0)
        filled = jnp.concatenate([marked, jnp.zeros((LANES - padded, block.shape[1]), jnp.float32)], axis=0)
        return filled.T.astype(jnp.bfloat16)

    for source in range(HEADS):
        here = slice(halo + source * count, halo + (source + 1) * count)
        there = slice(source * count, (source + 1) * count)
        values[:, here] = got_ref[source, 0:padded]
        keys[here, :] = turned_keys(here, got_ref[source, key_at : key_at + padded])
        queries[0:16, there] = with_rows(query_side[:, here], got_ref[source, query_at : query_at + 16])
        queries[16:padded, there] = got_ref[source, query_at + 16 : query_at + padded]
        queries[padded:, there] = blank.astype(jnp.bfloat16)
    if halo:
        for ref, here in ((left_ref, slice(0, halo)), (right_ref, slice(length - halo, length))):
            values[:, here] = ref[0:padded]
            keys[here, :] = turned_keys(here, ref[key_at : key_at + padded])

    def image_at(position):
        found = jnp.int32(0)
        for image in range(1, images):
            found += (starts[image] <= position).astype(jnp.int32)
        return found

    def following(state):
        at, image = state
        more = image < image_at(halo + at * tile + tile - 1)
        later = jnp.minimum(at + 1, tiles - 1)
        first = jnp.maximum(image_at(halo + later * tile), jnp.where(later == at, image, 0))
        return jnp.where(more, at, later), jnp.where(more, image + 1, first)

    def window_of(image):
        begin = jnp.minimum(starts[image] // LANES * LANES, length - window)
        return pl.ds(pl.multiple_of(begin, LANES), window)

    def score(state, scores, tops):
        at, image = state
        query = queries[:, pl.ds(pl.multiple_of(at * tile, tile), tile)]
        found = jnp.dot(keys[window_of(image), :], query, preferred_element_type=jnp.float32)
        scores[...] = found
        tops[...] = jnp.max(found, axis=0, keepdims=True)

    def weigh(state, scores, tops):
        at, image = state
        first = pl.multiple_of(at * tile, tile)
        labels = ids_ref[:, pl.ds(pl.multiple_of(halo + first, LANES), tile)]
        probs = jnp.exp2((scores[...] - tops[...]) * (size ** (-0.5) * math.log2(math.e)))
        total = jnp.sum(probs, axis=0, keepdims=True)
        weighted = jnp.dot(
            values[:, window_of(image)], probs.astype(jnp.bfloat16), preferred_element_type=jnp.float32
        )
        place = (slice(None), pl.ds(first, tile))
        attended[place] = jnp.where(labels == image, weighted / total, attended[place])

    pairs = jnp.int32(tiles)
    for image in range(1, images):
        offset = starts[image] - halo
        inside = jnp.logical_and(offset > 0, offset < total_rows)
        pairs += jnp.logical_and(inside, lax.rem(offset, tile) != 0).astype(jnp.int32)

    def two_pairs(_, state):
        second = following(state)
        score(second, scores_b, tops_b)
        weigh(state, scores_a, tops_a)
        third = following(second)
        score(third, scores_a, tops_a)
        weigh(second, scores_b, tops_b)
        return third

    begun = (jnp.int32(0), image_at(halo))
    score(begun, scores_a, tops_a)
    lax.fori_loop(0, (pairs + 1) // 2, two_pairs, begun)

    odd_head = lax.rem(lax.axis_index("grp"), 2) == 1
    mine = ids[:, halo : halo + total_rows]

    def placed(block, spare):
        even = jnp.concatenate([block[0:size], spare], axis=0)
        odd = jnp.concatenate([spare, block[0:size]], axis=0)
        return jnp.where(odd_head, odd, even)

    if piggy:
        nothing = jnp.zeros((SPARE, total_rows), jnp.float32)
        flat = placed(attended[...], nothing).astype(jnp.bfloat16)
        pooled = lax.dot_general(
            image_rows(mine, images), flat, (((1,), (1,)), ((), ())), preferred_element_type=jnp.float32
        )
        pooled = split_in_two(pooled, images)
        sums = jnp.zeros((SPARE, 2 * LANES), jnp.float32)
        for source in range(HEADS):
            sums += got_ref[source, query_at : query_at + 16].astype(jnp.float32)[0:SPARE, 0 : 2 * LANES]
        sums = split_in_two(sums + pltpu.roll(sums, images, axis=0), images)
        spare = jnp.concatenate(
            [pooled, jnp.zeros((SPARE, LANES - padded), jnp.float32), sums], axis=1
        )
    else:
        spare = jnp.zeros((SPARE, count), jnp.float32)
    for source in range(HEADS):
        block = placed(attended[:, source * count : (source + 1) * count], spare)
        out_ref[source] = block.astype(jnp.bfloat16)


def joined_heads(got_ref, out_weight_ref, flat, weight):
    padded = got_ref.shape[1]
    size = padded - SPARE
    spares = []
    for head in range(HEADS):
        at = head * padded
        from_row = head * size - (SPARE if head % 2 else 0)
        weight[at : at + padded] = out_weight_ref[from_row : from_row + padded]
        edge = 0 if head % 2 else padded - 16
        rest = slice(16, padded) if head % 2 else slice(0, padded - 16)
        mixed_rows = got_ref[head, edge : edge + 16].astype(jnp.float32)
        nothing = jnp.zeros((SPARE, mixed_rows.shape[1]), jnp.float32)
        if head % 2:
            spares.append(mixed_rows[:SPARE])
            block = jnp.concatenate([nothing, mixed_rows[SPARE:]], axis=0)
        else:
            spares.append(mixed_rows[SPARE:])
            block = jnp.concatenate([mixed_rows[:SPARE], nothing], axis=0)
        flat[at + edge : at + edge + 16] = block.astype(jnp.bfloat16)
        flat[at + rest.start : at + rest.stop] = got_ref[head, rest]
    return spares


def mixed_rows_of(rows_ref, flat, weight):
    added = lax.dot_general(
        flat[...], weight[...], (((0,), (0,)), ((), ())), preferred_element_type=jnp.float32
    )
    return (rows_ref[...].astype(jnp.float32) + added).astype(jnp.bfloat16)


def unit_rows(matrix):
    return matrix * lax.rsqrt(jnp.sum(matrix * matrix, axis=1, keepdims=True) + 1e-06)


def losses(cosine, labels):
    logits = -labels * (logit_scale * cosine + logit_bias)
    return jnp.maximum(logits, 0.0) + jnp.log1p(jnp.exp(-jnp.abs(logits)))


def finish_kernel(images, rows_ref, got_ref, out_weight_ref, text_ref, mixed_ref, loss_ref, flat, weight, pooled_heads):
    padded = got_ref.shape[1]
    spares = joined_heads(got_ref, out_weight_ref, flat, weight)
    for head in range(HEADS):
        pooled_heads[:, head * padded : (head + 1) * padded] = spares[head][:, 0:padded]
    pooled = jnp.dot(
        pooled_heads[...].astype(jnp.bfloat16), weight[...], preferred_element_type=jnp.float32
    )
    patch_sums = [spare[:, LANES : 2 * LANES] for spare in spares] + [spares[0][:, 2 * LANES :]]
    pooled = pooled + jnp.concatenate(patch_sums, axis=1)
    pooled = pooled + pltpu.roll(pooled, images, axis=0)
    image_vecs = unit_rows(pooled)
    text_vecs = unit_rows(text_ref[...].astype(jnp.float32))
    cosine = lax.dot_general(
        text_vecs,
        image_vecs,
        (((1,), (1,)), ((), ())),
        precision=lax.Precision.HIGHEST,
        preferred_element_type=jnp.float32,
    )
    text = lax.broadcasted_iota(jnp.int32, cosine.shape, 0)
    image = lax.broadcasted_iota(jnp.int32, cosine.shape, 1)
    terms = losses(cosine, jnp.where(text == image, 1.0, -1.0))
    loss_ref[...] = jnp.sum(terms, axis=0, keepdims=True)[:, 0:images]
    mixed_ref[...] = mixed_rows_of(rows_ref, flat, weight)


def mix_kernel(rows_ref, got_ref, out_weight_ref, mixed_ref, flat, weight):
    joined_heads(got_ref, out_weight_ref, flat, weight)
    mixed_ref[...] = mixed_rows_of(rows_ref, flat, weight)


def in_vmem(count):
    return [pl.BlockSpec(memory_space=pltpu.VMEM)] * count


def call(kernel, out_shape, scratch, in_specs, flops):
    out_specs = jax.tree.map(lambda _: pl.BlockSpec(memory_space=pltpu.VMEM), out_shape)
    return pl.pallas_call(
        kernel,
        out_shape=out_shape,
        in_specs=in_specs,
        out_specs=out_specs,
        scratch_shapes=scratch,
        compiler_params=pltpu.CompilerParams(vmem_limit_bytes=VMEM_LIMIT),
        cost_estimate=pl.CostEstimate(flops=flops, bytes_accessed=8 << 20, transcendentals=0),
    )


def moved(value, axis, pairs):
    return lax.ppermute(value, axis, pairs)


def all_texts(texts):
    peers = lax.axis_size("blk")
    if peers & (peers - 1):
        shifts = range(1, peers)
        others = [moved(texts, "blk", [(i, (i + by) % peers) for i in range(peers)]) for by in shifts]
        return jnp.concatenate([texts] + others, axis=0)
    by = 1
    while by < peers:
        other = moved(texts, "blk", [(i, i ^ by) for i in range(peers)])
        texts = jnp.concatenate([texts, other], axis=0)
        by *= 2
    return texts


def exchanged(blocks, groups):
    return lax.all_to_all(blocks, "grp", 0, 0, axis_index_groups=groups, tiled=True)


def local(patches, segment_ids, qkv_weight, out_weight, text_embed):
    rows = patches[0]
    count, depth = rows.shape
    width = out_weight.shape[0]
    size = width // HEADS
    padded = size + SPARE
    images = text_embed.shape[0]
    group_size = lax.axis_size("grp")
    parts = group_size // HEADS
    piggy = parts == 1 and 2 * images == SPARE and count >= depth - (HEADS - 2) * LANES
    groups = None if parts == 1 else [list(range(p * HEADS, (p + 1) * HEADS)) for p in range(parts)]
    bf16, f32 = jnp.bfloat16, jnp.float32
    shape = jax.ShapeDtypeStruct

    blocks = call(
        functools.partial(project_kernel, images, piggy),
        shape((HEADS, 3 * size + SPARE, count), bf16),
        [
            pltpu.VMEM((3 * width, depth), bf16),
            pltpu.VMEM((3 * width, count), f32),
            pltpu.SemaphoreType.DMA((4,)),
        ],
        in_vmem(2) + [pl.BlockSpec(memory_space=pl.ANY)],
        2 * count * depth * 3 * width,
    )(segment_ids, rows, qkv_weight.T)
    got = exchanged(blocks, groups)
    got, texts = lax.optimization_barrier((got, all_texts(text_embed)))

    length = HEADS * count
    halo = 0
    operands = [segment_ids, got]
    if parts > 1:
        halo = rounded_up(MAXP - 1, LANES)
        part = lax.axis_index("grp") // HEADS
        whole_ids = jnp.concatenate(
            [
                jnp.full((1, halo), -1, jnp.int32),
                segment_ids,
                jnp.full((1, halo), images, jnp.int32),
            ],
            axis=1,
        )
        near_ids = lax.dynamic_slice_in_dim(whole_ids, part * length, length + 2 * halo, axis=1)
        flat = got[:, : 2 * size].transpose(1, 0, 2).reshape(2 * size, length)
        flat = jnp.concatenate([flat, jnp.zeros((16, length), bf16)], axis=0)
        ahead = [(i, i + HEADS) for i in range(group_size - HEADS)]
        back = [(i + HEADS, i) for i in range(group_size - HEADS)]
        left = moved(flat[:, length - halo :], "grp", ahead)
        right = moved(flat[:, :halo], "grp", back)
        operands = [near_ids, got, left, right]
    reach = length + 2 * halo
    window = min(rounded_up(MAXP + LANES - 1, LANES), reach)
    tile = 2 * LANES
    answers = call(
        functools.partial(attend_kernel, images, piggy, halo),
        shape((HEADS, padded, count), bf16),
        [
            pltpu.VMEM((reach, LANES), bf16),
            pltpu.VMEM((padded, reach), bf16),
            pltpu.VMEM((LANES, length), bf16),
            pltpu.VMEM((padded, length), f32),
            pltpu.VMEM((window, tile), f32),
            pltpu.VMEM((window, tile), f32),
            pltpu.VMEM((1, tile), f32),
            pltpu.VMEM((1, tile), f32),
            pltpu.SMEM((images,), jnp.int32),
        ],
        in_vmem(len(operands)),
        4 * size * length * MAXP,
    )(*operands)
    back_home = exchanged(answers, groups)

    joined = [pltpu.VMEM((HEADS * padded, count), bf16), pltpu.VMEM((HEADS * padded, depth), bf16)]
    flops = 2 * count * depth * width
    if piggy:
        mixed, row_loss = call(
            functools.partial(finish_kernel, images),
            (shape((count, depth), bf16), shape((1, images), f32)),
            joined + [pltpu.VMEM((SPARE, HEADS * padded), f32)],
            in_vmem(4),
            flops,
        )(rows, back_home, out_weight, texts)
        return (mixed[None], row_loss[0])
    mixed = call(mix_kernel, shape((count, depth), bf16), joined, in_vmem(3), flops)(
        rows, back_home, out_weight
    )
    own_ids = lax.dynamic_slice_in_dim(segment_ids[0], lax.axis_index("grp") * count, count)
    onehot = (own_ids[None, :] == jnp.arange(images, dtype=jnp.int32)[:, None]).astype(bf16)
    pooled = lax.psum(jnp.dot(onehot, mixed, preferred_element_type=f32), "grp")
    text_vecs = unit_rows(texts.astype(f32))
    cosine = jnp.dot(unit_rows(pooled), text_vecs.T, precision=lax.Precision.HIGHEST)
    same = jnp.arange(images)[:, None] == jnp.arange(texts.shape[0])[None, :]
    row_loss = jnp.sum(losses(cosine, jnp.where(same, 1.0, -1.0)), axis=1)
    return (mixed[None], row_loss)


def solution(mesh):
    placed = (P("blk", "grp", None), P("blk", None), P(), P(), P("blk", None))
    return jax.shard_map(
        local,
        mesh=mesh,
        in_specs=placed,
        out_specs=(P("blk", "grp", None), P("blk")),
        check_vma=False,
    )
```

```python
import functools
import math

import jax
import jax.numpy as jnp
from jax import lax
from jax.experimental import pallas as pl
from jax.experimental.pallas import tpu as pltpu
from jax.sharding import PartitionSpec as P

HEADS = 8
MAXP = 1024
LANES = 128
SPARE = 8
HIDDEN = -1e30

logit_scale = 30.0
logit_bias = -5.0

VMEM_LIMIT = 32 * 1024 * 1024


def rounded_up(value, step):
    return (value + step - 1) // step * step


def split_in_two(total, images):
    row = lax.broadcasted_iota(jnp.int32, total.shape, 0)
    main = total.astype(jnp.bfloat16).astype(jnp.float32)
    return jnp.where(row < images, main, total - main)


def image_rows(ids, images):
    row = lax.broadcasted_iota(jnp.int32, (SPARE, ids.shape[1]), 0)
    return (lax.rem(row, images) == ids).astype(jnp.float32).astype(jnp.bfloat16)


def project_kernel(images, piggy, ids_ref, rows_ref, weight_ref, out_ref, own_ids, rows_held, weight, turned, id_sem, row_sem, sems):
    count, depth = rows_ref.shape
    rows_fetch = pltpu.make_async_copy(rows_ref, rows_held, row_sem)
    rows_fetch.start()
    own = pl.multiple_of(lax.axis_index("grp") * count, LANES)
    ids_fetch = pltpu.make_async_copy(ids_ref.at[:, pl.ds(own, count)], own_ids, id_sem)
    ids_fetch.start()
    width = weight.shape[0] // 3
    size = width // HEADS
    pieces = sems.shape[0]
    step = 3 * width // pieces
    cuts = [slice(piece * step, (piece + 1) * step) for piece in range(pieces)]
    fetches = [
        pltpu.make_async_copy(weight_ref.at[cut], weight.at[cut], sems.at[piece])
        for piece, cut in enumerate(cuts)
    ]
    for fetch in fetches:
        fetch.start()
    rows_fetch.wait()
    rows = rows_held[...]
    values = rows.astype(jnp.float32)
    center = values - jnp.mean(values, axis=1, keepdims=True)
    spread = jnp.mean(center * center, axis=1, keepdims=True)
    normed = (center * lax.rsqrt(spread + 1e-06)).astype(jnp.bfloat16)
    ids_fetch.wait()
    if piggy:
        sums = jnp.dot(image_rows(own_ids[...], images), rows, preferred_element_type=jnp.float32)
        sums = split_in_two(sums, images)
    for fetch, cut in zip(fetches, cuts):
        fetch.wait()
        turned[cut, :] = lax.dot_general(
            weight[cut, :], normed, (((1,), (1,)), ((), ())), preferred_element_type=jnp.float32
        )
    for head in range(HEADS):
        query, key, value = (
            turned[at * width + head * size : at * width + (head + 1) * size, :] for at in range(3)
        )
        if piggy:
            spare = jnp.concatenate(
                [
                    sums[:, head * LANES : (head + 1) * LANES],
                    sums[:, HEADS * LANES :],
                    jnp.zeros((SPARE, count - depth + (HEADS - 1) * LANES), jnp.float32),
                ],
                axis=1,
            )
        else:
            spare = jnp.zeros((SPARE, count), jnp.float32)
        block = jnp.concatenate([value, key, spare, query], axis=0)
        out_ref[head] = block.astype(jnp.bfloat16)


def attend_kernel(images, piggy, halo, ids_ref, got_ref, *rest):
    if halo:
        left_ref, right_ref, *rest = rest
    out_ref, keys, values, queries, attended, scores_a, scores_b, tops_a, tops_b, starts = rest
    count = got_ref.shape[2]
    padded = attended.shape[0]
    size = padded - SPARE
    total_rows = HEADS * count
    length = ids_ref.shape[1]
    window = scores_a.shape[0]
    tile = scores_a.shape[1]
    tiles = total_rows // tile
    bits = max(1, (images - 1).bit_length())
    ids = ids_ref[...]
    for image in range(images):
        starts[image] = jnp.sum((ids < image).astype(jnp.int32))

    row = lax.broadcasted_iota(jnp.int32, (SPARE, length), 0)
    bit = jnp.bitwise_and(lax.shift_right_logical(jnp.broadcast_to(ids, row.shape), row >> 1), 1)
    odd = jnp.bitwise_and(row, 1)
    used = row < 2 * bits
    outside = jnp.logical_or(ids < 0, ids >= images)
    key_side = jnp.where(odd == 1, bit, 1 - bit).astype(jnp.float32)
    key_side = jnp.where(outside, 1.0, key_side)
    key_side = jnp.where(used, key_side * HIDDEN, 0.0)
    query_side = jnp.where(used, jnp.where(odd == 1, 1 - bit, bit), 0).astype(jnp.float32)

    def with_rows(marks, block):
        return jnp.concatenate([marks, block.astype(jnp.float32)[SPARE:]], axis=0).astype(jnp.bfloat16)

    key_at = size - SPARE
    query_at = 2 * size
    blank = jnp.zeros((LANES - padded, count), jnp.float32)

    def turned_keys(here, block):
        marked = jnp.concatenate([key_side[:, here], block.astype(jnp.float32)[SPARE:]], axis=0)
        filled = jnp.concatenate([marked, jnp.zeros((LANES - padded, block.shape[1]), jnp.float32)], axis=0)
        return filled.T.astype(jnp.bfloat16)

    for source in range(HEADS):
        here = slice(halo + source * count, halo + (source + 1) * count)
        there = slice(source * count, (source + 1) * count)
        values[:, here] = got_ref[source, 0:padded]
        keys[here, :] = turned_keys(here, got_ref[source, key_at : key_at + padded])
        queries[0:16, there] = with_rows(query_side[:, here], got_ref[source, query_at : query_at + 16])
        queries[16:padded, there] = got_ref[source, query_at + 16 : query_at + padded]
        queries[padded:, there] = blank.astype(jnp.bfloat16)
    if halo:
        for ref, here in ((left_ref, slice(0, halo)), (right_ref, slice(length - halo, length))):
            values[:, here] = ref[0:padded]
            keys[here, :] = turned_keys(here, ref[key_at : key_at + padded])

    def image_at(position):
        found = jnp.int32(0)
        for image in range(1, images):
            found += (starts[image] <= position).astype(jnp.int32)
        return found

    def following(state):
        at, image = state
        more = image < image_at(halo + at * tile + tile - 1)
        later = jnp.minimum(at + 1, tiles - 1)
        first = jnp.maximum(image_at(halo + later * tile), jnp.where(later == at, image, 0))
        return jnp.where(more, at, later), jnp.where(more, image + 1, first)

    def window_of(image):
        begin = jnp.minimum(starts[image] // LANES * LANES, length - window)
        return pl.ds(pl.multiple_of(begin, LANES), window)

    def score(state, scores, tops):
        at, image = state
        query = queries[:, pl.ds(pl.multiple_of(at * tile, tile), tile)]
        found = jnp.dot(keys[window_of(image), :], query, preferred_element_type=jnp.float32)
        scores[...] = found
        tops[...] = jnp.max(found, axis=0, keepdims=True)

    def weigh(state, scores, tops):
        at, image = state
        first = pl.multiple_of(at * tile, tile)
        labels = ids_ref[:, pl.ds(pl.multiple_of(halo + first, LANES), tile)]
        probs = jnp.exp2((scores[...] - tops[...]) * (size ** (-0.5) * math.log2(math.e)))
        total = jnp.sum(probs, axis=0, keepdims=True)
        weighted = jnp.dot(
            values[:, window_of(image)], probs.astype(jnp.bfloat16), preferred_element_type=jnp.float32
        )
        place = (slice(None), pl.ds(first, tile))
        attended[place] = jnp.where(labels == image, weighted / total, attended[place])

    pairs = jnp.int32(tiles)
    for image in range(1, images):
        offset = starts[image] - halo
        inside = jnp.logical_and(offset > 0, offset < total_rows)
        pairs += jnp.logical_and(inside, lax.rem(offset, tile) != 0).astype(jnp.int32)

    def two_pairs(_, state):
        second = following(state)
        score(second, scores_b, tops_b)
        weigh(state, scores_a, tops_a)
        third = following(second)
        score(third, scores_a, tops_a)
        weigh(second, scores_b, tops_b)
        return third

    begun = (jnp.int32(0), image_at(halo))
    score(begun, scores_a, tops_a)
    lax.fori_loop(0, (pairs + 1) // 2, two_pairs, begun)

    odd_head = lax.rem(lax.axis_index("grp"), 2) == 1
    mine = ids[:, halo : halo + total_rows]

    def placed(block, spare):
        even = jnp.concatenate([block[0:size], spare], axis=0)
        odd = jnp.concatenate([spare, block[0:size]], axis=0)
        return jnp.where(odd_head, odd, even)

    if piggy:
        nothing = jnp.zeros((SPARE, total_rows), jnp.float32)
        flat = placed(attended[...], nothing).astype(jnp.bfloat16)
        pooled = lax.dot_general(
            image_rows(mine, images), flat, (((1,), (1,)), ((), ())), preferred_element_type=jnp.float32
        )
        pooled = split_in_two(pooled, images)
        sums = jnp.zeros((SPARE, 2 * LANES), jnp.float32)
        for source in range(HEADS):
            sums += got_ref[source, query_at : query_at + 16].astype(jnp.float32)[0:SPARE, 0 : 2 * LANES]
        sums = split_in_two(sums + pltpu.roll(sums, images, axis=0), images)
        spare = jnp.concatenate(
            [pooled, jnp.zeros((SPARE, LANES - padded), jnp.float32), sums], axis=1
        )
    else:
        spare = jnp.zeros((SPARE, count), jnp.float32)
    for source in range(HEADS):
        block = placed(attended[:, source * count : (source + 1) * count], spare)
        out_ref[source] = block.astype(jnp.bfloat16)


def joined_heads(got_ref, out_weight_ref, flat, weight):
    padded = got_ref.shape[1]
    size = padded - SPARE
    spares = []
    for head in range(HEADS):
        at = head * padded
        from_row = head * size - (SPARE if head % 2 else 0)
        weight[at : at + padded] = out_weight_ref[from_row : from_row + padded]
        edge = 0 if head % 2 else padded - 16
        rest = slice(16, padded) if head % 2 else slice(0, padded - 16)
        mixed_rows = got_ref[head, edge : edge + 16].astype(jnp.float32)
        nothing = jnp.zeros((SPARE, mixed_rows.shape[1]), jnp.float32)
        if head % 2:
            spares.append(mixed_rows[:SPARE])
            block = jnp.concatenate([nothing, mixed_rows[SPARE:]], axis=0)
        else:
            spares.append(mixed_rows[SPARE:])
            block = jnp.concatenate([mixed_rows[:SPARE], nothing], axis=0)
        flat[at + edge : at + edge + 16] = block.astype(jnp.bfloat16)
        flat[at + rest.start : at + rest.stop] = got_ref[head, rest]
    return spares


def mixed_rows_of(rows_ref, flat, weight):
    added = lax.dot_general(
        flat[...], weight[...], (((0,), (0,)), ((), ())), preferred_element_type=jnp.float32
    )
    return (rows_ref[...].astype(jnp.float32) + added).astype(jnp.bfloat16)


def unit_rows(matrix):
    return matrix * lax.rsqrt(jnp.sum(matrix * matrix, axis=1, keepdims=True) + 1e-06)


def losses(cosine, labels):
    logits = -labels * (logit_scale * cosine + logit_bias)
    return jnp.maximum(logits, 0.0) + jnp.log1p(jnp.exp(-jnp.abs(logits)))


def finish_kernel(images, rows_ref, got_ref, out_weight_ref, text_ref, mixed_ref, loss_ref, flat, weight, pooled_heads):
    padded = got_ref.shape[1]
    spares = joined_heads(got_ref, out_weight_ref, flat, weight)
    for head in range(HEADS):
        pooled_heads[:, head * padded : (head + 1) * padded] = spares[head][:, 0:padded]
    pooled = jnp.dot(
        pooled_heads[...].astype(jnp.bfloat16), weight[...], preferred_element_type=jnp.float32
    )
    patch_sums = [spare[:, LANES : 2 * LANES] for spare in spares] + [spares[0][:, 2 * LANES :]]
    pooled = pooled + jnp.concatenate(patch_sums, axis=1)
    pooled = pooled + pltpu.roll(pooled, images, axis=0)
    image_vecs = unit_rows(pooled)
    text_vecs = unit_rows(text_ref[...].astype(jnp.float32))
    cosine = lax.dot_general(
        text_vecs,
        image_vecs,
        (((1,), (1,)), ((), ())),
        precision=lax.Precision.HIGHEST,
        preferred_element_type=jnp.float32,
    )
    text = lax.broadcasted_iota(jnp.int32, cosine.shape, 0)
    image = lax.broadcasted_iota(jnp.int32, cosine.shape, 1)
    terms = losses(cosine, jnp.where(text == image, 1.0, -1.0))
    loss_ref[...] = jnp.sum(terms, axis=0, keepdims=True)[:, 0:images]
    mixed_ref[...] = mixed_rows_of(rows_ref, flat, weight)


def mix_kernel(rows_ref, got_ref, out_weight_ref, mixed_ref, flat, weight):
    joined_heads(got_ref, out_weight_ref, flat, weight)
    mixed_ref[...] = mixed_rows_of(rows_ref, flat, weight)


def in_vmem(count):
    return [pl.BlockSpec(memory_space=pltpu.VMEM)] * count


def in_hbm(value):
    return pltpu.with_memory_space_constraint(value, pltpu.HBM)


def call(kernel, out_shape, scratch, in_specs, flops):
    out_specs = jax.tree.map(lambda _: pl.BlockSpec(memory_space=pltpu.VMEM), out_shape)
    return pl.pallas_call(
        kernel,
        out_shape=out_shape,
        in_specs=in_specs,
        out_specs=out_specs,
        scratch_shapes=scratch,
        compiler_params=pltpu.CompilerParams(vmem_limit_bytes=VMEM_LIMIT),
        cost_estimate=pl.CostEstimate(flops=flops, bytes_accessed=8 << 20, transcendentals=0),
    )


def moved(value, axis, pairs):
    return lax.ppermute(value, axis, pairs)


def all_texts(texts):
    peers = lax.axis_size("blk")
    if peers & (peers - 1):
        shifts = range(1, peers)
        others = [moved(texts, "blk", [(i, (i + by) % peers) for i in range(peers)]) for by in shifts]
        return jnp.concatenate([texts] + others, axis=0)
    by = 1
    while by < peers:
        other = moved(texts, "blk", [(i, i ^ by) for i in range(peers)])
        texts = jnp.concatenate([texts, other], axis=0)
        by *= 2
    return texts


def exchanged(blocks, groups):
    return lax.all_to_all(blocks, "grp", 0, 0, axis_index_groups=groups, tiled=True)


def local(patches, segment_ids, qkv_weight, out_weight, text_embed):
    rows = patches[0]
    count, depth = rows.shape
    width = out_weight.shape[0]
    size = width // HEADS
    padded = size + SPARE
    images = text_embed.shape[0]
    group_size = lax.axis_size("grp")
    parts = group_size // HEADS
    piggy = parts == 1 and 2 * images == SPARE and count >= depth - (HEADS - 2) * LANES
    groups = None if parts == 1 else [list(range(p * HEADS, (p + 1) * HEADS)) for p in range(parts)]
    bf16, f32 = jnp.bfloat16, jnp.float32
    shape = jax.ShapeDtypeStruct

    blocks = call(
        functools.partial(project_kernel, images, piggy),
        shape((HEADS, 3 * size + SPARE, count), bf16),
        [
            pltpu.VMEM((1, count), jnp.int32),
            pltpu.VMEM((count, depth), bf16),
            pltpu.VMEM((3 * width, depth), bf16),
            pltpu.VMEM((3 * width, count), f32),
            pltpu.SemaphoreType.DMA,
            pltpu.SemaphoreType.DMA,
            pltpu.SemaphoreType.DMA((4,)),
        ],
        [pl.BlockSpec(memory_space=pltpu.HBM)] * 3,
        2 * count * depth * 3 * width,
    )(in_hbm(segment_ids), in_hbm(rows), in_hbm(qkv_weight.T))
    got = exchanged(blocks, groups)
    got, texts = lax.optimization_barrier((got, all_texts(text_embed)))

    length = HEADS * count
    halo = 0
    operands = [segment_ids, got]
    if parts > 1:
        halo = rounded_up(MAXP - 1, LANES)
        part = lax.axis_index("grp") // HEADS
        whole_ids = jnp.concatenate(
            [
                jnp.full((1, halo), -1, jnp.int32),
                segment_ids,
                jnp.full((1, halo), images, jnp.int32),
            ],
            axis=1,
        )
        near_ids = lax.dynamic_slice_in_dim(whole_ids, part * length, length + 2 * halo, axis=1)
        flat = got[:, : 2 * size].transpose(1, 0, 2).reshape(2 * size, length)
        flat = jnp.concatenate([flat, jnp.zeros((16, length), bf16)], axis=0)
        ahead = [(i, i + HEADS) for i in range(group_size - HEADS)]
        back = [(i + HEADS, i) for i in range(group_size - HEADS)]
        left = moved(flat[:, length - halo :], "grp", ahead)
        right = moved(flat[:, :halo], "grp", back)
        operands = [near_ids, got, left, right]
    reach = length + 2 * halo
    window = min(rounded_up(MAXP + LANES - 1, LANES), reach)
    tile = 2 * LANES
    answers = call(
        functools.partial(attend_kernel, images, piggy, halo),
        shape((HEADS, padded, count), bf16),
        [
            pltpu.VMEM((reach, LANES), bf16),
            pltpu.VMEM((padded, reach), bf16),
            pltpu.VMEM((LANES, length), bf16),
            pltpu.VMEM((padded, length), f32),
            pltpu.VMEM((window, tile), f32),
            pltpu.VMEM((window, tile), f32),
            pltpu.VMEM((1, tile), f32),
            pltpu.VMEM((1, tile), f32),
            pltpu.SMEM((images,), jnp.int32),
        ],
        in_vmem(len(operands)),
        4 * size * length * MAXP,
    )(*operands)
    back_home = exchanged(answers, groups)

    joined = [pltpu.VMEM((HEADS * padded, count), bf16), pltpu.VMEM((HEADS * padded, depth), bf16)]
    flops = 2 * count * depth * width
    if piggy:
        mixed, row_loss = call(
            functools.partial(finish_kernel, images),
            (shape((count, depth), bf16), shape((1, images), f32)),
            joined + [pltpu.VMEM((SPARE, HEADS * padded), f32)],
            in_vmem(4),
            flops,
        )(rows, back_home, out_weight, texts)
        return (mixed[None], row_loss[0])
    mixed = call(mix_kernel, shape((count, depth), bf16), joined, in_vmem(3), flops)(
        rows, back_home, out_weight
    )
    own_ids = lax.dynamic_slice_in_dim(segment_ids[0], lax.axis_index("grp") * count, count)
    onehot = (own_ids[None, :] == jnp.arange(images, dtype=jnp.int32)[:, None]).astype(bf16)
    pooled = lax.psum(jnp.dot(onehot, mixed, preferred_element_type=f32), "grp")
    text_vecs = unit_rows(texts.astype(f32))
    cosine = jnp.dot(unit_rows(pooled), text_vecs.T, precision=lax.Precision.HIGHEST)
    same = jnp.arange(images)[:, None] == jnp.arange(texts.shape[0])[None, :]
    row_loss = jnp.sum(losses(cosine, jnp.where(same, 1.0, -1.0)), axis=1)
    return (mixed[None], row_loss)


def solution(mesh):
    placed = (P("blk", "grp", None), P("blk", None), P(), P(), P("blk", None))
    return jax.shard_map(
        local,
        mesh=mesh,
        in_specs=placed,
        out_specs=(P("blk", "grp", None), P("blk")),
        check_vma=False,
    )
```

```python
import functools
import math

import jax
import jax.numpy as jnp
from jax import lax
from jax.experimental import pallas as pl
from jax.experimental.pallas import tpu as pltpu
from jax.sharding import PartitionSpec as P

HEADS = 8
MAXP = 1024
LANES = 128
SPARE = 8
HIDDEN = -1e30

logit_scale = 30.0
logit_bias = -5.0

VMEM_LIMIT = 32 * 1024 * 1024


def rounded_up(value, step):
    return (value + step - 1) // step * step


def split_in_two(total, images):
    row = lax.broadcasted_iota(jnp.int32, total.shape, 0)
    main = total.astype(jnp.bfloat16).astype(jnp.float32)
    return jnp.where(row < images, main, total - main)


def image_rows(ids, images):
    row = lax.broadcasted_iota(jnp.int32, (SPARE, ids.shape[1]), 0)
    return (lax.rem(row, images) == ids).astype(jnp.float32).astype(jnp.bfloat16)


def head_blocks(query, key, value, sums, pair):
    size = query.shape[0] // 2
    count = query.shape[1]
    for place in range(2):
        here = slice(place * size, (place + 1) * size)
        if sums is None:
            spare = jnp.zeros((SPARE, count), jnp.float32)
        else:
            first = pl.multiple_of((2 * pair + place) * LANES, LANES)
            parts = [sums[:, pl.ds(first, LANES)], sums[:, HEADS * LANES :]]
            held = sum(part.shape[1] for part in parts)
            spare = jnp.concatenate(parts + [jnp.zeros((SPARE, count - held), jnp.float32)], axis=1)
        block = jnp.concatenate([value[here], key[here], spare, query[here]], axis=0)
        yield block.astype(jnp.bfloat16)


def store_by_core(core, blocks, same_ref, cross_ref):
    first, second = blocks

    @pl.when(core == 0)
    def _():
        same_ref[...] = first
        cross_ref[...] = second

    @pl.when(core == 1)
    def _():
        same_ref[...] = second
        cross_ref[...] = first


def place_in_group():
    own = lax.rem(lax.axis_index("grp"), HEADS)
    return lax.div(own, 2), lax.rem(own, 2)


def far_kernel(images, piggy, ids_ref, rows_ref, weight_ref, normed_ref, sums_ref, same_ref, cross_ref, own_ids, rows_held, weight, id_sem, row_sem, sems):
    count, depth = rows_ref.shape
    width = weight_ref.shape[0] // 3
    wide = weight.shape[1]
    rows_fetch = pltpu.make_async_copy(rows_ref, rows_held, row_sem)
    rows_fetch.start()
    own = pl.multiple_of(lax.axis_index("grp") * count, LANES)
    ids_fetch = pltpu.make_async_copy(ids_ref.at[:, pl.ds(own, count)], own_ids, id_sem)
    ids_fetch.start()
    pair, core = place_in_group()
    pair = jnp.bitwise_xor(pair, 3)
    fetches = []
    for at in range(3):
        first = pl.multiple_of(at * width + pair * wide, 16)
        fetches.append(pltpu.make_async_copy(weight_ref.at[pl.ds(first, wide)], weight.at[at], sems.at[at]))
    for fetch in fetches:
        fetch.start()
    rows_fetch.wait()
    rows = rows_held[...]
    values = rows.astype(jnp.float32)
    center = values - jnp.mean(values, axis=1, keepdims=True)
    spread = jnp.mean(center * center, axis=1, keepdims=True)
    normed = (center * lax.rsqrt(spread + 1e-06)).astype(jnp.bfloat16)
    normed_ref[...] = normed.T
    ids_fetch.wait()
    if piggy:
        sums = jnp.dot(image_rows(own_ids[...], images), rows, preferred_element_type=jnp.float32)
        sums_ref[...] = split_in_two(sums, images)
    for fetch in fetches:
        fetch.wait()
    parts = [
        jnp.dot(weight[at], normed_ref[...], preferred_element_type=jnp.float32) for at in range(3)
    ]
    store_by_core(core, head_blocks(*parts, sums_ref if piggy else None, pair), same_ref, cross_ref)


def near_kernel(piggy, normed_ref, sums_ref, weight_ref, *out_refs):
    width = weight_ref.shape[0] // 3
    wide = 2 * width // HEADS
    own, core = place_in_group()
    for step, move in enumerate((1, 2, 0)):
        pair = jnp.bitwise_xor(own, move)
        parts = []
        for at in range(3):
            here = pl.ds(pl.multiple_of(at * width + pair * wide, 16), wide)
            parts.append(
                jnp.dot(weight_ref[here, :], normed_ref[...], preferred_element_type=jnp.float32)
            )
        blocks = head_blocks(*parts, sums_ref if piggy else None, pair)
        store_by_core(core, blocks, *out_refs[2 * step : 2 * step + 2])


def attend_kernel(images, piggy, halo, ids_ref, *rest):
    got_refs, rest = rest[:HEADS], rest[HEADS:]
    if halo:
        left_ref, right_ref, *rest = rest
    out_ref, keys, values, queries, attended, scores_a, scores_b, tops_a, tops_b, marks, starts = rest
    count = got_refs[0].shape[1]
    padded = attended.shape[0]
    size = padded - SPARE
    total_rows = HEADS * count
    length = ids_ref.shape[1]
    window = scores_a.shape[0]
    tile = scores_a.shape[1]
    tiles = total_rows // tile
    bits = max(1, (images - 1).bit_length())
    ids = ids_ref[...]
    for image in range(images):
        starts[image] = jnp.sum((ids < image).astype(jnp.int32))

    row = lax.broadcasted_iota(jnp.int32, (SPARE, length), 0)
    bit = jnp.bitwise_and(lax.shift_right_logical(jnp.broadcast_to(ids, row.shape), row >> 1), 1)
    odd = jnp.bitwise_and(row, 1)
    used = row < 2 * bits
    outside = jnp.logical_or(ids < 0, ids >= images)
    key_side = jnp.where(odd == 1, bit, 1 - bit).astype(jnp.float32)
    key_side = jnp.where(outside, 1.0, key_side)
    key_marks, query_marks = marks.at[0], marks.at[1]
    key_marks[...] = jnp.where(used, key_side * HIDDEN, 0.0)
    query_marks[...] = jnp.where(used, jnp.where(odd == 1, 1 - bit, bit), 0).astype(jnp.float32)

    key_at = size - SPARE
    query_at = 2 * size
    own = lax.rem(lax.axis_index("grp"), HEADS)
    blank = jnp.zeros((LANES - padded, count), jnp.bfloat16)

    def store_keys(here, ref):
        block = ref[key_at : key_at + padded].astype(jnp.float32)
        nothing = jnp.zeros((LANES - padded, block.shape[1]), jnp.float32)
        full = jnp.concatenate([key_marks[:, here], block[SPARE:], nothing], axis=0)
        keys[here, :] = full.T.astype(jnp.bfloat16)
        values[:, here] = ref[0:padded]

    for step, ref in enumerate(got_refs):
        first = jnp.bitwise_xor(own, step) * count
        here = pl.ds(pl.multiple_of(halo + first, LANES), count)
        there = pl.ds(pl.multiple_of(first, LANES), count)
        store_keys(here, ref)
        edge = ref[query_at : query_at + 16].astype(jnp.float32)
        edge = jnp.concatenate([query_marks[:, here], edge[SPARE:]], axis=0)
        queries[0:16, there] = edge.astype(jnp.bfloat16)
        queries[16:padded, there] = ref[query_at + 16 : query_at + padded]
        queries[padded:, there] = blank
    if halo:
        store_keys(slice(0, halo), left_ref)
        store_keys(slice(length - halo, length), right_ref)

    def image_at(position):
        found = jnp.int32(0)
        for image in range(1, images):
            found += (starts[image] <= position).astype(jnp.int32)
        return found

    def following(state):
        at, image = state
        more = image < image_at(halo + at * tile + tile - 1)
        later = jnp.minimum(at + 1, tiles - 1)
        first = jnp.maximum(image_at(halo + later * tile), jnp.where(later == at, image, 0))
        return jnp.where(more, at, later), jnp.where(more, image + 1, first)

    def window_of(image):
        begin = jnp.minimum(starts[image] // LANES * LANES, length - window)
        return pl.ds(pl.multiple_of(begin, LANES), window)

    def score(state, scores, tops):
        at, image = state
        query = queries[:, pl.ds(pl.multiple_of(at * tile, tile), tile)]
        found = jnp.dot(keys[window_of(image), :], query, preferred_element_type=jnp.float32)
        scores[...] = found
        tops[...] = jnp.max(found, axis=0, keepdims=True)

    def weigh(state, scores, tops):
        at, image = state
        first = pl.multiple_of(at * tile, tile)
        labels = ids_ref[:, pl.ds(pl.multiple_of(halo + first, LANES), tile)]
        probs = jnp.exp2((scores[...] - tops[...]) * (size ** (-0.5) * math.log2(math.e)))
        total = jnp.sum(probs, axis=0, keepdims=True)
        weighted = jnp.dot(
            values[:, window_of(image)], probs.astype(jnp.bfloat16), preferred_element_type=jnp.float32
        )
        place = (slice(None), pl.ds(first, tile))
        attended[place] = jnp.where(labels == image, weighted / total, attended[place])

    pairs = jnp.int32(tiles)
    for image in range(1, images):
        offset = starts[image] - halo
        inside = jnp.logical_and(offset > 0, offset < total_rows)
        pairs += jnp.logical_and(inside, lax.rem(offset, tile) != 0).astype(jnp.int32)

    def two_pairs(_, state):
        second = following(state)
        score(second, scores_b, tops_b)
        weigh(state, scores_a, tops_a)
        third = following(second)
        score(third, scores_a, tops_a)
        weigh(second, scores_b, tops_b)
        return third

    begun = (jnp.int32(0), image_at(halo))
    score(begun, scores_a, tops_a)
    lax.fori_loop(0, (pairs + 1) // 2, two_pairs, begun)

    odd_head = lax.rem(lax.axis_index("grp"), 2) == 1
    mine = ids[:, halo : halo + total_rows]

    def placed(block, spare):
        even = jnp.concatenate([block[0:size], spare], axis=0)
        odd = jnp.concatenate([spare, block[0:size]], axis=0)
        return jnp.where(odd_head, odd, even)

    if piggy:
        nothing = jnp.zeros((SPARE, total_rows), jnp.float32)
        flat = placed(attended[...], nothing).astype(jnp.bfloat16)
        pooled = lax.dot_general(
            image_rows(mine, images), flat, (((1,), (1,)), ((), ())), preferred_element_type=jnp.float32
        )
        pooled = split_in_two(pooled, images)
        sums = jnp.zeros((SPARE, 2 * LANES), jnp.float32)
        for ref in got_refs:
            sums += ref[query_at : query_at + 16].astype(jnp.float32)[0:SPARE, 0 : 2 * LANES]
        sums = split_in_two(sums + pltpu.roll(sums, images, axis=0), images)
        spare = jnp.concatenate(
            [pooled, jnp.zeros((SPARE, LANES - padded), jnp.float32), sums], axis=1
        )
    else:
        spare = jnp.zeros((SPARE, count), jnp.float32)
    for source in range(HEADS):
        block = placed(attended[:, source * count : (source + 1) * count], spare)
        out_ref[source] = block.astype(jnp.bfloat16)


def joined_heads(got_ref, out_weight_ref, flat, weight):
    padded = got_ref.shape[1]
    size = padded - SPARE
    spares = []
    for head in range(HEADS):
        at = head * padded
        from_row = head * size - (SPARE if head % 2 else 0)
        weight[at : at + padded] = out_weight_ref[from_row : from_row + padded]
        edge = 0 if head % 2 else padded - 16
        rest = slice(16, padded) if head % 2 else slice(0, padded - 16)
        mixed_rows = got_ref[head, edge : edge + 16].astype(jnp.float32)
        nothing = jnp.zeros((SPARE, mixed_rows.shape[1]), jnp.float32)
        if head % 2:
            spares.append(mixed_rows[:SPARE])
            block = jnp.concatenate([nothing, mixed_rows[SPARE:]], axis=0)
        else:
            spares.append(mixed_rows[SPARE:])
            block = jnp.concatenate([mixed_rows[:SPARE], nothing], axis=0)
        flat[at + edge : at + edge + 16] = block.astype(jnp.bfloat16)
        flat[at + rest.start : at + rest.stop] = got_ref[head, rest]
    return spares


def mixed_rows_of(rows_ref, flat, weight):
    added = lax.dot_general(
        flat[...], weight[...], (((0,), (0,)), ((), ())), preferred_element_type=jnp.float32
    )
    return (rows_ref[...].astype(jnp.float32) + added).astype(jnp.bfloat16)


def unit_rows(matrix):
    return matrix * lax.rsqrt(jnp.sum(matrix * matrix, axis=1, keepdims=True) + 1e-06)


def losses(cosine, labels):
    logits = -labels * (logit_scale * cosine + logit_bias)
    return jnp.maximum(logits, 0.0) + jnp.log1p(jnp.exp(-jnp.abs(logits)))


def finish_kernel(images, rows_ref, got_ref, out_weight_ref, text_ref, mixed_ref, loss_ref, flat, weight, pooled_heads):
    padded = got_ref.shape[1]
    spares = joined_heads(got_ref, out_weight_ref, flat, weight)
    for head in range(HEADS):
        pooled_heads[:, head * padded : (head + 1) * padded] = spares[head][:, 0:padded]
    pooled = jnp.dot(
        pooled_heads[...].astype(jnp.bfloat16), weight[...], preferred_element_type=jnp.float32
    )
    patch_sums = [spare[:, LANES : 2 * LANES] for spare in spares] + [spares[0][:, 2 * LANES :]]
    pooled = pooled + jnp.concatenate(patch_sums, axis=1)
    pooled = pooled + pltpu.roll(pooled, images, axis=0)
    image_vecs = unit_rows(pooled)
    text_vecs = unit_rows(text_ref[...].astype(jnp.float32))
    cosine = lax.dot_general(
        text_vecs,
        image_vecs,
        (((1,), (1,)), ((), ())),
        precision=lax.Precision.HIGHEST,
        preferred_element_type=jnp.float32,
    )
    text = lax.broadcasted_iota(jnp.int32, cosine.shape, 0)
    image = lax.broadcasted_iota(jnp.int32, cosine.shape, 1)
    terms = losses(cosine, jnp.where(text == image, 1.0, -1.0))
    loss_ref[...] = jnp.sum(terms, axis=0, keepdims=True)[:, 0:images]
    mixed_ref[...] = mixed_rows_of(rows_ref, flat, weight)


def mix_kernel(rows_ref, got_ref, out_weight_ref, mixed_ref, flat, weight):
    joined_heads(got_ref, out_weight_ref, flat, weight)
    mixed_ref[...] = mixed_rows_of(rows_ref, flat, weight)


def in_vmem(count):
    return [pl.BlockSpec(memory_space=pltpu.VMEM)] * count


def in_hbm(value):
    return pltpu.with_memory_space_constraint(value, pltpu.HBM)


def call(kernel, out_shape, scratch, in_specs, flops):
    out_specs = jax.tree.map(lambda _: pl.BlockSpec(memory_space=pltpu.VMEM), out_shape)
    return pl.pallas_call(
        kernel,
        out_shape=out_shape,
        in_specs=in_specs,
        out_specs=out_specs,
        scratch_shapes=scratch,
        compiler_params=pltpu.CompilerParams(vmem_limit_bytes=VMEM_LIMIT),
        cost_estimate=pl.CostEstimate(flops=flops, bytes_accessed=8 << 20, transcendentals=0),
    )


def moved(value, axis, pairs):
    return lax.ppermute(value, axis, pairs)


def all_texts(texts):
    peers = lax.axis_size("blk")
    if peers & (peers - 1):
        shifts = range(1, peers)
        others = [moved(texts, "blk", [(i, (i + by) % peers) for i in range(peers)]) for by in shifts]
        return jnp.concatenate([texts] + others, axis=0)
    by = 1
    while by < peers:
        other = moved(texts, "blk", [(i, i ^ by) for i in range(peers)])
        texts = jnp.concatenate([texts, other], axis=0)
        by *= 2
    return texts


def exchanged(blocks, groups):
    return lax.all_to_all(blocks, "grp", 0, 0, axis_index_groups=groups, tiled=True)


def local(patches, segment_ids, qkv_weight, out_weight, text_embed):
    rows = patches[0]
    count, depth = rows.shape
    width = out_weight.shape[0]
    size = width // HEADS
    padded = size + SPARE
    images = text_embed.shape[0]
    group_size = lax.axis_size("grp")
    parts = group_size // HEADS
    piggy = parts == 1 and 2 * images == SPARE and count >= depth - (HEADS - 2) * LANES
    groups = None if parts == 1 else [list(range(p * HEADS, (p + 1) * HEADS)) for p in range(parts)]
    bf16, f32 = jnp.bfloat16, jnp.float32
    shape = jax.ShapeDtypeStruct

    block = shape((3 * size + SPARE, count), bf16)
    hbm = pl.BlockSpec(memory_space=pltpu.HBM)
    turned_weight = qkv_weight.T
    normed, sums, *sent = call(
        functools.partial(far_kernel, images, piggy),
        (shape((depth, count), bf16), shape((SPARE, depth), f32), block, block),
        [
            pltpu.VMEM((1, count), jnp.int32),
            pltpu.VMEM((count, depth), bf16),
            pltpu.VMEM((3, 2 * size, depth), bf16),
            pltpu.SemaphoreType.DMA,
            pltpu.SemaphoreType.DMA,
            pltpu.SemaphoreType.DMA((3,)),
        ],
        [hbm] * 3,
        2 * count * depth * 6 * size,
    )(in_hbm(segment_ids), in_hbm(rows), in_hbm(turned_weight))
    sent += call(
        functools.partial(near_kernel, piggy),
        (block,) * 6,
        [],
        in_vmem(3),
        2 * count * depth * 18 * size,
    )(normed, sums, turned_weight)
    got = [None] * HEADS
    for value, by in zip(sent, (6, 7, 2, 3, 4, 5, 0, 1)):
        pairs = [(i, i ^ by) for i in range(group_size)]
        got[by] = moved(value, "grp", pairs) if by else value
    got, texts = lax.optimization_barrier((got, all_texts(text_embed)))

    length = HEADS * count
    halo = 0
    operands = [segment_ids, *got]
    if parts > 1:
        halo = rounded_up(MAXP - 1, LANES)
        part = lax.axis_index("grp") // HEADS
        whole_ids = jnp.concatenate(
            [
                jnp.full((1, halo), -1, jnp.int32),
                segment_ids,
                jnp.full((1, halo), images, jnp.int32),
            ],
            axis=1,
        )
        near_ids = lax.dynamic_slice_in_dim(whole_ids, part * length, length + 2 * halo, axis=1)
        order = jnp.bitwise_xor(lax.axis_index("grp") % HEADS, jnp.arange(HEADS))
        flat = jnp.stack(got)[order][:, : 2 * size].transpose(1, 0, 2).reshape(2 * size, length)
        flat = jnp.concatenate([flat, jnp.zeros((16, length), bf16)], axis=0)
        ahead = [(i, i + HEADS) for i in range(group_size - HEADS)]
        back = [(i + HEADS, i) for i in range(group_size - HEADS)]
        left = moved(flat[:, length - halo :], "grp", ahead)
        right = moved(flat[:, :halo], "grp", back)
        operands = [near_ids, *got, left, right]
    reach = length + 2 * halo
    window = min(rounded_up(MAXP + LANES - 1, LANES), reach)
    tile = 2 * LANES
    answers = call(
        functools.partial(attend_kernel, images, piggy, halo),
        shape((HEADS, padded, count), bf16),
        [
            pltpu.VMEM((reach, LANES), bf16),
            pltpu.VMEM((padded, reach), bf16),
            pltpu.VMEM((LANES, length), bf16),
            pltpu.VMEM((padded, length), f32),
            pltpu.VMEM((window, tile), f32),
            pltpu.VMEM((window, tile), f32),
            pltpu.VMEM((1, tile), f32),
            pltpu.VMEM((1, tile), f32),
            pltpu.VMEM((2, SPARE, reach), f32),
            pltpu.SMEM((images,), jnp.int32),
        ],
        in_vmem(len(operands)),
        4 * size * length * MAXP,
    )(*operands)
    back_home = exchanged(answers, groups)

    joined = [pltpu.VMEM((HEADS * padded, count), bf16), pltpu.VMEM((HEADS * padded, depth), bf16)]
    flops = 2 * count * depth * width
    if piggy:
        mixed, row_loss = call(
            functools.partial(finish_kernel, images),
            (shape((count, depth), bf16), shape((1, images), f32)),
            joined + [pltpu.VMEM((SPARE, HEADS * padded), f32)],
            in_vmem(4),
            flops,
        )(rows, back_home, out_weight, texts)
        return (mixed[None], row_loss[0])
    mixed = call(mix_kernel, shape((count, depth), bf16), joined, in_vmem(3), flops)(
        rows, back_home, out_weight
    )
    own_ids = lax.dynamic_slice_in_dim(segment_ids[0], lax.axis_index("grp") * count, count)
    onehot = (own_ids[None, :] == jnp.arange(images, dtype=jnp.int32)[:, None]).astype(bf16)
    pooled = lax.psum(jnp.dot(onehot, mixed, preferred_element_type=f32), "grp")
    text_vecs = unit_rows(texts.astype(f32))
    cosine = jnp.dot(unit_rows(pooled), text_vecs.T, precision=lax.Precision.HIGHEST)
    same = jnp.arange(images)[:, None] == jnp.arange(texts.shape[0])[None, :]
    row_loss = jnp.sum(losses(cosine, jnp.where(same, 1.0, -1.0)), axis=1)
    return (mixed[None], row_loss)


def solution(mesh):
    placed = (P("blk", "grp", None), P("blk", None), P(), P(), P("blk", None))
    return jax.shard_map(
        local,
        mesh=mesh,
        in_specs=placed,
        out_specs=(P("blk", "grp", None), P("blk")),
        check_vma=False,
    )
```

```python
import functools
import math

import jax
import jax.numpy as jnp
from jax import lax
from jax.experimental import pallas as pl
from jax.experimental.pallas import tpu as pltpu
from jax.sharding import PartitionSpec as P

HEADS = 8
MAXP = 1024
LANES = 128
SPARE = 8
HIDDEN = -1e30
ORDER = (6, 7, 2, 4, 3, 5, 1, 0)

logit_scale = 30.0
logit_bias = -5.0

VMEM_LIMIT = 32 * 1024 * 1024


def rounded_up(value, step):
    return (value + step - 1) // step * step


def split_in_two(total, images):
    row = lax.broadcasted_iota(jnp.int32, total.shape, 0)
    main = total.astype(jnp.bfloat16).astype(jnp.float32)
    return jnp.where(row < images, main, total - main)


def image_rows(ids, images):
    row = lax.broadcasted_iota(jnp.int32, (SPARE, ids.shape[1]), 0)
    return (lax.rem(row, images) == ids).astype(jnp.float32).astype(jnp.bfloat16)


def head_blocks(query, key, value, sums, pair):
    size = query.shape[0] // 2
    count = query.shape[1]
    for place in range(2):
        here = slice(place * size, (place + 1) * size)
        if sums is None:
            spare = jnp.zeros((SPARE, count), jnp.float32)
        else:
            first = pl.multiple_of((2 * pair + place) * LANES, LANES)
            parts = [sums[:, pl.ds(first, LANES)], sums[:, HEADS * LANES :]]
            held = sum(part.shape[1] for part in parts)
            spare = jnp.concatenate(parts + [jnp.zeros((SPARE, count - held), jnp.float32)], axis=1)
        block = jnp.concatenate([value[here], key[here], spare, query[here]], axis=0)
        yield block.astype(jnp.bfloat16)


def store_by_core(core, blocks, same_ref, cross_ref):
    first, second = blocks

    @pl.when(core == 0)
    def _():
        same_ref[...] = first
        cross_ref[...] = second

    @pl.when(core == 1)
    def _():
        same_ref[...] = second
        cross_ref[...] = first


def place_in_group():
    own = lax.rem(lax.axis_index("grp"), HEADS)
    return lax.div(own, 2), lax.rem(own, 2)


def far_kernel(images, piggy, ids_ref, rows_ref, weight_ref, normed_ref, sums_ref, same_ref, cross_ref, own_ids, rows_held, weight, id_sem, row_sem, sems):
    count, depth = rows_ref.shape
    width = weight_ref.shape[0] // 3
    wide = weight.shape[1]
    rows_fetch = pltpu.make_async_copy(rows_ref, rows_held, row_sem)
    rows_fetch.start()
    own = pl.multiple_of(lax.axis_index("grp") * count, LANES)
    ids_fetch = pltpu.make_async_copy(ids_ref.at[:, pl.ds(own, count)], own_ids, id_sem)
    ids_fetch.start()
    pair, core = place_in_group()
    pair = jnp.bitwise_xor(pair, 3)
    fetches = []
    for at in range(3):
        first = pl.multiple_of(at * width + pair * wide, 16)
        fetches.append(pltpu.make_async_copy(weight_ref.at[pl.ds(first, wide)], weight.at[at], sems.at[at]))
    for fetch in fetches:
        fetch.start()
    rows_fetch.wait()
    rows = rows_held[...]
    values = rows.astype(jnp.float32)
    center = values - jnp.mean(values, axis=1, keepdims=True)
    spread = jnp.mean(center * center, axis=1, keepdims=True)
    normed = (center * lax.rsqrt(spread + 1e-06)).astype(jnp.bfloat16)
    normed_ref[...] = normed.T
    ids_fetch.wait()
    if piggy:
        sums = jnp.dot(image_rows(own_ids[...], images), rows, preferred_element_type=jnp.float32)
        sums_ref[...] = split_in_two(sums, images)
    for fetch in fetches:
        fetch.wait()
    parts = [
        jnp.dot(weight[at], normed_ref[...], preferred_element_type=jnp.float32) for at in range(3)
    ]
    store_by_core(core, head_blocks(*parts, sums_ref if piggy else None, pair), same_ref, cross_ref)


def near_kernel(piggy, normed_ref, sums_ref, weight_ref, *out_refs):
    width = weight_ref.shape[0] // 3
    wide = 2 * width // HEADS
    own, core = place_in_group()
    for step, move in enumerate((1, 2, 0)):
        pair = jnp.bitwise_xor(own, move)
        parts = []
        for at in range(3):
            here = pl.ds(pl.multiple_of(at * width + pair * wide, 16), wide)
            parts.append(
                jnp.dot(weight_ref[here, :], normed_ref[...], preferred_element_type=jnp.float32)
            )
        blocks = head_blocks(*parts, sums_ref if piggy else None, pair)
        store_by_core(core, blocks, *out_refs[2 * step : 2 * step + 2])


def attend_kernel(images, piggy, halo, ids_ref, *rest):
    got_refs, rest = rest[:HEADS], rest[HEADS:]
    if halo:
        left_ref, right_ref, *rest = rest
    out_ref, keys, values, queries, attended, scores_a, scores_b, tops_a, tops_b, marks, starts = rest
    count = got_refs[0].shape[1]
    padded = attended.shape[0]
    size = padded - SPARE
    total_rows = HEADS * count
    length = ids_ref.shape[1]
    window = scores_a.shape[0]
    tile = scores_a.shape[1]
    tiles = total_rows // tile
    bits = max(1, (images - 1).bit_length())
    ids = ids_ref[...]
    for image in range(images):
        starts[image] = jnp.sum((ids < image).astype(jnp.int32))

    row = lax.broadcasted_iota(jnp.int32, (SPARE, length), 0)
    bit = jnp.bitwise_and(lax.shift_right_logical(jnp.broadcast_to(ids, row.shape), row >> 1), 1)
    odd = jnp.bitwise_and(row, 1)
    used = row < 2 * bits
    outside = jnp.logical_or(ids < 0, ids >= images)
    key_side = jnp.where(odd == 1, bit, 1 - bit).astype(jnp.float32)
    key_side = jnp.where(outside, 1.0, key_side)
    key_marks, query_marks = marks.at[0], marks.at[1]
    key_marks[...] = jnp.where(used, key_side * HIDDEN, 0.0)
    query_marks[...] = jnp.where(used, jnp.where(odd == 1, 1 - bit, bit), 0).astype(jnp.float32)

    key_at = size - SPARE
    query_at = 2 * size
    own = lax.rem(lax.axis_index("grp"), HEADS)
    blank = jnp.zeros((LANES - padded, count), jnp.bfloat16)

    def store_keys(here, ref):
        block = ref[key_at : key_at + padded].astype(jnp.float32)
        nothing = jnp.zeros((LANES - padded, block.shape[1]), jnp.float32)
        full = jnp.concatenate([key_marks[:, here], block[SPARE:], nothing], axis=0)
        keys[here, :] = full.T.astype(jnp.bfloat16)
        values[:, here] = ref[0:padded]

    for by, ref in zip(ORDER, got_refs):
        first = jnp.bitwise_xor(own, by) * count
        here = pl.ds(pl.multiple_of(halo + first, LANES), count)
        there = pl.ds(pl.multiple_of(first, LANES), count)
        store_keys(here, ref)
        edge = ref[query_at : query_at + 16].astype(jnp.float32)
        edge = jnp.concatenate([query_marks[:, here], edge[SPARE:]], axis=0)
        queries[0:16, there] = edge.astype(jnp.bfloat16)
        queries[16:padded, there] = ref[query_at + 16 : query_at + padded]
        queries[padded:, there] = blank
    if halo:
        store_keys(slice(0, halo), left_ref)
        store_keys(slice(length - halo, length), right_ref)

    def image_at(position):
        found = jnp.int32(0)
        for image in range(1, images):
            found += (starts[image] <= position).astype(jnp.int32)
        return found

    def following(state):
        at, image = state
        more = image < image_at(halo + at * tile + tile - 1)
        later = jnp.minimum(at + 1, tiles - 1)
        first = jnp.maximum(image_at(halo + later * tile), jnp.where(later == at, image, 0))
        return jnp.where(more, at, later), jnp.where(more, image + 1, first)

    def window_of(image):
        begin = jnp.minimum(starts[image] // LANES * LANES, length - window)
        return pl.ds(pl.multiple_of(begin, LANES), window)

    def score(state, scores, tops):
        at, image = state
        query = queries[:, pl.ds(pl.multiple_of(at * tile, tile), tile)]
        found = jnp.dot(keys[window_of(image), :], query, preferred_element_type=jnp.float32)
        scores[...] = found
        tops[...] = jnp.max(found, axis=0, keepdims=True)

    def weigh(state, scores, tops):
        at, image = state
        first = pl.multiple_of(at * tile, tile)
        labels = ids_ref[:, pl.ds(pl.multiple_of(halo + first, LANES), tile)]
        probs = jnp.exp2((scores[...] - tops[...]) * (size ** (-0.5) * math.log2(math.e)))
        total = jnp.sum(probs, axis=0, keepdims=True)
        weighted = jnp.dot(
            values[:, window_of(image)], probs.astype(jnp.bfloat16), preferred_element_type=jnp.float32
        )
        place = (slice(None), pl.ds(first, tile))
        attended[place] = jnp.where(labels == image, weighted / total, attended[place])

    pairs = jnp.int32(tiles)
    for image in range(1, images):
        offset = starts[image] - halo
        inside = jnp.logical_and(offset > 0, offset < total_rows)
        pairs += jnp.logical_and(inside, lax.rem(offset, tile) != 0).astype(jnp.int32)

    def two_pairs(_, state):
        second = following(state)
        score(second, scores_b, tops_b)
        weigh(state, scores_a, tops_a)
        third = following(second)
        score(third, scores_a, tops_a)
        weigh(second, scores_b, tops_b)
        return third

    begun = (jnp.int32(0), image_at(halo))
    score(begun, scores_a, tops_a)
    lax.fori_loop(0, (pairs + 1) // 2, two_pairs, begun)

    odd_head = lax.rem(lax.axis_index("grp"), 2) == 1
    mine = ids[:, halo : halo + total_rows]

    def placed(block, spare):
        even = jnp.concatenate([block[0:size], spare], axis=0)
        odd = jnp.concatenate([spare, block[0:size]], axis=0)
        return jnp.where(odd_head, odd, even)

    if piggy:
        nothing = jnp.zeros((SPARE, total_rows), jnp.float32)
        flat = placed(attended[...], nothing).astype(jnp.bfloat16)
        pooled = lax.dot_general(
            image_rows(mine, images), flat, (((1,), (1,)), ((), ())), preferred_element_type=jnp.float32
        )
        pooled = split_in_two(pooled, images)
        sums = jnp.zeros((SPARE, 2 * LANES), jnp.float32)
        for ref in got_refs:
            sums += ref[query_at : query_at + 16].astype(jnp.float32)[0:SPARE, 0 : 2 * LANES]
        sums = split_in_two(sums + pltpu.roll(sums, images, axis=0), images)
        spare = jnp.concatenate(
            [pooled, jnp.zeros((SPARE, LANES - padded), jnp.float32), sums], axis=1
        )
    else:
        spare = jnp.zeros((SPARE, count), jnp.float32)
    for source in range(HEADS):
        block = placed(attended[:, source * count : (source + 1) * count], spare)
        out_ref[source] = block.astype(jnp.bfloat16)


def joined_heads(got_ref, out_weight_ref, flat, weight):
    padded = got_ref.shape[1]
    size = padded - SPARE
    spares = []
    for head in range(HEADS):
        at = head * padded
        from_row = head * size - (SPARE if head % 2 else 0)
        weight[at : at + padded] = out_weight_ref[from_row : from_row + padded]
        edge = 0 if head % 2 else padded - 16
        rest = slice(16, padded) if head % 2 else slice(0, padded - 16)
        mixed_rows = got_ref[head, edge : edge + 16].astype(jnp.float32)
        nothing = jnp.zeros((SPARE, mixed_rows.shape[1]), jnp.float32)
        if head % 2:
            spares.append(mixed_rows[:SPARE])
            block = jnp.concatenate([nothing, mixed_rows[SPARE:]], axis=0)
        else:
            spares.append(mixed_rows[SPARE:])
            block = jnp.concatenate([mixed_rows[:SPARE], nothing], axis=0)
        flat[at + edge : at + edge + 16] = block.astype(jnp.bfloat16)
        flat[at + rest.start : at + rest.stop] = got_ref[head, rest]
    return spares


def mixed_rows_of(rows_ref, flat, weight):
    added = lax.dot_general(
        flat[...], weight[...], (((0,), (0,)), ((), ())), preferred_element_type=jnp.float32
    )
    return (rows_ref[...].astype(jnp.float32) + added).astype(jnp.bfloat16)


def unit_rows(matrix):
    return matrix * lax.rsqrt(jnp.sum(matrix * matrix, axis=1, keepdims=True) + 1e-06)


def losses(cosine, labels):
    logits = -labels * (logit_scale * cosine + logit_bias)
    return jnp.maximum(logits, 0.0) + jnp.log1p(jnp.exp(-jnp.abs(logits)))


def finish_kernel(images, rows_ref, got_ref, out_weight_ref, text_ref, mixed_ref, loss_ref, flat, weight, pooled_heads):
    padded = got_ref.shape[1]
    spares = joined_heads(got_ref, out_weight_ref, flat, weight)
    for head in range(HEADS):
        pooled_heads[:, head * padded : (head + 1) * padded] = spares[head][:, 0:padded]
    pooled = jnp.dot(
        pooled_heads[...].astype(jnp.bfloat16), weight[...], preferred_element_type=jnp.float32
    )
    patch_sums = [spare[:, LANES : 2 * LANES] for spare in spares] + [spares[0][:, 2 * LANES :]]
    pooled = pooled + jnp.concatenate(patch_sums, axis=1)
    pooled = pooled + pltpu.roll(pooled, images, axis=0)
    image_vecs = unit_rows(pooled)
    text_vecs = unit_rows(text_ref[...].astype(jnp.float32))
    cosine = lax.dot_general(
        text_vecs,
        image_vecs,
        (((1,), (1,)), ((), ())),
        precision=lax.Precision.HIGHEST,
        preferred_element_type=jnp.float32,
    )
    text = lax.broadcasted_iota(jnp.int32, cosine.shape, 0)
    image = lax.broadcasted_iota(jnp.int32, cosine.shape, 1)
    terms = losses(cosine, jnp.where(text == image, 1.0, -1.0))
    loss_ref[...] = jnp.sum(terms, axis=0, keepdims=True)[:, 0:images]
    mixed_ref[...] = mixed_rows_of(rows_ref, flat, weight)


def mix_kernel(rows_ref, got_ref, out_weight_ref, mixed_ref, flat, weight):
    joined_heads(got_ref, out_weight_ref, flat, weight)
    mixed_ref[...] = mixed_rows_of(rows_ref, flat, weight)


def in_vmem(count):
    return [pl.BlockSpec(memory_space=pltpu.VMEM)] * count


def in_hbm(value):
    return pltpu.with_memory_space_constraint(value, pltpu.HBM)


def call(kernel, out_shape, scratch, in_specs, flops):
    out_specs = jax.tree.map(lambda _: pl.BlockSpec(memory_space=pltpu.VMEM), out_shape)
    return pl.pallas_call(
        kernel,
        out_shape=out_shape,
        in_specs=in_specs,
        out_specs=out_specs,
        scratch_shapes=scratch,
        compiler_params=pltpu.CompilerParams(vmem_limit_bytes=VMEM_LIMIT),
        cost_estimate=pl.CostEstimate(flops=flops, bytes_accessed=8 << 20, transcendentals=0),
    )


def moved(value, axis, pairs):
    return lax.ppermute(value, axis, pairs)


def all_texts(texts):
    peers = lax.axis_size("blk")
    if peers & (peers - 1):
        shifts = range(1, peers)
        others = [moved(texts, "blk", [(i, (i + by) % peers) for i in range(peers)]) for by in shifts]
        return jnp.concatenate([texts] + others, axis=0)
    by = 1
    while by < peers:
        other = moved(texts, "blk", [(i, i ^ by) for i in range(peers)])
        texts = jnp.concatenate([texts, other], axis=0)
        by *= 2
    return texts


def exchanged(blocks, groups):
    return lax.all_to_all(blocks, "grp", 0, 0, axis_index_groups=groups, tiled=True)


def local(patches, segment_ids, qkv_weight, out_weight, text_embed):
    rows = patches[0]
    count, depth = rows.shape
    width = out_weight.shape[0]
    size = width // HEADS
    padded = size + SPARE
    images = text_embed.shape[0]
    group_size = lax.axis_size("grp")
    parts = group_size // HEADS
    piggy = parts == 1 and 2 * images == SPARE and count >= depth - (HEADS - 2) * LANES
    groups = None if parts == 1 else [list(range(p * HEADS, (p + 1) * HEADS)) for p in range(parts)]
    bf16, f32 = jnp.bfloat16, jnp.float32
    shape = jax.ShapeDtypeStruct

    block = shape((3 * size + SPARE, count), bf16)
    hbm = pl.BlockSpec(memory_space=pltpu.HBM)
    turned_weight = qkv_weight.T
    normed, sums, *sent = call(
        functools.partial(far_kernel, images, piggy),
        (shape((depth, count), bf16), shape((SPARE, depth), f32), block, block),
        [
            pltpu.VMEM((1, count), jnp.int32),
            pltpu.VMEM((count, depth), bf16),
            pltpu.VMEM((3, 2 * size, depth), bf16),
            pltpu.SemaphoreType.DMA,
            pltpu.SemaphoreType.DMA,
            pltpu.SemaphoreType.DMA((3,)),
        ],
        [hbm] * 3,
        2 * count * depth * 6 * size,
    )(in_hbm(segment_ids), in_hbm(rows), in_hbm(turned_weight))
    sent += call(
        functools.partial(near_kernel, piggy),
        (block,) * 6,
        [],
        in_vmem(3),
        2 * count * depth * 18 * size,
    )(normed, sums, turned_weight)
    sent = dict(zip((6, 7, 2, 3, 4, 5, 0, 1), sent))
    got = []
    for by in ORDER:
        pairs = [(i, i ^ by) for i in range(group_size)]
        got.append(moved(sent[by], "grp", pairs) if by else sent[by])
    text_embed, got[0] = lax.optimization_barrier((text_embed, got[0]))
    got, texts = lax.optimization_barrier((got, all_texts(text_embed)))

    length = HEADS * count
    halo = 0
    operands = [segment_ids, *got]
    if parts > 1:
        halo = rounded_up(MAXP - 1, LANES)
        part = lax.axis_index("grp") // HEADS
        whole_ids = jnp.concatenate(
            [
                jnp.full((1, halo), -1, jnp.int32),
                segment_ids,
                jnp.full((1, halo), images, jnp.int32),
            ],
            axis=1,
        )
        near_ids = lax.dynamic_slice_in_dim(whole_ids, part * length, length + 2 * halo, axis=1)
        order = jnp.bitwise_xor(lax.axis_index("grp") % HEADS, jnp.arange(HEADS))
        flat = jnp.stack([got[ORDER.index(by)] for by in range(HEADS)])[order][:, : 2 * size].transpose(1, 0, 2).reshape(2 * size, length)
        flat = jnp.concatenate([flat, jnp.zeros((16, length), bf16)], axis=0)
        ahead = [(i, i + HEADS) for i in range(group_size - HEADS)]
        back = [(i + HEADS, i) for i in range(group_size - HEADS)]
        left = moved(flat[:, length - halo :], "grp", ahead)
        right = moved(flat[:, :halo], "grp", back)
        operands = [near_ids, *got, left, right]
    reach = length + 2 * halo
    window = min(rounded_up(MAXP + LANES - 1, LANES), reach)
    tile = 2 * LANES
    answers = call(
        functools.partial(attend_kernel, images, piggy, halo),
        shape((HEADS, padded, count), bf16),
        [
            pltpu.VMEM((reach, LANES), bf16),
            pltpu.VMEM((padded, reach), bf16),
            pltpu.VMEM((LANES, length), bf16),
            pltpu.VMEM((padded, length), f32),
            pltpu.VMEM((window, tile), f32),
            pltpu.VMEM((window, tile), f32),
            pltpu.VMEM((1, tile), f32),
            pltpu.VMEM((1, tile), f32),
            pltpu.VMEM((2, SPARE, reach), f32),
            pltpu.SMEM((images,), jnp.int32),
        ],
        in_vmem(len(operands)),
        4 * size * length * MAXP,
    )(*operands)
    back_home = exchanged(answers, groups)

    joined = [pltpu.VMEM((HEADS * padded, count), bf16), pltpu.VMEM((HEADS * padded, depth), bf16)]
    flops = 2 * count * depth * width
    if piggy:
        mixed, row_loss = call(
            functools.partial(finish_kernel, images),
            (shape((count, depth), bf16), shape((1, images), f32)),
            joined + [pltpu.VMEM((SPARE, HEADS * padded), f32)],
            in_vmem(4),
            flops,
        )(rows, back_home, out_weight, texts)
        return (mixed[None], row_loss[0])
    mixed = call(mix_kernel, shape((count, depth), bf16), joined, in_vmem(3), flops)(
        rows, back_home, out_weight
    )
    own_ids = lax.dynamic_slice_in_dim(segment_ids[0], lax.axis_index("grp") * count, count)
    onehot = (own_ids[None, :] == jnp.arange(images, dtype=jnp.int32)[:, None]).astype(bf16)
    pooled = lax.psum(jnp.dot(onehot, mixed, preferred_element_type=f32), "grp")
    text_vecs = unit_rows(texts.astype(f32))
    cosine = jnp.dot(unit_rows(pooled), text_vecs.T, precision=lax.Precision.HIGHEST)
    same = jnp.arange(images)[:, None] == jnp.arange(texts.shape[0])[None, :]
    row_loss = jnp.sum(losses(cosine, jnp.where(same, 1.0, -1.0)), axis=1)
    return (mixed[None], row_loss)


def solution(mesh):
    placed = (P("blk", "grp", None), P("blk", None), P(), P(), P("blk", None))
    return jax.shard_map(
        local,
        mesh=mesh,
        in_specs=placed,
        out_specs=(P("blk", "grp", None), P("blk")),
        check_vma=False,
    )
```

```python
import functools
import math

import jax
import jax.numpy as jnp
from jax import lax
from jax.experimental import pallas as pl
from jax.experimental.pallas import tpu as pltpu
from jax.sharding import PartitionSpec as P

HEADS = 8
MAXP = 1024
LANES = 128
SPARE = 8
HIDDEN = -1e30
ORDER = (6, 7, 2, 4, 3, 5, 1, 0)

logit_scale = 30.0
logit_bias = -5.0

VMEM_LIMIT = 32 * 1024 * 1024


def rounded_up(value, step):
    return (value + step - 1) // step * step


def split_in_two(total, images):
    row = lax.broadcasted_iota(jnp.int32, total.shape, 0)
    main = total.astype(jnp.bfloat16).astype(jnp.float32)
    return jnp.where(row < images, main, total - main)


def image_rows(ids, images):
    row = lax.broadcasted_iota(jnp.int32, (SPARE, ids.shape[1]), 0)
    return (lax.rem(row, images) == ids).astype(jnp.float32).astype(jnp.bfloat16)


def head_blocks(query, key, value, sums, pair):
    size = query.shape[0] // 2
    count = query.shape[1]
    for place in range(2):
        here = slice(place * size, (place + 1) * size)
        if sums is None:
            spare = jnp.zeros((SPARE, count), jnp.float32)
        else:
            first = pl.multiple_of((2 * pair + place) * LANES, LANES)
            parts = [sums[:, pl.ds(first, LANES)], sums[:, HEADS * LANES :]]
            held = sum(part.shape[1] for part in parts)
            spare = jnp.concatenate(parts + [jnp.zeros((SPARE, count - held), jnp.float32)], axis=1)
        block = jnp.concatenate([value[here], key[here], spare, query[here]], axis=0)
        yield block.astype(jnp.bfloat16)


def store_by_core(core, blocks, same_ref, cross_ref):
    first, second = blocks

    @pl.when(core == 0)
    def _():
        same_ref[...] = first
        cross_ref[...] = second

    @pl.when(core == 1)
    def _():
        same_ref[...] = second
        cross_ref[...] = first


def place_in_group():
    own = lax.rem(lax.axis_index("grp"), HEADS)
    return lax.div(own, 2), lax.rem(own, 2)


def far_kernel(images, piggy, ids_ref, rows_ref, weight_ref, normed_ref, sums_ref, same_ref, cross_ref, own_ids, rows_held, weight, id_sem, row_sem, sems):
    count, depth = rows_ref.shape
    width = weight_ref.shape[0] // 3
    wide = weight.shape[1]
    rows_fetch = pltpu.make_async_copy(rows_ref, rows_held, row_sem)
    rows_fetch.start()
    own = pl.multiple_of(lax.axis_index("grp") * count, LANES)
    ids_fetch = pltpu.make_async_copy(ids_ref.at[:, pl.ds(own, count)], own_ids, id_sem)
    ids_fetch.start()
    pair, core = place_in_group()
    pair = jnp.bitwise_xor(pair, 3)
    fetches = []
    for at in range(3):
        first = pl.multiple_of(at * width + pair * wide, 16)
        fetches.append(pltpu.make_async_copy(weight_ref.at[pl.ds(first, wide)], weight.at[at], sems.at[at]))
    for fetch in fetches:
        fetch.start()
    rows_fetch.wait()
    rows = rows_held[...]
    values = rows.astype(jnp.float32)
    center = values - jnp.mean(values, axis=1, keepdims=True)
    spread = jnp.mean(center * center, axis=1, keepdims=True)
    normed = (center * lax.rsqrt(spread + 1e-06)).astype(jnp.bfloat16)
    normed_ref[...] = normed.T
    ids_fetch.wait()
    if piggy:
        sums = jnp.dot(image_rows(own_ids[...], images), rows, preferred_element_type=jnp.float32)
        sums_ref[...] = split_in_two(sums, images)
    for fetch in fetches:
        fetch.wait()
    parts = [
        jnp.dot(weight[at], normed_ref[...], preferred_element_type=jnp.float32) for at in range(3)
    ]
    store_by_core(core, head_blocks(*parts, sums_ref if piggy else None, pair), same_ref, cross_ref)


def near_kernel(piggy, normed_ref, sums_ref, weight_ref, *out_refs):
    width = weight_ref.shape[0] // 3
    wide = 2 * width // HEADS
    own, core = place_in_group()
    for step, move in enumerate((1, 2, 0)):
        pair = jnp.bitwise_xor(own, move)
        parts = []
        for at in range(3):
            here = pl.ds(pl.multiple_of(at * width + pair * wide, 16), wide)
            parts.append(
                jnp.dot(weight_ref[here, :], normed_ref[...], preferred_element_type=jnp.float32)
            )
        blocks = head_blocks(*parts, sums_ref if piggy else None, pair)
        store_by_core(core, blocks, *out_refs[2 * step : 2 * step + 2])


def attend_kernel(images, piggy, halo, ids_ref, *rest):
    got_refs, rest = rest[:HEADS], rest[HEADS:]
    if halo:
        left_ref, right_ref, *rest = rest
    out_ref, keys, values, queries, attended, scores_a, scores_b, tops_a, tops_b, marks, starts = rest
    count = got_refs[0].shape[1]
    padded = attended.shape[0]
    size = padded - SPARE
    total_rows = HEADS * count
    length = ids_ref.shape[1]
    window = scores_a.shape[0]
    tile = scores_a.shape[1]
    tiles = total_rows // tile
    bits = max(1, (images - 1).bit_length())
    ids = ids_ref[...]
    for image in range(images):
        starts[image] = jnp.sum((ids < image).astype(jnp.int32))

    row = lax.broadcasted_iota(jnp.int32, (SPARE, length), 0)
    bit = jnp.bitwise_and(lax.shift_right_logical(jnp.broadcast_to(ids, row.shape), row >> 1), 1)
    odd = jnp.bitwise_and(row, 1)
    used = row < 2 * bits
    outside = jnp.logical_or(ids < 0, ids >= images)
    key_side = jnp.where(odd == 1, bit, 1 - bit).astype(jnp.float32)
    key_side = jnp.where(outside, 1.0, key_side)
    key_marks, query_marks = marks.at[0], marks.at[1]
    key_marks[...] = jnp.where(used, key_side * HIDDEN, 0.0)
    query_marks[...] = jnp.where(used, jnp.where(odd == 1, 1 - bit, bit), 0).astype(jnp.float32)

    key_at = size - SPARE
    query_at = 2 * size
    own = lax.rem(lax.axis_index("grp"), HEADS)
    blank = jnp.zeros((LANES - padded, count), jnp.bfloat16)

    def store_keys(here, ref):
        block = ref[key_at : key_at + padded].astype(jnp.float32)
        nothing = jnp.zeros((LANES - padded, block.shape[1]), jnp.float32)
        full = jnp.concatenate([key_marks[:, here], block[SPARE:], nothing], axis=0)
        keys[here, :] = full.T.astype(jnp.bfloat16)
        values[:, here] = ref[0:padded]

    for by, ref in zip(ORDER, got_refs):
        first = jnp.bitwise_xor(own, by) * count
        here = pl.ds(pl.multiple_of(halo + first, LANES), count)
        there = pl.ds(pl.multiple_of(first, LANES), count)
        store_keys(here, ref)
        edge = ref[query_at : query_at + 16].astype(jnp.float32)
        edge = jnp.concatenate([query_marks[:, here], edge[SPARE:]], axis=0)
        queries[0:16, there] = edge.astype(jnp.bfloat16)
        queries[16:padded, there] = ref[query_at + 16 : query_at + padded]
        queries[padded:, there] = blank
    if halo:
        store_keys(slice(0, halo), left_ref)
        store_keys(slice(length - halo, length), right_ref)

    def image_at(position):
        found = jnp.int32(0)
        for image in range(1, images):
            found += (starts[image] <= position).astype(jnp.int32)
        return found

    def following(state):
        at, image = state
        more = image < image_at(halo + at * tile + tile - 1)
        later = jnp.minimum(at + 1, tiles - 1)
        first = jnp.maximum(image_at(halo + later * tile), jnp.where(later == at, image, 0))
        return jnp.where(more, at, later), jnp.where(more, image + 1, first)

    def window_of(image):
        begin = jnp.minimum(starts[image] // LANES * LANES, length - window)
        return pl.ds(pl.multiple_of(begin, LANES), window)

    def score(state, scores, tops):
        at, image = state
        query = queries[:, pl.ds(pl.multiple_of(at * tile, tile), tile)]
        found = jnp.dot(keys[window_of(image), :], query, preferred_element_type=jnp.float32)
        scores[...] = found
        tops[...] = jnp.max(found, axis=0, keepdims=True)

    def weigh(state, scores, tops):
        at, image = state
        first = pl.multiple_of(at * tile, tile)
        labels = ids_ref[:, pl.ds(pl.multiple_of(halo + first, LANES), tile)]
        probs = jnp.exp2((scores[...] - tops[...]) * (size ** (-0.5) * math.log2(math.e)))
        total = jnp.sum(probs, axis=0, keepdims=True)
        weighted = jnp.dot(
            values[:, window_of(image)], probs.astype(jnp.bfloat16), preferred_element_type=jnp.float32
        )
        place = (slice(None), pl.ds(first, tile))
        attended[place] = jnp.where(labels == image, weighted / total, attended[place])

    pairs = jnp.int32(tiles)
    for image in range(1, images):
        offset = starts[image] - halo
        inside = jnp.logical_and(offset > 0, offset < total_rows)
        pairs += jnp.logical_and(inside, lax.rem(offset, tile) != 0).astype(jnp.int32)

    def two_pairs(_, state):
        second = following(state)
        score(second, scores_b, tops_b)
        weigh(state, scores_a, tops_a)
        third = following(second)
        score(third, scores_a, tops_a)
        weigh(second, scores_b, tops_b)
        return third

    begun = (jnp.int32(0), image_at(halo))
    score(begun, scores_a, tops_a)
    lax.fori_loop(0, (pairs + 1) // 2, two_pairs, begun)

    odd_head = lax.rem(lax.axis_index("grp"), 2) == 1
    mine = ids[:, halo : halo + total_rows]

    def placed(block, spare):
        even = jnp.concatenate([block[0:size], spare], axis=0)
        odd = jnp.concatenate([spare, block[0:size]], axis=0)
        return jnp.where(odd_head, odd, even)

    if piggy:
        nothing = jnp.zeros((SPARE, total_rows), jnp.float32)
        flat = placed(attended[...], nothing).astype(jnp.bfloat16)
        pooled = lax.dot_general(
            image_rows(mine, images), flat, (((1,), (1,)), ((), ())), preferred_element_type=jnp.float32
        )
        pooled = split_in_two(pooled, images)
        sums = jnp.zeros((SPARE, 2 * LANES), jnp.float32)
        for ref in got_refs:
            sums += ref[query_at : query_at + 16].astype(jnp.float32)[0:SPARE, 0 : 2 * LANES]
        sums = split_in_two(sums + pltpu.roll(sums, images, axis=0), images)
        spare = jnp.concatenate(
            [pooled, jnp.zeros((SPARE, LANES - padded), jnp.float32), sums], axis=1
        )
    else:
        spare = jnp.zeros((SPARE, count), jnp.float32)
    for source in range(HEADS):
        block = placed(attended[:, source * count : (source + 1) * count], spare)
        out_ref[source] = block.astype(jnp.bfloat16)


def joined_heads(got_ref, out_weight_ref, flat, weight):
    padded = got_ref.shape[1]
    size = padded - SPARE
    spares = []
    for head in range(HEADS):
        at = head * padded
        from_row = head * size - (SPARE if head % 2 else 0)
        weight[at : at + padded] = out_weight_ref[from_row : from_row + padded]
        edge = 0 if head % 2 else padded - 16
        rest = slice(16, padded) if head % 2 else slice(0, padded - 16)
        mixed_rows = got_ref[head, edge : edge + 16].astype(jnp.float32)
        nothing = jnp.zeros((SPARE, mixed_rows.shape[1]), jnp.float32)
        if head % 2:
            spares.append(mixed_rows[:SPARE])
            block = jnp.concatenate([nothing, mixed_rows[SPARE:]], axis=0)
        else:
            spares.append(mixed_rows[SPARE:])
            block = jnp.concatenate([mixed_rows[:SPARE], nothing], axis=0)
        flat[at + edge : at + edge + 16] = block.astype(jnp.bfloat16)
        flat[at + rest.start : at + rest.stop] = got_ref[head, rest]
    return spares


def mixed_rows_of(rows_ref, flat, weight):
    added = lax.dot_general(
        flat[...], weight[...], (((0,), (0,)), ((), ())), preferred_element_type=jnp.float32
    )
    return (rows_ref[...].astype(jnp.float32) + added).astype(jnp.bfloat16)


def unit_rows(matrix):
    return matrix * lax.rsqrt(jnp.sum(matrix * matrix, axis=1, keepdims=True) + 1e-06)


def losses(cosine, labels):
    logits = -labels * (logit_scale * cosine + logit_bias)
    return jnp.maximum(logits, 0.0) + jnp.log1p(jnp.exp(-jnp.abs(logits)))


def finish_kernel(images, rows_ref, got_ref, out_weight_ref, text_ref, mixed_ref, loss_ref, flat, weight, pooled_heads):
    padded = got_ref.shape[1]
    spares = joined_heads(got_ref, out_weight_ref, flat, weight)
    for head in range(HEADS):
        pooled_heads[:, head * padded : (head + 1) * padded] = spares[head][:, 0:padded]
    pooled = jnp.dot(
        pooled_heads[...].astype(jnp.bfloat16), weight[...], preferred_element_type=jnp.float32
    )
    patch_sums = [spare[:, LANES : 2 * LANES] for spare in spares] + [spares[0][:, 2 * LANES :]]
    pooled = pooled + jnp.concatenate(patch_sums, axis=1)
    pooled = pooled + pltpu.roll(pooled, images, axis=0)
    image_vecs = unit_rows(pooled)
    text_vecs = unit_rows(text_ref[...].astype(jnp.float32))
    cosine = lax.dot_general(
        text_vecs,
        image_vecs,
        (((1,), (1,)), ((), ())),
        precision=lax.Precision.HIGHEST,
        preferred_element_type=jnp.float32,
    )
    text = lax.broadcasted_iota(jnp.int32, cosine.shape, 0)
    image = lax.broadcasted_iota(jnp.int32, cosine.shape, 1)
    terms = losses(cosine, jnp.where(text == image, 1.0, -1.0))
    loss_ref[...] = jnp.sum(terms, axis=0, keepdims=True)[:, 0:images]
    mixed_ref[...] = mixed_rows_of(rows_ref, flat, weight)


def mix_kernel(rows_ref, got_ref, out_weight_ref, mixed_ref, flat, weight):
    joined_heads(got_ref, out_weight_ref, flat, weight)
    mixed_ref[...] = mixed_rows_of(rows_ref, flat, weight)


def in_vmem(count):
    return [pl.BlockSpec(memory_space=pltpu.VMEM)] * count


def in_hbm(value):
    return pltpu.with_memory_space_constraint(value, pltpu.HBM)


def call(kernel, out_shape, scratch, in_specs, flops):
    out_specs = jax.tree.map(lambda _: pl.BlockSpec(memory_space=pltpu.VMEM), out_shape)
    return pl.pallas_call(
        kernel,
        out_shape=out_shape,
        in_specs=in_specs,
        out_specs=out_specs,
        scratch_shapes=scratch,
        compiler_params=pltpu.CompilerParams(vmem_limit_bytes=VMEM_LIMIT),
        cost_estimate=pl.CostEstimate(flops=flops, bytes_accessed=8 << 20, transcendentals=0),
    )


def moved(value, axis, pairs):
    return lax.ppermute(value, axis, pairs)


def all_texts(texts):
    peers = lax.axis_size("blk")
    shifts = range(1, peers)
    return [texts] + [moved(texts, "blk", [(i, (i + by) % peers) for i in range(peers)]) for by in shifts]


def exchanged(blocks, groups):
    return lax.all_to_all(blocks, "grp", 0, 0, axis_index_groups=groups, tiled=True)


def local(patches, segment_ids, qkv_weight, out_weight, text_embed):
    rows = patches[0]
    count, depth = rows.shape
    width = out_weight.shape[0]
    size = width // HEADS
    padded = size + SPARE
    images = text_embed.shape[0]
    group_size = lax.axis_size("grp")
    parts = group_size // HEADS
    piggy = parts == 1 and 2 * images == SPARE and count >= depth - (HEADS - 2) * LANES
    groups = None if parts == 1 else [list(range(p * HEADS, (p + 1) * HEADS)) for p in range(parts)]
    bf16, f32 = jnp.bfloat16, jnp.float32
    shape = jax.ShapeDtypeStruct

    block = shape((3 * size + SPARE, count), bf16)
    hbm = pl.BlockSpec(memory_space=pltpu.HBM)
    turned_weight = qkv_weight.T
    normed, sums, *sent = call(
        functools.partial(far_kernel, images, piggy),
        (shape((depth, count), bf16), shape((SPARE, depth), f32), block, block),
        [
            pltpu.VMEM((1, count), jnp.int32),
            pltpu.VMEM((count, depth), bf16),
            pltpu.VMEM((3, 2 * size, depth), bf16),
            pltpu.SemaphoreType.DMA,
            pltpu.SemaphoreType.DMA,
            pltpu.SemaphoreType.DMA((3,)),
        ],
        [hbm] * 3,
        2 * count * depth * 6 * size,
    )(in_hbm(segment_ids), in_hbm(rows), in_hbm(turned_weight))
    sent += call(
        functools.partial(near_kernel, piggy),
        (block,) * 6,
        [],
        in_vmem(3),
        2 * count * depth * 18 * size,
    )(normed, sums, turned_weight)
    sent = dict(zip((6, 7, 2, 3, 4, 5, 0, 1), sent))
    got = []
    for by in ORDER:
        pairs = [(i, i ^ by) for i in range(group_size)]
        got.append(moved(sent[by], "grp", pairs) if by else sent[by])
    text_embed, got[-1] = lax.optimization_barrier((text_embed, got[-1]))
    got, texts = lax.optimization_barrier((got, all_texts(text_embed)))
    texts = jnp.concatenate(texts, axis=0)

    length = HEADS * count
    halo = 0
    operands = [segment_ids, *got]
    if parts > 1:
        halo = rounded_up(MAXP - 1, LANES)
        part = lax.axis_index("grp") // HEADS
        whole_ids = jnp.concatenate(
            [
                jnp.full((1, halo), -1, jnp.int32),
                segment_ids,
                jnp.full((1, halo), images, jnp.int32),
            ],
            axis=1,
        )
        near_ids = lax.dynamic_slice_in_dim(whole_ids, part * length, length + 2 * halo, axis=1)
        order = jnp.bitwise_xor(lax.axis_index("grp") % HEADS, jnp.arange(HEADS))
        flat = jnp.stack([got[ORDER.index(by)] for by in range(HEADS)])[order][:, : 2 * size].transpose(1, 0, 2).reshape(2 * size, length)
        flat = jnp.concatenate([flat, jnp.zeros((16, length), bf16)], axis=0)
        ahead = [(i, i + HEADS) for i in range(group_size - HEADS)]
        back = [(i + HEADS, i) for i in range(group_size - HEADS)]
        left = moved(flat[:, length - halo :], "grp", ahead)
        right = moved(flat[:, :halo], "grp", back)
        operands = [near_ids, *got, left, right]
    reach = length + 2 * halo
    window = min(rounded_up(MAXP + LANES - 1, LANES), reach)
    tile = 2 * LANES
    answers = call(
        functools.partial(attend_kernel, images, piggy, halo),
        shape((HEADS, padded, count), bf16),
        [
            pltpu.VMEM((reach, LANES), bf16),
            pltpu.VMEM((padded, reach), bf16),
            pltpu.VMEM((LANES, length), bf16),
            pltpu.VMEM((padded, length), f32),
            pltpu.VMEM((window, tile), f32),
            pltpu.VMEM((window, tile), f32),
            pltpu.VMEM((1, tile), f32),
            pltpu.VMEM((1, tile), f32),
            pltpu.VMEM((2, SPARE, reach), f32),
            pltpu.SMEM((images,), jnp.int32),
        ],
        in_vmem(len(operands)),
        4 * size * length * MAXP,
    )(*operands)
    back_home = exchanged(answers, groups)

    joined = [pltpu.VMEM((HEADS * padded, count), bf16), pltpu.VMEM((HEADS * padded, depth), bf16)]
    flops = 2 * count * depth * width
    if piggy:
        mixed, row_loss = call(
            functools.partial(finish_kernel, images),
            (shape((count, depth), bf16), shape((1, images), f32)),
            joined + [pltpu.VMEM((SPARE, HEADS * padded), f32)],
            in_vmem(4),
            flops,
        )(rows, back_home, out_weight, texts)
        return (mixed[None], row_loss[0])
    mixed = call(mix_kernel, shape((count, depth), bf16), joined, in_vmem(3), flops)(
        rows, back_home, out_weight
    )
    own_ids = lax.dynamic_slice_in_dim(segment_ids[0], lax.axis_index("grp") * count, count)
    onehot = (own_ids[None, :] == jnp.arange(images, dtype=jnp.int32)[:, None]).astype(bf16)
    pooled = lax.psum(jnp.dot(onehot, mixed, preferred_element_type=f32), "grp")
    text_vecs = unit_rows(texts.astype(f32))
    cosine = jnp.dot(unit_rows(pooled), text_vecs.T, precision=lax.Precision.HIGHEST)
    same = jnp.arange(images)[:, None] == jnp.arange(texts.shape[0])[None, :]
    row_loss = jnp.sum(losses(cosine, jnp.where(same, 1.0, -1.0)), axis=1)
    return (mixed[None], row_loss)


def solution(mesh):
    placed = (P("blk", "grp", None), P("blk", None), P(), P(), P("blk", None))
    return jax.shard_map(
        local,
        mesh=mesh,
        in_specs=placed,
        out_specs=(P("blk", "grp", None), P("blk")),
        check_vma=False,
    )
```

```python
import functools
import math

import jax
import jax.numpy as jnp
from jax import lax
from jax.experimental import pallas as pl
from jax.experimental.pallas import tpu as pltpu
from jax.sharding import PartitionSpec as P

HEADS = 8
MAXP = 1024
LANES = 128
SPARE = 8
HIDDEN = -1e30
ORDER = (6, 7, 2, 4, 3, 5, 1, 0)

logit_scale = 30.0
logit_bias = -5.0

VMEM_LIMIT = 32 * 1024 * 1024


def rounded_up(value, step):
    return (value + step - 1) // step * step


def split_in_two(total, images):
    row = lax.broadcasted_iota(jnp.int32, total.shape, 0)
    main = total.astype(jnp.bfloat16).astype(jnp.float32)
    return jnp.where(row < images, main, total - main)


def image_rows(ids, images):
    row = lax.broadcasted_iota(jnp.int32, (SPARE, ids.shape[1]), 0)
    return (lax.rem(row, images) == ids).astype(jnp.float32).astype(jnp.bfloat16)


def head_blocks(query, key, value, sums, pair):
    size = query.shape[0] // 2
    count = query.shape[1]
    for place in range(2):
        here = slice(place * size, (place + 1) * size)
        if sums is None:
            spare = jnp.zeros((SPARE, count), jnp.float32)
        else:
            first = pl.multiple_of((2 * pair + place) * LANES, LANES)
            parts = [sums[:, pl.ds(first, LANES)], sums[:, HEADS * LANES :]]
            held = sum(part.shape[1] for part in parts)
            spare = jnp.concatenate(parts + [jnp.zeros((SPARE, count - held), jnp.float32)], axis=1)
        block = jnp.concatenate([value[here], key[here], spare, query[here]], axis=0)
        yield block.astype(jnp.bfloat16)


def store_by_core(core, blocks, same_ref, cross_ref):
    first, second = blocks

    @pl.when(core == 0)
    def _():
        same_ref[...] = first
        cross_ref[...] = second

    @pl.when(core == 1)
    def _():
        same_ref[...] = second
        cross_ref[...] = first


def place_in_group():
    own = lax.rem(lax.axis_index("grp"), HEADS)
    return lax.div(own, 2), lax.rem(own, 2)


def far_kernel(images, piggy, ids_ref, rows_ref, weight_ref, normed_ref, sums_ref, same_ref, cross_ref, own_ids, rows_held, weight, id_sem, row_sem, sems):
    count, depth = rows_ref.shape
    width = weight_ref.shape[0] // 3
    wide = weight.shape[1]
    rows_fetch = pltpu.make_async_copy(rows_ref, rows_held, row_sem)
    rows_fetch.start()
    own = pl.multiple_of(lax.axis_index("grp") * count, LANES)
    ids_fetch = pltpu.make_async_copy(ids_ref.at[:, pl.ds(own, count)], own_ids, id_sem)
    ids_fetch.start()
    pair, core = place_in_group()
    pair = jnp.bitwise_xor(pair, 3)
    fetches = []
    for at in range(3):
        first = pl.multiple_of(at * width + pair * wide, 16)
        fetches.append(pltpu.make_async_copy(weight_ref.at[pl.ds(first, wide)], weight.at[at], sems.at[at]))
    for fetch in fetches:
        fetch.start()
    rows_fetch.wait()
    rows = rows_held[...]
    values = rows.astype(jnp.float32)
    center = values - jnp.mean(values, axis=1, keepdims=True)
    spread = jnp.mean(center * center, axis=1, keepdims=True)
    normed = (center * lax.rsqrt(spread + 1e-06)).astype(jnp.bfloat16)
    normed_ref[...] = normed.T
    ids_fetch.wait()
    if piggy:
        sums = jnp.dot(image_rows(own_ids[...], images), rows, preferred_element_type=jnp.float32)
        sums_ref[...] = split_in_two(sums, images)
    for fetch in fetches:
        fetch.wait()
    parts = [
        jnp.dot(weight[at], normed_ref[...], preferred_element_type=jnp.float32) for at in range(3)
    ]
    store_by_core(core, head_blocks(*parts, sums_ref if piggy else None, pair), same_ref, cross_ref)


def near_kernel(piggy, normed_ref, sums_ref, weight_ref, *out_refs):
    width = weight_ref.shape[0] // 3
    wide = 2 * width // HEADS
    own, core = place_in_group()
    for step, move in enumerate((1, 2, 0)):
        pair = jnp.bitwise_xor(own, move)
        parts = []
        for at in range(3):
            here = pl.ds(pl.multiple_of(at * width + pair * wide, 16), wide)
            parts.append(
                jnp.dot(weight_ref[here, :], normed_ref[...], preferred_element_type=jnp.float32)
            )
        blocks = head_blocks(*parts, sums_ref if piggy else None, pair)
        store_by_core(core, blocks, *out_refs[2 * step : 2 * step + 2])


def attend_kernel(images, piggy, halo, ids_ref, *rest):
    got_refs, rest = rest[:HEADS], rest[HEADS:]
    if halo:
        left_ref, right_ref, *rest = rest
    out_ref, keys, values, queries, attended, scores_a, scores_b, tops_a, tops_b, marks, starts = rest
    count = got_refs[0].shape[1]
    padded = attended.shape[0]
    size = padded - SPARE
    total_rows = HEADS * count
    length = ids_ref.shape[1]
    window = scores_a.shape[0]
    tile = scores_a.shape[1]
    tiles = total_rows // tile
    bits = max(1, (images - 1).bit_length())
    ids = ids_ref[...]
    for image in range(images):
        starts[image] = jnp.sum((ids < image).astype(jnp.int32))

    row = lax.broadcasted_iota(jnp.int32, (SPARE, length), 0)
    bit = jnp.bitwise_and(lax.shift_right_logical(jnp.broadcast_to(ids, row.shape), row >> 1), 1)
    odd = jnp.bitwise_and(row, 1)
    used = row < 2 * bits
    outside = jnp.logical_or(ids < 0, ids >= images)
    key_side = jnp.where(odd == 1, bit, 1 - bit).astype(jnp.float32)
    key_side = jnp.where(outside, 1.0, key_side)
    key_marks, query_marks = marks.at[0], marks.at[1]
    key_marks[...] = jnp.where(used, key_side * HIDDEN, 0.0)
    query_marks[...] = jnp.where(used, jnp.where(odd == 1, 1 - bit, bit), 0).astype(jnp.float32)

    key_at = size - SPARE
    query_at = 2 * size
    own = lax.rem(lax.axis_index("grp"), HEADS)
    blank = jnp.zeros((LANES - padded, count), jnp.bfloat16)

    def store_keys(here, ref):
        block = ref[key_at : key_at + padded].astype(jnp.float32)
        nothing = jnp.zeros((LANES - padded, block.shape[1]), jnp.float32)
        full = jnp.concatenate([key_marks[:, here], block[SPARE:], nothing], axis=0)
        keys[here, :] = full.T.astype(jnp.bfloat16)
        values[:, here] = ref[0:padded]

    for by, ref in zip(ORDER, got_refs):
        first = jnp.bitwise_xor(own, by) * count
        here = pl.ds(pl.multiple_of(halo + first, LANES), count)
        there = pl.ds(pl.multiple_of(first, LANES), count)
        store_keys(here, ref)
        edge = ref[query_at : query_at + 16].astype(jnp.float32)
        edge = jnp.concatenate([query_marks[:, here], edge[SPARE:]], axis=0)
        queries[0:16, there] = edge.astype(jnp.bfloat16)
        queries[16:padded, there] = ref[query_at + 16 : query_at + padded]
        queries[padded:, there] = blank
    if halo:
        store_keys(slice(0, halo), left_ref)
        store_keys(slice(length - halo, length), right_ref)

    def image_at(position):
        found = jnp.int32(0)
        for image in range(1, images):
            found += (starts[image] <= position).astype(jnp.int32)
        return found

    def following(state):
        at, image = state
        more = image < image_at(halo + at * tile + tile - 1)
        later = jnp.minimum(at + 1, tiles - 1)
        first = jnp.maximum(image_at(halo + later * tile), jnp.where(later == at, image, 0))
        return jnp.where(more, at, later), jnp.where(more, image + 1, first)

    def window_of(image):
        begin = jnp.minimum(starts[image] // LANES * LANES, length - window)
        return pl.ds(pl.multiple_of(begin, LANES), window)

    def score(state, scores, tops):
        at, image = state
        query = queries[:, pl.ds(pl.multiple_of(at * tile, tile), tile)]
        found = jnp.dot(keys[window_of(image), :], query, preferred_element_type=jnp.float32)
        scores[...] = found
        tops[...] = jnp.max(found, axis=0, keepdims=True)

    def weigh(state, scores, tops):
        at, image = state
        first = pl.multiple_of(at * tile, tile)
        labels = ids_ref[:, pl.ds(pl.multiple_of(halo + first, LANES), tile)]
        probs = jnp.exp2((scores[...] - tops[...]) * (size ** (-0.5) * math.log2(math.e)))
        total = jnp.sum(probs, axis=0, keepdims=True)
        weighted = jnp.dot(
            values[:, window_of(image)], probs.astype(jnp.bfloat16), preferred_element_type=jnp.float32
        )
        place = (slice(None), pl.ds(first, tile))
        attended[place] = jnp.where(labels == image, weighted / total, attended[place])

    pairs = jnp.int32(tiles)
    for image in range(1, images):
        offset = starts[image] - halo
        inside = jnp.logical_and(offset > 0, offset < total_rows)
        pairs += jnp.logical_and(inside, lax.rem(offset, tile) != 0).astype(jnp.int32)

    def two_pairs(_, state):
        second = following(state)
        score(second, scores_b, tops_b)
        weigh(state, scores_a, tops_a)
        third = following(second)
        score(third, scores_a, tops_a)
        weigh(second, scores_b, tops_b)
        return third

    begun = (jnp.int32(0), image_at(halo))
    score(begun, scores_a, tops_a)
    lax.fori_loop(0, (pairs + 1) // 2, two_pairs, begun)

    odd_head = lax.rem(lax.axis_index("grp"), 2) == 1
    mine = ids[:, halo : halo + total_rows]

    def placed(block, spare):
        even = jnp.concatenate([block[0:size], spare], axis=0)
        odd = jnp.concatenate([spare, block[0:size]], axis=0)
        return jnp.where(odd_head, odd, even)

    if piggy:
        nothing = jnp.zeros((SPARE, total_rows), jnp.float32)
        flat = placed(attended[...], nothing).astype(jnp.bfloat16)
        pooled = lax.dot_general(
            image_rows(mine, images), flat, (((1,), (1,)), ((), ())), preferred_element_type=jnp.float32
        )
        pooled = split_in_two(pooled, images)
        sums = jnp.zeros((SPARE, 2 * LANES), jnp.float32)
        for ref in got_refs:
            sums += ref[query_at : query_at + 16].astype(jnp.float32)[0:SPARE, 0 : 2 * LANES]
        sums = split_in_two(sums + pltpu.roll(sums, images, axis=0), images)
        spare = jnp.concatenate(
            [pooled, jnp.zeros((SPARE, LANES - padded), jnp.float32), sums], axis=1
        )
    else:
        spare = jnp.zeros((SPARE, count), jnp.float32)
    for source in range(HEADS):
        block = placed(attended[:, source * count : (source + 1) * count], spare)
        out_ref[source] = block.astype(jnp.bfloat16)


def joined_heads(got_ref, out_weight_ref, flat, weight):
    padded = got_ref.shape[1]
    size = padded - SPARE
    spares = []
    for head in range(HEADS):
        at = head * padded
        from_row = head * size - (SPARE if head % 2 else 0)
        weight[at : at + padded] = out_weight_ref[from_row : from_row + padded]
        edge = 0 if head % 2 else padded - 16
        rest = slice(16, padded) if head % 2 else slice(0, padded - 16)
        mixed_rows = got_ref[head, edge : edge + 16].astype(jnp.float32)
        nothing = jnp.zeros((SPARE, mixed_rows.shape[1]), jnp.float32)
        if head % 2:
            spares.append(mixed_rows[:SPARE])
            block = jnp.concatenate([nothing, mixed_rows[SPARE:]], axis=0)
        else:
            spares.append(mixed_rows[SPARE:])
            block = jnp.concatenate([mixed_rows[:SPARE], nothing], axis=0)
        flat[at + edge : at + edge + 16] = block.astype(jnp.bfloat16)
        flat[at + rest.start : at + rest.stop] = got_ref[head, rest]
    return spares


def mixed_rows_of(rows_ref, flat, weight):
    added = lax.dot_general(
        flat[...], weight[...], (((0,), (0,)), ((), ())), preferred_element_type=jnp.float32
    )
    return (rows_ref[...].astype(jnp.float32) + added).astype(jnp.bfloat16)


def unit_rows(matrix):
    return matrix * lax.rsqrt(jnp.sum(matrix * matrix, axis=1, keepdims=True) + 1e-06)


def losses(cosine, labels):
    logits = -labels * (logit_scale * cosine + logit_bias)
    return jnp.maximum(logits, 0.0) + jnp.log1p(jnp.exp(-jnp.abs(logits)))


def finish_kernel(images, rows_ref, got_ref, out_weight_ref, text_ref, mixed_ref, loss_ref, flat, weight, pooled_heads):
    padded = got_ref.shape[1]
    spares = joined_heads(got_ref, out_weight_ref, flat, weight)
    for head in range(HEADS):
        pooled_heads[:, head * padded : (head + 1) * padded] = spares[head][:, 0:padded]
    pooled = jnp.dot(
        pooled_heads[...].astype(jnp.bfloat16), weight[...], preferred_element_type=jnp.float32
    )
    patch_sums = [spare[:, LANES : 2 * LANES] for spare in spares] + [spares[0][:, 2 * LANES :]]
    pooled = pooled + jnp.concatenate(patch_sums, axis=1)
    pooled = pooled + pltpu.roll(pooled, images, axis=0)
    image_vecs = unit_rows(pooled)
    text_vecs = unit_rows(text_ref[...].astype(jnp.float32))
    cosine = lax.dot_general(
        text_vecs,
        image_vecs,
        (((1,), (1,)), ((), ())),
        precision=lax.Precision.HIGHEST,
        preferred_element_type=jnp.float32,
    )
    text = lax.broadcasted_iota(jnp.int32, cosine.shape, 0)
    image = lax.broadcasted_iota(jnp.int32, cosine.shape, 1)
    terms = losses(cosine, jnp.where(text == image, 1.0, -1.0))
    loss_ref[...] = jnp.sum(terms, axis=0, keepdims=True)[:, 0:images]
    mixed_ref[...] = mixed_rows_of(rows_ref, flat, weight)


def mix_kernel(rows_ref, got_ref, out_weight_ref, mixed_ref, flat, weight):
    joined_heads(got_ref, out_weight_ref, flat, weight)
    mixed_ref[...] = mixed_rows_of(rows_ref, flat, weight)


def in_vmem(count):
    return [pl.BlockSpec(memory_space=pltpu.VMEM)] * count


def in_hbm(value):
    return pltpu.with_memory_space_constraint(value, pltpu.HBM)


def call(kernel, out_shape, scratch, in_specs, flops):
    out_specs = jax.tree.map(lambda _: pl.BlockSpec(memory_space=pltpu.VMEM), out_shape)
    return pl.pallas_call(
        kernel,
        out_shape=out_shape,
        in_specs=in_specs,
        out_specs=out_specs,
        scratch_shapes=scratch,
        compiler_params=pltpu.CompilerParams(vmem_limit_bytes=VMEM_LIMIT),
        cost_estimate=pl.CostEstimate(flops=flops, bytes_accessed=8 << 20, transcendentals=0),
    )


def moved(value, axis, pairs):
    return lax.ppermute(value, axis, pairs)


def all_texts(texts):
    peers = lax.axis_size("blk")
    shifts = range(1, peers)
    return [texts] + [moved(texts, "blk", [(i, (i + by) % peers) for i in range(peers)]) for by in shifts]


def exchanged(blocks, groups):
    return lax.all_to_all(blocks, "grp", 0, 0, axis_index_groups=groups, tiled=True)


def local(patches, segment_ids, qkv_weight, out_weight, text_embed):
    rows = patches[0]
    count, depth = rows.shape
    width = out_weight.shape[0]
    size = width // HEADS
    padded = size + SPARE
    images = text_embed.shape[0]
    group_size = lax.axis_size("grp")
    parts = group_size // HEADS
    piggy = parts == 1 and 2 * images == SPARE and count >= depth - (HEADS - 2) * LANES
    groups = None if parts == 1 else [list(range(p * HEADS, (p + 1) * HEADS)) for p in range(parts)]
    bf16, f32 = jnp.bfloat16, jnp.float32
    shape = jax.ShapeDtypeStruct

    block = shape((3 * size + SPARE, count), bf16)
    hbm = pl.BlockSpec(memory_space=pltpu.HBM)
    turned_weight = qkv_weight.T
    normed, sums, *sent = call(
        functools.partial(far_kernel, images, piggy),
        (shape((depth, count), bf16), shape((SPARE, depth), f32), block, block),
        [
            pltpu.VMEM((1, count), jnp.int32),
            pltpu.VMEM((count, depth), bf16),
            pltpu.VMEM((3, 2 * size, depth), bf16),
            pltpu.SemaphoreType.DMA,
            pltpu.SemaphoreType.DMA,
            pltpu.SemaphoreType.DMA((3,)),
        ],
        [hbm] * 3,
        2 * count * depth * 6 * size,
    )(in_hbm(segment_ids), in_hbm(rows), in_hbm(turned_weight))
    sent += call(
        functools.partial(near_kernel, piggy),
        (block,) * 6,
        [],
        in_vmem(3),
        2 * count * depth * 18 * size,
    )(normed, sums, turned_weight)
    sent = dict(zip((6, 7, 2, 3, 4, 5, 0, 1), sent))
    got = []
    for by in ORDER:
        pairs = [(i, i ^ by) for i in range(group_size)]
        got.append(moved(sent[by], "grp", pairs) if by else sent[by])

    length = HEADS * count
    halo = 0
    operands = [segment_ids, *got]
    if parts > 1:
        halo = rounded_up(MAXP - 1, LANES)
        part = lax.axis_index("grp") // HEADS
        whole_ids = jnp.concatenate(
            [
                jnp.full((1, halo), -1, jnp.int32),
                segment_ids,
                jnp.full((1, halo), images, jnp.int32),
            ],
            axis=1,
        )
        near_ids = lax.dynamic_slice_in_dim(whole_ids, part * length, length + 2 * halo, axis=1)
        order = jnp.bitwise_xor(lax.axis_index("grp") % HEADS, jnp.arange(HEADS))
        flat = jnp.stack([got[ORDER.index(by)] for by in range(HEADS)])[order][:, : 2 * size].transpose(1, 0, 2).reshape(2 * size, length)
        flat = jnp.concatenate([flat, jnp.zeros((16, length), bf16)], axis=0)
        ahead = [(i, i + HEADS) for i in range(group_size - HEADS)]
        back = [(i + HEADS, i) for i in range(group_size - HEADS)]
        left = moved(flat[:, length - halo :], "grp", ahead)
        right = moved(flat[:, :halo], "grp", back)
        operands = [near_ids, *got, left, right]
    reach = length + 2 * halo
    window = min(rounded_up(MAXP + LANES - 1, LANES), reach)
    tile = 2 * LANES
    answers = call(
        functools.partial(attend_kernel, images, piggy, halo),
        shape((HEADS, padded, count), bf16),
        [
            pltpu.VMEM((reach, LANES), bf16),
            pltpu.VMEM((padded, reach), bf16),
            pltpu.VMEM((LANES, length), bf16),
            pltpu.VMEM((padded, length), f32),
            pltpu.VMEM((window, tile), f32),
            pltpu.VMEM((window, tile), f32),
            pltpu.VMEM((1, tile), f32),
            pltpu.VMEM((1, tile), f32),
            pltpu.VMEM((2, SPARE, reach), f32),
            pltpu.SMEM((images,), jnp.int32),
        ],
        in_vmem(len(operands)),
        4 * size * length * MAXP,
    )(*operands)
    back_home = exchanged(answers, groups)
    text_embed, _ = lax.optimization_barrier((text_embed, answers))
    texts = jnp.concatenate(all_texts(text_embed), axis=0)

    joined = [pltpu.VMEM((HEADS * padded, count), bf16), pltpu.VMEM((HEADS * padded, depth), bf16)]
    flops = 2 * count * depth * width
    if piggy:
        mixed, row_loss = call(
            functools.partial(finish_kernel, images),
            (shape((count, depth), bf16), shape((1, images), f32)),
            joined + [pltpu.VMEM((SPARE, HEADS * padded), f32)],
            in_vmem(4),
            flops,
        )(rows, back_home, out_weight, texts)
        return (mixed[None], row_loss[0])
    mixed = call(mix_kernel, shape((count, depth), bf16), joined, in_vmem(3), flops)(
        rows, back_home, out_weight
    )
    own_ids = lax.dynamic_slice_in_dim(segment_ids[0], lax.axis_index("grp") * count, count)
    onehot = (own_ids[None, :] == jnp.arange(images, dtype=jnp.int32)[:, None]).astype(bf16)
    pooled = lax.psum(jnp.dot(onehot, mixed, preferred_element_type=f32), "grp")
    text_vecs = unit_rows(texts.astype(f32))
    cosine = jnp.dot(unit_rows(pooled), text_vecs.T, precision=lax.Precision.HIGHEST)
    same = jnp.arange(images)[:, None] == jnp.arange(texts.shape[0])[None, :]
    row_loss = jnp.sum(losses(cosine, jnp.where(same, 1.0, -1.0)), axis=1)
    return (mixed[None], row_loss)


def solution(mesh):
    placed = (P("blk", "grp", None), P("blk", None), P(), P(), P("blk", None))
    return jax.shard_map(
        local,
        mesh=mesh,
        in_specs=placed,
        out_specs=(P("blk", "grp", None), P("blk")),
        check_vma=False,
    )
```

```python
import functools
import math

import jax
import jax.numpy as jnp
from jax import lax
from jax.experimental import pallas as pl
from jax.experimental.pallas import tpu as pltpu
from jax.sharding import PartitionSpec as P

HEADS = 8
MAXP = 1024
LANES = 128
SPARE = 8
HIDDEN = -1e30
ORDER = (6, 7, 2, 4, 3, 5, 1, 0)

logit_scale = 30.0
logit_bias = -5.0

VMEM_LIMIT = 32 * 1024 * 1024


def rounded_up(value, step):
    return (value + step - 1) // step * step


def split_in_two(total, images):
    row = lax.broadcasted_iota(jnp.int32, total.shape, 0)
    main = total.astype(jnp.bfloat16).astype(jnp.float32)
    return jnp.where(row < images, main, total - main)


def image_rows(ids, images):
    row = lax.broadcasted_iota(jnp.int32, (SPARE, ids.shape[1]), 0)
    return (lax.rem(row, images) == ids).astype(jnp.float32).astype(jnp.bfloat16)


def head_blocks(query, key, value, sums, pair):
    size = query.shape[0] // 2
    count = query.shape[1]
    for place in range(2):
        here = slice(place * size, (place + 1) * size)
        if sums is None:
            spare = jnp.zeros((SPARE, count), jnp.float32)
        else:
            first = pl.multiple_of((2 * pair + place) * LANES, LANES)
            parts = [sums[:, pl.ds(first, LANES)], sums[:, HEADS * LANES :]]
            held = sum(part.shape[1] for part in parts)
            spare = jnp.concatenate(parts + [jnp.zeros((SPARE, count - held), jnp.float32)], axis=1)
        block = jnp.concatenate([value[here], key[here], spare, query[here]], axis=0)
        yield block.astype(jnp.bfloat16)


def store_by_core(core, blocks, same_ref, cross_ref):
    first, second = blocks

    @pl.when(core == 0)
    def _():
        same_ref[...] = first
        cross_ref[...] = second

    @pl.when(core == 1)
    def _():
        same_ref[...] = second
        cross_ref[...] = first


def place_in_group():
    own = lax.rem(lax.axis_index("grp"), HEADS)
    return lax.div(own, 2), lax.rem(own, 2)


def far_kernel(images, piggy, ids_ref, rows_ref, weight_ref, normed_ref, sums_ref, same_ref, cross_ref, own_ids, rows_held, weight, id_sem, row_sem, sems):
    count, depth = rows_ref.shape
    width = weight_ref.shape[0] // 3
    wide = weight.shape[1]
    rows_fetch = pltpu.make_async_copy(rows_ref, rows_held, row_sem)
    rows_fetch.start()
    own = pl.multiple_of(lax.axis_index("grp") * count, LANES)
    ids_fetch = pltpu.make_async_copy(ids_ref.at[:, pl.ds(own, count)], own_ids, id_sem)
    ids_fetch.start()
    pair, core = place_in_group()
    pair = jnp.bitwise_xor(pair, 3)
    fetches = []
    for at in range(3):
        first = pl.multiple_of(at * width + pair * wide, 16)
        fetches.append(pltpu.make_async_copy(weight_ref.at[pl.ds(first, wide)], weight.at[at], sems.at[at]))
    for fetch in fetches:
        fetch.start()
    rows_fetch.wait()
    rows = rows_held[...]
    values = rows.astype(jnp.float32)
    center = values - jnp.mean(values, axis=1, keepdims=True)
    spread = jnp.mean(center * center, axis=1, keepdims=True)
    normed = (center * lax.rsqrt(spread + 1e-06)).astype(jnp.bfloat16)
    normed_ref[...] = normed.T
    ids_fetch.wait()
    if piggy:
        sums = jnp.dot(image_rows(own_ids[...], images), rows, preferred_element_type=jnp.float32)
        sums_ref[...] = split_in_two(sums, images)
    for fetch in fetches:
        fetch.wait()
    parts = [
        jnp.dot(weight[at], normed_ref[...], preferred_element_type=jnp.float32) for at in range(3)
    ]
    store_by_core(core, head_blocks(*parts, sums_ref if piggy else None, pair), same_ref, cross_ref)


def near_kernel(piggy, normed_ref, sums_ref, weight_ref, *out_refs):
    width = weight_ref.shape[0] // 3
    wide = 2 * width // HEADS
    own, core = place_in_group()
    for step, move in enumerate((1, 2, 0)):
        pair = jnp.bitwise_xor(own, move)
        parts = []
        for at in range(3):
            here = pl.ds(pl.multiple_of(at * width + pair * wide, 16), wide)
            parts.append(
                jnp.dot(weight_ref[here, :], normed_ref[...], preferred_element_type=jnp.float32)
            )
        blocks = head_blocks(*parts, sums_ref if piggy else None, pair)
        store_by_core(core, blocks, *out_refs[2 * step : 2 * step + 2])


def attend_kernel(images, piggy, halo, ids_ref, *rest):
    got_refs, rest = rest[:HEADS], rest[HEADS:]
    if halo:
        left_ref, right_ref, *rest = rest
    out_ref, keys, values, queries, attended, scores_a, scores_b, tops_a, tops_b, marks, starts = rest
    count = got_refs[0].shape[1]
    padded = attended.shape[0]
    size = padded - SPARE
    total_rows = HEADS * count
    length = ids_ref.shape[1]
    window = scores_a.shape[0]
    tile = scores_a.shape[1]
    tiles = total_rows // tile
    bits = max(1, (images - 1).bit_length())
    ids = ids_ref[...]
    for image in range(images):
        starts[image] = jnp.sum((ids < image).astype(jnp.int32))

    row = lax.broadcasted_iota(jnp.int32, (SPARE, length), 0)
    bit = jnp.bitwise_and(lax.shift_right_logical(jnp.broadcast_to(ids, row.shape), row >> 1), 1)
    odd = jnp.bitwise_and(row, 1)
    used = row < 2 * bits
    outside = jnp.logical_or(ids < 0, ids >= images)
    key_side = jnp.where(odd == 1, bit, 1 - bit).astype(jnp.float32)
    key_side = jnp.where(outside, 1.0, key_side)
    key_marks, query_marks = marks.at[0], marks.at[1]
    key_marks[...] = jnp.where(used, key_side * HIDDEN, 0.0)
    query_marks[...] = jnp.where(used, jnp.where(odd == 1, 1 - bit, bit), 0).astype(jnp.float32)

    key_at = size - SPARE
    query_at = 2 * size
    own = lax.rem(lax.axis_index("grp"), HEADS)
    blank = jnp.zeros((LANES - padded, count), jnp.bfloat16)

    def store_keys(here, ref):
        block = ref[key_at : key_at + padded].astype(jnp.float32)
        nothing = jnp.zeros((LANES - padded, block.shape[1]), jnp.float32)
        full = jnp.concatenate([key_marks[:, here], block[SPARE:], nothing], axis=0)
        keys[here, :] = full.astype(jnp.bfloat16).T
        values[:, here] = ref[0:padded]

    for by, ref in zip(ORDER, got_refs):
        first = jnp.bitwise_xor(own, by) * count
        here = pl.ds(pl.multiple_of(halo + first, LANES), count)
        there = pl.ds(pl.multiple_of(first, LANES), count)
        store_keys(here, ref)
        edge = ref[query_at : query_at + 16].astype(jnp.float32)
        edge = jnp.concatenate([query_marks[:, here], edge[SPARE:]], axis=0)
        queries[0:16, there] = edge.astype(jnp.bfloat16)
        queries[16:padded, there] = ref[query_at + 16 : query_at + padded]
        queries[padded:, there] = blank
    if halo:
        store_keys(slice(0, halo), left_ref)
        store_keys(slice(length - halo, length), right_ref)

    def image_at(position):
        found = jnp.int32(0)
        for image in range(1, images):
            found += (starts[image] <= position).astype(jnp.int32)
        return found

    def following(state):
        at, image = state
        more = image < image_at(halo + at * tile + tile - 1)
        later = jnp.minimum(at + 1, tiles - 1)
        first = jnp.maximum(image_at(halo + later * tile), jnp.where(later == at, image, 0))
        return jnp.where(more, at, later), jnp.where(more, image + 1, first)

    def window_of(image):
        begin = jnp.minimum(starts[image] // LANES * LANES, length - window)
        return pl.ds(pl.multiple_of(begin, LANES), window)

    def score(state, scores, tops):
        at, image = state
        query = queries[:, pl.ds(pl.multiple_of(at * tile, tile), tile)]
        found = jnp.dot(keys[window_of(image), :], query, preferred_element_type=jnp.float32)
        scores[...] = found
        tops[...] = jnp.max(found, axis=0, keepdims=True)

    def weigh(state, scores, tops):
        at, image = state
        first = pl.multiple_of(at * tile, tile)
        labels = ids_ref[:, pl.ds(pl.multiple_of(halo + first, LANES), tile)]
        probs = jnp.exp2((scores[...] - tops[...]) * (size ** (-0.5) * math.log2(math.e)))
        share = 1.0 / jnp.sum(probs, axis=0, keepdims=True)
        weighted = jnp.dot(
            values[:, window_of(image)], probs.astype(jnp.bfloat16), preferred_element_type=jnp.float32
        )
        place = (slice(None), pl.ds(first, tile))
        attended[place] = jnp.where(labels == image, weighted * share, attended[place])

    pairs = jnp.int32(tiles)
    for image in range(1, images):
        offset = starts[image] - halo
        inside = jnp.logical_and(offset > 0, offset < total_rows)
        pairs += jnp.logical_and(inside, lax.rem(offset, tile) != 0).astype(jnp.int32)

    def two_pairs(_, state):
        second = following(state)
        score(second, scores_b, tops_b)
        weigh(state, scores_a, tops_a)
        third = following(second)
        score(third, scores_a, tops_a)
        weigh(second, scores_b, tops_b)
        return third

    begun = (jnp.int32(0), image_at(halo))
    score(begun, scores_a, tops_a)
    last = lax.fori_loop(0, pairs // 2, two_pairs, begun)

    @pl.when(lax.rem(pairs, 2) == 1)
    def _():
        weigh(last, scores_a, tops_a)

    odd_head = lax.rem(lax.axis_index("grp"), 2) == 1
    mine = ids[:, halo : halo + total_rows]

    def placed(block, spare):
        even = jnp.concatenate([block[0:size], spare], axis=0)
        odd = jnp.concatenate([spare, block[0:size]], axis=0)
        return jnp.where(odd_head, odd, even)

    if piggy:
        nothing = jnp.zeros((SPARE, total_rows), jnp.float32)
        flat = placed(attended[...], nothing).astype(jnp.bfloat16)
        pooled = lax.dot_general(
            image_rows(mine, images), flat, (((1,), (1,)), ((), ())), preferred_element_type=jnp.float32
        )
        pooled = split_in_two(pooled, images)
        sums = jnp.zeros((SPARE, 2 * LANES), jnp.float32)
        for ref in got_refs:
            sums += ref[query_at : query_at + 16].astype(jnp.float32)[0:SPARE, 0 : 2 * LANES]
        sums = split_in_two(sums + pltpu.roll(sums, images, axis=0), images)
        spare = jnp.concatenate(
            [pooled, jnp.zeros((SPARE, LANES - padded), jnp.float32), sums], axis=1
        )
    else:
        spare = jnp.zeros((SPARE, count), jnp.float32)
    for source in range(HEADS):
        block = placed(attended[:, source * count : (source + 1) * count], spare)
        out_ref[source] = block.astype(jnp.bfloat16)


def joined_heads(got_ref, out_weight_ref, flat, weight):
    padded = got_ref.shape[1]
    size = padded - SPARE
    spares = []
    for head in range(HEADS):
        at = head * padded
        from_row = head * size - (SPARE if head % 2 else 0)
        weight[at : at + padded] = out_weight_ref[from_row : from_row + padded]
        edge = 0 if head % 2 else padded - 16
        rest = slice(16, padded) if head % 2 else slice(0, padded - 16)
        mixed_rows = got_ref[head, edge : edge + 16].astype(jnp.float32)
        nothing = jnp.zeros((SPARE, mixed_rows.shape[1]), jnp.float32)
        if head % 2:
            spares.append(mixed_rows[:SPARE])
            block = jnp.concatenate([nothing, mixed_rows[SPARE:]], axis=0)
        else:
            spares.append(mixed_rows[SPARE:])
            block = jnp.concatenate([mixed_rows[:SPARE], nothing], axis=0)
        flat[at + edge : at + edge + 16] = block.astype(jnp.bfloat16)
        flat[at + rest.start : at + rest.stop] = got_ref[head, rest]
    return spares


def send_mixed_rows(rows_ref, flat, weight, turned, mixed, mixed_ref, sems):
    turned[...] = flat[...].T
    pieces = sems.shape[0]
    step = rows_ref.shape[0] // pieces
    copies = []
    for piece in range(pieces):
        cut = slice(piece * step, (piece + 1) * step)
        added = jnp.dot(turned[cut, :], weight[...], preferred_element_type=jnp.float32)
        mixed[cut, :] = (rows_ref[cut, :].astype(jnp.float32) + added).astype(jnp.bfloat16)
        copies.append(pltpu.make_async_copy(mixed.at[cut], mixed_ref.at[cut], sems.at[piece]))
        copies[-1].start()
    return copies


def unit_rows(matrix):
    return matrix * lax.rsqrt(jnp.sum(matrix * matrix, axis=1, keepdims=True) + 1e-06)


def losses(cosine, labels):
    logits = -labels * (logit_scale * cosine + logit_bias)
    return jnp.maximum(logits, 0.0) + jnp.log1p(jnp.exp(-jnp.abs(logits)))


def finish_kernel(images, rows_ref, got_ref, out_weight_ref, text_ref, mixed_ref, loss_ref, flat, weight, turned, mixed, sems, pooled_heads):
    padded = got_ref.shape[1]
    spares = joined_heads(got_ref, out_weight_ref, flat, weight)
    copies = send_mixed_rows(rows_ref, flat, weight, turned, mixed, mixed_ref, sems)
    for head in range(HEADS):
        pooled_heads[:, head * padded : (head + 1) * padded] = spares[head][:, 0:padded]
    pooled = jnp.dot(
        pooled_heads[...].astype(jnp.bfloat16), weight[...], preferred_element_type=jnp.float32
    )
    patch_sums = [spare[:, LANES : 2 * LANES] for spare in spares] + [spares[0][:, 2 * LANES :]]
    pooled = pooled + jnp.concatenate(patch_sums, axis=1)
    pooled = pooled + pltpu.roll(pooled, images, axis=0)
    image_vecs = unit_rows(pooled)
    text_vecs = unit_rows(text_ref[...].astype(jnp.float32))
    cosine = lax.dot_general(
        text_vecs,
        image_vecs,
        (((1,), (1,)), ((), ())),
        precision=lax.Precision.HIGHEST,
        preferred_element_type=jnp.float32,
    )
    text = lax.broadcasted_iota(jnp.int32, cosine.shape, 0)
    image = lax.broadcasted_iota(jnp.int32, cosine.shape, 1)
    terms = losses(cosine, jnp.where(text == image, 1.0, -1.0))
    loss_ref[...] = jnp.sum(terms, axis=0, keepdims=True)[:, 0:images]
    for copy in copies:
        copy.wait()


def mix_kernel(rows_ref, got_ref, out_weight_ref, mixed_ref, flat, weight, turned, mixed, sems):
    joined_heads(got_ref, out_weight_ref, flat, weight)
    for copy in send_mixed_rows(rows_ref, flat, weight, turned, mixed, mixed_ref, sems):
        copy.wait()


def in_vmem(count):
    return [pl.BlockSpec(memory_space=pltpu.VMEM)] * count


def in_hbm(value):
    return pltpu.with_memory_space_constraint(value, pltpu.HBM)


def call(kernel, out_shape, scratch, in_specs, flops, out_specs=None):
    if out_specs is None:
        out_specs = jax.tree.map(lambda _: pl.BlockSpec(memory_space=pltpu.VMEM), out_shape)
    return pl.pallas_call(
        kernel,
        out_shape=out_shape,
        in_specs=in_specs,
        out_specs=out_specs,
        scratch_shapes=scratch,
        compiler_params=pltpu.CompilerParams(vmem_limit_bytes=VMEM_LIMIT),
        cost_estimate=pl.CostEstimate(flops=flops, bytes_accessed=8 << 20, transcendentals=0),
    )


def moved(value, axis, pairs):
    return lax.ppermute(value, axis, pairs)


def all_texts(texts):
    peers = lax.axis_size("blk")
    shifts = range(1, peers)
    return [texts] + [moved(texts, "blk", [(i, (i + by) % peers) for i in range(peers)]) for by in shifts]


def exchanged(blocks, groups):
    return lax.all_to_all(blocks, "grp", 0, 0, axis_index_groups=groups, tiled=True)


def local(patches, segment_ids, qkv_weight, out_weight, text_embed):
    rows = patches[0]
    count, depth = rows.shape
    width = out_weight.shape[0]
    size = width // HEADS
    padded = size + SPARE
    images = text_embed.shape[0]
    group_size = lax.axis_size("grp")
    parts = group_size // HEADS
    piggy = parts == 1 and 2 * images == SPARE and count >= depth - (HEADS - 2) * LANES
    groups = None if parts == 1 else [list(range(p * HEADS, (p + 1) * HEADS)) for p in range(parts)]
    bf16, f32 = jnp.bfloat16, jnp.float32
    shape = jax.ShapeDtypeStruct

    block = shape((3 * size + SPARE, count), bf16)
    hbm = pl.BlockSpec(memory_space=pltpu.HBM)
    turned_weight = qkv_weight.T
    normed, sums, *sent = call(
        functools.partial(far_kernel, images, piggy),
        (shape((depth, count), bf16), shape((SPARE, depth), f32), block, block),
        [
            pltpu.VMEM((1, count), jnp.int32),
            pltpu.VMEM((count, depth), bf16),
            pltpu.VMEM((3, 2 * size, depth), bf16),
            pltpu.SemaphoreType.DMA,
            pltpu.SemaphoreType.DMA,
            pltpu.SemaphoreType.DMA((3,)),
        ],
        [hbm] * 3,
        2 * count * depth * 6 * size,
    )(in_hbm(segment_ids), in_hbm(rows), in_hbm(turned_weight))
    sent += call(
        functools.partial(near_kernel, piggy),
        (block,) * 6,
        [],
        in_vmem(3),
        2 * count * depth * 18 * size,
    )(normed, sums, turned_weight)
    sent = dict(zip((6, 7, 2, 3, 4, 5, 0, 1), sent))
    got = []
    for by in ORDER:
        pairs = [(i, i ^ by) for i in range(group_size)]
        got.append(moved(sent[by], "grp", pairs) if by else sent[by])

    length = HEADS * count
    halo = 0
    operands = [segment_ids, *got]
    if parts > 1:
        halo = rounded_up(MAXP - 1, LANES)
        part = lax.axis_index("grp") // HEADS
        whole_ids = jnp.concatenate(
            [
                jnp.full((1, halo), -1, jnp.int32),
                segment_ids,
                jnp.full((1, halo), images, jnp.int32),
            ],
            axis=1,
        )
        near_ids = lax.dynamic_slice_in_dim(whole_ids, part * length, length + 2 * halo, axis=1)
        order = jnp.bitwise_xor(lax.axis_index("grp") % HEADS, jnp.arange(HEADS))
        flat = jnp.stack([got[ORDER.index(by)] for by in range(HEADS)])[order][:, : 2 * size].transpose(1, 0, 2).reshape(2 * size, length)
        flat = jnp.concatenate([flat, jnp.zeros((16, length), bf16)], axis=0)
        ahead = [(i, i + HEADS) for i in range(group_size - HEADS)]
        back = [(i + HEADS, i) for i in range(group_size - HEADS)]
        left = moved(flat[:, length - halo :], "grp", ahead)
        right = moved(flat[:, :halo], "grp", back)
        operands = [near_ids, *got, left, right]
    reach = length + 2 * halo
    window = min(rounded_up(MAXP + LANES - 1, LANES), reach)
    tile = 2 * LANES
    answers = call(
        functools.partial(attend_kernel, images, piggy, halo),
        shape((HEADS, padded, count), bf16),
        [
            pltpu.VMEM((reach, LANES), bf16),
            pltpu.VMEM((padded, reach), bf16),
            pltpu.VMEM((LANES, length), bf16),
            pltpu.VMEM((padded, length), f32),
            pltpu.VMEM((window, tile), f32),
            pltpu.VMEM((window, tile), f32),
            pltpu.VMEM((1, tile), f32),
            pltpu.VMEM((1, tile), f32),
            pltpu.VMEM((2, SPARE, reach), f32),
            pltpu.SMEM((images,), jnp.int32),
        ],
        in_vmem(len(operands)),
        4 * size * length * MAXP,
    )(*operands)
    back_home = exchanged(answers, groups)
    text_embed, _ = lax.optimization_barrier((text_embed, answers))
    texts = jnp.concatenate(all_texts(text_embed), axis=0)

    joined = [
        pltpu.VMEM((HEADS * padded, count), bf16),
        pltpu.VMEM((HEADS * padded, depth), bf16),
        pltpu.VMEM((count, HEADS * padded), bf16),
        pltpu.VMEM((count, depth), bf16),
        pltpu.SemaphoreType.DMA((3,)),
    ]
    flops = 2 * count * depth * width
    if piggy:
        mixed, row_loss = call(
            functools.partial(finish_kernel, images),
            (shape((count, depth), bf16), shape((1, images), f32)),
            joined + [pltpu.VMEM((SPARE, HEADS * padded), f32)],
            in_vmem(4),
            flops,
            (hbm, pl.BlockSpec(memory_space=pltpu.VMEM)),
        )(rows, back_home, out_weight, texts)
        return (mixed[None], row_loss[0])
    mixed = call(mix_kernel, shape((count, depth), bf16), joined, in_vmem(3), flops, hbm)(
        rows, back_home, out_weight
    )
    own_ids = lax.dynamic_slice_in_dim(segment_ids[0], lax.axis_index("grp") * count, count)
    onehot = (own_ids[None, :] == jnp.arange(images, dtype=jnp.int32)[:, None]).astype(bf16)
    pooled = lax.psum(jnp.dot(onehot, mixed, preferred_element_type=f32), "grp")
    text_vecs = unit_rows(texts.astype(f32))
    cosine = jnp.dot(unit_rows(pooled), text_vecs.T, precision=lax.Precision.HIGHEST)
    same = jnp.arange(images)[:, None] == jnp.arange(texts.shape[0])[None, :]
    row_loss = jnp.sum(losses(cosine, jnp.where(same, 1.0, -1.0)), axis=1)
    return (mixed[None], row_loss)


def solution(mesh):
    placed = (P("blk", "grp", None), P("blk", None), P(), P(), P("blk", None))
    return jax.shard_map(
        local,
        mesh=mesh,
        in_specs=placed,
        out_specs=(P("blk", "grp", None), P("blk")),
        check_vma=False,
    )
```

```python
import functools
import math

import jax
import jax.numpy as jnp
from jax import lax
from jax.experimental import pallas as pl
from jax.experimental.pallas import tpu as pltpu
from jax.sharding import PartitionSpec as P

HEADS = 8
MAXP = 1024
LANES = 128
SPARE = 8
HIDDEN = -1e30
NEAR = (2, 4, 3, 5, 1)
FAR = (6, 7)
EARLY = (2, 3, 1, 0)
LATE = (4, 5, 6, 7)
FIRST = (1, 2)
SECOND = (3, 0)

logit_scale = 30.0
logit_bias = -5.0

VMEM_LIMIT = 32 * 1024 * 1024


def rounded_up(value, step):
    return (value + step - 1) // step * step


def split_in_two(total, images):
    row = lax.broadcasted_iota(jnp.int32, total.shape, 0)
    main = total.astype(jnp.bfloat16).astype(jnp.float32)
    return jnp.where(row < images, main, total - main)


def image_rows(ids, images):
    row = lax.broadcasted_iota(jnp.int32, (SPARE, ids.shape[1]), 0)
    return (lax.rem(row, images) == ids).astype(jnp.float32).astype(jnp.bfloat16)


def head_blocks(query, key, value, sums, pair):
    size = query.shape[0] // 2
    count = query.shape[1]
    for place in range(2):
        here = slice(place * size, (place + 1) * size)
        if sums is None:
            spare = jnp.zeros((SPARE, count), jnp.float32)
        else:
            first = pl.multiple_of((2 * pair + place) * LANES, LANES)
            parts = [sums[:, pl.ds(first, LANES)], sums[:, HEADS * LANES :]]
            held = sum(part.shape[1] for part in parts)
            spare = jnp.concatenate(parts + [jnp.zeros((SPARE, count - held), jnp.float32)], axis=1)
        block = jnp.concatenate([value[here], key[here], spare, query[here]], axis=0)
        yield block.astype(jnp.bfloat16)


def store_by_core(core, blocks, same_ref, cross_ref):
    first, second = blocks

    @pl.when(core == 0)
    def _():
        same_ref[...] = first
        cross_ref[...] = second

    @pl.when(core == 1)
    def _():
        same_ref[...] = second
        cross_ref[...] = first


def place_in_group():
    own = lax.rem(lax.axis_index("grp"), HEADS)
    return lax.div(own, 2), lax.rem(own, 2)


def first_kernel(images, piggy, ids_ref, rows_ref, weight_ref, normed_ref, sums_ref, *rest):
    out_refs, rest = rest[: 2 * len(FIRST)], rest[2 * len(FIRST) :]
    own_ids, rows_held, weight, id_sem, row_sem, sems = rest
    count, depth = rows_ref.shape
    width = weight_ref.shape[0] // 3
    wide = weight.shape[1]
    rows_fetch = pltpu.make_async_copy(rows_ref, rows_held, row_sem)
    rows_fetch.start()
    own = pl.multiple_of(lax.axis_index("grp") * count, LANES)
    ids_fetch = pltpu.make_async_copy(ids_ref.at[:, pl.ds(own, count)], own_ids, id_sem)
    ids_fetch.start()
    own_pair, core = place_in_group()
    fetches = []
    for step, move in enumerate(FIRST):
        pair = jnp.bitwise_xor(own_pair, move)
        for at in range(3):
            first = pl.multiple_of(at * width + pair * wide, 16)
            place = 3 * step + at
            fetches.append(
                pltpu.make_async_copy(
                    weight_ref.at[pl.ds(first, wide)], weight.at[place], sems.at[place]
                )
            )
            fetches[-1].start()
    rows_fetch.wait()
    rows = rows_held[...]
    values = rows.astype(jnp.float32)
    center = values - jnp.mean(values, axis=1, keepdims=True)
    spread = jnp.mean(center * center, axis=1, keepdims=True)
    normed = (center * lax.rsqrt(spread + 1e-06)).astype(jnp.bfloat16)
    normed_ref[...] = normed.T
    ids_fetch.wait()
    if piggy:
        sums = jnp.dot(image_rows(own_ids[...], images), rows, preferred_element_type=jnp.float32)
        sums_ref[...] = split_in_two(sums, images)
    for step, move in enumerate(FIRST):
        parts = []
        for place in range(3 * step, 3 * step + 3):
            fetches[place].wait()
            parts.append(
                jnp.dot(weight[place], normed_ref[...], preferred_element_type=jnp.float32)
            )
        blocks = head_blocks(*parts, sums_ref if piggy else None, jnp.bitwise_xor(own_pair, move))
        store_by_core(core, blocks, *out_refs[2 * step : 2 * step + 2])


def second_kernel(piggy, normed_ref, sums_ref, weight_ref, *out_refs):
    width = weight_ref.shape[0] // 3
    wide = 2 * width // HEADS
    own, core = place_in_group()
    for step, move in enumerate(SECOND):
        pair = jnp.bitwise_xor(own, move)
        parts = []
        for at in range(3):
            here = pl.ds(pl.multiple_of(at * width + pair * wide, 16), wide)
            parts.append(
                jnp.dot(weight_ref[here, :], normed_ref[...], preferred_element_type=jnp.float32)
            )
        blocks = head_blocks(*parts, sums_ref if piggy else None, pair)
        store_by_core(core, blocks, *out_refs[2 * step : 2 * step + 2])


def find_starts(images, ids, starts):
    for image in range(images + 1):
        starts[image] = jnp.sum((ids < image).astype(jnp.int32))


def write_marks(images, ids, marks):
    bits = max(1, (images - 1).bit_length())
    row = lax.broadcasted_iota(jnp.int32, (SPARE, ids.shape[1]), 0)
    bit = jnp.bitwise_and(lax.shift_right_logical(jnp.broadcast_to(ids, row.shape), row >> 1), 1)
    odd = jnp.bitwise_and(row, 1)
    used = row < 2 * bits
    outside = jnp.logical_or(ids < 0, ids >= images)
    key_side = jnp.where(odd == 1, bit, 1 - bit).astype(jnp.float32)
    key_side = jnp.where(outside, 1.0, key_side)
    marks[0] = jnp.where(used, key_side * HIDDEN, 0.0)
    marks[1] = jnp.where(used, jnp.where(odd == 1, 1 - bit, bit), 0).astype(jnp.float32)


def store_keys(marked, block_ref, keys, values, here):
    padded = values.shape[0]
    key_at = padded - 2 * SPARE
    block = block_ref[key_at : key_at + padded].astype(jnp.float32)
    nothing = jnp.zeros((LANES - padded, block.shape[1]), jnp.float32)
    full = jnp.concatenate([marked, block[SPARE:], nothing], axis=0)
    keys[here, :] = full.astype(jnp.bfloat16).T
    values[:, here] = block_ref[0:padded]


def store_queries(marked, block_ref, queries, padded, there):
    query_at = 2 * (padded - SPARE)
    edge = block_ref[query_at : query_at + 16].astype(jnp.float32)
    edge = jnp.concatenate([marked, edge[SPARE:]], axis=0)
    queries[0:16, there] = edge.astype(jnp.bfloat16)
    queries[16:padded, there] = block_ref[query_at + 16 : query_at + padded]
    queries[padded:, there] = jnp.zeros((LANES - padded, block_ref.shape[1]), jnp.bfloat16)


def spare_sums(refs, padded):
    query_at = 2 * (padded - SPARE)
    parts = [ref[query_at : query_at + 16].astype(jnp.float32)[0:SPARE, 0 : 2 * LANES] for ref in refs]
    return sum(parts[1:], parts[0])


def image_at(images, starts, position):
    found = jnp.int32(0)
    for image in range(1, images):
        found += (starts[image] <= position).astype(jnp.int32)
    return found


def near_images(images, starts, begin, end):
    first = image_at(images, starts, begin)
    first += (starts[first] < begin).astype(jnp.int32)
    last = image_at(images, starts, end - 1)
    last -= (starts[last + 1] > end).astype(jnp.int32)
    return first, last


def attend_images(images, ids_ref, keys, values, queries, attended, work, starts, bases, low, high, skipped):
    scores_a, scores_b, tops_a, tops_b = work
    key_base, query_base = bases
    window, tile = scores_a.shape
    size = attended.shape[0] - SPARE
    held = queries.shape[1]
    tiles = held // tile

    def bounds(image):
        first = lax.div(jnp.maximum(starts[image] - query_base, 0), tile)
        last = lax.div(jnp.minimum(starts[image + 1] - query_base, held) - 1, tile)
        return jnp.minimum(first, tiles - 1), last

    def after(image):
        later = image + 1
        if skipped is not None:
            jump = jnp.logical_and(later == skipped[0], skipped[0] <= skipped[1])
            later = jnp.where(jump, skipped[1] + 1, later)
        return jnp.clip(later, 0, images - 1)

    def following(state):
        at, image = state
        more = at < bounds(image)[1]
        later = after(image)
        return jnp.where(more, at + 1, bounds(later)[0]), jnp.where(more, image, later)

    def window_of(image):
        begin = lax.div(jnp.maximum(starts[image] - key_base, 0), LANES) * LANES
        return pl.ds(pl.multiple_of(jnp.minimum(begin, keys.shape[0] - window), LANES), window)

    def score(state, scores, tops):
        at, image = state
        query = queries[:, pl.ds(pl.multiple_of(at * tile, tile), tile)]
        found = jnp.dot(keys[window_of(image), :], query, preferred_element_type=jnp.float32)
        scores[...] = found
        tops[...] = jnp.max(found, axis=0, keepdims=True)

    def weigh(state, scores, tops):
        at, image = state
        first = pl.multiple_of(at * tile, tile)
        labels = ids_ref[:, pl.ds(pl.multiple_of(query_base + first, LANES), tile)]
        probs = jnp.exp2((scores[...] - tops[...]) * (size ** (-0.5) * math.log2(math.e)))
        share = 1.0 / jnp.sum(probs, axis=0, keepdims=True)
        weighted = jnp.dot(
            values[:, window_of(image)], probs.astype(jnp.bfloat16), preferred_element_type=jnp.float32
        )
        place = (slice(None), pl.ds(first, tile))
        attended[place] = jnp.where(labels == image, weighted * share, attended[place])

    pairs = jnp.int32(0)
    for image in range(images):
        first, last = bounds(image)
        wanted = jnp.logical_and(low <= image, image <= high)
        if skipped is not None:
            wanted = jnp.logical_and(wanted, jnp.logical_or(image < skipped[0], image > skipped[1]))
        pairs += jnp.where(wanted, last - first + 1, 0)

    def two_pairs(_, state):
        second = following(state)
        score(second, scores_b, tops_b)
        weigh(state, scores_a, tops_a)
        third = following(second)
        score(third, scores_a, tops_a)
        weigh(second, scores_b, tops_b)
        return third

    begin = after(low - 1)
    begun = (bounds(begin)[0], begin)
    score(begun, scores_a, tops_a)
    last_state = lax.fori_loop(0, lax.div(pairs, 2), two_pairs, begun)

    @pl.when(lax.rem(pairs, 2) == 1)
    def _():
        weigh(last_state, scores_a, tops_a)


def early_kernel(images, halo, ids_ref, *rest):
    got_refs, rest = rest[: len(EARLY)], rest[len(EARLY) :]
    keys, values, queries, attended, sums, *work, marks, starts = rest
    count = got_refs[0].shape[1]
    padded = attended.shape[0]
    ids = ids_ref[...]
    find_starts(images, ids, starts)
    write_marks(images, ids, marks)
    own = lax.rem(lax.axis_index("grp"), HEADS)
    half = lax.div(own, len(EARLY)) * (len(EARLY) * count)
    for by, ref in zip(EARLY, got_refs):
        first = jnp.bitwise_xor(own, by) * count
        marked = pl.ds(pl.multiple_of(halo + first, LANES), count)
        here = pl.ds(pl.multiple_of(first - half, LANES), count)
        store_keys(marks[0, :, marked], ref, keys, values, here)
        store_queries(marks[1, :, marked], ref, queries, padded, here)
    sums[...] = spare_sums(got_refs, padded)
    base = halo + half
    low, high = near_images(images, starts, base, base + len(EARLY) * count)
    attend_images(
        images, ids_ref, keys, values, queries, attended, work, starts, (base, base), low, high, None
    )


def late_kernel(images, piggy, halo, ids_ref, *rest):
    near_keys, near_values, near_queries, near_attended, near_sums, *rest = rest
    got_refs, rest = rest[: len(LATE)], rest[len(LATE) :]
    if halo:
        left_ref, right_ref, *rest = rest
    out_ref, keys, values, queries, attended, *work, marks, starts = rest
    count = got_refs[0].shape[1]
    padded = attended.shape[0]
    size = padded - SPARE
    total_rows = HEADS * count
    length = ids_ref.shape[1]
    ids = ids_ref[...]
    find_starts(images, ids, starts)
    write_marks(images, ids, marks)

    own = lax.rem(lax.axis_index("grp"), HEADS)
    half = lax.div(own, len(EARLY)) * (len(EARLY) * count)
    near = pl.ds(pl.multiple_of(half, LANES), len(EARLY) * count)
    near_here = pl.ds(pl.multiple_of(halo + half, LANES), len(EARLY) * count)
    keys[near_here, :] = near_keys[...]
    values[:, near_here] = near_values[...]
    queries[:, near] = near_queries[...]
    attended[:, near] = near_attended[...]
    for by, ref in zip(LATE, got_refs):
        first = jnp.bitwise_xor(own, by) * count
        here = pl.ds(pl.multiple_of(halo + first, LANES), count)
        there = pl.ds(pl.multiple_of(first, LANES), count)
        store_keys(marks[0, :, here], ref, keys, values, here)
        store_queries(marks[1, :, here], ref, queries, padded, there)
    if halo:
        for ref, here in ((left_ref, slice(0, halo)), (right_ref, slice(length - halo, length))):
            store_keys(marks[0, :, here], ref, keys, values, here)
    done = near_images(images, starts, halo + half, halo + half + len(EARLY) * count)
    low = image_at(images, starts, halo)
    high = image_at(images, starts, halo + total_rows - 1)
    attend_images(
        images, ids_ref, keys, values, queries, attended, work, starts, (0, halo), low, high, done
    )

    odd_head = lax.rem(own, 2) == 1
    mine = ids[:, halo : halo + total_rows]

    def placed(block, spare):
        even = jnp.concatenate([block[0:size], spare], axis=0)
        odd = jnp.concatenate([spare, block[0:size]], axis=0)
        return jnp.where(odd_head, odd, even)

    if piggy:
        nothing = jnp.zeros((SPARE, total_rows), jnp.float32)
        flat = placed(attended[...], nothing).astype(jnp.bfloat16)
        pooled = lax.dot_general(
            image_rows(mine, images), flat, (((1,), (1,)), ((), ())), preferred_element_type=jnp.float32
        )
        pooled = split_in_two(pooled, images)
        sums = near_sums[...] + spare_sums(got_refs, padded)
        sums = split_in_two(sums + pltpu.roll(sums, images, axis=0), images)
        spare = jnp.concatenate(
            [pooled, jnp.zeros((SPARE, LANES - padded), jnp.float32), sums], axis=1
        )
    else:
        spare = jnp.zeros((SPARE, count), jnp.float32)
    for source in range(HEADS):
        block = placed(attended[:, source * count : (source + 1) * count], spare)
        out_ref[source] = block.astype(jnp.bfloat16)


def joined_heads(got_ref, out_weight_ref, flat, weight):
    padded = got_ref.shape[1]
    size = padded - SPARE
    spares = []
    for head in range(HEADS):
        at = head * padded
        from_row = head * size - (SPARE if head % 2 else 0)
        weight[at : at + padded] = out_weight_ref[from_row : from_row + padded]
        edge = 0 if head % 2 else padded - 16
        rest = slice(16, padded) if head % 2 else slice(0, padded - 16)
        mixed_rows = got_ref[head, edge : edge + 16].astype(jnp.float32)
        nothing = jnp.zeros((SPARE, mixed_rows.shape[1]), jnp.float32)
        if head % 2:
            spares.append(mixed_rows[:SPARE])
            block = jnp.concatenate([nothing, mixed_rows[SPARE:]], axis=0)
        else:
            spares.append(mixed_rows[SPARE:])
            block = jnp.concatenate([mixed_rows[:SPARE], nothing], axis=0)
        flat[at + edge : at + edge + 16] = block.astype(jnp.bfloat16)
        flat[at + rest.start : at + rest.stop] = got_ref[head, rest]
    return spares


def send_mixed_rows(rows_ref, flat, weight, turned, mixed, mixed_ref, sems):
    turned[...] = flat[...].T
    pieces = sems.shape[0]
    step = rows_ref.shape[0] // pieces
    copies = []
    for piece in range(pieces):
        cut = slice(piece * step, (piece + 1) * step)
        added = jnp.dot(turned[cut, :], weight[...], preferred_element_type=jnp.float32)
        mixed[cut, :] = (rows_ref[cut, :].astype(jnp.float32) + added).astype(jnp.bfloat16)
        copies.append(pltpu.make_async_copy(mixed.at[cut], mixed_ref.at[cut], sems.at[piece]))
        copies[-1].start()
    return copies


def unit_rows(matrix):
    return matrix * lax.rsqrt(jnp.sum(matrix * matrix, axis=1, keepdims=True) + 1e-06)


def losses(cosine, labels):
    logits = -labels * (logit_scale * cosine + logit_bias)
    return jnp.maximum(logits, 0.0) + jnp.log1p(jnp.exp(-jnp.abs(logits)))


def finish_kernel(images, rows_ref, got_ref, out_weight_ref, text_ref, mixed_ref, loss_ref, flat, weight, turned, mixed, sems, pooled_heads):
    padded = got_ref.shape[1]
    spares = joined_heads(got_ref, out_weight_ref, flat, weight)
    copies = send_mixed_rows(rows_ref, flat, weight, turned, mixed, mixed_ref, sems)
    for head in range(HEADS):
        pooled_heads[:, head * padded : (head + 1) * padded] = spares[head][:, 0:padded]
    pooled = jnp.dot(
        pooled_heads[...].astype(jnp.bfloat16), weight[...], preferred_element_type=jnp.float32
    )
    patch_sums = [spare[:, LANES : 2 * LANES] for spare in spares] + [spares[0][:, 2 * LANES :]]
    pooled = pooled + jnp.concatenate(patch_sums, axis=1)
    pooled = pooled + pltpu.roll(pooled, images, axis=0)
    image_vecs = unit_rows(pooled)
    text_vecs = unit_rows(text_ref[...].astype(jnp.float32))
    cosine = lax.dot_general(
        text_vecs,
        image_vecs,
        (((1,), (1,)), ((), ())),
        precision=lax.Precision.HIGHEST,
        preferred_element_type=jnp.float32,
    )
    text = lax.broadcasted_iota(jnp.int32, cosine.shape, 0)
    image = lax.broadcasted_iota(jnp.int32, cosine.shape, 1)
    terms = losses(cosine, jnp.where(text == image, 1.0, -1.0))
    loss_ref[...] = jnp.sum(terms, axis=0, keepdims=True)[:, 0:images]
    for copy in copies:
        copy.wait()


def mix_kernel(rows_ref, got_ref, out_weight_ref, mixed_ref, flat, weight, turned, mixed, sems):
    joined_heads(got_ref, out_weight_ref, flat, weight)
    for copy in send_mixed_rows(rows_ref, flat, weight, turned, mixed, mixed_ref, sems):
        copy.wait()


def in_vmem(count):
    return [pl.BlockSpec(memory_space=pltpu.VMEM)] * count


def in_hbm(value):
    return pltpu.with_memory_space_constraint(value, pltpu.HBM)


def call(kernel, out_shape, scratch, in_specs, flops, out_specs=None):
    if out_specs is None:
        out_specs = jax.tree.map(lambda _: pl.BlockSpec(memory_space=pltpu.VMEM), out_shape)
    return pl.pallas_call(
        kernel,
        out_shape=out_shape,
        in_specs=in_specs,
        out_specs=out_specs,
        scratch_shapes=scratch,
        compiler_params=pltpu.CompilerParams(vmem_limit_bytes=VMEM_LIMIT),
        cost_estimate=pl.CostEstimate(flops=flops, bytes_accessed=8 << 20, transcendentals=0),
    )


def moved(value, axis, pairs):
    return lax.ppermute(value, axis, pairs)


def all_texts(texts):
    peers = lax.axis_size("blk")
    shifts = range(1, peers)
    return [texts] + [moved(texts, "blk", [(i, (i + by) % peers) for i in range(peers)]) for by in shifts]


def exchanged(blocks, groups):
    return lax.all_to_all(blocks, "grp", 0, 0, axis_index_groups=groups, tiled=True)


def local(patches, segment_ids, qkv_weight, out_weight, text_embed):
    rows = patches[0]
    count, depth = rows.shape
    width = out_weight.shape[0]
    size = width // HEADS
    padded = size + SPARE
    images = text_embed.shape[0]
    group_size = lax.axis_size("grp")
    parts = group_size // HEADS
    piggy = parts == 1 and 2 * images == SPARE and count >= depth - (HEADS - 2) * LANES
    groups = None if parts == 1 else [list(range(p * HEADS, (p + 1) * HEADS)) for p in range(parts)]
    bf16, f32 = jnp.bfloat16, jnp.float32
    shape = jax.ShapeDtypeStruct

    block = shape((3 * size + SPARE, count), bf16)
    hbm = pl.BlockSpec(memory_space=pltpu.HBM)
    turned_weight = qkv_weight.T
    normed, sums, *sent = call(
        functools.partial(first_kernel, images, piggy),
        (shape((depth, count), bf16), shape((SPARE, depth), f32)) + (block,) * (2 * len(FIRST)),
        [
            pltpu.VMEM((1, count), jnp.int32),
            pltpu.VMEM((count, depth), bf16),
            pltpu.VMEM((3 * len(FIRST), 2 * size, depth), bf16),
            pltpu.SemaphoreType.DMA,
            pltpu.SemaphoreType.DMA,
            pltpu.SemaphoreType.DMA((3 * len(FIRST),)),
        ],
        [hbm] * 3,
        2 * count * depth * 6 * size * len(FIRST),
    )(in_hbm(segment_ids), in_hbm(rows), in_hbm(turned_weight))
    sent += call(
        functools.partial(second_kernel, piggy),
        (block,) * (2 * len(SECOND)),
        [],
        in_vmem(3),
        2 * count * depth * 6 * size * len(SECOND),
    )(normed, sums, turned_weight)
    sent = dict(zip([2 * move + cross for move in FIRST + SECOND for cross in range(2)], sent))
    got = {0: sent[0]}
    for by in NEAR + FAR:
        got[by] = moved(sent[by], "grp", [(i, i ^ by) for i in range(group_size)])
    got.update(zip(NEAR, lax.optimization_barrier(tuple(got[by] for by in NEAR))))

    length = HEADS * count
    halo = 0
    near_ids = segment_ids
    halos = []
    if parts > 1:
        halo = rounded_up(MAXP - 1, LANES)
        part = lax.axis_index("grp") // HEADS
        whole_ids = jnp.concatenate(
            [
                jnp.full((1, halo), -1, jnp.int32),
                segment_ids,
                jnp.full((1, halo), images, jnp.int32),
            ],
            axis=1,
        )
        near_ids = lax.dynamic_slice_in_dim(whole_ids, part * length, length + 2 * halo, axis=1)
        order = jnp.bitwise_xor(lax.axis_index("grp") % HEADS, jnp.arange(HEADS))
        flat = jnp.stack([got[by] for by in range(HEADS)])[order][:, : 2 * size].transpose(1, 0, 2).reshape(2 * size, length)
        flat = jnp.concatenate([flat, jnp.zeros((16, length), bf16)], axis=0)
        ahead = [(i, i + HEADS) for i in range(group_size - HEADS)]
        back = [(i + HEADS, i) for i in range(group_size - HEADS)]
        left = moved(flat[:, length - halo :], "grp", ahead)
        right = moved(flat[:, :halo], "grp", back)
        halos = [left, right]
    reach = length + 2 * halo
    window = min(rounded_up(MAXP + LANES - 1, LANES), reach)
    tile = 2 * LANES
    work = [
        pltpu.VMEM((window, tile), f32),
        pltpu.VMEM((window, tile), f32),
        pltpu.VMEM((1, tile), f32),
        pltpu.VMEM((1, tile), f32),
        pltpu.VMEM((2, SPARE, reach), f32),
        pltpu.SMEM((images + 1,), jnp.int32),
    ]
    half = len(EARLY) * count
    early = call(
        functools.partial(early_kernel, images, halo),
        (
            shape((half, LANES), bf16),
            shape((padded, half), bf16),
            shape((LANES, half), bf16),
            shape((padded, half), f32),
            shape((SPARE, 2 * LANES), f32),
        ),
        work,
        in_vmem(1 + len(EARLY)),
        4 * size * half * MAXP,
    )(near_ids, *[got[by] for by in EARLY])
    operands = [near_ids, *early, *[got[by] for by in LATE], *halos]
    answers = call(
        functools.partial(late_kernel, images, piggy, halo),
        shape((HEADS, padded, count), bf16),
        [
            pltpu.VMEM((reach, LANES), bf16),
            pltpu.VMEM((padded, reach), bf16),
            pltpu.VMEM((LANES, length), bf16),
            pltpu.VMEM((padded, length), f32),
        ]
        + work,
        in_vmem(len(operands)),
        4 * size * length * MAXP,
    )(*operands)
    back_home = exchanged(answers, groups)
    text_embed, _ = lax.optimization_barrier((text_embed, answers))
    texts = jnp.concatenate(all_texts(text_embed), axis=0)

    joined = [
        pltpu.VMEM((HEADS * padded, count), bf16),
        pltpu.VMEM((HEADS * padded, depth), bf16),
        pltpu.VMEM((count, HEADS * padded), bf16),
        pltpu.VMEM((count, depth), bf16),
        pltpu.SemaphoreType.DMA((3,)),
    ]
    flops = 2 * count * depth * width
    if piggy:
        mixed, row_loss = call(
            functools.partial(finish_kernel, images),
            (shape((count, depth), bf16), shape((1, images), f32)),
            joined + [pltpu.VMEM((SPARE, HEADS * padded), f32)],
            in_vmem(4),
            flops,
            (hbm, pl.BlockSpec(memory_space=pltpu.VMEM)),
        )(rows, back_home, out_weight, texts)
        return (mixed[None], row_loss[0])
    mixed = call(mix_kernel, shape((count, depth), bf16), joined, in_vmem(3), flops, hbm)(
        rows, back_home, out_weight
    )
    own_ids = lax.dynamic_slice_in_dim(segment_ids[0], lax.axis_index("grp") * count, count)
    onehot = (own_ids[None, :] == jnp.arange(images, dtype=jnp.int32)[:, None]).astype(bf16)
    pooled = lax.psum(jnp.dot(onehot, mixed, preferred_element_type=f32), "grp")
    text_vecs = unit_rows(texts.astype(f32))
    cosine = jnp.dot(unit_rows(pooled), text_vecs.T, precision=lax.Precision.HIGHEST)
    same = jnp.arange(images)[:, None] == jnp.arange(texts.shape[0])[None, :]
    row_loss = jnp.sum(losses(cosine, jnp.where(same, 1.0, -1.0)), axis=1)
    return (mixed[None], row_loss)


def solution(mesh):
    placed = (P("blk", "grp", None), P("blk", None), P(), P(), P("blk", None))
    return jax.shard_map(
        local,
        mesh=mesh,
        in_specs=placed,
        out_specs=(P("blk", "grp", None), P("blk")),
        check_vma=False,
    )
```

```python
import functools
import math

import jax
import jax.numpy as jnp
from jax import lax
from jax.experimental import pallas as pl
from jax.experimental.pallas import tpu as pltpu
from jax.sharding import PartitionSpec as P

HEADS = 8
MAXP = 1024
LANES = 128
SPARE = 8
SIZE = 72
PADDED = SIZE + SPARE
KEY_AT = SIZE - SPARE
QUERY_AT = 2 * SIZE
HIDDEN = -1e30
ORDER = (6, 7, 2, 4, 3, 5, 1, 0)
EARLY = (6, 7, 1, 0)
LATE = (2, 4, 3, 5)

logit_scale = 30.0
logit_bias = -5.0

VMEM_LIMIT = 32 * 1024 * 1024


def rounded_up(value, step):
    return (value + step - 1) // step * step


def split_in_two(total, images):
    row = lax.broadcasted_iota(jnp.int32, total.shape, 0)
    main = total.astype(jnp.bfloat16).astype(jnp.float32)
    return jnp.where(row < images, main, total - main)


def image_rows(ids, images):
    row = lax.broadcasted_iota(jnp.int32, (SPARE, ids.shape[1]), 0)
    return (lax.rem(row, images) == ids).astype(jnp.float32).astype(jnp.bfloat16)


def head_blocks(query, key, value, sums, pair):
    size = query.shape[0] // 2
    count = query.shape[1]
    for place in range(2):
        here = slice(place * size, (place + 1) * size)
        if sums is None:
            spare = jnp.zeros((SPARE, count), jnp.float32)
        else:
            first = pl.multiple_of((2 * pair + place) * LANES, LANES)
            parts = [sums[:, pl.ds(first, LANES)], sums[:, HEADS * LANES :]]
            held = sum(part.shape[1] for part in parts)
            spare = jnp.concatenate(parts + [jnp.zeros((SPARE, count - held), jnp.float32)], axis=1)
        block = jnp.concatenate([value[here], key[here], spare, query[here]], axis=0)
        yield block.astype(jnp.bfloat16)


def store_by_core(core, blocks, same_ref, cross_ref):
    first, second = blocks

    @pl.when(core == 0)
    def _():
        same_ref[...] = first
        cross_ref[...] = second

    @pl.when(core == 1)
    def _():
        same_ref[...] = second
        cross_ref[...] = first


def place_in_group():
    own = lax.rem(lax.axis_index("grp"), HEADS)
    return lax.div(own, 2), lax.rem(own, 2)


def far_kernel(images, piggy, ids_ref, rows_ref, weight_ref, normed_ref, sums_ref, same_ref, cross_ref, own_ids, rows_held, weight, id_sem, row_sem, sems):
    count, depth = rows_ref.shape
    width = weight_ref.shape[0] // 3
    wide = weight.shape[1]
    rows_fetch = pltpu.make_async_copy(rows_ref, rows_held, row_sem)
    rows_fetch.start()
    own = pl.multiple_of(lax.axis_index("grp") * count, LANES)
    ids_fetch = pltpu.make_async_copy(ids_ref.at[:, pl.ds(own, count)], own_ids, id_sem)
    ids_fetch.start()
    pair, core = place_in_group()
    pair = jnp.bitwise_xor(pair, 3)
    fetches = []
    for at in range(3):
        first = pl.multiple_of(at * width + pair * wide, 16)
        fetches.append(pltpu.make_async_copy(weight_ref.at[pl.ds(first, wide)], weight.at[at], sems.at[at]))
    for fetch in fetches:
        fetch.start()
    rows_fetch.wait()
    rows = rows_held[...]
    values = rows.astype(jnp.float32)
    center = values - jnp.mean(values, axis=1, keepdims=True)
    spread = jnp.mean(center * center, axis=1, keepdims=True)
    normed = (center * lax.rsqrt(spread + 1e-06)).astype(jnp.bfloat16)
    normed_ref[...] = normed.T
    ids_fetch.wait()
    if piggy:
        sums = jnp.dot(image_rows(own_ids[...], images), rows, preferred_element_type=jnp.float32)
        sums_ref[...] = split_in_two(sums, images)
    for fetch in fetches:
        fetch.wait()
    parts = [
        jnp.dot(weight[at], normed_ref[...], preferred_element_type=jnp.float32) for at in range(3)
    ]
    store_by_core(core, head_blocks(*parts, sums_ref if piggy else None, pair), same_ref, cross_ref)


def near_kernel(piggy, normed_ref, sums_ref, weight_ref, *out_refs):
    width = weight_ref.shape[0] // 3
    wide = 2 * width // HEADS
    own, core = place_in_group()
    for step, move in enumerate((1, 2, 0)):
        pair = jnp.bitwise_xor(own, move)
        parts = []
        for at in range(3):
            here = pl.ds(pl.multiple_of(at * width + pair * wide, 16), wide)
            parts.append(
                jnp.dot(weight_ref[here, :], normed_ref[...], preferred_element_type=jnp.float32)
            )
        blocks = head_blocks(*parts, sums_ref if piggy else None, pair)
        store_by_core(core, blocks, *out_refs[2 * step : 2 * step + 2])


def find_starts(images, ids, starts):
    for image in range(images + 1):
        starts[image] = jnp.sum((ids < image).astype(jnp.int32))


def write_marks(images, ids, marks):
    bits = max(1, (images - 1).bit_length())
    row = lax.broadcasted_iota(jnp.int32, (SPARE, ids.shape[1]), 0)
    bit = jnp.bitwise_and(lax.shift_right_logical(jnp.broadcast_to(ids, row.shape), row >> 1), 1)
    odd = jnp.bitwise_and(row, 1)
    used = row < 2 * bits
    outside = jnp.logical_or(ids < 0, ids >= images)
    key_side = jnp.where(odd == 1, bit, 1 - bit).astype(jnp.float32)
    key_side = jnp.where(outside, 1.0, key_side)
    marks[0] = jnp.where(used, key_side * HIDDEN, 0.0)
    marks[1] = jnp.where(used, jnp.where(odd == 1, 1 - bit, bit), 0).astype(jnp.float32)


def spare_sums(refs):
    parts = [ref[QUERY_AT : QUERY_AT + 16].astype(jnp.float32)[0:SPARE, 0 : 2 * LANES] for ref in refs]
    return sum(parts[1:], parts[0])


def image_at(images, starts, position):
    found = jnp.int32(0)
    for image in range(1, images):
        found += (starts[image] <= position).astype(jnp.int32)
    return found


def attend_images(images, ids_ref, keys, values, queries, attended, work, starts, halo):
    scores_a, scores_b, tops_a, tops_b = work
    query_base = halo
    window, tile = scores_a.shape
    size = attended.shape[0] - SPARE
    held = queries.shape[1]
    tiles = held // tile

    def bounds(image):
        first = lax.div(jnp.maximum(starts[image] - query_base, 0), tile)
        last = lax.div(jnp.minimum(starts[image + 1] - query_base, held) - 1, tile)
        return jnp.minimum(first, tiles - 1), last

    def after(image):
        return jnp.minimum(image + 1, images - 1)

    def following(state):
        at, image = state
        more = at < bounds(image)[1]
        later = after(image)
        return jnp.where(more, at + 1, bounds(later)[0]), jnp.where(more, image, later)

    def window_of(image):
        begin = lax.div(starts[image], LANES) * LANES
        return pl.ds(pl.multiple_of(jnp.minimum(begin, keys.shape[0] - window), LANES), window)

    def score(state, scores, tops):
        at, image = state
        query = queries[:, pl.ds(pl.multiple_of(at * tile, tile), tile)]
        found = jnp.dot(keys[window_of(image), :], query, preferred_element_type=jnp.float32)
        scores[...] = found
        tops[...] = jnp.max(found, axis=0, keepdims=True)

    def weigh(state, scores, tops):
        at, image = state
        first = pl.multiple_of(at * tile, tile)
        labels = ids_ref[:, pl.ds(pl.multiple_of(query_base + first, LANES), tile)]
        probs = jnp.exp2((scores[...] - tops[...]) * (size ** (-0.5) * math.log2(math.e)))
        weighted = jnp.dot(
            values[:, window_of(image)], probs.astype(jnp.bfloat16), preferred_element_type=jnp.float32
        )
        share = 1.0 / weighted[size : size + 1]
        place = (slice(None), pl.ds(first, tile))
        attended[place] = jnp.where(labels == image, weighted * share, attended[place])

    low = image_at(images, starts, query_base)
    high = image_at(images, starts, query_base + held - 1)
    pairs = jnp.int32(0)
    for image in range(images):
        first, last = bounds(image)
        wanted = jnp.logical_and(low <= image, image <= high)
        pairs += jnp.where(wanted, last - first + 1, 0)

    def two_pairs(_, state):
        second = following(state)
        score(second, scores_b, tops_b)
        weigh(state, scores_a, tops_a)
        third = following(second)
        score(third, scores_a, tops_a)
        weigh(second, scores_b, tops_b)
        return third

    begun = (jnp.int32(0), low)
    score(begun, scores_a, tops_a)
    last_state = lax.fori_loop(0, lax.div(pairs, 2), two_pairs, begun)

    @pl.when(lax.rem(pairs, 2) == 1)
    def _():
        weigh(last_state, scores_a, tops_a)


def turned_keys(marked, block_ref):
    block = block_ref[KEY_AT : KEY_AT + PADDED].astype(jnp.float32)
    nothing = jnp.zeros((LANES - PADDED, block.shape[1]), jnp.float32)
    full = jnp.concatenate([marked, block[SPARE:], nothing], axis=0)
    return full.astype(jnp.bfloat16).T


def store_queries(marked, block_ref, queries, there):
    edge = block_ref[QUERY_AT : QUERY_AT + 16].astype(jnp.float32)
    edge = jnp.concatenate([marked, edge[SPARE:]], axis=0)
    queries[0:16, there] = edge.astype(jnp.bfloat16)
    queries[16:PADDED, there] = block_ref[QUERY_AT + 16 : QUERY_AT + PADDED]
    queries[PADDED:, there] = jnp.zeros((LANES - PADDED, block_ref.shape[1]), jnp.bfloat16)


def store_values(block_ref, values, here):
    edge = block_ref[PADDED - 16 : PADDED].astype(jnp.float32)
    ones = jnp.ones((SPARE, edge.shape[1]), jnp.float32)
    values[0 : PADDED - 16, here] = block_ref[0 : PADDED - 16]
    values[PADDED - 16 : PADDED, here] = jnp.concatenate([edge[:SPARE], ones], axis=0).astype(jnp.bfloat16)


def prepare_kernel(images, halo, ids_ref, *rest):
    got_refs, (keys, marks) = rest[: len(EARLY)], rest[len(EARLY) :]
    count = got_refs[0].shape[1]
    write_marks(images, ids_ref[...], marks)
    own = lax.rem(lax.axis_index("grp"), HEADS)
    for step, (by, ref) in enumerate(zip(EARLY, got_refs)):
        first = jnp.bitwise_xor(own, by) * count
        here = pl.ds(pl.multiple_of(halo + first, LANES), count)
        keys[step * count : (step + 1) * count, :] = turned_keys(marks[0, :, here], ref)


def attend_kernel(images, piggy, halo, ids_ref, marks, early_keys, *rest):
    got_refs, rest = rest[:HEADS], rest[HEADS:]
    if halo:
        left_ref, right_ref, *rest = rest
    out_ref, keys, values, queries, attended, *work, starts = rest
    count = got_refs[0].shape[1]
    padded = attended.shape[0]
    size = padded - SPARE
    total_rows = HEADS * count
    length = ids_ref.shape[1]
    ids = ids_ref[...]
    find_starts(images, ids, starts)

    own = lax.rem(lax.axis_index("grp"), HEADS)
    for step, (by, ref) in enumerate(zip(EARLY + LATE, got_refs)):
        first = jnp.bitwise_xor(own, by) * count
        here = pl.ds(pl.multiple_of(halo + first, LANES), count)
        there = pl.ds(pl.multiple_of(first, LANES), count)
        if by in EARLY:
            keys[here, :] = early_keys[step * count : (step + 1) * count, :]
        else:
            keys[here, :] = turned_keys(marks[0, :, here], ref)
        store_values(ref, values, here)
        store_queries(marks[1, :, here], ref, queries, there)
    if halo:
        for ref, here in ((left_ref, slice(0, halo)), (right_ref, slice(length - halo, length))):
            keys[here, :] = turned_keys(marks[0, :, here], ref)
            store_values(ref, values, here)
    attend_images(images, ids_ref, keys, values, queries, attended, work, starts, halo)

    odd_head = lax.rem(own, 2) == 1
    mine = ids[:, halo : halo + total_rows]

    def placed(block, spare):
        even = jnp.concatenate([block[0:size], spare], axis=0)
        odd = jnp.concatenate([spare, block[0:size]], axis=0)
        return jnp.where(odd_head, odd, even)

    if piggy:
        nothing = jnp.zeros((SPARE, total_rows), jnp.float32)
        flat = placed(attended[...], nothing).astype(jnp.bfloat16)
        pooled = lax.dot_general(
            image_rows(mine, images), flat, (((1,), (1,)), ((), ())), preferred_element_type=jnp.float32
        )
        pooled = split_in_two(pooled, images)
        sums = spare_sums(got_refs)
        sums = split_in_two(sums + pltpu.roll(sums, images, axis=0), images)
        spare = jnp.concatenate(
            [pooled, jnp.zeros((SPARE, LANES - padded), jnp.float32), sums], axis=1
        )
    else:
        spare = jnp.zeros((SPARE, count), jnp.float32)
    for source in range(HEADS):
        block = placed(attended[:, source * count : (source + 1) * count], spare)
        out_ref[source] = block.astype(jnp.bfloat16)


def joined_heads(got_ref, out_weight_ref, flat, weight):
    padded = got_ref.shape[1]
    size = padded - SPARE
    spares = []
    for head in range(HEADS):
        at = head * padded
        from_row = head * size - (SPARE if head % 2 else 0)
        weight[at : at + padded] = out_weight_ref[from_row : from_row + padded]
        edge = 0 if head % 2 else padded - 16
        rest = slice(16, padded) if head % 2 else slice(0, padded - 16)
        mixed_rows = got_ref[head, edge : edge + 16].astype(jnp.float32)
        nothing = jnp.zeros((SPARE, mixed_rows.shape[1]), jnp.float32)
        if head % 2:
            spares.append(mixed_rows[:SPARE])
            block = jnp.concatenate([nothing, mixed_rows[SPARE:]], axis=0)
        else:
            spares.append(mixed_rows[SPARE:])
            block = jnp.concatenate([mixed_rows[:SPARE], nothing], axis=0)
        flat[at + edge : at + edge + 16] = block.astype(jnp.bfloat16)
        flat[at + rest.start : at + rest.stop] = got_ref[head, rest]
    return spares


def send_mixed_rows(rows_ref, flat, weight, turned, mixed, mixed_ref, sems):
    turned[...] = flat[...].T
    pieces = sems.shape[0]
    step = rows_ref.shape[0] // pieces
    copies = []
    for piece in range(pieces):
        cut = slice(piece * step, (piece + 1) * step)
        added = jnp.dot(turned[cut, :], weight[...], preferred_element_type=jnp.float32)
        mixed[cut, :] = (rows_ref[cut, :].astype(jnp.float32) + added).astype(jnp.bfloat16)
        copies.append(pltpu.make_async_copy(mixed.at[cut], mixed_ref.at[cut], sems.at[piece]))
        copies[-1].start()
    return copies


def unit_rows(matrix):
    return matrix * lax.rsqrt(jnp.sum(matrix * matrix, axis=1, keepdims=True) + 1e-06)


def losses(cosine, labels):
    logits = -labels * (logit_scale * cosine + logit_bias)
    return jnp.maximum(logits, 0.0) + jnp.log1p(jnp.exp(-jnp.abs(logits)))


def finish_kernel(images, rows_ref, got_ref, out_weight_ref, text_ref, mixed_ref, loss_ref, flat, weight, turned, mixed, sems, pooled_heads):
    padded = got_ref.shape[1]
    spares = joined_heads(got_ref, out_weight_ref, flat, weight)
    copies = send_mixed_rows(rows_ref, flat, weight, turned, mixed, mixed_ref, sems)
    for head in range(HEADS):
        pooled_heads[:, head * padded : (head + 1) * padded] = spares[head][:, 0:padded]
    pooled = jnp.dot(
        pooled_heads[...].astype(jnp.bfloat16), weight[...], preferred_element_type=jnp.float32
    )
    patch_sums = [spare[:, LANES : 2 * LANES] for spare in spares] + [spares[0][:, 2 * LANES :]]
    pooled = pooled + jnp.concatenate(patch_sums, axis=1)
    pooled = pooled + pltpu.roll(pooled, images, axis=0)
    image_vecs = unit_rows(pooled)
    text_vecs = unit_rows(text_ref[...].astype(jnp.float32))
    cosine = lax.dot_general(
        text_vecs,
        image_vecs,
        (((1,), (1,)), ((), ())),
        precision=lax.Precision.HIGHEST,
        preferred_element_type=jnp.float32,
    )
    text = lax.broadcasted_iota(jnp.int32, cosine.shape, 0)
    image = lax.broadcasted_iota(jnp.int32, cosine.shape, 1)
    terms = losses(cosine, jnp.where(text == image, 1.0, -1.0))
    loss_ref[...] = jnp.sum(terms, axis=0, keepdims=True)[:, 0:images]
    for copy in copies:
        copy.wait()


def mix_kernel(rows_ref, got_ref, out_weight_ref, mixed_ref, flat, weight, turned, mixed, sems):
    joined_heads(got_ref, out_weight_ref, flat, weight)
    for copy in send_mixed_rows(rows_ref, flat, weight, turned, mixed, mixed_ref, sems):
        copy.wait()


def in_vmem(count):
    return [pl.BlockSpec(memory_space=pltpu.VMEM)] * count


def in_hbm(value):
    return pltpu.with_memory_space_constraint(value, pltpu.HBM)


def call(kernel, out_shape, scratch, in_specs, flops, out_specs=None):
    if out_specs is None:
        out_specs = jax.tree.map(lambda _: pl.BlockSpec(memory_space=pltpu.VMEM), out_shape)
    return pl.pallas_call(
        kernel,
        out_shape=out_shape,
        in_specs=in_specs,
        out_specs=out_specs,
        scratch_shapes=scratch,
        compiler_params=pltpu.CompilerParams(vmem_limit_bytes=VMEM_LIMIT),
        cost_estimate=pl.CostEstimate(flops=flops, bytes_accessed=8 << 20, transcendentals=0),
    )


def moved(value, axis, pairs):
    return lax.ppermute(value, axis, pairs)


def all_texts(texts):
    peers = lax.axis_size("blk")
    shifts = range(1, peers)
    return [texts] + [moved(texts, "blk", [(i, (i + by) % peers) for i in range(peers)]) for by in shifts]


def exchanged(blocks, groups):
    return lax.all_to_all(blocks, "grp", 0, 0, axis_index_groups=groups, tiled=True)


def local(patches, segment_ids, qkv_weight, out_weight, text_embed):
    rows = patches[0]
    count, depth = rows.shape
    width = out_weight.shape[0]
    size = width // HEADS
    padded = size + SPARE
    images = text_embed.shape[0]
    group_size = lax.axis_size("grp")
    parts = group_size // HEADS
    piggy = parts == 1 and 2 * images == SPARE and count >= depth - (HEADS - 2) * LANES
    groups = None if parts == 1 else [list(range(p * HEADS, (p + 1) * HEADS)) for p in range(parts)]
    bf16, f32 = jnp.bfloat16, jnp.float32
    shape = jax.ShapeDtypeStruct

    block = shape((3 * size + SPARE, count), bf16)
    hbm = pl.BlockSpec(memory_space=pltpu.HBM)
    turned_weight = qkv_weight.T
    normed, sums, *sent = call(
        functools.partial(far_kernel, images, piggy),
        (shape((depth, count), bf16), shape((SPARE, depth), f32), block, block),
        [
            pltpu.VMEM((1, count), jnp.int32),
            pltpu.VMEM((count, depth), bf16),
            pltpu.VMEM((3, 2 * size, depth), bf16),
            pltpu.SemaphoreType.DMA,
            pltpu.SemaphoreType.DMA,
            pltpu.SemaphoreType.DMA((3,)),
        ],
        [hbm] * 3,
        2 * count * depth * 6 * size,
    )(in_hbm(segment_ids), in_hbm(rows), in_hbm(turned_weight))
    sent += call(
        functools.partial(near_kernel, piggy),
        (block,) * 6,
        [],
        in_vmem(3),
        2 * count * depth * 18 * size,
    )(normed, sums, turned_weight)
    sent = dict(zip((6, 7, 2, 3, 4, 5, 0, 1), sent))
    got = {0: sent[0]}
    for by in ORDER[:-1]:
        got[by] = moved(sent[by], "grp", [(i, i ^ by) for i in range(group_size)])

    length = HEADS * count
    halo = 0
    near_ids = segment_ids
    halos = []
    if parts > 1:
        halo = rounded_up(MAXP - 1, LANES)
        part = lax.axis_index("grp") // HEADS
        whole_ids = jnp.concatenate(
            [
                jnp.full((1, halo), -1, jnp.int32),
                segment_ids,
                jnp.full((1, halo), images, jnp.int32),
            ],
            axis=1,
        )
        near_ids = lax.dynamic_slice_in_dim(whole_ids, part * length, length + 2 * halo, axis=1)
        order = jnp.bitwise_xor(lax.axis_index("grp") % HEADS, jnp.arange(HEADS))
        flat = jnp.stack([got[by] for by in range(HEADS)])[order][:, : 2 * size].transpose(1, 0, 2).reshape(2 * size, length)
        flat = jnp.concatenate([flat, jnp.zeros((16, length), bf16)], axis=0)
        ahead = [(i, i + HEADS) for i in range(group_size - HEADS)]
        back = [(i + HEADS, i) for i in range(group_size - HEADS)]
        left = moved(flat[:, length - halo :], "grp", ahead)
        right = moved(flat[:, :halo], "grp", back)
        halos = [left, right]
    reach = length + 2 * halo
    window = min(rounded_up(MAXP + LANES - 1, LANES), reach)
    tile = 2 * LANES
    early_keys, marks = call(
        functools.partial(prepare_kernel, images, halo),
        (shape((len(EARLY) * count, LANES), bf16), shape((2, SPARE, reach), f32)),
        [],
        in_vmem(1 + len(EARLY)),
        1 << 30,
    )(near_ids, *[got[by] for by in EARLY])
    operands = [near_ids, marks, early_keys, *[got[by] for by in EARLY + LATE], *halos]
    answers = call(
        functools.partial(attend_kernel, images, piggy, halo),
        shape((HEADS, padded, count), bf16),
        [
            pltpu.VMEM((reach, LANES), bf16),
            pltpu.VMEM((padded, reach), bf16),
            pltpu.VMEM((LANES, length), bf16),
            pltpu.VMEM((padded, length), f32),
            pltpu.VMEM((window, tile), f32),
            pltpu.VMEM((window, tile), f32),
            pltpu.VMEM((1, tile), f32),
            pltpu.VMEM((1, tile), f32),
            pltpu.SMEM((images + 1,), jnp.int32),
        ],
        in_vmem(len(operands)),
        4 * size * length * MAXP,
    )(*operands)
    back_home = exchanged(answers, groups)
    text_embed, _ = lax.optimization_barrier((text_embed, answers))
    texts = jnp.concatenate(all_texts(text_embed), axis=0)

    joined = [
        pltpu.VMEM((HEADS * padded, count), bf16),
        pltpu.VMEM((HEADS * padded, depth), bf16),
        pltpu.VMEM((count, HEADS * padded), bf16),
        pltpu.VMEM((count, depth), bf16),
        pltpu.SemaphoreType.DMA((3,)),
    ]
    flops = 2 * count * depth * width
    if piggy:
        mixed, row_loss = call(
            functools.partial(finish_kernel, images),
            (shape((count, depth), bf16), shape((1, images), f32)),
            joined + [pltpu.VMEM((SPARE, HEADS * padded), f32)],
            in_vmem(4),
            flops,
            (hbm, pl.BlockSpec(memory_space=pltpu.VMEM)),
        )(rows, back_home, out_weight, texts)
        return (mixed[None], row_loss[0])
    mixed = call(mix_kernel, shape((count, depth), bf16), joined, in_vmem(3), flops, hbm)(
        rows, back_home, out_weight
    )
    own_ids = lax.dynamic_slice_in_dim(segment_ids[0], lax.axis_index("grp") * count, count)
    onehot = (own_ids[None, :] == jnp.arange(images, dtype=jnp.int32)[:, None]).astype(bf16)
    pooled = lax.psum(jnp.dot(onehot, mixed, preferred_element_type=f32), "grp")
    text_vecs = unit_rows(texts.astype(f32))
    cosine = jnp.dot(unit_rows(pooled), text_vecs.T, precision=lax.Precision.HIGHEST)
    same = jnp.arange(images)[:, None] == jnp.arange(texts.shape[0])[None, :]
    row_loss = jnp.sum(losses(cosine, jnp.where(same, 1.0, -1.0)), axis=1)
    return (mixed[None], row_loss)


def solution(mesh):
    placed = (P("blk", "grp", None), P("blk", None), P(), P(), P("blk", None))
    return jax.shard_map(
        local,
        mesh=mesh,
        in_specs=placed,
        out_specs=(P("blk", "grp", None), P("blk")),
        check_vma=False,
    )
```

```python
import functools
import math

import jax
import jax.numpy as jnp
from jax import lax
from jax.experimental import pallas as pl
from jax.experimental.pallas import tpu as pltpu
from jax.sharding import PartitionSpec as P

HEADS = 8
MAXP = 1024
LANES = 128
SPARE = 8
SIZE = 72
PADDED = SIZE + SPARE
KEY_AT = SIZE - SPARE
QUERY_AT = 2 * SIZE
HIDDEN = -1e30
ORDER = (6, 7, 2, 4, 3, 5, 1, 0)
EARLY = (6, 7, 1, 0)
LATE = (2, 4, 3, 5)

logit_scale = 30.0
logit_bias = -5.0

VMEM_LIMIT = 32 * 1024 * 1024


def rounded_up(value, step):
    return (value + step - 1) // step * step


def split_in_two(total, images):
    row = lax.broadcasted_iota(jnp.int32, total.shape, 0)
    main = total.astype(jnp.bfloat16).astype(jnp.float32)
    return jnp.where(row < images, main, total - main)


def image_rows(ids, images):
    row = lax.broadcasted_iota(jnp.int32, (SPARE, ids.shape[1]), 0)
    return (lax.rem(row, images) == ids).astype(jnp.float32).astype(jnp.bfloat16)


def head_blocks(query, key, value, sums, pair):
    size = query.shape[0] // 2
    count = query.shape[1]
    for place in range(2):
        here = slice(place * size, (place + 1) * size)
        if sums is None:
            spare = jnp.zeros((SPARE, count), jnp.float32)
        else:
            first = pl.multiple_of((2 * pair + place) * LANES, LANES)
            parts = [sums[:, pl.ds(first, LANES)], sums[:, HEADS * LANES :]]
            held = sum(part.shape[1] for part in parts)
            spare = jnp.concatenate(parts + [jnp.zeros((SPARE, count - held), jnp.float32)], axis=1)
        block = jnp.concatenate([value[here], key[here], spare, query[here]], axis=0)
        yield block.astype(jnp.bfloat16)


def store_by_core(core, blocks, same_ref, cross_ref):
    first, second = blocks

    @pl.when(core == 0)
    def _():
        same_ref[...] = first
        cross_ref[...] = second

    @pl.when(core == 1)
    def _():
        same_ref[...] = second
        cross_ref[...] = first


def place_in_group():
    own = lax.rem(lax.axis_index("grp"), HEADS)
    return lax.div(own, 2), lax.rem(own, 2)


def far_kernel(images, piggy, ids_ref, rows_ref, weight_ref, normed_ref, sums_ref, same_ref, cross_ref, own_ids, rows_held, weight, id_sem, row_sem, sems):
    count, depth = rows_ref.shape
    width = weight_ref.shape[0] // 3
    wide = weight.shape[1]
    rows_fetch = pltpu.make_async_copy(rows_ref, rows_held, row_sem)
    rows_fetch.start()
    own = pl.multiple_of(lax.axis_index("grp") * count, LANES)
    ids_fetch = pltpu.make_async_copy(ids_ref.at[:, pl.ds(own, count)], own_ids, id_sem)
    ids_fetch.start()
    pair, core = place_in_group()
    pair = jnp.bitwise_xor(pair, 3)
    fetches = []
    for at in range(3):
        first = pl.multiple_of(at * width + pair * wide, 16)
        fetches.append(pltpu.make_async_copy(weight_ref.at[pl.ds(first, wide)], weight.at[at], sems.at[at]))
    for fetch in fetches:
        fetch.start()
    rows_fetch.wait()
    rows = rows_held[...]
    values = rows.astype(jnp.float32)
    center = values - jnp.mean(values, axis=1, keepdims=True)
    spread = jnp.mean(center * center, axis=1, keepdims=True)
    normed = (center * lax.rsqrt(spread + 1e-06)).astype(jnp.bfloat16)
    normed_ref[...] = normed.T
    ids_fetch.wait()
    if piggy:
        sums = jnp.dot(image_rows(own_ids[...], images), rows, preferred_element_type=jnp.float32)
        sums_ref[...] = split_in_two(sums, images)
    for fetch in fetches:
        fetch.wait()
    parts = [
        jnp.dot(weight[at], normed_ref[...], preferred_element_type=jnp.float32) for at in range(3)
    ]
    store_by_core(core, head_blocks(*parts, sums_ref if piggy else None, pair), same_ref, cross_ref)


def near_kernel(piggy, normed_ref, sums_ref, weight_ref, *out_refs):
    width = weight_ref.shape[0] // 3
    wide = 2 * width // HEADS
    own, core = place_in_group()
    for step, move in enumerate((1, 2, 0)):
        pair = jnp.bitwise_xor(own, move)
        parts = []
        for at in range(3):
            here = pl.ds(pl.multiple_of(at * width + pair * wide, 16), wide)
            parts.append(
                jnp.dot(weight_ref[here, :], normed_ref[...], preferred_element_type=jnp.float32)
            )
        blocks = head_blocks(*parts, sums_ref if piggy else None, pair)
        store_by_core(core, blocks, *out_refs[2 * step : 2 * step + 2])


def find_starts(images, ids, starts):
    image = lax.broadcasted_iota(jnp.int32, (rounded_up(images + 1, SPARE), ids.shape[1]), 0)
    before = jnp.sum((ids < image).astype(jnp.int32), axis=1, keepdims=True)
    for image in range(images + 1):
        starts[image] = before[image, 0]


def write_marks(images, ids, marks):
    bits = max(1, (images - 1).bit_length())
    row = lax.broadcasted_iota(jnp.int32, (SPARE, ids.shape[1]), 0)
    bit = jnp.bitwise_and(lax.shift_right_logical(jnp.broadcast_to(ids, row.shape), row >> 1), 1)
    odd = jnp.bitwise_and(row, 1)
    used = row < 2 * bits
    outside = jnp.logical_or(ids < 0, ids >= images)
    key_side = jnp.where(odd == 1, bit, 1 - bit).astype(jnp.float32)
    key_side = jnp.where(outside, 1.0, key_side)
    marks[0] = jnp.where(used, key_side * HIDDEN, 0.0)
    marks[1] = jnp.where(used, jnp.where(odd == 1, 1 - bit, bit), 0).astype(jnp.float32)


def spare_sums(refs):
    parts = [ref[QUERY_AT : QUERY_AT + 16].astype(jnp.float32)[0:SPARE, 0 : 2 * LANES] for ref in refs]
    return sum(parts[1:], parts[0])


def image_at(images, starts, position):
    found = jnp.int32(0)
    for image in range(1, images):
        found += (starts[image] <= position).astype(jnp.int32)
    return found


def attend_images(ids_ref, keys, values, queries, attended, work, table, halo):
    scores_a, scores_b, tops_a, tops_b = work
    window, tile = scores_a.shape
    size = attended.shape[0] - SPARE

    def state_of(step):
        at = pl.multiple_of(table[0, step] * tile, tile)
        return at, table[1, step], pl.ds(pl.multiple_of(table[2, step], LANES), window)

    def score(state, scores, tops):
        first, _, here = state
        found = jnp.dot(keys[here, :], queries[:, pl.ds(first, tile)], preferred_element_type=jnp.float32)
        scores[...] = found
        tops[...] = jnp.max(found, axis=0, keepdims=True)

    def weigh(state, scores, tops):
        first, image, here = state
        labels = ids_ref[:, pl.ds(pl.multiple_of(halo + first, LANES), tile)]
        probs = jnp.exp2((scores[...] - tops[...]) * (size ** (-0.5) * math.log2(math.e)))
        weighted = jnp.dot(values[:, here], probs.astype(jnp.bfloat16), preferred_element_type=jnp.float32)
        share = 1.0 / weighted[size : size + 1]
        place = (slice(None), pl.ds(first, tile))
        attended[place] = jnp.where(labels == image, weighted * share, attended[place])

    def two_pairs(step, _):
        first, second, third = (state_of(2 * step + more) for more in range(3))
        score(second, scores_b, tops_b)
        weigh(first, scores_a, tops_a)
        score(third, scores_a, tops_a)
        weigh(second, scores_b, tops_b)
        return 0

    pairs = table[3, 0]
    score(state_of(0), scores_a, tops_a)
    lax.fori_loop(0, lax.div(pairs, 2), two_pairs, 0)

    @pl.when(lax.rem(pairs, 2) == 1)
    def _():
        weigh(state_of(pairs - 1), scores_a, tops_a)


def turned_keys(marked, block_ref):
    block = block_ref[KEY_AT : KEY_AT + PADDED].astype(jnp.float32)
    nothing = jnp.zeros((LANES - PADDED, block.shape[1]), jnp.float32)
    full = jnp.concatenate([marked, block[SPARE:], nothing], axis=0)
    return full.astype(jnp.bfloat16).T


def store_queries(marked, block_ref, queries, there):
    edge = block_ref[QUERY_AT : QUERY_AT + 16].astype(jnp.float32)
    edge = jnp.concatenate([marked, edge[SPARE:]], axis=0)
    queries[0:16, there] = edge.astype(jnp.bfloat16)
    queries[16:PADDED, there] = block_ref[QUERY_AT + 16 : QUERY_AT + PADDED]
    queries[PADDED:, there] = jnp.zeros((LANES - PADDED, block_ref.shape[1]), jnp.bfloat16)


def store_values(block_ref, values, here):
    edge = block_ref[PADDED - 16 : PADDED].astype(jnp.float32)
    ones = jnp.ones((SPARE, edge.shape[1]), jnp.float32)
    values[0 : PADDED - 16, here] = block_ref[0 : PADDED - 16]
    values[PADDED - 16 : PADDED, here] = jnp.concatenate([edge[:SPARE], ones], axis=0).astype(jnp.bfloat16)


def list_pairs(images, held, tile, window, length, halo, starts, table):
    low = image_at(images, starts, halo)
    high = image_at(images, starts, halo + held - 1)

    def one_image(image, count):
        first = lax.div(jnp.maximum(starts[image] - halo, 0), tile)
        last = lax.div(jnp.minimum(starts[image + 1] - halo, held) - 1, tile)
        begin = jnp.minimum(lax.div(starts[image], LANES) * LANES, length - window)

        def one_tile(at, count):
            table[0, count] = at
            table[1, count] = image
            table[2, count] = begin
            return count + 1

        return lax.fori_loop(first, last + 1, one_tile, count)

    pairs = lax.fori_loop(low, high + 1, one_image, jnp.int32(0))
    for row in range(3):
        table[row, pairs] = table[row, pairs - 1]
    table[3, 0] = pairs


def prepare_kernel(images, halo, tile, window, ids_ref, *rest):
    got_refs, (keys, marks, table, starts) = rest[: len(EARLY)], rest[len(EARLY) :]
    count = got_refs[0].shape[1]
    find_starts(images, ids_ref[...], starts)
    write_marks(images, ids_ref[...], marks)
    own = lax.rem(lax.axis_index("grp"), HEADS)
    for step, (by, ref) in enumerate(zip(EARLY, got_refs)):
        first = jnp.bitwise_xor(own, by) * count
        here = pl.ds(pl.multiple_of(halo + first, LANES), count)
        keys[step * count : (step + 1) * count, :] = turned_keys(marks[0, :, here], ref)
    list_pairs(images, HEADS * count, tile, window, ids_ref.shape[1], halo, starts, table)


def attend_kernel(images, piggy, halo, ids_ref, table_ref, marks, early_keys, *rest):
    got_refs, rest = rest[:HEADS], rest[HEADS:]
    if halo:
        left_ref, right_ref, *rest = rest
    out_ref, keys, values, queries, attended, *work, table, sem = rest
    fetch = pltpu.make_async_copy(table_ref, table, sem)
    fetch.start()
    count = got_refs[0].shape[1]
    padded = attended.shape[0]
    size = padded - SPARE
    total_rows = HEADS * count
    length = ids_ref.shape[1]
    ids = ids_ref[...]

    own = lax.rem(lax.axis_index("grp"), HEADS)
    for step, (by, ref) in enumerate(zip(EARLY + LATE, got_refs)):
        first = jnp.bitwise_xor(own, by) * count
        here = pl.ds(pl.multiple_of(halo + first, LANES), count)
        there = pl.ds(pl.multiple_of(first, LANES), count)
        if by in EARLY:
            keys[here, :] = early_keys[step * count : (step + 1) * count, :]
        else:
            keys[here, :] = turned_keys(marks[0, :, here], ref)
        store_values(ref, values, here)
        store_queries(marks[1, :, here], ref, queries, there)
    if halo:
        for ref, here in ((left_ref, slice(0, halo)), (right_ref, slice(length - halo, length))):
            keys[here, :] = turned_keys(marks[0, :, here], ref)
            store_values(ref, values, here)
    fetch.wait()
    attend_images(ids_ref, keys, values, queries, attended, work, table, halo)

    odd_head = lax.rem(own, 2) == 1
    mine = ids[:, halo : halo + total_rows]

    @pl.when(odd_head)
    def _():
        attended[SPARE:padded, :] = attended[0:size, :]

    row = lax.broadcasted_iota(jnp.int32, (padded, count), 0)
    lowest = jnp.where(odd_head, SPARE, 0)
    kept = jnp.logical_and(row >= lowest, row < lowest + size)
    pooled = jnp.zeros((SPARE, padded), jnp.float32)
    for source in range(HEADS):
        here = slice(source * count, (source + 1) * count)
        block = jnp.where(kept, attended[:, here], 0.0).astype(jnp.bfloat16)
        out_ref[source] = block
        if piggy:
            pooled += lax.dot_general(
                image_rows(mine[:, here], images),
                block,
                (((1,), (1,)), ((), ())),
                preferred_element_type=jnp.float32,
            )
    if piggy:
        pooled = split_in_two(pooled, images)
        sums = spare_sums(got_refs)
        sums = split_in_two(sums + pltpu.roll(sums, images, axis=0), images)
        spare = jnp.concatenate(
            [pooled, jnp.zeros((SPARE, LANES - padded), jnp.float32), sums], axis=1
        )

        def store_spare(edge, rows):
            for source in range(HEADS):
                block = attended[edge, source * count : (source + 1) * count]
                parts = [spare, block[SPARE:]] if rows == 0 else [block[:SPARE], spare]
                out_ref[source, edge] = jnp.concatenate(parts, axis=0).astype(jnp.bfloat16)

        pl.when(odd_head)(lambda: store_spare(slice(0, 16), 0))
        pl.when(jnp.logical_not(odd_head))(lambda: store_spare(slice(padded - 16, padded), SPARE))


def joined_heads(got_ref, out_weight_ref, flat, weight):
    padded = got_ref.shape[1]
    size = padded - SPARE
    spares = []
    for head in range(HEADS):
        at = head * padded
        from_row = head * size - (SPARE if head % 2 else 0)
        weight[at : at + padded] = out_weight_ref[from_row : from_row + padded]
        edge = 0 if head % 2 else padded - 16
        rest = slice(16, padded) if head % 2 else slice(0, padded - 16)
        mixed_rows = got_ref[head, edge : edge + 16].astype(jnp.float32)
        nothing = jnp.zeros((SPARE, mixed_rows.shape[1]), jnp.float32)
        if head % 2:
            spares.append(mixed_rows[:SPARE])
            block = jnp.concatenate([nothing, mixed_rows[SPARE:]], axis=0)
        else:
            spares.append(mixed_rows[SPARE:])
            block = jnp.concatenate([mixed_rows[:SPARE], nothing], axis=0)
        flat[at + edge : at + edge + 16] = block.astype(jnp.bfloat16)
        flat[at + rest.start : at + rest.stop] = got_ref[head, rest]
    return spares


def send_mixed_rows(rows_ref, flat, weight, turned, mixed, mixed_ref, sems):
    turned[...] = flat[...].T
    pieces = sems.shape[0]
    step = rows_ref.shape[0] // pieces
    copies = []
    for piece in range(pieces):
        cut = slice(piece * step, (piece + 1) * step)
        added = jnp.dot(turned[cut, :], weight[...], preferred_element_type=jnp.float32)
        mixed[cut, :] = (rows_ref[cut, :].astype(jnp.float32) + added).astype(jnp.bfloat16)
        copies.append(pltpu.make_async_copy(mixed.at[cut], mixed_ref.at[cut], sems.at[piece]))
        copies[-1].start()
    return copies


def unit_rows(matrix):
    return matrix * lax.rsqrt(jnp.sum(matrix * matrix, axis=1, keepdims=True) + 1e-06)


def losses(cosine, labels):
    logits = -labels * (logit_scale * cosine + logit_bias)
    return jnp.maximum(logits, 0.0) + jnp.log1p(jnp.exp(-jnp.abs(logits)))


def finish_kernel(images, rows_ref, got_ref, out_weight_ref, text_ref, mixed_ref, loss_ref, flat, weight, turned, mixed, sems, pooled_heads):
    padded = got_ref.shape[1]
    spares = joined_heads(got_ref, out_weight_ref, flat, weight)
    copies = send_mixed_rows(rows_ref, flat, weight, turned, mixed, mixed_ref, sems)
    for head in range(HEADS):
        pooled_heads[:, head * padded : (head + 1) * padded] = spares[head][:, 0:padded]
    pooled = jnp.dot(
        pooled_heads[...].astype(jnp.bfloat16), weight[...], preferred_element_type=jnp.float32
    )
    patch_sums = [spare[:, LANES : 2 * LANES] for spare in spares] + [spares[0][:, 2 * LANES :]]
    pooled = pooled + jnp.concatenate(patch_sums, axis=1)
    pooled = pooled + pltpu.roll(pooled, images, axis=0)
    image_vecs = unit_rows(pooled)
    text_vecs = unit_rows(text_ref[...].astype(jnp.float32))
    cosine = lax.dot_general(
        text_vecs,
        image_vecs,
        (((1,), (1,)), ((), ())),
        precision=lax.Precision.HIGHEST,
        preferred_element_type=jnp.float32,
    )
    text = lax.broadcasted_iota(jnp.int32, cosine.shape, 0)
    image = lax.broadcasted_iota(jnp.int32, cosine.shape, 1)
    terms = losses(cosine, jnp.where(text == image, 1.0, -1.0))
    loss_ref[...] = jnp.sum(terms, axis=0, keepdims=True)[:, 0:images]
    for copy in copies:
        copy.wait()


def mix_kernel(rows_ref, got_ref, out_weight_ref, mixed_ref, flat, weight, turned, mixed, sems):
    joined_heads(got_ref, out_weight_ref, flat, weight)
    for copy in send_mixed_rows(rows_ref, flat, weight, turned, mixed, mixed_ref, sems):
        copy.wait()


def in_vmem(count):
    return [pl.BlockSpec(memory_space=pltpu.VMEM)] * count


def in_hbm(value):
    return pltpu.with_memory_space_constraint(value, pltpu.HBM)


def call(kernel, out_shape, scratch, in_specs, flops, out_specs=None):
    if out_specs is None:
        out_specs = jax.tree.map(lambda _: pl.BlockSpec(memory_space=pltpu.VMEM), out_shape)
    return pl.pallas_call(
        kernel,
        out_shape=out_shape,
        in_specs=in_specs,
        out_specs=out_specs,
        scratch_shapes=scratch,
        compiler_params=pltpu.CompilerParams(vmem_limit_bytes=VMEM_LIMIT),
        cost_estimate=pl.CostEstimate(flops=flops, bytes_accessed=8 << 20, transcendentals=0),
    )


def moved(value, axis, pairs):
    return lax.ppermute(value, axis, pairs)


def all_texts(texts):
    peers = lax.axis_size("blk")
    shifts = range(1, peers)
    return [texts] + [moved(texts, "blk", [(i, (i + by) % peers) for i in range(peers)]) for by in shifts]


def exchanged(blocks, groups):
    return lax.all_to_all(blocks, "grp", 0, 0, axis_index_groups=groups, tiled=True)


def local(patches, segment_ids, qkv_weight, out_weight, text_embed):
    rows = patches[0]
    count, depth = rows.shape
    width = out_weight.shape[0]
    size = width // HEADS
    padded = size + SPARE
    images = text_embed.shape[0]
    group_size = lax.axis_size("grp")
    parts = group_size // HEADS
    piggy = parts == 1 and 2 * images == SPARE and count >= depth - (HEADS - 2) * LANES
    groups = None if parts == 1 else [list(range(p * HEADS, (p + 1) * HEADS)) for p in range(parts)]
    bf16, f32 = jnp.bfloat16, jnp.float32
    shape = jax.ShapeDtypeStruct

    block = shape((3 * size + SPARE, count), bf16)
    hbm = pl.BlockSpec(memory_space=pltpu.HBM)
    turned_weight = qkv_weight.T
    normed, sums, *sent = call(
        functools.partial(far_kernel, images, piggy),
        (shape((depth, count), bf16), shape((SPARE, depth), f32), block, block),
        [
            pltpu.VMEM((1, count), jnp.int32),
            pltpu.VMEM((count, depth), bf16),
            pltpu.VMEM((3, 2 * size, depth), bf16),
            pltpu.SemaphoreType.DMA,
            pltpu.SemaphoreType.DMA,
            pltpu.SemaphoreType.DMA((3,)),
        ],
        [hbm] * 3,
        2 * count * depth * 6 * size,
    )(in_hbm(segment_ids), in_hbm(rows), in_hbm(turned_weight))
    sent += call(
        functools.partial(near_kernel, piggy),
        (block,) * 6,
        [],
        in_vmem(3),
        2 * count * depth * 18 * size,
    )(normed, sums, turned_weight)
    sent = dict(zip((6, 7, 2, 3, 4, 5, 0, 1), sent))
    got = {0: sent[0]}
    for by in ORDER[:-1]:
        got[by] = moved(sent[by], "grp", [(i, i ^ by) for i in range(group_size)])

    length = HEADS * count
    halo = 0
    near_ids = segment_ids
    halos = []
    if parts > 1:
        halo = rounded_up(MAXP - 1, LANES)
        part = lax.axis_index("grp") // HEADS
        whole_ids = jnp.concatenate(
            [
                jnp.full((1, halo), -1, jnp.int32),
                segment_ids,
                jnp.full((1, halo), images, jnp.int32),
            ],
            axis=1,
        )
        near_ids = lax.dynamic_slice_in_dim(whole_ids, part * length, length + 2 * halo, axis=1)
        order = jnp.bitwise_xor(lax.axis_index("grp") % HEADS, jnp.arange(HEADS))
        flat = jnp.stack([got[by] for by in range(HEADS)])[order][:, : 2 * size].transpose(1, 0, 2).reshape(2 * size, length)
        flat = jnp.concatenate([flat, jnp.zeros((16, length), bf16)], axis=0)
        ahead = [(i, i + HEADS) for i in range(group_size - HEADS)]
        back = [(i + HEADS, i) for i in range(group_size - HEADS)]
        left = moved(flat[:, length - halo :], "grp", ahead)
        right = moved(flat[:, :halo], "grp", back)
        halos = [left, right]
    reach = length + 2 * halo
    window = min(rounded_up(MAXP + LANES - 1, LANES), reach)
    tile = 2 * LANES
    vmem = pl.BlockSpec(memory_space=pltpu.VMEM)
    listed = (4, rounded_up(length // tile + images, LANES))
    early_keys, marks, table = call(
        functools.partial(prepare_kernel, images, halo, tile, window),
        (
            shape((len(EARLY) * count, LANES), bf16),
            shape((2, SPARE, reach), f32),
            shape(listed, jnp.int32),
        ),
        [pltpu.SMEM((images + 1,), jnp.int32)],
        in_vmem(1 + len(EARLY)),
        1 << 30,
        (vmem, vmem, pl.BlockSpec(memory_space=pltpu.SMEM)),
    )(near_ids, *[got[by] for by in EARLY])
    operands = [marks, early_keys, *[got[by] for by in EARLY + LATE], *halos]
    answers = call(
        functools.partial(attend_kernel, images, piggy, halo),
        shape((HEADS, padded, count), bf16),
        [
            pltpu.VMEM((reach, LANES), bf16),
            pltpu.VMEM((padded, reach), bf16),
            pltpu.VMEM((LANES, length), bf16),
            pltpu.VMEM((padded, length), f32),
            pltpu.VMEM((window, tile), f32),
            pltpu.VMEM((window, tile), f32),
            pltpu.VMEM((1, tile), f32),
            pltpu.VMEM((1, tile), f32),
            pltpu.SMEM(listed, jnp.int32),
            pltpu.SemaphoreType.DMA,
        ],
        in_vmem(1) + [hbm] + in_vmem(len(operands)),
        4 * size * length * MAXP,
    )(near_ids, table, *operands)
    back_home = exchanged(answers, groups)
    text_embed, _ = lax.optimization_barrier((text_embed, answers))
    texts = jnp.concatenate(all_texts(text_embed), axis=0)

    joined = [
        pltpu.VMEM((HEADS * padded, count), bf16),
        pltpu.VMEM((HEADS * padded, depth), bf16),
        pltpu.VMEM((count, HEADS * padded), bf16),
        pltpu.VMEM((count, depth), bf16),
        pltpu.SemaphoreType.DMA((3,)),
    ]
    flops = 2 * count * depth * width
    if piggy:
        mixed, row_loss = call(
            functools.partial(finish_kernel, images),
            (shape((count, depth), bf16), shape((1, images), f32)),
            joined + [pltpu.VMEM((SPARE, HEADS * padded), f32)],
            in_vmem(4),
            flops,
            (hbm, pl.BlockSpec(memory_space=pltpu.VMEM)),
        )(rows, back_home, out_weight, texts)
        return (mixed[None], row_loss[0])
    mixed = call(mix_kernel, shape((count, depth), bf16), joined, in_vmem(3), flops, hbm)(
        rows, back_home, out_weight
    )
    own_ids = lax.dynamic_slice_in_dim(segment_ids[0], lax.axis_index("grp") * count, count)
    onehot = (own_ids[None, :] == jnp.arange(images, dtype=jnp.int32)[:, None]).astype(bf16)
    pooled = lax.psum(jnp.dot(onehot, mixed, preferred_element_type=f32), "grp")
    text_vecs = unit_rows(texts.astype(f32))
    cosine = jnp.dot(unit_rows(pooled), text_vecs.T, precision=lax.Precision.HIGHEST)
    same = jnp.arange(images)[:, None] == jnp.arange(texts.shape[0])[None, :]
    row_loss = jnp.sum(losses(cosine, jnp.where(same, 1.0, -1.0)), axis=1)
    return (mixed[None], row_loss)


def solution(mesh):
    placed = (P("blk", "grp", None), P("blk", None), P(), P(), P("blk", None))
    return jax.shard_map(
        local,
        mesh=mesh,
        in_specs=placed,
        out_specs=(P("blk", "grp", None), P("blk")),
        check_vma=False,
    )
```

```python
import functools
import math

import jax
import jax.numpy as jnp
from jax import lax
from jax.experimental import pallas as pl
from jax.experimental.pallas import tpu as pltpu
from jax.sharding import PartitionSpec as P

HEADS = 8
MAXP = 1024
LANES = 128
SPARE = 8
SIZE = 72
PADDED = SIZE + SPARE
KEY_AT = SIZE - SPARE
QUERY_AT = 2 * SIZE
HIDDEN = -1e30
ORDER = (6, 7, 2, 4, 3, 5, 1, 0)
EARLY = (6, 7, 1, 0)
LATE = (2, 4, 3, 5)

logit_scale = 30.0
logit_bias = -5.0

VMEM_LIMIT = 32 * 1024 * 1024


def rounded_up(value, step):
    return (value + step - 1) // step * step


def split_in_two(total, images):
    row = lax.broadcasted_iota(jnp.int32, total.shape, 0)
    main = total.astype(jnp.bfloat16).astype(jnp.float32)
    return jnp.where(row < images, main, total - main)


def image_rows(ids, images):
    row = lax.broadcasted_iota(jnp.int32, (SPARE, ids.shape[1]), 0)
    return (lax.rem(row, images) == ids).astype(jnp.float32).astype(jnp.bfloat16)


def head_blocks(query, key, value, sums, pair):
    size = query.shape[0] // 2
    count = query.shape[1]
    for place in range(2):
        here = slice(place * size, (place + 1) * size)
        if sums is None:
            spare = jnp.zeros((SPARE, count), jnp.float32)
        else:
            first = pl.multiple_of((2 * pair + place) * LANES, LANES)
            parts = [sums[:, pl.ds(first, LANES)], sums[:, HEADS * LANES :]]
            held = sum(part.shape[1] for part in parts)
            spare = jnp.concatenate(parts + [jnp.zeros((SPARE, count - held), jnp.float32)], axis=1)
        block = jnp.concatenate([value[here], key[here], spare, query[here]], axis=0)
        yield block.astype(jnp.bfloat16)


def store_by_core(core, blocks, same_ref, cross_ref):
    first, second = blocks

    @pl.when(core == 0)
    def _():
        same_ref[...] = first
        cross_ref[...] = second

    @pl.when(core == 1)
    def _():
        same_ref[...] = second
        cross_ref[...] = first


def place_in_group():
    own = lax.rem(lax.axis_index("grp"), HEADS)
    return lax.div(own, 2), lax.rem(own, 2)


def far_kernel(images, piggy, ids_ref, rows_ref, weight_ref, normed_ref, sums_ref, same_ref, cross_ref, own_ids, rows_held, weight, id_sem, row_sem, sems):
    count, depth = rows_ref.shape
    width = weight_ref.shape[0] // 3
    wide = weight.shape[1]
    rows_fetch = pltpu.make_async_copy(rows_ref, rows_held, row_sem)
    rows_fetch.start()
    own = pl.multiple_of(lax.axis_index("grp") * count, LANES)
    ids_fetch = pltpu.make_async_copy(ids_ref.at[:, pl.ds(own, count)], own_ids, id_sem)
    ids_fetch.start()
    pair, core = place_in_group()
    pair = jnp.bitwise_xor(pair, 3)
    fetches = []
    for at in range(3):
        first = pl.multiple_of(at * width + pair * wide, 16)
        fetches.append(pltpu.make_async_copy(weight_ref.at[pl.ds(first, wide)], weight.at[at], sems.at[at]))
    for fetch in fetches:
        fetch.start()
    rows_fetch.wait()
    rows = rows_held[...]
    values = rows.astype(jnp.float32)
    center = values - jnp.mean(values, axis=1, keepdims=True)
    spread = jnp.mean(center * center, axis=1, keepdims=True)
    normed = (center * lax.rsqrt(spread + 1e-06)).astype(jnp.bfloat16)
    normed_ref[...] = normed.T
    ids_fetch.wait()
    if piggy:
        sums = jnp.dot(image_rows(own_ids[...], images), rows, preferred_element_type=jnp.float32)
        sums_ref[...] = split_in_two(sums, images)
    for fetch in fetches:
        fetch.wait()
    parts = [
        jnp.dot(weight[at], normed_ref[...], preferred_element_type=jnp.float32) for at in range(3)
    ]
    store_by_core(core, head_blocks(*parts, sums_ref if piggy else None, pair), same_ref, cross_ref)


def near_kernel(piggy, normed_ref, sums_ref, weight_ref, *out_refs):
    width = weight_ref.shape[0] // 3
    wide = 2 * width // HEADS
    own, core = place_in_group()
    for step, move in enumerate((1, 2, 0)):
        pair = jnp.bitwise_xor(own, move)
        parts = []
        for at in range(3):
            here = pl.ds(pl.multiple_of(at * width + pair * wide, 16), wide)
            parts.append(
                jnp.dot(weight_ref[here, :], normed_ref[...], preferred_element_type=jnp.float32)
            )
        blocks = head_blocks(*parts, sums_ref if piggy else None, pair)
        store_by_core(core, blocks, *out_refs[2 * step : 2 * step + 2])


def count_before(images, ids):
    image = lax.broadcasted_iota(jnp.int32, (rounded_up(images + 1, SPARE), ids.shape[1]), 0)
    before = jnp.sum((ids < image).astype(jnp.int32), axis=1, keepdims=True)
    return jnp.broadcast_to(before, (before.shape[0], LANES))


def write_marks(images, ids, marks):
    bits = max(1, (images - 1).bit_length())
    row = lax.broadcasted_iota(jnp.int32, (SPARE, ids.shape[1]), 0)
    bit = jnp.bitwise_and(lax.shift_right_logical(jnp.broadcast_to(ids, row.shape), row >> 1), 1)
    odd = jnp.bitwise_and(row, 1)
    used = row < 2 * bits
    outside = jnp.logical_or(ids < 0, ids >= images)
    key_side = jnp.where(odd == 1, bit, 1 - bit).astype(jnp.float32)
    key_side = jnp.where(outside, 1.0, key_side)
    marks[0] = jnp.where(used, key_side * HIDDEN, 0.0)
    marks[1] = jnp.where(used, jnp.where(odd == 1, 1 - bit, bit), 0).astype(jnp.float32)


def spare_sums(refs):
    parts = [ref[QUERY_AT : QUERY_AT + 16].astype(jnp.float32)[0:SPARE, 0 : 2 * LANES] for ref in refs]
    return sum(parts[1:], parts[0])


def image_at(images, starts, position):
    found = jnp.int32(0)
    for image in range(1, images):
        found += (starts[image] <= position).astype(jnp.int32)
    return found


def attend_images(images, ids_ref, keys, values, queries, attended, work, starts, halo):
    scores_a, scores_b, tops_a, tops_b = work
    query_base = halo
    window, tile = scores_a.shape
    size = attended.shape[0] - SPARE
    held = queries.shape[1]
    tiles = held // tile

    def bounds(image):
        first = lax.div(jnp.maximum(starts[image] - query_base, 0), tile)
        last = lax.div(jnp.minimum(starts[image + 1] - query_base, held) - 1, tile)
        return jnp.minimum(first, tiles - 1), last

    def after(image):
        return jnp.minimum(image + 1, images - 1)

    def following(state):
        at, image = state
        more = at < bounds(image)[1]
        later = after(image)
        return jnp.where(more, at + 1, bounds(later)[0]), jnp.where(more, image, later)

    def window_of(image):
        begin = lax.div(starts[image], LANES) * LANES
        return pl.ds(pl.multiple_of(jnp.minimum(begin, keys.shape[0] - window), LANES), window)

    def score(state, scores, tops):
        at, image = state
        query = queries[:, pl.ds(pl.multiple_of(at * tile, tile), tile)]
        found = jnp.dot(keys[window_of(image), :], query, preferred_element_type=jnp.float32)
        scores[...] = found
        tops[...] = jnp.max(found, axis=0, keepdims=True)

    def weigh(state, scores, tops):
        at, image = state
        first = pl.multiple_of(at * tile, tile)
        labels = ids_ref[:, pl.ds(pl.multiple_of(query_base + first, LANES), tile)]
        probs = jnp.exp2((scores[...] - tops[...]) * (size ** (-0.5) * math.log2(math.e)))
        share = 1.0 / jnp.sum(probs, axis=0, keepdims=True)
        weighted = jnp.dot(
            values[:, window_of(image)], probs.astype(jnp.bfloat16), preferred_element_type=jnp.float32
        )
        place = (slice(None), pl.ds(first, tile))
        attended[place] = jnp.where(labels == image, weighted * share, attended[place])

    low = image_at(images, starts, query_base)
    high = image_at(images, starts, query_base + held - 1)
    pairs = jnp.int32(0)
    for image in range(images):
        first, last = bounds(image)
        wanted = jnp.logical_and(low <= image, image <= high)
        pairs += jnp.where(wanted, last - first + 1, 0)

    def two_pairs(_, state):
        second = following(state)
        score(second, scores_b, tops_b)
        weigh(state, scores_a, tops_a)
        third = following(second)
        score(third, scores_a, tops_a)
        weigh(second, scores_b, tops_b)
        return third

    begun = (jnp.int32(0), low)
    score(begun, scores_a, tops_a)
    last_state = lax.fori_loop(0, lax.div(pairs, 2), two_pairs, begun)

    @pl.when(lax.rem(pairs, 2) == 1)
    def _():
        weigh(last_state, scores_a, tops_a)


def turned_keys(marked, block_ref):
    block = block_ref[KEY_AT : KEY_AT + PADDED].astype(jnp.float32)
    nothing = jnp.zeros((LANES - PADDED, block.shape[1]), jnp.float32)
    full = jnp.concatenate([marked, block[SPARE:], nothing], axis=0)
    return full.astype(jnp.bfloat16).T


def store_queries(marked, block_ref, queries, there):
    edge = block_ref[QUERY_AT : QUERY_AT + 16].astype(jnp.float32)
    edge = jnp.concatenate([marked, edge[SPARE:]], axis=0)
    queries[0:16, there] = edge.astype(jnp.bfloat16)
    queries[16:PADDED, there] = block_ref[QUERY_AT + 16 : QUERY_AT + PADDED]
    queries[PADDED:, there] = jnp.zeros((LANES - PADDED, block_ref.shape[1]), jnp.bfloat16)


def prepare_kernel(images, halo, ids_ref, *rest):
    got_refs, (keys, marks, before) = rest[: len(EARLY)], rest[len(EARLY) :]
    count = got_refs[0].shape[1]
    before[...] = count_before(images, ids_ref[...])
    write_marks(images, ids_ref[...], marks)
    own = lax.rem(lax.axis_index("grp"), HEADS)
    for step, (by, ref) in enumerate(zip(EARLY, got_refs)):
        first = jnp.bitwise_xor(own, by) * count
        here = pl.ds(pl.multiple_of(halo + first, LANES), count)
        keys[step * count : (step + 1) * count, :] = turned_keys(marks[0, :, here], ref)


def attend_kernel(images, piggy, halo, ids_ref, before_ref, marks, early_keys, *rest):
    got_refs, rest = rest[:HEADS], rest[HEADS:]
    if halo:
        left_ref, right_ref, *rest = rest
    out_refs, rest = rest[:HEADS], rest[HEADS:]
    keys, values, queries, attended, *work, starts = rest
    count = got_refs[0].shape[1]
    padded = attended.shape[0]
    size = padded - SPARE
    total_rows = HEADS * count
    length = ids_ref.shape[1]
    ids = ids_ref[...]
    before = before_ref[...]
    for image in range(images + 1):
        starts[image] = before[image, 0]

    own = lax.rem(lax.axis_index("grp"), HEADS)
    for step, (by, ref) in enumerate(zip(EARLY + LATE, got_refs)):
        first = jnp.bitwise_xor(own, by) * count
        here = pl.ds(pl.multiple_of(halo + first, LANES), count)
        there = pl.ds(pl.multiple_of(first, LANES), count)
        if by in EARLY:
            keys[here, :] = early_keys[step * count : (step + 1) * count, :]
        else:
            keys[here, :] = turned_keys(marks[0, :, here], ref)
        values[:, here] = ref[0:PADDED]
        store_queries(marks[1, :, here], ref, queries, there)
    if halo:
        for ref, here in ((left_ref, slice(0, halo)), (right_ref, slice(length - halo, length))):
            keys[here, :] = turned_keys(marks[0, :, here], ref)
            values[:, here] = ref[0:PADDED]
    attend_images(images, ids_ref, keys, values, queries, attended, work, starts, halo)

    odd_head = lax.rem(own, 2) == 1
    mine = ids[:, halo : halo + total_rows]

    def placed(block, spare):
        even = jnp.concatenate([block[0:size], spare], axis=0)
        odd = jnp.concatenate([spare, block[0:size]], axis=0)
        return jnp.where(odd_head, odd, even)

    if piggy:
        nothing = jnp.zeros((SPARE, total_rows), jnp.float32)
        flat = placed(attended[...], nothing).astype(jnp.bfloat16)
        pooled = lax.dot_general(
            image_rows(mine, images), flat, (((1,), (1,)), ((), ())), preferred_element_type=jnp.float32
        )
        pooled = split_in_two(pooled, images)
        sums = spare_sums(got_refs)
        sums = split_in_two(sums + pltpu.roll(sums, images, axis=0), images)
        spare = jnp.concatenate(
            [pooled, jnp.zeros((SPARE, LANES - padded), jnp.float32), sums], axis=1
        )
    else:
        spare = jnp.zeros((SPARE, count), jnp.float32)
    for by, out_ref in zip(ORDER, out_refs):
        there = pl.multiple_of(jnp.bitwise_xor(own, by) * count, LANES)
        out_ref[...] = placed(attended[:, pl.ds(there, count)], spare).astype(jnp.bfloat16)


def joined_heads(got_refs, out_weight_ref, flat, weight):
    own = lax.rem(lax.axis_index("grp"), HEADS)
    spares = []
    for step, (by, got_ref) in enumerate(zip(ORDER, got_refs)):
        head = jnp.bitwise_xor(own, by)
        odd = lax.rem(head, 2)
        first = pl.multiple_of(lax.div(head, 2) * (2 * SIZE) + odd * (SIZE - SPARE), 16)
        at = step * PADDED
        weight[at : at + PADDED] = out_weight_ref[pl.ds(first, PADDED), :]
        top = got_ref[0:16].astype(jnp.float32)
        bottom = got_ref[PADDED - 16 : PADDED].astype(jnp.float32)
        spares.append(jnp.where(odd == 1, top[:SPARE], bottom[SPARE:]))
        top = jnp.concatenate([jnp.where(odd == 1, 0.0, top[:SPARE]), top[SPARE:]], axis=0)
        bottom = jnp.concatenate([bottom[:SPARE], jnp.where(odd == 1, bottom[SPARE:], 0.0)], axis=0)
        flat[at : at + 16] = top.astype(jnp.bfloat16)
        flat[at + 16 : at + PADDED - 16] = got_ref[16 : PADDED - 16]
        flat[at + PADDED - 16 : at + PADDED] = bottom.astype(jnp.bfloat16)
    return spares


def send_mixed_rows(rows_ref, flat, weight, turned, mixed, mixed_ref, sems):
    turned[...] = flat[...].T
    pieces = sems.shape[0]
    step = rows_ref.shape[0] // pieces
    copies = []
    for piece in range(pieces):
        cut = slice(piece * step, (piece + 1) * step)
        added = jnp.dot(turned[cut, :], weight[...], preferred_element_type=jnp.float32)
        mixed[cut, :] = (rows_ref[cut, :].astype(jnp.float32) + added).astype(jnp.bfloat16)
        copies.append(pltpu.make_async_copy(mixed.at[cut], mixed_ref.at[cut], sems.at[piece]))
        copies[-1].start()
    return copies


def unit_rows(matrix):
    return matrix * lax.rsqrt(jnp.sum(matrix * matrix, axis=1, keepdims=True) + 1e-06)


def losses(cosine, labels):
    logits = -labels * (logit_scale * cosine + logit_bias)
    return jnp.maximum(logits, 0.0) + jnp.log1p(jnp.exp(-jnp.abs(logits)))


def finish_kernel(images, rows_ref, out_weight_ref, text_ref, *rest):
    got_refs, rest = rest[:HEADS], rest[HEADS:]
    mixed_ref, loss_ref, flat, weight, turned, mixed, sems, pooled_heads, patch_sums = rest
    spares = joined_heads(got_refs, out_weight_ref, flat, weight)
    copies = send_mixed_rows(rows_ref, flat, weight, turned, mixed, mixed_ref, sems)
    own = lax.rem(lax.axis_index("grp"), HEADS)
    patch_sums[:, HEADS * LANES :] = spares[0][:, 2 * LANES :]
    for step, (by, spare) in enumerate(zip(ORDER, spares)):
        pooled_heads[:, step * PADDED : (step + 1) * PADDED] = spare[:, 0:PADDED]
        head = jnp.bitwise_xor(own, by)
        patch_sums[:, pl.ds(pl.multiple_of(head * LANES, LANES), LANES)] = spare[:, LANES : 2 * LANES]
    pooled = jnp.dot(
        pooled_heads[...].astype(jnp.bfloat16), weight[...], preferred_element_type=jnp.float32
    )
    pooled = pooled + patch_sums[...]
    pooled = pooled + pltpu.roll(pooled, images, axis=0)
    image_vecs = unit_rows(pooled)
    text_vecs = unit_rows(text_ref[...].astype(jnp.float32))
    cosine = lax.dot_general(
        text_vecs,
        image_vecs,
        (((1,), (1,)), ((), ())),
        precision=lax.Precision.HIGHEST,
        preferred_element_type=jnp.float32,
    )
    text = lax.broadcasted_iota(jnp.int32, cosine.shape, 0)
    image = lax.broadcasted_iota(jnp.int32, cosine.shape, 1)
    terms = losses(cosine, jnp.where(text == image, 1.0, -1.0))
    loss_ref[...] = jnp.sum(terms, axis=0, keepdims=True)[:, 0:images]
    for copy in copies:
        copy.wait()


def mix_kernel(rows_ref, out_weight_ref, *rest):
    got_refs, rest = rest[:HEADS], rest[HEADS:]
    mixed_ref, flat, weight, turned, mixed, sems = rest
    joined_heads(got_refs, out_weight_ref, flat, weight)
    for copy in send_mixed_rows(rows_ref, flat, weight, turned, mixed, mixed_ref, sems):
        copy.wait()


def in_vmem(count):
    return [pl.BlockSpec(memory_space=pltpu.VMEM)] * count


def in_hbm(value):
    return pltpu.with_memory_space_constraint(value, pltpu.HBM)


def call(kernel, out_shape, scratch, in_specs, flops, out_specs=None):
    if out_specs is None:
        out_specs = jax.tree.map(lambda _: pl.BlockSpec(memory_space=pltpu.VMEM), out_shape)
    return pl.pallas_call(
        kernel,
        out_shape=out_shape,
        in_specs=in_specs,
        out_specs=out_specs,
        scratch_shapes=scratch,
        compiler_params=pltpu.CompilerParams(vmem_limit_bytes=VMEM_LIMIT),
        cost_estimate=pl.CostEstimate(flops=flops, bytes_accessed=8 << 20, transcendentals=0),
    )


def moved(value, axis, pairs):
    return lax.ppermute(value, axis, pairs)


def all_texts(texts):
    peers = lax.axis_size("blk")
    shifts = range(1, peers)
    return [texts] + [moved(texts, "blk", [(i, (i + by) % peers) for i in range(peers)]) for by in shifts]


def traded(blocks):
    peers = range(lax.axis_size("grp"))
    trades = {by: moved(blocks[by], "grp", [(i, i ^ by) for i in peers]) for by in ORDER if by}
    return {**trades, 0: blocks[0]}


def local(patches, segment_ids, qkv_weight, out_weight, text_embed):
    rows = patches[0]
    count, depth = rows.shape
    width = out_weight.shape[0]
    size = width // HEADS
    padded = size + SPARE
    images = text_embed.shape[0]
    group_size = lax.axis_size("grp")
    parts = group_size // HEADS
    piggy = parts == 1 and 2 * images == SPARE and count >= depth - (HEADS - 2) * LANES
    bf16, f32 = jnp.bfloat16, jnp.float32
    shape = jax.ShapeDtypeStruct

    block = shape((3 * size + SPARE, count), bf16)
    hbm = pl.BlockSpec(memory_space=pltpu.HBM)
    turned_weight = qkv_weight.T
    normed, sums, *sent = call(
        functools.partial(far_kernel, images, piggy),
        (shape((depth, count), bf16), shape((SPARE, depth), f32), block, block),
        [
            pltpu.VMEM((1, count), jnp.int32),
            pltpu.VMEM((count, depth), bf16),
            pltpu.VMEM((3, 2 * size, depth), bf16),
            pltpu.SemaphoreType.DMA,
            pltpu.SemaphoreType.DMA,
            pltpu.SemaphoreType.DMA((3,)),
        ],
        [hbm] * 3,
        2 * count * depth * 6 * size,
    )(in_hbm(segment_ids), in_hbm(rows), in_hbm(turned_weight))
    sent += call(
        functools.partial(near_kernel, piggy),
        (block,) * 6,
        [],
        in_vmem(3),
        2 * count * depth * 18 * size,
    )(normed, sums, turned_weight)
    sent = dict(zip((6, 7, 2, 3, 4, 5, 0, 1), sent))
    got = traded(sent)

    length = HEADS * count
    halo = 0
    near_ids = segment_ids
    halos = []
    if parts > 1:
        halo = rounded_up(MAXP - 1, LANES)
        part = lax.axis_index("grp") // HEADS
        whole_ids = jnp.concatenate(
            [
                jnp.full((1, halo), -1, jnp.int32),
                segment_ids,
                jnp.full((1, halo), images, jnp.int32),
            ],
            axis=1,
        )
        near_ids = lax.dynamic_slice_in_dim(whole_ids, part * length, length + 2 * halo, axis=1)
        order = jnp.bitwise_xor(lax.axis_index("grp") % HEADS, jnp.arange(HEADS))
        flat = jnp.stack([got[by] for by in range(HEADS)])[order][:, : 2 * size].transpose(1, 0, 2).reshape(2 * size, length)
        flat = jnp.concatenate([flat, jnp.zeros((16, length), bf16)], axis=0)
        ahead = [(i, i + HEADS) for i in range(group_size - HEADS)]
        back = [(i + HEADS, i) for i in range(group_size - HEADS)]
        left = moved(flat[:, length - halo :], "grp", ahead)
        right = moved(flat[:, :halo], "grp", back)
        halos = [left, right]
    reach = length + 2 * halo
    window = min(rounded_up(MAXP + LANES - 1, LANES), reach)
    tile = 2 * LANES
    early_keys, marks, before = call(
        functools.partial(prepare_kernel, images, halo),
        (
            shape((len(EARLY) * count, LANES), bf16),
            shape((2, SPARE, reach), f32),
            shape((rounded_up(images + 1, SPARE), LANES), jnp.int32),
        ),
        [],
        in_vmem(1 + len(EARLY)),
        1 << 30,
    )(near_ids, *[got[by] for by in EARLY])
    text_embed, marks = lax.optimization_barrier((text_embed, marks))
    texts, marks = lax.optimization_barrier((all_texts(text_embed), marks))
    texts = jnp.concatenate(texts, axis=0)
    operands = [near_ids, before, marks, early_keys, *[got[by] for by in EARLY + LATE], *halos]
    answers = call(
        functools.partial(attend_kernel, images, piggy, halo),
        (shape((padded, count), bf16),) * HEADS,
        [
            pltpu.VMEM((reach, LANES), bf16),
            pltpu.VMEM((padded, reach), bf16),
            pltpu.VMEM((LANES, length), bf16),
            pltpu.VMEM((padded, length), f32),
            pltpu.VMEM((window, tile), f32),
            pltpu.VMEM((window, tile), f32),
            pltpu.VMEM((1, tile), f32),
            pltpu.VMEM((1, tile), f32),
            pltpu.SMEM((images + 1,), jnp.int32),
        ],
        in_vmem(len(operands)),
        4 * size * length * MAXP,
    )(*operands)
    home = traded(dict(zip(ORDER, answers)))
    home = [home[by] for by in ORDER]

    joined = [
        pltpu.VMEM((HEADS * padded, count), bf16),
        pltpu.VMEM((HEADS * padded, depth), bf16),
        pltpu.VMEM((count, HEADS * padded), bf16),
        pltpu.VMEM((count, depth), bf16),
        pltpu.SemaphoreType.DMA((3,)),
    ]
    flops = 2 * count * depth * width
    if piggy:
        mixed, row_loss = call(
            functools.partial(finish_kernel, images),
            (shape((count, depth), bf16), shape((1, images), f32)),
            joined + [pltpu.VMEM((SPARE, HEADS * padded), f32), pltpu.VMEM((SPARE, depth), f32)],
            in_vmem(3 + HEADS),
            flops,
            (hbm, pl.BlockSpec(memory_space=pltpu.VMEM)),
        )(rows, out_weight, texts, *home)
        return (mixed[None], row_loss[0])
    mixed = call(mix_kernel, shape((count, depth), bf16), joined, in_vmem(2 + HEADS), flops, hbm)(
        rows, out_weight, *home
    )
    own_ids = lax.dynamic_slice_in_dim(segment_ids[0], lax.axis_index("grp") * count, count)
    onehot = (own_ids[None, :] == jnp.arange(images, dtype=jnp.int32)[:, None]).astype(bf16)
    pooled = lax.psum(jnp.dot(onehot, mixed, preferred_element_type=f32), "grp")
    text_vecs = unit_rows(texts.astype(f32))
    cosine = jnp.dot(unit_rows(pooled), text_vecs.T, precision=lax.Precision.HIGHEST)
    same = jnp.arange(images)[:, None] == jnp.arange(texts.shape[0])[None, :]
    row_loss = jnp.sum(losses(cosine, jnp.where(same, 1.0, -1.0)), axis=1)
    return (mixed[None], row_loss)


def solution(mesh):
    placed = (P("blk", "grp", None), P("blk", None), P(), P(), P("blk", None))
    return jax.shard_map(
        local,
        mesh=mesh,
        in_specs=placed,
        out_specs=(P("blk", "grp", None), P("blk")),
        check_vma=False,
    )
```

```python
import functools
import math

import jax
import jax.numpy as jnp
from jax import lax
from jax.experimental import pallas as pl
from jax.experimental.pallas import tpu as pltpu
from jax.sharding import PartitionSpec as P

HEADS = 8
MAXP = 1024
LANES = 128
SPARE = 8
SIZE = 72
PADDED = SIZE + SPARE
KEY_AT = SIZE - SPARE
QUERY_AT = 2 * SIZE
HIDDEN = -1e30
ORDER = (6, 7, 2, 4, 3, 5, 1, 0)
EARLY = (6, 7, 1, 0)
LATE = (2, 4, 3, 5)

logit_scale = 30.0
logit_bias = -5.0

VMEM_LIMIT = 32 * 1024 * 1024


def rounded_up(value, step):
    return (value + step - 1) // step * step


def split_in_two(total, images):
    row = lax.broadcasted_iota(jnp.int32, total.shape, 0)
    main = total.astype(jnp.bfloat16).astype(jnp.float32)
    return jnp.where(row < images, main, total - main)


def image_rows(ids, images):
    row = lax.broadcasted_iota(jnp.int32, (SPARE, ids.shape[1]), 0)
    return (lax.rem(row, images) == ids).astype(jnp.float32).astype(jnp.bfloat16)


def head_blocks(query, key, value, sums, pair):
    size = query.shape[0] // 2
    count = query.shape[1]
    for place in range(2):
        here = slice(place * size, (place + 1) * size)
        if sums is None:
            spare = jnp.zeros((SPARE, count), jnp.float32)
        else:
            first = pl.multiple_of((2 * pair + place) * LANES, LANES)
            parts = [sums[:, pl.ds(first, LANES)], sums[:, HEADS * LANES :]]
            held = sum(part.shape[1] for part in parts)
            spare = jnp.concatenate(parts + [jnp.zeros((SPARE, count - held), jnp.float32)], axis=1)
        block = jnp.concatenate([value[here], key[here], spare, query[here]], axis=0)
        yield block.astype(jnp.bfloat16)


def store_by_core(core, blocks, same_ref, cross_ref):
    first, second = blocks

    @pl.when(core == 0)
    def _():
        same_ref[...] = first
        cross_ref[...] = second

    @pl.when(core == 1)
    def _():
        same_ref[...] = second
        cross_ref[...] = first


def place_in_group():
    own = lax.rem(lax.axis_index("grp"), HEADS)
    return lax.div(own, 2), lax.rem(own, 2)


def far_kernel(images, piggy, ids_ref, rows_ref, weight_ref, normed_ref, sums_ref, same_ref, cross_ref, own_ids, rows_held, weight, id_sem, row_sem, sems):
    count, depth = rows_ref.shape
    width = weight_ref.shape[0] // 3
    wide = weight.shape[1]
    rows_fetch = pltpu.make_async_copy(rows_ref, rows_held, row_sem)
    rows_fetch.start()
    own = pl.multiple_of(lax.axis_index("grp") * count, LANES)
    ids_fetch = pltpu.make_async_copy(ids_ref.at[:, pl.ds(own, count)], own_ids, id_sem)
    ids_fetch.start()
    pair, core = place_in_group()
    pair = jnp.bitwise_xor(pair, 3)
    fetches = []
    for at in range(3):
        first = pl.multiple_of(at * width + pair * wide, 16)
        fetches.append(pltpu.make_async_copy(weight_ref.at[pl.ds(first, wide)], weight.at[at], sems.at[at]))
    for fetch in fetches:
        fetch.start()
    rows_fetch.wait()
    rows = rows_held[...]
    values = rows.astype(jnp.float32)
    center = values - jnp.mean(values, axis=1, keepdims=True)
    spread = jnp.mean(center * center, axis=1, keepdims=True)
    normed = (center * lax.rsqrt(spread + 1e-06)).astype(jnp.bfloat16)
    normed_ref[...] = normed.T
    ids_fetch.wait()
    if piggy:
        sums = jnp.dot(image_rows(own_ids[...], images), rows, preferred_element_type=jnp.float32)
        sums_ref[...] = split_in_two(sums, images)
    for fetch in fetches:
        fetch.wait()
    parts = [
        jnp.dot(weight[at], normed_ref[...], preferred_element_type=jnp.float32) for at in range(3)
    ]
    store_by_core(core, head_blocks(*parts, sums_ref if piggy else None, pair), same_ref, cross_ref)


def near_kernel(piggy, normed_ref, sums_ref, weight_ref, *out_refs):
    width = weight_ref.shape[0] // 3
    wide = 2 * width // HEADS
    own, core = place_in_group()
    for step, move in enumerate((1, 2, 0)):
        pair = jnp.bitwise_xor(own, move)
        parts = []
        for at in range(3):
            here = pl.ds(pl.multiple_of(at * width + pair * wide, 16), wide)
            parts.append(
                jnp.dot(weight_ref[here, :], normed_ref[...], preferred_element_type=jnp.float32)
            )
        blocks = head_blocks(*parts, sums_ref if piggy else None, pair)
        store_by_core(core, blocks, *out_refs[2 * step : 2 * step + 2])


def count_before(images, ids):
    image = lax.broadcasted_iota(jnp.int32, (rounded_up(images + 1, SPARE), ids.shape[1]), 0)
    before = jnp.sum((ids < image).astype(jnp.int32), axis=1, keepdims=True)
    return jnp.broadcast_to(before, (before.shape[0], LANES))


def write_marks(images, ids, marks):
    bits = max(1, (images - 1).bit_length())
    row = lax.broadcasted_iota(jnp.int32, (SPARE, ids.shape[1]), 0)
    bit = jnp.bitwise_and(lax.shift_right_logical(jnp.broadcast_to(ids, row.shape), row >> 1), 1)
    odd = jnp.bitwise_and(row, 1)
    used = row < 2 * bits
    outside = jnp.logical_or(ids < 0, ids >= images)
    key_side = jnp.where(odd == 1, bit, 1 - bit).astype(jnp.float32)
    key_side = jnp.where(outside, 1.0, key_side)
    marks[0] = jnp.where(used, key_side * HIDDEN, 0.0)
    marks[1] = jnp.where(used, jnp.where(odd == 1, 1 - bit, bit), 0).astype(jnp.float32)


def spare_sums(refs):
    parts = [ref[QUERY_AT : QUERY_AT + 16].astype(jnp.float32)[0:SPARE, 0 : 2 * LANES] for ref in refs]
    return sum(parts[1:], parts[0])


def image_at(images, starts, position):
    found = jnp.int32(0)
    for image in range(1, images):
        found += (starts[image] <= position).astype(jnp.int32)
    return found


def attend_images(images, ids_ref, keys, values, queries, attended, work, starts, halo):
    scores_a, scores_b, tops_a, tops_b = work
    query_base = halo
    window, tile = scores_a.shape
    size = attended.shape[0] - SPARE
    held = queries.shape[1]
    tiles = held // tile

    def bounds(image):
        first = lax.div(jnp.maximum(starts[image] - query_base, 0), tile)
        last = lax.div(jnp.minimum(starts[image + 1] - query_base, held) - 1, tile)
        return jnp.minimum(first, tiles - 1), last

    def after(image):
        return jnp.minimum(image + 1, images - 1)

    def following(state):
        at, image = state
        more = at < bounds(image)[1]
        later = after(image)
        return jnp.where(more, at + 1, bounds(later)[0]), jnp.where(more, image, later)

    def window_of(image):
        begin = lax.div(starts[image], LANES) * LANES
        return pl.ds(pl.multiple_of(jnp.minimum(begin, keys.shape[0] - window), LANES), window)

    def score(state, scores, tops):
        at, image = state
        query = queries[:, pl.ds(pl.multiple_of(at * tile, tile), tile)]
        found = jnp.dot(keys[window_of(image), :], query, preferred_element_type=jnp.float32)
        scores[...] = found
        tops[...] = jnp.max(found, axis=0, keepdims=True)

    def weigh(state, scores, tops):
        at, image = state
        first = pl.multiple_of(at * tile, tile)
        labels = ids_ref[:, pl.ds(pl.multiple_of(query_base + first, LANES), tile)]
        probs = jnp.exp2((scores[...] - tops[...]) * (size ** (-0.5) * math.log2(math.e)))
        share = 1.0 / jnp.sum(probs, axis=0, keepdims=True)
        weighted = jnp.dot(
            values[:, window_of(image)], probs.astype(jnp.bfloat16), preferred_element_type=jnp.float32
        )
        place = (slice(None), pl.ds(first, tile))
        attended[place] = jnp.where(labels == image, weighted * share, attended[place])

    low = image_at(images, starts, query_base)
    high = image_at(images, starts, query_base + held - 1)
    pairs = jnp.int32(0)
    for image in range(images):
        first, last = bounds(image)
        wanted = jnp.logical_and(low <= image, image <= high)
        pairs += jnp.where(wanted, last - first + 1, 0)

    def two_pairs(_, state):
        second = following(state)
        score(second, scores_b, tops_b)
        weigh(state, scores_a, tops_a)
        third = following(second)
        score(third, scores_a, tops_a)
        weigh(second, scores_b, tops_b)
        return third

    begun = (jnp.int32(0), low)
    score(begun, scores_a, tops_a)
    last_state = lax.fori_loop(0, lax.div(pairs, 2), two_pairs, begun)

    @pl.when(lax.rem(pairs, 2) == 1)
    def _():
        weigh(last_state, scores_a, tops_a)


def turned_keys(marked, block_ref):
    block = block_ref[KEY_AT : KEY_AT + PADDED].astype(jnp.float32)
    nothing = jnp.zeros((LANES - PADDED, block.shape[1]), jnp.float32)
    full = jnp.concatenate([marked, block[SPARE:], nothing], axis=0)
    return full.astype(jnp.bfloat16).T


def store_queries(marked, block_ref, queries, there):
    edge = block_ref[QUERY_AT : QUERY_AT + 16].astype(jnp.float32)
    edge = jnp.concatenate([marked, edge[SPARE:]], axis=0)
    queries[0:16, there] = edge.astype(jnp.bfloat16)
    queries[16:PADDED, there] = block_ref[QUERY_AT + 16 : QUERY_AT + PADDED]
    queries[PADDED:, there] = jnp.zeros((LANES - PADDED, block_ref.shape[1]), jnp.bfloat16)


def prepare_kernel(images, halo, ids_ref, *rest):
    got_refs, (keys, marks, before) = rest[: len(EARLY)], rest[len(EARLY) :]
    count = got_refs[0].shape[1]
    before[...] = count_before(images, ids_ref[...])
    write_marks(images, ids_ref[...], marks)
    own = lax.rem(lax.axis_index("grp"), HEADS)
    for step, (by, ref) in enumerate(zip(EARLY, got_refs)):
        first = jnp.bitwise_xor(own, by) * count
        here = pl.ds(pl.multiple_of(halo + first, LANES), count)
        keys[step * count : (step + 1) * count, :] = turned_keys(marks[0, :, here], ref)


def attend_kernel(images, piggy, halo, ids_ref, before_ref, marks, early_keys, *rest):
    got_refs, rest = rest[:HEADS], rest[HEADS:]
    if halo:
        left_ref, right_ref, *rest = rest
    out_ref, keys, values, queries, attended, *work, starts = rest
    count = got_refs[0].shape[1]
    padded = attended.shape[0]
    size = padded - SPARE
    total_rows = HEADS * count
    length = ids_ref.shape[1]
    ids = ids_ref[...]
    before = before_ref[...]
    for image in range(images + 1):
        starts[image] = before[image, 0]

    own = lax.rem(lax.axis_index("grp"), HEADS)
    for step, (by, ref) in enumerate(zip(EARLY + LATE, got_refs)):
        first = jnp.bitwise_xor(own, by) * count
        here = pl.ds(pl.multiple_of(halo + first, LANES), count)
        there = pl.ds(pl.multiple_of(first, LANES), count)
        if by in EARLY:
            keys[here, :] = early_keys[step * count : (step + 1) * count, :]
        else:
            keys[here, :] = turned_keys(marks[0, :, here], ref)
        values[:, here] = ref[0:PADDED]
        store_queries(marks[1, :, here], ref, queries, there)
    if halo:
        for ref, here in ((left_ref, slice(0, halo)), (right_ref, slice(length - halo, length))):
            keys[here, :] = turned_keys(marks[0, :, here], ref)
            values[:, here] = ref[0:PADDED]
    attend_images(images, ids_ref, keys, values, queries, attended, work, starts, halo)

    odd_head = lax.rem(own, 2) == 1
    mine = ids[:, halo : halo + total_rows]

    def placed(block, spare):
        even = jnp.concatenate([block[0:size], spare], axis=0)
        odd = jnp.concatenate([spare, block[0:size]], axis=0)
        return jnp.where(odd_head, odd, even)

    if piggy:
        nothing = jnp.zeros((SPARE, total_rows), jnp.float32)
        flat = placed(attended[...], nothing).astype(jnp.bfloat16)
        pooled = lax.dot_general(
            image_rows(mine, images), flat, (((1,), (1,)), ((), ())), preferred_element_type=jnp.float32
        )
        pooled = split_in_two(pooled, images)
        sums = spare_sums(got_refs)
        sums = split_in_two(sums + pltpu.roll(sums, images, axis=0), images)
        spare = jnp.concatenate(
            [pooled, jnp.zeros((SPARE, LANES - padded), jnp.float32), sums], axis=1
        )
    else:
        spare = jnp.zeros((SPARE, count), jnp.float32)
    for source in range(HEADS):
        block = placed(attended[:, source * count : (source + 1) * count], spare)
        out_ref[source] = block.astype(jnp.bfloat16)


def joined_heads(got_ref, out_weight_ref, flat, weight):
    padded = got_ref.shape[1]
    size = padded - SPARE
    spares = []
    for head in range(HEADS):
        at = head * padded
        from_row = head * size - (SPARE if head % 2 else 0)
        weight[at : at + padded] = out_weight_ref[from_row : from_row + padded]
        edge = 0 if head % 2 else padded - 16
        rest = slice(16, padded) if head % 2 else slice(0, padded - 16)
        mixed_rows = got_ref[head, edge : edge + 16].astype(jnp.float32)
        nothing = jnp.zeros((SPARE, mixed_rows.shape[1]), jnp.float32)
        if head % 2:
            spares.append(mixed_rows[:SPARE])
            block = jnp.concatenate([nothing, mixed_rows[SPARE:]], axis=0)
        else:
            spares.append(mixed_rows[SPARE:])
            block = jnp.concatenate([mixed_rows[:SPARE], nothing], axis=0)
        flat[at + edge : at + edge + 16] = block.astype(jnp.bfloat16)
        flat[at + rest.start : at + rest.stop] = got_ref[head, rest]
    return spares


def send_mixed_rows(rows_ref, flat, weight, turned, mixed, mixed_ref, sems):
    turned[...] = flat[...].T
    pieces = sems.shape[0]
    step = rows_ref.shape[0] // pieces
    copies = []
    for piece in range(pieces):
        cut = slice(piece * step, (piece + 1) * step)
        added = jnp.dot(turned[cut, :], weight[...], preferred_element_type=jnp.float32)
        mixed[cut, :] = (rows_ref[cut, :].astype(jnp.float32) + added).astype(jnp.bfloat16)
        copies.append(pltpu.make_async_copy(mixed.at[cut], mixed_ref.at[cut], sems.at[piece]))
        copies[-1].start()
    return copies


def unit_rows(matrix):
    return matrix * lax.rsqrt(jnp.sum(matrix * matrix, axis=1, keepdims=True) + 1e-06)


def losses(cosine, labels):
    logits = -labels * (logit_scale * cosine + logit_bias)
    return jnp.maximum(logits, 0.0) + jnp.log1p(jnp.exp(-jnp.abs(logits)))


def finish_kernel(images, rows_ref, got_ref, out_weight_ref, text_ref, mixed_ref, loss_ref, flat, weight, turned, mixed, sems, pooled_heads):
    padded = got_ref.shape[1]
    spares = joined_heads(got_ref, out_weight_ref, flat, weight)
    copies = send_mixed_rows(rows_ref, flat, weight, turned, mixed, mixed_ref, sems)
    for head in range(HEADS):
        pooled_heads[:, head * padded : (head + 1) * padded] = spares[head][:, 0:padded]
    pooled = jnp.dot(
        pooled_heads[...].astype(jnp.bfloat16), weight[...], preferred_element_type=jnp.float32
    )
    patch_sums = [spare[:, LANES : 2 * LANES] for spare in spares] + [spares[0][:, 2 * LANES :]]
    pooled = pooled + jnp.concatenate(patch_sums, axis=1)
    pooled = pooled + pltpu.roll(pooled, images, axis=0)
    image_vecs = unit_rows(pooled)
    text_vecs = unit_rows(text_ref[...].astype(jnp.float32))
    cosine = lax.dot_general(
        text_vecs,
        image_vecs,
        (((1,), (1,)), ((), ())),
        precision=lax.Precision.HIGHEST,
        preferred_element_type=jnp.float32,
    )
    text = lax.broadcasted_iota(jnp.int32, cosine.shape, 0)
    image = lax.broadcasted_iota(jnp.int32, cosine.shape, 1)
    terms = losses(cosine, jnp.where(text == image, 1.0, -1.0))
    loss_ref[...] = jnp.sum(terms, axis=0, keepdims=True)[:, 0:images]
    for copy in copies:
        copy.wait()


def mix_kernel(rows_ref, got_ref, out_weight_ref, mixed_ref, flat, weight, turned, mixed, sems):
    joined_heads(got_ref, out_weight_ref, flat, weight)
    for copy in send_mixed_rows(rows_ref, flat, weight, turned, mixed, mixed_ref, sems):
        copy.wait()


def in_vmem(count):
    return [pl.BlockSpec(memory_space=pltpu.VMEM)] * count


def in_hbm(value):
    return pltpu.with_memory_space_constraint(value, pltpu.HBM)


def call(kernel, out_shape, scratch, in_specs, flops, out_specs=None):
    if out_specs is None:
        out_specs = jax.tree.map(lambda _: pl.BlockSpec(memory_space=pltpu.VMEM), out_shape)
    return pl.pallas_call(
        kernel,
        out_shape=out_shape,
        in_specs=in_specs,
        out_specs=out_specs,
        scratch_shapes=scratch,
        compiler_params=pltpu.CompilerParams(vmem_limit_bytes=VMEM_LIMIT),
        cost_estimate=pl.CostEstimate(flops=flops, bytes_accessed=8 << 20, transcendentals=0),
    )


def moved(value, axis, pairs):
    return lax.ppermute(value, axis, pairs)


def all_texts(texts):
    peers = lax.axis_size("blk")
    paired = peers & (peers - 1) == 0
    others = []
    for by in range(1, peers):
        pairs = [(i, i ^ by if paired else (i + by) % peers) for i in range(peers)]
        others.append(moved(texts, "blk", pairs))
    return [texts] + others


def exchanged(blocks, groups):
    return lax.all_to_all(blocks, "grp", 0, 0, axis_index_groups=groups, tiled=True)


def local(patches, segment_ids, qkv_weight, out_weight, text_embed):
    rows = patches[0]
    count, depth = rows.shape
    width = out_weight.shape[0]
    size = width // HEADS
    padded = size + SPARE
    images = text_embed.shape[0]
    group_size = lax.axis_size("grp")
    parts = group_size // HEADS
    piggy = parts == 1 and 2 * images == SPARE and count >= depth - (HEADS - 2) * LANES
    groups = None if parts == 1 else [list(range(p * HEADS, (p + 1) * HEADS)) for p in range(parts)]
    bf16, f32 = jnp.bfloat16, jnp.float32
    shape = jax.ShapeDtypeStruct

    block = shape((3 * size + SPARE, count), bf16)
    hbm = pl.BlockSpec(memory_space=pltpu.HBM)
    turned_weight = qkv_weight.T
    normed, sums, *sent = call(
        functools.partial(far_kernel, images, piggy),
        (shape((depth, count), bf16), shape((SPARE, depth), f32), block, block),
        [
            pltpu.VMEM((1, count), jnp.int32),
            pltpu.VMEM((count, depth), bf16),
            pltpu.VMEM((3, 2 * size, depth), bf16),
            pltpu.SemaphoreType.DMA,
            pltpu.SemaphoreType.DMA,
            pltpu.SemaphoreType.DMA((3,)),
        ],
        [hbm] * 3,
        2 * count * depth * 6 * size,
    )(in_hbm(segment_ids), in_hbm(rows), in_hbm(turned_weight))
    sent += call(
        functools.partial(near_kernel, piggy),
        (block,) * 6,
        [],
        in_vmem(3),
        2 * count * depth * 18 * size,
    )(normed, sums, turned_weight)
    sent = dict(zip((6, 7, 2, 3, 4, 5, 0, 1), sent))
    got = {0: sent[0]}
    for by in ORDER[:-1]:
        got[by] = moved(sent[by], "grp", [(i, i ^ by) for i in range(group_size)])

    length = HEADS * count
    halo = 0
    near_ids = segment_ids
    halos = []
    if parts > 1:
        halo = rounded_up(MAXP - 1, LANES)
        part = lax.axis_index("grp") // HEADS
        whole_ids = jnp.concatenate(
            [
                jnp.full((1, halo), -1, jnp.int32),
                segment_ids,
                jnp.full((1, halo), images, jnp.int32),
            ],
            axis=1,
        )
        near_ids = lax.dynamic_slice_in_dim(whole_ids, part * length, length + 2 * halo, axis=1)
        order = jnp.bitwise_xor(lax.axis_index("grp") % HEADS, jnp.arange(HEADS))
        flat = jnp.stack([got[by] for by in range(HEADS)])[order][:, : 2 * size].transpose(1, 0, 2).reshape(2 * size, length)
        flat = jnp.concatenate([flat, jnp.zeros((16, length), bf16)], axis=0)
        ahead = [(i, i + HEADS) for i in range(group_size - HEADS)]
        back = [(i + HEADS, i) for i in range(group_size - HEADS)]
        left = moved(flat[:, length - halo :], "grp", ahead)
        right = moved(flat[:, :halo], "grp", back)
        halos = [left, right]
    reach = length + 2 * halo
    window = min(rounded_up(MAXP + LANES - 1, LANES), reach)
    tile = 2 * LANES
    early_keys, marks, before = call(
        functools.partial(prepare_kernel, images, halo),
        (
            shape((len(EARLY) * count, LANES), bf16),
            shape((2, SPARE, reach), f32),
            shape((rounded_up(images + 1, SPARE), LANES), jnp.int32),
        ),
        [],
        in_vmem(1 + len(EARLY)),
        1 << 30,
    )(near_ids, *[got[by] for by in EARLY])
    operands = [near_ids, before, marks, early_keys, *[got[by] for by in EARLY + LATE], *halos]
    answers = call(
        functools.partial(attend_kernel, images, piggy, halo),
        shape((HEADS, padded, count), bf16),
        [
            pltpu.VMEM((reach, LANES), bf16),
            pltpu.VMEM((padded, reach), bf16),
            pltpu.VMEM((LANES, length), bf16),
            pltpu.VMEM((padded, length), f32),
            pltpu.VMEM((window, tile), f32),
            pltpu.VMEM((window, tile), f32),
            pltpu.VMEM((1, tile), f32),
            pltpu.VMEM((1, tile), f32),
            pltpu.SMEM((images + 1,), jnp.int32),
        ],
        in_vmem(len(operands)),
        4 * size * length * MAXP,
    )(*operands)
    back_home = exchanged(answers, groups)
    text_embed, _ = lax.optimization_barrier((text_embed, answers))
    texts = jnp.concatenate(all_texts(text_embed), axis=0)

    joined = [
        pltpu.VMEM((HEADS * padded, count), bf16),
        pltpu.VMEM((HEADS * padded, depth), bf16),
        pltpu.VMEM((count, HEADS * padded), bf16),
        pltpu.VMEM((count, depth), bf16),
        pltpu.SemaphoreType.DMA((3,)),
    ]
    flops = 2 * count * depth * width
    if piggy:
        mixed, row_loss = call(
            functools.partial(finish_kernel, images),
            (shape((count, depth), bf16), shape((1, images), f32)),
            joined + [pltpu.VMEM((SPARE, HEADS * padded), f32)],
            in_vmem(4),
            flops,
            (hbm, pl.BlockSpec(memory_space=pltpu.VMEM)),
        )(rows, back_home, out_weight, texts)
        return (mixed[None], row_loss[0])
    mixed = call(mix_kernel, shape((count, depth), bf16), joined, in_vmem(3), flops, hbm)(
        rows, back_home, out_weight
    )
    own_ids = lax.dynamic_slice_in_dim(segment_ids[0], lax.axis_index("grp") * count, count)
    onehot = (own_ids[None, :] == jnp.arange(images, dtype=jnp.int32)[:, None]).astype(bf16)
    pooled = lax.psum(jnp.dot(onehot, mixed, preferred_element_type=f32), "grp")
    text_vecs = unit_rows(texts.astype(f32))
    cosine = jnp.dot(unit_rows(pooled), text_vecs.T, precision=lax.Precision.HIGHEST)
    same = jnp.arange(images)[:, None] == jnp.arange(texts.shape[0])[None, :]
    row_loss = jnp.sum(losses(cosine, jnp.where(same, 1.0, -1.0)), axis=1)
    return (mixed[None], row_loss)


def solution(mesh):
    placed = (P("blk", "grp", None), P("blk", None), P(), P(), P("blk", None))
    return jax.shard_map(
        local,
        mesh=mesh,
        in_specs=placed,
        out_specs=(P("blk", "grp", None), P("blk")),
        check_vma=False,
    )
```

```python
import functools
import math

import jax
import jax.numpy as jnp
from jax import lax
from jax.experimental import pallas as pl
from jax.experimental.pallas import tpu as pltpu
from jax.sharding import PartitionSpec as P

HEADS = 8
MAXP = 1024
LANES = 128
SPARE = 8
SIZE = 72
PADDED = SIZE + SPARE
KEY_AT = SIZE - SPARE
QUERY_AT = 2 * SIZE
TEXT_ROWS = 16
HIDDEN = -1e30
ORDER = (6, 7, 2, 4, 3, 5, 1, 0)
EARLY = (6, 7, 1, 0)
LATE = (2, 4, 3, 5)

logit_scale = 30.0
logit_bias = -5.0

VMEM_LIMIT = 32 * 1024 * 1024


def rounded_up(value, step):
    return (value + step - 1) // step * step


def split_in_two(total, images):
    row = lax.broadcasted_iota(jnp.int32, total.shape, 0)
    main = total.astype(jnp.bfloat16).astype(jnp.float32)
    return jnp.where(row < images, main, total - main)


def image_rows(ids, images):
    row = lax.broadcasted_iota(jnp.int32, (SPARE, ids.shape[1]), 0)
    return (lax.rem(row, images) == ids).astype(jnp.float32).astype(jnp.bfloat16)


def head_blocks(query, key, value, sums, pair):
    size = query.shape[0] // 2
    count = query.shape[1]
    for place in range(2):
        here = slice(place * size, (place + 1) * size)
        if sums is None:
            spare = jnp.zeros((SPARE, count), jnp.float32)
        else:
            first = pl.multiple_of((2 * pair + place) * LANES, LANES)
            parts = [sums[:, pl.ds(first, LANES)], sums[:, HEADS * LANES :]]
            held = sum(part.shape[1] for part in parts)
            spare = jnp.concatenate(parts + [jnp.zeros((SPARE, count - held), jnp.float32)], axis=1)
        block = jnp.concatenate([value[here], key[here], spare, query[here]], axis=0)
        yield block.astype(jnp.bfloat16)


def store_by_core(core, blocks, same_ref, cross_ref):
    first, second = blocks

    @pl.when(core == 0)
    def _():
        same_ref[...] = first
        cross_ref[...] = second

    @pl.when(core == 1)
    def _():
        same_ref[...] = second
        cross_ref[...] = first


def place_in_group():
    own = lax.rem(lax.axis_index("grp"), HEADS)
    return lax.div(own, 2), lax.rem(own, 2)


def far_kernel(images, piggy, ids_ref, rows_ref, weight_ref, normed_ref, sums_ref, same_ref, cross_ref, own_ids, rows_held, weight, id_sem, row_sem, sems):
    count, depth = rows_ref.shape
    width = weight_ref.shape[0] // 3
    wide = weight.shape[1]
    rows_fetch = pltpu.make_async_copy(rows_ref, rows_held, row_sem)
    rows_fetch.start()
    own = pl.multiple_of(lax.axis_index("grp") * count, LANES)
    ids_fetch = pltpu.make_async_copy(ids_ref.at[:, pl.ds(own, count)], own_ids, id_sem)
    ids_fetch.start()
    pair, core = place_in_group()
    pair = jnp.bitwise_xor(pair, 3)
    fetches = []
    for at in range(3):
        first = pl.multiple_of(at * width + pair * wide, 16)
        fetches.append(pltpu.make_async_copy(weight_ref.at[pl.ds(first, wide)], weight.at[at], sems.at[at]))
    for fetch in fetches:
        fetch.start()
    rows_fetch.wait()
    rows = rows_held[...]
    values = rows.astype(jnp.float32)
    center = values - jnp.mean(values, axis=1, keepdims=True)
    spread = jnp.mean(center * center, axis=1, keepdims=True)
    normed = (center * lax.rsqrt(spread + 1e-06)).astype(jnp.bfloat16)
    normed_ref[...] = normed.T
    ids_fetch.wait()
    if piggy:
        sums = jnp.dot(image_rows(own_ids[...], images), rows, preferred_element_type=jnp.float32)
        sums_ref[...] = split_in_two(sums, images)
    for fetch in fetches:
        fetch.wait()
    parts = [
        jnp.dot(weight[at], normed_ref[...], preferred_element_type=jnp.float32) for at in range(3)
    ]
    store_by_core(core, head_blocks(*parts, sums_ref if piggy else None, pair), same_ref, cross_ref)


def near_kernel(piggy, normed_ref, sums_ref, weight_ref, *out_refs):
    width = weight_ref.shape[0] // 3
    wide = 2 * width // HEADS
    own, core = place_in_group()
    for step, move in enumerate((1, 2, 0)):
        pair = jnp.bitwise_xor(own, move)
        parts = []
        for at in range(3):
            here = pl.ds(pl.multiple_of(at * width + pair * wide, 16), wide)
            parts.append(
                jnp.dot(weight_ref[here, :], normed_ref[...], preferred_element_type=jnp.float32)
            )
        blocks = head_blocks(*parts, sums_ref if piggy else None, pair)
        store_by_core(core, blocks, *out_refs[2 * step : 2 * step + 2])


def count_before(images, ids):
    image = lax.broadcasted_iota(jnp.int32, (rounded_up(images + 1, SPARE), ids.shape[1]), 0)
    before = jnp.sum((ids < image).astype(jnp.int32), axis=1, keepdims=True)
    return jnp.broadcast_to(before, (before.shape[0], LANES))


def write_marks(images, ids, marks):
    bits = max(1, (images - 1).bit_length())
    row = lax.broadcasted_iota(jnp.int32, (SPARE, ids.shape[1]), 0)
    bit = jnp.bitwise_and(lax.shift_right_logical(jnp.broadcast_to(ids, row.shape), row >> 1), 1)
    odd = jnp.bitwise_and(row, 1)
    used = row < 2 * bits
    outside = jnp.logical_or(ids < 0, ids >= images)
    key_side = jnp.where(odd == 1, bit, 1 - bit).astype(jnp.float32)
    key_side = jnp.where(outside, 1.0, key_side)
    marks[0] = jnp.where(used, key_side * HIDDEN, 0.0)
    marks[1] = jnp.where(used, jnp.where(odd == 1, 1 - bit, bit), 0).astype(jnp.float32)


def spare_sums(refs):
    parts = [ref[QUERY_AT : QUERY_AT + 16].astype(jnp.float32)[0:SPARE, 0 : 2 * LANES] for ref in refs]
    return sum(parts[1:], parts[0])


def image_at(images, starts, position):
    found = jnp.int32(0)
    for image in range(1, images):
        found += (starts[image] <= position).astype(jnp.int32)
    return found


def attend_images(images, ids_ref, keys, values, queries, attended, work, starts, halo):
    scores_a, scores_b, tops_a, tops_b = work
    query_base = halo
    window, tile = scores_a.shape
    size = attended.shape[0] - SPARE
    held = queries.shape[1]
    tiles = held // tile

    def bounds(image):
        first = lax.div(jnp.maximum(starts[image] - query_base, 0), tile)
        last = lax.div(jnp.minimum(starts[image + 1] - query_base, held) - 1, tile)
        return jnp.minimum(first, tiles - 1), last

    def after(image):
        return jnp.minimum(image + 1, images - 1)

    def following(state):
        at, image = state
        more = at < bounds(image)[1]
        later = after(image)
        return jnp.where(more, at + 1, bounds(later)[0]), jnp.where(more, image, later)

    def window_of(image):
        begin = lax.div(starts[image], LANES) * LANES
        return pl.ds(pl.multiple_of(jnp.minimum(begin, keys.shape[0] - window), LANES), window)

    def score(state, scores, tops):
        at, image = state
        query = queries[:, pl.ds(pl.multiple_of(at * tile, tile), tile)]
        found = jnp.dot(keys[window_of(image), :], query, preferred_element_type=jnp.float32)
        scores[...] = found
        tops[...] = jnp.max(found, axis=0, keepdims=True)

    def weigh(state, scores, tops):
        at, image = state
        first = pl.multiple_of(at * tile, tile)
        labels = ids_ref[:, pl.ds(pl.multiple_of(query_base + first, LANES), tile)]
        probs = jnp.exp2((scores[...] - tops[...]) * (size ** (-0.5) * math.log2(math.e)))
        share = 1.0 / jnp.sum(probs, axis=0, keepdims=True)
        weighted = jnp.dot(
            values[:, window_of(image)], probs.astype(jnp.bfloat16), preferred_element_type=jnp.float32
        )
        place = (slice(None), pl.ds(first, tile))
        attended[place] = jnp.where(labels == image, weighted * share, attended[place])

    low = image_at(images, starts, query_base)
    high = image_at(images, starts, query_base + held - 1)
    pairs = jnp.int32(0)
    for image in range(images):
        first, last = bounds(image)
        wanted = jnp.logical_and(low <= image, image <= high)
        pairs += jnp.where(wanted, last - first + 1, 0)

    def two_pairs(_, state):
        second = following(state)
        score(second, scores_b, tops_b)
        weigh(state, scores_a, tops_a)
        third = following(second)
        score(third, scores_a, tops_a)
        weigh(second, scores_b, tops_b)
        return third

    begun = (jnp.int32(0), low)
    score(begun, scores_a, tops_a)
    last_state = lax.fori_loop(0, lax.div(pairs, 2), two_pairs, begun)

    @pl.when(lax.rem(pairs, 2) == 1)
    def _():
        weigh(last_state, scores_a, tops_a)


def turned_keys(marked, block_ref):
    block = block_ref[KEY_AT : KEY_AT + PADDED].astype(jnp.float32)
    nothing = jnp.zeros((LANES - PADDED, block.shape[1]), jnp.float32)
    full = jnp.concatenate([marked, block[SPARE:], nothing], axis=0)
    return full.astype(jnp.bfloat16).T


def store_queries(marked, block_ref, queries, there):
    edge = block_ref[QUERY_AT : QUERY_AT + 16].astype(jnp.float32)
    edge = jnp.concatenate([marked, edge[SPARE:]], axis=0)
    queries[0:16, there] = edge.astype(jnp.bfloat16)
    queries[16:PADDED, there] = block_ref[QUERY_AT + 16 : QUERY_AT + PADDED]
    queries[PADDED:, there] = jnp.zeros((LANES - PADDED, block_ref.shape[1]), jnp.bfloat16)


def prepare_kernel(images, halo, ids_ref, *rest):
    got_refs, (keys, marks, before) = rest[: len(EARLY)], rest[len(EARLY) :]
    count = got_refs[0].shape[1]
    before[...] = count_before(images, ids_ref[...])
    write_marks(images, ids_ref[...], marks)
    own = lax.rem(lax.axis_index("grp"), HEADS)
    for step, (by, ref) in enumerate(zip(EARLY, got_refs)):
        first = jnp.bitwise_xor(own, by) * count
        here = pl.ds(pl.multiple_of(halo + first, LANES), count)
        keys[step * count : (step + 1) * count, :] = turned_keys(marks[0, :, here], ref)


def attend_kernel(images, piggy, halo, ids_ref, before_ref, marks, early_keys, *rest):
    got_refs, rest = rest[:HEADS], rest[HEADS:]
    if piggy:
        text_ref, *rest = rest
    if halo:
        left_ref, right_ref, *rest = rest
    out_refs, rest = rest[:HEADS], rest[HEADS:]
    keys, values, queries, attended, *work, starts = rest
    count = got_refs[0].shape[1]
    padded = attended.shape[0]
    size = padded - SPARE
    total_rows = HEADS * count
    length = ids_ref.shape[1]
    ids = ids_ref[...]
    before = before_ref[...]
    for image in range(images + 1):
        starts[image] = before[image, 0]

    own = lax.rem(lax.axis_index("grp"), HEADS)
    for step, (by, ref) in enumerate(zip(EARLY + LATE, got_refs)):
        first = jnp.bitwise_xor(own, by) * count
        here = pl.ds(pl.multiple_of(halo + first, LANES), count)
        there = pl.ds(pl.multiple_of(first, LANES), count)
        if by in EARLY:
            keys[here, :] = early_keys[step * count : (step + 1) * count, :]
        else:
            keys[here, :] = turned_keys(marks[0, :, here], ref)
        values[:, here] = ref[0:PADDED]
        store_queries(marks[1, :, here], ref, queries, there)
    if halo:
        for ref, here in ((left_ref, slice(0, halo)), (right_ref, slice(length - halo, length))):
            keys[here, :] = turned_keys(marks[0, :, here], ref)
            values[:, here] = ref[0:PADDED]
    attend_images(images, ids_ref, keys, values, queries, attended, work, starts, halo)

    odd_head = lax.rem(own, 2) == 1
    mine = ids[:, halo : halo + total_rows]

    def placed(block, spare):
        even = jnp.concatenate([block[0:size], spare], axis=0)
        odd = jnp.concatenate([spare, block[0:size]], axis=0)
        return jnp.where(odd_head, odd, even)

    if piggy:
        nothing = jnp.zeros((SPARE, total_rows), jnp.float32)
        flat = placed(attended[...], nothing).astype(jnp.bfloat16)
        pooled = lax.dot_general(
            image_rows(mine, images), flat, (((1,), (1,)), ((), ())), preferred_element_type=jnp.float32
        )
        pooled = split_in_two(pooled, images)
        sums = spare_sums(got_refs)
        sums = split_in_two(sums + pltpu.roll(sums, images, axis=0), images)
        spare = jnp.concatenate(
            [pooled, jnp.zeros((SPARE, LANES - padded), jnp.float32), sums], axis=1
        )
        texts = text_ref[...].astype(jnp.float32)
        parts = [texts[:, at : at + count] for at in range(0, texts.shape[1], count)]
        unused = TEXT_ROWS - images * len(parts)
        below = jnp.concatenate(parts + [jnp.zeros((unused, count), jnp.float32)] * (unused > 0), axis=0)
        below = below.astype(jnp.bfloat16)
    else:
        spare = jnp.zeros((SPARE, count), jnp.float32)
    for by, out_ref in zip(ORDER, out_refs):
        there = pl.multiple_of(jnp.bitwise_xor(own, by) * count, LANES)
        out_ref[0:padded] = placed(attended[:, pl.ds(there, count)], spare).astype(jnp.bfloat16)
        if piggy:
            out_ref[padded:] = below


def joined_heads(got_refs, out_weight_ref, flat, weight):
    own = lax.rem(lax.axis_index("grp"), HEADS)
    spares = []
    for step, (by, got_ref) in enumerate(zip(ORDER, got_refs)):
        head = jnp.bitwise_xor(own, by)
        odd = lax.rem(head, 2)
        first = pl.multiple_of(lax.div(head, 2) * (2 * SIZE) + odd * (SIZE - SPARE), 16)
        at = step * PADDED
        weight[at : at + PADDED] = out_weight_ref[pl.ds(first, PADDED), :]
        top = got_ref[0:16].astype(jnp.float32)
        bottom = got_ref[PADDED - 16 : PADDED].astype(jnp.float32)
        spares.append(jnp.where(odd == 1, top[:SPARE], bottom[SPARE:]))
        top = jnp.concatenate([jnp.where(odd == 1, 0.0, top[:SPARE]), top[SPARE:]], axis=0)
        bottom = jnp.concatenate([bottom[:SPARE], jnp.where(odd == 1, bottom[SPARE:], 0.0)], axis=0)
        flat[at : at + 16] = top.astype(jnp.bfloat16)
        flat[at + 16 : at + PADDED - 16] = got_ref[16 : PADDED - 16]
        flat[at + PADDED - 16 : at + PADDED] = bottom.astype(jnp.bfloat16)
    return spares


def send_mixed_rows(rows_ref, flat, weight, turned, mixed, mixed_ref, sems):
    turned[...] = flat[...].T
    pieces = sems.shape[0]
    step = rows_ref.shape[0] // pieces
    copies = []
    for piece in range(pieces):
        cut = slice(piece * step, (piece + 1) * step)
        added = jnp.dot(turned[cut, :], weight[...], preferred_element_type=jnp.float32)
        mixed[cut, :] = (rows_ref[cut, :].astype(jnp.float32) + added).astype(jnp.bfloat16)
        copies.append(pltpu.make_async_copy(mixed.at[cut], mixed_ref.at[cut], sems.at[piece]))
        copies[-1].start()
    return copies


def unit_rows(matrix):
    return matrix * lax.rsqrt(jnp.sum(matrix * matrix, axis=1, keepdims=True) + 1e-06)


def losses(cosine, labels):
    logits = -labels * (logit_scale * cosine + logit_bias)
    return jnp.maximum(logits, 0.0) + jnp.log1p(jnp.exp(-jnp.abs(logits)))


def finish_kernel(images, rows_ref, out_weight_ref, text_ref, *rest):
    got_refs, rest = rest[:HEADS], rest[HEADS:]
    mixed_ref, loss_ref, flat, weight, turned, mixed, sems, pooled_heads, patch_sums, far_texts = rest
    spares = joined_heads(got_refs, out_weight_ref, flat, weight)
    copies = send_mixed_rows(rows_ref, flat, weight, turned, mixed, mixed_ref, sems)
    own = lax.rem(lax.axis_index("grp"), HEADS)
    patch_sums[:, HEADS * LANES :] = spares[0][:, 2 * LANES :]
    for step, (by, spare) in enumerate(zip(ORDER, spares)):
        pooled_heads[:, step * PADDED : (step + 1) * PADDED] = spare[:, 0:PADDED]
        head = jnp.bitwise_xor(own, by)
        patch_sums[:, pl.ds(pl.multiple_of(head * LANES, LANES), LANES)] = spare[:, LANES : 2 * LANES]
        below = got_refs[step][PADDED:].astype(jnp.float32)
        count = below.shape[1]
        for part in range(patch_sums.shape[1] // count):
            here = slice(part * count, (part + 1) * count)
            far_texts[head, :, here] = below[part * images : (part + 1) * images]
    pooled = jnp.dot(
        pooled_heads[...].astype(jnp.bfloat16), weight[...], preferred_element_type=jnp.float32
    )
    pooled = pooled + patch_sums[...]
    pooled = pooled + pltpu.roll(pooled, images, axis=0)
    image_vecs = unit_rows(pooled)
    others = [far_texts[place] for place in range(lax.axis_size("blk") - 1)]
    texts = jnp.concatenate([text_ref[...].astype(jnp.float32)] + others, axis=0)
    text_vecs = unit_rows(texts)
    cosine = lax.dot_general(
        text_vecs,
        image_vecs,
        (((1,), (1,)), ((), ())),
        precision=lax.Precision.HIGHEST,
        preferred_element_type=jnp.float32,
    )
    text = lax.broadcasted_iota(jnp.int32, cosine.shape, 0)
    image = lax.broadcasted_iota(jnp.int32, cosine.shape, 1)
    terms = losses(cosine, jnp.where(text == image, 1.0, -1.0))
    loss_ref[...] = jnp.sum(terms, axis=0, keepdims=True)[:, 0:images]
    for copy in copies:
        copy.wait()


def mix_kernel(rows_ref, out_weight_ref, *rest):
    got_refs, rest = rest[:HEADS], rest[HEADS:]
    mixed_ref, flat, weight, turned, mixed, sems = rest
    joined_heads(got_refs, out_weight_ref, flat, weight)
    for copy in send_mixed_rows(rows_ref, flat, weight, turned, mixed, mixed_ref, sems):
        copy.wait()


def in_vmem(count):
    return [pl.BlockSpec(memory_space=pltpu.VMEM)] * count


def in_hbm(value):
    return pltpu.with_memory_space_constraint(value, pltpu.HBM)


def call(kernel, out_shape, scratch, in_specs, flops, out_specs=None):
    if out_specs is None:
        out_specs = jax.tree.map(lambda _: pl.BlockSpec(memory_space=pltpu.VMEM), out_shape)
    return pl.pallas_call(
        kernel,
        out_shape=out_shape,
        in_specs=in_specs,
        out_specs=out_specs,
        scratch_shapes=scratch,
        compiler_params=pltpu.CompilerParams(vmem_limit_bytes=VMEM_LIMIT),
        cost_estimate=pl.CostEstimate(flops=flops, bytes_accessed=8 << 20, transcendentals=0),
    )


def moved(value, axis, pairs):
    return lax.ppermute(value, axis, pairs)


def partner(place, by, peers):
    return place ^ by if peers & (peers - 1) == 0 else (place + by) % peers


def all_texts(texts):
    peers = lax.axis_size("blk")
    steps = [[(partner(i, by, peers), i) for i in range(peers)] for by in range(1, peers)]
    return jnp.concatenate([texts] + [moved(texts, "blk", pairs) for pairs in steps], axis=0)


def one_text_block(texts):
    peers = lax.axis_size("blk")
    pairs = []
    for place in range(lax.axis_size("grp")):
        by = place % (peers - 1) + 1
        pairs += [(place * peers + partner(i, by, peers), place * peers + i) for i in range(peers)]
    return moved(texts, ("grp", "blk"), pairs)


def traded(blocks):
    peers = range(lax.axis_size("grp"))
    trades = {by: moved(blocks[by], "grp", [(i, i ^ by) for i in peers]) for by in ORDER if by}
    return {**trades, 0: blocks[0]}


def local(patches, segment_ids, qkv_weight, out_weight, text_embed):
    rows = patches[0]
    count, depth = rows.shape
    width = out_weight.shape[0]
    size = width // HEADS
    padded = size + SPARE
    images = text_embed.shape[0]
    group_size = lax.axis_size("grp")
    parts = group_size // HEADS
    piggy = (
        parts == 1
        and 2 * images == SPARE
        and count >= depth - (HEADS - 2) * LANES
        and depth % count == 0
        and images * (depth // count) <= TEXT_ROWS
        and 1 < lax.axis_size("blk") <= HEADS + 1
    )
    bf16, f32 = jnp.bfloat16, jnp.float32
    shape = jax.ShapeDtypeStruct

    block = shape((3 * size + SPARE, count), bf16)
    hbm = pl.BlockSpec(memory_space=pltpu.HBM)
    turned_weight = qkv_weight.T
    normed, sums, *sent = call(
        functools.partial(far_kernel, images, piggy),
        (shape((depth, count), bf16), shape((SPARE, depth), f32), block, block),
        [
            pltpu.VMEM((1, count), jnp.int32),
            pltpu.VMEM((count, depth), bf16),
            pltpu.VMEM((3, 2 * size, depth), bf16),
            pltpu.SemaphoreType.DMA,
            pltpu.SemaphoreType.DMA,
            pltpu.SemaphoreType.DMA((3,)),
        ],
        [hbm] * 3,
        2 * count * depth * 6 * size,
    )(in_hbm(segment_ids), in_hbm(rows), in_hbm(turned_weight))
    sent += call(
        functools.partial(near_kernel, piggy),
        (block,) * 6,
        [],
        in_vmem(3),
        2 * count * depth * 18 * size,
    )(normed, sums, turned_weight)
    sent = dict(zip((6, 7, 2, 3, 4, 5, 0, 1), sent))
    if piggy:
        late_texts, sent[0] = lax.optimization_barrier((text_embed, sent[0]))
        halos_and_texts = [one_text_block(late_texts)]
    else:
        halos_and_texts = []
    got = traded(sent)

    length = HEADS * count
    halo = 0
    near_ids = segment_ids
    if parts > 1:
        halo = rounded_up(MAXP - 1, LANES)
        part = lax.axis_index("grp") // HEADS
        whole_ids = jnp.concatenate(
            [
                jnp.full((1, halo), -1, jnp.int32),
                segment_ids,
                jnp.full((1, halo), images, jnp.int32),
            ],
            axis=1,
        )
        near_ids = lax.dynamic_slice_in_dim(whole_ids, part * length, length + 2 * halo, axis=1)
        order = jnp.bitwise_xor(lax.axis_index("grp") % HEADS, jnp.arange(HEADS))
        flat = jnp.stack([got[by] for by in range(HEADS)])[order][:, : 2 * size].transpose(1, 0, 2).reshape(2 * size, length)
        flat = jnp.concatenate([flat, jnp.zeros((16, length), bf16)], axis=0)
        ahead = [(i, i + HEADS) for i in range(group_size - HEADS)]
        back = [(i + HEADS, i) for i in range(group_size - HEADS)]
        left = moved(flat[:, length - halo :], "grp", ahead)
        right = moved(flat[:, :halo], "grp", back)
        halos_and_texts += [left, right]
    reach = length + 2 * halo
    window = min(rounded_up(MAXP + LANES - 1, LANES), reach)
    tile = 2 * LANES
    early_keys, marks, before = call(
        functools.partial(prepare_kernel, images, halo),
        (
            shape((len(EARLY) * count, LANES), bf16),
            shape((2, SPARE, reach), f32),
            shape((rounded_up(images + 1, SPARE), LANES), jnp.int32),
        ),
        [],
        in_vmem(1 + len(EARLY)),
        1 << 30,
    )(near_ids, *[got[by] for by in EARLY])
    operands = [near_ids, before, marks, early_keys, *[got[by] for by in EARLY + LATE], *halos_and_texts]
    answers = call(
        functools.partial(attend_kernel, images, piggy, halo),
        (shape((padded + TEXT_ROWS * piggy, count), bf16),) * HEADS,
        [
            pltpu.VMEM((reach, LANES), bf16),
            pltpu.VMEM((padded, reach), bf16),
            pltpu.VMEM((LANES, length), bf16),
            pltpu.VMEM((padded, length), f32),
            pltpu.VMEM((window, tile), f32),
            pltpu.VMEM((window, tile), f32),
            pltpu.VMEM((1, tile), f32),
            pltpu.VMEM((1, tile), f32),
            pltpu.SMEM((images + 1,), jnp.int32),
        ],
        in_vmem(len(operands)),
        4 * size * length * MAXP,
    )(*operands)
    home = traded(dict(zip(ORDER, answers)))
    home = [home[by] for by in ORDER]

    joined = [
        pltpu.VMEM((HEADS * padded, count), bf16),
        pltpu.VMEM((HEADS * padded, depth), bf16),
        pltpu.VMEM((count, HEADS * padded), bf16),
        pltpu.VMEM((count, depth), bf16),
        pltpu.SemaphoreType.DMA((3,)),
    ]
    flops = 2 * count * depth * width
    if piggy:
        mixed, row_loss = call(
            functools.partial(finish_kernel, images),
            (shape((count, depth), bf16), shape((1, images), f32)),
            joined
            + [
                pltpu.VMEM((SPARE, HEADS * padded), f32),
                pltpu.VMEM((SPARE, depth), f32),
                pltpu.VMEM((HEADS, images, depth), f32),
            ],
            in_vmem(3 + HEADS),
            flops,
            (hbm, pl.BlockSpec(memory_space=pltpu.VMEM)),
        )(rows, out_weight, text_embed, *home)
        return (mixed[None], row_loss[0])
    mixed = call(mix_kernel, shape((count, depth), bf16), joined, in_vmem(2 + HEADS), flops, hbm)(
        rows, out_weight, *home
    )
    own_ids = lax.dynamic_slice_in_dim(segment_ids[0], lax.axis_index("grp") * count, count)
    onehot = (own_ids[None, :] == jnp.arange(images, dtype=jnp.int32)[:, None]).astype(bf16)
    pooled = lax.psum(jnp.dot(onehot, mixed, preferred_element_type=f32), "grp")
    text_vecs = unit_rows(all_texts(text_embed).astype(f32))
    cosine = jnp.dot(unit_rows(pooled), text_vecs.T, precision=lax.Precision.HIGHEST)
    same = jnp.arange(images)[:, None] == jnp.arange(text_vecs.shape[0])[None, :]
    row_loss = jnp.sum(losses(cosine, jnp.where(same, 1.0, -1.0)), axis=1)
    return (mixed[None], row_loss)


def solution(mesh):
    placed = (P("blk", "grp", None), P("blk", None), P(), P(), P("blk", None))
    return jax.shard_map(
        local,
        mesh=mesh,
        in_specs=placed,
        out_specs=(P("blk", "grp", None), P("blk")),
        check_vma=False,
    )
```

```python
import functools
import math

import jax
import jax.numpy as jnp
from jax import lax
from jax.experimental import pallas as pl
from jax.experimental.pallas import tpu as pltpu
from jax.sharding import PartitionSpec as P

HEADS = 8
MAXP = 1024
LANES = 128
SPARE = 8
SIZE = 72
PADDED = SIZE + SPARE
KEY_AT = SIZE - SPARE
QUERY_AT = 2 * SIZE
TEXT_ROWS = 16
HIDDEN = -1e30
ORDER = (6, 7, 2, 4, 3, 5, 1, 0)
EARLY = (6, 7, 1, 0)
LATE = (2, 4, 3, 5)
SECOND = (1, 2, 0)

logit_scale = 30.0
logit_bias = -5.0

VMEM_LIMIT = 32 * 1024 * 1024


def rounded_up(value, step):
    return (value + step - 1) // step * step


def split_in_two(total, images):
    row = lax.broadcasted_iota(jnp.int32, total.shape, 0)
    main = total.astype(jnp.bfloat16).astype(jnp.float32)
    return jnp.where(row < images, main, total - main)


def image_rows(ids, images):
    row = lax.broadcasted_iota(jnp.int32, (SPARE, ids.shape[1]), 0)
    return (lax.rem(row, images) == ids).astype(jnp.float32).astype(jnp.bfloat16)


def head_blocks(query, key, value, sums, pair):
    size = query.shape[0] // 2
    count = query.shape[1]
    for place in range(2):
        here = slice(place * size, (place + 1) * size)
        if sums is None:
            spare = jnp.zeros((SPARE, count), jnp.float32)
        else:
            first = pl.multiple_of((2 * pair + place) * LANES, LANES)
            parts = [sums[:, pl.ds(first, LANES)], sums[:, HEADS * LANES :]]
            held = sum(part.shape[1] for part in parts)
            spare = jnp.concatenate(parts + [jnp.zeros((SPARE, count - held), jnp.float32)], axis=1)
        block = jnp.concatenate([value[here], key[here], spare, query[here]], axis=0)
        yield block.astype(jnp.bfloat16)


def store_by_core(core, blocks, same_ref, cross_ref):
    first, second = blocks

    @pl.when(core == 0)
    def _():
        same_ref[...] = first
        cross_ref[...] = second

    @pl.when(core == 1)
    def _():
        same_ref[...] = second
        cross_ref[...] = first


def place_in_group():
    own = lax.rem(lax.axis_index("grp"), HEADS)
    return lax.div(own, 2), lax.rem(own, 2)


def project_pair(weight, normed, sums, pair):
    turned = jnp.dot(weight, normed, preferred_element_type=jnp.float32)
    wide = turned.shape[0] // 3
    return head_blocks(turned[:wide], turned[wide : 2 * wide], turned[2 * wide :], sums, pair)


def far_kernel(images, piggy, ids_ref, rows_ref, weight_ref, normed_ref, sums_ref, rest_ref, same_ref, cross_ref, own_ids, rows_held, weight, id_sem, row_sems, sems):
    count, depth = rows_ref.shape
    width = weight_ref.shape[0] // 3
    wide = weight.shape[0] // 3
    pieces = row_sems.shape[0]
    step = count // pieces
    cuts = [slice(piece * step, (piece + 1) * step) for piece in range(pieces)]
    row_fetches = [
        pltpu.make_async_copy(rows_ref.at[cut], rows_held.at[cut], row_sems.at[piece])
        for piece, cut in enumerate(cuts)
    ]
    for fetch in row_fetches:
        fetch.start()
    own = pl.multiple_of(lax.axis_index("grp") * count, LANES)
    ids_fetch = pltpu.make_async_copy(ids_ref.at[:, pl.ds(own, count)], own_ids, id_sem)
    ids_fetch.start()
    pair, core = place_in_group()
    fetches = []
    for place, move in enumerate((3,) + SECOND):
        for at in range(3):
            first = pl.multiple_of(at * width + jnp.bitwise_xor(pair, move) * wide, 16)
            if place == 0:
                target = weight.at[at * wide : (at + 1) * wide]
            else:
                target = rest_ref.at[place - 1, at * wide : (at + 1) * wide]
            fetches.append(
                pltpu.make_async_copy(weight_ref.at[pl.ds(first, wide)], target, sems.at[3 * place + at])
            )
            fetches[-1].start()
    for fetch, cut in zip(row_fetches, cuts):
        fetch.wait()
        values = rows_held[cut, :].astype(jnp.float32)
        center = values - jnp.mean(values, axis=1, keepdims=True)
        spread = jnp.mean(center * center, axis=1, keepdims=True)
        normed_ref[:, cut] = (center * lax.rsqrt(spread + 1e-06)).astype(jnp.bfloat16).T
    ids_fetch.wait()
    if piggy:
        sums = jnp.dot(image_rows(own_ids[...], images), rows_held[...], preferred_element_type=jnp.float32)
        sums_ref[...] = split_in_two(sums, images)
    for fetch in fetches[:3]:
        fetch.wait()
    blocks = project_pair(
        weight[...], normed_ref[...], sums_ref if piggy else None, jnp.bitwise_xor(pair, 3)
    )
    store_by_core(core, blocks, same_ref, cross_ref)
    for fetch in fetches[3:]:
        fetch.wait()


def near_kernel(piggy, normed_ref, sums_ref, weight_ref, *out_refs):
    own, core = place_in_group()
    for step, move in enumerate(SECOND):
        blocks = project_pair(
            weight_ref[step], normed_ref[...], sums_ref if piggy else None, jnp.bitwise_xor(own, move)
        )
        store_by_core(core, blocks, *out_refs[2 * step : 2 * step + 2])


def count_before(images, ids):
    image = lax.broadcasted_iota(jnp.int32, (rounded_up(images + 1, SPARE), ids.shape[1]), 0)
    before = jnp.sum((ids < image).astype(jnp.int32), axis=1, keepdims=True)
    return jnp.broadcast_to(before, (before.shape[0], LANES))


def write_marks(images, ids, marks):
    bits = max(1, (images - 1).bit_length())
    row = lax.broadcasted_iota(jnp.int32, (SPARE, ids.shape[1]), 0)
    bit = jnp.bitwise_and(lax.shift_right_logical(jnp.broadcast_to(ids, row.shape), row >> 1), 1)
    odd = jnp.bitwise_and(row, 1)
    used = row < 2 * bits
    outside = jnp.logical_or(ids < 0, ids >= images)
    key_side = jnp.where(odd == 1, bit, 1 - bit).astype(jnp.float32)
    key_side = jnp.where(outside, 1.0, key_side)
    marks[0] = jnp.where(used, key_side * HIDDEN, 0.0)
    marks[1] = jnp.where(used, jnp.where(odd == 1, 1 - bit, bit), 0).astype(jnp.float32)


def spare_sums(refs):
    parts = [ref[QUERY_AT : QUERY_AT + 16].astype(jnp.float32)[0:SPARE, 0 : 2 * LANES] for ref in refs]
    return sum(parts[1:], parts[0])


def image_at(images, starts, position):
    found = jnp.int32(0)
    for image in range(1, images):
        found += (starts[image] <= position).astype(jnp.int32)
    return found


def attend_images(images, ids_ref, keys, values, queries, attended, work, starts, halo):
    scores_a, scores_b, tops_a, tops_b = work
    query_base = halo
    window, tile = scores_a.shape
    size = attended.shape[0] - SPARE
    held = queries.shape[1]
    tiles = held // tile

    def bounds(image):
        first = lax.div(jnp.maximum(starts[image] - query_base, 0), tile)
        last = lax.div(jnp.minimum(starts[image + 1] - query_base, held) - 1, tile)
        return jnp.minimum(first, tiles - 1), last

    def after(image):
        return jnp.minimum(image + 1, images - 1)

    def following(state):
        at, image = state
        more = at < bounds(image)[1]
        later = after(image)
        return jnp.where(more, at + 1, bounds(later)[0]), jnp.where(more, image, later)

    def window_of(image):
        begin = lax.div(starts[image], LANES) * LANES
        return pl.ds(pl.multiple_of(jnp.minimum(begin, keys.shape[0] - window), LANES), window)

    def score(state, scores, tops):
        at, image = state
        query = queries[:, pl.ds(pl.multiple_of(at * tile, tile), tile)]
        found = jnp.dot(keys[window_of(image), :], query, preferred_element_type=jnp.float32)
        scores[...] = found
        tops[...] = jnp.max(found, axis=0, keepdims=True)

    def weigh(state, scores, tops):
        at, image = state
        first = pl.multiple_of(at * tile, tile)
        labels = ids_ref[:, pl.ds(pl.multiple_of(query_base + first, LANES), tile)]
        probs = jnp.exp2((scores[...] - tops[...]) * (size ** (-0.5) * math.log2(math.e)))
        share = 1.0 / jnp.sum(probs, axis=0, keepdims=True)
        weighted = jnp.dot(
            values[:, window_of(image)], probs.astype(jnp.bfloat16), preferred_element_type=jnp.float32
        )
        place = (slice(None), pl.ds(first, tile))
        attended[place] = jnp.where(labels == image, weighted * share, attended[place])

    low = image_at(images, starts, query_base)
    high = image_at(images, starts, query_base + held - 1)
    pairs = jnp.int32(0)
    for image in range(images):
        first, last = bounds(image)
        wanted = jnp.logical_and(low <= image, image <= high)
        pairs += jnp.where(wanted, last - first + 1, 0)

    def two_pairs(_, state):
        second = following(state)
        score(second, scores_b, tops_b)
        weigh(state, scores_a, tops_a)
        third = following(second)
        score(third, scores_a, tops_a)
        weigh(second, scores_b, tops_b)
        return third

    begun = (jnp.int32(0), low)
    score(begun, scores_a, tops_a)
    last_state = lax.fori_loop(0, lax.div(pairs, 2), two_pairs, begun)

    @pl.when(lax.rem(pairs, 2) == 1)
    def _():
        weigh(last_state, scores_a, tops_a)


def turned_keys(marked, block_ref):
    block = block_ref[KEY_AT : KEY_AT + PADDED].astype(jnp.float32)
    nothing = jnp.zeros((LANES - PADDED, block.shape[1]), jnp.float32)
    full = jnp.concatenate([marked, block[SPARE:], nothing], axis=0)
    return full.astype(jnp.bfloat16).T


def store_queries(marked, block_ref, queries, there):
    edge = block_ref[QUERY_AT : QUERY_AT + 16].astype(jnp.float32)
    edge = jnp.concatenate([marked, edge[SPARE:]], axis=0)
    queries[0:16, there] = edge.astype(jnp.bfloat16)
    queries[16:PADDED, there] = block_ref[QUERY_AT + 16 : QUERY_AT + PADDED]
    queries[PADDED:, there] = jnp.zeros((LANES - PADDED, block_ref.shape[1]), jnp.bfloat16)


def prepare_kernel(images, halo, ids_ref, out_weight_ref, *rest):
    got_refs, (keys, marks, before, weight, sems) = rest[: len(EARLY)], rest[len(EARLY) :]
    count = got_refs[0].shape[1]
    fetches = []
    for step, by in enumerate(ORDER):
        head = jnp.bitwise_xor(lax.rem(lax.axis_index("grp"), HEADS), by)
        first = lax.div(head, 2) * (2 * SIZE) + lax.rem(head, 2) * (SIZE - SPARE)
        fetches.append(
            pltpu.make_async_copy(
                out_weight_ref.at[pl.ds(pl.multiple_of(first, 16), PADDED)],
                weight.at[step * PADDED : (step + 1) * PADDED],
                sems.at[step],
            )
        )
        fetches[-1].start()
    before[...] = count_before(images, ids_ref[...])
    write_marks(images, ids_ref[...], marks)
    own = lax.rem(lax.axis_index("grp"), HEADS)
    for step, (by, ref) in enumerate(zip(EARLY, got_refs)):
        first = jnp.bitwise_xor(own, by) * count
        here = pl.ds(pl.multiple_of(halo + first, LANES), count)
        keys[step * count : (step + 1) * count, :] = turned_keys(marks[0, :, here], ref)
    for fetch in fetches:
        fetch.wait()


def attend_kernel(images, piggy, halo, ids_ref, before_ref, marks, early_keys, *rest):
    got_refs, rest = rest[:HEADS], rest[HEADS:]
    if piggy:
        text_ref, *rest = rest
    if halo:
        left_ref, right_ref, *rest = rest
    out_refs, rest = rest[:HEADS], rest[HEADS:]
    keys, values, queries, attended, *work, starts = rest
    count = got_refs[0].shape[1]
    padded = attended.shape[0]
    size = padded - SPARE
    total_rows = HEADS * count
    length = ids_ref.shape[1]
    ids = ids_ref[...]
    before = before_ref[...]
    for image in range(images + 1):
        starts[image] = before[image, 0]

    own = lax.rem(lax.axis_index("grp"), HEADS)
    for step, (by, ref) in enumerate(zip(EARLY + LATE, got_refs)):
        first = jnp.bitwise_xor(own, by) * count
        here = pl.ds(pl.multiple_of(halo + first, LANES), count)
        there = pl.ds(pl.multiple_of(first, LANES), count)
        if by in EARLY:
            keys[here, :] = early_keys[step * count : (step + 1) * count, :]
        else:
            keys[here, :] = turned_keys(marks[0, :, here], ref)
        values[:, here] = ref[0:PADDED]
        store_queries(marks[1, :, here], ref, queries, there)
    if halo:
        for ref, here in ((left_ref, slice(0, halo)), (right_ref, slice(length - halo, length))):
            keys[here, :] = turned_keys(marks[0, :, here], ref)
            values[:, here] = ref[0:PADDED]
    attend_images(images, ids_ref, keys, values, queries, attended, work, starts, halo)

    odd_head = lax.rem(own, 2) == 1
    mine = ids[:, halo : halo + total_rows]

    def placed(block, spare):
        even = jnp.concatenate([block[0:size], spare], axis=0)
        odd = jnp.concatenate([spare, block[0:size]], axis=0)
        return jnp.where(odd_head, odd, even)

    if piggy:
        nothing = jnp.zeros((SPARE, total_rows), jnp.float32)
        flat = placed(attended[...], nothing).astype(jnp.bfloat16)
        pooled = lax.dot_general(
            image_rows(mine, images), flat, (((1,), (1,)), ((), ())), preferred_element_type=jnp.float32
        )
        pooled = split_in_two(pooled, images)
        sums = spare_sums(got_refs)
        sums = split_in_two(sums + pltpu.roll(sums, images, axis=0), images)
        spare = jnp.concatenate(
            [pooled, jnp.zeros((SPARE, LANES - padded), jnp.float32), sums], axis=1
        )
        texts = text_ref[...].astype(jnp.float32)
        parts = [texts[:, at : at + count] for at in range(0, texts.shape[1], count)]
        unused = TEXT_ROWS - images * len(parts)
        below = jnp.concatenate(parts + [jnp.zeros((unused, count), jnp.float32)] * (unused > 0), axis=0)
        below = below.astype(jnp.bfloat16)
    else:
        spare = jnp.zeros((SPARE, count), jnp.float32)
    for by, out_ref in zip(ORDER, out_refs):
        there = pl.multiple_of(jnp.bitwise_xor(own, by) * count, LANES)
        out_ref[0:padded] = placed(attended[:, pl.ds(there, count)], spare).astype(jnp.bfloat16)
        if piggy:
            out_ref[padded:] = below


def joined_heads(got_refs, flat):
    own = lax.rem(lax.axis_index("grp"), HEADS)
    spares = []
    for step, (by, got_ref) in enumerate(zip(ORDER, got_refs)):
        odd = lax.rem(jnp.bitwise_xor(own, by), 2)
        at = step * PADDED
        top = got_ref[0:16].astype(jnp.float32)
        bottom = got_ref[PADDED - 16 : PADDED].astype(jnp.float32)
        spares.append(jnp.where(odd == 1, top[:SPARE], bottom[SPARE:]))
        top = jnp.concatenate([jnp.where(odd == 1, 0.0, top[:SPARE]), top[SPARE:]], axis=0)
        bottom = jnp.concatenate([bottom[:SPARE], jnp.where(odd == 1, bottom[SPARE:], 0.0)], axis=0)
        flat[at : at + 16] = top.astype(jnp.bfloat16)
        flat[at + 16 : at + PADDED - 16] = got_ref[16 : PADDED - 16]
        flat[at + PADDED - 16 : at + PADDED] = bottom.astype(jnp.bfloat16)
    return spares


def send_mixed_rows(rows_ref, weight_ref, turned, mixed, mixed_ref, sems):
    pieces = sems.shape[0]
    count = rows_ref.shape[0]
    step = rows_ref.shape[1] // pieces
    copies, below = [], []
    for piece in range(pieces):
        cut = slice(piece * step, (piece + 1) * step)
        added = jnp.dot(turned[...], weight_ref[:, cut], preferred_element_type=jnp.float32)
        mixed[:, cut] = (rows_ref[:, cut].astype(jnp.float32) + added[:count]).astype(jnp.bfloat16)
        below.append(added[count:])
        copies.append(pltpu.make_async_copy(mixed.at[:, cut], mixed_ref.at[:, cut], sems.at[piece]))
        copies[-1].start()
    return copies, jnp.concatenate(below, axis=1)


def unit_rows(matrix):
    return matrix * lax.rsqrt(jnp.sum(matrix * matrix, axis=1, keepdims=True) + 1e-06)


def losses(cosine, labels):
    logits = -labels * (logit_scale * cosine + logit_bias)
    return jnp.maximum(logits, 0.0) + jnp.log1p(jnp.exp(-jnp.abs(logits)))


def finish_kernel(images, rows_ref, weight_ref, text_ref, *rest):
    got_refs, rest = rest[:HEADS], rest[HEADS:]
    mixed_ref, loss_ref, flat, turned, mixed, sems, pooled_heads, patch_sums, far_texts = rest
    spares = joined_heads(got_refs, flat)
    own = lax.rem(lax.axis_index("grp"), HEADS)
    count = rows_ref.shape[0]
    patch_sums[:, HEADS * LANES :] = spares[0][:, 2 * LANES :]
    for step, (by, spare) in enumerate(zip(ORDER, spares)):
        pooled_heads[0:SPARE, step * PADDED : (step + 1) * PADDED] = spare[:, 0:PADDED]
        head = jnp.bitwise_xor(own, by)
        patch_sums[:, pl.ds(pl.multiple_of(head * LANES, LANES), LANES)] = spare[:, LANES : 2 * LANES]
        below = got_refs[step][PADDED:].astype(jnp.float32)
        for part in range(patch_sums.shape[1] // count):
            here = slice(part * count, (part + 1) * count)
            far_texts[head, :, here] = below[part * images : (part + 1) * images]
    pooled_heads[SPARE:, :] = jnp.zeros_like(pooled_heads[SPARE:, :])
    turned[0:count, :] = flat[...].T
    turned[count:, :] = pooled_heads[...].astype(jnp.bfloat16)
    copies, pooled = send_mixed_rows(rows_ref, weight_ref, turned, mixed, mixed_ref, sems)
    pooled = pooled[0:SPARE] + patch_sums[...]
    pooled = pooled + pltpu.roll(pooled, images, axis=0)
    image_vecs = unit_rows(pooled)
    others = [far_texts[place] for place in range(lax.axis_size("blk") - 1)]
    texts = jnp.concatenate([text_ref[...].astype(jnp.float32)] + others, axis=0)
    text_vecs = unit_rows(texts)
    cosine = lax.dot_general(
        text_vecs,
        image_vecs,
        (((1,), (1,)), ((), ())),
        precision=lax.Precision.HIGHEST,
        preferred_element_type=jnp.float32,
    )
    text = lax.broadcasted_iota(jnp.int32, cosine.shape, 0)
    image = lax.broadcasted_iota(jnp.int32, cosine.shape, 1)
    terms = losses(cosine, jnp.where(text == image, 1.0, -1.0))
    loss_ref[...] = jnp.sum(terms, axis=0, keepdims=True)[:, 0:images]
    for copy in copies:
        copy.wait()


def mix_kernel(rows_ref, weight_ref, *rest):
    got_refs, rest = rest[:HEADS], rest[HEADS:]
    mixed_ref, flat, turned, mixed, sems = rest
    joined_heads(got_refs, flat)
    turned[...] = flat[...].T
    for copy in send_mixed_rows(rows_ref, weight_ref, turned, mixed, mixed_ref, sems)[0]:
        copy.wait()


def in_vmem(count):
    return [pl.BlockSpec(memory_space=pltpu.VMEM)] * count


def in_hbm(value):
    return pltpu.with_memory_space_constraint(value, pltpu.HBM)


def call(kernel, out_shape, scratch, in_specs, flops, out_specs=None):
    if out_specs is None:
        out_specs = jax.tree.map(lambda _: pl.BlockSpec(memory_space=pltpu.VMEM), out_shape)
    return pl.pallas_call(
        kernel,
        out_shape=out_shape,
        in_specs=in_specs,
        out_specs=out_specs,
        scratch_shapes=scratch,
        compiler_params=pltpu.CompilerParams(vmem_limit_bytes=VMEM_LIMIT),
        cost_estimate=pl.CostEstimate(flops=flops, bytes_accessed=8 << 20, transcendentals=0),
    )


def moved(value, axis, pairs):
    return lax.ppermute(value, axis, pairs)


def partner(place, by, peers):
    return place ^ by if peers & (peers - 1) == 0 else (place + by) % peers


def all_texts(texts):
    peers = lax.axis_size("blk")
    steps = [[(partner(i, by, peers), i) for i in range(peers)] for by in range(1, peers)]
    return jnp.concatenate([texts] + [moved(texts, "blk", pairs) for pairs in steps], axis=0)


def one_text_block(texts):
    peers = lax.axis_size("blk")
    pairs = []
    for place in range(lax.axis_size("grp")):
        by = place % (peers - 1) + 1
        pairs += [(place * peers + partner(i, by, peers), place * peers + i) for i in range(peers)]
    return moved(texts, ("grp", "blk"), pairs)


def traded(blocks):
    peers = range(lax.axis_size("grp"))
    trades = {by: moved(blocks[by], "grp", [(i, i ^ by) for i in peers]) for by in ORDER if by}
    return {**trades, 0: blocks[0]}


def local(patches, segment_ids, qkv_weight, out_weight, text_embed):
    rows = patches[0]
    count, depth = rows.shape
    width = out_weight.shape[0]
    size = width // HEADS
    padded = size + SPARE
    images = text_embed.shape[0]
    group_size = lax.axis_size("grp")
    parts = group_size // HEADS
    piggy = (
        parts == 1
        and 2 * images == SPARE
        and count >= depth - (HEADS - 2) * LANES
        and depth % count == 0
        and images * (depth // count) <= TEXT_ROWS
        and 1 < lax.axis_size("blk") <= HEADS + 1
    )
    bf16, f32 = jnp.bfloat16, jnp.float32
    shape = jax.ShapeDtypeStruct

    block = shape((3 * size + SPARE, count), bf16)
    hbm = pl.BlockSpec(memory_space=pltpu.HBM)
    normed, sums, rest, *sent = call(
        functools.partial(far_kernel, images, piggy),
        (
            shape((depth, count), bf16),
            shape((SPARE, depth), f32),
            shape((len(SECOND), 6 * size, depth), bf16),
            block,
            block,
        ),
        [
            pltpu.VMEM((1, count), jnp.int32),
            pltpu.VMEM((count, depth), bf16),
            pltpu.VMEM((6 * size, depth), bf16),
            pltpu.SemaphoreType.DMA,
            pltpu.SemaphoreType.DMA((3,)),
            pltpu.SemaphoreType.DMA((3 + 3 * len(SECOND),)),
        ],
        [hbm] * 3,
        2 * count * depth * 6 * size,
    )(in_hbm(segment_ids), in_hbm(rows), in_hbm(qkv_weight.T))
    sent += call(
        functools.partial(near_kernel, piggy),
        (block,) * (2 * len(SECOND)),
        [],
        in_vmem(3),
        2 * count * depth * 18 * size,
    )(normed, sums, rest)
    sent = dict(zip((6, 7, 2, 3, 4, 5, 0, 1), sent))
    if piggy:
        late_texts, sent[0] = lax.optimization_barrier((text_embed, sent[0]))
        halos_and_texts = [one_text_block(late_texts)]
    else:
        halos_and_texts = []
    got = traded(sent)

    length = HEADS * count
    halo = 0
    near_ids = segment_ids
    if parts > 1:
        halo = rounded_up(MAXP - 1, LANES)
        part = lax.axis_index("grp") // HEADS
        whole_ids = jnp.concatenate(
            [
                jnp.full((1, halo), -1, jnp.int32),
                segment_ids,
                jnp.full((1, halo), images, jnp.int32),
            ],
            axis=1,
        )
        near_ids = lax.dynamic_slice_in_dim(whole_ids, part * length, length + 2 * halo, axis=1)
        order = jnp.bitwise_xor(lax.axis_index("grp") % HEADS, jnp.arange(HEADS))
        flat = jnp.stack([got[by] for by in range(HEADS)])[order][:, : 2 * size].transpose(1, 0, 2).reshape(2 * size, length)
        flat = jnp.concatenate([flat, jnp.zeros((16, length), bf16)], axis=0)
        ahead = [(i, i + HEADS) for i in range(group_size - HEADS)]
        back = [(i + HEADS, i) for i in range(group_size - HEADS)]
        left = moved(flat[:, length - halo :], "grp", ahead)
        right = moved(flat[:, :halo], "grp", back)
        halos_and_texts += [left, right]
    reach = length + 2 * halo
    window = min(rounded_up(MAXP + LANES - 1, LANES), reach)
    tile = 2 * LANES
    early_keys, marks, before, weight = call(
        functools.partial(prepare_kernel, images, halo),
        (
            shape((len(EARLY) * count, LANES), bf16),
            shape((2, SPARE, reach), f32),
            shape((rounded_up(images + 1, SPARE), LANES), jnp.int32),
            shape((HEADS * padded, depth), bf16),
        ),
        [pltpu.SemaphoreType.DMA((HEADS,))],
        in_vmem(1) + [hbm] + in_vmem(len(EARLY)),
        1 << 30,
    )(near_ids, in_hbm(out_weight), *[got[by] for by in EARLY])
    operands = [near_ids, before, marks, early_keys, *[got[by] for by in EARLY + LATE], *halos_and_texts]
    answers = call(
        functools.partial(attend_kernel, images, piggy, halo),
        (shape((padded + TEXT_ROWS * piggy, count), bf16),) * HEADS,
        [
            pltpu.VMEM((reach, LANES), bf16),
            pltpu.VMEM((padded, reach), bf16),
            pltpu.VMEM((LANES, length), bf16),
            pltpu.VMEM((padded, length), f32),
            pltpu.VMEM((window, tile), f32),
            pltpu.VMEM((window, tile), f32),
            pltpu.VMEM((1, tile), f32),
            pltpu.VMEM((1, tile), f32),
            pltpu.SMEM((images + 1,), jnp.int32),
        ],
        in_vmem(len(operands)),
        4 * size * length * MAXP,
    )(*operands)
    home = traded(dict(zip(ORDER, answers)))
    home = [home[by] for by in ORDER]

    joined = [
        pltpu.VMEM((HEADS * padded, count), bf16),
        pltpu.VMEM((count + 2 * SPARE * piggy, HEADS * padded), bf16),
        pltpu.VMEM((count, depth), bf16),
        pltpu.SemaphoreType.DMA((3,)),
    ]
    flops = 2 * count * depth * width
    if piggy:
        mixed, row_loss = call(
            functools.partial(finish_kernel, images),
            (shape((count, depth), bf16), shape((1, images), f32)),
            joined
            + [
                pltpu.VMEM((2 * SPARE, HEADS * padded), f32),
                pltpu.VMEM((SPARE, depth), f32),
                pltpu.VMEM((HEADS, images, depth), f32),
            ],
            in_vmem(3 + HEADS),
            flops,
            (hbm, pl.BlockSpec(memory_space=pltpu.VMEM)),
        )(rows, weight, text_embed, *home)
        return (mixed[None], row_loss[0])
    mixed = call(mix_kernel, shape((count, depth), bf16), joined, in_vmem(2 + HEADS), flops, hbm)(
        rows, weight, *home
    )
    own_ids = lax.dynamic_slice_in_dim(segment_ids[0], lax.axis_index("grp") * count, count)
    onehot = (own_ids[None, :] == jnp.arange(images, dtype=jnp.int32)[:, None]).astype(bf16)
    pooled = lax.psum(jnp.dot(onehot, mixed, preferred_element_type=f32), "grp")
    text_vecs = unit_rows(all_texts(text_embed).astype(f32))
    cosine = jnp.dot(unit_rows(pooled), text_vecs.T, precision=lax.Precision.HIGHEST)
    same = jnp.arange(images)[:, None] == jnp.arange(text_vecs.shape[0])[None, :]
    row_loss = jnp.sum(losses(cosine, jnp.where(same, 1.0, -1.0)), axis=1)
    return (mixed[None], row_loss)


def solution(mesh):
    placed = (P("blk", "grp", None), P("blk", None), P(), P(), P("blk", None))
    return jax.shard_map(
        local,
        mesh=mesh,
        in_specs=placed,
        out_specs=(P("blk", "grp", None), P("blk")),
        check_vma=False,
    )
```

```python
import functools
import math

import jax
import jax.numpy as jnp
from jax import lax
from jax.experimental import pallas as pl
from jax.experimental.pallas import tpu as pltpu
from jax.sharding import PartitionSpec as P

HEADS = 8
MAXP = 1024
LANES = 128
SPARE = 8
SIZE = 72
PADDED = SIZE + SPARE
KEY_AT = SIZE - SPARE
QUERY_AT = 2 * SIZE
TEXT_ROWS = 16
HIDDEN = -1e30
ORDER = (6, 7, 2, 4, 3, 5, 1, 0)
EARLY = (6, 7, 1, 0)
LATE = (2, 4, 3, 5)

logit_scale = 30.0
logit_bias = -5.0

VMEM_LIMIT = 32 * 1024 * 1024


def rounded_up(value, step):
    return (value + step - 1) // step * step


def split_in_two(total, images):
    row = lax.broadcasted_iota(jnp.int32, total.shape, 0)
    main = total.astype(jnp.bfloat16).astype(jnp.float32)
    return jnp.where(row < images, main, total - main)


def image_rows(ids, images):
    row = lax.broadcasted_iota(jnp.int32, (SPARE, ids.shape[1]), 0)
    return (lax.rem(row, images) == ids).astype(jnp.float32).astype(jnp.bfloat16)


def head_blocks(query, key, value, sums, pair):
    size = query.shape[0] // 2
    count = query.shape[1]
    for place in range(2):
        here = slice(place * size, (place + 1) * size)
        if sums is None:
            spare = jnp.zeros((SPARE, count), jnp.float32)
        else:
            first = pl.multiple_of((2 * pair + place) * LANES, LANES)
            parts = [sums[:, pl.ds(first, LANES)], sums[:, HEADS * LANES :]]
            held = sum(part.shape[1] for part in parts)
            spare = jnp.concatenate(parts + [jnp.zeros((SPARE, count - held), jnp.float32)], axis=1)
        block = jnp.concatenate([value[here], key[here], spare, query[here]], axis=0)
        yield block.astype(jnp.bfloat16)


def store_by_core(core, blocks, same_ref, cross_ref):
    first, second = blocks

    @pl.when(core == 0)
    def _():
        same_ref[...] = first
        cross_ref[...] = second

    @pl.when(core == 1)
    def _():
        same_ref[...] = second
        cross_ref[...] = first


def place_in_group():
    own = lax.rem(lax.axis_index("grp"), HEADS)
    return lax.div(own, 2), lax.rem(own, 2)


def far_kernel(images, piggy, ids_ref, rows_ref, weight_ref, normed_ref, sums_ref, same_ref, cross_ref, own_ids, rows_held, weight, id_sem, row_sems, sems):
    count, depth = rows_ref.shape
    width = weight_ref.shape[0] // 3
    wide = weight.shape[0] // 3
    pieces = row_sems.shape[0]
    step = count // pieces
    cuts = [slice(piece * step, (piece + 1) * step) for piece in range(pieces)]
    row_fetches = [
        pltpu.make_async_copy(rows_ref.at[cut], rows_held.at[cut], row_sems.at[piece])
        for piece, cut in enumerate(cuts)
    ]
    for fetch in row_fetches:
        fetch.start()
    own = pl.multiple_of(lax.axis_index("grp") * count, LANES)
    ids_fetch = pltpu.make_async_copy(ids_ref.at[:, pl.ds(own, count)], own_ids, id_sem)
    ids_fetch.start()
    pair, core = place_in_group()
    pair = jnp.bitwise_xor(pair, 3)
    fetches = []
    for at in range(3):
        first = pl.multiple_of(at * width + pair * wide, 16)
        fetches.append(pltpu.make_async_copy(weight_ref.at[pl.ds(first, wide)], weight.at[at * wide : (at + 1) * wide], sems.at[at]))
    for fetch in fetches:
        fetch.start()
    for fetch, cut in zip(row_fetches, cuts):
        fetch.wait()
        values = rows_held[cut, :].astype(jnp.float32)
        center = values - jnp.mean(values, axis=1, keepdims=True)
        spread = jnp.mean(center * center, axis=1, keepdims=True)
        normed_ref[:, cut] = (center * lax.rsqrt(spread + 1e-06)).astype(jnp.bfloat16).T
    ids_fetch.wait()
    if piggy:
        sums = jnp.dot(image_rows(own_ids[...], images), rows_held[...], preferred_element_type=jnp.float32)
        sums_ref[...] = split_in_two(sums, images)
    for fetch in fetches:
        fetch.wait()
    turned = jnp.dot(weight[...], normed_ref[...], preferred_element_type=jnp.float32)
    parts = [turned[at * wide : (at + 1) * wide] for at in range(3)]
    store_by_core(core, head_blocks(*parts, sums_ref if piggy else None, pair), same_ref, cross_ref)


def near_kernel(piggy, normed_ref, sums_ref, weight_ref, *out_refs):
    width = weight_ref.shape[0] // 3
    wide = 2 * width // HEADS
    own, core = place_in_group()
    for step, move in enumerate((1, 2, 0)):
        pair = jnp.bitwise_xor(own, move)
        parts = []
        for at in range(3):
            here = pl.ds(pl.multiple_of(at * width + pair * wide, 16), wide)
            parts.append(
                jnp.dot(weight_ref[here, :], normed_ref[...], preferred_element_type=jnp.float32)
            )
        blocks = head_blocks(*parts, sums_ref if piggy else None, pair)
        store_by_core(core, blocks, *out_refs[2 * step : 2 * step + 2])


def count_before(images, ids):
    image = lax.broadcasted_iota(jnp.int32, (rounded_up(images + 1, SPARE), ids.shape[1]), 0)
    before = jnp.sum((ids < image).astype(jnp.int32), axis=1, keepdims=True)
    return jnp.broadcast_to(before, (before.shape[0], LANES))


def write_marks(images, ids, marks):
    bits = max(1, (images - 1).bit_length())
    row = lax.broadcasted_iota(jnp.int32, (SPARE, ids.shape[1]), 0)
    bit = jnp.bitwise_and(lax.shift_right_logical(jnp.broadcast_to(ids, row.shape), row >> 1), 1)
    odd = jnp.bitwise_and(row, 1)
    used = row < 2 * bits
    outside = jnp.logical_or(ids < 0, ids >= images)
    key_side = jnp.where(odd == 1, bit, 1 - bit).astype(jnp.float32)
    key_side = jnp.where(outside, 1.0, key_side)
    marks[0] = jnp.where(used, key_side * HIDDEN, 0.0)
    marks[1] = jnp.where(used, jnp.where(odd == 1, 1 - bit, bit), 0).astype(jnp.float32)


def spare_sums(refs):
    parts = [ref[QUERY_AT : QUERY_AT + 16].astype(jnp.float32)[0:SPARE, 0 : 2 * LANES] for ref in refs]
    return sum(parts[1:], parts[0])


def image_at(images, starts, position):
    found = jnp.int32(0)
    for image in range(1, images):
        found += (starts[image] <= position).astype(jnp.int32)
    return found


def attend_images(images, ids_ref, keys, values, queries, attended, work, starts, halo):
    scores_a, scores_b, tops_a, tops_b = work
    query_base = halo
    window, tile = scores_a.shape
    size = attended.shape[0] - SPARE
    held = queries.shape[1]
    tiles = held // tile

    def bounds(image):
        first = lax.div(jnp.maximum(starts[image] - query_base, 0), tile)
        last = lax.div(jnp.minimum(starts[image + 1] - query_base, held) - 1, tile)
        return jnp.minimum(first, tiles - 1), last

    def after(image):
        return jnp.minimum(image + 1, images - 1)

    def following(state):
        at, image = state
        more = at < bounds(image)[1]
        later = after(image)
        return jnp.where(more, at + 1, bounds(later)[0]), jnp.where(more, image, later)

    def window_of(image):
        begin = lax.div(starts[image], LANES) * LANES
        return pl.ds(pl.multiple_of(jnp.minimum(begin, keys.shape[0] - window), LANES), window)

    def score(state, scores, tops):
        at, image = state
        query = queries[:, pl.ds(pl.multiple_of(at * tile, tile), tile)]
        found = jnp.dot(keys[window_of(image), :], query, preferred_element_type=jnp.float32)
        scores[...] = found
        tops[...] = jnp.max(found, axis=0, keepdims=True)

    def weigh(state, scores, tops):
        at, image = state
        first = pl.multiple_of(at * tile, tile)
        labels = ids_ref[:, pl.ds(pl.multiple_of(query_base + first, LANES), tile)]
        probs = jnp.exp2((scores[...] - tops[...]) * (size ** (-0.5) * math.log2(math.e)))
        share = 1.0 / jnp.sum(probs, axis=0, keepdims=True)
        weighted = jnp.dot(
            values[:, window_of(image)], probs.astype(jnp.bfloat16), preferred_element_type=jnp.float32
        )
        place = (slice(None), pl.ds(first, tile))
        attended[place] = jnp.where(labels == image, weighted * share, attended[place])

    low = image_at(images, starts, query_base)
    high = image_at(images, starts, query_base + held - 1)
    pairs = jnp.int32(0)
    for image in range(images):
        first, last = bounds(image)
        wanted = jnp.logical_and(low <= image, image <= high)
        pairs += jnp.where(wanted, last - first + 1, 0)

    def two_pairs(_, state):
        second = following(state)
        score(second, scores_b, tops_b)
        weigh(state, scores_a, tops_a)
        third = following(second)
        score(third, scores_a, tops_a)
        weigh(second, scores_b, tops_b)
        return third

    begun = (jnp.int32(0), low)
    score(begun, scores_a, tops_a)
    last_state = lax.fori_loop(0, lax.div(pairs, 2), two_pairs, begun)

    @pl.when(lax.rem(pairs, 2) == 1)
    def _():
        weigh(last_state, scores_a, tops_a)


def turned_keys(marked, block_ref):
    block = block_ref[KEY_AT : KEY_AT + PADDED].astype(jnp.float32)
    nothing = jnp.zeros((LANES - PADDED, block.shape[1]), jnp.float32)
    full = jnp.concatenate([marked, block[SPARE:], nothing], axis=0)
    return full.astype(jnp.bfloat16).T


def store_queries(marked, block_ref, queries, there):
    edge = block_ref[QUERY_AT : QUERY_AT + 16].astype(jnp.float32)
    edge = jnp.concatenate([marked, edge[SPARE:]], axis=0)
    queries[0:16, there] = edge.astype(jnp.bfloat16)
    queries[16:PADDED, there] = block_ref[QUERY_AT + 16 : QUERY_AT + PADDED]
    queries[PADDED:, there] = jnp.zeros((LANES - PADDED, block_ref.shape[1]), jnp.bfloat16)


def prepare_kernel(images, halo, ids_ref, out_weight_ref, *rest):
    got_refs, (keys, marks, before, weight, sems) = rest[: len(EARLY)], rest[len(EARLY) :]
    count = got_refs[0].shape[1]
    fetches = []
    for step, by in enumerate(ORDER):
        head = jnp.bitwise_xor(lax.rem(lax.axis_index("grp"), HEADS), by)
        first = lax.div(head, 2) * (2 * SIZE) + lax.rem(head, 2) * (SIZE - SPARE)
        fetches.append(
            pltpu.make_async_copy(
                out_weight_ref.at[pl.ds(pl.multiple_of(first, 16), PADDED)],
                weight.at[step * PADDED : (step + 1) * PADDED],
                sems.at[step],
            )
        )
        fetches[-1].start()
    before[...] = count_before(images, ids_ref[...])
    write_marks(images, ids_ref[...], marks)
    own = lax.rem(lax.axis_index("grp"), HEADS)
    for step, (by, ref) in enumerate(zip(EARLY, got_refs)):
        first = jnp.bitwise_xor(own, by) * count
        here = pl.ds(pl.multiple_of(halo + first, LANES), count)
        keys[step * count : (step + 1) * count, :] = turned_keys(marks[0, :, here], ref)
    for fetch in fetches:
        fetch.wait()


def attend_kernel(images, piggy, halo, ids_ref, before_ref, marks, early_keys, *rest):
    got_refs, rest = rest[:HEADS], rest[HEADS:]
    if piggy:
        text_ref, *rest = rest
    if halo:
        left_ref, right_ref, *rest = rest
    out_refs, rest = rest[:HEADS], rest[HEADS:]
    keys, values, queries, attended, *work, starts = rest
    count = got_refs[0].shape[1]
    padded = attended.shape[0]
    size = padded - SPARE
    total_rows = HEADS * count
    length = ids_ref.shape[1]
    ids = ids_ref[...]
    before = before_ref[...]
    for image in range(images + 1):
        starts[image] = before[image, 0]

    own = lax.rem(lax.axis_index("grp"), HEADS)
    for step, (by, ref) in enumerate(zip(EARLY + LATE, got_refs)):
        first = jnp.bitwise_xor(own, by) * count
        here = pl.ds(pl.multiple_of(halo + first, LANES), count)
        there = pl.ds(pl.multiple_of(first, LANES), count)
        if by in EARLY:
            keys[here, :] = early_keys[step * count : (step + 1) * count, :]
        else:
            keys[here, :] = turned_keys(marks[0, :, here], ref)
        values[:, here] = ref[0:PADDED]
        store_queries(marks[1, :, here], ref, queries, there)
    if halo:
        for ref, here in ((left_ref, slice(0, halo)), (right_ref, slice(length - halo, length))):
            keys[here, :] = turned_keys(marks[0, :, here], ref)
            values[:, here] = ref[0:PADDED]
    attend_images(images, ids_ref, keys, values, queries, attended, work, starts, halo)

    odd_head = lax.rem(own, 2) == 1
    mine = ids[:, halo : halo + total_rows]

    def placed(block, spare):
        even = jnp.concatenate([block[0:size], spare], axis=0)
        odd = jnp.concatenate([spare, block[0:size]], axis=0)
        return jnp.where(odd_head, odd, even)

    if piggy:
        nothing = jnp.zeros((SPARE, total_rows), jnp.float32)
        flat = placed(attended[...], nothing).astype(jnp.bfloat16)
        pooled = lax.dot_general(
            image_rows(mine, images), flat, (((1,), (1,)), ((), ())), preferred_element_type=jnp.float32
        )
        pooled = split_in_two(pooled, images)
        sums = spare_sums(got_refs)
        sums = split_in_two(sums + pltpu.roll(sums, images, axis=0), images)
        spare = jnp.concatenate(
            [pooled, jnp.zeros((SPARE, LANES - padded), jnp.float32), sums], axis=1
        )
        texts = text_ref[...].astype(jnp.float32)
        parts = [texts[:, at : at + count] for at in range(0, texts.shape[1], count)]
        unused = TEXT_ROWS - images * len(parts)
        below = jnp.concatenate(parts + [jnp.zeros((unused, count), jnp.float32)] * (unused > 0), axis=0)
        below = below.astype(jnp.bfloat16)
    else:
        spare = jnp.zeros((SPARE, count), jnp.float32)
    for by, out_ref in zip(ORDER, out_refs):
        there = pl.multiple_of(jnp.bitwise_xor(own, by) * count, LANES)
        out_ref[0:padded] = placed(attended[:, pl.ds(there, count)], spare).astype(jnp.bfloat16)
        if piggy:
            out_ref[padded:] = below


def joined_heads(got_refs, flat):
    own = lax.rem(lax.axis_index("grp"), HEADS)
    spares = []
    for step, (by, got_ref) in enumerate(zip(ORDER, got_refs)):
        odd = lax.rem(jnp.bitwise_xor(own, by), 2)
        at = step * PADDED
        top = got_ref[0:16].astype(jnp.float32)
        bottom = got_ref[PADDED - 16 : PADDED].astype(jnp.float32)
        spares.append(jnp.where(odd == 1, top[:SPARE], bottom[SPARE:]))
        top = jnp.concatenate([jnp.where(odd == 1, 0.0, top[:SPARE]), top[SPARE:]], axis=0)
        bottom = jnp.concatenate([bottom[:SPARE], jnp.where(odd == 1, bottom[SPARE:], 0.0)], axis=0)
        flat[at : at + 16] = top.astype(jnp.bfloat16)
        flat[at + 16 : at + PADDED - 16] = got_ref[16 : PADDED - 16]
        flat[at + PADDED - 16 : at + PADDED] = bottom.astype(jnp.bfloat16)
    return spares


def send_mixed_rows(rows_ref, weight_ref, flat, turned, mixed, mixed_ref, sems):
    turned[...] = flat[...].T
    pieces = sems.shape[0]
    step = rows_ref.shape[0] // pieces
    copies = []
    for piece in range(pieces):
        cut = slice(piece * step, (piece + 1) * step)
        added = jnp.dot(turned[cut, :], weight_ref[...], preferred_element_type=jnp.float32)
        mixed[cut, :] = (rows_ref[cut, :].astype(jnp.float32) + added).astype(jnp.bfloat16)
        copies.append(pltpu.make_async_copy(mixed.at[cut], mixed_ref.at[cut], sems.at[piece]))
        copies[-1].start()
    return copies


def unit_rows(matrix):
    return matrix * lax.rsqrt(jnp.sum(matrix * matrix, axis=1, keepdims=True) + 1e-06)


def losses(cosine, labels):
    logits = -labels * (logit_scale * cosine + logit_bias)
    return jnp.maximum(logits, 0.0) + jnp.log1p(jnp.exp(-jnp.abs(logits)))


def finish_kernel(images, rows_ref, weight_ref, text_ref, *rest):
    got_refs, rest = rest[:HEADS], rest[HEADS:]
    mixed_ref, loss_ref, flat, turned, mixed, sems, pooled_heads, patch_sums, far_texts = rest
    spares = joined_heads(got_refs, flat)
    copies = send_mixed_rows(rows_ref, weight_ref, flat, turned, mixed, mixed_ref, sems)
    own = lax.rem(lax.axis_index("grp"), HEADS)
    patch_sums[:, HEADS * LANES :] = spares[0][:, 2 * LANES :]
    for step, (by, spare) in enumerate(zip(ORDER, spares)):
        pooled_heads[:, step * PADDED : (step + 1) * PADDED] = spare[:, 0:PADDED]
        head = jnp.bitwise_xor(own, by)
        patch_sums[:, pl.ds(pl.multiple_of(head * LANES, LANES), LANES)] = spare[:, LANES : 2 * LANES]
        below = got_refs[step][PADDED:].astype(jnp.float32)
        count = below.shape[1]
        for part in range(patch_sums.shape[1] // count):
            here = slice(part * count, (part + 1) * count)
            far_texts[head, :, here] = below[part * images : (part + 1) * images]
    pooled = jnp.dot(
        pooled_heads[...].astype(jnp.bfloat16), weight_ref[...], preferred_element_type=jnp.float32
    )
    pooled = pooled + patch_sums[...]
    pooled = pooled + pltpu.roll(pooled, images, axis=0)
    image_vecs = unit_rows(pooled)
    others = [far_texts[place] for place in range(lax.axis_size("blk") - 1)]
    texts = jnp.concatenate([text_ref[...].astype(jnp.float32)] + others, axis=0)
    text_vecs = unit_rows(texts)
    cosine = lax.dot_general(
        text_vecs,
        image_vecs,
        (((1,), (1,)), ((), ())),
        precision=lax.Precision.HIGHEST,
        preferred_element_type=jnp.float32,
    )
    text = lax.broadcasted_iota(jnp.int32, cosine.shape, 0)
    image = lax.broadcasted_iota(jnp.int32, cosine.shape, 1)
    terms = losses(cosine, jnp.where(text == image, 1.0, -1.0))
    loss_ref[...] = jnp.sum(terms, axis=0, keepdims=True)[:, 0:images]
    for copy in copies:
        copy.wait()


def mix_kernel(rows_ref, weight_ref, *rest):
    got_refs, rest = rest[:HEADS], rest[HEADS:]
    mixed_ref, flat, turned, mixed, sems = rest
    joined_heads(got_refs, flat)
    for copy in send_mixed_rows(rows_ref, weight_ref, flat, turned, mixed, mixed_ref, sems):
        copy.wait()


def in_vmem(count):
    return [pl.BlockSpec(memory_space=pltpu.VMEM)] * count


def in_hbm(value):
    return pltpu.with_memory_space_constraint(value, pltpu.HBM)


def call(kernel, out_shape, scratch, in_specs, flops, out_specs=None):
    if out_specs is None:
        out_specs = jax.tree.map(lambda _: pl.BlockSpec(memory_space=pltpu.VMEM), out_shape)
    return pl.pallas_call(
        kernel,
        out_shape=out_shape,
        in_specs=in_specs,
        out_specs=out_specs,
        scratch_shapes=scratch,
        compiler_params=pltpu.CompilerParams(vmem_limit_bytes=VMEM_LIMIT),
        cost_estimate=pl.CostEstimate(flops=flops, bytes_accessed=8 << 20, transcendentals=0),
    )


def moved(value, axis, pairs):
    return lax.ppermute(value, axis, pairs)


def partner(place, by, peers):
    return place ^ by if peers & (peers - 1) == 0 else (place + by) % peers


def all_texts(texts):
    peers = lax.axis_size("blk")
    steps = [[(partner(i, by, peers), i) for i in range(peers)] for by in range(1, peers)]
    return jnp.concatenate([texts] + [moved(texts, "blk", pairs) for pairs in steps], axis=0)


def one_text_block(texts):
    peers = lax.axis_size("blk")
    pairs = []
    for place in range(lax.axis_size("grp")):
        by = place % (peers - 1) + 1
        pairs += [(place * peers + partner(i, by, peers), place * peers + i) for i in range(peers)]
    return moved(texts, ("grp", "blk"), pairs)


def traded(blocks):
    peers = range(lax.axis_size("grp"))
    trades = {by: moved(blocks[by], "grp", [(i, i ^ by) for i in peers]) for by in ORDER if by}
    return {**trades, 0: blocks[0]}


def local(patches, segment_ids, qkv_weight, out_weight, text_embed):
    rows = patches[0]
    count, depth = rows.shape
    width = out_weight.shape[0]
    size = width // HEADS
    padded = size + SPARE
    images = text_embed.shape[0]
    group_size = lax.axis_size("grp")
    parts = group_size // HEADS
    piggy = (
        parts == 1
        and 2 * images == SPARE
        and count >= depth - (HEADS - 2) * LANES
        and depth % count == 0
        and images * (depth // count) <= TEXT_ROWS
        and 1 < lax.axis_size("blk") <= HEADS + 1
    )
    bf16, f32 = jnp.bfloat16, jnp.float32
    shape = jax.ShapeDtypeStruct

    block = shape((3 * size + SPARE, count), bf16)
    hbm = pl.BlockSpec(memory_space=pltpu.HBM)
    turned_weight = qkv_weight.T
    normed, sums, *sent = call(
        functools.partial(far_kernel, images, piggy),
        (shape((depth, count), bf16), shape((SPARE, depth), f32), block, block),
        [
            pltpu.VMEM((1, count), jnp.int32),
            pltpu.VMEM((count, depth), bf16),
            pltpu.VMEM((6 * size, depth), bf16),
            pltpu.SemaphoreType.DMA,
            pltpu.SemaphoreType.DMA((3,)),
            pltpu.SemaphoreType.DMA((3,)),
        ],
        [hbm] * 3,
        2 * count * depth * 6 * size,
    )(in_hbm(segment_ids), in_hbm(rows), in_hbm(turned_weight))
    sent += call(
        functools.partial(near_kernel, piggy),
        (block,) * 6,
        [],
        in_vmem(3),
        2 * count * depth * 18 * size,
    )(normed, sums, turned_weight)
    sent = dict(zip((6, 7, 2, 3, 4, 5, 0, 1), sent))
    if piggy:
        late_texts, sent[0] = lax.optimization_barrier((text_embed, sent[0]))
        halos_and_texts = [one_text_block(late_texts)]
    else:
        halos_and_texts = []
    got = traded(sent)

    length = HEADS * count
    halo = 0
    near_ids = segment_ids
    if parts > 1:
        halo = rounded_up(MAXP - 1, LANES)
        part = lax.axis_index("grp") // HEADS
        whole_ids = jnp.concatenate(
            [
                jnp.full((1, halo), -1, jnp.int32),
                segment_ids,
                jnp.full((1, halo), images, jnp.int32),
            ],
            axis=1,
        )
        near_ids = lax.dynamic_slice_in_dim(whole_ids, part * length, length + 2 * halo, axis=1)
        order = jnp.bitwise_xor(lax.axis_index("grp") % HEADS, jnp.arange(HEADS))
        flat = jnp.stack([got[by] for by in range(HEADS)])[order][:, : 2 * size].transpose(1, 0, 2).reshape(2 * size, length)
        flat = jnp.concatenate([flat, jnp.zeros((16, length), bf16)], axis=0)
        ahead = [(i, i + HEADS) for i in range(group_size - HEADS)]
        back = [(i + HEADS, i) for i in range(group_size - HEADS)]
        left = moved(flat[:, length - halo :], "grp", ahead)
        right = moved(flat[:, :halo], "grp", back)
        halos_and_texts += [left, right]
    reach = length + 2 * halo
    window = min(rounded_up(MAXP + LANES - 1, LANES), reach)
    tile = 2 * LANES
    early_keys, marks, before, weight = call(
        functools.partial(prepare_kernel, images, halo),
        (
            shape((len(EARLY) * count, LANES), bf16),
            shape((2, SPARE, reach), f32),
            shape((rounded_up(images + 1, SPARE), LANES), jnp.int32),
            shape((HEADS * padded, depth), bf16),
        ),
        [pltpu.SemaphoreType.DMA((HEADS,))],
        in_vmem(1) + [hbm] + in_vmem(len(EARLY)),
        1 << 30,
    )(near_ids, in_hbm(out_weight), *[got[by] for by in EARLY])
    operands = [near_ids, before, marks, early_keys, *[got[by] for by in EARLY + LATE], *halos_and_texts]
    answers = call(
        functools.partial(attend_kernel, images, piggy, halo),
        (shape((padded + TEXT_ROWS * piggy, count), bf16),) * HEADS,
        [
            pltpu.VMEM((reach, LANES), bf16),
            pltpu.VMEM((padded, reach), bf16),
            pltpu.VMEM((LANES, length), bf16),
            pltpu.VMEM((padded, length), f32),
            pltpu.VMEM((window, tile), f32),
            pltpu.VMEM((window, tile), f32),
            pltpu.VMEM((1, tile), f32),
            pltpu.VMEM((1, tile), f32),
            pltpu.SMEM((images + 1,), jnp.int32),
        ],
        in_vmem(len(operands)),
        4 * size * length * MAXP,
    )(*operands)
    home = traded(dict(zip(ORDER, answers)))
    home = [home[by] for by in ORDER]

    joined = [
        pltpu.VMEM((HEADS * padded, count), bf16),
        pltpu.VMEM((count, HEADS * padded), bf16),
        pltpu.VMEM((count, depth), bf16),
        pltpu.SemaphoreType.DMA((3,)),
    ]
    flops = 2 * count * depth * width
    if piggy:
        mixed, row_loss = call(
            functools.partial(finish_kernel, images),
            (shape((count, depth), bf16), shape((1, images), f32)),
            joined
            + [
                pltpu.VMEM((SPARE, HEADS * padded), f32),
                pltpu.VMEM((SPARE, depth), f32),
                pltpu.VMEM((HEADS, images, depth), f32),
            ],
            in_vmem(3 + HEADS),
            flops,
            (hbm, pl.BlockSpec(memory_space=pltpu.VMEM)),
        )(rows, weight, text_embed, *home)
        return (mixed[None], row_loss[0])
    mixed = call(mix_kernel, shape((count, depth), bf16), joined, in_vmem(2 + HEADS), flops, hbm)(
        rows, weight, *home
    )
    own_ids = lax.dynamic_slice_in_dim(segment_ids[0], lax.axis_index("grp") * count, count)
    onehot = (own_ids[None, :] == jnp.arange(images, dtype=jnp.int32)[:, None]).astype(bf16)
    pooled = lax.psum(jnp.dot(onehot, mixed, preferred_element_type=f32), "grp")
    text_vecs = unit_rows(all_texts(text_embed).astype(f32))
    cosine = jnp.dot(unit_rows(pooled), text_vecs.T, precision=lax.Precision.HIGHEST)
    same = jnp.arange(images)[:, None] == jnp.arange(text_vecs.shape[0])[None, :]
    row_loss = jnp.sum(losses(cosine, jnp.where(same, 1.0, -1.0)), axis=1)
    return (mixed[None], row_loss)


def solution(mesh):
    placed = (P("blk", "grp", None), P("blk", None), P(), P(), P("blk", None))
    return jax.shard_map(
        local,
        mesh=mesh,
        in_specs=placed,
        out_specs=(P("blk", "grp", None), P("blk")),
        check_vma=False,
    )
```

```python
import functools
import math

import jax
import jax.numpy as jnp
from jax import lax
from jax.experimental import pallas as pl
from jax.experimental.pallas import tpu as pltpu
from jax.sharding import PartitionSpec as P

HEADS = 8
MAXP = 1024
LANES = 128
SPARE = 8
SIZE = 72
PADDED = SIZE + SPARE
KEY_AT = SIZE - SPARE
QUERY_AT = 2 * SIZE
TEXT_ROWS = 16
HIDDEN = -1e30
ORDER = (6, 7, 2, 4, 3, 5, 1, 0)
EARLY = (6, 7, 1, 0)
LATE = (2, 4, 3, 5)

logit_scale = 30.0
logit_bias = -5.0

VMEM_LIMIT = 32 * 1024 * 1024


def rounded_up(value, step):
    return (value + step - 1) // step * step


def split_in_two(total, images):
    row = lax.broadcasted_iota(jnp.int32, total.shape, 0)
    main = total.astype(jnp.bfloat16).astype(jnp.float32)
    return jnp.where(row < images, main, total - main)


def image_rows(ids, images):
    row = lax.broadcasted_iota(jnp.int32, (SPARE, ids.shape[1]), 0)
    return (lax.rem(row, images) == ids).astype(jnp.float32).astype(jnp.bfloat16)


def head_blocks(query, key, value, sums, pair):
    size = query.shape[0] // 2
    count = query.shape[1]
    for place in range(2):
        here = slice(place * size, (place + 1) * size)
        if sums is None:
            spare = jnp.zeros((SPARE, count), jnp.float32)
        else:
            first = pl.multiple_of((2 * pair + place) * LANES, LANES)
            parts = [sums[:, pl.ds(first, LANES)], sums[:, HEADS * LANES :]]
            held = sum(part.shape[1] for part in parts)
            spare = jnp.concatenate(parts + [jnp.zeros((SPARE, count - held), jnp.float32)], axis=1)
        block = jnp.concatenate([value[here], key[here], spare, query[here]], axis=0)
        yield block.astype(jnp.bfloat16)


def store_by_core(core, blocks, same_ref, cross_ref):
    first, second = blocks

    @pl.when(core == 0)
    def _():
        same_ref[...] = first
        cross_ref[...] = second

    @pl.when(core == 1)
    def _():
        same_ref[...] = second
        cross_ref[...] = first


def place_in_group():
    own = lax.rem(lax.axis_index("grp"), HEADS)
    return lax.div(own, 2), lax.rem(own, 2)


def far_kernel(images, piggy, ids_ref, rows_ref, weight_ref, normed_ref, sums_ref, same_ref, cross_ref, own_ids, rows_held, weight, id_sem, row_sem, sems):
    count, depth = rows_ref.shape
    width = weight_ref.shape[0] // 3
    wide = weight.shape[1]
    rows_fetch = pltpu.make_async_copy(rows_ref, rows_held, row_sem)
    rows_fetch.start()
    own = pl.multiple_of(lax.axis_index("grp") * count, LANES)
    ids_fetch = pltpu.make_async_copy(ids_ref.at[:, pl.ds(own, count)], own_ids, id_sem)
    ids_fetch.start()
    pair, core = place_in_group()
    pair = jnp.bitwise_xor(pair, 3)
    fetches = []
    for at in range(3):
        first = pl.multiple_of(at * width + pair * wide, 16)
        fetches.append(pltpu.make_async_copy(weight_ref.at[pl.ds(first, wide)], weight.at[at], sems.at[at]))
    for fetch in fetches:
        fetch.start()
    ids_fetch.wait()
    rows_fetch.wait()
    rows = rows_held[...]
    if piggy:
        sums = jnp.dot(image_rows(own_ids[...], images), rows, preferred_element_type=jnp.float32)
        sums_ref[...] = split_in_two(sums, images)
    values = rows.astype(jnp.float32)
    center = values - jnp.mean(values, axis=1, keepdims=True)
    spread = jnp.mean(center * center, axis=1, keepdims=True)
    normed = (center * lax.rsqrt(spread + 1e-06)).astype(jnp.bfloat16)
    normed_ref[...] = normed.T
    for fetch in fetches:
        fetch.wait()
    parts = [
        jnp.dot(weight[at], normed_ref[...], preferred_element_type=jnp.float32) for at in range(3)
    ]
    store_by_core(core, head_blocks(*parts, sums_ref if piggy else None, pair), same_ref, cross_ref)


def near_kernel(piggy, normed_ref, sums_ref, weight_ref, *out_refs):
    width = weight_ref.shape[0] // 3
    wide = 2 * width // HEADS
    own, core = place_in_group()
    for step, move in enumerate((1, 2, 0)):
        pair = jnp.bitwise_xor(own, move)
        parts = []
        for at in range(3):
            here = pl.ds(pl.multiple_of(at * width + pair * wide, 16), wide)
            parts.append(
                jnp.dot(weight_ref[here, :], normed_ref[...], preferred_element_type=jnp.float32)
            )
        blocks = head_blocks(*parts, sums_ref if piggy else None, pair)
        store_by_core(core, blocks, *out_refs[2 * step : 2 * step + 2])


def count_before(images, ids):
    image = lax.broadcasted_iota(jnp.int32, (rounded_up(images + 1, SPARE), ids.shape[1]), 0)
    before = jnp.sum((ids < image).astype(jnp.int32), axis=1, keepdims=True)
    return jnp.broadcast_to(before, (before.shape[0], LANES))


def write_marks(images, ids, marks):
    bits = max(1, (images - 1).bit_length())
    row = lax.broadcasted_iota(jnp.int32, (SPARE, ids.shape[1]), 0)
    bit = jnp.bitwise_and(lax.shift_right_logical(jnp.broadcast_to(ids, row.shape), row >> 1), 1)
    odd = jnp.bitwise_and(row, 1)
    used = row < 2 * bits
    outside = jnp.logical_or(ids < 0, ids >= images)
    key_side = jnp.where(odd == 1, bit, 1 - bit).astype(jnp.float32)
    key_side = jnp.where(outside, 1.0, key_side)
    marks[0] = jnp.where(used, key_side * HIDDEN, 0.0)
    marks[1] = jnp.where(used, jnp.where(odd == 1, 1 - bit, bit), 0).astype(jnp.float32)


def spare_sums(refs):
    parts = [ref[QUERY_AT : QUERY_AT + 16].astype(jnp.float32)[0:SPARE, 0 : 2 * LANES] for ref in refs]
    return sum(parts[1:], parts[0])


def image_at(images, starts, position):
    found = jnp.int32(0)
    for image in range(1, images):
        found += (starts[image] <= position).astype(jnp.int32)
    return found


def attend_images(images, ids_ref, keys, values, queries, attended, work, starts, halo):
    scores_a, scores_b, tops_a, tops_b = work
    query_base = halo
    window, tile = scores_a.shape
    size = attended.shape[0] - SPARE
    held = queries.shape[1]
    tiles = held // tile

    def bounds(image):
        first = lax.div(jnp.maximum(starts[image] - query_base, 0), tile)
        last = lax.div(jnp.minimum(starts[image + 1] - query_base, held) - 1, tile)
        return jnp.minimum(first, tiles - 1), last

    def after(image):
        return jnp.minimum(image + 1, images - 1)

    def following(state):
        at, image = state
        more = at < bounds(image)[1]
        later = after(image)
        return jnp.where(more, at + 1, bounds(later)[0]), jnp.where(more, image, later)

    def window_of(image):
        begin = lax.div(starts[image], LANES) * LANES
        return pl.ds(pl.multiple_of(jnp.minimum(begin, keys.shape[0] - window), LANES), window)

    def score(state, scores, tops):
        at, image = state
        query = queries[:, pl.ds(pl.multiple_of(at * tile, tile), tile)]
        found = jnp.dot(keys[window_of(image), :], query, preferred_element_type=jnp.float32)
        scores[...] = found
        tops[...] = jnp.max(found, axis=0, keepdims=True)

    def weigh(state, scores, tops):
        at, image = state
        first = pl.multiple_of(at * tile, tile)
        labels = ids_ref[:, pl.ds(pl.multiple_of(query_base + first, LANES), tile)]
        probs = jnp.exp2((scores[...] - tops[...]) * (size ** (-0.5) * math.log2(math.e)))
        share = 1.0 / jnp.sum(probs, axis=0, keepdims=True)
        weighted = jnp.dot(
            values[:, window_of(image)], probs.astype(jnp.bfloat16), preferred_element_type=jnp.float32
        )
        place = (slice(None), pl.ds(first, tile))
        attended[place] = jnp.where(labels == image, weighted * share, attended[place])

    low = image_at(images, starts, query_base)
    high = image_at(images, starts, query_base + held - 1)
    pairs = jnp.int32(0)
    for image in range(images):
        first, last = bounds(image)
        wanted = jnp.logical_and(low <= image, image <= high)
        pairs += jnp.where(wanted, last - first + 1, 0)

    def two_pairs(_, state):
        second = following(state)
        score(second, scores_b, tops_b)
        weigh(state, scores_a, tops_a)
        third = following(second)
        score(third, scores_a, tops_a)
        weigh(second, scores_b, tops_b)
        return third

    def four_pairs(step, state):
        return two_pairs(step, two_pairs(step, state))

    begun = (jnp.int32(0), low)
    score(begun, scores_a, tops_a)
    reached = lax.fori_loop(0, lax.div(pairs, 4), four_pairs, begun)
    reached = lax.fori_loop(0, lax.div(lax.rem(pairs, 4), 2), two_pairs, reached)

    @pl.when(lax.rem(pairs, 2) == 1)
    def _():
        weigh(reached, scores_a, tops_a)


def turned_keys(marked, block_ref):
    block = block_ref[KEY_AT : KEY_AT + PADDED].astype(jnp.float32)
    nothing = jnp.zeros((LANES - PADDED, block.shape[1]), jnp.float32)
    full = jnp.concatenate([marked, block[SPARE:], nothing], axis=0)
    return full.astype(jnp.bfloat16).T


def store_queries(marked, block_ref, queries, there):
    edge = block_ref[QUERY_AT : QUERY_AT + 16].astype(jnp.float32)
    edge = jnp.concatenate([marked, edge[SPARE:]], axis=0)
    queries[0:16, there] = edge.astype(jnp.bfloat16)
    queries[16:PADDED, there] = block_ref[QUERY_AT + 16 : QUERY_AT + PADDED]
    queries[PADDED:, there] = jnp.zeros((LANES - PADDED, block_ref.shape[1]), jnp.bfloat16)


def prepare_kernel(images, halo, ids_ref, out_weight_ref, *rest):
    got_refs, (keys, marks, before, weight, sems) = rest[: len(EARLY)], rest[len(EARLY) :]
    count = got_refs[0].shape[1]
    fetches = []
    for step, by in enumerate(ORDER):
        head = jnp.bitwise_xor(lax.rem(lax.axis_index("grp"), HEADS), by)
        first = lax.div(head, 2) * (2 * SIZE) + lax.rem(head, 2) * (SIZE - SPARE)
        fetches.append(
            pltpu.make_async_copy(
                out_weight_ref.at[pl.ds(pl.multiple_of(first, 16), PADDED)],
                weight.at[step * PADDED : (step + 1) * PADDED],
                sems.at[step],
            )
        )
        fetches[-1].start()
    before[...] = count_before(images, ids_ref[...])
    write_marks(images, ids_ref[...], marks)
    own = lax.rem(lax.axis_index("grp"), HEADS)
    for step, (by, ref) in enumerate(zip(EARLY, got_refs)):
        first = jnp.bitwise_xor(own, by) * count
        here = pl.ds(pl.multiple_of(halo + first, LANES), count)
        keys[step * count : (step + 1) * count, :] = turned_keys(marks[0, :, here], ref)
    for fetch in fetches:
        fetch.wait()


def attend_kernel(images, piggy, halo, ids_ref, before_ref, marks, early_keys, *rest):
    got_refs, rest = rest[:HEADS], rest[HEADS:]
    if piggy:
        text_ref, *rest = rest
    if halo:
        left_ref, right_ref, *rest = rest
    out_refs, rest = rest[:HEADS], rest[HEADS:]
    keys, values, queries, attended, *work, starts = rest
    count = got_refs[0].shape[1]
    padded = attended.shape[0]
    size = padded - SPARE
    total_rows = HEADS * count
    length = ids_ref.shape[1]
    ids = ids_ref[...]
    before = before_ref[...]
    for image in range(images + 1):
        starts[image] = before[image, 0]

    own = lax.rem(lax.axis_index("grp"), HEADS)
    for step, (by, ref) in enumerate(zip(EARLY + LATE, got_refs)):
        first = jnp.bitwise_xor(own, by) * count
        here = pl.ds(pl.multiple_of(halo + first, LANES), count)
        there = pl.ds(pl.multiple_of(first, LANES), count)
        if by in EARLY:
            keys[here, :] = early_keys[step * count : (step + 1) * count, :]
        else:
            keys[here, :] = turned_keys(marks[0, :, here], ref)
        values[:, here] = ref[0:PADDED]
        store_queries(marks[1, :, here], ref, queries, there)
    if halo:
        for ref, here in ((left_ref, slice(0, halo)), (right_ref, slice(length - halo, length))):
            keys[here, :] = turned_keys(marks[0, :, here], ref)
            values[:, here] = ref[0:PADDED]
    attend_images(images, ids_ref, keys, values, queries, attended, work, starts, halo)

    odd_head = lax.rem(own, 2) == 1
    mine = ids[:, halo : halo + total_rows]

    def placed(block, spare):
        even = jnp.concatenate([block[0:size], spare], axis=0)
        odd = jnp.concatenate([spare, block[0:size]], axis=0)
        return jnp.where(odd_head, odd, even)

    if piggy:
        nothing = jnp.zeros((SPARE, total_rows), jnp.float32)
        flat = placed(attended[...], nothing).astype(jnp.bfloat16)
        pooled = lax.dot_general(
            image_rows(mine, images), flat, (((1,), (1,)), ((), ())), preferred_element_type=jnp.float32
        )
        pooled = split_in_two(pooled, images)
        sums = spare_sums(got_refs)
        sums = split_in_two(sums + pltpu.roll(sums, images, axis=0), images)
        spare = jnp.concatenate(
            [pooled, jnp.zeros((SPARE, LANES - padded), jnp.float32), sums], axis=1
        )
        texts = text_ref[...].astype(jnp.float32)
        parts = [texts[:, at : at + count] for at in range(0, texts.shape[1], count)]
        unused = TEXT_ROWS - images * len(parts)
        below = jnp.concatenate(parts + [jnp.zeros((unused, count), jnp.float32)] * (unused > 0), axis=0)
        below = below.astype(jnp.bfloat16)
    else:
        spare = jnp.zeros((SPARE, count), jnp.float32)
    for by, out_ref in zip(ORDER, out_refs):
        there = pl.multiple_of(jnp.bitwise_xor(own, by) * count, LANES)
        out_ref[0:padded] = placed(attended[:, pl.ds(there, count)], spare).astype(jnp.bfloat16)
        if piggy:
            out_ref[padded:] = below


def joined_heads(got_refs, flat):
    own = lax.rem(lax.axis_index("grp"), HEADS)
    spares = []
    for step, (by, got_ref) in enumerate(zip(ORDER, got_refs)):
        odd = lax.rem(jnp.bitwise_xor(own, by), 2)
        at = step * PADDED
        top = got_ref[0:16].astype(jnp.float32)
        bottom = got_ref[PADDED - 16 : PADDED].astype(jnp.float32)
        spares.append(jnp.where(odd == 1, top[:SPARE], bottom[SPARE:]))
        top = jnp.concatenate([jnp.where(odd == 1, 0.0, top[:SPARE]), top[SPARE:]], axis=0)
        bottom = jnp.concatenate([bottom[:SPARE], jnp.where(odd == 1, bottom[SPARE:], 0.0)], axis=0)
        flat[at : at + 16] = top.astype(jnp.bfloat16)
        flat[at + 16 : at + PADDED - 16] = got_ref[16 : PADDED - 16]
        flat[at + PADDED - 16 : at + PADDED] = bottom.astype(jnp.bfloat16)
    return spares


def send_mixed_rows(rows_ref, weight_ref, flat, turned, mixed, mixed_ref, sems, meanwhile=None):
    turned[...] = flat[...].T
    pieces = sems.shape[0]
    step = rows_ref.shape[0] // pieces
    copies, value = [], None
    for piece in range(pieces):
        cut = slice(piece * step, (piece + 1) * step)
        if meanwhile is not None:
            value = meanwhile[piece](value)
        added = jnp.dot(turned[cut, :], weight_ref[...], preferred_element_type=jnp.float32)
        mixed[cut, :] = (rows_ref[cut, :].astype(jnp.float32) + added).astype(jnp.bfloat16)
        copies.append(pltpu.make_async_copy(mixed.at[cut], mixed_ref.at[cut], sems.at[piece]))
        copies[-1].start()
    return copies


def unit_rows(matrix):
    return matrix * lax.rsqrt(jnp.sum(matrix * matrix, axis=1, keepdims=True) + 1e-06)


def losses(cosine, labels):
    logits = -labels * (logit_scale * cosine + logit_bias)
    return jnp.maximum(logits, 0.0) + jnp.log1p(jnp.exp(-jnp.abs(logits)))


def finish_kernel(images, rows_ref, weight_ref, text_ref, *rest):
    got_refs, rest = rest[:HEADS], rest[HEADS:]
    mixed_ref, loss_ref, flat, turned, mixed, sems, pooled_heads, patch_sums, far_texts, loss, loss_sem = rest
    spares = joined_heads(got_refs, flat)
    own = lax.rem(lax.axis_index("grp"), HEADS)
    patch_sums[:, HEADS * LANES :] = spares[0][:, 2 * LANES :]
    for step, (by, spare) in enumerate(zip(ORDER, spares)):
        pooled_heads[:, step * PADDED : (step + 1) * PADDED] = spare[:, 0:PADDED]
        head = jnp.bitwise_xor(own, by)
        patch_sums[:, pl.ds(pl.multiple_of(head * LANES, LANES), LANES)] = spare[:, LANES : 2 * LANES]
        below = got_refs[step][PADDED:].astype(jnp.float32)
        count = below.shape[1]
        for part in range(patch_sums.shape[1] // count):
            here = slice(part * count, (part + 1) * count)
            far_texts[head, :, here] = below[part * images : (part + 1) * images]

    def find_images(_):
        pooled = jnp.dot(
            pooled_heads[...].astype(jnp.bfloat16), weight_ref[...], preferred_element_type=jnp.float32
        )
        pooled = pooled + patch_sums[...]
        others = [far_texts[place] for place in range(lax.axis_size("blk") - 1)]
        texts = jnp.concatenate([text_ref[...].astype(jnp.float32)] + others, axis=0)
        return pooled + pltpu.roll(pooled, images, axis=0), unit_rows(texts)

    def find_cosines(vectors):
        pooled, text_vecs = vectors
        return lax.dot_general(
            text_vecs,
            unit_rows(pooled),
            (((1,), (1,)), ((), ())),
            precision=lax.Precision.HIGHEST,
            preferred_element_type=jnp.float32,
        )

    def find_losses(cosine):
        text = lax.broadcasted_iota(jnp.int32, cosine.shape, 0)
        image = lax.broadcasted_iota(jnp.int32, cosine.shape, 1)
        terms = losses(cosine, jnp.where(text == image, 1.0, -1.0))
        loss[...] = jnp.sum(terms, axis=0, keepdims=True)[:, 0:images]
        loss_copy.start()

    loss_copy = pltpu.make_async_copy(loss, loss_ref, loss_sem)
    meanwhile = (find_images, find_cosines, find_losses)
    copies = send_mixed_rows(rows_ref, weight_ref, flat, turned, mixed, mixed_ref, sems, meanwhile)
    for copy in copies + [loss_copy]:
        copy.wait()


def mix_kernel(rows_ref, weight_ref, *rest):
    got_refs, rest = rest[:HEADS], rest[HEADS:]
    mixed_ref, flat, turned, mixed, sems = rest
    joined_heads(got_refs, flat)
    for copy in send_mixed_rows(rows_ref, weight_ref, flat, turned, mixed, mixed_ref, sems):
        copy.wait()


def in_vmem(count):
    return [pl.BlockSpec(memory_space=pltpu.VMEM)] * count


def in_hbm(value):
    return pltpu.with_memory_space_constraint(value, pltpu.HBM)


def call(kernel, out_shape, scratch, in_specs, flops, out_specs=None):
    if out_specs is None:
        out_specs = jax.tree.map(lambda _: pl.BlockSpec(memory_space=pltpu.VMEM), out_shape)
    return pl.pallas_call(
        kernel,
        out_shape=out_shape,
        in_specs=in_specs,
        out_specs=out_specs,
        scratch_shapes=scratch,
        compiler_params=pltpu.CompilerParams(vmem_limit_bytes=VMEM_LIMIT),
        cost_estimate=pl.CostEstimate(flops=flops, bytes_accessed=8 << 20, transcendentals=0),
    )


def moved(value, axis, pairs):
    return lax.ppermute(value, axis, pairs)


def partner(place, by, peers):
    return place ^ by if peers & (peers - 1) == 0 else (place + by) % peers


def all_texts(texts):
    peers = lax.axis_size("blk")
    steps = [[(partner(i, by, peers), i) for i in range(peers)] for by in range(1, peers)]
    return jnp.concatenate([texts] + [moved(texts, "blk", pairs) for pairs in steps], axis=0)


def one_text_block(texts):
    peers = lax.axis_size("blk")
    pairs = []
    for place in range(lax.axis_size("grp")):
        by = place % (peers - 1) + 1
        pairs += [(place * peers + partner(i, by, peers), place * peers + i) for i in range(peers)]
    return moved(texts, ("grp", "blk"), pairs)


def traded(blocks):
    peers = range(lax.axis_size("grp"))
    trades = {by: moved(blocks[by], "grp", [(i, i ^ by) for i in peers]) for by in ORDER if by}
    return {**trades, 0: blocks[0]}


def local(patches, segment_ids, qkv_weight, out_weight, text_embed):
    rows = patches[0]
    count, depth = rows.shape
    width = out_weight.shape[0]
    size = width // HEADS
    padded = size + SPARE
    images = text_embed.shape[0]
    group_size = lax.axis_size("grp")
    parts = group_size // HEADS
    piggy = (
        parts == 1
        and 2 * images == SPARE
        and count >= depth - (HEADS - 2) * LANES
        and depth % count == 0
        and images * (depth // count) <= TEXT_ROWS
        and 1 < lax.axis_size("blk") <= HEADS + 1
    )
    bf16, f32 = jnp.bfloat16, jnp.float32
    shape = jax.ShapeDtypeStruct

    block = shape((3 * size + SPARE, count), bf16)
    hbm = pl.BlockSpec(memory_space=pltpu.HBM)
    turned_weight = qkv_weight.T
    normed, sums, *sent = call(
        functools.partial(far_kernel, images, piggy),
        (shape((depth, count), bf16), shape((SPARE, depth), f32), block, block),
        [
            pltpu.VMEM((1, count), jnp.int32),
            pltpu.VMEM((count, depth), bf16),
            pltpu.VMEM((3, 2 * size, depth), bf16),
            pltpu.SemaphoreType.DMA,
            pltpu.SemaphoreType.DMA,
            pltpu.SemaphoreType.DMA((3,)),
        ],
        [hbm] * 3,
        2 * count * depth * 6 * size,
    )(in_hbm(segment_ids), in_hbm(rows), in_hbm(turned_weight))
    sent += call(
        functools.partial(near_kernel, piggy),
        (block,) * 6,
        [],
        in_vmem(3),
        2 * count * depth * 18 * size,
    )(normed, sums, turned_weight)
    sent = dict(zip((6, 7, 2, 3, 4, 5, 0, 1), sent))
    if piggy:
        late_texts, sent[0] = lax.optimization_barrier((text_embed, sent[0]))
        halos_and_texts = [one_text_block(late_texts)]
    else:
        halos_and_texts = []
    got = traded(sent)

    length = HEADS * count
    halo = 0
    near_ids = segment_ids
    if parts > 1:
        halo = rounded_up(MAXP - 1, LANES)
        part = lax.axis_index("grp") // HEADS
        whole_ids = jnp.concatenate(
            [
                jnp.full((1, halo), -1, jnp.int32),
                segment_ids,
                jnp.full((1, halo), images, jnp.int32),
            ],
            axis=1,
        )
        near_ids = lax.dynamic_slice_in_dim(whole_ids, part * length, length + 2 * halo, axis=1)
        order = jnp.bitwise_xor(lax.axis_index("grp") % HEADS, jnp.arange(HEADS))
        flat = jnp.stack([got[by] for by in range(HEADS)])[order][:, : 2 * size].transpose(1, 0, 2).reshape(2 * size, length)
        flat = jnp.concatenate([flat, jnp.zeros((16, length), bf16)], axis=0)
        ahead = [(i, i + HEADS) for i in range(group_size - HEADS)]
        back = [(i + HEADS, i) for i in range(group_size - HEADS)]
        left = moved(flat[:, length - halo :], "grp", ahead)
        right = moved(flat[:, :halo], "grp", back)
        halos_and_texts += [left, right]
    reach = length + 2 * halo
    window = min(rounded_up(MAXP + LANES - 1, LANES), reach)
    tile = 2 * LANES
    early_keys, marks, before, weight = call(
        functools.partial(prepare_kernel, images, halo),
        (
            shape((len(EARLY) * count, LANES), bf16),
            shape((2, SPARE, reach), f32),
            shape((rounded_up(images + 1, SPARE), LANES), jnp.int32),
            shape((HEADS * padded, depth), bf16),
        ),
        [pltpu.SemaphoreType.DMA((HEADS,))],
        in_vmem(1) + [hbm] + in_vmem(len(EARLY)),
        1 << 30,
    )(near_ids, in_hbm(out_weight), *[got[by] for by in EARLY])
    operands = [near_ids, before, marks, early_keys, *[got[by] for by in EARLY + LATE], *halos_and_texts]
    answers = call(
        functools.partial(attend_kernel, images, piggy, halo),
        (shape((padded + TEXT_ROWS * piggy, count), bf16),) * HEADS,
        [
            pltpu.VMEM((reach, LANES), bf16),
            pltpu.VMEM((padded, reach), bf16),
            pltpu.VMEM((LANES, length), bf16),
            pltpu.VMEM((padded, length), f32),
            pltpu.VMEM((window, tile), f32),
            pltpu.VMEM((window, tile), f32),
            pltpu.VMEM((1, tile), f32),
            pltpu.VMEM((1, tile), f32),
            pltpu.SMEM((images + 1,), jnp.int32),
        ],
        in_vmem(len(operands)),
        4 * size * length * MAXP,
    )(*operands)
    home = traded(dict(zip(ORDER, answers)))
    home = [home[by] for by in ORDER]

    joined = [
        pltpu.VMEM((HEADS * padded, count), bf16),
        pltpu.VMEM((count, HEADS * padded), bf16),
        pltpu.VMEM((count, depth), bf16),
        pltpu.SemaphoreType.DMA((3,)),
    ]
    flops = 2 * count * depth * width
    if piggy:
        mixed, row_loss = call(
            functools.partial(finish_kernel, images),
            (shape((count, depth), bf16), shape((1, images), f32)),
            joined
            + [
                pltpu.VMEM((SPARE, HEADS * padded), f32),
                pltpu.VMEM((SPARE, depth), f32),
                pltpu.VMEM((HEADS, images, depth), f32),
                pltpu.VMEM((1, images), f32),
                pltpu.SemaphoreType.DMA,
            ],
            in_vmem(3 + HEADS),
            flops,
            (hbm, hbm),
        )(rows, weight, text_embed, *home)
        return (mixed[None], row_loss[0])
    mixed = call(mix_kernel, shape((count, depth), bf16), joined, in_vmem(2 + HEADS), flops, hbm)(
        rows, weight, *home
    )
    own_ids = lax.dynamic_slice_in_dim(segment_ids[0], lax.axis_index("grp") * count, count)
    onehot = (own_ids[None, :] == jnp.arange(images, dtype=jnp.int32)[:, None]).astype(bf16)
    pooled = lax.psum(jnp.dot(onehot, mixed, preferred_element_type=f32), "grp")
    text_vecs = unit_rows(all_texts(text_embed).astype(f32))
    cosine = jnp.dot(unit_rows(pooled), text_vecs.T, precision=lax.Precision.HIGHEST)
    same = jnp.arange(images)[:, None] == jnp.arange(text_vecs.shape[0])[None, :]
    row_loss = jnp.sum(losses(cosine, jnp.where(same, 1.0, -1.0)), axis=1)
    return (mixed[None], row_loss)


def solution(mesh):
    placed = (P("blk", "grp", None), P("blk", None), P(), P(), P("blk", None))
    return jax.shard_map(
        local,
        mesh=mesh,
        in_specs=placed,
        out_specs=(P("blk", "grp", None), P("blk")),
        check_vma=False,
    )
```

```python
import functools
import math

import jax
import jax.numpy as jnp
from jax import lax
from jax.experimental import pallas as pl
from jax.experimental.pallas import tpu as pltpu
from jax.sharding import PartitionSpec as P

HEADS = 8
MAXP = 1024
LANES = 128
SPARE = 8
SIZE = 72
PADDED = SIZE + SPARE
KEY_AT = SIZE - SPARE
QUERY_AT = 2 * SIZE
TEXT_ROWS = 16
RUN = 16
HIDDEN = -1e30
ORDER = (6, 7, 2, 4, 3, 5, 1, 0)
EARLY = (6, 7, 1, 0)
LATE = (2, 4, 3, 5)

logit_scale = 30.0
logit_bias = -5.0

VMEM_LIMIT = 32 * 1024 * 1024


def rounded_up(value, step):
    return (value + step - 1) // step * step


def split_in_two(total, images):
    row = lax.broadcasted_iota(jnp.int32, total.shape, 0)
    main = total.astype(jnp.bfloat16).astype(jnp.float32)
    return jnp.where(row < images, main, total - main)


def image_rows(ids, images):
    row = lax.broadcasted_iota(jnp.int32, (SPARE, ids.shape[1]), 0)
    return (lax.rem(row, images) == ids).astype(jnp.float32).astype(jnp.bfloat16)


def head_blocks(query, key, value, sums, pair):
    size = query.shape[0] // 2
    count = query.shape[1]
    for place in range(2):
        here = slice(place * size, (place + 1) * size)
        if sums is None:
            spare = jnp.zeros((SPARE, count), jnp.float32)
        else:
            first = pl.multiple_of((2 * pair + place) * LANES, LANES)
            parts = [sums[:, pl.ds(first, LANES)], sums[:, HEADS * LANES :]]
            held = sum(part.shape[1] for part in parts)
            spare = jnp.concatenate(parts + [jnp.zeros((SPARE, count - held), jnp.float32)], axis=1)
        yield jnp.concatenate([value[here], key[here], spare, query[here]], axis=0)


def store_by_core(core, blocks, same_ref, cross_ref):
    first, second = blocks
    same_ref[...] = jnp.where(core == 0, first, second).astype(jnp.bfloat16)
    cross_ref[...] = jnp.where(core == 0, second, first).astype(jnp.bfloat16)


def place_in_group():
    own = lax.rem(lax.axis_index("grp"), HEADS)
    return lax.div(own, 2), lax.rem(own, 2)


def far_kernel(images, piggy, ids_ref, rows_ref, weight_ref, normed_ref, sums_ref, same_ref, cross_ref, own_ids, rows_held, weight, id_sem, row_sem, sems):
    count, depth = rows_ref.shape
    width = weight_ref.shape[0] // 3
    wide = weight.shape[1]
    rows_fetch = pltpu.make_async_copy(rows_ref, rows_held, row_sem)
    rows_fetch.start()
    own = pl.multiple_of(lax.axis_index("grp") * count, LANES)
    ids_fetch = pltpu.make_async_copy(ids_ref.at[:, pl.ds(own, count)], own_ids, id_sem)
    ids_fetch.start()
    pair, core = place_in_group()
    pair = jnp.bitwise_xor(pair, 3)
    fetches = []
    for at in range(3):
        first = pl.multiple_of(at * width + pair * wide, 16)
        fetches.append(pltpu.make_async_copy(weight_ref.at[pl.ds(first, wide)], weight.at[at], sems.at[at]))
    for fetch in fetches:
        fetch.start()
    ids_fetch.wait()
    rows_fetch.wait()
    rows = rows_held[...]
    if piggy:
        sums = jnp.dot(image_rows(own_ids[...], images), rows, preferred_element_type=jnp.float32)
        sums_ref[...] = split_in_two(sums, images)
    values = rows.astype(jnp.float32)
    center = values - jnp.mean(values, axis=1, keepdims=True)
    spread = jnp.mean(center * center, axis=1, keepdims=True)
    normed = (center * lax.rsqrt(spread + 1e-06)).astype(jnp.bfloat16)
    normed_ref[...] = normed.T
    for fetch in fetches:
        fetch.wait()
    parts = [
        jnp.dot(weight[at], normed_ref[...], preferred_element_type=jnp.float32) for at in range(3)
    ]
    store_by_core(core, head_blocks(*parts, sums_ref if piggy else None, pair), same_ref, cross_ref)


def near_kernel(piggy, normed_ref, sums_ref, weight_ref, *out_refs):
    width = weight_ref.shape[0] // 3
    wide = 2 * width // HEADS
    own, core = place_in_group()
    for step, move in enumerate((1, 2, 0)):
        pair = jnp.bitwise_xor(own, move)
        parts = []
        for at in range(3):
            here = pl.ds(pl.multiple_of(at * width + pair * wide, 16), wide)
            parts.append(
                jnp.dot(weight_ref[here, :], normed_ref[...], preferred_element_type=jnp.float32)
            )
        blocks = head_blocks(*parts, sums_ref if piggy else None, pair)
        store_by_core(core, blocks, *out_refs[2 * step : 2 * step + 2])


def count_before(images, ids):
    image = lax.broadcasted_iota(jnp.int32, (rounded_up(images + 1, SPARE), ids.shape[1]), 0)
    before = jnp.sum((ids < image).astype(jnp.int32), axis=1, keepdims=True)
    return jnp.broadcast_to(before, (before.shape[0], LANES))


def write_marks(images, ids, marks):
    bits = max(1, (images - 1).bit_length())
    row = lax.broadcasted_iota(jnp.int32, (SPARE, ids.shape[1]), 0)
    bit = jnp.bitwise_and(lax.shift_right_logical(jnp.broadcast_to(ids, row.shape), row >> 1), 1)
    odd = jnp.bitwise_and(row, 1)
    used = row < 2 * bits
    outside = jnp.logical_or(ids < 0, ids >= images)
    key_side = jnp.where(odd == 1, bit, 1 - bit).astype(jnp.float32)
    key_side = jnp.where(outside, 1.0, key_side)
    marks[0] = jnp.where(used, key_side * HIDDEN, 0.0)
    marks[1] = jnp.where(used, jnp.where(odd == 1, 1 - bit, bit), 0).astype(jnp.float32)


def spare_sums(refs):
    parts = [ref[QUERY_AT : QUERY_AT + 16].astype(jnp.float32)[0:SPARE, 0 : 2 * LANES] for ref in refs]
    return sum(parts[1:], parts[0])


def image_at(images, starts, position):
    found = jnp.int32(0)
    for image in range(1, images):
        found += (starts[image] <= position).astype(jnp.int32)
    return found


def attend_images(images, ids_ref, keys, values, queries, attended, work, starts, halo):
    work = list(zip(work[0::2], work[1::2]))
    query_base = halo
    window, tile = work[0][0].shape
    size = attended.shape[0] - SPARE
    held = queries.shape[1]
    tiles = held // tile

    low = image_at(images, starts, query_base)
    high = image_at(images, starts, query_base + held - 1)

    def bounds(image):
        first = lax.div(jnp.maximum(starts[image] - query_base, 0), tile)
        last = lax.div(jnp.minimum(starts[image + 1] - query_base, held) - 1, tile)
        return jnp.minimum(first, tiles - 1), last

    def following(state):
        at, image = state
        more = at < bounds(image)[1]
        later = jnp.minimum(image + 1, high)
        first = jnp.where(image == high, at, bounds(later)[0])
        return jnp.where(more, at + 1, first), jnp.where(more, image, later)

    def window_of(image):
        begin = lax.div(starts[image], LANES) * LANES
        return pl.ds(pl.multiple_of(jnp.minimum(begin, keys.shape[0] - window), LANES), window)

    def score(state, scores, tops):
        at, image = state
        query = queries[:, pl.ds(pl.multiple_of(at * tile, tile), tile)]
        found = jnp.dot(keys[window_of(image), :], query, preferred_element_type=jnp.float32)
        scores[...] = found
        tops[...] = jnp.max(found, axis=0, keepdims=True)

    def weigh(state, scores, tops):
        at, image = state
        first = pl.multiple_of(at * tile, tile)
        labels = ids_ref[:, pl.ds(pl.multiple_of(query_base + first, LANES), tile)]
        probs = jnp.exp2((scores[...] - tops[...]) * (size ** (-0.5) * math.log2(math.e)))
        share = 1.0 / jnp.sum(probs, axis=0, keepdims=True)
        weighted = jnp.dot(
            values[:, window_of(image)], probs.astype(jnp.bfloat16), preferred_element_type=jnp.float32
        )
        place = (slice(None), pl.ds(first, tile))
        attended[place] = jnp.where(labels == image, weighted * share, attended[place])

    pairs = jnp.int32(0)
    for image in range(images):
        first, last = bounds(image)
        wanted = jnp.logical_and(low <= image, image <= high)
        pairs += jnp.where(wanted, last - first + 1, 0)

    def run(state, steps, ends):
        for step in range(steps):
            later = following(state)
            if step < steps - 1 or not ends:
                score(later, *work[(step + 1) % len(work)])
            weigh(state, *work[step % len(work)])
            state = later
        return state

    state = (jnp.int32(0), low)
    score(state, *work[0])
    limit = tiles + images - 1
    if limit <= RUN:
        run(state, limit, True)
    else:
        step = len(work) * max(1, RUN // (2 * len(work)))
        lax.fori_loop(0, lax.div(pairs + step - 1, step), lambda _, state: run(state, step, False), state)


def turned_keys(marked, block_ref):
    block = block_ref[KEY_AT : KEY_AT + PADDED].astype(jnp.float32)
    nothing = jnp.zeros((LANES - PADDED, block.shape[1]), jnp.float32)
    full = jnp.concatenate([marked, block[SPARE:], nothing], axis=0)
    return full.astype(jnp.bfloat16).T


def store_queries(marked, block_ref, queries, there):
    edge = block_ref[QUERY_AT : QUERY_AT + 16].astype(jnp.float32)
    edge = jnp.concatenate([marked, edge[SPARE:]], axis=0)
    queries[0:16, there] = edge.astype(jnp.bfloat16)
    queries[16:PADDED, there] = block_ref[QUERY_AT + 16 : QUERY_AT + PADDED]
    queries[PADDED:, there] = jnp.zeros((LANES - PADDED, block_ref.shape[1]), jnp.bfloat16)


def prepare_kernel(images, halo, ids_ref, out_weight_ref, *rest):
    got_refs, (keys, marks, before, weight, sems) = rest[: len(EARLY)], rest[len(EARLY) :]
    count = got_refs[0].shape[1]
    fetches = []
    for step, by in enumerate(ORDER):
        head = jnp.bitwise_xor(lax.rem(lax.axis_index("grp"), HEADS), by)
        first = lax.div(head, 2) * (2 * SIZE) + lax.rem(head, 2) * (SIZE - SPARE)
        fetches.append(
            pltpu.make_async_copy(
                out_weight_ref.at[pl.ds(pl.multiple_of(first, 16), PADDED)],
                weight.at[step * PADDED : (step + 1) * PADDED],
                sems.at[step],
            )
        )
        fetches[-1].start()
    before[...] = count_before(images, ids_ref[...])
    write_marks(images, ids_ref[...], marks)
    own = lax.rem(lax.axis_index("grp"), HEADS)
    for step, (by, ref) in enumerate(zip(EARLY, got_refs)):
        first = jnp.bitwise_xor(own, by) * count
        here = pl.ds(pl.multiple_of(halo + first, LANES), count)
        keys[step * count : (step + 1) * count, :] = turned_keys(marks[0, :, here], ref)
    for fetch in fetches:
        fetch.wait()


def attend_kernel(images, piggy, halo, ids_ref, before_ref, marks, early_keys, *rest):
    got_refs, rest = rest[:HEADS], rest[HEADS:]
    if piggy:
        text_ref, *rest = rest
    if halo:
        left_ref, right_ref, *rest = rest
    out_refs, rest = rest[:HEADS], rest[HEADS:]
    keys, values, queries, attended, *work, starts = rest
    count = got_refs[0].shape[1]
    padded = attended.shape[0]
    size = padded - SPARE
    total_rows = HEADS * count
    length = ids_ref.shape[1]
    ids = ids_ref[...]
    before = before_ref[...]
    for image in range(images + 1):
        starts[image] = before[image, 0]

    own = lax.rem(lax.axis_index("grp"), HEADS)
    for step, (by, ref) in enumerate(zip(EARLY + LATE, got_refs)):
        first = jnp.bitwise_xor(own, by) * count
        here = pl.ds(pl.multiple_of(halo + first, LANES), count)
        there = pl.ds(pl.multiple_of(first, LANES), count)
        if by in EARLY:
            keys[here, :] = early_keys[step * count : (step + 1) * count, :]
        else:
            keys[here, :] = turned_keys(marks[0, :, here], ref)
        values[:, here] = ref[0:PADDED]
        store_queries(marks[1, :, here], ref, queries, there)
    if halo:
        for ref, here in ((left_ref, slice(0, halo)), (right_ref, slice(length - halo, length))):
            keys[here, :] = turned_keys(marks[0, :, here], ref)
            values[:, here] = ref[0:PADDED]
    attend_images(images, ids_ref, keys, values, queries, attended, work, starts, halo)

    odd_head = lax.rem(own, 2) == 1
    mine = ids[:, halo : halo + total_rows]

    def placed(block, spare):
        even = jnp.concatenate([block[0:size], spare], axis=0)
        odd = jnp.concatenate([spare, block[0:size]], axis=0)
        return jnp.where(odd_head, odd, even)

    if piggy:
        nothing = jnp.zeros((SPARE, total_rows), jnp.float32)
        flat = placed(attended[...], nothing).astype(jnp.bfloat16)
        pooled = lax.dot_general(
            image_rows(mine, images), flat, (((1,), (1,)), ((), ())), preferred_element_type=jnp.float32
        )
        pooled = split_in_two(pooled, images)
        sums = spare_sums(got_refs)
        sums = split_in_two(sums + pltpu.roll(sums, images, axis=0), images)
        spare = jnp.concatenate(
            [pooled, jnp.zeros((SPARE, LANES - padded), jnp.float32), sums], axis=1
        )
        texts = text_ref[...].astype(jnp.float32)
        parts = [texts[:, at : at + count] for at in range(0, texts.shape[1], count)]
        unused = TEXT_ROWS - images * len(parts)
        below = jnp.concatenate(parts + [jnp.zeros((unused, count), jnp.float32)] * (unused > 0), axis=0)
        below = below.astype(jnp.bfloat16)
    else:
        spare = jnp.zeros((SPARE, count), jnp.float32)
    for by, out_ref in zip(ORDER, out_refs):
        there = pl.multiple_of(jnp.bitwise_xor(own, by) * count, LANES)
        out_ref[0:padded] = placed(attended[:, pl.ds(there, count)], spare).astype(jnp.bfloat16)
        if piggy:
            out_ref[padded:] = below


def joined_heads(got_refs, flat):
    own = lax.rem(lax.axis_index("grp"), HEADS)
    spares = []
    for step, (by, got_ref) in enumerate(zip(ORDER, got_refs)):
        odd = lax.rem(jnp.bitwise_xor(own, by), 2)
        at = step * PADDED
        top = got_ref[0:16].astype(jnp.float32)
        bottom = got_ref[PADDED - 16 : PADDED].astype(jnp.float32)
        spares.append(jnp.where(odd == 1, top[:SPARE], bottom[SPARE:]))
        top = jnp.concatenate([jnp.where(odd == 1, 0.0, top[:SPARE]), top[SPARE:]], axis=0)
        bottom = jnp.concatenate([bottom[:SPARE], jnp.where(odd == 1, bottom[SPARE:], 0.0)], axis=0)
        flat[at : at + 16] = top.astype(jnp.bfloat16)
        flat[at + 16 : at + PADDED - 16] = got_ref[16 : PADDED - 16]
        flat[at + PADDED - 16 : at + PADDED] = bottom.astype(jnp.bfloat16)
    return spares


def send_mixed_rows(rows_ref, weight_ref, flat, turned, mixed, mixed_ref, sems, meanwhile=None):
    turned[...] = flat[...].T
    pieces = sems.shape[0]
    step = rows_ref.shape[0] // pieces
    copies, value = [], None
    for piece in range(pieces):
        cut = slice(piece * step, (piece + 1) * step)
        if meanwhile is not None:
            value = meanwhile[piece](value)
        added = jnp.dot(turned[cut, :], weight_ref[...], preferred_element_type=jnp.float32)
        mixed[cut, :] = (rows_ref[cut, :].astype(jnp.float32) + added).astype(jnp.bfloat16)
        copies.append(pltpu.make_async_copy(mixed.at[cut], mixed_ref.at[cut], sems.at[piece]))
        copies[-1].start()
    return copies


def unit_rows(matrix):
    return matrix * lax.rsqrt(jnp.sum(matrix * matrix, axis=1, keepdims=True) + 1e-06)


def losses(cosine, labels):
    logits = -labels * (logit_scale * cosine + logit_bias)
    return jnp.maximum(logits, 0.0) + jnp.log1p(jnp.exp(-jnp.abs(logits)))


def finish_kernel(images, rows_ref, weight_ref, text_ref, *rest):
    got_refs, rest = rest[:HEADS], rest[HEADS:]
    mixed_ref, loss_ref, flat, turned, mixed, sems, pooled_heads, patch_sums, far_texts, loss, loss_sem = rest
    spares = joined_heads(got_refs, flat)
    own = lax.rem(lax.axis_index("grp"), HEADS)
    patch_sums[:, HEADS * LANES :] = spares[0][:, 2 * LANES :]
    for step, (by, spare) in enumerate(zip(ORDER, spares)):
        pooled_heads[:, step * PADDED : (step + 1) * PADDED] = spare[:, 0:PADDED]
        head = jnp.bitwise_xor(own, by)
        patch_sums[:, pl.ds(pl.multiple_of(head * LANES, LANES), LANES)] = spare[:, LANES : 2 * LANES]
        below = got_refs[step][PADDED:].astype(jnp.float32)
        count = below.shape[1]
        for part in range(patch_sums.shape[1] // count):
            here = slice(part * count, (part + 1) * count)
            far_texts[head, :, here] = below[part * images : (part + 1) * images]

    def find_images(_):
        pooled = jnp.dot(
            pooled_heads[...].astype(jnp.bfloat16), weight_ref[...], preferred_element_type=jnp.float32
        )
        pooled = pooled + patch_sums[...]
        others = [far_texts[place] for place in range(lax.axis_size("blk") - 1)]
        texts = jnp.concatenate([text_ref[...].astype(jnp.float32)] + others, axis=0)
        return pooled + pltpu.roll(pooled, images, axis=0), unit_rows(texts)

    def find_cosines(vectors):
        pooled, text_vecs = vectors
        return lax.dot_general(
            text_vecs,
            unit_rows(pooled),
            (((1,), (1,)), ((), ())),
            precision=lax.Precision.HIGHEST,
            preferred_element_type=jnp.float32,
        )

    def find_losses(cosine):
        text = lax.broadcasted_iota(jnp.int32, cosine.shape, 0)
        image = lax.broadcasted_iota(jnp.int32, cosine.shape, 1)
        terms = losses(cosine, jnp.where(text == image, 1.0, -1.0))
        loss[...] = jnp.sum(terms, axis=0, keepdims=True)[:, 0:images]
        loss_copy.start()

    loss_copy = pltpu.make_async_copy(loss, loss_ref, loss_sem)
    meanwhile = (find_images, find_cosines, find_losses)
    copies = send_mixed_rows(rows_ref, weight_ref, flat, turned, mixed, mixed_ref, sems, meanwhile)
    for copy in copies + [loss_copy]:
        copy.wait()


def mix_kernel(rows_ref, weight_ref, *rest):
    got_refs, rest = rest[:HEADS], rest[HEADS:]
    mixed_ref, flat, turned, mixed, sems = rest
    joined_heads(got_refs, flat)
    for copy in send_mixed_rows(rows_ref, weight_ref, flat, turned, mixed, mixed_ref, sems):
        copy.wait()


def in_vmem(count):
    return [pl.BlockSpec(memory_space=pltpu.VMEM)] * count


def in_hbm(value):
    return pltpu.with_memory_space_constraint(value, pltpu.HBM)


def call(kernel, out_shape, scratch, in_specs, flops, out_specs=None):
    if out_specs is None:
        out_specs = jax.tree.map(lambda _: pl.BlockSpec(memory_space=pltpu.VMEM), out_shape)
    return pl.pallas_call(
        kernel,
        out_shape=out_shape,
        in_specs=in_specs,
        out_specs=out_specs,
        scratch_shapes=scratch,
        compiler_params=pltpu.CompilerParams(vmem_limit_bytes=VMEM_LIMIT),
        cost_estimate=pl.CostEstimate(flops=flops, bytes_accessed=8 << 20, transcendentals=0),
    )


def moved(value, axis, pairs):
    return lax.ppermute(value, axis, pairs)


def partner(place, by, peers):
    return place ^ by if peers & (peers - 1) == 0 else (place + by) % peers


def all_texts(texts):
    peers = lax.axis_size("blk")
    steps = [[(partner(i, by, peers), i) for i in range(peers)] for by in range(1, peers)]
    return jnp.concatenate([texts] + [moved(texts, "blk", pairs) for pairs in steps], axis=0)


def one_text_block(texts):
    peers = lax.axis_size("blk")
    pairs = []
    for place in range(lax.axis_size("grp")):
        by = place % (peers - 1) + 1
        pairs += [(place * peers + partner(i, by, peers), place * peers + i) for i in range(peers)]
    return moved(texts, ("grp", "blk"), pairs)


def traded(blocks):
    peers = range(lax.axis_size("grp"))
    trades = {by: moved(blocks[by], "grp", [(i, i ^ by) for i in peers]) for by in ORDER if by}
    return {**trades, 0: blocks[0]}


def local(patches, segment_ids, qkv_weight, out_weight, text_embed):
    rows = patches[0]
    count, depth = rows.shape
    width = out_weight.shape[0]
    size = width // HEADS
    padded = size + SPARE
    images = text_embed.shape[0]
    group_size = lax.axis_size("grp")
    parts = group_size // HEADS
    piggy = (
        parts == 1
        and 2 * images == SPARE
        and count >= depth - (HEADS - 2) * LANES
        and depth % count == 0
        and images * (depth // count) <= TEXT_ROWS
        and 1 < lax.axis_size("blk") <= HEADS + 1
    )
    bf16, f32 = jnp.bfloat16, jnp.float32
    shape = jax.ShapeDtypeStruct

    block = shape((3 * size + SPARE, count), bf16)
    hbm = pl.BlockSpec(memory_space=pltpu.HBM)
    turned_weight = qkv_weight.T
    normed, sums, *sent = call(
        functools.partial(far_kernel, images, piggy),
        (shape((depth, count), bf16), shape((SPARE, depth), f32), block, block),
        [
            pltpu.VMEM((1, count), jnp.int32),
            pltpu.VMEM((count, depth), bf16),
            pltpu.VMEM((3, 2 * size, depth), bf16),
            pltpu.SemaphoreType.DMA,
            pltpu.SemaphoreType.DMA,
            pltpu.SemaphoreType.DMA((3,)),
        ],
        [hbm] * 3,
        2 * count * depth * 6 * size,
    )(in_hbm(segment_ids), in_hbm(rows), in_hbm(turned_weight))
    sent += call(
        functools.partial(near_kernel, piggy),
        (block,) * 6,
        [],
        in_vmem(3),
        2 * count * depth * 18 * size,
    )(normed, sums, turned_weight)
    sent = dict(zip((6, 7, 2, 3, 4, 5, 0, 1), sent))
    if piggy:
        late_texts, sent[0] = lax.optimization_barrier((text_embed, sent[0]))
        halos_and_texts = [one_text_block(late_texts)]
    else:
        halos_and_texts = []
    got = traded(sent)

    length = HEADS * count
    halo = 0
    near_ids = segment_ids
    if parts > 1:
        halo = rounded_up(MAXP - 1, LANES)
        part = lax.axis_index("grp") // HEADS
        whole_ids = jnp.concatenate(
            [
                jnp.full((1, halo), -1, jnp.int32),
                segment_ids,
                jnp.full((1, halo), images, jnp.int32),
            ],
            axis=1,
        )
        near_ids = lax.dynamic_slice_in_dim(whole_ids, part * length, length + 2 * halo, axis=1)
        order = jnp.bitwise_xor(lax.axis_index("grp") % HEADS, jnp.arange(HEADS))
        flat = jnp.stack([got[by] for by in range(HEADS)])[order][:, : 2 * size].transpose(1, 0, 2).reshape(2 * size, length)
        flat = jnp.concatenate([flat, jnp.zeros((16, length), bf16)], axis=0)
        ahead = [(i, i + HEADS) for i in range(group_size - HEADS)]
        back = [(i + HEADS, i) for i in range(group_size - HEADS)]
        left = moved(flat[:, length - halo :], "grp", ahead)
        right = moved(flat[:, :halo], "grp", back)
        halos_and_texts += [left, right]
    reach = length + 2 * halo
    window = min(rounded_up(MAXP + LANES - 1, LANES), reach)
    tile = 2 * LANES
    early_keys, marks, before, weight = call(
        functools.partial(prepare_kernel, images, halo),
        (
            shape((len(EARLY) * count, LANES), bf16),
            shape((2, SPARE, reach), f32),
            shape((rounded_up(images + 1, SPARE), LANES), jnp.int32),
            shape((HEADS * padded, depth), bf16),
        ),
        [pltpu.SemaphoreType.DMA((HEADS,))],
        in_vmem(1) + [hbm] + in_vmem(len(EARLY)),
        1 << 30,
    )(near_ids, in_hbm(out_weight), *[got[by] for by in EARLY])
    operands = [near_ids, before, marks, early_keys, *[got[by] for by in EARLY + LATE], *halos_and_texts]
    answers = call(
        functools.partial(attend_kernel, images, piggy, halo),
        (shape((padded + TEXT_ROWS * piggy, count), bf16),) * HEADS,
        [
            pltpu.VMEM((reach, LANES), bf16),
            pltpu.VMEM((padded, reach), bf16),
            pltpu.VMEM((LANES, length), bf16),
            pltpu.VMEM((padded, length), f32),
        ]
        + [pltpu.VMEM((window, tile), f32), pltpu.VMEM((1, tile), f32)] * 3
        + [pltpu.SMEM((images + 1,), jnp.int32)],
        in_vmem(len(operands)),
        4 * size * length * MAXP,
    )(*operands)
    home = traded(dict(zip(ORDER, answers)))
    home = [home[by] for by in ORDER]

    joined = [
        pltpu.VMEM((HEADS * padded, count), bf16),
        pltpu.VMEM((count, HEADS * padded), bf16),
        pltpu.VMEM((count, depth), bf16),
        pltpu.SemaphoreType.DMA((3,)),
    ]
    flops = 2 * count * depth * width
    if piggy:
        mixed, row_loss = call(
            functools.partial(finish_kernel, images),
            (shape((count, depth), bf16), shape((1, images), f32)),
            joined
            + [
                pltpu.VMEM((SPARE, HEADS * padded), f32),
                pltpu.VMEM((SPARE, depth), f32),
                pltpu.VMEM((HEADS, images, depth), f32),
                pltpu.VMEM((1, images), f32),
                pltpu.SemaphoreType.DMA,
            ],
            in_vmem(3 + HEADS),
            flops,
            (hbm, hbm),
        )(rows, weight, text_embed, *home)
        return (mixed[None], row_loss[0])
    mixed = call(mix_kernel, shape((count, depth), bf16), joined, in_vmem(2 + HEADS), flops, hbm)(
        rows, weight, *home
    )
    own_ids = lax.dynamic_slice_in_dim(segment_ids[0], lax.axis_index("grp") * count, count)
    onehot = (own_ids[None, :] == jnp.arange(images, dtype=jnp.int32)[:, None]).astype(bf16)
    pooled = lax.psum(jnp.dot(onehot, mixed, preferred_element_type=f32), "grp")
    text_vecs = unit_rows(all_texts(text_embed).astype(f32))
    cosine = jnp.dot(unit_rows(pooled), text_vecs.T, precision=lax.Precision.HIGHEST)
    same = jnp.arange(images)[:, None] == jnp.arange(text_vecs.shape[0])[None, :]
    row_loss = jnp.sum(losses(cosine, jnp.where(same, 1.0, -1.0)), axis=1)
    return (mixed[None], row_loss)


def solution(mesh):
    placed = (P("blk", "grp", None), P("blk", None), P(), P(), P("blk", None))
    return jax.shard_map(
        local,
        mesh=mesh,
        in_specs=placed,
        out_specs=(P("blk", "grp", None), P("blk")),
        check_vma=False,
    )
```

```python
import functools
import math

import jax
import jax.numpy as jnp
from jax import lax
from jax.experimental import pallas as pl
from jax.experimental.pallas import tpu as pltpu
from jax.sharding import PartitionSpec as P

HEADS = 8
MAXP = 1024
LANES = 128
SPARE = 8
SIZE = 72
PADDED = SIZE + SPARE
KEY_AT = SIZE - SPARE
QUERY_AT = 2 * SIZE
TEXT_ROWS = 16
RUN = 5
HIDDEN = -1e30
ORDER = (6, 7, 2, 4, 3, 5, 1, 0)
EARLY = (6, 7, 1, 0)
LATE = (2, 4, 3, 5)

logit_scale = 30.0
logit_bias = -5.0

VMEM_LIMIT = 32 * 1024 * 1024


def rounded_up(value, step):
    return (value + step - 1) // step * step


def split_in_two(total, images):
    row = lax.broadcasted_iota(jnp.int32, total.shape, 0)
    main = total.astype(jnp.bfloat16).astype(jnp.float32)
    return jnp.where(row < images, main, total - main)


def image_rows(ids, images):
    row = lax.broadcasted_iota(jnp.int32, (SPARE, ids.shape[1]), 0)
    return (lax.rem(row, images) == ids).astype(jnp.float32).astype(jnp.bfloat16)


def head_blocks(query, key, value, sums, pair):
    size = query.shape[0] // 2
    count = query.shape[1]
    for place in range(2):
        here = slice(place * size, (place + 1) * size)
        if sums is None:
            spare = jnp.zeros((SPARE, count), jnp.float32)
        else:
            first = pl.multiple_of((2 * pair + place) * LANES, LANES)
            parts = [sums[:, pl.ds(first, LANES)], sums[:, HEADS * LANES :]]
            held = sum(part.shape[1] for part in parts)
            spare = jnp.concatenate(parts + [jnp.zeros((SPARE, count - held), jnp.float32)], axis=1)
        yield jnp.concatenate([value[here], key[here], spare, query[here]], axis=0)


def store_by_core(core, blocks, same_ref, cross_ref):
    first, second = blocks
    same_ref[...] = jnp.where(core == 0, first, second).astype(jnp.bfloat16)
    cross_ref[...] = jnp.where(core == 0, second, first).astype(jnp.bfloat16)


def place_in_group():
    own = lax.rem(lax.axis_index("grp"), HEADS)
    return lax.div(own, 2), lax.rem(own, 2)


def far_kernel(images, piggy, ids_ref, rows_ref, weight_ref, normed_ref, sums_ref, same_ref, cross_ref, own_ids, rows_held, weight, id_sem, row_sem, sems):
    count, depth = rows_ref.shape
    width = weight_ref.shape[0] // 3
    wide = weight.shape[1]
    rows_fetch = pltpu.make_async_copy(rows_ref, rows_held, row_sem)
    rows_fetch.start()
    own = pl.multiple_of(lax.axis_index("grp") * count, LANES)
    ids_fetch = pltpu.make_async_copy(ids_ref.at[:, pl.ds(own, count)], own_ids, id_sem)
    ids_fetch.start()
    pair, core = place_in_group()
    pair = jnp.bitwise_xor(pair, 3)
    fetches = []
    for at in range(3):
        first = pl.multiple_of(at * width + pair * wide, 16)
        fetches.append(pltpu.make_async_copy(weight_ref.at[pl.ds(first, wide)], weight.at[at], sems.at[at]))
    for fetch in fetches:
        fetch.start()
    ids_fetch.wait()
    rows_fetch.wait()
    rows = rows_held[...]
    if piggy:
        sums = jnp.dot(image_rows(own_ids[...], images), rows, preferred_element_type=jnp.float32)
        sums_ref[...] = split_in_two(sums, images)
    values = rows.astype(jnp.float32)
    center = values - jnp.mean(values, axis=1, keepdims=True)
    spread = jnp.mean(center * center, axis=1, keepdims=True)
    normed = (center * lax.rsqrt(spread + 1e-06)).astype(jnp.bfloat16)
    normed_ref[...] = normed.T
    for fetch in fetches:
        fetch.wait()
    parts = [
        jnp.dot(weight[at], normed_ref[...], preferred_element_type=jnp.float32) for at in range(3)
    ]
    store_by_core(core, head_blocks(*parts, sums_ref if piggy else None, pair), same_ref, cross_ref)


def near_kernel(piggy, normed_ref, sums_ref, weight_ref, *out_refs):
    width = weight_ref.shape[0] // 3
    wide = 2 * width // HEADS
    own, core = place_in_group()
    for step, move in enumerate((1, 2, 0)):
        pair = jnp.bitwise_xor(own, move)
        parts = []
        for at in range(3):
            here = pl.ds(pl.multiple_of(at * width + pair * wide, 16), wide)
            parts.append(
                jnp.dot(weight_ref[here, :], normed_ref[...], preferred_element_type=jnp.float32)
            )
        blocks = head_blocks(*parts, sums_ref if piggy else None, pair)
        store_by_core(core, blocks, *out_refs[2 * step : 2 * step + 2])


def count_before(images, ids):
    image = lax.broadcasted_iota(jnp.int32, (rounded_up(images + 1, SPARE), ids.shape[1]), 0)
    before = jnp.sum((ids < image).astype(jnp.int32), axis=1, keepdims=True)
    return jnp.broadcast_to(before, (before.shape[0], LANES))


def write_marks(images, ids, marks):
    bits = max(1, (images - 1).bit_length())
    row = lax.broadcasted_iota(jnp.int32, (SPARE, ids.shape[1]), 0)
    bit = jnp.bitwise_and(lax.shift_right_logical(jnp.broadcast_to(ids, row.shape), row >> 1), 1)
    odd = jnp.bitwise_and(row, 1)
    used = row < 2 * bits
    outside = jnp.logical_or(ids < 0, ids >= images)
    key_side = jnp.where(odd == 1, bit, 1 - bit).astype(jnp.float32)
    key_side = jnp.where(outside, 1.0, key_side)
    marks[0] = jnp.where(used, key_side * HIDDEN, 0.0)
    marks[1] = jnp.where(used, jnp.where(odd == 1, 1 - bit, bit), 0).astype(jnp.float32)


def spare_sums(refs):
    parts = [ref[QUERY_AT : QUERY_AT + 16].astype(jnp.float32)[0:SPARE, 0 : 2 * LANES] for ref in refs]
    return sum(parts[1:], parts[0])


def image_at(images, starts, position):
    found = jnp.int32(0)
    for image in range(1, images):
        found += (starts[image] <= position).astype(jnp.int32)
    return found


def attend_images(images, ids_ref, keys, values, queries, attended, work, starts, halo):
    work = list(zip(work[0::2], work[1::2]))
    query_base = halo
    window, tile = work[0][0].shape
    size = attended.shape[0] - SPARE
    held = queries.shape[1]
    tiles = held // tile

    low = image_at(images, starts, query_base)
    high = image_at(images, starts, query_base + held - 1)

    def bounds(image):
        first = lax.div(jnp.maximum(starts[image] - query_base, 0), tile)
        last = lax.div(jnp.minimum(starts[image + 1] - query_base, held) - 1, tile)
        return jnp.minimum(first, tiles - 1), last

    def following(state):
        at, image = state
        more = at < bounds(image)[1]
        later = jnp.minimum(image + 1, high)
        first = jnp.where(image == high, at, bounds(later)[0])
        return jnp.where(more, at + 1, first), jnp.where(more, image, later)

    def window_of(image):
        begin = lax.div(starts[image], LANES) * LANES
        return pl.ds(pl.multiple_of(jnp.minimum(begin, keys.shape[0] - window), LANES), window)

    def score(state, scores, tops):
        at, image = state
        query = queries[:, pl.ds(pl.multiple_of(at * tile, tile), tile)]
        found = jnp.dot(keys[window_of(image), :], query, preferred_element_type=jnp.float32)
        scores[...] = found
        tops[...] = jnp.max(found, axis=0, keepdims=True)

    def weigh(state, scores, tops):
        at, image = state
        first = pl.multiple_of(at * tile, tile)
        labels = ids_ref[:, pl.ds(pl.multiple_of(query_base + first, LANES), tile)]
        probs = jnp.exp2((scores[...] - tops[...]) * (size ** (-0.5) * math.log2(math.e)))
        share = 1.0 / jnp.sum(probs, axis=0, keepdims=True)
        weighted = jnp.dot(
            values[:, window_of(image)], probs.astype(jnp.bfloat16), preferred_element_type=jnp.float32
        )
        place = (slice(None), pl.ds(first, tile))
        attended[place] = jnp.where(labels == image, weighted * share, attended[place])

    pairs = jnp.int32(0)
    for image in range(images):
        first, last = bounds(image)
        wanted = jnp.logical_and(low <= image, image <= high)
        pairs += jnp.where(wanted, last - first + 1, 0)

    def run(_, state):
        for step in range(len(work)):
            later = following(state)
            score(later, *work[(step + 1) % len(work)])
            weigh(state, *work[step])
            state = later
        return state

    begun = (jnp.int32(0), low)
    score(begun, *work[0])
    lax.fori_loop(0, lax.div(pairs + len(work) - 1, len(work)), run, begun)


def turned_keys(marked, block_ref):
    block = block_ref[KEY_AT : KEY_AT + PADDED].astype(jnp.float32)
    nothing = jnp.zeros((LANES - PADDED, block.shape[1]), jnp.float32)
    full = jnp.concatenate([marked, block[SPARE:], nothing], axis=0)
    return full.astype(jnp.bfloat16).T


def store_queries(marked, block_ref, queries, there):
    edge = block_ref[QUERY_AT : QUERY_AT + 16].astype(jnp.float32)
    edge = jnp.concatenate([marked, edge[SPARE:]], axis=0)
    queries[0:16, there] = edge.astype(jnp.bfloat16)
    queries[16:PADDED, there] = block_ref[QUERY_AT + 16 : QUERY_AT + PADDED]
    queries[PADDED:, there] = jnp.zeros((LANES - PADDED, block_ref.shape[1]), jnp.bfloat16)


def prepare_kernel(images, halo, ids_ref, out_weight_ref, *rest):
    got_refs, (keys, marks, before, weight, sems) = rest[: len(EARLY)], rest[len(EARLY) :]
    count = got_refs[0].shape[1]
    fetches = []
    for step, by in enumerate(ORDER):
        head = jnp.bitwise_xor(lax.rem(lax.axis_index("grp"), HEADS), by)
        first = lax.div(head, 2) * (2 * SIZE) + lax.rem(head, 2) * (SIZE - SPARE)
        fetches.append(
            pltpu.make_async_copy(
                out_weight_ref.at[pl.ds(pl.multiple_of(first, 16), PADDED)],
                weight.at[step * PADDED : (step + 1) * PADDED],
                sems.at[step],
            )
        )
        fetches[-1].start()
    before[...] = count_before(images, ids_ref[...])
    write_marks(images, ids_ref[...], marks)
    own = lax.rem(lax.axis_index("grp"), HEADS)
    for step, (by, ref) in enumerate(zip(EARLY, got_refs)):
        first = jnp.bitwise_xor(own, by) * count
        here = pl.ds(pl.multiple_of(halo + first, LANES), count)
        keys[step * count : (step + 1) * count, :] = turned_keys(marks[0, :, here], ref)
    for fetch in fetches:
        fetch.wait()


def attend_kernel(images, piggy, halo, ids_ref, before_ref, marks, early_keys, *rest):
    got_refs, rest = rest[:HEADS], rest[HEADS:]
    if piggy:
        text_ref, *rest = rest
    if halo:
        left_ref, right_ref, *rest = rest
    out_refs, rest = rest[:HEADS], rest[HEADS:]
    keys, values, queries, attended, *work, starts = rest
    count = got_refs[0].shape[1]
    padded = attended.shape[0]
    size = padded - SPARE
    total_rows = HEADS * count
    length = ids_ref.shape[1]
    ids = ids_ref[...]
    before = before_ref[...]
    for image in range(images + 1):
        starts[image] = before[image, 0]

    own = lax.rem(lax.axis_index("grp"), HEADS)
    for step, (by, ref) in enumerate(zip(EARLY + LATE, got_refs)):
        first = jnp.bitwise_xor(own, by) * count
        here = pl.ds(pl.multiple_of(halo + first, LANES), count)
        there = pl.ds(pl.multiple_of(first, LANES), count)
        if by in EARLY:
            keys[here, :] = early_keys[step * count : (step + 1) * count, :]
        else:
            keys[here, :] = turned_keys(marks[0, :, here], ref)
        values[:, here] = ref[0:PADDED]
        store_queries(marks[1, :, here], ref, queries, there)
    if halo:
        for ref, here in ((left_ref, slice(0, halo)), (right_ref, slice(length - halo, length))):
            keys[here, :] = turned_keys(marks[0, :, here], ref)
            values[:, here] = ref[0:PADDED]
    attend_images(images, ids_ref, keys, values, queries, attended, work, starts, halo)

    odd_head = lax.rem(own, 2) == 1
    mine = ids[:, halo : halo + total_rows]

    def placed(block, spare):
        even = jnp.concatenate([block[0:size], spare], axis=0)
        odd = jnp.concatenate([spare, block[0:size]], axis=0)
        return jnp.where(odd_head, odd, even)

    if piggy:
        nothing = jnp.zeros((SPARE, total_rows), jnp.float32)
        flat = placed(attended[...], nothing).astype(jnp.bfloat16)
        pooled = lax.dot_general(
            image_rows(mine, images), flat, (((1,), (1,)), ((), ())), preferred_element_type=jnp.float32
        )
        pooled = split_in_two(pooled, images)
        sums = spare_sums(got_refs)
        sums = split_in_two(sums + pltpu.roll(sums, images, axis=0), images)
        spare = jnp.concatenate(
            [pooled, jnp.zeros((SPARE, LANES - padded), jnp.float32), sums], axis=1
        )
        texts = text_ref[...].astype(jnp.float32)
        parts = [texts[:, at : at + count] for at in range(0, texts.shape[1], count)]
        unused = TEXT_ROWS - images * len(parts)
        below = jnp.concatenate(parts + [jnp.zeros((unused, count), jnp.float32)] * (unused > 0), axis=0)
        below = below.astype(jnp.bfloat16)
    else:
        spare = jnp.zeros((SPARE, count), jnp.float32)
    for by, out_ref in zip(ORDER, out_refs):
        there = pl.multiple_of(jnp.bitwise_xor(own, by) * count, LANES)
        out_ref[0:padded] = placed(attended[:, pl.ds(there, count)], spare).astype(jnp.bfloat16)
        if piggy:
            out_ref[padded:] = below


def joined_heads(got_refs, flat):
    own = lax.rem(lax.axis_index("grp"), HEADS)
    spares = []
    for step, (by, got_ref) in enumerate(zip(ORDER, got_refs)):
        odd = lax.rem(jnp.bitwise_xor(own, by), 2)
        at = step * PADDED
        top = got_ref[0:16].astype(jnp.float32)
        bottom = got_ref[PADDED - 16 : PADDED].astype(jnp.float32)
        spares.append(jnp.where(odd == 1, top[:SPARE], bottom[SPARE:]))
        top = jnp.concatenate([jnp.where(odd == 1, 0.0, top[:SPARE]), top[SPARE:]], axis=0)
        bottom = jnp.concatenate([bottom[:SPARE], jnp.where(odd == 1, bottom[SPARE:], 0.0)], axis=0)
        flat[at : at + 16] = top.astype(jnp.bfloat16)
        flat[at + 16 : at + PADDED - 16] = got_ref[16 : PADDED - 16]
        flat[at + PADDED - 16 : at + PADDED] = bottom.astype(jnp.bfloat16)
    return spares


def send_mixed_rows(rows_ref, weight_ref, flat, turned, mixed, mixed_ref, sems, meanwhile=None):
    turned[...] = flat[...].T
    pieces = sems.shape[0]
    step = rows_ref.shape[0] // pieces
    copies, value = [], None
    for piece in range(pieces):
        cut = slice(piece * step, (piece + 1) * step)
        if meanwhile is not None:
            value = meanwhile[piece](value)
        added = jnp.dot(turned[cut, :], weight_ref[...], preferred_element_type=jnp.float32)
        mixed[cut, :] = (rows_ref[cut, :].astype(jnp.float32) + added).astype(jnp.bfloat16)
        copies.append(pltpu.make_async_copy(mixed.at[cut], mixed_ref.at[cut], sems.at[piece]))
        copies[-1].start()
    return copies


def unit_rows(matrix):
    return matrix * lax.rsqrt(jnp.sum(matrix * matrix, axis=1, keepdims=True) + 1e-06)


def losses(cosine, labels):
    logits = -labels * (logit_scale * cosine + logit_bias)
    return jnp.maximum(logits, 0.0) + jnp.log1p(jnp.exp(-jnp.abs(logits)))


def finish_kernel(images, rows_ref, weight_ref, text_ref, *rest):
    got_refs, rest = rest[:HEADS], rest[HEADS:]
    mixed_ref, loss_ref, flat, turned, mixed, sems, pooled_heads, patch_sums, far_texts, loss, loss_sem = rest
    spares = joined_heads(got_refs, flat)
    own = lax.rem(lax.axis_index("grp"), HEADS)
    patch_sums[:, HEADS * LANES :] = spares[0][:, 2 * LANES :]
    for step, (by, spare) in enumerate(zip(ORDER, spares)):
        pooled_heads[:, step * PADDED : (step + 1) * PADDED] = spare[:, 0:PADDED]
        head = jnp.bitwise_xor(own, by)
        patch_sums[:, pl.ds(pl.multiple_of(head * LANES, LANES), LANES)] = spare[:, LANES : 2 * LANES]
        below = got_refs[step][PADDED:].astype(jnp.float32)
        count = below.shape[1]
        for part in range(patch_sums.shape[1] // count):
            here = slice(part * count, (part + 1) * count)
            far_texts[head, :, here] = below[part * images : (part + 1) * images]

    def find_images(_):
        pooled = jnp.dot(
            pooled_heads[...].astype(jnp.bfloat16), weight_ref[...], preferred_element_type=jnp.float32
        )
        pooled = pooled + patch_sums[...]
        others = [far_texts[place] for place in range(lax.axis_size("blk") - 1)]
        texts = jnp.concatenate([text_ref[...].astype(jnp.float32)] + others, axis=0)
        return pooled + pltpu.roll(pooled, images, axis=0), unit_rows(texts)

    def find_cosines(vectors):
        pooled, text_vecs = vectors
        return lax.dot_general(
            text_vecs,
            unit_rows(pooled),
            (((1,), (1,)), ((), ())),
            precision=lax.Precision.HIGHEST,
            preferred_element_type=jnp.float32,
        )

    def find_losses(cosine):
        text = lax.broadcasted_iota(jnp.int32, cosine.shape, 0)
        image = lax.broadcasted_iota(jnp.int32, cosine.shape, 1)
        terms = losses(cosine, jnp.where(text == image, 1.0, -1.0))
        loss[...] = jnp.sum(terms, axis=0, keepdims=True)[:, 0:images]
        loss_copy.start()

    loss_copy = pltpu.make_async_copy(loss, loss_ref, loss_sem)
    meanwhile = (find_images, find_cosines, find_losses)
    copies = send_mixed_rows(rows_ref, weight_ref, flat, turned, mixed, mixed_ref, sems, meanwhile)
    for copy in copies + [loss_copy]:
        copy.wait()


def mix_kernel(rows_ref, weight_ref, *rest):
    got_refs, rest = rest[:HEADS], rest[HEADS:]
    mixed_ref, flat, turned, mixed, sems = rest
    joined_heads(got_refs, flat)
    for copy in send_mixed_rows(rows_ref, weight_ref, flat, turned, mixed, mixed_ref, sems):
        copy.wait()


def in_vmem(count):
    return [pl.BlockSpec(memory_space=pltpu.VMEM)] * count


def in_hbm(value):
    return pltpu.with_memory_space_constraint(value, pltpu.HBM)


def call(kernel, out_shape, scratch, in_specs, flops, out_specs=None):
    if out_specs is None:
        out_specs = jax.tree.map(lambda _: pl.BlockSpec(memory_space=pltpu.VMEM), out_shape)
    return pl.pallas_call(
        kernel,
        out_shape=out_shape,
        in_specs=in_specs,
        out_specs=out_specs,
        scratch_shapes=scratch,
        compiler_params=pltpu.CompilerParams(vmem_limit_bytes=VMEM_LIMIT),
        cost_estimate=pl.CostEstimate(flops=flops, bytes_accessed=8 << 20, transcendentals=0),
    )


def moved(value, axis, pairs):
    return lax.ppermute(value, axis, pairs)


def partner(place, by, peers):
    return place ^ by if peers & (peers - 1) == 0 else (place + by) % peers


def all_texts(texts):
    peers = lax.axis_size("blk")
    steps = [[(partner(i, by, peers), i) for i in range(peers)] for by in range(1, peers)]
    return jnp.concatenate([texts] + [moved(texts, "blk", pairs) for pairs in steps], axis=0)


def one_text_block(texts):
    peers = lax.axis_size("blk")
    pairs = []
    for place in range(lax.axis_size("grp")):
        by = place % (peers - 1) + 1
        pairs += [(place * peers + partner(i, by, peers), place * peers + i) for i in range(peers)]
    return moved(texts, ("grp", "blk"), pairs)


def traded(blocks):
    peers = range(lax.axis_size("grp"))
    trades = {by: moved(blocks[by], "grp", [(i, i ^ by) for i in peers]) for by in ORDER if by}
    return {**trades, 0: blocks[0]}


def local(patches, segment_ids, qkv_weight, out_weight, text_embed):
    rows = patches[0]
    count, depth = rows.shape
    width = out_weight.shape[0]
    size = width // HEADS
    padded = size + SPARE
    images = text_embed.shape[0]
    group_size = lax.axis_size("grp")
    parts = group_size // HEADS
    piggy = (
        parts == 1
        and 2 * images == SPARE
        and count >= depth - (HEADS - 2) * LANES
        and depth % count == 0
        and images * (depth // count) <= TEXT_ROWS
        and 1 < lax.axis_size("blk") <= HEADS + 1
    )
    bf16, f32 = jnp.bfloat16, jnp.float32
    shape = jax.ShapeDtypeStruct

    block = shape((3 * size + SPARE, count), bf16)
    hbm = pl.BlockSpec(memory_space=pltpu.HBM)
    turned_weight = qkv_weight.T
    normed, sums, *sent = call(
        functools.partial(far_kernel, images, piggy),
        (shape((depth, count), bf16), shape((SPARE, depth), f32), block, block),
        [
            pltpu.VMEM((1, count), jnp.int32),
            pltpu.VMEM((count, depth), bf16),
            pltpu.VMEM((3, 2 * size, depth), bf16),
            pltpu.SemaphoreType.DMA,
            pltpu.SemaphoreType.DMA,
            pltpu.SemaphoreType.DMA((3,)),
        ],
        [hbm] * 3,
        2 * count * depth * 6 * size,
    )(in_hbm(segment_ids), in_hbm(rows), in_hbm(turned_weight))
    sent += call(
        functools.partial(near_kernel, piggy),
        (block,) * 6,
        [],
        in_vmem(3),
        2 * count * depth * 18 * size,
    )(normed, sums, turned_weight)
    sent = dict(zip((6, 7, 2, 3, 4, 5, 0, 1), sent))
    if piggy:
        late_texts, sent[0] = lax.optimization_barrier((text_embed, sent[0]))
        halos_and_texts = [one_text_block(late_texts)]
    else:
        halos_and_texts = []
    got = traded(sent)

    length = HEADS * count
    halo = 0
    near_ids = segment_ids
    if parts > 1:
        halo = rounded_up(MAXP - 1, LANES)
        part = lax.axis_index("grp") // HEADS
        whole_ids = jnp.concatenate(
            [
                jnp.full((1, halo), -1, jnp.int32),
                segment_ids,
                jnp.full((1, halo), images, jnp.int32),
            ],
            axis=1,
        )
        near_ids = lax.dynamic_slice_in_dim(whole_ids, part * length, length + 2 * halo, axis=1)
        order = jnp.bitwise_xor(lax.axis_index("grp") % HEADS, jnp.arange(HEADS))
        flat = jnp.stack([got[by] for by in range(HEADS)])[order][:, : 2 * size].transpose(1, 0, 2).reshape(2 * size, length)
        flat = jnp.concatenate([flat, jnp.zeros((16, length), bf16)], axis=0)
        ahead = [(i, i + HEADS) for i in range(group_size - HEADS)]
        back = [(i + HEADS, i) for i in range(group_size - HEADS)]
        left = moved(flat[:, length - halo :], "grp", ahead)
        right = moved(flat[:, :halo], "grp", back)
        halos_and_texts += [left, right]
    reach = length + 2 * halo
    window = min(rounded_up(MAXP + LANES - 1, LANES), reach)
    tile = 2 * LANES
    early_keys, marks, before, weight = call(
        functools.partial(prepare_kernel, images, halo),
        (
            shape((len(EARLY) * count, LANES), bf16),
            shape((2, SPARE, reach), f32),
            shape((rounded_up(images + 1, SPARE), LANES), jnp.int32),
            shape((HEADS * padded, depth), bf16),
        ),
        [pltpu.SemaphoreType.DMA((HEADS,))],
        in_vmem(1) + [hbm] + in_vmem(len(EARLY)),
        1 << 30,
    )(near_ids, in_hbm(out_weight), *[got[by] for by in EARLY])
    operands = [near_ids, before, marks, early_keys, *[got[by] for by in EARLY + LATE], *halos_and_texts]
    answers = call(
        functools.partial(attend_kernel, images, piggy, halo),
        (shape((padded + TEXT_ROWS * piggy, count), bf16),) * HEADS,
        [
            pltpu.VMEM((reach, LANES), bf16),
            pltpu.VMEM((padded, reach), bf16),
            pltpu.VMEM((LANES, length), bf16),
            pltpu.VMEM((padded, length), f32),
        ]
        + [pltpu.VMEM((window, tile), f32), pltpu.VMEM((1, tile), f32)] * RUN
        + [pltpu.SMEM((images + 1,), jnp.int32)],
        in_vmem(len(operands)),
        4 * size * length * MAXP,
    )(*operands)
    home = traded(dict(zip(ORDER, answers)))
    home = [home[by] for by in ORDER]

    joined = [
        pltpu.VMEM((HEADS * padded, count), bf16),
        pltpu.VMEM((count, HEADS * padded), bf16),
        pltpu.VMEM((count, depth), bf16),
        pltpu.SemaphoreType.DMA((3,)),
    ]
    flops = 2 * count * depth * width
    if piggy:
        mixed, row_loss = call(
            functools.partial(finish_kernel, images),
            (shape((count, depth), bf16), shape((1, images), f32)),
            joined
            + [
                pltpu.VMEM((SPARE, HEADS * padded), f32),
                pltpu.VMEM((SPARE, depth), f32),
                pltpu.VMEM((HEADS, images, depth), f32),
                pltpu.VMEM((1, images), f32),
                pltpu.SemaphoreType.DMA,
            ],
            in_vmem(3 + HEADS),
            flops,
            (hbm, hbm),
        )(rows, weight, text_embed, *home)
        return (mixed[None], row_loss[0])
    mixed = call(mix_kernel, shape((count, depth), bf16), joined, in_vmem(2 + HEADS), flops, hbm)(
        rows, weight, *home
    )
    own_ids = lax.dynamic_slice_in_dim(segment_ids[0], lax.axis_index("grp") * count, count)
    onehot = (own_ids[None, :] == jnp.arange(images, dtype=jnp.int32)[:, None]).astype(bf16)
    pooled = lax.psum(jnp.dot(onehot, mixed, preferred_element_type=f32), "grp")
    text_vecs = unit_rows(all_texts(text_embed).astype(f32))
    cosine = jnp.dot(unit_rows(pooled), text_vecs.T, precision=lax.Precision.HIGHEST)
    same = jnp.arange(images)[:, None] == jnp.arange(text_vecs.shape[0])[None, :]
    row_loss = jnp.sum(losses(cosine, jnp.where(same, 1.0, -1.0)), axis=1)
    return (mixed[None], row_loss)


def solution(mesh):
    placed = (P("blk", "grp", None), P("blk", None), P(), P(), P("blk", None))
    return jax.shard_map(
        local,
        mesh=mesh,
        in_specs=placed,
        out_specs=(P("blk", "grp", None), P("blk")),
        check_vma=False,
    )
```

```python
import functools
import math

import jax
import jax.numpy as jnp
from jax import lax
from jax.experimental import pallas as pl
from jax.experimental.pallas import tpu as pltpu
from jax.sharding import PartitionSpec as P

HEADS = 8
MAXP = 1024
LANES = 128
SPARE = 8
SIZE = 72
PADDED = SIZE + SPARE
KEY_AT = SIZE - SPARE
QUERY_AT = 2 * SIZE
TEXT_ROWS = 16
RUN = 8
HIDDEN = -1e30
ORDER = (6, 7, 2, 4, 3, 5, 1, 0)
EARLY = (6, 7, 1, 0)
LATE = (2, 4, 3, 5)

logit_scale = 30.0
logit_bias = -5.0

VMEM_LIMIT = 32 * 1024 * 1024


def rounded_up(value, step):
    return (value + step - 1) // step * step


def split_in_two(total, images):
    row = lax.broadcasted_iota(jnp.int32, total.shape, 0)
    main = total.astype(jnp.bfloat16).astype(jnp.float32)
    return jnp.where(row < images, main, total - main)


def image_rows(ids, images):
    row = lax.broadcasted_iota(jnp.int32, (SPARE, ids.shape[1]), 0)
    return (lax.rem(row, images) == ids).astype(jnp.float32).astype(jnp.bfloat16)


def head_blocks(query, key, value, sums, pair):
    size = query.shape[0] // 2
    count = query.shape[1]
    for place in range(2):
        here = slice(place * size, (place + 1) * size)
        if sums is None:
            spare = jnp.zeros((SPARE, count), jnp.float32)
        else:
            first = pl.multiple_of((2 * pair + place) * LANES, LANES)
            parts = [sums[:, pl.ds(first, LANES)], sums[:, HEADS * LANES :]]
            held = sum(part.shape[1] for part in parts)
            spare = jnp.concatenate(parts + [jnp.zeros((SPARE, count - held), jnp.float32)], axis=1)
        yield jnp.concatenate([value[here], key[here], spare, query[here]], axis=0)


def store_by_core(core, blocks, same_ref, cross_ref):
    first, second = blocks
    same_ref[...] = jnp.where(core == 0, first, second).astype(jnp.bfloat16)
    cross_ref[...] = jnp.where(core == 0, second, first).astype(jnp.bfloat16)


def place_in_group():
    own = lax.rem(lax.axis_index("grp"), HEADS)
    return lax.div(own, 2), lax.rem(own, 2)


def far_kernel(images, piggy, ids_ref, rows_ref, weight_ref, normed_ref, sums_ref, same_ref, cross_ref, own_ids, rows_held, weight, id_sem, row_sem, sems):
    count, depth = rows_ref.shape
    width = weight_ref.shape[0] // 3
    wide = weight.shape[1]
    rows_fetch = pltpu.make_async_copy(rows_ref, rows_held, row_sem)
    rows_fetch.start()
    own = pl.multiple_of(lax.axis_index("grp") * count, LANES)
    ids_fetch = pltpu.make_async_copy(ids_ref.at[:, pl.ds(own, count)], own_ids, id_sem)
    ids_fetch.start()
    pair, core = place_in_group()
    pair = jnp.bitwise_xor(pair, 3)
    fetches = []
    for at in range(3):
        first = pl.multiple_of(at * width + pair * wide, 16)
        fetches.append(pltpu.make_async_copy(weight_ref.at[pl.ds(first, wide)], weight.at[at], sems.at[at]))
    for fetch in fetches:
        fetch.start()
    ids_fetch.wait()
    rows_fetch.wait()
    rows = rows_held[...]
    if piggy:
        sums = jnp.dot(image_rows(own_ids[...], images), rows, preferred_element_type=jnp.float32)
        sums_ref[...] = split_in_two(sums, images)
    values = rows.astype(jnp.float32)
    center = values - jnp.mean(values, axis=1, keepdims=True)
    spread = jnp.mean(center * center, axis=1, keepdims=True)
    normed = (center * lax.rsqrt(spread + 1e-06)).astype(jnp.bfloat16)
    normed_ref[...] = normed.T
    for fetch in fetches:
        fetch.wait()
    parts = [
        jnp.dot(weight[at], normed_ref[...], preferred_element_type=jnp.float32) for at in range(3)
    ]
    store_by_core(core, head_blocks(*parts, sums_ref if piggy else None, pair), same_ref, cross_ref)


def near_kernel(piggy, normed_ref, sums_ref, weight_ref, *out_refs):
    width = weight_ref.shape[0] // 3
    wide = 2 * width // HEADS
    own, core = place_in_group()
    for step, move in enumerate((1, 2, 0)):
        pair = jnp.bitwise_xor(own, move)
        parts = []
        for at in range(3):
            here = pl.ds(pl.multiple_of(at * width + pair * wide, 16), wide)
            parts.append(
                jnp.dot(weight_ref[here, :], normed_ref[...], preferred_element_type=jnp.float32)
            )
        blocks = head_blocks(*parts, sums_ref if piggy else None, pair)
        store_by_core(core, blocks, *out_refs[2 * step : 2 * step + 2])


def count_before(images, ids):
    image = lax.broadcasted_iota(jnp.int32, (rounded_up(images + 1, SPARE), ids.shape[1]), 0)
    before = jnp.sum((ids < image).astype(jnp.int32), axis=1, keepdims=True)
    return jnp.broadcast_to(before, (before.shape[0], LANES))


def write_marks(images, ids, marks):
    bits = max(1, (images - 1).bit_length())
    row = lax.broadcasted_iota(jnp.int32, (SPARE, ids.shape[1]), 0)
    bit = jnp.bitwise_and(lax.shift_right_logical(jnp.broadcast_to(ids, row.shape), row >> 1), 1)
    odd = jnp.bitwise_and(row, 1)
    used = row < 2 * bits
    outside = jnp.logical_or(ids < 0, ids >= images)
    key_side = jnp.where(odd == 1, bit, 1 - bit).astype(jnp.float32)
    key_side = jnp.where(outside, 1.0, key_side)
    marks[0] = jnp.where(used, key_side * HIDDEN, 0.0)
    marks[1] = jnp.where(used, jnp.where(odd == 1, 1 - bit, bit), 0).astype(jnp.float32)


def spare_sums(refs):
    parts = [ref[QUERY_AT : QUERY_AT + 16].astype(jnp.float32)[0:SPARE, 0 : 2 * LANES] for ref in refs]
    return sum(parts[1:], parts[0])


def image_at(images, starts, position):
    found = jnp.int32(0)
    for image in range(1, images):
        found += (starts[image] <= position).astype(jnp.int32)
    return found


def attend_images(images, ids_ref, keys, values, queries, attended, work, starts, halo):
    work = list(zip(work[0::2], work[1::2]))
    query_base = halo
    window, tile = work[0][0].shape
    size = attended.shape[0] - SPARE
    held = queries.shape[1]
    tiles = held // tile

    low = image_at(images, starts, query_base)
    high = image_at(images, starts, query_base + held - 1)

    def bounds(image):
        first = lax.div(jnp.maximum(starts[image] - query_base, 0), tile)
        last = lax.div(jnp.minimum(starts[image + 1] - query_base, held) - 1, tile)
        return jnp.minimum(first, tiles - 1), last

    def following(state):
        at, image = state
        more = at < bounds(image)[1]
        later = jnp.minimum(image + 1, high)
        first = jnp.where(image == high, at, bounds(later)[0])
        return jnp.where(more, at + 1, first), jnp.where(more, image, later)

    def window_of(image):
        begin = lax.div(starts[image], LANES) * LANES
        return pl.ds(pl.multiple_of(jnp.minimum(begin, keys.shape[0] - window), LANES), window)

    def score(state, scores, tops):
        at, image = state
        query = queries[:, pl.ds(pl.multiple_of(at * tile, tile), tile)]
        found = jnp.dot(keys[window_of(image), :], query, preferred_element_type=jnp.float32)
        scores[...] = found
        tops[...] = jnp.max(found, axis=0, keepdims=True)

    def weigh(state, scores, tops):
        at, image = state
        first = pl.multiple_of(at * tile, tile)
        labels = ids_ref[:, pl.ds(pl.multiple_of(query_base + first, LANES), tile)]
        probs = jnp.exp2((scores[...] - tops[...]) * (size ** (-0.5) * math.log2(math.e)))
        share = 1.0 / jnp.sum(probs, axis=0, keepdims=True)
        weighted = jnp.dot(
            values[:, window_of(image)], probs.astype(jnp.bfloat16), preferred_element_type=jnp.float32
        )
        place = (slice(None), pl.ds(first, tile))
        attended[place] = jnp.where(labels == image, weighted * share, attended[place])

    pairs = jnp.int32(0)
    for image in range(images):
        first, last = bounds(image)
        wanted = jnp.logical_and(low <= image, image <= high)
        pairs += jnp.where(wanted, last - first + 1, 0)

    def run(_, state):
        for step in range(RUN):
            later = following(state)
            score(later, *work[(step + 1) % 2])
            weigh(state, *work[step % 2])
            state = later
        return state

    begun = (jnp.int32(0), low)
    score(begun, *work[0])
    lax.fori_loop(0, lax.div(pairs + RUN - 1, RUN), run, begun)


def turned_keys(marked, block_ref):
    block = block_ref[KEY_AT : KEY_AT + PADDED].astype(jnp.float32)
    nothing = jnp.zeros((LANES - PADDED, block.shape[1]), jnp.float32)
    full = jnp.concatenate([marked, block[SPARE:], nothing], axis=0)
    return full.astype(jnp.bfloat16).T


def store_queries(marked, block_ref, queries, there):
    edge = block_ref[QUERY_AT : QUERY_AT + 16].astype(jnp.float32)
    edge = jnp.concatenate([marked, edge[SPARE:]], axis=0)
    queries[0:16, there] = edge.astype(jnp.bfloat16)
    queries[16:PADDED, there] = block_ref[QUERY_AT + 16 : QUERY_AT + PADDED]
    queries[PADDED:, there] = jnp.zeros((LANES - PADDED, block_ref.shape[1]), jnp.bfloat16)


def prepare_kernel(images, halo, ids_ref, out_weight_ref, *rest):
    got_refs, (keys, marks, before, weight, sems) = rest[: len(EARLY)], rest[len(EARLY) :]
    count = got_refs[0].shape[1]
    fetches = []
    for step, by in enumerate(ORDER):
        head = jnp.bitwise_xor(lax.rem(lax.axis_index("grp"), HEADS), by)
        first = lax.div(head, 2) * (2 * SIZE) + lax.rem(head, 2) * (SIZE - SPARE)
        fetches.append(
            pltpu.make_async_copy(
                out_weight_ref.at[pl.ds(pl.multiple_of(first, 16), PADDED)],
                weight.at[step * PADDED : (step + 1) * PADDED],
                sems.at[step],
            )
        )
        fetches[-1].start()
    before[...] = count_before(images, ids_ref[...])
    write_marks(images, ids_ref[...], marks)
    own = lax.rem(lax.axis_index("grp"), HEADS)
    for step, (by, ref) in enumerate(zip(EARLY, got_refs)):
        first = jnp.bitwise_xor(own, by) * count
        here = pl.ds(pl.multiple_of(halo + first, LANES), count)
        keys[step * count : (step + 1) * count, :] = turned_keys(marks[0, :, here], ref)
    for fetch in fetches:
        fetch.wait()


def attend_kernel(images, piggy, halo, ids_ref, before_ref, marks, early_keys, *rest):
    got_refs, rest = rest[:HEADS], rest[HEADS:]
    if piggy:
        text_ref, *rest = rest
    if halo:
        left_ref, right_ref, *rest = rest
    out_refs, rest = rest[:HEADS], rest[HEADS:]
    keys, values, queries, attended, *work, starts = rest
    count = got_refs[0].shape[1]
    padded = attended.shape[0]
    size = padded - SPARE
    total_rows = HEADS * count
    length = ids_ref.shape[1]
    ids = ids_ref[...]
    before = before_ref[...]
    for image in range(images + 1):
        starts[image] = before[image, 0]

    own = lax.rem(lax.axis_index("grp"), HEADS)
    for step, (by, ref) in enumerate(zip(EARLY + LATE, got_refs)):
        first = jnp.bitwise_xor(own, by) * count
        here = pl.ds(pl.multiple_of(halo + first, LANES), count)
        there = pl.ds(pl.multiple_of(first, LANES), count)
        if by in EARLY:
            keys[here, :] = early_keys[step * count : (step + 1) * count, :]
        else:
            keys[here, :] = turned_keys(marks[0, :, here], ref)
        values[:, here] = ref[0:PADDED]
        store_queries(marks[1, :, here], ref, queries, there)
    if halo:
        for ref, here in ((left_ref, slice(0, halo)), (right_ref, slice(length - halo, length))):
            keys[here, :] = turned_keys(marks[0, :, here], ref)
            values[:, here] = ref[0:PADDED]
    attend_images(images, ids_ref, keys, values, queries, attended, work, starts, halo)

    odd_head = lax.rem(own, 2) == 1
    mine = ids[:, halo : halo + total_rows]

    def placed(block, spare):
        even = jnp.concatenate([block[0:size], spare], axis=0)
        odd = jnp.concatenate([spare, block[0:size]], axis=0)
        return jnp.where(odd_head, odd, even)

    if piggy:
        nothing = jnp.zeros((SPARE, total_rows), jnp.float32)
        flat = placed(attended[...], nothing).astype(jnp.bfloat16)
        pooled = lax.dot_general(
            image_rows(mine, images), flat, (((1,), (1,)), ((), ())), preferred_element_type=jnp.float32
        )
        pooled = split_in_two(pooled, images)
        sums = spare_sums(got_refs)
        sums = split_in_two(sums + pltpu.roll(sums, images, axis=0), images)
        spare = jnp.concatenate(
            [pooled, jnp.zeros((SPARE, LANES - padded), jnp.float32), sums], axis=1
        )
        texts = text_ref[...].astype(jnp.float32)
        parts = [texts[:, at : at + count] for at in range(0, texts.shape[1], count)]
        unused = TEXT_ROWS - images * len(parts)
        below = jnp.concatenate(parts + [jnp.zeros((unused, count), jnp.float32)] * (unused > 0), axis=0)
        below = below.astype(jnp.bfloat16)
    else:
        spare = jnp.zeros((SPARE, count), jnp.float32)
    for by, out_ref in zip(ORDER, out_refs):
        there = pl.multiple_of(jnp.bitwise_xor(own, by) * count, LANES)
        out_ref[0:padded] = placed(attended[:, pl.ds(there, count)], spare).astype(jnp.bfloat16)
        if piggy:
            out_ref[padded:] = below


def joined_heads(got_refs, flat):
    own = lax.rem(lax.axis_index("grp"), HEADS)
    spares = []
    for step, (by, got_ref) in enumerate(zip(ORDER, got_refs)):
        odd = lax.rem(jnp.bitwise_xor(own, by), 2)
        at = step * PADDED
        top = got_ref[0:16].astype(jnp.float32)
        bottom = got_ref[PADDED - 16 : PADDED].astype(jnp.float32)
        spares.append(jnp.where(odd == 1, top[:SPARE], bottom[SPARE:]))
        top = jnp.concatenate([jnp.where(odd == 1, 0.0, top[:SPARE]), top[SPARE:]], axis=0)
        bottom = jnp.concatenate([bottom[:SPARE], jnp.where(odd == 1, bottom[SPARE:], 0.0)], axis=0)
        flat[at : at + 16] = top.astype(jnp.bfloat16)
        flat[at + 16 : at + PADDED - 16] = got_ref[16 : PADDED - 16]
        flat[at + PADDED - 16 : at + PADDED] = bottom.astype(jnp.bfloat16)
    return spares


def send_mixed_rows(rows_ref, weight_ref, flat, turned, mixed, mixed_ref, sems, meanwhile=None):
    turned[...] = flat[...].T
    pieces = sems.shape[0]
    step = rows_ref.shape[0] // pieces
    copies, value = [], None
    for piece in range(pieces):
        cut = slice(piece * step, (piece + 1) * step)
        if meanwhile is not None:
            value = meanwhile[piece](value)
        added = jnp.dot(turned[cut, :], weight_ref[...], preferred_element_type=jnp.float32)
        mixed[cut, :] = (rows_ref[cut, :].astype(jnp.float32) + added).astype(jnp.bfloat16)
        copies.append(pltpu.make_async_copy(mixed.at[cut], mixed_ref.at[cut], sems.at[piece]))
        copies[-1].start()
    return copies


def unit_rows(matrix):
    return matrix * lax.rsqrt(jnp.sum(matrix * matrix, axis=1, keepdims=True) + 1e-06)


def losses(cosine, labels):
    logits = -labels * (logit_scale * cosine + logit_bias)
    return jnp.maximum(logits, 0.0) + jnp.log1p(jnp.exp(-jnp.abs(logits)))


def finish_kernel(images, rows_ref, weight_ref, text_ref, *rest):
    got_refs, rest = rest[:HEADS], rest[HEADS:]
    mixed_ref, loss_ref, flat, turned, mixed, sems, pooled_heads, patch_sums, far_texts, loss, loss_sem = rest
    spares = joined_heads(got_refs, flat)
    own = lax.rem(lax.axis_index("grp"), HEADS)
    patch_sums[:, HEADS * LANES :] = spares[0][:, 2 * LANES :]
    for step, (by, spare) in enumerate(zip(ORDER, spares)):
        pooled_heads[:, step * PADDED : (step + 1) * PADDED] = spare[:, 0:PADDED]
        head = jnp.bitwise_xor(own, by)
        patch_sums[:, pl.ds(pl.multiple_of(head * LANES, LANES), LANES)] = spare[:, LANES : 2 * LANES]
        below = got_refs[step][PADDED:].astype(jnp.float32)
        count = below.shape[1]
        for part in range(patch_sums.shape[1] // count):
            here = slice(part * count, (part + 1) * count)
            far_texts[head, :, here] = below[part * images : (part + 1) * images]

    def find_images(_):
        pooled = jnp.dot(
            pooled_heads[...].astype(jnp.bfloat16), weight_ref[...], preferred_element_type=jnp.float32
        )
        pooled = pooled + patch_sums[...]
        others = [far_texts[place] for place in range(lax.axis_size("blk") - 1)]
        texts = jnp.concatenate([text_ref[...].astype(jnp.float32)] + others, axis=0)
        return pooled + pltpu.roll(pooled, images, axis=0), unit_rows(texts)

    def find_cosines(vectors):
        pooled, text_vecs = vectors
        return lax.dot_general(
            text_vecs,
            unit_rows(pooled),
            (((1,), (1,)), ((), ())),
            precision=lax.Precision.HIGHEST,
            preferred_element_type=jnp.float32,
        )

    def find_losses(cosine):
        text = lax.broadcasted_iota(jnp.int32, cosine.shape, 0)
        image = lax.broadcasted_iota(jnp.int32, cosine.shape, 1)
        terms = losses(cosine, jnp.where(text == image, 1.0, -1.0))
        loss[...] = jnp.sum(terms, axis=0, keepdims=True)[:, 0:images]
        loss_copy.start()

    loss_copy = pltpu.make_async_copy(loss, loss_ref, loss_sem)
    meanwhile = (find_images, find_cosines, find_losses)
    copies = send_mixed_rows(rows_ref, weight_ref, flat, turned, mixed, mixed_ref, sems, meanwhile)
    for copy in copies + [loss_copy]:
        copy.wait()


def mix_kernel(rows_ref, weight_ref, *rest):
    got_refs, rest = rest[:HEADS], rest[HEADS:]
    mixed_ref, flat, turned, mixed, sems = rest
    joined_heads(got_refs, flat)
    for copy in send_mixed_rows(rows_ref, weight_ref, flat, turned, mixed, mixed_ref, sems):
        copy.wait()


def in_vmem(count):
    return [pl.BlockSpec(memory_space=pltpu.VMEM)] * count


def in_hbm(value):
    return pltpu.with_memory_space_constraint(value, pltpu.HBM)


def call(kernel, out_shape, scratch, in_specs, flops, out_specs=None):
    if out_specs is None:
        out_specs = jax.tree.map(lambda _: pl.BlockSpec(memory_space=pltpu.VMEM), out_shape)
    return pl.pallas_call(
        kernel,
        out_shape=out_shape,
        in_specs=in_specs,
        out_specs=out_specs,
        scratch_shapes=scratch,
        compiler_params=pltpu.CompilerParams(vmem_limit_bytes=VMEM_LIMIT),
        cost_estimate=pl.CostEstimate(flops=flops, bytes_accessed=8 << 20, transcendentals=0),
    )


def moved(value, axis, pairs):
    return lax.ppermute(value, axis, pairs)


def partner(place, by, peers):
    return place ^ by if peers & (peers - 1) == 0 else (place + by) % peers


def all_texts(texts):
    peers = lax.axis_size("blk")
    steps = [[(partner(i, by, peers), i) for i in range(peers)] for by in range(1, peers)]
    return jnp.concatenate([texts] + [moved(texts, "blk", pairs) for pairs in steps], axis=0)


def one_text_block(texts):
    peers = lax.axis_size("blk")
    pairs = []
    for place in range(lax.axis_size("grp")):
        by = place % (peers - 1) + 1
        pairs += [(place * peers + partner(i, by, peers), place * peers + i) for i in range(peers)]
    return moved(texts, ("grp", "blk"), pairs)


def traded(blocks):
    peers = range(lax.axis_size("grp"))
    trades = {by: moved(blocks[by], "grp", [(i, i ^ by) for i in peers]) for by in ORDER if by}
    return {**trades, 0: blocks[0]}


def local(patches, segment_ids, qkv_weight, out_weight, text_embed):
    rows = patches[0]
    count, depth = rows.shape
    width = out_weight.shape[0]
    size = width // HEADS
    padded = size + SPARE
    images = text_embed.shape[0]
    group_size = lax.axis_size("grp")
    parts = group_size // HEADS
    piggy = (
        parts == 1
        and 2 * images == SPARE
        and count >= depth - (HEADS - 2) * LANES
        and depth % count == 0
        and images * (depth // count) <= TEXT_ROWS
        and 1 < lax.axis_size("blk") <= HEADS + 1
    )
    bf16, f32 = jnp.bfloat16, jnp.float32
    shape = jax.ShapeDtypeStruct

    block = shape((3 * size + SPARE, count), bf16)
    hbm = pl.BlockSpec(memory_space=pltpu.HBM)
    turned_weight = qkv_weight.T
    normed, sums, *sent = call(
        functools.partial(far_kernel, images, piggy),
        (shape((depth, count), bf16), shape((SPARE, depth), f32), block, block),
        [
            pltpu.VMEM((1, count), jnp.int32),
            pltpu.VMEM((count, depth), bf16),
            pltpu.VMEM((3, 2 * size, depth), bf16),
            pltpu.SemaphoreType.DMA,
            pltpu.SemaphoreType.DMA,
            pltpu.SemaphoreType.DMA((3,)),
        ],
        [hbm] * 3,
        2 * count * depth * 6 * size,
    )(in_hbm(segment_ids), in_hbm(rows), in_hbm(turned_weight))
    sent += call(
        functools.partial(near_kernel, piggy),
        (block,) * 6,
        [],
        in_vmem(3),
        2 * count * depth * 18 * size,
    )(normed, sums, turned_weight)
    sent = dict(zip((6, 7, 2, 3, 4, 5, 0, 1), sent))
    if piggy:
        late_texts, sent[0] = lax.optimization_barrier((text_embed, sent[0]))
        halos_and_texts = [one_text_block(late_texts)]
    else:
        halos_and_texts = []
    got = traded(sent)

    length = HEADS * count
    halo = 0
    near_ids = segment_ids
    if parts > 1:
        halo = rounded_up(MAXP - 1, LANES)
        part = lax.axis_index("grp") // HEADS
        whole_ids = jnp.concatenate(
            [
                jnp.full((1, halo), -1, jnp.int32),
                segment_ids,
                jnp.full((1, halo), images, jnp.int32),
            ],
            axis=1,
        )
        near_ids = lax.dynamic_slice_in_dim(whole_ids, part * length, length + 2 * halo, axis=1)
        order = jnp.bitwise_xor(lax.axis_index("grp") % HEADS, jnp.arange(HEADS))
        flat = jnp.stack([got[by] for by in range(HEADS)])[order][:, : 2 * size].transpose(1, 0, 2).reshape(2 * size, length)
        flat = jnp.concatenate([flat, jnp.zeros((16, length), bf16)], axis=0)
        ahead = [(i, i + HEADS) for i in range(group_size - HEADS)]
        back = [(i + HEADS, i) for i in range(group_size - HEADS)]
        left = moved(flat[:, length - halo :], "grp", ahead)
        right = moved(flat[:, :halo], "grp", back)
        halos_and_texts += [left, right]
    reach = length + 2 * halo
    window = min(rounded_up(MAXP + LANES - 1, LANES), reach)
    tile = 2 * LANES
    early_keys, marks, before, weight = call(
        functools.partial(prepare_kernel, images, halo),
        (
            shape((len(EARLY) * count, LANES), bf16),
            shape((2, SPARE, reach), f32),
            shape((rounded_up(images + 1, SPARE), LANES), jnp.int32),
            shape((HEADS * padded, depth), bf16),
        ),
        [pltpu.SemaphoreType.DMA((HEADS,))],
        in_vmem(1) + [hbm] + in_vmem(len(EARLY)),
        1 << 30,
    )(near_ids, in_hbm(out_weight), *[got[by] for by in EARLY])
    operands = [near_ids, before, marks, early_keys, *[got[by] for by in EARLY + LATE], *halos_and_texts]
    answers = call(
        functools.partial(attend_kernel, images, piggy, halo),
        (shape((padded + TEXT_ROWS * piggy, count), bf16),) * HEADS,
        [
            pltpu.VMEM((reach, LANES), bf16),
            pltpu.VMEM((padded, reach), bf16),
            pltpu.VMEM((LANES, length), bf16),
            pltpu.VMEM((padded, length), f32),
        ]
        + [pltpu.VMEM((window, tile), f32), pltpu.VMEM((1, tile), f32)] * 2
        + [pltpu.SMEM((images + 1,), jnp.int32)],
        in_vmem(len(operands)),
        4 * size * length * MAXP,
    )(*operands)
    home = traded(dict(zip(ORDER, answers)))
    home = [home[by] for by in ORDER]

    joined = [
        pltpu.VMEM((HEADS * padded, count), bf16),
        pltpu.VMEM((count, HEADS * padded), bf16),
        pltpu.VMEM((count, depth), bf16),
        pltpu.SemaphoreType.DMA((3,)),
    ]
    flops = 2 * count * depth * width
    if piggy:
        mixed, row_loss = call(
            functools.partial(finish_kernel, images),
            (shape((count, depth), bf16), shape((1, images), f32)),
            joined
            + [
                pltpu.VMEM((SPARE, HEADS * padded), f32),
                pltpu.VMEM((SPARE, depth), f32),
                pltpu.VMEM((HEADS, images, depth), f32),
                pltpu.VMEM((1, images), f32),
                pltpu.SemaphoreType.DMA,
            ],
            in_vmem(3 + HEADS),
            flops,
            (hbm, hbm),
        )(rows, weight, text_embed, *home)
        return (mixed[None], row_loss[0])
    mixed = call(mix_kernel, shape((count, depth), bf16), joined, in_vmem(2 + HEADS), flops, hbm)(
        rows, weight, *home
    )
    own_ids = lax.dynamic_slice_in_dim(segment_ids[0], lax.axis_index("grp") * count, count)
    onehot = (own_ids[None, :] == jnp.arange(images, dtype=jnp.int32)[:, None]).astype(bf16)
    pooled = lax.psum(jnp.dot(onehot, mixed, preferred_element_type=f32), "grp")
    text_vecs = unit_rows(all_texts(text_embed).astype(f32))
    cosine = jnp.dot(unit_rows(pooled), text_vecs.T, precision=lax.Precision.HIGHEST)
    same = jnp.arange(images)[:, None] == jnp.arange(text_vecs.shape[0])[None, :]
    row_loss = jnp.sum(losses(cosine, jnp.where(same, 1.0, -1.0)), axis=1)
    return (mixed[None], row_loss)


def solution(mesh):
    placed = (P("blk", "grp", None), P("blk", None), P(), P(), P("blk", None))
    return jax.shard_map(
        local,
        mesh=mesh,
        in_specs=placed,
        out_specs=(P("blk", "grp", None), P("blk")),
        check_vma=False,
    )
```

```python
import functools
import math

import jax
import jax.numpy as jnp
from jax import lax
from jax.experimental import pallas as pl
from jax.experimental.pallas import tpu as pltpu
from jax.sharding import PartitionSpec as P

HEADS = 8
MAXP = 1024
LANES = 128
SPARE = 8
SIZE = 72
PADDED = SIZE + SPARE
KEY_AT = SIZE - SPARE
QUERY_AT = 2 * SIZE
TEXT_ROWS = 16
RUN = 4
HIDDEN = -1e30
ORDER = (6, 7, 2, 4, 3, 5, 1, 0)
EARLY = (6, 7, 1, 0)
LATE = (2, 4, 3, 5)

logit_scale = 30.0
logit_bias = -5.0

VMEM_LIMIT = 32 * 1024 * 1024


def rounded_up(value, step):
    return (value + step - 1) // step * step


def split_in_two(total, images):
    row = lax.broadcasted_iota(jnp.int32, total.shape, 0)
    main = total.astype(jnp.bfloat16).astype(jnp.float32)
    return jnp.where(row < images, main, total - main)


def image_rows(ids, images):
    row = lax.broadcasted_iota(jnp.int32, (SPARE, ids.shape[1]), 0)
    return (lax.rem(row, images) == ids).astype(jnp.float32).astype(jnp.bfloat16)


def head_blocks(query, key, value, sums, pair):
    size = query.shape[0] // 2
    count = query.shape[1]
    for place in range(2):
        here = slice(place * size, (place + 1) * size)
        if sums is None:
            spare = jnp.zeros((SPARE, count), jnp.float32)
        else:
            first = pl.multiple_of((2 * pair + place) * LANES, LANES)
            parts = [sums[:, pl.ds(first, LANES)], sums[:, HEADS * LANES :]]
            held = sum(part.shape[1] for part in parts)
            spare = jnp.concatenate(parts + [jnp.zeros((SPARE, count - held), jnp.float32)], axis=1)
        yield jnp.concatenate([value[here], key[here], spare, query[here]], axis=0)


def store_by_core(core, blocks, same_ref, cross_ref):
    first, second = blocks
    same_ref[...] = jnp.where(core == 0, first, second).astype(jnp.bfloat16)
    cross_ref[...] = jnp.where(core == 0, second, first).astype(jnp.bfloat16)


def place_in_group():
    own = lax.rem(lax.axis_index("grp"), HEADS)
    return lax.div(own, 2), lax.rem(own, 2)


def far_kernel(images, piggy, ids_ref, rows_ref, weight_ref, normed_ref, sums_ref, same_ref, cross_ref, own_ids, rows_held, weight, id_sem, row_sem, sems):
    count, depth = rows_ref.shape
    width = weight_ref.shape[0] // 3
    wide = weight.shape[1]
    rows_fetch = pltpu.make_async_copy(rows_ref, rows_held, row_sem)
    rows_fetch.start()
    own = pl.multiple_of(lax.axis_index("grp") * count, LANES)
    ids_fetch = pltpu.make_async_copy(ids_ref.at[:, pl.ds(own, count)], own_ids, id_sem)
    ids_fetch.start()
    pair, core = place_in_group()
    pair = jnp.bitwise_xor(pair, 3)
    fetches = []
    for at in range(3):
        first = pl.multiple_of(at * width + pair * wide, 16)
        fetches.append(pltpu.make_async_copy(weight_ref.at[pl.ds(first, wide)], weight.at[at], sems.at[at]))
    for fetch in fetches:
        fetch.start()
    ids_fetch.wait()
    rows_fetch.wait()
    rows = rows_held[...]
    if piggy:
        sums = jnp.dot(image_rows(own_ids[...], images), rows, preferred_element_type=jnp.float32)
        sums_ref[...] = split_in_two(sums, images)
    values = rows.astype(jnp.float32)
    center = values - jnp.mean(values, axis=1, keepdims=True)
    spread = jnp.mean(center * center, axis=1, keepdims=True)
    normed = (center * lax.rsqrt(spread + 1e-06)).astype(jnp.bfloat16)
    normed_ref[...] = normed.T
    for fetch in fetches:
        fetch.wait()
    parts = [
        jnp.dot(weight[at], normed_ref[...], preferred_element_type=jnp.float32) for at in range(3)
    ]
    store_by_core(core, head_blocks(*parts, sums_ref if piggy else None, pair), same_ref, cross_ref)


def near_kernel(piggy, normed_ref, sums_ref, weight_ref, *out_refs):
    width = weight_ref.shape[0] // 3
    wide = 2 * width // HEADS
    own, core = place_in_group()
    for step, move in enumerate((1, 2, 0)):
        pair = jnp.bitwise_xor(own, move)
        parts = []
        for at in range(3):
            here = pl.ds(pl.multiple_of(at * width + pair * wide, 16), wide)
            parts.append(
                jnp.dot(weight_ref[here, :], normed_ref[...], preferred_element_type=jnp.float32)
            )
        blocks = head_blocks(*parts, sums_ref if piggy else None, pair)
        store_by_core(core, blocks, *out_refs[2 * step : 2 * step + 2])


def count_before(images, ids):
    image = lax.broadcasted_iota(jnp.int32, (rounded_up(images + 1, SPARE), ids.shape[1]), 0)
    before = jnp.sum((ids < image).astype(jnp.int32), axis=1, keepdims=True)
    return jnp.broadcast_to(before, (before.shape[0], LANES))


def write_marks(images, ids, marks):
    bits = max(1, (images - 1).bit_length())
    row = lax.broadcasted_iota(jnp.int32, (SPARE, ids.shape[1]), 0)
    bit = jnp.bitwise_and(lax.shift_right_logical(jnp.broadcast_to(ids, row.shape), row >> 1), 1)
    odd = jnp.bitwise_and(row, 1)
    used = row < 2 * bits
    outside = jnp.logical_or(ids < 0, ids >= images)
    key_side = jnp.where(odd == 1, bit, 1 - bit).astype(jnp.float32)
    key_side = jnp.where(outside, 1.0, key_side)
    marks[0] = jnp.where(used, key_side * HIDDEN, 0.0)
    marks[1] = jnp.where(used, jnp.where(odd == 1, 1 - bit, bit), 0).astype(jnp.float32)


def spare_sums(refs):
    parts = [ref[QUERY_AT : QUERY_AT + 16].astype(jnp.float32)[0:SPARE, 0 : 2 * LANES] for ref in refs]
    return sum(parts[1:], parts[0])


def image_at(images, starts, position):
    found = jnp.int32(0)
    for image in range(1, images):
        found += (starts[image] <= position).astype(jnp.int32)
    return found


def attend_images(images, ids_ref, keys, values, queries, attended, work, starts, halo):
    work = list(zip(work[0::2], work[1::2]))
    query_base = halo
    window, tile = work[0][0].shape
    size = attended.shape[0] - SPARE
    held = queries.shape[1]
    tiles = held // tile

    low = image_at(images, starts, query_base)
    high = image_at(images, starts, query_base + held - 1)

    def bounds(image):
        first = lax.div(jnp.maximum(starts[image] - query_base, 0), tile)
        last = lax.div(jnp.minimum(starts[image + 1] - query_base, held) - 1, tile)
        return jnp.minimum(first, tiles - 1), last

    def following(state):
        at, image = state
        more = at < bounds(image)[1]
        later = jnp.minimum(image + 1, high)
        first = jnp.where(image == high, at, bounds(later)[0])
        return jnp.where(more, at + 1, first), jnp.where(more, image, later)

    def window_of(image):
        begin = lax.div(starts[image], LANES) * LANES
        return pl.ds(pl.multiple_of(jnp.minimum(begin, keys.shape[0] - window), LANES), window)

    def score(state, scores, tops):
        at, image = state
        query = queries[:, pl.ds(pl.multiple_of(at * tile, tile), tile)]
        found = jnp.dot(keys[window_of(image), :], query, preferred_element_type=jnp.float32)
        scores[...] = found
        tops[...] = jnp.max(found, axis=0, keepdims=True)

    def weigh(state, scores, tops):
        at, image = state
        first = pl.multiple_of(at * tile, tile)
        labels = ids_ref[:, pl.ds(pl.multiple_of(query_base + first, LANES), tile)]
        probs = jnp.exp2((scores[...] - tops[...]) * (size ** (-0.5) * math.log2(math.e)))
        share = 1.0 / jnp.sum(probs, axis=0, keepdims=True)
        weighted = jnp.dot(
            values[:, window_of(image)], probs.astype(jnp.bfloat16), preferred_element_type=jnp.float32
        )
        place = (slice(None), pl.ds(first, tile))
        attended[place] = jnp.where(labels == image, weighted * share, attended[place])

    pairs = jnp.int32(0)
    for image in range(images):
        first, last = bounds(image)
        wanted = jnp.logical_and(low <= image, image <= high)
        pairs += jnp.where(wanted, last - first + 1, 0)

    def run(_, state):
        for step in range(RUN):
            later = following(state)
            score(later, *work[(step + 1) % 2])
            weigh(state, *work[step % 2])
            state = later
        return state

    begun = (jnp.int32(0), low)
    score(begun, *work[0])
    lax.fori_loop(0, lax.div(pairs + RUN - 1, RUN), run, begun)


def turned_keys(marked, block_ref):
    block = block_ref[KEY_AT : KEY_AT + PADDED].astype(jnp.float32)
    nothing = jnp.zeros((LANES - PADDED, block.shape[1]), jnp.float32)
    full = jnp.concatenate([marked, block[SPARE:], nothing], axis=0)
    return full.astype(jnp.bfloat16).T


def store_queries(marked, block_ref, queries, there):
    edge = block_ref[QUERY_AT : QUERY_AT + 16].astype(jnp.float32)
    edge = jnp.concatenate([marked, edge[SPARE:]], axis=0)
    queries[0:16, there] = edge.astype(jnp.bfloat16)
    queries[16:PADDED, there] = block_ref[QUERY_AT + 16 : QUERY_AT + PADDED]
    queries[PADDED:, there] = jnp.zeros((LANES - PADDED, block_ref.shape[1]), jnp.bfloat16)


def prepare_kernel(images, halo, ids_ref, out_weight_ref, *rest):
    got_refs, (keys, marks, before, weight, sems) = rest[: len(EARLY)], rest[len(EARLY) :]
    count = got_refs[0].shape[1]
    fetches = []
    for step, by in enumerate(ORDER):
        head = jnp.bitwise_xor(lax.rem(lax.axis_index("grp"), HEADS), by)
        first = lax.div(head, 2) * (2 * SIZE) + lax.rem(head, 2) * (SIZE - SPARE)
        fetches.append(
            pltpu.make_async_copy(
                out_weight_ref.at[pl.ds(pl.multiple_of(first, 16), PADDED)],
                weight.at[step * PADDED : (step + 1) * PADDED],
                sems.at[step],
            )
        )
        fetches[-1].start()
    before[...] = count_before(images, ids_ref[...])
    write_marks(images, ids_ref[...], marks)
    own = lax.rem(lax.axis_index("grp"), HEADS)
    for step, (by, ref) in enumerate(zip(EARLY, got_refs)):
        first = jnp.bitwise_xor(own, by) * count
        here = pl.ds(pl.multiple_of(halo + first, LANES), count)
        keys[step * count : (step + 1) * count, :] = turned_keys(marks[0, :, here], ref)
    for fetch in fetches:
        fetch.wait()


def attend_kernel(images, piggy, halo, ids_ref, before_ref, marks, early_keys, *rest):
    got_refs, rest = rest[:HEADS], rest[HEADS:]
    if piggy:
        text_ref, *rest = rest
    if halo:
        left_ref, right_ref, *rest = rest
    out_refs, rest = rest[:HEADS], rest[HEADS:]
    keys, values, queries, attended, *work, starts = rest
    count = got_refs[0].shape[1]
    padded = attended.shape[0]
    size = padded - SPARE
    total_rows = HEADS * count
    length = ids_ref.shape[1]
    ids = ids_ref[...]
    before = before_ref[...]
    for image in range(images + 1):
        starts[image] = before[image, 0]

    own = lax.rem(lax.axis_index("grp"), HEADS)
    for step, (by, ref) in enumerate(zip(EARLY + LATE, got_refs)):
        first = jnp.bitwise_xor(own, by) * count
        here = pl.ds(pl.multiple_of(halo + first, LANES), count)
        there = pl.ds(pl.multiple_of(first, LANES), count)
        if by in EARLY:
            keys[here, :] = early_keys[step * count : (step + 1) * count, :]
        else:
            keys[here, :] = turned_keys(marks[0, :, here], ref)
        values[:, here] = ref[0:PADDED]
        store_queries(marks[1, :, here], ref, queries, there)
    if halo:
        for ref, here in ((left_ref, slice(0, halo)), (right_ref, slice(length - halo, length))):
            keys[here, :] = turned_keys(marks[0, :, here], ref)
            values[:, here] = ref[0:PADDED]
    attend_images(images, ids_ref, keys, values, queries, attended, work, starts, halo)

    odd_head = lax.rem(own, 2) == 1
    mine = ids[:, halo : halo + total_rows]

    def placed(block, spare):
        even = jnp.concatenate([block[0:size], spare], axis=0)
        odd = jnp.concatenate([spare, block[0:size]], axis=0)
        return jnp.where(odd_head, odd, even)

    if piggy:
        nothing = jnp.zeros((SPARE, total_rows), jnp.float32)
        flat = placed(attended[...], nothing).astype(jnp.bfloat16)
        pooled = lax.dot_general(
            image_rows(mine, images), flat, (((1,), (1,)), ((), ())), preferred_element_type=jnp.float32
        )
        pooled = split_in_two(pooled, images)
        sums = spare_sums(got_refs)
        sums = split_in_two(sums + pltpu.roll(sums, images, axis=0), images)
        spare = jnp.concatenate(
            [pooled, jnp.zeros((SPARE, LANES - padded), jnp.float32), sums], axis=1
        )
        texts = text_ref[...].astype(jnp.float32)
        parts = [texts[:, at : at + count] for at in range(0, texts.shape[1], count)]
        unused = TEXT_ROWS - images * len(parts)
        below = jnp.concatenate(parts + [jnp.zeros((unused, count), jnp.float32)] * (unused > 0), axis=0)
        below = below.astype(jnp.bfloat16)
    else:
        spare = jnp.zeros((SPARE, count), jnp.float32)
    for by, out_ref in zip(ORDER, out_refs):
        there = pl.multiple_of(jnp.bitwise_xor(own, by) * count, LANES)
        out_ref[0:padded] = placed(attended[:, pl.ds(there, count)], spare).astype(jnp.bfloat16)
        if piggy:
            out_ref[padded:] = below


def joined_heads(got_refs, flat):
    own = lax.rem(lax.axis_index("grp"), HEADS)
    spares = []
    for step, (by, got_ref) in enumerate(zip(ORDER, got_refs)):
        odd = lax.rem(jnp.bitwise_xor(own, by), 2)
        at = step * PADDED
        top = got_ref[0:16].astype(jnp.float32)
        bottom = got_ref[PADDED - 16 : PADDED].astype(jnp.float32)
        spares.append(jnp.where(odd == 1, top[:SPARE], bottom[SPARE:]))
        top = jnp.concatenate([jnp.where(odd == 1, 0.0, top[:SPARE]), top[SPARE:]], axis=0)
        bottom = jnp.concatenate([bottom[:SPARE], jnp.where(odd == 1, bottom[SPARE:], 0.0)], axis=0)
        flat[at : at + 16] = top.astype(jnp.bfloat16)
        flat[at + 16 : at + PADDED - 16] = got_ref[16 : PADDED - 16]
        flat[at + PADDED - 16 : at + PADDED] = bottom.astype(jnp.bfloat16)
    return spares


def send_mixed_rows(rows_ref, weight_ref, flat, turned, mixed, mixed_ref, sems, meanwhile=None):
    turned[...] = flat[...].T
    pieces = sems.shape[0]
    step = rows_ref.shape[0] // pieces
    copies, value = [], None
    for piece in range(pieces):
        cut = slice(piece * step, (piece + 1) * step)
        if meanwhile is not None:
            value = meanwhile[piece](value)
        added = jnp.dot(turned[cut, :], weight_ref[...], preferred_element_type=jnp.float32)
        mixed[cut, :] = (rows_ref[cut, :].astype(jnp.float32) + added).astype(jnp.bfloat16)
        copies.append(pltpu.make_async_copy(mixed.at[cut], mixed_ref.at[cut], sems.at[piece]))
        copies[-1].start()
    return copies


def unit_rows(matrix):
    return matrix * lax.rsqrt(jnp.sum(matrix * matrix, axis=1, keepdims=True) + 1e-06)


def losses(cosine, labels):
    logits = -labels * (logit_scale * cosine + logit_bias)
    return jnp.maximum(logits, 0.0) + jnp.log1p(jnp.exp(-jnp.abs(logits)))


def finish_kernel(images, rows_ref, weight_ref, text_ref, *rest):
    got_refs, rest = rest[:HEADS], rest[HEADS:]
    mixed_ref, loss_ref, flat, turned, mixed, sems, pooled_heads, patch_sums, far_texts, loss, loss_sem = rest
    spares = joined_heads(got_refs, flat)
    own = lax.rem(lax.axis_index("grp"), HEADS)
    patch_sums[:, HEADS * LANES :] = spares[0][:, 2 * LANES :]
    for step, (by, spare) in enumerate(zip(ORDER, spares)):
        pooled_heads[:, step * PADDED : (step + 1) * PADDED] = spare[:, 0:PADDED]
        head = jnp.bitwise_xor(own, by)
        patch_sums[:, pl.ds(pl.multiple_of(head * LANES, LANES), LANES)] = spare[:, LANES : 2 * LANES]
        below = got_refs[step][PADDED:].astype(jnp.float32)
        count = below.shape[1]
        for part in range(patch_sums.shape[1] // count):
            here = slice(part * count, (part + 1) * count)
            far_texts[head, :, here] = below[part * images : (part + 1) * images]

    def find_images(_):
        pooled = jnp.dot(
            pooled_heads[...].astype(jnp.bfloat16), weight_ref[...], preferred_element_type=jnp.float32
        )
        pooled = pooled + patch_sums[...]
        others = [far_texts[place] for place in range(lax.axis_size("blk") - 1)]
        texts = jnp.concatenate([text_ref[...].astype(jnp.float32)] + others, axis=0)
        return pooled + pltpu.roll(pooled, images, axis=0), unit_rows(texts)

    def find_cosines(vectors):
        pooled, text_vecs = vectors
        return lax.dot_general(
            text_vecs,
            unit_rows(pooled),
            (((1,), (1,)), ((), ())),
            precision=lax.Precision.HIGHEST,
            preferred_element_type=jnp.float32,
        )

    def find_losses(cosine):
        text = lax.broadcasted_iota(jnp.int32, cosine.shape, 0)
        image = lax.broadcasted_iota(jnp.int32, cosine.shape, 1)
        terms = losses(cosine, jnp.where(text == image, 1.0, -1.0))
        loss[...] = jnp.sum(terms, axis=0, keepdims=True)[:, 0:images]
        loss_copy.start()

    loss_copy = pltpu.make_async_copy(loss, loss_ref, loss_sem)
    meanwhile = (find_images, find_cosines, find_losses)
    copies = send_mixed_rows(rows_ref, weight_ref, flat, turned, mixed, mixed_ref, sems, meanwhile)
    for copy in copies + [loss_copy]:
        copy.wait()


def mix_kernel(rows_ref, weight_ref, *rest):
    got_refs, rest = rest[:HEADS], rest[HEADS:]
    mixed_ref, flat, turned, mixed, sems = rest
    joined_heads(got_refs, flat)
    for copy in send_mixed_rows(rows_ref, weight_ref, flat, turned, mixed, mixed_ref, sems):
        copy.wait()


def in_vmem(count):
    return [pl.BlockSpec(memory_space=pltpu.VMEM)] * count


def in_hbm(value):
    return pltpu.with_memory_space_constraint(value, pltpu.HBM)


def call(kernel, out_shape, scratch, in_specs, flops, out_specs=None):
    if out_specs is None:
        out_specs = jax.tree.map(lambda _: pl.BlockSpec(memory_space=pltpu.VMEM), out_shape)
    return pl.pallas_call(
        kernel,
        out_shape=out_shape,
        in_specs=in_specs,
        out_specs=out_specs,
        scratch_shapes=scratch,
        compiler_params=pltpu.CompilerParams(vmem_limit_bytes=VMEM_LIMIT),
        cost_estimate=pl.CostEstimate(flops=flops, bytes_accessed=8 << 20, transcendentals=0),
    )


def moved(value, axis, pairs):
    return lax.ppermute(value, axis, pairs)


def partner(place, by, peers):
    return place ^ by if peers & (peers - 1) == 0 else (place + by) % peers


def all_texts(texts):
    peers = lax.axis_size("blk")
    steps = [[(partner(i, by, peers), i) for i in range(peers)] for by in range(1, peers)]
    return jnp.concatenate([texts] + [moved(texts, "blk", pairs) for pairs in steps], axis=0)


def one_text_block(texts):
    peers = lax.axis_size("blk")
    pairs = []
    for place in range(lax.axis_size("grp")):
        by = place % (peers - 1) + 1
        pairs += [(place * peers + partner(i, by, peers), place * peers + i) for i in range(peers)]
    return moved(texts, ("grp", "blk"), pairs)


def traded(blocks):
    peers = range(lax.axis_size("grp"))
    trades = {by: moved(blocks[by], "grp", [(i, i ^ by) for i in peers]) for by in ORDER if by}
    return {**trades, 0: blocks[0]}


def local(patches, segment_ids, qkv_weight, out_weight, text_embed):
    rows = patches[0]
    count, depth = rows.shape
    width = out_weight.shape[0]
    size = width // HEADS
    padded = size + SPARE
    images = text_embed.shape[0]
    group_size = lax.axis_size("grp")
    parts = group_size // HEADS
    piggy = (
        parts == 1
        and 2 * images == SPARE
        and count >= depth - (HEADS - 2) * LANES
        and depth % count == 0
        and images * (depth // count) <= TEXT_ROWS
        and 1 < lax.axis_size("blk") <= HEADS + 1
    )
    bf16, f32 = jnp.bfloat16, jnp.float32
    shape = jax.ShapeDtypeStruct

    block = shape((3 * size + SPARE, count), bf16)
    hbm = pl.BlockSpec(memory_space=pltpu.HBM)
    turned_weight = qkv_weight.T
    normed, sums, *sent = call(
        functools.partial(far_kernel, images, piggy),
        (shape((depth, count), bf16), shape((SPARE, depth), f32), block, block),
        [
            pltpu.VMEM((1, count), jnp.int32),
            pltpu.VMEM((count, depth), bf16),
            pltpu.VMEM((3, 2 * size, depth), bf16),
            pltpu.SemaphoreType.DMA,
            pltpu.SemaphoreType.DMA,
            pltpu.SemaphoreType.DMA((3,)),
        ],
        [hbm] * 3,
        2 * count * depth * 6 * size,
    )(in_hbm(segment_ids), in_hbm(rows), in_hbm(turned_weight))
    sent += call(
        functools.partial(near_kernel, piggy),
        (block,) * 6,
        [],
        in_vmem(3),
        2 * count * depth * 18 * size,
    )(normed, sums, turned_weight)
    sent = dict(zip((6, 7, 2, 3, 4, 5, 0, 1), sent))
    if piggy:
        late_texts, sent[0] = lax.optimization_barrier((text_embed, sent[0]))
        halos_and_texts = [one_text_block(late_texts)]
    else:
        halos_and_texts = []
    got = traded(sent)

    length = HEADS * count
    halo = 0
    near_ids = segment_ids
    if parts > 1:
        halo = rounded_up(MAXP - 1, LANES)
        part = lax.axis_index("grp") // HEADS
        whole_ids = jnp.concatenate(
            [
                jnp.full((1, halo), -1, jnp.int32),
                segment_ids,
                jnp.full((1, halo), images, jnp.int32),
            ],
            axis=1,
        )
        near_ids = lax.dynamic_slice_in_dim(whole_ids, part * length, length + 2 * halo, axis=1)
        order = jnp.bitwise_xor(lax.axis_index("grp") % HEADS, jnp.arange(HEADS))
        flat = jnp.stack([got[by] for by in range(HEADS)])[order][:, : 2 * size].transpose(1, 0, 2).reshape(2 * size, length)
        flat = jnp.concatenate([flat, jnp.zeros((16, length), bf16)], axis=0)
        ahead = [(i, i + HEADS) for i in range(group_size - HEADS)]
        back = [(i + HEADS, i) for i in range(group_size - HEADS)]
        left = moved(flat[:, length - halo :], "grp", ahead)
        right = moved(flat[:, :halo], "grp", back)
        halos_and_texts += [left, right]
    reach = length + 2 * halo
    window = min(rounded_up(MAXP + LANES - 1, LANES), reach)
    tile = 2 * LANES
    early_keys, marks, before, weight = call(
        functools.partial(prepare_kernel, images, halo),
        (
            shape((len(EARLY) * count, LANES), bf16),
            shape((2, SPARE, reach), f32),
            shape((rounded_up(images + 1, SPARE), LANES), jnp.int32),
            shape((HEADS * padded, depth), bf16),
        ),
        [pltpu.SemaphoreType.DMA((HEADS,))],
        in_vmem(1) + [hbm] + in_vmem(len(EARLY)),
        1 << 30,
    )(near_ids, in_hbm(out_weight), *[got[by] for by in EARLY])
    operands = [near_ids, before, marks, early_keys, *[got[by] for by in EARLY + LATE], *halos_and_texts]
    answers = call(
        functools.partial(attend_kernel, images, piggy, halo),
        (shape((padded + TEXT_ROWS * piggy, count), bf16),) * HEADS,
        [
            pltpu.VMEM((reach, LANES), bf16),
            pltpu.VMEM((padded, reach), bf16),
            pltpu.VMEM((LANES, length), bf16),
            pltpu.VMEM((padded, length), f32),
        ]
        + [pltpu.VMEM((window, tile), f32), pltpu.VMEM((1, tile), f32)] * 2
        + [pltpu.SMEM((images + 1,), jnp.int32)],
        in_vmem(len(operands)),
        4 * size * length * MAXP,
    )(*operands)
    home = traded(dict(zip(ORDER, answers)))
    home = [home[by] for by in ORDER]

    joined = [
        pltpu.VMEM((HEADS * padded, count), bf16),
        pltpu.VMEM((count, HEADS * padded), bf16),
        pltpu.VMEM((count, depth), bf16),
        pltpu.SemaphoreType.DMA((3,)),
    ]
    flops = 2 * count * depth * width
    if piggy:
        mixed, row_loss = call(
            functools.partial(finish_kernel, images),
            (shape((count, depth), bf16), shape((1, images), f32)),
            joined
            + [
                pltpu.VMEM((SPARE, HEADS * padded), f32),
                pltpu.VMEM((SPARE, depth), f32),
                pltpu.VMEM((HEADS, images, depth), f32),
                pltpu.VMEM((1, images), f32),
                pltpu.SemaphoreType.DMA,
            ],
            in_vmem(3 + HEADS),
            flops,
            (hbm, hbm),
        )(rows, weight, text_embed, *home)
        return (mixed[None], row_loss[0])
    mixed = call(mix_kernel, shape((count, depth), bf16), joined, in_vmem(2 + HEADS), flops, hbm)(
        rows, weight, *home
    )
    own_ids = lax.dynamic_slice_in_dim(segment_ids[0], lax.axis_index("grp") * count, count)
    onehot = (own_ids[None, :] == jnp.arange(images, dtype=jnp.int32)[:, None]).astype(bf16)
    pooled = lax.psum(jnp.dot(onehot, mixed, preferred_element_type=f32), "grp")
    text_vecs = unit_rows(all_texts(text_embed).astype(f32))
    cosine = jnp.dot(unit_rows(pooled), text_vecs.T, precision=lax.Precision.HIGHEST)
    same = jnp.arange(images)[:, None] == jnp.arange(text_vecs.shape[0])[None, :]
    row_loss = jnp.sum(losses(cosine, jnp.where(same, 1.0, -1.0)), axis=1)
    return (mixed[None], row_loss)


def solution(mesh):
    placed = (P("blk", "grp", None), P("blk", None), P(), P(), P("blk", None))
    return jax.shard_map(
        local,
        mesh=mesh,
        in_specs=placed,
        out_specs=(P("blk", "grp", None), P("blk")),
        check_vma=False,
    )
```

```python
import functools
import math

import jax
import jax.numpy as jnp
from jax import lax
from jax.experimental import pallas as pl
from jax.experimental.pallas import tpu as pltpu
from jax.sharding import PartitionSpec as P

HEADS = 8
MAXP = 1024
LANES = 128
SPARE = 8
SIZE = 72
PADDED = SIZE + SPARE
KEY_AT = SIZE - SPARE
QUERY_AT = 2 * SIZE
TEXT_ROWS = 16
HIDDEN = -1e30
ORDER = (6, 7, 2, 4, 3, 5, 1, 0)
EARLY = (6, 7, 1, 0)
LATE = (2, 4, 3, 5)

logit_scale = 30.0
logit_bias = -5.0

VMEM_LIMIT = 32 * 1024 * 1024


def rounded_up(value, step):
    return (value + step - 1) // step * step


def split_in_two(total, images):
    row = lax.broadcasted_iota(jnp.int32, total.shape, 0)
    main = total.astype(jnp.bfloat16).astype(jnp.float32)
    return jnp.where(row < images, main, total - main)


def image_rows(ids, images):
    row = lax.broadcasted_iota(jnp.int32, (SPARE, ids.shape[1]), 0)
    return (lax.rem(row, images) == ids).astype(jnp.float32).astype(jnp.bfloat16)


def head_blocks(query, key, value, sums, pair):
    size = query.shape[0] // 2
    count = query.shape[1]
    for place in range(2):
        here = slice(place * size, (place + 1) * size)
        if sums is None:
            spare = jnp.zeros((SPARE, count), jnp.float32)
        else:
            first = pl.multiple_of((2 * pair + place) * LANES, LANES)
            parts = [sums[:, pl.ds(first, LANES)], sums[:, HEADS * LANES :]]
            held = sum(part.shape[1] for part in parts)
            spare = jnp.concatenate(parts + [jnp.zeros((SPARE, count - held), jnp.float32)], axis=1)
        yield jnp.concatenate([value[here], key[here], spare, query[here]], axis=0)


def store_by_core(core, blocks, same_ref, cross_ref):
    first, second = blocks
    same_ref[...] = jnp.where(core == 0, first, second).astype(jnp.bfloat16)
    cross_ref[...] = jnp.where(core == 0, second, first).astype(jnp.bfloat16)


def place_in_group():
    own = lax.rem(lax.axis_index("grp"), HEADS)
    return lax.div(own, 2), lax.rem(own, 2)


def far_kernel(images, piggy, ids_ref, rows_ref, weight_ref, normed_ref, sums_ref, same_ref, cross_ref, own_ids, rows_held, weight, id_sem, row_sem, sems):
    count, depth = rows_ref.shape
    width = weight_ref.shape[0] // 3
    wide = weight.shape[1]
    rows_fetch = pltpu.make_async_copy(rows_ref, rows_held, row_sem)
    rows_fetch.start()
    own = pl.multiple_of(lax.axis_index("grp") * count, LANES)
    ids_fetch = pltpu.make_async_copy(ids_ref.at[:, pl.ds(own, count)], own_ids, id_sem)
    ids_fetch.start()
    pair, core = place_in_group()
    pair = jnp.bitwise_xor(pair, 3)
    fetches = []
    for at in range(3):
        first = pl.multiple_of(at * width + pair * wide, 16)
        fetches.append(pltpu.make_async_copy(weight_ref.at[pl.ds(first, wide)], weight.at[at], sems.at[at]))
    for fetch in fetches:
        fetch.start()
    ids_fetch.wait()
    rows_fetch.wait()
    rows = rows_held[...]
    if piggy:
        sums = jnp.dot(image_rows(own_ids[...], images), rows, preferred_element_type=jnp.float32)
        sums_ref[...] = split_in_two(sums, images)
    values = rows.astype(jnp.float32)
    center = values - jnp.mean(values, axis=1, keepdims=True)
    spread = jnp.mean(center * center, axis=1, keepdims=True)
    normed = (center * lax.rsqrt(spread + 1e-06)).astype(jnp.bfloat16)
    normed_ref[...] = normed.T
    for fetch in fetches:
        fetch.wait()
    parts = [
        jnp.dot(weight[at], normed_ref[...], preferred_element_type=jnp.float32) for at in range(3)
    ]
    store_by_core(core, head_blocks(*parts, sums_ref if piggy else None, pair), same_ref, cross_ref)


def near_kernel(piggy, normed_ref, sums_ref, weight_ref, *out_refs):
    width = weight_ref.shape[0] // 3
    wide = 2 * width // HEADS
    own, core = place_in_group()
    for step, move in enumerate((1, 2, 0)):
        pair = jnp.bitwise_xor(own, move)
        parts = []
        for at in range(3):
            here = pl.ds(pl.multiple_of(at * width + pair * wide, 16), wide)
            parts.append(
                jnp.dot(weight_ref[here, :], normed_ref[...], preferred_element_type=jnp.float32)
            )
        blocks = head_blocks(*parts, sums_ref if piggy else None, pair)
        store_by_core(core, blocks, *out_refs[2 * step : 2 * step + 2])


def count_before(images, ids):
    image = lax.broadcasted_iota(jnp.int32, (rounded_up(images + 1, SPARE), ids.shape[1]), 0)
    before = jnp.sum((ids < image).astype(jnp.int32), axis=1, keepdims=True)
    return jnp.broadcast_to(before, (before.shape[0], LANES))


def write_marks(images, ids, marks):
    bits = max(1, (images - 1).bit_length())
    row = lax.broadcasted_iota(jnp.int32, (SPARE, ids.shape[1]), 0)
    bit = jnp.bitwise_and(lax.shift_right_logical(jnp.broadcast_to(ids, row.shape), row >> 1), 1)
    odd = jnp.bitwise_and(row, 1)
    used = row < 2 * bits
    outside = jnp.logical_or(ids < 0, ids >= images)
    key_side = jnp.where(odd == 1, bit, 1 - bit).astype(jnp.float32)
    key_side = jnp.where(outside, 1.0, key_side)
    marks[0] = jnp.where(used, key_side * HIDDEN, 0.0)
    marks[1] = jnp.where(used, jnp.where(odd == 1, 1 - bit, bit), 0).astype(jnp.float32)


def spare_sums(refs):
    parts = [ref[QUERY_AT : QUERY_AT + 16].astype(jnp.float32)[0:SPARE, 0 : 2 * LANES] for ref in refs]
    return sum(parts[1:], parts[0])


def image_at(images, starts, position):
    found = jnp.int32(0)
    for image in range(1, images):
        found += (starts[image] <= position).astype(jnp.int32)
    return found


def attend_images(images, ids_ref, keys, values, queries, attended, work, starts, halo):
    scores_a, scores_b, tops_a, tops_b = work
    query_base = halo
    window, tile = scores_a.shape
    size = attended.shape[0] - SPARE
    held = queries.shape[1]
    tiles = held // tile
    shift = tile.bit_length() - 1

    def bounds(image):
        first = jnp.maximum(starts[image] - query_base, 0) >> shift
        last = (jnp.minimum(starts[image + 1] - query_base, held) - 1) >> shift
        return jnp.minimum(first, tiles - 1), last

    def after(image):
        return jnp.minimum(image + 1, images - 1)

    def following(state):
        at, image = state
        more = at < bounds(image)[1]
        later = after(image)
        return jnp.where(more, at + 1, bounds(later)[0]), jnp.where(more, image, later)

    def window_of(image):
        begin = jnp.bitwise_and(starts[image], -LANES)
        return pl.ds(pl.multiple_of(jnp.minimum(begin, keys.shape[0] - window), LANES), window)

    def score(state, scores, tops):
        at, image = state
        query = queries[:, pl.ds(pl.multiple_of(at * tile, tile), tile)]
        found = jnp.dot(keys[window_of(image), :], query, preferred_element_type=jnp.float32)
        scores[...] = found
        tops[...] = jnp.max(found, axis=0, keepdims=True)

    def weigh(state, scores, tops):
        at, image = state
        first = pl.multiple_of(at * tile, tile)
        labels = ids_ref[:, pl.ds(pl.multiple_of(query_base + first, LANES), tile)]
        probs = jnp.exp2((scores[...] - tops[...]) * (size ** (-0.5) * math.log2(math.e)))
        share = 1.0 / jnp.sum(probs, axis=0, keepdims=True)
        weighted = jnp.dot(
            values[:, window_of(image)], probs.astype(jnp.bfloat16), preferred_element_type=jnp.float32
        )
        place = (slice(None), pl.ds(first, tile))
        attended[place] = jnp.where(labels == image, weighted * share, attended[place])

    low = image_at(images, starts, query_base)
    high = image_at(images, starts, query_base + held - 1)
    pairs = jnp.int32(0)
    for image in range(images):
        first, last = bounds(image)
        wanted = jnp.logical_and(low <= image, image <= high)
        pairs += jnp.where(wanted, last - first + 1, 0)

    def two_pairs(_, state):
        second = following(state)
        score(second, scores_b, tops_b)
        weigh(state, scores_a, tops_a)
        third = following(second)
        score(third, scores_a, tops_a)
        weigh(second, scores_b, tops_b)
        return third

    def four_pairs(step, state):
        return two_pairs(step, two_pairs(step, state))

    begun = (jnp.int32(0), low)
    score(begun, scores_a, tops_a)
    reached = lax.fori_loop(0, lax.div(pairs, 4), four_pairs, begun)
    reached = lax.fori_loop(0, lax.div(lax.rem(pairs, 4), 2), two_pairs, reached)

    @pl.when(lax.rem(pairs, 2) == 1)
    def _():
        weigh(reached, scores_a, tops_a)


def turned_keys(marked, block_ref):
    block = block_ref[KEY_AT : KEY_AT + PADDED].astype(jnp.float32)
    nothing = jnp.zeros((LANES - PADDED, block.shape[1]), jnp.float32)
    full = jnp.concatenate([marked, block[SPARE:], nothing], axis=0)
    return full.astype(jnp.bfloat16).T


def store_queries(marked, block_ref, queries, there):
    edge = block_ref[QUERY_AT : QUERY_AT + 16].astype(jnp.float32)
    edge = jnp.concatenate([marked, edge[SPARE:]], axis=0)
    queries[0:16, there] = edge.astype(jnp.bfloat16)
    queries[16:PADDED, there] = block_ref[QUERY_AT + 16 : QUERY_AT + PADDED]
    queries[PADDED:, there] = jnp.zeros((LANES - PADDED, block_ref.shape[1]), jnp.bfloat16)


def prepare_kernel(images, halo, ids_ref, out_weight_ref, *rest):
    got_refs, (keys, marks, before, weight, sems) = rest[: len(EARLY)], rest[len(EARLY) :]
    count = got_refs[0].shape[1]
    fetches = []
    for step, by in enumerate(ORDER):
        head = jnp.bitwise_xor(lax.rem(lax.axis_index("grp"), HEADS), by)
        first = lax.div(head, 2) * (2 * SIZE) + lax.rem(head, 2) * (SIZE - SPARE)
        fetches.append(
            pltpu.make_async_copy(
                out_weight_ref.at[pl.ds(pl.multiple_of(first, 16), PADDED)],
                weight.at[step * PADDED : (step + 1) * PADDED],
                sems.at[step],
            )
        )
        fetches[-1].start()
    before[...] = count_before(images, ids_ref[...])
    write_marks(images, ids_ref[...], marks)
    own = lax.rem(lax.axis_index("grp"), HEADS)
    for step, (by, ref) in enumerate(zip(EARLY, got_refs)):
        first = jnp.bitwise_xor(own, by) * count
        here = pl.ds(pl.multiple_of(halo + first, LANES), count)
        keys[step * count : (step + 1) * count, :] = turned_keys(marks[0, :, here], ref)
    for fetch in fetches:
        fetch.wait()


def attend_kernel(images, piggy, halo, ids_ref, before_ref, marks, early_keys, *rest):
    got_refs, rest = rest[:HEADS], rest[HEADS:]
    if piggy:
        text_ref, *rest = rest
    if halo:
        left_ref, right_ref, *rest = rest
    out_refs, rest = rest[:HEADS], rest[HEADS:]
    keys, values, queries, attended, *work, starts = rest
    count = got_refs[0].shape[1]
    padded = attended.shape[0]
    size = padded - SPARE
    total_rows = HEADS * count
    length = ids_ref.shape[1]
    ids = ids_ref[...]
    before = before_ref[...]
    for image in range(images + 1):
        starts[image] = before[image, 0]

    own = lax.rem(lax.axis_index("grp"), HEADS)
    for step, (by, ref) in enumerate(zip(EARLY + LATE, got_refs)):
        first = jnp.bitwise_xor(own, by) * count
        here = pl.ds(pl.multiple_of(halo + first, LANES), count)
        there = pl.ds(pl.multiple_of(first, LANES), count)
        if by in EARLY:
            keys[here, :] = early_keys[step * count : (step + 1) * count, :]
        else:
            keys[here, :] = turned_keys(marks[0, :, here], ref)
        values[:, here] = ref[0:PADDED]
        store_queries(marks[1, :, here], ref, queries, there)
    if halo:
        for ref, here in ((left_ref, slice(0, halo)), (right_ref, slice(length - halo, length))):
            keys[here, :] = turned_keys(marks[0, :, here], ref)
            values[:, here] = ref[0:PADDED]
    attend_images(images, ids_ref, keys, values, queries, attended, work, starts, halo)

    odd_head = lax.rem(own, 2) == 1
    mine = ids[:, halo : halo + total_rows]

    def placed(block, spare):
        even = jnp.concatenate([block[0:size], spare], axis=0)
        odd = jnp.concatenate([spare, block[0:size]], axis=0)
        return jnp.where(odd_head, odd, even)

    if piggy:
        nothing = jnp.zeros((SPARE, total_rows), jnp.float32)
        flat = placed(attended[...], nothing).astype(jnp.bfloat16)
        pooled = lax.dot_general(
            image_rows(mine, images), flat, (((1,), (1,)), ((), ())), preferred_element_type=jnp.float32
        )
        pooled = split_in_two(pooled, images)
        sums = spare_sums(got_refs)
        sums = split_in_two(sums + pltpu.roll(sums, images, axis=0), images)
        spare = jnp.concatenate(
            [pooled, jnp.zeros((SPARE, LANES - padded), jnp.float32), sums], axis=1
        )
        texts = text_ref[...].astype(jnp.float32)
        parts = [texts[:, at : at + count] for at in range(0, texts.shape[1], count)]
        unused = TEXT_ROWS - images * len(parts)
        below = jnp.concatenate(parts + [jnp.zeros((unused, count), jnp.float32)] * (unused > 0), axis=0)
        below = below.astype(jnp.bfloat16)
    else:
        spare = jnp.zeros((SPARE, count), jnp.float32)
    for by, out_ref in zip(ORDER, out_refs):
        there = pl.multiple_of(jnp.bitwise_xor(own, by) * count, LANES)
        out_ref[0:padded] = placed(attended[:, pl.ds(there, count)], spare).astype(jnp.bfloat16)
        if piggy:
            out_ref[padded:] = below


def joined_heads(got_refs, flat):
    own = lax.rem(lax.axis_index("grp"), HEADS)
    spares = []
    for step, (by, got_ref) in enumerate(zip(ORDER, got_refs)):
        odd = lax.rem(jnp.bitwise_xor(own, by), 2)
        at = step * PADDED
        top = got_ref[0:16].astype(jnp.float32)
        bottom = got_ref[PADDED - 16 : PADDED].astype(jnp.float32)
        spares.append(jnp.where(odd == 1, top[:SPARE], bottom[SPARE:]))
        top = jnp.concatenate([jnp.where(odd == 1, 0.0, top[:SPARE]), top[SPARE:]], axis=0)
        bottom = jnp.concatenate([bottom[:SPARE], jnp.where(odd == 1, bottom[SPARE:], 0.0)], axis=0)
        flat[at : at + 16] = top.astype(jnp.bfloat16)
        flat[at + 16 : at + PADDED - 16] = got_ref[16 : PADDED - 16]
        flat[at + PADDED - 16 : at + PADDED] = bottom.astype(jnp.bfloat16)
    return spares


def send_mixed_rows(rows_ref, weight_ref, flat, turned, mixed, mixed_ref, sems, meanwhile=None):
    turned[...] = flat[...].T
    pieces = sems.shape[0]
    step = rows_ref.shape[0] // pieces
    copies, value = [], None
    for piece in range(pieces):
        cut = slice(piece * step, (piece + 1) * step)
        if meanwhile is not None:
            value = meanwhile[piece](value)
        added = jnp.dot(turned[cut, :], weight_ref[...], preferred_element_type=jnp.float32)
        mixed[cut, :] = (rows_ref[cut, :].astype(jnp.float32) + added).astype(jnp.bfloat16)
        copies.append(pltpu.make_async_copy(mixed.at[cut], mixed_ref.at[cut], sems.at[piece]))
        copies[-1].start()
    return copies


def unit_rows(matrix):
    return matrix * lax.rsqrt(jnp.sum(matrix * matrix, axis=1, keepdims=True) + 1e-06)


def losses(cosine, labels):
    logits = -labels * (logit_scale * cosine + logit_bias)
    return jnp.maximum(logits, 0.0) + jnp.log1p(jnp.exp(-jnp.abs(logits)))


def finish_kernel(images, rows_ref, weight_ref, text_ref, *rest):
    got_refs, rest = rest[:HEADS], rest[HEADS:]
    mixed_ref, loss_ref, flat, turned, mixed, sems, pooled_heads, patch_sums, far_texts, loss, loss_sem = rest
    spares = joined_heads(got_refs, flat)
    own = lax.rem(lax.axis_index("grp"), HEADS)
    patch_sums[:, HEADS * LANES :] = spares[0][:, 2 * LANES :]
    for step, (by, spare) in enumerate(zip(ORDER, spares)):
        pooled_heads[:, step * PADDED : (step + 1) * PADDED] = spare[:, 0:PADDED]
        head = jnp.bitwise_xor(own, by)
        patch_sums[:, pl.ds(pl.multiple_of(head * LANES, LANES), LANES)] = spare[:, LANES : 2 * LANES]
        below = got_refs[step][PADDED:].astype(jnp.float32)
        count = below.shape[1]
        for part in range(patch_sums.shape[1] // count):
            here = slice(part * count, (part + 1) * count)
            far_texts[head, :, here] = below[part * images : (part + 1) * images]

    def find_images(_):
        pooled = jnp.dot(
            pooled_heads[...].astype(jnp.bfloat16), weight_ref[...], preferred_element_type=jnp.float32
        )
        pooled = pooled + patch_sums[...]
        others = [far_texts[place] for place in range(lax.axis_size("blk") - 1)]
        texts = jnp.concatenate([text_ref[...].astype(jnp.float32)] + others, axis=0)
        return pooled + pltpu.roll(pooled, images, axis=0), unit_rows(texts)

    def find_cosines(vectors):
        pooled, text_vecs = vectors
        return lax.dot_general(
            text_vecs,
            unit_rows(pooled),
            (((1,), (1,)), ((), ())),
            precision=lax.Precision.HIGHEST,
            preferred_element_type=jnp.float32,
        )

    def find_losses(cosine):
        text = lax.broadcasted_iota(jnp.int32, cosine.shape, 0)
        image = lax.broadcasted_iota(jnp.int32, cosine.shape, 1)
        terms = losses(cosine, jnp.where(text == image, 1.0, -1.0))
        loss[...] = jnp.sum(terms, axis=0, keepdims=True)[:, 0:images]
        loss_copy.start()

    loss_copy = pltpu.make_async_copy(loss, loss_ref, loss_sem)
    meanwhile = (find_images, find_cosines, find_losses)
    copies = send_mixed_rows(rows_ref, weight_ref, flat, turned, mixed, mixed_ref, sems, meanwhile)
    for copy in copies + [loss_copy]:
        copy.wait()


def mix_kernel(rows_ref, weight_ref, *rest):
    got_refs, rest = rest[:HEADS], rest[HEADS:]
    mixed_ref, flat, turned, mixed, sems = rest
    joined_heads(got_refs, flat)
    for copy in send_mixed_rows(rows_ref, weight_ref, flat, turned, mixed, mixed_ref, sems):
        copy.wait()


def in_vmem(count):
    return [pl.BlockSpec(memory_space=pltpu.VMEM)] * count


def in_hbm(value):
    return pltpu.with_memory_space_constraint(value, pltpu.HBM)


def call(kernel, out_shape, scratch, in_specs, flops, out_specs=None):
    if out_specs is None:
        out_specs = jax.tree.map(lambda _: pl.BlockSpec(memory_space=pltpu.VMEM), out_shape)
    return pl.pallas_call(
        kernel,
        out_shape=out_shape,
        in_specs=in_specs,
        out_specs=out_specs,
        scratch_shapes=scratch,
        compiler_params=pltpu.CompilerParams(vmem_limit_bytes=VMEM_LIMIT),
        cost_estimate=pl.CostEstimate(flops=flops, bytes_accessed=8 << 20, transcendentals=0),
    )


def moved(value, axis, pairs):
    return lax.ppermute(value, axis, pairs)


def partner(place, by, peers):
    return place ^ by if peers & (peers - 1) == 0 else (place + by) % peers


def all_texts(texts):
    peers = lax.axis_size("blk")
    steps = [[(partner(i, by, peers), i) for i in range(peers)] for by in range(1, peers)]
    return jnp.concatenate([texts] + [moved(texts, "blk", pairs) for pairs in steps], axis=0)


def one_text_block(texts):
    peers = lax.axis_size("blk")
    pairs = []
    for place in range(lax.axis_size("grp")):
        by = place % (peers - 1) + 1
        pairs += [(place * peers + partner(i, by, peers), place * peers + i) for i in range(peers)]
    return moved(texts, ("grp", "blk"), pairs)


def traded(blocks):
    peers = range(lax.axis_size("grp"))
    trades = {by: moved(blocks[by], "grp", [(i, i ^ by) for i in peers]) for by in ORDER if by}
    return {**trades, 0: blocks[0]}


def local(patches, segment_ids, qkv_weight, out_weight, text_embed):
    rows = patches[0]
    count, depth = rows.shape
    width = out_weight.shape[0]
    size = width // HEADS
    padded = size + SPARE
    images = text_embed.shape[0]
    group_size = lax.axis_size("grp")
    parts = group_size // HEADS
    piggy = (
        parts == 1
        and 2 * images == SPARE
        and count >= depth - (HEADS - 2) * LANES
        and depth % count == 0
        and images * (depth // count) <= TEXT_ROWS
        and 1 < lax.axis_size("blk") <= HEADS + 1
    )
    bf16, f32 = jnp.bfloat16, jnp.float32
    shape = jax.ShapeDtypeStruct

    block = shape((3 * size + SPARE, count), bf16)
    hbm = pl.BlockSpec(memory_space=pltpu.HBM)
    turned_weight = qkv_weight.T
    normed, sums, *sent = call(
        functools.partial(far_kernel, images, piggy),
        (shape((depth, count), bf16), shape((SPARE, depth), f32), block, block),
        [
            pltpu.VMEM((1, count), jnp.int32),
            pltpu.VMEM((count, depth), bf16),
            pltpu.VMEM((3, 2 * size, depth), bf16),
            pltpu.SemaphoreType.DMA,
            pltpu.SemaphoreType.DMA,
            pltpu.SemaphoreType.DMA((3,)),
        ],
        [hbm] * 3,
        2 * count * depth * 6 * size,
    )(in_hbm(segment_ids), in_hbm(rows), in_hbm(turned_weight))
    sent += call(
        functools.partial(near_kernel, piggy),
        (block,) * 6,
        [],
        in_vmem(3),
        2 * count * depth * 18 * size,
    )(normed, sums, turned_weight)
    sent = dict(zip((6, 7, 2, 3, 4, 5, 0, 1), sent))
    if piggy:
        late_texts, sent[0] = lax.optimization_barrier((text_embed, sent[0]))
        halos_and_texts = [one_text_block(late_texts)]
    else:
        halos_and_texts = []
    got = traded(sent)

    length = HEADS * count
    halo = 0
    near_ids = segment_ids
    if parts > 1:
        halo = rounded_up(MAXP - 1, LANES)
        part = lax.axis_index("grp") // HEADS
        whole_ids = jnp.concatenate(
            [
                jnp.full((1, halo), -1, jnp.int32),
                segment_ids,
                jnp.full((1, halo), images, jnp.int32),
            ],
            axis=1,
        )
        near_ids = lax.dynamic_slice_in_dim(whole_ids, part * length, length + 2 * halo, axis=1)
        order = jnp.bitwise_xor(lax.axis_index("grp") % HEADS, jnp.arange(HEADS))
        flat = jnp.stack([got[by] for by in range(HEADS)])[order][:, : 2 * size].transpose(1, 0, 2).reshape(2 * size, length)
        flat = jnp.concatenate([flat, jnp.zeros((16, length), bf16)], axis=0)
        ahead = [(i, i + HEADS) for i in range(group_size - HEADS)]
        back = [(i + HEADS, i) for i in range(group_size - HEADS)]
        left = moved(flat[:, length - halo :], "grp", ahead)
        right = moved(flat[:, :halo], "grp", back)
        halos_and_texts += [left, right]
    reach = length + 2 * halo
    window = min(rounded_up(MAXP + LANES - 1, LANES), reach)
    tile = 2 * LANES
    early_keys, marks, before, weight = call(
        functools.partial(prepare_kernel, images, halo),
        (
            shape((len(EARLY) * count, LANES), bf16),
            shape((2, SPARE, reach), f32),
            shape((rounded_up(images + 1, SPARE), LANES), jnp.int32),
            shape((HEADS * padded, depth), bf16),
        ),
        [pltpu.SemaphoreType.DMA((HEADS,))],
        in_vmem(1) + [hbm] + in_vmem(len(EARLY)),
        1 << 30,
    )(near_ids, in_hbm(out_weight), *[got[by] for by in EARLY])
    operands = [near_ids, before, marks, early_keys, *[got[by] for by in EARLY + LATE], *halos_and_texts]
    answers = call(
        functools.partial(attend_kernel, images, piggy, halo),
        (shape((padded + TEXT_ROWS * piggy, count), bf16),) * HEADS,
        [
            pltpu.VMEM((reach, LANES), bf16),
            pltpu.VMEM((padded, reach), bf16),
            pltpu.VMEM((LANES, length), bf16),
            pltpu.VMEM((padded, length), f32),
            pltpu.VMEM((window, tile), f32),
            pltpu.VMEM((window, tile), f32),
            pltpu.VMEM((1, tile), f32),
            pltpu.VMEM((1, tile), f32),
            pltpu.SMEM((images + 1,), jnp.int32),
        ],
        in_vmem(len(operands)),
        4 * size * length * MAXP,
    )(*operands)
    home = traded(dict(zip(ORDER, answers)))
    home = [home[by] for by in ORDER]

    joined = [
        pltpu.VMEM((HEADS * padded, count), bf16),
        pltpu.VMEM((count, HEADS * padded), bf16),
        pltpu.VMEM((count, depth), bf16),
        pltpu.SemaphoreType.DMA((3,)),
    ]
    flops = 2 * count * depth * width
    if piggy:
        mixed, row_loss = call(
            functools.partial(finish_kernel, images),
            (shape((count, depth), bf16), shape((1, images), f32)),
            joined
            + [
                pltpu.VMEM((SPARE, HEADS * padded), f32),
                pltpu.VMEM((SPARE, depth), f32),
                pltpu.VMEM((HEADS, images, depth), f32),
                pltpu.VMEM((1, images), f32),
                pltpu.SemaphoreType.DMA,
            ],
            in_vmem(3 + HEADS),
            flops,
            (hbm, hbm),
        )(rows, weight, text_embed, *home)
        return (mixed[None], row_loss[0])
    mixed = call(mix_kernel, shape((count, depth), bf16), joined, in_vmem(2 + HEADS), flops, hbm)(
        rows, weight, *home
    )
    own_ids = lax.dynamic_slice_in_dim(segment_ids[0], lax.axis_index("grp") * count, count)
    onehot = (own_ids[None, :] == jnp.arange(images, dtype=jnp.int32)[:, None]).astype(bf16)
    pooled = lax.psum(jnp.dot(onehot, mixed, preferred_element_type=f32), "grp")
    text_vecs = unit_rows(all_texts(text_embed).astype(f32))
    cosine = jnp.dot(unit_rows(pooled), text_vecs.T, precision=lax.Precision.HIGHEST)
    same = jnp.arange(images)[:, None] == jnp.arange(text_vecs.shape[0])[None, :]
    row_loss = jnp.sum(losses(cosine, jnp.where(same, 1.0, -1.0)), axis=1)
    return (mixed[None], row_loss)


def solution(mesh):
    placed = (P("blk", "grp", None), P("blk", None), P(), P(), P("blk", None))
    return jax.shard_map(
        local,
        mesh=mesh,
        in_specs=placed,
        out_specs=(P("blk", "grp", None), P("blk")),
        check_vma=False,
    )
```

```python
import functools
import math

import jax
import jax.numpy as jnp
from jax import lax
from jax.experimental import pallas as pl
from jax.experimental.pallas import tpu as pltpu
from jax.sharding import PartitionSpec as P

HEADS = 8
MAXP = 1024
LANES = 128
SPARE = 8
SIZE = 72
PADDED = SIZE + SPARE
KEY_AT = SIZE - SPARE
QUERY_AT = 2 * SIZE
TEXT_ROWS = 16
HIDDEN = -1e30
ORDER = (6, 7, 2, 4, 3, 5, 1, 0)
EARLY = (6, 7, 1, 0)
LATE = (2, 4, 3, 5)

logit_scale = 30.0
logit_bias = -5.0

VMEM_LIMIT = 32 * 1024 * 1024


def rounded_up(value, step):
    return (value + step - 1) // step * step


def split_in_two(total, images):
    row = lax.broadcasted_iota(jnp.int32, total.shape, 0)
    main = total.astype(jnp.bfloat16).astype(jnp.float32)
    return jnp.where(row < images, main, total - main)


def image_rows(ids, images):
    row = lax.broadcasted_iota(jnp.int32, (SPARE, ids.shape[1]), 0)
    return (lax.rem(row, images) == ids).astype(jnp.float32).astype(jnp.bfloat16)


def head_blocks(query, key, value, sums, pair):
    size = query.shape[0] // 2
    count = query.shape[1]
    for place in range(2):
        here = slice(place * size, (place + 1) * size)
        if sums is None:
            spare = jnp.zeros((SPARE, count), jnp.float32)
        else:
            first = pl.multiple_of((2 * pair + place) * LANES, LANES)
            parts = [sums[:, pl.ds(first, LANES)], sums[:, HEADS * LANES :]]
            held = sum(part.shape[1] for part in parts)
            spare = jnp.concatenate(parts + [jnp.zeros((SPARE, count - held), jnp.float32)], axis=1)
        yield jnp.concatenate([value[here], key[here], spare, query[here]], axis=0)


def store_by_core(core, blocks, same_ref, cross_ref):
    first, second = blocks
    same_ref[...] = jnp.where(core == 0, first, second).astype(jnp.bfloat16)
    cross_ref[...] = jnp.where(core == 0, second, first).astype(jnp.bfloat16)


def place_in_group():
    own = lax.rem(lax.axis_index("grp"), HEADS)
    return lax.div(own, 2), lax.rem(own, 2)


def far_kernel(images, piggy, ids_ref, rows_ref, weight_ref, normed_ref, sums_ref, same_ref, cross_ref, own_ids, rows_held, weight, id_sem, row_sem, sems):
    count, depth = rows_ref.shape
    width = weight_ref.shape[0] // 3
    wide = weight.shape[1]
    rows_fetch = pltpu.make_async_copy(rows_ref, rows_held, row_sem)
    rows_fetch.start()
    own = pl.multiple_of(lax.axis_index("grp") * count, LANES)
    ids_fetch = pltpu.make_async_copy(ids_ref.at[:, pl.ds(own, count)], own_ids, id_sem)
    ids_fetch.start()
    pair, core = place_in_group()
    pair = jnp.bitwise_xor(pair, 3)
    fetches = []
    for at in range(3):
        first = pl.multiple_of(at * width + pair * wide, 16)
        fetches.append(pltpu.make_async_copy(weight_ref.at[pl.ds(first, wide)], weight.at[at], sems.at[at]))
    for fetch in fetches:
        fetch.start()
    ids_fetch.wait()
    rows_fetch.wait()
    rows = rows_held[...]
    if piggy:
        sums = jnp.dot(image_rows(own_ids[...], images), rows, preferred_element_type=jnp.float32)
        sums_ref[...] = split_in_two(sums, images)
    values = rows.astype(jnp.float32)
    center = values - jnp.mean(values, axis=1, keepdims=True)
    spread = jnp.mean(center * center, axis=1, keepdims=True)
    normed = (center * lax.rsqrt(spread + 1e-06)).astype(jnp.bfloat16)
    normed_ref[...] = normed.T
    for fetch in fetches:
        fetch.wait()
    parts = [
        jnp.dot(weight[at], normed_ref[...], preferred_element_type=jnp.float32) for at in range(3)
    ]
    store_by_core(core, head_blocks(*parts, sums_ref if piggy else None, pair), same_ref, cross_ref)


def near_kernel(piggy, normed_ref, sums_ref, weight_ref, *out_refs):
    width = weight_ref.shape[0] // 3
    wide = 2 * width // HEADS
    own, core = place_in_group()
    for step, move in enumerate((1, 2, 0)):
        pair = jnp.bitwise_xor(own, move)
        parts = []
        for at in range(3):
            here = pl.ds(pl.multiple_of(at * width + pair * wide, 16), wide)
            parts.append(
                jnp.dot(weight_ref[here, :], normed_ref[...], preferred_element_type=jnp.float32)
            )
        blocks = head_blocks(*parts, sums_ref if piggy else None, pair)
        store_by_core(core, blocks, *out_refs[2 * step : 2 * step + 2])


def count_before(images, ids):
    image = lax.broadcasted_iota(jnp.int32, (rounded_up(images + 1, SPARE), ids.shape[1]), 0)
    before = jnp.sum((ids < image).astype(jnp.int32), axis=1, keepdims=True)
    return jnp.broadcast_to(before, (before.shape[0], LANES))


def write_marks(images, ids, marks):
    bits = max(1, (images - 1).bit_length())
    row = lax.broadcasted_iota(jnp.int32, (SPARE, ids.shape[1]), 0)
    bit = jnp.bitwise_and(lax.shift_right_logical(jnp.broadcast_to(ids, row.shape), row >> 1), 1)
    odd = jnp.bitwise_and(row, 1)
    used = row < 2 * bits
    outside = jnp.logical_or(ids < 0, ids >= images)
    key_side = jnp.where(odd == 1, bit, 1 - bit).astype(jnp.float32)
    key_side = jnp.where(outside, 1.0, key_side)
    marks[0] = jnp.where(used, key_side * HIDDEN, 0.0)
    marks[1] = jnp.where(used, jnp.where(odd == 1, 1 - bit, bit), 0).astype(jnp.float32)


def spare_sums(refs):
    parts = [ref[QUERY_AT : QUERY_AT + 16].astype(jnp.float32)[0:SPARE, 0 : 2 * LANES] for ref in refs]
    return sum(parts[1:], parts[0])


def image_at(images, starts, position):
    found = jnp.int32(0)
    for image in range(1, images):
        found += (starts[image] <= position).astype(jnp.int32)
    return found


def list_pairs(images, held, tile, last_begin, base, starts, table):
    tiles = held // tile
    shift = tile.bit_length() - 1
    low = image_at(images, starts, base)
    high = image_at(images, starts, base + held - 1)

    def bounds(image):
        first = jnp.maximum(starts[image] - base, 0) >> shift
        last = (jnp.minimum(starts[image + 1] - base, held) - 1) >> shift
        return jnp.minimum(first, tiles - 1), last

    pairs = jnp.int32(0)
    for image in range(images):
        first, last = bounds(image)
        wanted = jnp.logical_and(low <= image, image <= high)
        pairs += jnp.where(wanted, last - first + 1, 0)
    at, image = jnp.int32(0), low
    for step in range(tiles + images):
        table[0, step] = at
        table[1, step] = image
        table[2, step] = jnp.minimum(jnp.bitwise_and(starts[image], -LANES), last_begin)
        more = at < bounds(image)[1]
        later = jnp.minimum(image + 1, images - 1)
        at, image = jnp.where(more, at + 1, bounds(later)[0]), jnp.where(more, image, later)
    return pairs


def attend_images(pairs, table, ids_ref, keys, values, queries, attended, work, query_base):
    scores_a, scores_b, tops_a, tops_b = work
    window, tile = scores_a.shape
    size = attended.shape[0] - SPARE

    def window_of(state):
        return pl.ds(pl.multiple_of(table[2, state], LANES), window)

    def score(state, scores, tops):
        query = queries[:, pl.ds(pl.multiple_of(table[0, state] * tile, tile), tile)]
        found = jnp.dot(keys[window_of(state), :], query, preferred_element_type=jnp.float32)
        scores[...] = found
        tops[...] = jnp.max(found, axis=0, keepdims=True)

    def weigh(state, scores, tops):
        first = pl.multiple_of(table[0, state] * tile, tile)
        labels = ids_ref[:, pl.ds(pl.multiple_of(query_base + first, LANES), tile)]
        probs = jnp.exp2((scores[...] - tops[...]) * (size ** (-0.5) * math.log2(math.e)))
        share = 1.0 / jnp.sum(probs, axis=0, keepdims=True)
        weighted = jnp.dot(
            values[:, window_of(state)], probs.astype(jnp.bfloat16), preferred_element_type=jnp.float32
        )
        place = (slice(None), pl.ds(first, tile))
        attended[place] = jnp.where(labels == table[1, state], weighted * share, attended[place])

    def two_pairs(state):
        score(state + 1, scores_b, tops_b)
        weigh(state, scores_a, tops_a)
        score(state + 2, scores_a, tops_a)
        weigh(state + 1, scores_b, tops_b)

    def four_pairs(step, _):
        two_pairs(4 * step)
        two_pairs(4 * step + 2)
        return 0

    score(0, scores_a, tops_a)
    lax.fori_loop(0, pairs >> 2, four_pairs, 0)

    @pl.when(jnp.bitwise_and(pairs, 2) == 2)
    def _():
        two_pairs(jnp.bitwise_and(pairs, -4))

    @pl.when(jnp.bitwise_and(pairs, 1) == 1)
    def _():
        weigh(pairs - 1, scores_a, tops_a)


def turned_keys(marked, block_ref):
    block = block_ref[KEY_AT : KEY_AT + PADDED].astype(jnp.float32)
    nothing = jnp.zeros((LANES - PADDED, block.shape[1]), jnp.float32)
    full = jnp.concatenate([marked, block[SPARE:], nothing], axis=0)
    return full.astype(jnp.bfloat16).T


def store_queries(marked, block_ref, queries, there):
    edge = block_ref[QUERY_AT : QUERY_AT + 16].astype(jnp.float32)
    edge = jnp.concatenate([marked, edge[SPARE:]], axis=0)
    queries[0:16, there] = edge.astype(jnp.bfloat16)
    queries[16:PADDED, there] = block_ref[QUERY_AT + 16 : QUERY_AT + PADDED]
    queries[PADDED:, there] = jnp.zeros((LANES - PADDED, block_ref.shape[1]), jnp.bfloat16)


def prepare_kernel(images, halo, ids_ref, out_weight_ref, *rest):
    got_refs, (keys, marks, before, weight, sems) = rest[: len(EARLY)], rest[len(EARLY) :]
    count = got_refs[0].shape[1]
    fetches = []
    for step, by in enumerate(ORDER):
        head = jnp.bitwise_xor(lax.rem(lax.axis_index("grp"), HEADS), by)
        first = lax.div(head, 2) * (2 * SIZE) + lax.rem(head, 2) * (SIZE - SPARE)
        fetches.append(
            pltpu.make_async_copy(
                out_weight_ref.at[pl.ds(pl.multiple_of(first, 16), PADDED)],
                weight.at[step * PADDED : (step + 1) * PADDED],
                sems.at[step],
            )
        )
        fetches[-1].start()
    before[...] = count_before(images, ids_ref[...])
    write_marks(images, ids_ref[...], marks)
    own = lax.rem(lax.axis_index("grp"), HEADS)
    for step, (by, ref) in enumerate(zip(EARLY, got_refs)):
        first = jnp.bitwise_xor(own, by) * count
        here = pl.ds(pl.multiple_of(halo + first, LANES), count)
        keys[step * count : (step + 1) * count, :] = turned_keys(marks[0, :, here], ref)
    for fetch in fetches:
        fetch.wait()


def attend_kernel(images, piggy, halo, ids_ref, before_ref, marks, early_keys, *rest):
    got_refs, rest = rest[:HEADS], rest[HEADS:]
    if piggy:
        text_ref, *rest = rest
    if halo:
        left_ref, right_ref, *rest = rest
    out_refs, rest = rest[:HEADS], rest[HEADS:]
    keys, values, queries, attended, *work, starts, table = rest
    count = got_refs[0].shape[1]
    padded = attended.shape[0]
    size = padded - SPARE
    total_rows = HEADS * count
    length = ids_ref.shape[1]
    ids = ids_ref[...]
    before = before_ref[...]
    for image in range(images + 1):
        starts[image] = before[image, 0]
    window, tile = work[0].shape
    pairs = list_pairs(images, total_rows, tile, length - window, halo, starts, table)

    own = lax.rem(lax.axis_index("grp"), HEADS)
    for step, (by, ref) in enumerate(zip(EARLY + LATE, got_refs)):
        first = jnp.bitwise_xor(own, by) * count
        here = pl.ds(pl.multiple_of(halo + first, LANES), count)
        there = pl.ds(pl.multiple_of(first, LANES), count)
        if by in EARLY:
            keys[here, :] = early_keys[step * count : (step + 1) * count, :]
        else:
            keys[here, :] = turned_keys(marks[0, :, here], ref)
        values[:, here] = ref[0:PADDED]
        store_queries(marks[1, :, here], ref, queries, there)
    if halo:
        for ref, here in ((left_ref, slice(0, halo)), (right_ref, slice(length - halo, length))):
            keys[here, :] = turned_keys(marks[0, :, here], ref)
            values[:, here] = ref[0:PADDED]
    attend_images(pairs, table, ids_ref, keys, values, queries, attended, work, halo)

    odd_head = lax.rem(own, 2) == 1
    mine = ids[:, halo : halo + total_rows]

    def placed(block, spare):
        even = jnp.concatenate([block[0:size], spare], axis=0)
        odd = jnp.concatenate([spare, block[0:size]], axis=0)
        return jnp.where(odd_head, odd, even)

    if piggy:
        nothing = jnp.zeros((SPARE, total_rows), jnp.float32)
        flat = placed(attended[...], nothing).astype(jnp.bfloat16)
        pooled = lax.dot_general(
            image_rows(mine, images), flat, (((1,), (1,)), ((), ())), preferred_element_type=jnp.float32
        )
        pooled = split_in_two(pooled, images)
        sums = spare_sums(got_refs)
        sums = split_in_two(sums + pltpu.roll(sums, images, axis=0), images)
        spare = jnp.concatenate(
            [pooled, jnp.zeros((SPARE, LANES - padded), jnp.float32), sums], axis=1
        )
        texts = text_ref[...].astype(jnp.float32)
        parts = [texts[:, at : at + count] for at in range(0, texts.shape[1], count)]
        unused = TEXT_ROWS - images * len(parts)
        below = jnp.concatenate(parts + [jnp.zeros((unused, count), jnp.float32)] * (unused > 0), axis=0)
        below = below.astype(jnp.bfloat16)
    else:
        spare = jnp.zeros((SPARE, count), jnp.float32)
    for by, out_ref in zip(ORDER, out_refs):
        there = pl.multiple_of(jnp.bitwise_xor(own, by) * count, LANES)
        out_ref[0:padded] = placed(attended[:, pl.ds(there, count)], spare).astype(jnp.bfloat16)
        if piggy:
            out_ref[padded:] = below


def joined_heads(got_refs, flat):
    own = lax.rem(lax.axis_index("grp"), HEADS)
    spares = []
    for step, (by, got_ref) in enumerate(zip(ORDER, got_refs)):
        odd = lax.rem(jnp.bitwise_xor(own, by), 2)
        at = step * PADDED
        top = got_ref[0:16].astype(jnp.float32)
        bottom = got_ref[PADDED - 16 : PADDED].astype(jnp.float32)
        spares.append(jnp.where(odd == 1, top[:SPARE], bottom[SPARE:]))
        top = jnp.concatenate([jnp.where(odd == 1, 0.0, top[:SPARE]), top[SPARE:]], axis=0)
        bottom = jnp.concatenate([bottom[:SPARE], jnp.where(odd == 1, bottom[SPARE:], 0.0)], axis=0)
        flat[at : at + 16] = top.astype(jnp.bfloat16)
        flat[at + 16 : at + PADDED - 16] = got_ref[16 : PADDED - 16]
        flat[at + PADDED - 16 : at + PADDED] = bottom.astype(jnp.bfloat16)
    return spares


def send_mixed_rows(rows_ref, weight_ref, flat, turned, mixed, mixed_ref, sems, meanwhile=None):
    turned[...] = flat[...].T
    pieces = sems.shape[0]
    step = rows_ref.shape[0] // pieces
    copies, value = [], None
    for piece in range(pieces):
        cut = slice(piece * step, (piece + 1) * step)
        if meanwhile is not None:
            value = meanwhile[piece](value)
        added = jnp.dot(turned[cut, :], weight_ref[...], preferred_element_type=jnp.float32)
        mixed[cut, :] = (rows_ref[cut, :].astype(jnp.float32) + added).astype(jnp.bfloat16)
        copies.append(pltpu.make_async_copy(mixed.at[cut], mixed_ref.at[cut], sems.at[piece]))
        copies[-1].start()
    return copies


def unit_rows(matrix):
    return matrix * lax.rsqrt(jnp.sum(matrix * matrix, axis=1, keepdims=True) + 1e-06)


def losses(cosine, labels):
    logits = -labels * (logit_scale * cosine + logit_bias)
    return jnp.maximum(logits, 0.0) + jnp.log1p(jnp.exp(-jnp.abs(logits)))


def finish_kernel(images, rows_ref, weight_ref, text_ref, *rest):
    got_refs, rest = rest[:HEADS], rest[HEADS:]
    mixed_ref, loss_ref, flat, turned, mixed, sems, pooled_heads, patch_sums, far_texts, loss, loss_sem = rest
    spares = joined_heads(got_refs, flat)
    own = lax.rem(lax.axis_index("grp"), HEADS)
    patch_sums[:, HEADS * LANES :] = spares[0][:, 2 * LANES :]
    for step, (by, spare) in enumerate(zip(ORDER, spares)):
        pooled_heads[:, step * PADDED : (step + 1) * PADDED] = spare[:, 0:PADDED]
        head = jnp.bitwise_xor(own, by)
        patch_sums[:, pl.ds(pl.multiple_of(head * LANES, LANES), LANES)] = spare[:, LANES : 2 * LANES]
        below = got_refs[step][PADDED:].astype(jnp.float32)
        count = below.shape[1]
        for part in range(patch_sums.shape[1] // count):
            here = slice(part * count, (part + 1) * count)
            far_texts[head, :, here] = below[part * images : (part + 1) * images]

    def find_images(_):
        pooled = jnp.dot(
            pooled_heads[...].astype(jnp.bfloat16), weight_ref[...], preferred_element_type=jnp.float32
        )
        pooled = pooled + patch_sums[...]
        others = [far_texts[place] for place in range(lax.axis_size("blk") - 1)]
        texts = jnp.concatenate([text_ref[...].astype(jnp.float32)] + others, axis=0)
        return pooled + pltpu.roll(pooled, images, axis=0), unit_rows(texts)

    def find_cosines(vectors):
        pooled, text_vecs = vectors
        return lax.dot_general(
            text_vecs,
            unit_rows(pooled),
            (((1,), (1,)), ((), ())),
            precision=lax.Precision.HIGHEST,
            preferred_element_type=jnp.float32,
        )

    def find_losses(cosine):
        text = lax.broadcasted_iota(jnp.int32, cosine.shape, 0)
        image = lax.broadcasted_iota(jnp.int32, cosine.shape, 1)
        terms = losses(cosine, jnp.where(text == image, 1.0, -1.0))
        loss[...] = jnp.sum(terms, axis=0, keepdims=True)[:, 0:images]
        loss_copy.start()

    loss_copy = pltpu.make_async_copy(loss, loss_ref, loss_sem)
    meanwhile = (find_images, find_cosines, find_losses)
    copies = send_mixed_rows(rows_ref, weight_ref, flat, turned, mixed, mixed_ref, sems, meanwhile)
    for copy in copies + [loss_copy]:
        copy.wait()


def mix_kernel(rows_ref, weight_ref, *rest):
    got_refs, rest = rest[:HEADS], rest[HEADS:]
    mixed_ref, flat, turned, mixed, sems = rest
    joined_heads(got_refs, flat)
    for copy in send_mixed_rows(rows_ref, weight_ref, flat, turned, mixed, mixed_ref, sems):
        copy.wait()


def in_vmem(count):
    return [pl.BlockSpec(memory_space=pltpu.VMEM)] * count


def in_hbm(value):
    return pltpu.with_memory_space_constraint(value, pltpu.HBM)


def call(kernel, out_shape, scratch, in_specs, flops, out_specs=None):
    if out_specs is None:
        out_specs = jax.tree.map(lambda _: pl.BlockSpec(memory_space=pltpu.VMEM), out_shape)
    return pl.pallas_call(
        kernel,
        out_shape=out_shape,
        in_specs=in_specs,
        out_specs=out_specs,
        scratch_shapes=scratch,
        compiler_params=pltpu.CompilerParams(vmem_limit_bytes=VMEM_LIMIT),
        cost_estimate=pl.CostEstimate(flops=flops, bytes_accessed=8 << 20, transcendentals=0),
    )


def moved(value, axis, pairs):
    return lax.ppermute(value, axis, pairs)


def partner(place, by, peers):
    return place ^ by if peers & (peers - 1) == 0 else (place + by) % peers


def all_texts(texts):
    peers = lax.axis_size("blk")
    steps = [[(partner(i, by, peers), i) for i in range(peers)] for by in range(1, peers)]
    return jnp.concatenate([texts] + [moved(texts, "blk", pairs) for pairs in steps], axis=0)


def one_text_block(texts):
    peers = lax.axis_size("blk")
    pairs = []
    for place in range(lax.axis_size("grp")):
        by = place % (peers - 1) + 1
        pairs += [(place * peers + partner(i, by, peers), place * peers + i) for i in range(peers)]
    return moved(texts, ("grp", "blk"), pairs)


def traded(blocks):
    peers = range(lax.axis_size("grp"))
    trades = {by: moved(blocks[by], "grp", [(i, i ^ by) for i in peers]) for by in ORDER if by}
    return {**trades, 0: blocks[0]}


def local(patches, segment_ids, qkv_weight, out_weight, text_embed):
    rows = patches[0]
    count, depth = rows.shape
    width = out_weight.shape[0]
    size = width // HEADS
    padded = size + SPARE
    images = text_embed.shape[0]
    group_size = lax.axis_size("grp")
    parts = group_size // HEADS
    piggy = (
        parts == 1
        and 2 * images == SPARE
        and count >= depth - (HEADS - 2) * LANES
        and depth % count == 0
        and images * (depth // count) <= TEXT_ROWS
        and 1 < lax.axis_size("blk") <= HEADS + 1
    )
    bf16, f32 = jnp.bfloat16, jnp.float32
    shape = jax.ShapeDtypeStruct

    block = shape((3 * size + SPARE, count), bf16)
    hbm = pl.BlockSpec(memory_space=pltpu.HBM)
    turned_weight = qkv_weight.T
    normed, sums, *sent = call(
        functools.partial(far_kernel, images, piggy),
        (shape((depth, count), bf16), shape((SPARE, depth), f32), block, block),
        [
            pltpu.VMEM((1, count), jnp.int32),
            pltpu.VMEM((count, depth), bf16),
            pltpu.VMEM((3, 2 * size, depth), bf16),
            pltpu.SemaphoreType.DMA,
            pltpu.SemaphoreType.DMA,
            pltpu.SemaphoreType.DMA((3,)),
        ],
        [hbm] * 3,
        2 * count * depth * 6 * size,
    )(in_hbm(segment_ids), in_hbm(rows), in_hbm(turned_weight))
    sent += call(
        functools.partial(near_kernel, piggy),
        (block,) * 6,
        [],
        in_vmem(3),
        2 * count * depth * 18 * size,
    )(normed, sums, turned_weight)
    sent = dict(zip((6, 7, 2, 3, 4, 5, 0, 1), sent))
    if piggy:
        late_texts, sent[0] = lax.optimization_barrier((text_embed, sent[0]))
        halos_and_texts = [one_text_block(late_texts)]
    else:
        halos_and_texts = []
    got = traded(sent)

    length = HEADS * count
    halo = 0
    near_ids = segment_ids
    if parts > 1:
        halo = rounded_up(MAXP - 1, LANES)
        part = lax.axis_index("grp") // HEADS
        whole_ids = jnp.concatenate(
            [
                jnp.full((1, halo), -1, jnp.int32),
                segment_ids,
                jnp.full((1, halo), images, jnp.int32),
            ],
            axis=1,
        )
        near_ids = lax.dynamic_slice_in_dim(whole_ids, part * length, length + 2 * halo, axis=1)
        order = jnp.bitwise_xor(lax.axis_index("grp") % HEADS, jnp.arange(HEADS))
        flat = jnp.stack([got[by] for by in range(HEADS)])[order][:, : 2 * size].transpose(1, 0, 2).reshape(2 * size, length)
        flat = jnp.concatenate([flat, jnp.zeros((16, length), bf16)], axis=0)
        ahead = [(i, i + HEADS) for i in range(group_size - HEADS)]
        back = [(i + HEADS, i) for i in range(group_size - HEADS)]
        left = moved(flat[:, length - halo :], "grp", ahead)
        right = moved(flat[:, :halo], "grp", back)
        halos_and_texts += [left, right]
    reach = length + 2 * halo
    window = min(rounded_up(MAXP + LANES - 1, LANES), reach)
    tile = 2 * LANES
    early_keys, marks, before, weight = call(
        functools.partial(prepare_kernel, images, halo),
        (
            shape((len(EARLY) * count, LANES), bf16),
            shape((2, SPARE, reach), f32),
            shape((rounded_up(images + 1, SPARE), LANES), jnp.int32),
            shape((HEADS * padded, depth), bf16),
        ),
        [pltpu.SemaphoreType.DMA((HEADS,))],
        in_vmem(1) + [hbm] + in_vmem(len(EARLY)),
        1 << 30,
    )(near_ids, in_hbm(out_weight), *[got[by] for by in EARLY])
    operands = [near_ids, before, marks, early_keys, *[got[by] for by in EARLY + LATE], *halos_and_texts]
    answers = call(
        functools.partial(attend_kernel, images, piggy, halo),
        (shape((padded + TEXT_ROWS * piggy, count), bf16),) * HEADS,
        [
            pltpu.VMEM((reach, LANES), bf16),
            pltpu.VMEM((padded, reach), bf16),
            pltpu.VMEM((LANES, length), bf16),
            pltpu.VMEM((padded, length), f32),
            pltpu.VMEM((window, tile), f32),
            pltpu.VMEM((window, tile), f32),
            pltpu.VMEM((1, tile), f32),
            pltpu.VMEM((1, tile), f32),
            pltpu.SMEM((images + 1,), jnp.int32),
            pltpu.SMEM((3, length // tile + images), jnp.int32),
        ],
        in_vmem(len(operands)),
        4 * size * length * MAXP,
    )(*operands)
    home = traded(dict(zip(ORDER, answers)))
    home = [home[by] for by in ORDER]

    joined = [
        pltpu.VMEM((HEADS * padded, count), bf16),
        pltpu.VMEM((count, HEADS * padded), bf16),
        pltpu.VMEM((count, depth), bf16),
        pltpu.SemaphoreType.DMA((3,)),
    ]
    flops = 2 * count * depth * width
    if piggy:
        mixed, row_loss = call(
            functools.partial(finish_kernel, images),
            (shape((count, depth), bf16), shape((1, images), f32)),
            joined
            + [
                pltpu.VMEM((SPARE, HEADS * padded), f32),
                pltpu.VMEM((SPARE, depth), f32),
                pltpu.VMEM((HEADS, images, depth), f32),
                pltpu.VMEM((1, images), f32),
                pltpu.SemaphoreType.DMA,
            ],
            in_vmem(3 + HEADS),
            flops,
            (hbm, hbm),
        )(rows, weight, text_embed, *home)
        return (mixed[None], row_loss[0])
    mixed = call(mix_kernel, shape((count, depth), bf16), joined, in_vmem(2 + HEADS), flops, hbm)(
        rows, weight, *home
    )
    own_ids = lax.dynamic_slice_in_dim(segment_ids[0], lax.axis_index("grp") * count, count)
    onehot = (own_ids[None, :] == jnp.arange(images, dtype=jnp.int32)[:, None]).astype(bf16)
    pooled = lax.psum(jnp.dot(onehot, mixed, preferred_element_type=f32), "grp")
    text_vecs = unit_rows(all_texts(text_embed).astype(f32))
    cosine = jnp.dot(unit_rows(pooled), text_vecs.T, precision=lax.Precision.HIGHEST)
    same = jnp.arange(images)[:, None] == jnp.arange(text_vecs.shape[0])[None, :]
    row_loss = jnp.sum(losses(cosine, jnp.where(same, 1.0, -1.0)), axis=1)
    return (mixed[None], row_loss)


def solution(mesh):
    placed = (P("blk", "grp", None), P("blk", None), P(), P(), P("blk", None))
    return jax.shard_map(
        local,
        mesh=mesh,
        in_specs=placed,
        out_specs=(P("blk", "grp", None), P("blk")),
        check_vma=False,
    )
```

```python
import functools
import math

import jax
import jax.numpy as jnp
from jax import lax
from jax.experimental import pallas as pl
from jax.experimental.pallas import tpu as pltpu
from jax.sharding import PartitionSpec as P

HEADS = 8
MAXP = 1024
LANES = 128
SPARE = 8
SIZE = 72
PADDED = SIZE + SPARE
KEY_AT = SIZE - SPARE
QUERY_AT = 2 * SIZE
TEXT_ROWS = 16
RUN = 5
HIDDEN = -1e30
ORDER = (6, 7, 2, 4, 3, 5, 1, 0)
EARLY = (6, 7, 1, 0)
LATE = (2, 4, 3, 5)

logit_scale = 30.0
logit_bias = -5.0

VMEM_LIMIT = 32 * 1024 * 1024


def rounded_up(value, step):
    return (value + step - 1) // step * step


def split_in_two(total, images):
    row = lax.broadcasted_iota(jnp.int32, total.shape, 0)
    main = total.astype(jnp.bfloat16).astype(jnp.float32)
    return jnp.where(row < images, main, total - main)


def image_rows(ids, images):
    row = lax.broadcasted_iota(jnp.int32, (SPARE, ids.shape[1]), 0)
    return (lax.rem(row, images) == ids).astype(jnp.float32).astype(jnp.bfloat16)


def head_blocks(query, key, value, sums, pair):
    size = query.shape[0] // 2
    count = query.shape[1]
    for place in range(2):
        here = slice(place * size, (place + 1) * size)
        if sums is None:
            spare = jnp.zeros((SPARE, count), jnp.float32)
        else:
            first = pl.multiple_of((2 * pair + place) * LANES, LANES)
            parts = [sums[:, pl.ds(first, LANES)], sums[:, HEADS * LANES :]]
            held = sum(part.shape[1] for part in parts)
            spare = jnp.concatenate(parts + [jnp.zeros((SPARE, count - held), jnp.float32)], axis=1)
        yield jnp.concatenate([value[here], key[here], spare, query[here]], axis=0)


def store_by_core(core, blocks, same_ref, cross_ref):
    first, second = blocks
    same_ref[...] = jnp.where(core == 0, first, second).astype(jnp.bfloat16)
    cross_ref[...] = jnp.where(core == 0, second, first).astype(jnp.bfloat16)


def place_in_group():
    own = lax.rem(lax.axis_index("grp"), HEADS)
    return lax.div(own, 2), lax.rem(own, 2)


def far_kernel(images, piggy, ids_ref, rows_ref, weight_ref, normed_ref, sums_ref, same_ref, cross_ref, own_ids, rows_held, weight, id_sem, row_sems, sems):
    count, depth = rows_ref.shape
    width = weight_ref.shape[0] // 3
    wide = weight.shape[1]
    pieces = row_sems.shape[0]
    step = count // pieces
    row_fetches = []
    for piece in range(pieces):
        cut = slice(piece * step, (piece + 1) * step)
        row_fetches.append(pltpu.make_async_copy(rows_ref.at[cut], rows_held.at[cut], row_sems.at[piece]))
        row_fetches[-1].start()
    own = pl.multiple_of(lax.axis_index("grp") * count, LANES)
    ids_fetch = pltpu.make_async_copy(ids_ref.at[:, pl.ds(own, count)], own_ids, id_sem)
    ids_fetch.start()
    pair, core = place_in_group()
    pair = jnp.bitwise_xor(pair, 3)
    fetches = []
    for at in range(3):
        first = pl.multiple_of(at * width + pair * wide, 16)
        fetches.append(pltpu.make_async_copy(weight_ref.at[pl.ds(first, wide)], weight.at[at], sems.at[at]))
    for fetch in fetches:
        fetch.start()
    ids_fetch.wait()
    for fetch in row_fetches:
        fetch.wait()
    rows = rows_held[...]
    if piggy:
        sums = jnp.dot(image_rows(own_ids[...], images), rows, preferred_element_type=jnp.float32)
        sums_ref[...] = split_in_two(sums, images)
    values = rows.astype(jnp.float32)
    center = values - jnp.mean(values, axis=1, keepdims=True)
    spread = jnp.mean(center * center, axis=1, keepdims=True)
    normed = (center * lax.rsqrt(spread + 1e-06)).astype(jnp.bfloat16)
    normed_ref[...] = normed.T
    for fetch in fetches:
        fetch.wait()
    parts = [
        jnp.dot(weight[at], normed_ref[...], preferred_element_type=jnp.float32) for at in range(3)
    ]
    store_by_core(core, head_blocks(*parts, sums_ref if piggy else None, pair), same_ref, cross_ref)


def near_kernel(piggy, normed_ref, sums_ref, weight_ref, *out_refs):
    width = weight_ref.shape[0] // 3
    wide = 2 * width // HEADS
    own, core = place_in_group()
    for step, move in enumerate((1, 2, 0)):
        pair = jnp.bitwise_xor(own, move)
        parts = []
        for at in range(3):
            here = pl.ds(pl.multiple_of(at * width + pair * wide, 16), wide)
            parts.append(
                jnp.dot(weight_ref[here, :], normed_ref[...], preferred_element_type=jnp.float32)
            )
        blocks = head_blocks(*parts, sums_ref if piggy else None, pair)
        store_by_core(core, blocks, *out_refs[2 * step : 2 * step + 2])


def count_before(images, ids):
    image = lax.broadcasted_iota(jnp.int32, (rounded_up(images + 1, SPARE), ids.shape[1]), 0)
    before = jnp.sum((ids < image).astype(jnp.int32), axis=1, keepdims=True)
    return jnp.broadcast_to(before, (before.shape[0], LANES))


def write_marks(images, ids, marks):
    bits = max(1, (images - 1).bit_length())
    row = lax.broadcasted_iota(jnp.int32, (SPARE, ids.shape[1]), 0)
    bit = jnp.bitwise_and(lax.shift_right_logical(jnp.broadcast_to(ids, row.shape), row >> 1), 1)
    odd = jnp.bitwise_and(row, 1)
    used = row < 2 * bits
    outside = jnp.logical_or(ids < 0, ids >= images)
    key_side = jnp.where(odd == 1, bit, 1 - bit).astype(jnp.float32)
    key_side = jnp.where(outside, 1.0, key_side)
    marks[0] = jnp.where(used, key_side * HIDDEN, 0.0)
    marks[1] = jnp.where(used, jnp.where(odd == 1, 1 - bit, bit), 0).astype(jnp.float32)


def spare_sums(refs):
    parts = [ref[QUERY_AT : QUERY_AT + 16].astype(jnp.float32)[0:SPARE, 0 : 2 * LANES] for ref in refs]
    return sum(parts[1:], parts[0])


def image_at(images, starts, position):
    found = jnp.int32(0)
    for image in range(1, images):
        found += (starts[image] <= position).astype(jnp.int32)
    return found


def list_pairs(images, held, tile, last_begin, base, starts, table):
    tiles = held // tile
    shift = tile.bit_length() - 1
    low = image_at(images, starts, base)
    high = image_at(images, starts, base + held - 1)

    def bounds(image):
        first = jnp.maximum(starts[image] - base, 0) >> shift
        last = (jnp.minimum(starts[image + 1] - base, held) - 1) >> shift
        return jnp.minimum(first, tiles - 1), last

    pairs = jnp.int32(0)
    for image in range(images):
        first, last = bounds(image)
        wanted = jnp.logical_and(low <= image, image <= high)
        pairs += jnp.where(wanted, last - first + 1, 0)
    at, image = jnp.int32(0), low
    for step in range(table.shape[1]):
        table[0, step] = at
        table[1, step] = image
        table[2, step] = jnp.minimum(jnp.bitwise_and(starts[image], -LANES), last_begin)
        more = at < bounds(image)[1]
        later = jnp.minimum(image + 1, images - 1)
        at, image = jnp.where(more, at + 1, bounds(later)[0]), jnp.where(more, image, later)
    return pairs


def attend_images(pairs, table, ids_ref, keys, values, queries, attended, work, query_base):
    work = list(zip(work[0::2], work[1::2]))
    window, tile = work[0][0].shape
    size = attended.shape[0] - SPARE

    def window_of(state):
        return pl.ds(pl.multiple_of(table[2, state], LANES), window)

    def score(state, scores, tops):
        query = queries[:, pl.ds(pl.multiple_of(table[0, state] * tile, tile), tile)]
        found = jnp.dot(keys[window_of(state), :], query, preferred_element_type=jnp.float32)
        scores[...] = found
        tops[...] = jnp.max(found, axis=0, keepdims=True)

    def weigh(state, scores, tops):
        first = pl.multiple_of(table[0, state] * tile, tile)
        labels = ids_ref[:, pl.ds(pl.multiple_of(query_base + first, LANES), tile)]
        probs = jnp.exp2((scores[...] - tops[...]) * (size ** (-0.5) * math.log2(math.e)))
        share = 1.0 / jnp.sum(probs, axis=0, keepdims=True)
        weighted = jnp.dot(
            values[:, window_of(state)], probs.astype(jnp.bfloat16), preferred_element_type=jnp.float32
        )
        place = (slice(None), pl.ds(first, tile))
        attended[place] = jnp.where(labels == table[1, state], weighted * share, attended[place])

    def run(step, _):
        for place in range(RUN):
            state = step * RUN + place
            score(state + 1, *work[(place + 1) % RUN])
            weigh(state, *work[place])
        return 0

    score(0, *work[0])
    lax.fori_loop(0, lax.div(pairs + RUN - 1, RUN), run, 0)


def turned_keys(marked, block_ref):
    block = block_ref[KEY_AT : KEY_AT + PADDED].astype(jnp.float32)
    nothing = jnp.zeros((LANES - PADDED, block.shape[1]), jnp.float32)
    full = jnp.concatenate([marked, block[SPARE:], nothing], axis=0)
    return full.astype(jnp.bfloat16).T


def store_queries(marked, block_ref, queries, there):
    edge = block_ref[QUERY_AT : QUERY_AT + 16].astype(jnp.float32)
    edge = jnp.concatenate([marked, edge[SPARE:]], axis=0)
    queries[0:16, there] = edge.astype(jnp.bfloat16)
    queries[16:PADDED, there] = block_ref[QUERY_AT + 16 : QUERY_AT + PADDED]
    queries[PADDED:, there] = jnp.zeros((LANES - PADDED, block_ref.shape[1]), jnp.bfloat16)


def prepare_kernel(images, halo, ids_ref, out_weight_ref, *rest):
    got_refs, (keys, marks, before, weight, sems) = rest[: len(EARLY)], rest[len(EARLY) :]
    count = got_refs[0].shape[1]
    fetches = []
    for step, by in enumerate(ORDER):
        head = jnp.bitwise_xor(lax.rem(lax.axis_index("grp"), HEADS), by)
        first = lax.div(head, 2) * (2 * SIZE) + lax.rem(head, 2) * (SIZE - SPARE)
        fetches.append(
            pltpu.make_async_copy(
                out_weight_ref.at[pl.ds(pl.multiple_of(first, 16), PADDED)],
                weight.at[step * PADDED : (step + 1) * PADDED],
                sems.at[step],
            )
        )
        fetches[-1].start()
    before[...] = count_before(images, ids_ref[...])
    write_marks(images, ids_ref[...], marks)
    own = lax.rem(lax.axis_index("grp"), HEADS)
    for step, (by, ref) in enumerate(zip(EARLY, got_refs)):
        first = jnp.bitwise_xor(own, by) * count
        here = pl.ds(pl.multiple_of(halo + first, LANES), count)
        keys[step * count : (step + 1) * count, :] = turned_keys(marks[0, :, here], ref)
    for fetch in fetches:
        fetch.wait()


def attend_kernel(images, piggy, halo, ids_ref, before_ref, marks, early_keys, *rest):
    got_refs, rest = rest[:HEADS], rest[HEADS:]
    if piggy:
        text_ref, *rest = rest
    if halo:
        left_ref, right_ref, *rest = rest
    out_refs, rest = rest[:HEADS], rest[HEADS:]
    keys, values, queries, attended, *work, starts, table = rest
    count = got_refs[0].shape[1]
    padded = attended.shape[0]
    size = padded - SPARE
    total_rows = HEADS * count
    length = ids_ref.shape[1]
    ids = ids_ref[...]
    before = before_ref[...]
    for image in range(images + 1):
        starts[image] = before[image, 0]
    window, tile = work[0].shape
    pairs = list_pairs(images, total_rows, tile, length - window, halo, starts, table)

    own = lax.rem(lax.axis_index("grp"), HEADS)
    for step, (by, ref) in enumerate(zip(EARLY + LATE, got_refs)):
        first = jnp.bitwise_xor(own, by) * count
        here = pl.ds(pl.multiple_of(halo + first, LANES), count)
        there = pl.ds(pl.multiple_of(first, LANES), count)
        if by in EARLY:
            keys[here, :] = early_keys[step * count : (step + 1) * count, :]
        else:
            keys[here, :] = turned_keys(marks[0, :, here], ref)
        values[:, here] = ref[0:PADDED]
        store_queries(marks[1, :, here], ref, queries, there)
    if halo:
        for ref, here in ((left_ref, slice(0, halo)), (right_ref, slice(length - halo, length))):
            keys[here, :] = turned_keys(marks[0, :, here], ref)
            values[:, here] = ref[0:PADDED]
    attend_images(pairs, table, ids_ref, keys, values, queries, attended, work, halo)

    odd_head = lax.rem(own, 2) == 1
    mine = ids[:, halo : halo + total_rows]

    def placed(block, spare):
        even = jnp.concatenate([block[0:size], spare], axis=0)
        odd = jnp.concatenate([spare, block[0:size]], axis=0)
        return jnp.where(odd_head, odd, even)

    if piggy:
        nothing = jnp.zeros((SPARE, total_rows), jnp.float32)
        flat = placed(attended[...], nothing).astype(jnp.bfloat16)
        pooled = lax.dot_general(
            image_rows(mine, images), flat, (((1,), (1,)), ((), ())), preferred_element_type=jnp.float32
        )
        pooled = split_in_two(pooled, images)
        sums = spare_sums(got_refs)
        sums = split_in_two(sums + pltpu.roll(sums, images, axis=0), images)
        spare = jnp.concatenate(
            [pooled, jnp.zeros((SPARE, LANES - padded), jnp.float32), sums], axis=1
        )
        texts = text_ref[...].astype(jnp.float32)
        parts = [texts[:, at : at + count] for at in range(0, texts.shape[1], count)]
        unused = TEXT_ROWS - images * len(parts)
        below = jnp.concatenate(parts + [jnp.zeros((unused, count), jnp.float32)] * (unused > 0), axis=0)
        below = below.astype(jnp.bfloat16)
    else:
        spare = jnp.zeros((SPARE, count), jnp.float32)
    for by, out_ref in zip(ORDER, out_refs):
        there = pl.multiple_of(jnp.bitwise_xor(own, by) * count, LANES)
        out_ref[0:padded] = placed(attended[:, pl.ds(there, count)], spare).astype(jnp.bfloat16)
        if piggy:
            out_ref[padded:] = below


def joined_heads(got_refs, flat):
    own = lax.rem(lax.axis_index("grp"), HEADS)
    spares = []
    for step, (by, got_ref) in enumerate(zip(ORDER, got_refs)):
        odd = lax.rem(jnp.bitwise_xor(own, by), 2)
        at = step * PADDED
        top = got_ref[0:16].astype(jnp.float32)
        bottom = got_ref[PADDED - 16 : PADDED].astype(jnp.float32)
        spares.append(jnp.where(odd == 1, top[:SPARE], bottom[SPARE:]))
        top = jnp.concatenate([jnp.where(odd == 1, 0.0, top[:SPARE]), top[SPARE:]], axis=0)
        bottom = jnp.concatenate([bottom[:SPARE], jnp.where(odd == 1, bottom[SPARE:], 0.0)], axis=0)
        flat[at : at + 16] = top.astype(jnp.bfloat16)
        flat[at + 16 : at + PADDED - 16] = got_ref[16 : PADDED - 16]
        flat[at + PADDED - 16 : at + PADDED] = bottom.astype(jnp.bfloat16)
    return spares


def send_mixed_rows(rows_ref, weight_ref, flat, turned, mixed, mixed_ref, sems, meanwhile=None):
    turned[...] = flat[...].T
    pieces = sems.shape[0]
    step = rows_ref.shape[0] // pieces
    copies, value = [], None
    for piece in range(pieces):
        cut = slice(piece * step, (piece + 1) * step)
        if meanwhile is not None:
            value = meanwhile[piece](value)
        added = jnp.dot(turned[cut, :], weight_ref[...], preferred_element_type=jnp.float32)
        mixed[cut, :] = (rows_ref[cut, :].astype(jnp.float32) + added).astype(jnp.bfloat16)
        copies.append(pltpu.make_async_copy(mixed.at[cut], mixed_ref.at[cut], sems.at[piece]))
        copies[-1].start()
    return copies


def unit_rows(matrix):
    return matrix * lax.rsqrt(jnp.sum(matrix * matrix, axis=1, keepdims=True) + 1e-06)


def losses(cosine, labels):
    logits = -labels * (logit_scale * cosine + logit_bias)
    return jnp.maximum(logits, 0.0) + jnp.log1p(jnp.exp(-jnp.abs(logits)))


def finish_kernel(images, rows_ref, weight_ref, text_ref, *rest):
    got_refs, rest = rest[:HEADS], rest[HEADS:]
    mixed_ref, loss_ref, flat, turned, mixed, sems, pooled_heads, patch_sums, far_texts, loss, loss_sem = rest
    spares = joined_heads(got_refs, flat)
    own = lax.rem(lax.axis_index("grp"), HEADS)
    patch_sums[:, HEADS * LANES :] = spares[0][:, 2 * LANES :]
    for step, (by, spare) in enumerate(zip(ORDER, spares)):
        pooled_heads[:, step * PADDED : (step + 1) * PADDED] = spare[:, 0:PADDED]
        head = jnp.bitwise_xor(own, by)
        patch_sums[:, pl.ds(pl.multiple_of(head * LANES, LANES), LANES)] = spare[:, LANES : 2 * LANES]
        below = got_refs[step][PADDED:].astype(jnp.float32)
        count = below.shape[1]
        for part in range(patch_sums.shape[1] // count):
            here = slice(part * count, (part + 1) * count)
            far_texts[head, :, here] = below[part * images : (part + 1) * images]

    def find_images(_):
        pooled = jnp.dot(
            pooled_heads[...].astype(jnp.bfloat16), weight_ref[...], preferred_element_type=jnp.float32
        )
        pooled = pooled + patch_sums[...]
        others = [far_texts[place] for place in range(lax.axis_size("blk") - 1)]
        texts = jnp.concatenate([text_ref[...].astype(jnp.float32)] + others, axis=0)
        return pooled + pltpu.roll(pooled, images, axis=0), unit_rows(texts)

    def find_cosines(vectors):
        pooled, text_vecs = vectors
        return lax.dot_general(
            text_vecs,
            unit_rows(pooled),
            (((1,), (1,)), ((), ())),
            precision=lax.Precision.HIGHEST,
            preferred_element_type=jnp.float32,
        )

    def find_losses(cosine):
        text = lax.broadcasted_iota(jnp.int32, cosine.shape, 0)
        image = lax.broadcasted_iota(jnp.int32, cosine.shape, 1)
        terms = losses(cosine, jnp.where(text == image, 1.0, -1.0))
        loss[...] = jnp.sum(terms, axis=0, keepdims=True)[:, 0:images]
        loss_copy.start()

    loss_copy = pltpu.make_async_copy(loss, loss_ref, loss_sem)
    meanwhile = (find_images, find_cosines, find_losses)
    copies = send_mixed_rows(rows_ref, weight_ref, flat, turned, mixed, mixed_ref, sems, meanwhile)
    for copy in copies + [loss_copy]:
        copy.wait()


def mix_kernel(rows_ref, weight_ref, *rest):
    got_refs, rest = rest[:HEADS], rest[HEADS:]
    mixed_ref, flat, turned, mixed, sems = rest
    joined_heads(got_refs, flat)
    for copy in send_mixed_rows(rows_ref, weight_ref, flat, turned, mixed, mixed_ref, sems):
        copy.wait()


def in_vmem(count):
    return [pl.BlockSpec(memory_space=pltpu.VMEM)] * count


def in_hbm(value):
    return pltpu.with_memory_space_constraint(value, pltpu.HBM)


def call(kernel, out_shape, scratch, in_specs, flops, out_specs=None):
    if out_specs is None:
        out_specs = jax.tree.map(lambda _: pl.BlockSpec(memory_space=pltpu.VMEM), out_shape)
    return pl.pallas_call(
        kernel,
        out_shape=out_shape,
        in_specs=in_specs,
        out_specs=out_specs,
        scratch_shapes=scratch,
        compiler_params=pltpu.CompilerParams(vmem_limit_bytes=VMEM_LIMIT),
        cost_estimate=pl.CostEstimate(flops=flops, bytes_accessed=8 << 20, transcendentals=0),
    )


def moved(value, axis, pairs):
    return lax.ppermute(value, axis, pairs)


def partner(place, by, peers):
    return place ^ by if peers & (peers - 1) == 0 else (place + by) % peers


def all_texts(texts):
    peers = lax.axis_size("blk")
    steps = [[(partner(i, by, peers), i) for i in range(peers)] for by in range(1, peers)]
    return jnp.concatenate([texts] + [moved(texts, "blk", pairs) for pairs in steps], axis=0)


def one_text_block(texts):
    peers = lax.axis_size("blk")
    pairs = []
    for place in range(lax.axis_size("grp")):
        by = place % (peers - 1) + 1
        pairs += [(place * peers + partner(i, by, peers), place * peers + i) for i in range(peers)]
    return moved(texts, ("grp", "blk"), pairs)


def traded(blocks):
    peers = range(lax.axis_size("grp"))
    trades = {by: moved(blocks[by], "grp", [(i, i ^ by) for i in peers]) for by in ORDER if by}
    return {**trades, 0: blocks[0]}


def local(patches, segment_ids, qkv_weight, out_weight, text_embed):
    rows = patches[0]
    count, depth = rows.shape
    width = out_weight.shape[0]
    size = width // HEADS
    padded = size + SPARE
    images = text_embed.shape[0]
    group_size = lax.axis_size("grp")
    parts = group_size // HEADS
    piggy = (
        parts == 1
        and 2 * images == SPARE
        and count >= depth - (HEADS - 2) * LANES
        and depth % count == 0
        and images * (depth // count) <= TEXT_ROWS
        and 1 < lax.axis_size("blk") <= HEADS + 1
    )
    bf16, f32 = jnp.bfloat16, jnp.float32
    shape = jax.ShapeDtypeStruct

    block = shape((3 * size + SPARE, count), bf16)
    hbm = pl.BlockSpec(memory_space=pltpu.HBM)
    turned_weight = qkv_weight.T
    normed, sums, *sent = call(
        functools.partial(far_kernel, images, piggy),
        (shape((depth, count), bf16), shape((SPARE, depth), f32), block, block),
        [
            pltpu.VMEM((1, count), jnp.int32),
            pltpu.VMEM((count, depth), bf16),
            pltpu.VMEM((3, 2 * size, depth), bf16),
            pltpu.SemaphoreType.DMA,
            pltpu.SemaphoreType.DMA((3,)),
            pltpu.SemaphoreType.DMA((3,)),
        ],
        [hbm] * 3,
        2 * count * depth * 6 * size,
    )(in_hbm(segment_ids), in_hbm(rows), in_hbm(turned_weight))
    sent += call(
        functools.partial(near_kernel, piggy),
        (block,) * 6,
        [],
        in_vmem(3),
        2 * count * depth * 18 * size,
    )(normed, sums, turned_weight)
    sent = dict(zip((6, 7, 2, 3, 4, 5, 0, 1), sent))
    if piggy:
        late_texts, sent[0] = lax.optimization_barrier((text_embed, sent[0]))
        halos_and_texts = [one_text_block(late_texts)]
    else:
        halos_and_texts = []
    got = traded(sent)

    length = HEADS * count
    halo = 0
    near_ids = segment_ids
    if parts > 1:
        halo = rounded_up(MAXP - 1, LANES)
        part = lax.axis_index("grp") // HEADS
        whole_ids = jnp.concatenate(
            [
                jnp.full((1, halo), -1, jnp.int32),
                segment_ids,
                jnp.full((1, halo), images, jnp.int32),
            ],
            axis=1,
        )
        near_ids = lax.dynamic_slice_in_dim(whole_ids, part * length, length + 2 * halo, axis=1)
        order = jnp.bitwise_xor(lax.axis_index("grp") % HEADS, jnp.arange(HEADS))
        flat = jnp.stack([got[by] for by in range(HEADS)])[order][:, : 2 * size].transpose(1, 0, 2).reshape(2 * size, length)
        flat = jnp.concatenate([flat, jnp.zeros((16, length), bf16)], axis=0)
        ahead = [(i, i + HEADS) for i in range(group_size - HEADS)]
        back = [(i + HEADS, i) for i in range(group_size - HEADS)]
        left = moved(flat[:, length - halo :], "grp", ahead)
        right = moved(flat[:, :halo], "grp", back)
        halos_and_texts += [left, right]
    reach = length + 2 * halo
    window = min(rounded_up(MAXP + LANES - 1, LANES), reach)
    tile = 2 * LANES
    early_keys, marks, before, weight = call(
        functools.partial(prepare_kernel, images, halo),
        (
            shape((len(EARLY) * count, LANES), bf16),
            shape((2, SPARE, reach), f32),
            shape((rounded_up(images + 1, SPARE), LANES), jnp.int32),
            shape((HEADS * padded, depth), bf16),
        ),
        [pltpu.SemaphoreType.DMA((HEADS,))],
        in_vmem(1) + [hbm] + in_vmem(len(EARLY)),
        1 << 30,
    )(near_ids, in_hbm(out_weight), *[got[by] for by in EARLY])
    operands = [near_ids, before, marks, early_keys, *[got[by] for by in EARLY + LATE], *halos_and_texts]
    answers = call(
        functools.partial(attend_kernel, images, piggy, halo),
        (shape((padded + TEXT_ROWS * piggy, count), bf16),) * HEADS,
        [
            pltpu.VMEM((reach, LANES), bf16),
            pltpu.VMEM((padded, reach), bf16),
            pltpu.VMEM((LANES, length), bf16),
            pltpu.VMEM((padded, length), f32),
        ]
        + [pltpu.VMEM((window, tile), f32), pltpu.VMEM((1, tile), f32)] * RUN
        + [
            pltpu.SMEM((images + 1,), jnp.int32),
            pltpu.SMEM((3, rounded_up(length // tile + images, RUN) + 1), jnp.int32),
        ],
        in_vmem(len(operands)),
        4 * size * length * MAXP,
    )(*operands)
    home = traded(dict(zip(ORDER, answers)))
    home = [home[by] for by in ORDER]

    joined = [
        pltpu.VMEM((HEADS * padded, count), bf16),
        pltpu.VMEM((count, HEADS * padded), bf16),
        pltpu.VMEM((count, depth), bf16),
        pltpu.SemaphoreType.DMA((3,)),
    ]
    flops = 2 * count * depth * width
    if piggy:
        mixed, row_loss = call(
            functools.partial(finish_kernel, images),
            (shape((count, depth), bf16), shape((1, images), f32)),
            joined
            + [
                pltpu.VMEM((SPARE, HEADS * padded), f32),
                pltpu.VMEM((SPARE, depth), f32),
                pltpu.VMEM((HEADS, images, depth), f32),
                pltpu.VMEM((1, images), f32),
                pltpu.SemaphoreType.DMA,
            ],
            in_vmem(3 + HEADS),
            flops,
            (hbm, hbm),
        )(rows, weight, text_embed, *home)
        return (mixed[None], row_loss[0])
    mixed = call(mix_kernel, shape((count, depth), bf16), joined, in_vmem(2 + HEADS), flops, hbm)(
        rows, weight, *home
    )
    own_ids = lax.dynamic_slice_in_dim(segment_ids[0], lax.axis_index("grp") * count, count)
    onehot = (own_ids[None, :] == jnp.arange(images, dtype=jnp.int32)[:, None]).astype(bf16)
    pooled = lax.psum(jnp.dot(onehot, mixed, preferred_element_type=f32), "grp")
    text_vecs = unit_rows(all_texts(text_embed).astype(f32))
    cosine = jnp.dot(unit_rows(pooled), text_vecs.T, precision=lax.Precision.HIGHEST)
    same = jnp.arange(images)[:, None] == jnp.arange(text_vecs.shape[0])[None, :]
    row_loss = jnp.sum(losses(cosine, jnp.where(same, 1.0, -1.0)), axis=1)
    return (mixed[None], row_loss)


def solution(mesh):
    placed = (P("blk", "grp", None), P("blk", None), P(), P(), P("blk", None))
    return jax.shard_map(
        local,
        mesh=mesh,
        in_specs=placed,
        out_specs=(P("blk", "grp", None), P("blk")),
        check_vma=False,
    )
```

```python
import functools
import math

import jax
import jax.numpy as jnp
from jax import lax
from jax.experimental import pallas as pl
from jax.experimental.pallas import tpu as pltpu
from jax.sharding import PartitionSpec as P

HEADS = 8
MAXP = 1024
LANES = 128
SPARE = 8
SIZE = 72
PADDED = SIZE + SPARE
KEY_AT = SIZE - SPARE
QUERY_AT = 2 * SIZE
TEXT_ROWS = 16
RUN = 5
HIDDEN = -1e30
ORDER = (6, 7, 2, 4, 3, 5, 1, 0)
EARLY = (6, 7, 1, 0)
LATE = (2, 4, 3, 5)

logit_scale = 30.0
logit_bias = -5.0

VMEM_LIMIT = 32 * 1024 * 1024


def rounded_up(value, step):
    return (value + step - 1) // step * step


def split_in_two(total, images):
    row = lax.broadcasted_iota(jnp.int32, total.shape, 0)
    main = total.astype(jnp.bfloat16).astype(jnp.float32)
    return jnp.where(row < images, main, total - main)


def image_rows(ids, images):
    row = lax.broadcasted_iota(jnp.int32, (SPARE, ids.shape[1]), 0)
    return (lax.rem(row, images) == ids).astype(jnp.float32).astype(jnp.bfloat16)


def head_blocks(query, key, value, sums, pair):
    size = query.shape[0] // 2
    count = query.shape[1]
    for place in range(2):
        here = slice(place * size, (place + 1) * size)
        if sums is None:
            spare = jnp.zeros((SPARE, count), jnp.float32)
        else:
            first = pl.multiple_of((2 * pair + place) * LANES, LANES)
            parts = [sums[:, pl.ds(first, LANES)], sums[:, HEADS * LANES :]]
            held = sum(part.shape[1] for part in parts)
            spare = jnp.concatenate(parts + [jnp.zeros((SPARE, count - held), jnp.float32)], axis=1)
        yield jnp.concatenate([value[here], key[here], spare, query[here]], axis=0)


def store_by_core(core, blocks, same_ref, cross_ref):
    first, second = blocks
    same_ref[...] = jnp.where(core == 0, first, second).astype(jnp.bfloat16)
    cross_ref[...] = jnp.where(core == 0, second, first).astype(jnp.bfloat16)


def place_in_group():
    own = lax.rem(lax.axis_index("grp"), HEADS)
    return lax.div(own, 2), lax.rem(own, 2)


def far_kernel(images, piggy, ids_ref, rows_ref, weight_ref, normed_ref, sums_ref, same_ref, cross_ref, own_ids, rows_held, weight, id_sem, row_sems, sems):
    count, depth = rows_ref.shape
    width = weight_ref.shape[0] // 3
    wide = weight.shape[1]
    pieces = row_sems.shape[0]
    step = count // pieces
    row_fetches = []
    for piece in range(pieces):
        cut = slice(piece * step, (piece + 1) * step)
        row_fetches.append(pltpu.make_async_copy(rows_ref.at[cut], rows_held.at[cut], row_sems.at[piece]))
        row_fetches[-1].start()
    own = pl.multiple_of(lax.axis_index("grp") * count, LANES)
    ids_fetch = pltpu.make_async_copy(ids_ref.at[:, pl.ds(own, count)], own_ids, id_sem)
    ids_fetch.start()
    pair, core = place_in_group()
    pair = jnp.bitwise_xor(pair, 3)
    fetches = []
    for at in range(3):
        first = pl.multiple_of(at * width + pair * wide, 16)
        fetches.append(pltpu.make_async_copy(weight_ref.at[pl.ds(first, wide)], weight.at[at], sems.at[at]))
    for fetch in fetches:
        fetch.start()
    ids_fetch.wait()
    for fetch in row_fetches:
        fetch.wait()
    rows = rows_held[...]
    if piggy:
        sums = jnp.dot(image_rows(own_ids[...], images), rows, preferred_element_type=jnp.float32)
        sums_ref[...] = split_in_two(sums, images)
    values = rows.astype(jnp.float32)
    center = values - jnp.mean(values, axis=1, keepdims=True)
    spread = jnp.mean(center * center, axis=1, keepdims=True)
    normed = (center * lax.rsqrt(spread + 1e-06)).astype(jnp.bfloat16)
    normed_ref[...] = normed.T
    for fetch in fetches:
        fetch.wait()
    parts = [
        jnp.dot(weight[at], normed_ref[...], preferred_element_type=jnp.float32) for at in range(3)
    ]
    store_by_core(core, head_blocks(*parts, sums_ref if piggy else None, pair), same_ref, cross_ref)


def near_kernel(piggy, normed_ref, sums_ref, weight_ref, *out_refs):
    width = weight_ref.shape[0] // 3
    wide = 2 * width // HEADS
    own, core = place_in_group()
    for step, move in enumerate((1, 2, 0)):
        pair = jnp.bitwise_xor(own, move)
        parts = []
        for at in range(3):
            here = pl.ds(pl.multiple_of(at * width + pair * wide, 16), wide)
            parts.append(
                jnp.dot(weight_ref[here, :], normed_ref[...], preferred_element_type=jnp.float32)
            )
        blocks = head_blocks(*parts, sums_ref if piggy else None, pair)
        store_by_core(core, blocks, *out_refs[2 * step : 2 * step + 2])


def count_before(images, ids):
    image = lax.broadcasted_iota(jnp.int32, (rounded_up(images + 1, SPARE), ids.shape[1]), 0)
    before = jnp.sum((ids < image).astype(jnp.int32), axis=1, keepdims=True)
    return jnp.broadcast_to(before, (before.shape[0], LANES))


def write_marks(images, ids, marks):
    bits = max(1, (images - 1).bit_length())
    row = lax.broadcasted_iota(jnp.int32, (SPARE, ids.shape[1]), 0)
    bit = jnp.bitwise_and(lax.shift_right_logical(jnp.broadcast_to(ids, row.shape), row >> 1), 1)
    odd = jnp.bitwise_and(row, 1)
    used = row < 2 * bits
    outside = jnp.logical_or(ids < 0, ids >= images)
    key_side = jnp.where(odd == 1, bit, 1 - bit).astype(jnp.float32)
    key_side = jnp.where(outside, 1.0, key_side)
    marks[0] = jnp.where(used, key_side * HIDDEN, 0.0)
    marks[1] = jnp.where(used, jnp.where(odd == 1, 1 - bit, bit), 0).astype(jnp.float32)


def spare_sums(refs):
    parts = [ref[QUERY_AT : QUERY_AT + 16].astype(jnp.float32)[0:SPARE, 0 : 2 * LANES] for ref in refs]
    return sum(parts[1:], parts[0])


def image_at(images, starts, position):
    found = jnp.int32(0)
    for image in range(1, images):
        found += (starts[image] <= position).astype(jnp.int32)
    return found


def list_pairs(images, held, tile, last_begin, base, starts, table):
    tiles = held // tile
    shift = tile.bit_length() - 1
    low = image_at(images, starts, base)
    high = image_at(images, starts, base + held - 1)

    def bounds(image):
        first = jnp.maximum(starts[image] - base, 0) >> shift
        last = (jnp.minimum(starts[image + 1] - base, held) - 1) >> shift
        return jnp.minimum(first, tiles - 1), last

    pairs = jnp.int32(0)
    for image in range(images):
        first, last = bounds(image)
        wanted = jnp.logical_and(low <= image, image <= high)
        pairs += jnp.where(wanted, last - first + 1, 0)
    at, image = jnp.int32(0), low
    for step in range(table.shape[1]):
        table[0, step] = at
        table[1, step] = image
        table[2, step] = jnp.minimum(jnp.bitwise_and(starts[image], -LANES), last_begin)
        more = at < bounds(image)[1]
        later = jnp.minimum(image + 1, images - 1)
        at, image = jnp.where(more, at + 1, bounds(later)[0]), jnp.where(more, image, later)
    return pairs


def attend_images(pairs, table, ids_ref, keys, values, queries, attended, work, query_base):
    work = list(zip(work[:RUN], work[RUN:]))
    window, tile = work[0][0].shape
    size = attended.shape[0] - SPARE

    def window_of(state):
        return pl.ds(pl.multiple_of(table[2, state], LANES), window)

    def score(state, scores, tops):
        query = queries[:, pl.ds(pl.multiple_of(table[0, state] * tile, tile), tile)]
        found = jnp.dot(keys[window_of(state), :], query, preferred_element_type=jnp.float32)
        scores[...] = found
        tops[...] = jnp.max(found, axis=0, keepdims=True)

    def weigh(state, scores, tops):
        first = pl.multiple_of(table[0, state] * tile, tile)
        labels = ids_ref[:, pl.ds(pl.multiple_of(query_base + first, LANES), tile)]
        probs = jnp.exp2((scores[...] - tops[...]) * (size ** (-0.5) * math.log2(math.e)))
        share = 1.0 / jnp.sum(probs, axis=0, keepdims=True)
        weighted = jnp.dot(
            values[:, window_of(state)], probs.astype(jnp.bfloat16), preferred_element_type=jnp.float32
        )
        place = (slice(None), pl.ds(first, tile))
        attended[place] = jnp.where(labels == table[1, state], weighted * share, attended[place])

    def run(step, _):
        for place in range(RUN):
            state = step * RUN + place
            score(state + 1, *work[(place + 1) % RUN])
            weigh(state, *work[place])
        return 0

    score(0, *work[0])
    lax.fori_loop(0, lax.div(pairs + RUN - 1, RUN), run, 0)


def turned_keys(marked, block_ref):
    block = block_ref[KEY_AT : KEY_AT + PADDED].astype(jnp.float32)
    nothing = jnp.zeros((LANES - PADDED, block.shape[1]), jnp.float32)
    full = jnp.concatenate([marked, block[SPARE:], nothing], axis=0)
    return full.astype(jnp.bfloat16).T


def store_queries(marked, block_ref, queries, there):
    edge = block_ref[QUERY_AT : QUERY_AT + 16].astype(jnp.float32)
    edge = jnp.concatenate([marked, edge[SPARE:]], axis=0)
    queries[0:16, there] = edge.astype(jnp.bfloat16)
    queries[16:PADDED, there] = block_ref[QUERY_AT + 16 : QUERY_AT + PADDED]
    queries[PADDED:, there] = jnp.zeros((LANES - PADDED, block_ref.shape[1]), jnp.bfloat16)


def prepare_kernel(images, halo, ids_ref, out_weight_ref, *rest):
    got_refs, (keys, marks, before, weight, sems) = rest[: len(EARLY)], rest[len(EARLY) :]
    count = got_refs[0].shape[1]
    fetches = []
    for step, by in enumerate(ORDER):
        head = jnp.bitwise_xor(lax.rem(lax.axis_index("grp"), HEADS), by)
        first = lax.div(head, 2) * (2 * SIZE) + lax.rem(head, 2) * (SIZE - SPARE)
        fetches.append(
            pltpu.make_async_copy(
                out_weight_ref.at[pl.ds(pl.multiple_of(first, 16), PADDED)],
                weight.at[step * PADDED : (step + 1) * PADDED],
                sems.at[step],
            )
        )
        fetches[-1].start()
    before[...] = count_before(images, ids_ref[...])
    write_marks(images, ids_ref[...], marks)
    own = lax.rem(lax.axis_index("grp"), HEADS)
    for step, (by, ref) in enumerate(zip(EARLY, got_refs)):
        first = jnp.bitwise_xor(own, by) * count
        here = pl.ds(pl.multiple_of(halo + first, LANES), count)
        keys[step * count : (step + 1) * count, :] = turned_keys(marks[0, :, here], ref)
    for fetch in fetches:
        fetch.wait()


def attend_kernel(images, piggy, halo, ids_ref, before_ref, marks, early_keys, *rest):
    got_refs, rest = rest[:HEADS], rest[HEADS:]
    if piggy:
        text_ref, *rest = rest
    if halo:
        left_ref, right_ref, *rest = rest
    out_refs, rest = rest[:HEADS], rest[HEADS:]
    keys, values, queries, attended, *work, starts, table = rest
    count = got_refs[0].shape[1]
    padded = attended.shape[0]
    size = padded - SPARE
    total_rows = HEADS * count
    length = ids_ref.shape[1]
    ids = ids_ref[...]
    before = before_ref[...]
    for image in range(images + 1):
        starts[image] = before[image, 0]
    window, tile = work[0].shape
    pairs = list_pairs(images, total_rows, tile, length - window, halo, starts, table)

    own = lax.rem(lax.axis_index("grp"), HEADS)
    for step, (by, ref) in enumerate(zip(EARLY + LATE, got_refs)):
        first = jnp.bitwise_xor(own, by) * count
        here = pl.ds(pl.multiple_of(halo + first, LANES), count)
        there = pl.ds(pl.multiple_of(first, LANES), count)
        if by in EARLY:
            keys[here, :] = early_keys[step * count : (step + 1) * count, :]
        else:
            keys[here, :] = turned_keys(marks[0, :, here], ref)
        values[:, here] = ref[0:PADDED]
        store_queries(marks[1, :, here], ref, queries, there)
    if halo:
        for ref, here in ((left_ref, slice(0, halo)), (right_ref, slice(length - halo, length))):
            keys[here, :] = turned_keys(marks[0, :, here], ref)
            values[:, here] = ref[0:PADDED]
    attend_images(pairs, table, ids_ref, keys, values, queries, attended, work, halo)

    odd_head = lax.rem(own, 2) == 1
    mine = ids[:, halo : halo + total_rows]

    def placed(block, spare):
        even = jnp.concatenate([block[0:size], spare], axis=0)
        odd = jnp.concatenate([spare, block[0:size]], axis=0)
        return jnp.where(odd_head, odd, even)

    if piggy:
        nothing = jnp.zeros((SPARE, total_rows), jnp.float32)
        flat = placed(attended[...], nothing).astype(jnp.bfloat16)
        pooled = lax.dot_general(
            image_rows(mine, images), flat, (((1,), (1,)), ((), ())), preferred_element_type=jnp.float32
        )
        pooled = split_in_two(pooled, images)
        sums = spare_sums(got_refs)
        sums = split_in_two(sums + pltpu.roll(sums, images, axis=0), images)
        spare = jnp.concatenate(
            [pooled, jnp.zeros((SPARE, LANES - padded), jnp.float32), sums], axis=1
        )
        texts = text_ref[...].astype(jnp.float32)
        parts = [texts[:, at : at + count] for at in range(0, texts.shape[1], count)]
        unused = TEXT_ROWS - images * len(parts)
        below = jnp.concatenate(parts + [jnp.zeros((unused, count), jnp.float32)] * (unused > 0), axis=0)
        below = below.astype(jnp.bfloat16)
    else:
        spare = jnp.zeros((SPARE, count), jnp.float32)
    for by, out_ref in zip(ORDER, out_refs):
        there = pl.multiple_of(jnp.bitwise_xor(own, by) * count, LANES)
        out_ref[0:padded] = placed(attended[:, pl.ds(there, count)], spare).astype(jnp.bfloat16)
        if piggy:
            out_ref[padded:] = below


def joined_heads(got_refs, flat):
    own = lax.rem(lax.axis_index("grp"), HEADS)
    spares = []
    for step, (by, got_ref) in enumerate(zip(ORDER, got_refs)):
        odd = lax.rem(jnp.bitwise_xor(own, by), 2)
        at = step * PADDED
        top = got_ref[0:16].astype(jnp.float32)
        bottom = got_ref[PADDED - 16 : PADDED].astype(jnp.float32)
        spares.append(jnp.where(odd == 1, top[:SPARE], bottom[SPARE:]))
        top = jnp.concatenate([jnp.where(odd == 1, 0.0, top[:SPARE]), top[SPARE:]], axis=0)
        bottom = jnp.concatenate([bottom[:SPARE], jnp.where(odd == 1, bottom[SPARE:], 0.0)], axis=0)
        flat[at : at + 16] = top.astype(jnp.bfloat16)
        flat[at + 16 : at + PADDED - 16] = got_ref[16 : PADDED - 16]
        flat[at + PADDED - 16 : at + PADDED] = bottom.astype(jnp.bfloat16)
    return spares


def send_mixed_rows(rows_ref, weight_ref, flat, turned, mixed, mixed_ref, sems, meanwhile=None):
    turned[...] = flat[...].T
    pieces = sems.shape[0]
    step = rows_ref.shape[0] // pieces
    copies, value = [], None
    for piece in range(pieces):
        cut = slice(piece * step, (piece + 1) * step)
        if meanwhile is not None:
            value = meanwhile[piece](value)
        added = jnp.dot(turned[cut, :], weight_ref[...], preferred_element_type=jnp.float32)
        mixed[cut, :] = (rows_ref[cut, :].astype(jnp.float32) + added).astype(jnp.bfloat16)
        copies.append(pltpu.make_async_copy(mixed.at[cut], mixed_ref.at[cut], sems.at[piece]))
        copies[-1].start()
    return copies


def unit_rows(matrix):
    return matrix * lax.rsqrt(jnp.sum(matrix * matrix, axis=1, keepdims=True) + 1e-06)


def losses(cosine, labels):
    logits = -labels * (logit_scale * cosine + logit_bias)
    return jnp.maximum(logits, 0.0) + jnp.log1p(jnp.exp(-jnp.abs(logits)))


def finish_kernel(images, rows_ref, weight_ref, text_ref, *rest):
    got_refs, rest = rest[:HEADS], rest[HEADS:]
    mixed_ref, loss_ref, flat, turned, mixed, sems, pooled_heads, patch_sums, far_texts, loss, loss_sem = rest
    spares = joined_heads(got_refs, flat)
    own = lax.rem(lax.axis_index("grp"), HEADS)
    patch_sums[:, HEADS * LANES :] = spares[0][:, 2 * LANES :]
    for step, (by, spare) in enumerate(zip(ORDER, spares)):
        pooled_heads[:, step * PADDED : (step + 1) * PADDED] = spare[:, 0:PADDED]
        head = jnp.bitwise_xor(own, by)
        patch_sums[:, pl.ds(pl.multiple_of(head * LANES, LANES), LANES)] = spare[:, LANES : 2 * LANES]
        below = got_refs[step][PADDED:].astype(jnp.float32)
        count = below.shape[1]
        for part in range(patch_sums.shape[1] // count):
            here = slice(part * count, (part + 1) * count)
            far_texts[head, :, here] = below[part * images : (part + 1) * images]

    def find_images(_):
        pooled = jnp.dot(
            pooled_heads[...].astype(jnp.bfloat16), weight_ref[...], preferred_element_type=jnp.float32
        )
        pooled = pooled + patch_sums[...]
        others = [far_texts[place] for place in range(lax.axis_size("blk") - 1)]
        texts = jnp.concatenate([text_ref[...].astype(jnp.float32)] + others, axis=0)
        return pooled + pltpu.roll(pooled, images, axis=0), unit_rows(texts)

    def find_cosines(vectors):
        pooled, text_vecs = vectors
        return lax.dot_general(
            text_vecs,
            unit_rows(pooled),
            (((1,), (1,)), ((), ())),
            precision=lax.Precision.HIGHEST,
            preferred_element_type=jnp.float32,
        )

    def find_losses(cosine):
        text = lax.broadcasted_iota(jnp.int32, cosine.shape, 0)
        image = lax.broadcasted_iota(jnp.int32, cosine.shape, 1)
        terms = losses(cosine, jnp.where(text == image, 1.0, -1.0))
        loss[...] = jnp.sum(terms, axis=0, keepdims=True)[:, 0:images]
        loss_copy.start()

    loss_copy = pltpu.make_async_copy(loss, loss_ref, loss_sem)
    meanwhile = (find_images, find_cosines, find_losses)
    copies = send_mixed_rows(rows_ref, weight_ref, flat, turned, mixed, mixed_ref, sems, meanwhile)
    for copy in copies + [loss_copy]:
        copy.wait()


def mix_kernel(rows_ref, weight_ref, *rest):
    got_refs, rest = rest[:HEADS], rest[HEADS:]
    mixed_ref, flat, turned, mixed, sems = rest
    joined_heads(got_refs, flat)
    for copy in send_mixed_rows(rows_ref, weight_ref, flat, turned, mixed, mixed_ref, sems):
        copy.wait()


def in_vmem(count):
    return [pl.BlockSpec(memory_space=pltpu.VMEM)] * count


def in_hbm(value):
    return pltpu.with_memory_space_constraint(value, pltpu.HBM)


def call(kernel, out_shape, scratch, in_specs, flops, out_specs=None):
    if out_specs is None:
        out_specs = jax.tree.map(lambda _: pl.BlockSpec(memory_space=pltpu.VMEM), out_shape)
    return pl.pallas_call(
        kernel,
        out_shape=out_shape,
        in_specs=in_specs,
        out_specs=out_specs,
        scratch_shapes=scratch,
        compiler_params=pltpu.CompilerParams(vmem_limit_bytes=VMEM_LIMIT),
        cost_estimate=pl.CostEstimate(flops=flops, bytes_accessed=8 << 20, transcendentals=0),
    )


def moved(value, axis, pairs):
    return lax.ppermute(value, axis, pairs)


def partner(place, by, peers):
    return place ^ by if peers & (peers - 1) == 0 else (place + by) % peers


def all_texts(texts):
    peers = lax.axis_size("blk")
    steps = [[(partner(i, by, peers), i) for i in range(peers)] for by in range(1, peers)]
    return jnp.concatenate([texts] + [moved(texts, "blk", pairs) for pairs in steps], axis=0)


def one_text_block(texts):
    peers = lax.axis_size("blk")
    pairs = []
    for place in range(lax.axis_size("grp")):
        by = place % (peers - 1) + 1
        pairs += [(place * peers + partner(i, by, peers), place * peers + i) for i in range(peers)]
    return moved(texts, ("grp", "blk"), pairs)


def traded(blocks):
    peers = range(lax.axis_size("grp"))
    trades = {by: moved(blocks[by], "grp", [(i, i ^ by) for i in peers]) for by in ORDER if by}
    return {**trades, 0: blocks[0]}


def local(patches, segment_ids, qkv_weight, out_weight, text_embed):
    rows = patches[0]
    count, depth = rows.shape
    width = out_weight.shape[0]
    size = width // HEADS
    padded = size + SPARE
    images = text_embed.shape[0]
    group_size = lax.axis_size("grp")
    parts = group_size // HEADS
    piggy = (
        parts == 1
        and 2 * images == SPARE
        and count >= depth - (HEADS - 2) * LANES
        and depth % count == 0
        and images * (depth // count) <= TEXT_ROWS
        and 1 < lax.axis_size("blk") <= HEADS + 1
    )
    bf16, f32 = jnp.bfloat16, jnp.float32
    shape = jax.ShapeDtypeStruct

    block = shape((3 * size + SPARE, count), bf16)
    hbm = pl.BlockSpec(memory_space=pltpu.HBM)
    turned_weight = qkv_weight.T
    normed, sums, *sent = call(
        functools.partial(far_kernel, images, piggy),
        (shape((depth, count), bf16), shape((SPARE, depth), f32), block, block),
        [
            pltpu.VMEM((1, count), jnp.int32),
            pltpu.VMEM((count, depth), bf16),
            pltpu.VMEM((3, 2 * size, depth), bf16),
            pltpu.SemaphoreType.DMA,
            pltpu.SemaphoreType.DMA((3,)),
            pltpu.SemaphoreType.DMA((3,)),
        ],
        [hbm] * 3,
        2 * count * depth * 6 * size,
    )(in_hbm(segment_ids), in_hbm(rows), in_hbm(turned_weight))
    sent += call(
        functools.partial(near_kernel, piggy),
        (block,) * 6,
        [],
        in_vmem(3),
        2 * count * depth * 18 * size,
    )(normed, sums, turned_weight)
    sent = dict(zip((6, 7, 2, 3, 4, 5, 0, 1), sent))
    if piggy:
        late_texts, sent[0] = lax.optimization_barrier((text_embed, sent[0]))
        halos_and_texts = [one_text_block(late_texts)]
    else:
        halos_and_texts = []
    got = traded(sent)

    length = HEADS * count
    halo = 0
    near_ids = segment_ids
    if parts > 1:
        halo = rounded_up(MAXP - 1, LANES)
        part = lax.axis_index("grp") // HEADS
        whole_ids = jnp.concatenate(
            [
                jnp.full((1, halo), -1, jnp.int32),
                segment_ids,
                jnp.full((1, halo), images, jnp.int32),
            ],
            axis=1,
        )
        near_ids = lax.dynamic_slice_in_dim(whole_ids, part * length, length + 2 * halo, axis=1)
        order = jnp.bitwise_xor(lax.axis_index("grp") % HEADS, jnp.arange(HEADS))
        flat = jnp.stack([got[by] for by in range(HEADS)])[order][:, : 2 * size].transpose(1, 0, 2).reshape(2 * size, length)
        flat = jnp.concatenate([flat, jnp.zeros((16, length), bf16)], axis=0)
        ahead = [(i, i + HEADS) for i in range(group_size - HEADS)]
        back = [(i + HEADS, i) for i in range(group_size - HEADS)]
        left = moved(flat[:, length - halo :], "grp", ahead)
        right = moved(flat[:, :halo], "grp", back)
        halos_and_texts += [left, right]
    reach = length + 2 * halo
    window = min(rounded_up(MAXP + LANES - 1, LANES), reach)
    tile = 2 * LANES
    early_keys, marks, before, weight = call(
        functools.partial(prepare_kernel, images, halo),
        (
            shape((len(EARLY) * count, LANES), bf16),
            shape((2, SPARE, reach), f32),
            shape((rounded_up(images + 1, SPARE), LANES), jnp.int32),
            shape((HEADS * padded, depth), bf16),
        ),
        [pltpu.SemaphoreType.DMA((HEADS,))],
        in_vmem(1) + [hbm] + in_vmem(len(EARLY)),
        1 << 30,
    )(near_ids, in_hbm(out_weight), *[got[by] for by in EARLY])
    operands = [near_ids, before, marks, early_keys, *[got[by] for by in EARLY + LATE], *halos_and_texts]
    answers = call(
        functools.partial(attend_kernel, images, piggy, halo),
        (shape((padded + TEXT_ROWS * piggy, count), bf16),) * HEADS,
        [
            pltpu.VMEM((reach, LANES), bf16),
            pltpu.VMEM((padded, reach), bf16),
            pltpu.VMEM((LANES, length), bf16),
            pltpu.VMEM((padded, length), f32),
        ]
        + [pltpu.VMEM((window, tile), f32)] * RUN
        + [pltpu.VMEM((1, tile), f32)] * RUN
        + [
            pltpu.SMEM((images + 1,), jnp.int32),
            pltpu.SMEM((3, rounded_up(length // tile + images, RUN) + 1), jnp.int32),
        ],
        in_vmem(len(operands)),
        4 * size * length * MAXP,
    )(*operands)
    home = traded(dict(zip(ORDER, answers)))
    home = [home[by] for by in ORDER]

    joined = [
        pltpu.VMEM((HEADS * padded, count), bf16),
        pltpu.VMEM((count, HEADS * padded), bf16),
        pltpu.VMEM((count, depth), bf16),
        pltpu.SemaphoreType.DMA((3,)),
    ]
    flops = 2 * count * depth * width
    if piggy:
        mixed, row_loss = call(
            functools.partial(finish_kernel, images),
            (shape((count, depth), bf16), shape((1, images), f32)),
            joined
            + [
                pltpu.VMEM((SPARE, HEADS * padded), f32),
                pltpu.VMEM((SPARE, depth), f32),
                pltpu.VMEM((HEADS, images, depth), f32),
                pltpu.VMEM((1, images), f32),
                pltpu.SemaphoreType.DMA,
            ],
            in_vmem(3 + HEADS),
            flops,
            (hbm, hbm),
        )(rows, weight, text_embed, *home)
        return (mixed[None], row_loss[0])
    mixed = call(mix_kernel, shape((count, depth), bf16), joined, in_vmem(2 + HEADS), flops, hbm)(
        rows, weight, *home
    )
    own_ids = lax.dynamic_slice_in_dim(segment_ids[0], lax.axis_index("grp") * count, count)
    onehot = (own_ids[None, :] == jnp.arange(images, dtype=jnp.int32)[:, None]).astype(bf16)
    pooled = lax.psum(jnp.dot(onehot, mixed, preferred_element_type=f32), "grp")
    text_vecs = unit_rows(all_texts(text_embed).astype(f32))
    cosine = jnp.dot(unit_rows(pooled), text_vecs.T, precision=lax.Precision.HIGHEST)
    same = jnp.arange(images)[:, None] == jnp.arange(text_vecs.shape[0])[None, :]
    row_loss = jnp.sum(losses(cosine, jnp.where(same, 1.0, -1.0)), axis=1)
    return (mixed[None], row_loss)


def solution(mesh):
    placed = (P("blk", "grp", None), P("blk", None), P(), P(), P("blk", None))
    return jax.shard_map(
        local,
        mesh=mesh,
        in_specs=placed,
        out_specs=(P("blk", "grp", None), P("blk")),
        check_vma=False,
    )
```

```python
import functools
import math

import jax
import jax.numpy as jnp
from jax import lax
from jax.experimental import pallas as pl
from jax.experimental.pallas import tpu as pltpu
from jax.sharding import PartitionSpec as P

HEADS = 8
MAXP = 1024
LANES = 128
SPARE = 8
SIZE = 72
PADDED = SIZE + SPARE
KEY_AT = SIZE - SPARE
QUERY_AT = 2 * SIZE
TEXT_ROWS = 16
RUN = 3
HIDDEN = -1e30
ORDER = (6, 7, 2, 4, 3, 5, 1, 0)
EARLY = (6, 7, 1, 0)
LATE = (2, 4, 3, 5)

logit_scale = 30.0
logit_bias = -5.0

VMEM_LIMIT = 32 * 1024 * 1024


def rounded_up(value, step):
    return (value + step - 1) // step * step


def split_in_two(total, images):
    row = lax.broadcasted_iota(jnp.int32, total.shape, 0)
    main = total.astype(jnp.bfloat16).astype(jnp.float32)
    return jnp.where(row < images, main, total - main)


def image_rows(ids, images):
    row = lax.broadcasted_iota(jnp.int32, (SPARE, ids.shape[1]), 0)
    return (lax.rem(row, images) == ids).astype(jnp.float32).astype(jnp.bfloat16)


def head_blocks(query, key, value, sums, pair):
    size = query.shape[0] // 2
    count = query.shape[1]
    for place in range(2):
        here = slice(place * size, (place + 1) * size)
        if sums is None:
            spare = jnp.zeros((SPARE, count), jnp.float32)
        else:
            first = pl.multiple_of((2 * pair + place) * LANES, LANES)
            parts = [sums[:, pl.ds(first, LANES)], sums[:, HEADS * LANES :]]
            held = sum(part.shape[1] for part in parts)
            spare = jnp.concatenate(parts + [jnp.zeros((SPARE, count - held), jnp.float32)], axis=1)
        yield jnp.concatenate([value[here], key[here], spare, query[here]], axis=0)


def store_by_core(core, blocks, same_ref, cross_ref):
    first, second = blocks
    same_ref[...] = jnp.where(core == 0, first, second).astype(jnp.bfloat16)
    cross_ref[...] = jnp.where(core == 0, second, first).astype(jnp.bfloat16)


def place_in_group():
    own = lax.rem(lax.axis_index("grp"), HEADS)
    return lax.div(own, 2), lax.rem(own, 2)


def far_kernel(images, piggy, ids_ref, rows_ref, weight_ref, normed_ref, sums_ref, same_ref, cross_ref, own_ids, rows_held, weight, id_sem, row_sems, sems):
    count, depth = rows_ref.shape
    width = weight_ref.shape[0] // 3
    wide = weight.shape[1]
    pieces = row_sems.shape[0]
    step = count // pieces
    row_fetches = []
    for piece in range(pieces):
        cut = slice(piece * step, (piece + 1) * step)
        row_fetches.append(pltpu.make_async_copy(rows_ref.at[cut], rows_held.at[cut], row_sems.at[piece]))
        row_fetches[-1].start()
    own = pl.multiple_of(lax.axis_index("grp") * count, LANES)
    ids_fetch = pltpu.make_async_copy(ids_ref.at[:, pl.ds(own, count)], own_ids, id_sem)
    ids_fetch.start()
    pair, core = place_in_group()
    pair = jnp.bitwise_xor(pair, 3)
    fetches = []
    for at in range(3):
        first = pl.multiple_of(at * width + pair * wide, 16)
        fetches.append(pltpu.make_async_copy(weight_ref.at[pl.ds(first, wide)], weight.at[at], sems.at[at]))
    for fetch in fetches:
        fetch.start()
    ids_fetch.wait()
    for fetch in row_fetches:
        fetch.wait()
    rows = rows_held[...]
    if piggy:
        sums = jnp.dot(image_rows(own_ids[...], images), rows, preferred_element_type=jnp.float32)
        sums_ref[...] = split_in_two(sums, images)
    values = rows.astype(jnp.float32)
    center = values - jnp.mean(values, axis=1, keepdims=True)
    spread = jnp.mean(center * center, axis=1, keepdims=True)
    normed = (center * lax.rsqrt(spread + 1e-06)).astype(jnp.bfloat16)
    normed_ref[...] = normed.T
    for fetch in fetches:
        fetch.wait()
    parts = [
        jnp.dot(weight[at], normed_ref[...], preferred_element_type=jnp.float32) for at in range(3)
    ]
    store_by_core(core, head_blocks(*parts, sums_ref if piggy else None, pair), same_ref, cross_ref)


def near_kernel(piggy, normed_ref, sums_ref, weight_ref, *out_refs):
    width = weight_ref.shape[0] // 3
    wide = 2 * width // HEADS
    own, core = place_in_group()
    for step, move in enumerate((1, 2, 0)):
        pair = jnp.bitwise_xor(own, move)
        parts = []
        for at in range(3):
            here = pl.ds(pl.multiple_of(at * width + pair * wide, 16), wide)
            parts.append(
                jnp.dot(weight_ref[here, :], normed_ref[...], preferred_element_type=jnp.float32)
            )
        blocks = head_blocks(*parts, sums_ref if piggy else None, pair)
        store_by_core(core, blocks, *out_refs[2 * step : 2 * step + 2])


def count_before(images, ids):
    image = lax.broadcasted_iota(jnp.int32, (rounded_up(images + 1, SPARE), ids.shape[1]), 0)
    before = jnp.sum((ids < image).astype(jnp.int32), axis=1, keepdims=True)
    return jnp.broadcast_to(before, (before.shape[0], LANES))


def write_marks(images, ids, marks):
    bits = max(1, (images - 1).bit_length())
    row = lax.broadcasted_iota(jnp.int32, (SPARE, ids.shape[1]), 0)
    bit = jnp.bitwise_and(lax.shift_right_logical(jnp.broadcast_to(ids, row.shape), row >> 1), 1)
    odd = jnp.bitwise_and(row, 1)
    used = row < 2 * bits
    outside = jnp.logical_or(ids < 0, ids >= images)
    key_side = jnp.where(odd == 1, bit, 1 - bit).astype(jnp.float32)
    key_side = jnp.where(outside, 1.0, key_side)
    marks[0] = jnp.where(used, key_side * HIDDEN, 0.0)
    marks[1] = jnp.where(used, jnp.where(odd == 1, 1 - bit, bit), 0).astype(jnp.float32)


def spare_sums(refs):
    parts = [ref[QUERY_AT : QUERY_AT + 16].astype(jnp.float32)[0:SPARE, 0 : 2 * LANES] for ref in refs]
    return sum(parts[1:], parts[0])


def image_at(images, starts, position):
    found = jnp.int32(0)
    for image in range(1, images):
        found += (starts[image] <= position).astype(jnp.int32)
    return found


def list_pairs(images, held, tile, last_begin, base, starts, table):
    tiles = held // tile
    shift = tile.bit_length() - 1
    low = image_at(images, starts, base)
    high = image_at(images, starts, base + held - 1)

    def bounds(image):
        first = jnp.maximum(starts[image] - base, 0) >> shift
        last = (jnp.minimum(starts[image + 1] - base, held) - 1) >> shift
        return jnp.minimum(first, tiles - 1), last

    pairs = jnp.int32(0)
    for image in range(images):
        first, last = bounds(image)
        wanted = jnp.logical_and(low <= image, image <= high)
        pairs += jnp.where(wanted, last - first + 1, 0)
    at, image = jnp.int32(0), low
    for step in range(table.shape[1]):
        table[0, step] = at
        table[1, step] = image
        table[2, step] = jnp.minimum(jnp.bitwise_and(starts[image], -LANES), last_begin)
        more = at < bounds(image)[1]
        later = jnp.minimum(image + 1, images - 1)
        at, image = jnp.where(more, at + 1, bounds(later)[0]), jnp.where(more, image, later)
    return pairs


def attend_images(pairs, table, ids_ref, keys, values, queries, attended, work, query_base):
    work = list(zip(work[:RUN], work[RUN:]))
    window, tile = work[0][0].shape
    size = attended.shape[0] - SPARE

    def window_of(state):
        return pl.ds(pl.multiple_of(table[2, state], LANES), window)

    def score(state, scores, tops):
        query = queries[:, pl.ds(pl.multiple_of(table[0, state] * tile, tile), tile)]
        found = jnp.dot(keys[window_of(state), :], query, preferred_element_type=jnp.float32)
        scores[...] = found
        tops[...] = jnp.max(found, axis=0, keepdims=True)

    def weigh(state, scores, tops):
        first = pl.multiple_of(table[0, state] * tile, tile)
        labels = ids_ref[:, pl.ds(pl.multiple_of(query_base + first, LANES), tile)]
        probs = jnp.exp2((scores[...] - tops[...]) * (size ** (-0.5) * math.log2(math.e)))
        share = 1.0 / jnp.sum(probs, axis=0, keepdims=True)
        weighted = jnp.dot(
            values[:, window_of(state)], probs.astype(jnp.bfloat16), preferred_element_type=jnp.float32
        )
        place = (slice(None), pl.ds(first, tile))
        attended[place] = jnp.where(labels == table[1, state], weighted * share, attended[place])

    def run(step, _):
        for place in range(RUN):
            state = step * RUN + place
            score(state + 1, *work[(place + 1) % RUN])
            weigh(state, *work[place])
        return 0

    score(0, *work[0])
    lax.fori_loop(0, lax.div(pairs + RUN - 1, RUN), run, 0)


def turned_keys(marked, block_ref):
    block = block_ref[KEY_AT : KEY_AT + PADDED].astype(jnp.float32)
    nothing = jnp.zeros((LANES - PADDED, block.shape[1]), jnp.float32)
    full = jnp.concatenate([marked, block[SPARE:], nothing], axis=0)
    return full.astype(jnp.bfloat16).T


def store_queries(marked, block_ref, queries, there):
    edge = block_ref[QUERY_AT : QUERY_AT + 16].astype(jnp.float32)
    edge = jnp.concatenate([marked, edge[SPARE:]], axis=0)
    queries[0:16, there] = edge.astype(jnp.bfloat16)
    queries[16:PADDED, there] = block_ref[QUERY_AT + 16 : QUERY_AT + PADDED]
    queries[PADDED:, there] = jnp.zeros((LANES - PADDED, block_ref.shape[1]), jnp.bfloat16)


def prepare_kernel(images, halo, ids_ref, out_weight_ref, *rest):
    got_refs, (keys, marks, before, weight, sems) = rest[: len(EARLY)], rest[len(EARLY) :]
    count = got_refs[0].shape[1]
    fetches = []
    for step, by in enumerate(ORDER):
        head = jnp.bitwise_xor(lax.rem(lax.axis_index("grp"), HEADS), by)
        first = lax.div(head, 2) * (2 * SIZE) + lax.rem(head, 2) * (SIZE - SPARE)
        fetches.append(
            pltpu.make_async_copy(
                out_weight_ref.at[pl.ds(pl.multiple_of(first, 16), PADDED)],
                weight.at[step * PADDED : (step + 1) * PADDED],
                sems.at[step],
            )
        )
        fetches[-1].start()
    before[...] = count_before(images, ids_ref[...])
    write_marks(images, ids_ref[...], marks)
    own = lax.rem(lax.axis_index("grp"), HEADS)
    for step, (by, ref) in enumerate(zip(EARLY, got_refs)):
        first = jnp.bitwise_xor(own, by) * count
        here = pl.ds(pl.multiple_of(halo + first, LANES), count)
        keys[step * count : (step + 1) * count, :] = turned_keys(marks[0, :, here], ref)
    for fetch in fetches:
        fetch.wait()


def attend_kernel(images, piggy, halo, ids_ref, before_ref, marks, early_keys, *rest):
    got_refs, rest = rest[:HEADS], rest[HEADS:]
    if piggy:
        text_ref, *rest = rest
    if halo:
        left_ref, right_ref, *rest = rest
    out_refs, rest = rest[:HEADS], rest[HEADS:]
    keys, values, queries, attended, *work, starts, table = rest
    count = got_refs[0].shape[1]
    padded = attended.shape[0]
    size = padded - SPARE
    total_rows = HEADS * count
    length = ids_ref.shape[1]
    ids = ids_ref[...]
    before = before_ref[...]
    for image in range(images + 1):
        starts[image] = before[image, 0]
    window, tile = work[0].shape
    pairs = list_pairs(images, total_rows, tile, length - window, halo, starts, table)

    own = lax.rem(lax.axis_index("grp"), HEADS)
    for step, (by, ref) in enumerate(zip(EARLY + LATE, got_refs)):
        first = jnp.bitwise_xor(own, by) * count
        here = pl.ds(pl.multiple_of(halo + first, LANES), count)
        there = pl.ds(pl.multiple_of(first, LANES), count)
        if by in EARLY:
            keys[here, :] = early_keys[step * count : (step + 1) * count, :]
        else:
            keys[here, :] = turned_keys(marks[0, :, here], ref)
        values[:, here] = ref[0:PADDED]
        store_queries(marks[1, :, here], ref, queries, there)
    if halo:
        for ref, here in ((left_ref, slice(0, halo)), (right_ref, slice(length - halo, length))):
            keys[here, :] = turned_keys(marks[0, :, here], ref)
            values[:, here] = ref[0:PADDED]
    attend_images(pairs, table, ids_ref, keys, values, queries, attended, work, halo)

    odd_head = lax.rem(own, 2) == 1
    mine = ids[:, halo : halo + total_rows]

    def placed(block, spare):
        even = jnp.concatenate([block[0:size], spare], axis=0)
        odd = jnp.concatenate([spare, block[0:size]], axis=0)
        return jnp.where(odd_head, odd, even)

    if piggy:
        nothing = jnp.zeros((SPARE, total_rows), jnp.float32)
        flat = placed(attended[...], nothing).astype(jnp.bfloat16)
        pooled = lax.dot_general(
            image_rows(mine, images), flat, (((1,), (1,)), ((), ())), preferred_element_type=jnp.float32
        )
        pooled = split_in_two(pooled, images)
        sums = spare_sums(got_refs)
        sums = split_in_two(sums + pltpu.roll(sums, images, axis=0), images)
        spare = jnp.concatenate(
            [pooled, jnp.zeros((SPARE, LANES - padded), jnp.float32), sums], axis=1
        )
        texts = text_ref[...].astype(jnp.float32)
        parts = [texts[:, at : at + count] for at in range(0, texts.shape[1], count)]
        unused = TEXT_ROWS - images * len(parts)
        below = jnp.concatenate(parts + [jnp.zeros((unused, count), jnp.float32)] * (unused > 0), axis=0)
        below = below.astype(jnp.bfloat16)
    else:
        spare = jnp.zeros((SPARE, count), jnp.float32)
    for by, out_ref in zip(ORDER, out_refs):
        there = pl.multiple_of(jnp.bitwise_xor(own, by) * count, LANES)
        out_ref[0:padded] = placed(attended[:, pl.ds(there, count)], spare).astype(jnp.bfloat16)
        if piggy:
            out_ref[padded:] = below


def joined_heads(got_refs, flat):
    own = lax.rem(lax.axis_index("grp"), HEADS)
    spares = []
    for step, (by, got_ref) in enumerate(zip(ORDER, got_refs)):
        odd = lax.rem(jnp.bitwise_xor(own, by), 2)
        at = step * PADDED
        top = got_ref[0:16].astype(jnp.float32)
        bottom = got_ref[PADDED - 16 : PADDED].astype(jnp.float32)
        spares.append(jnp.where(odd == 1, top[:SPARE], bottom[SPARE:]))
        top = jnp.concatenate([jnp.where(odd == 1, 0.0, top[:SPARE]), top[SPARE:]], axis=0)
        bottom = jnp.concatenate([bottom[:SPARE], jnp.where(odd == 1, bottom[SPARE:], 0.0)], axis=0)
        flat[at : at + 16] = top.astype(jnp.bfloat16)
        flat[at + 16 : at + PADDED - 16] = got_ref[16 : PADDED - 16]
        flat[at + PADDED - 16 : at + PADDED] = bottom.astype(jnp.bfloat16)
    return spares


def send_mixed_rows(rows_ref, weight_ref, flat, turned, mixed, mixed_ref, sems, meanwhile=None):
    turned[...] = flat[...].T
    pieces = sems.shape[0]
    step = rows_ref.shape[0] // pieces
    copies, value = [], None
    for piece in range(pieces):
        cut = slice(piece * step, (piece + 1) * step)
        if meanwhile is not None:
            value = meanwhile[piece](value)
        added = jnp.dot(turned[cut, :], weight_ref[...], preferred_element_type=jnp.float32)
        mixed[cut, :] = (rows_ref[cut, :].astype(jnp.float32) + added).astype(jnp.bfloat16)
        copies.append(pltpu.make_async_copy(mixed.at[cut], mixed_ref.at[cut], sems.at[piece]))
        copies[-1].start()
    return copies


def unit_rows(matrix):
    return matrix * lax.rsqrt(jnp.sum(matrix * matrix, axis=1, keepdims=True) + 1e-06)


def losses(cosine, labels):
    logits = -labels * (logit_scale * cosine + logit_bias)
    return jnp.maximum(logits, 0.0) + jnp.log1p(jnp.exp(-jnp.abs(logits)))


def finish_kernel(images, rows_ref, weight_ref, text_ref, *rest):
    got_refs, rest = rest[:HEADS], rest[HEADS:]
    mixed_ref, loss_ref, flat, turned, mixed, sems, pooled_heads, patch_sums, far_texts, loss, loss_sem = rest
    spares = joined_heads(got_refs, flat)
    own = lax.rem(lax.axis_index("grp"), HEADS)
    patch_sums[:, HEADS * LANES :] = spares[0][:, 2 * LANES :]
    for step, (by, spare) in enumerate(zip(ORDER, spares)):
        pooled_heads[:, step * PADDED : (step + 1) * PADDED] = spare[:, 0:PADDED]
        head = jnp.bitwise_xor(own, by)
        patch_sums[:, pl.ds(pl.multiple_of(head * LANES, LANES), LANES)] = spare[:, LANES : 2 * LANES]
        below = got_refs[step][PADDED:].astype(jnp.float32)
        count = below.shape[1]
        for part in range(patch_sums.shape[1] // count):
            here = slice(part * count, (part + 1) * count)
            far_texts[head, :, here] = below[part * images : (part + 1) * images]

    def find_images(_):
        pooled = jnp.dot(
            pooled_heads[...].astype(jnp.bfloat16), weight_ref[...], preferred_element_type=jnp.float32
        )
        pooled = pooled + patch_sums[...]
        others = [far_texts[place] for place in range(lax.axis_size("blk") - 1)]
        texts = jnp.concatenate([text_ref[...].astype(jnp.float32)] + others, axis=0)
        return pooled + pltpu.roll(pooled, images, axis=0), unit_rows(texts)

    def find_cosines(vectors):
        pooled, text_vecs = vectors
        return lax.dot_general(
            text_vecs,
            unit_rows(pooled),
            (((1,), (1,)), ((), ())),
            precision=lax.Precision.HIGHEST,
            preferred_element_type=jnp.float32,
        )

    def find_losses(cosine):
        text = lax.broadcasted_iota(jnp.int32, cosine.shape, 0)
        image = lax.broadcasted_iota(jnp.int32, cosine.shape, 1)
        terms = losses(cosine, jnp.where(text == image, 1.0, -1.0))
        loss[...] = jnp.sum(terms, axis=0, keepdims=True)[:, 0:images]
        loss_copy.start()

    loss_copy = pltpu.make_async_copy(loss, loss_ref, loss_sem)
    meanwhile = (find_images, find_cosines, find_losses)
    copies = send_mixed_rows(rows_ref, weight_ref, flat, turned, mixed, mixed_ref, sems, meanwhile)
    for copy in copies + [loss_copy]:
        copy.wait()


def mix_kernel(rows_ref, weight_ref, *rest):
    got_refs, rest = rest[:HEADS], rest[HEADS:]
    mixed_ref, flat, turned, mixed, sems = rest
    joined_heads(got_refs, flat)
    for copy in send_mixed_rows(rows_ref, weight_ref, flat, turned, mixed, mixed_ref, sems):
        copy.wait()


def in_vmem(count):
    return [pl.BlockSpec(memory_space=pltpu.VMEM)] * count


def in_hbm(value):
    return pltpu.with_memory_space_constraint(value, pltpu.HBM)


def call(kernel, out_shape, scratch, in_specs, flops, out_specs=None):
    if out_specs is None:
        out_specs = jax.tree.map(lambda _: pl.BlockSpec(memory_space=pltpu.VMEM), out_shape)
    return pl.pallas_call(
        kernel,
        out_shape=out_shape,
        in_specs=in_specs,
        out_specs=out_specs,
        scratch_shapes=scratch,
        compiler_params=pltpu.CompilerParams(vmem_limit_bytes=VMEM_LIMIT),
        cost_estimate=pl.CostEstimate(flops=flops, bytes_accessed=8 << 20, transcendentals=0),
    )


def moved(value, axis, pairs):
    return lax.ppermute(value, axis, pairs)


def partner(place, by, peers):
    return place ^ by if peers & (peers - 1) == 0 else (place + by) % peers


def all_texts(texts):
    peers = lax.axis_size("blk")
    steps = [[(partner(i, by, peers), i) for i in range(peers)] for by in range(1, peers)]
    return jnp.concatenate([texts] + [moved(texts, "blk", pairs) for pairs in steps], axis=0)


def one_text_block(texts):
    peers = lax.axis_size("blk")
    pairs = []
    for place in range(lax.axis_size("grp")):
        by = place % (peers - 1) + 1
        pairs += [(place * peers + partner(i, by, peers), place * peers + i) for i in range(peers)]
    return moved(texts, ("grp", "blk"), pairs)


def traded(blocks):
    peers = range(lax.axis_size("grp"))
    trades = {by: moved(blocks[by], "grp", [(i, i ^ by) for i in peers]) for by in ORDER if by}
    return {**trades, 0: blocks[0]}


def local(patches, segment_ids, qkv_weight, out_weight, text_embed):
    rows = patches[0]
    count, depth = rows.shape
    width = out_weight.shape[0]
    size = width // HEADS
    padded = size + SPARE
    images = text_embed.shape[0]
    group_size = lax.axis_size("grp")
    parts = group_size // HEADS
    piggy = (
        parts == 1
        and 2 * images == SPARE
        and count >= depth - (HEADS - 2) * LANES
        and depth % count == 0
        and images * (depth // count) <= TEXT_ROWS
        and 1 < lax.axis_size("blk") <= HEADS + 1
    )
    bf16, f32 = jnp.bfloat16, jnp.float32
    shape = jax.ShapeDtypeStruct

    block = shape((3 * size + SPARE, count), bf16)
    hbm = pl.BlockSpec(memory_space=pltpu.HBM)
    turned_weight = qkv_weight.T
    normed, sums, *sent = call(
        functools.partial(far_kernel, images, piggy),
        (shape((depth, count), bf16), shape((SPARE, depth), f32), block, block),
        [
            pltpu.VMEM((1, count), jnp.int32),
            pltpu.VMEM((count, depth), bf16),
            pltpu.VMEM((3, 2 * size, depth), bf16),
            pltpu.SemaphoreType.DMA,
            pltpu.SemaphoreType.DMA((3,)),
            pltpu.SemaphoreType.DMA((3,)),
        ],
        [hbm] * 3,
        2 * count * depth * 6 * size,
    )(in_hbm(segment_ids), in_hbm(rows), in_hbm(turned_weight))
    sent += call(
        functools.partial(near_kernel, piggy),
        (block,) * 6,
        [],
        in_vmem(3),
        2 * count * depth * 18 * size,
    )(normed, sums, turned_weight)
    sent = dict(zip((6, 7, 2, 3, 4, 5, 0, 1), sent))
    if piggy:
        late_texts, sent[0] = lax.optimization_barrier((text_embed, sent[0]))
        halos_and_texts = [one_text_block(late_texts)]
    else:
        halos_and_texts = []
    got = traded(sent)

    length = HEADS * count
    halo = 0
    near_ids = segment_ids
    if parts > 1:
        halo = rounded_up(MAXP - 1, LANES)
        part = lax.axis_index("grp") // HEADS
        whole_ids = jnp.concatenate(
            [
                jnp.full((1, halo), -1, jnp.int32),
                segment_ids,
                jnp.full((1, halo), images, jnp.int32),
            ],
            axis=1,
        )
        near_ids = lax.dynamic_slice_in_dim(whole_ids, part * length, length + 2 * halo, axis=1)
        order = jnp.bitwise_xor(lax.axis_index("grp") % HEADS, jnp.arange(HEADS))
        flat = jnp.stack([got[by] for by in range(HEADS)])[order][:, : 2 * size].transpose(1, 0, 2).reshape(2 * size, length)
        flat = jnp.concatenate([flat, jnp.zeros((16, length), bf16)], axis=0)
        ahead = [(i, i + HEADS) for i in range(group_size - HEADS)]
        back = [(i + HEADS, i) for i in range(group_size - HEADS)]
        left = moved(flat[:, length - halo :], "grp", ahead)
        right = moved(flat[:, :halo], "grp", back)
        halos_and_texts += [left, right]
    reach = length + 2 * halo
    window = min(rounded_up(MAXP + LANES - 1, LANES), reach)
    tile = 2 * LANES
    early_keys, marks, before, weight = call(
        functools.partial(prepare_kernel, images, halo),
        (
            shape((len(EARLY) * count, LANES), bf16),
            shape((2, SPARE, reach), f32),
            shape((rounded_up(images + 1, SPARE), LANES), jnp.int32),
            shape((HEADS * padded, depth), bf16),
        ),
        [pltpu.SemaphoreType.DMA((HEADS,))],
        in_vmem(1) + [hbm] + in_vmem(len(EARLY)),
        1 << 30,
    )(near_ids, in_hbm(out_weight), *[got[by] for by in EARLY])
    operands = [near_ids, before, marks, early_keys, *[got[by] for by in EARLY + LATE], *halos_and_texts]
    answers = call(
        functools.partial(attend_kernel, images, piggy, halo),
        (shape((padded + TEXT_ROWS * piggy, count), bf16),) * HEADS,
        [
            pltpu.VMEM((reach, LANES), bf16),
            pltpu.VMEM((padded, reach), bf16),
            pltpu.VMEM((LANES, length), bf16),
            pltpu.VMEM((padded, length), f32),
        ]
        + [pltpu.VMEM((window, tile), f32)] * RUN
        + [pltpu.VMEM((1, tile), f32)] * RUN
        + [
            pltpu.SMEM((images + 1,), jnp.int32),
            pltpu.SMEM((3, rounded_up(length // tile + images, RUN) + 1), jnp.int32),
        ],
        in_vmem(len(operands)),
        4 * size * length * MAXP,
    )(*operands)
    home = traded(dict(zip(ORDER, answers)))
    home = [home[by] for by in ORDER]

    joined = [
        pltpu.VMEM((HEADS * padded, count), bf16),
        pltpu.VMEM((count, HEADS * padded), bf16),
        pltpu.VMEM((count, depth), bf16),
        pltpu.SemaphoreType.DMA((3,)),
    ]
    flops = 2 * count * depth * width
    if piggy:
        mixed, row_loss = call(
            functools.partial(finish_kernel, images),
            (shape((count, depth), bf16), shape((1, images), f32)),
            joined
            + [
                pltpu.VMEM((SPARE, HEADS * padded), f32),
                pltpu.VMEM((SPARE, depth), f32),
                pltpu.VMEM((HEADS, images, depth), f32),
                pltpu.VMEM((1, images), f32),
                pltpu.SemaphoreType.DMA,
            ],
            in_vmem(3 + HEADS),
            flops,
            (hbm, hbm),
        )(rows, weight, text_embed, *home)
        return (mixed[None], row_loss[0])
    mixed = call(mix_kernel, shape((count, depth), bf16), joined, in_vmem(2 + HEADS), flops, hbm)(
        rows, weight, *home
    )
    own_ids = lax.dynamic_slice_in_dim(segment_ids[0], lax.axis_index("grp") * count, count)
    onehot = (own_ids[None, :] == jnp.arange(images, dtype=jnp.int32)[:, None]).astype(bf16)
    pooled = lax.psum(jnp.dot(onehot, mixed, preferred_element_type=f32), "grp")
    text_vecs = unit_rows(all_texts(text_embed).astype(f32))
    cosine = jnp.dot(unit_rows(pooled), text_vecs.T, precision=lax.Precision.HIGHEST)
    same = jnp.arange(images)[:, None] == jnp.arange(text_vecs.shape[0])[None, :]
    row_loss = jnp.sum(losses(cosine, jnp.where(same, 1.0, -1.0)), axis=1)
    return (mixed[None], row_loss)


def solution(mesh):
    placed = (P("blk", "grp", None), P("blk", None), P(), P(), P("blk", None))
    return jax.shard_map(
        local,
        mesh=mesh,
        in_specs=placed,
        out_specs=(P("blk", "grp", None), P("blk")),
        check_vma=False,
    )
```

```python
import functools
import math

import jax
import jax.numpy as jnp
from jax import lax
from jax.experimental import pallas as pl
from jax.experimental.pallas import tpu as pltpu
from jax.sharding import PartitionSpec as P

HEADS = 8
MAXP = 1024
LANES = 128
SPARE = 8
SIZE = 72
PADDED = SIZE + SPARE
KEY_AT = SIZE - SPARE
QUERY_AT = 2 * SIZE
TEXT_ROWS = 16
RUN = 8
HIDDEN = -1e30
ORDER = (6, 7, 2, 4, 3, 5, 1, 0)
EARLY = (6, 7, 1, 0)
LATE = (2, 4, 3, 5)

logit_scale = 30.0
logit_bias = -5.0

VMEM_LIMIT = 32 * 1024 * 1024


def rounded_up(value, step):
    return (value + step - 1) // step * step


def split_in_two(total, images):
    row = lax.broadcasted_iota(jnp.int32, total.shape, 0)
    main = total.astype(jnp.bfloat16).astype(jnp.float32)
    return jnp.where(row < images, main, total - main)


def image_rows(ids, images):
    row = lax.broadcasted_iota(jnp.int32, (SPARE, ids.shape[1]), 0)
    return (lax.rem(row, images) == ids).astype(jnp.float32).astype(jnp.bfloat16)


def head_blocks(query, key, value, sums, pair):
    size = query.shape[0] // 2
    count = query.shape[1]
    for place in range(2):
        here = slice(place * size, (place + 1) * size)
        if sums is None:
            spare = jnp.zeros((SPARE, count), jnp.float32)
        else:
            first = pl.multiple_of((2 * pair + place) * LANES, LANES)
            parts = [sums[:, pl.ds(first, LANES)], sums[:, HEADS * LANES :]]
            held = sum(part.shape[1] for part in parts)
            spare = jnp.concatenate(parts + [jnp.zeros((SPARE, count - held), jnp.float32)], axis=1)
        yield jnp.concatenate([value[here], key[here], spare, query[here]], axis=0)


def store_by_core(core, blocks, same_ref, cross_ref):
    first, second = blocks
    same_ref[...] = jnp.where(core == 0, first, second).astype(jnp.bfloat16)
    cross_ref[...] = jnp.where(core == 0, second, first).astype(jnp.bfloat16)


def place_in_group():
    own = lax.rem(lax.axis_index("grp"), HEADS)
    return lax.div(own, 2), lax.rem(own, 2)


def far_kernel(images, piggy, ids_ref, rows_ref, weight_ref, normed_ref, sums_ref, same_ref, cross_ref, own_ids, rows_held, weight, id_sem, row_sems, sems):
    count, depth = rows_ref.shape
    width = weight_ref.shape[0] // 3
    wide = weight.shape[1]
    pieces = row_sems.shape[0]
    step = count // pieces
    row_fetches = []
    for piece in range(pieces):
        cut = slice(piece * step, (piece + 1) * step)
        row_fetches.append(pltpu.make_async_copy(rows_ref.at[cut], rows_held.at[cut], row_sems.at[piece]))
        row_fetches[-1].start()
    own = pl.multiple_of(lax.axis_index("grp") * count, LANES)
    ids_fetch = pltpu.make_async_copy(ids_ref.at[:, pl.ds(own, count)], own_ids, id_sem)
    ids_fetch.start()
    pair, core = place_in_group()
    pair = jnp.bitwise_xor(pair, 3)
    fetches = []
    for at in range(3):
        first = pl.multiple_of(at * width + pair * wide, 16)
        fetches.append(pltpu.make_async_copy(weight_ref.at[pl.ds(first, wide)], weight.at[at], sems.at[at]))
    for fetch in fetches:
        fetch.start()
    ids_fetch.wait()
    for fetch in row_fetches:
        fetch.wait()
    rows = rows_held[...]
    if piggy:
        sums = jnp.dot(image_rows(own_ids[...], images), rows, preferred_element_type=jnp.float32)
        sums_ref[...] = split_in_two(sums, images)
    values = rows.astype(jnp.float32)
    center = values - jnp.mean(values, axis=1, keepdims=True)
    spread = jnp.mean(center * center, axis=1, keepdims=True)
    normed = (center * lax.rsqrt(spread + 1e-06)).astype(jnp.bfloat16)
    normed_ref[...] = normed.T
    for fetch in fetches:
        fetch.wait()
    parts = [
        jnp.dot(weight[at], normed_ref[...], preferred_element_type=jnp.float32) for at in range(3)
    ]
    store_by_core(core, head_blocks(*parts, sums_ref if piggy else None, pair), same_ref, cross_ref)


def near_kernel(piggy, normed_ref, sums_ref, weight_ref, *out_refs):
    width = weight_ref.shape[0] // 3
    wide = 2 * width // HEADS
    own, core = place_in_group()
    for step, move in enumerate((1, 2, 0)):
        pair = jnp.bitwise_xor(own, move)
        parts = []
        for at in range(3):
            here = pl.ds(pl.multiple_of(at * width + pair * wide, 16), wide)
            parts.append(
                jnp.dot(weight_ref[here, :], normed_ref[...], preferred_element_type=jnp.float32)
            )
        blocks = head_blocks(*parts, sums_ref if piggy else None, pair)
        store_by_core(core, blocks, *out_refs[2 * step : 2 * step + 2])


def count_before(images, ids):
    image = lax.broadcasted_iota(jnp.int32, (rounded_up(images + 1, SPARE), ids.shape[1]), 0)
    before = jnp.sum((ids < image).astype(jnp.int32), axis=1, keepdims=True)
    return jnp.broadcast_to(before, (before.shape[0], LANES))


def write_marks(images, ids, marks):
    bits = max(1, (images - 1).bit_length())
    row = lax.broadcasted_iota(jnp.int32, (SPARE, ids.shape[1]), 0)
    bit = jnp.bitwise_and(lax.shift_right_logical(jnp.broadcast_to(ids, row.shape), row >> 1), 1)
    odd = jnp.bitwise_and(row, 1)
    used = row < 2 * bits
    outside = jnp.logical_or(ids < 0, ids >= images)
    key_side = jnp.where(odd == 1, bit, 1 - bit).astype(jnp.float32)
    key_side = jnp.where(outside, 1.0, key_side)
    marks[0] = jnp.where(used, key_side * HIDDEN, 0.0)
    marks[1] = jnp.where(used, jnp.where(odd == 1, 1 - bit, bit), 0).astype(jnp.float32)


def spare_sums(refs):
    parts = [ref[QUERY_AT : QUERY_AT + 16].astype(jnp.float32)[0:SPARE, 0 : 2 * LANES] for ref in refs]
    return sum(parts[1:], parts[0])


def image_at(images, starts, position):
    found = jnp.int32(0)
    for image in range(1, images):
        found += (starts[image] <= position).astype(jnp.int32)
    return found


def list_pairs(images, held, tile, last_begin, base, starts, table):
    tiles = held // tile
    shift = tile.bit_length() - 1
    low = image_at(images, starts, base)
    high = image_at(images, starts, base + held - 1)

    def bounds(image):
        first = jnp.maximum(starts[image] - base, 0) >> shift
        last = (jnp.minimum(starts[image + 1] - base, held) - 1) >> shift
        return jnp.minimum(first, tiles - 1), last

    pairs = jnp.int32(0)
    for image in range(images):
        first, last = bounds(image)
        wanted = jnp.logical_and(low <= image, image <= high)
        pairs += jnp.where(wanted, last - first + 1, 0)
    at, image = jnp.int32(0), low
    for step in range(table.shape[1]):
        table[0, step] = at
        table[1, step] = image
        table[2, step] = jnp.minimum(jnp.bitwise_and(starts[image], -LANES), last_begin)
        more = at < bounds(image)[1]
        later = jnp.minimum(image + 1, images - 1)
        at, image = jnp.where(more, at + 1, bounds(later)[0]), jnp.where(more, image, later)
    return pairs


def attend_images(pairs, table, ids_ref, keys, values, queries, attended, work, query_base):
    work = list(zip(work[:2], work[2:]))
    window, tile = work[0][0].shape
    size = attended.shape[0] - SPARE

    def window_of(state):
        return pl.ds(pl.multiple_of(table[2, state], LANES), window)

    def score(state, scores, tops):
        query = queries[:, pl.ds(pl.multiple_of(table[0, state] * tile, tile), tile)]
        found = jnp.dot(keys[window_of(state), :], query, preferred_element_type=jnp.float32)
        scores[...] = found
        tops[...] = jnp.max(found, axis=0, keepdims=True)

    def weigh(state, scores, tops):
        first = pl.multiple_of(table[0, state] * tile, tile)
        labels = ids_ref[:, pl.ds(pl.multiple_of(query_base + first, LANES), tile)]
        probs = jnp.exp2((scores[...] - tops[...]) * (size ** (-0.5) * math.log2(math.e)))
        share = 1.0 / jnp.sum(probs, axis=0, keepdims=True)
        weighted = jnp.dot(
            values[:, window_of(state)], probs.astype(jnp.bfloat16), preferred_element_type=jnp.float32
        )
        place = (slice(None), pl.ds(first, tile))
        attended[place] = jnp.where(labels == table[1, state], weighted * share, attended[place])

    def run(step, _):
        for place in range(RUN):
            state = step * RUN + place
            score(state + 1, *work[(place + 1) % 2])
            weigh(state, *work[place % 2])
        return 0

    score(0, *work[0])
    lax.fori_loop(0, lax.div(pairs + RUN - 1, RUN), run, 0)


def turned_keys(marked, block_ref):
    block = block_ref[KEY_AT : KEY_AT + PADDED].astype(jnp.float32)
    nothing = jnp.zeros((LANES - PADDED, block.shape[1]), jnp.float32)
    full = jnp.concatenate([marked, block[SPARE:], nothing], axis=0)
    return full.astype(jnp.bfloat16).T


def store_queries(marked, block_ref, queries, there):
    edge = block_ref[QUERY_AT : QUERY_AT + 16].astype(jnp.float32)
    edge = jnp.concatenate([marked, edge[SPARE:]], axis=0)
    queries[0:16, there] = edge.astype(jnp.bfloat16)
    queries[16:PADDED, there] = block_ref[QUERY_AT + 16 : QUERY_AT + PADDED]
    queries[PADDED:, there] = jnp.zeros((LANES - PADDED, block_ref.shape[1]), jnp.bfloat16)


def prepare_kernel(images, halo, ids_ref, out_weight_ref, *rest):
    got_refs, (keys, marks, before, weight, sems) = rest[: len(EARLY)], rest[len(EARLY) :]
    count = got_refs[0].shape[1]
    fetches = []
    for step, by in enumerate(ORDER):
        head = jnp.bitwise_xor(lax.rem(lax.axis_index("grp"), HEADS), by)
        first = lax.div(head, 2) * (2 * SIZE) + lax.rem(head, 2) * (SIZE - SPARE)
        fetches.append(
            pltpu.make_async_copy(
                out_weight_ref.at[pl.ds(pl.multiple_of(first, 16), PADDED)],
                weight.at[step * PADDED : (step + 1) * PADDED],
                sems.at[step],
            )
        )
        fetches[-1].start()
    before[...] = count_before(images, ids_ref[...])
    write_marks(images, ids_ref[...], marks)
    own = lax.rem(lax.axis_index("grp"), HEADS)
    for step, (by, ref) in enumerate(zip(EARLY, got_refs)):
        first = jnp.bitwise_xor(own, by) * count
        here = pl.ds(pl.multiple_of(halo + first, LANES), count)
        keys[step * count : (step + 1) * count, :] = turned_keys(marks[0, :, here], ref)
    for fetch in fetches:
        fetch.wait()


def attend_kernel(images, piggy, halo, ids_ref, before_ref, marks, early_keys, *rest):
    got_refs, rest = rest[:HEADS], rest[HEADS:]
    if piggy:
        text_ref, *rest = rest
    if halo:
        left_ref, right_ref, *rest = rest
    out_refs, rest = rest[:HEADS], rest[HEADS:]
    keys, values, queries, attended, *work, starts, table = rest
    count = got_refs[0].shape[1]
    padded = attended.shape[0]
    size = padded - SPARE
    total_rows = HEADS * count
    length = ids_ref.shape[1]
    ids = ids_ref[...]
    before = before_ref[...]
    for image in range(images + 1):
        starts[image] = before[image, 0]
    window, tile = work[0].shape
    pairs = list_pairs(images, total_rows, tile, length - window, halo, starts, table)

    own = lax.rem(lax.axis_index("grp"), HEADS)
    for step, (by, ref) in enumerate(zip(EARLY + LATE, got_refs)):
        first = jnp.bitwise_xor(own, by) * count
        here = pl.ds(pl.multiple_of(halo + first, LANES), count)
        there = pl.ds(pl.multiple_of(first, LANES), count)
        if by in EARLY:
            keys[here, :] = early_keys[step * count : (step + 1) * count, :]
        else:
            keys[here, :] = turned_keys(marks[0, :, here], ref)
        values[:, here] = ref[0:PADDED]
        store_queries(marks[1, :, here], ref, queries, there)
    if halo:
        for ref, here in ((left_ref, slice(0, halo)), (right_ref, slice(length - halo, length))):
            keys[here, :] = turned_keys(marks[0, :, here], ref)
            values[:, here] = ref[0:PADDED]
    attend_images(pairs, table, ids_ref, keys, values, queries, attended, work, halo)

    odd_head = lax.rem(own, 2) == 1
    mine = ids[:, halo : halo + total_rows]

    def placed(block, spare):
        even = jnp.concatenate([block[0:size], spare], axis=0)
        odd = jnp.concatenate([spare, block[0:size]], axis=0)
        return jnp.where(odd_head, odd, even)

    if piggy:
        nothing = jnp.zeros((SPARE, total_rows), jnp.float32)
        flat = placed(attended[...], nothing).astype(jnp.bfloat16)
        pooled = lax.dot_general(
            image_rows(mine, images), flat, (((1,), (1,)), ((), ())), preferred_element_type=jnp.float32
        )
        pooled = split_in_two(pooled, images)
        sums = spare_sums(got_refs)
        sums = split_in_two(sums + pltpu.roll(sums, images, axis=0), images)
        spare = jnp.concatenate(
            [pooled, jnp.zeros((SPARE, LANES - padded), jnp.float32), sums], axis=1
        )
        texts = text_ref[...].astype(jnp.float32)
        parts = [texts[:, at : at + count] for at in range(0, texts.shape[1], count)]
        unused = TEXT_ROWS - images * len(parts)
        below = jnp.concatenate(parts + [jnp.zeros((unused, count), jnp.float32)] * (unused > 0), axis=0)
        below = below.astype(jnp.bfloat16)
    else:
        spare = jnp.zeros((SPARE, count), jnp.float32)
    for by, out_ref in zip(ORDER, out_refs):
        there = pl.multiple_of(jnp.bitwise_xor(own, by) * count, LANES)
        out_ref[0:padded] = placed(attended[:, pl.ds(there, count)], spare).astype(jnp.bfloat16)
        if piggy:
            out_ref[padded:] = below


def joined_heads(got_refs, flat):
    own = lax.rem(lax.axis_index("grp"), HEADS)
    spares = []
    for step, (by, got_ref) in enumerate(zip(ORDER, got_refs)):
        odd = lax.rem(jnp.bitwise_xor(own, by), 2)
        at = step * PADDED
        top = got_ref[0:16].astype(jnp.float32)
        bottom = got_ref[PADDED - 16 : PADDED].astype(jnp.float32)
        spares.append(jnp.where(odd == 1, top[:SPARE], bottom[SPARE:]))
        top = jnp.concatenate([jnp.where(odd == 1, 0.0, top[:SPARE]), top[SPARE:]], axis=0)
        bottom = jnp.concatenate([bottom[:SPARE], jnp.where(odd == 1, bottom[SPARE:], 0.0)], axis=0)
        flat[at : at + 16] = top.astype(jnp.bfloat16)
        flat[at + 16 : at + PADDED - 16] = got_ref[16 : PADDED - 16]
        flat[at + PADDED - 16 : at + PADDED] = bottom.astype(jnp.bfloat16)
    return spares


def send_mixed_rows(rows_ref, weight_ref, flat, turned, mixed, mixed_ref, sems, meanwhile=None):
    turned[...] = flat[...].T
    pieces = sems.shape[0]
    step = rows_ref.shape[0] // pieces
    copies, value = [], None
    for piece in range(pieces):
        cut = slice(piece * step, (piece + 1) * step)
        if meanwhile is not None:
            value = meanwhile[piece](value)
        added = jnp.dot(turned[cut, :], weight_ref[...], preferred_element_type=jnp.float32)
        mixed[cut, :] = (rows_ref[cut, :].astype(jnp.float32) + added).astype(jnp.bfloat16)
        copies.append(pltpu.make_async_copy(mixed.at[cut], mixed_ref.at[cut], sems.at[piece]))
        copies[-1].start()
    return copies


def unit_rows(matrix):
    return matrix * lax.rsqrt(jnp.sum(matrix * matrix, axis=1, keepdims=True) + 1e-06)


def losses(cosine, labels):
    logits = -labels * (logit_scale * cosine + logit_bias)
    return jnp.maximum(logits, 0.0) + jnp.log1p(jnp.exp(-jnp.abs(logits)))


def finish_kernel(images, rows_ref, weight_ref, text_ref, *rest):
    got_refs, rest = rest[:HEADS], rest[HEADS:]
    mixed_ref, loss_ref, flat, turned, mixed, sems, pooled_heads, patch_sums, far_texts, loss, loss_sem = rest
    spares = joined_heads(got_refs, flat)
    own = lax.rem(lax.axis_index("grp"), HEADS)
    patch_sums[:, HEADS * LANES :] = spares[0][:, 2 * LANES :]
    for step, (by, spare) in enumerate(zip(ORDER, spares)):
        pooled_heads[:, step * PADDED : (step + 1) * PADDED] = spare[:, 0:PADDED]
        head = jnp.bitwise_xor(own, by)
        patch_sums[:, pl.ds(pl.multiple_of(head * LANES, LANES), LANES)] = spare[:, LANES : 2 * LANES]
        below = got_refs[step][PADDED:].astype(jnp.float32)
        count = below.shape[1]
        for part in range(patch_sums.shape[1] // count):
            here = slice(part * count, (part + 1) * count)
            far_texts[head, :, here] = below[part * images : (part + 1) * images]

    def find_images(_):
        pooled = jnp.dot(
            pooled_heads[...].astype(jnp.bfloat16), weight_ref[...], preferred_element_type=jnp.float32
        )
        pooled = pooled + patch_sums[...]
        others = [far_texts[place] for place in range(lax.axis_size("blk") - 1)]
        texts = jnp.concatenate([text_ref[...].astype(jnp.float32)] + others, axis=0)
        return pooled + pltpu.roll(pooled, images, axis=0), unit_rows(texts)

    def find_cosines(vectors):
        pooled, text_vecs = vectors
        return lax.dot_general(
            text_vecs,
            unit_rows(pooled),
            (((1,), (1,)), ((), ())),
            precision=lax.Precision.HIGHEST,
            preferred_element_type=jnp.float32,
        )

    def find_losses(cosine):
        text = lax.broadcasted_iota(jnp.int32, cosine.shape, 0)
        image = lax.broadcasted_iota(jnp.int32, cosine.shape, 1)
        terms = losses(cosine, jnp.where(text == image, 1.0, -1.0))
        loss[...] = jnp.sum(terms, axis=0, keepdims=True)[:, 0:images]
        loss_copy.start()

    loss_copy = pltpu.make_async_copy(loss, loss_ref, loss_sem)
    meanwhile = (find_images, find_cosines, find_losses)
    copies = send_mixed_rows(rows_ref, weight_ref, flat, turned, mixed, mixed_ref, sems, meanwhile)
    for copy in copies + [loss_copy]:
        copy.wait()


def mix_kernel(rows_ref, weight_ref, *rest):
    got_refs, rest = rest[:HEADS], rest[HEADS:]
    mixed_ref, flat, turned, mixed, sems = rest
    joined_heads(got_refs, flat)
    for copy in send_mixed_rows(rows_ref, weight_ref, flat, turned, mixed, mixed_ref, sems):
        copy.wait()


def in_vmem(count):
    return [pl.BlockSpec(memory_space=pltpu.VMEM)] * count


def in_hbm(value):
    return pltpu.with_memory_space_constraint(value, pltpu.HBM)


def call(kernel, out_shape, scratch, in_specs, flops, out_specs=None):
    if out_specs is None:
        out_specs = jax.tree.map(lambda _: pl.BlockSpec(memory_space=pltpu.VMEM), out_shape)
    return pl.pallas_call(
        kernel,
        out_shape=out_shape,
        in_specs=in_specs,
        out_specs=out_specs,
        scratch_shapes=scratch,
        compiler_params=pltpu.CompilerParams(vmem_limit_bytes=VMEM_LIMIT),
        cost_estimate=pl.CostEstimate(flops=flops, bytes_accessed=8 << 20, transcendentals=0),
    )


def moved(value, axis, pairs):
    return lax.ppermute(value, axis, pairs)


def partner(place, by, peers):
    return place ^ by if peers & (peers - 1) == 0 else (place + by) % peers


def all_texts(texts):
    peers = lax.axis_size("blk")
    steps = [[(partner(i, by, peers), i) for i in range(peers)] for by in range(1, peers)]
    return jnp.concatenate([texts] + [moved(texts, "blk", pairs) for pairs in steps], axis=0)


def one_text_block(texts):
    peers = lax.axis_size("blk")
    pairs = []
    for place in range(lax.axis_size("grp")):
        by = place % (peers - 1) + 1
        pairs += [(place * peers + partner(i, by, peers), place * peers + i) for i in range(peers)]
    return moved(texts, ("grp", "blk"), pairs)


def traded(blocks):
    peers = range(lax.axis_size("grp"))
    trades = {by: moved(blocks[by], "grp", [(i, i ^ by) for i in peers]) for by in ORDER if by}
    return {**trades, 0: blocks[0]}


def local(patches, segment_ids, qkv_weight, out_weight, text_embed):
    rows = patches[0]
    count, depth = rows.shape
    width = out_weight.shape[0]
    size = width // HEADS
    padded = size + SPARE
    images = text_embed.shape[0]
    group_size = lax.axis_size("grp")
    parts = group_size // HEADS
    piggy = (
        parts == 1
        and 2 * images == SPARE
        and count >= depth - (HEADS - 2) * LANES
        and depth % count == 0
        and images * (depth // count) <= TEXT_ROWS
        and 1 < lax.axis_size("blk") <= HEADS + 1
    )
    bf16, f32 = jnp.bfloat16, jnp.float32
    shape = jax.ShapeDtypeStruct

    block = shape((3 * size + SPARE, count), bf16)
    hbm = pl.BlockSpec(memory_space=pltpu.HBM)
    turned_weight = qkv_weight.T
    normed, sums, *sent = call(
        functools.partial(far_kernel, images, piggy),
        (shape((depth, count), bf16), shape((SPARE, depth), f32), block, block),
        [
            pltpu.VMEM((1, count), jnp.int32),
            pltpu.VMEM((count, depth), bf16),
            pltpu.VMEM((3, 2 * size, depth), bf16),
            pltpu.SemaphoreType.DMA,
            pltpu.SemaphoreType.DMA((3,)),
            pltpu.SemaphoreType.DMA((3,)),
        ],
        [hbm] * 3,
        2 * count * depth * 6 * size,
    )(in_hbm(segment_ids), in_hbm(rows), in_hbm(turned_weight))
    sent += call(
        functools.partial(near_kernel, piggy),
        (block,) * 6,
        [],
        in_vmem(3),
        2 * count * depth * 18 * size,
    )(normed, sums, turned_weight)
    sent = dict(zip((6, 7, 2, 3, 4, 5, 0, 1), sent))
    if piggy:
        late_texts, sent[0] = lax.optimization_barrier((text_embed, sent[0]))
        halos_and_texts = [one_text_block(late_texts)]
    else:
        halos_and_texts = []
    got = traded(sent)

    length = HEADS * count
    halo = 0
    near_ids = segment_ids
    if parts > 1:
        halo = rounded_up(MAXP - 1, LANES)
        part = lax.axis_index("grp") // HEADS
        whole_ids = jnp.concatenate(
            [
                jnp.full((1, halo), -1, jnp.int32),
                segment_ids,
                jnp.full((1, halo), images, jnp.int32),
            ],
            axis=1,
        )
        near_ids = lax.dynamic_slice_in_dim(whole_ids, part * length, length + 2 * halo, axis=1)
        order = jnp.bitwise_xor(lax.axis_index("grp") % HEADS, jnp.arange(HEADS))
        flat = jnp.stack([got[by] for by in range(HEADS)])[order][:, : 2 * size].transpose(1, 0, 2).reshape(2 * size, length)
        flat = jnp.concatenate([flat, jnp.zeros((16, length), bf16)], axis=0)
        ahead = [(i, i + HEADS) for i in range(group_size - HEADS)]
        back = [(i + HEADS, i) for i in range(group_size - HEADS)]
        left = moved(flat[:, length - halo :], "grp", ahead)
        right = moved(flat[:, :halo], "grp", back)
        halos_and_texts += [left, right]
    reach = length + 2 * halo
    window = min(rounded_up(MAXP + LANES - 1, LANES), reach)
    tile = 2 * LANES
    early_keys, marks, before, weight = call(
        functools.partial(prepare_kernel, images, halo),
        (
            shape((len(EARLY) * count, LANES), bf16),
            shape((2, SPARE, reach), f32),
            shape((rounded_up(images + 1, SPARE), LANES), jnp.int32),
            shape((HEADS * padded, depth), bf16),
        ),
        [pltpu.SemaphoreType.DMA((HEADS,))],
        in_vmem(1) + [hbm] + in_vmem(len(EARLY)),
        1 << 30,
    )(near_ids, in_hbm(out_weight), *[got[by] for by in EARLY])
    operands = [near_ids, before, marks, early_keys, *[got[by] for by in EARLY + LATE], *halos_and_texts]
    answers = call(
        functools.partial(attend_kernel, images, piggy, halo),
        (shape((padded + TEXT_ROWS * piggy, count), bf16),) * HEADS,
        [
            pltpu.VMEM((reach, LANES), bf16),
            pltpu.VMEM((padded, reach), bf16),
            pltpu.VMEM((LANES, length), bf16),
            pltpu.VMEM((padded, length), f32),
        ]
        + [pltpu.VMEM((window, tile), f32)] * 2
        + [pltpu.VMEM((1, tile), f32)] * 2
        + [
            pltpu.SMEM((images + 1,), jnp.int32),
            pltpu.SMEM((3, rounded_up(length // tile + images, RUN) + 1), jnp.int32),
        ],
        in_vmem(len(operands)),
        4 * size * length * MAXP,
    )(*operands)
    home = traded(dict(zip(ORDER, answers)))
    home = [home[by] for by in ORDER]

    joined = [
        pltpu.VMEM((HEADS * padded, count), bf16),
        pltpu.VMEM((count, HEADS * padded), bf16),
        pltpu.VMEM((count, depth), bf16),
        pltpu.SemaphoreType.DMA((3,)),
    ]
    flops = 2 * count * depth * width
    if piggy:
        mixed, row_loss = call(
            functools.partial(finish_kernel, images),
            (shape((count, depth), bf16), shape((1, images), f32)),
            joined
            + [
                pltpu.VMEM((SPARE, HEADS * padded), f32),
                pltpu.VMEM((SPARE, depth), f32),
                pltpu.VMEM((HEADS, images, depth), f32),
                pltpu.VMEM((1, images), f32),
                pltpu.SemaphoreType.DMA,
            ],
            in_vmem(3 + HEADS),
            flops,
            (hbm, hbm),
        )(rows, weight, text_embed, *home)
        return (mixed[None], row_loss[0])
    mixed = call(mix_kernel, shape((count, depth), bf16), joined, in_vmem(2 + HEADS), flops, hbm)(
        rows, weight, *home
    )
    own_ids = lax.dynamic_slice_in_dim(segment_ids[0], lax.axis_index("grp") * count, count)
    onehot = (own_ids[None, :] == jnp.arange(images, dtype=jnp.int32)[:, None]).astype(bf16)
    pooled = lax.psum(jnp.dot(onehot, mixed, preferred_element_type=f32), "grp")
    text_vecs = unit_rows(all_texts(text_embed).astype(f32))
    cosine = jnp.dot(unit_rows(pooled), text_vecs.T, precision=lax.Precision.HIGHEST)
    same = jnp.arange(images)[:, None] == jnp.arange(text_vecs.shape[0])[None, :]
    row_loss = jnp.sum(losses(cosine, jnp.where(same, 1.0, -1.0)), axis=1)
    return (mixed[None], row_loss)


def solution(mesh):
    placed = (P("blk", "grp", None), P("blk", None), P(), P(), P("blk", None))
    return jax.shard_map(
        local,
        mesh=mesh,
        in_specs=placed,
        out_specs=(P("blk", "grp", None), P("blk")),
        check_vma=False,
    )
```

```python
import functools
import math

import jax
import jax.numpy as jnp
from jax import lax
from jax.experimental import pallas as pl
from jax.experimental.pallas import tpu as pltpu
from jax.sharding import PartitionSpec as P

HEADS = 8
MAXP = 1024
LANES = 128
SPARE = 8
SIZE = 72
PADDED = SIZE + SPARE
KEY_AT = SIZE - SPARE
QUERY_AT = 2 * SIZE
TEXT_ROWS = 16
HIDDEN = -1e30
ORDER = (6, 7, 2, 4, 3, 5, 1, 0)
EARLY = (6, 7, 1, 0)
LATE = (2, 4, 3, 5)

logit_scale = 30.0
logit_bias = -5.0

VMEM_LIMIT = 32 * 1024 * 1024


def rounded_up(value, step):
    return (value + step - 1) // step * step


def split_in_two(total, images):
    row = lax.broadcasted_iota(jnp.int32, total.shape, 0)
    main = total.astype(jnp.bfloat16).astype(jnp.float32)
    return jnp.where(row < images, main, total - main)


def image_rows(ids, images):
    row = lax.broadcasted_iota(jnp.int32, (SPARE, ids.shape[1]), 0)
    return (lax.rem(row, images) == ids).astype(jnp.float32).astype(jnp.bfloat16)


def turned_product(weight, normed):
    return lax.dot_general(
        weight, normed, (((1,), (1,)), ((), ())), preferred_element_type=jnp.float32
    )


def head_blocks(query, key, value, sums, pair):
    size = query.shape[0] // 2
    count = query.shape[1]
    for place in range(2):
        here = slice(place * size, (place + 1) * size)
        if sums is None:
            spare = jnp.zeros((SPARE, count), jnp.float32)
        else:
            first = pl.multiple_of((2 * pair + place) * LANES, LANES)
            parts = [sums[:, pl.ds(first, LANES)], sums[:, HEADS * LANES :]]
            held = sum(part.shape[1] for part in parts)
            spare = jnp.concatenate(parts + [jnp.zeros((SPARE, count - held), jnp.float32)], axis=1)
        yield jnp.concatenate([value[here], key[here], spare, query[here]], axis=0)


def store_by_core(core, blocks, same_ref, cross_ref):
    first, second = blocks
    same_ref[...] = jnp.where(core == 0, first, second).astype(jnp.bfloat16)
    cross_ref[...] = jnp.where(core == 0, second, first).astype(jnp.bfloat16)


def place_in_group():
    own = lax.rem(lax.axis_index("grp"), HEADS)
    return lax.div(own, 2), lax.rem(own, 2)


def far_kernel(images, piggy, ids_ref, rows_ref, weight_ref, normed_ref, sums_ref, same_ref, cross_ref, own_ids, rows_held, weight, id_sem, row_sem, sems):
    count, depth = rows_ref.shape
    width = weight_ref.shape[0] // 3
    wide = weight.shape[1]
    rows_fetch = pltpu.make_async_copy(rows_ref, rows_held, row_sem)
    rows_fetch.start()
    own = pl.multiple_of(lax.axis_index("grp") * count, LANES)
    ids_fetch = pltpu.make_async_copy(ids_ref.at[:, pl.ds(own, count)], own_ids, id_sem)
    ids_fetch.start()
    pair, core = place_in_group()
    pair = jnp.bitwise_xor(pair, 3)
    fetches = []
    for at in range(3):
        first = pl.multiple_of(at * width + pair * wide, 16)
        fetches.append(pltpu.make_async_copy(weight_ref.at[pl.ds(first, wide)], weight.at[at], sems.at[at]))
    for fetch in fetches:
        fetch.start()
    ids_fetch.wait()
    rows_fetch.wait()
    rows = rows_held[...]
    if piggy:
        sums = jnp.dot(image_rows(own_ids[...], images), rows, preferred_element_type=jnp.float32)
        sums_ref[...] = split_in_two(sums, images)
    values = rows.astype(jnp.float32)
    center = values - jnp.mean(values, axis=1, keepdims=True)
    spread = jnp.mean(center * center, axis=1, keepdims=True)
    normed = (center * lax.rsqrt(spread + 1e-06)).astype(jnp.bfloat16)
    normed_ref[...] = normed
    for fetch in fetches:
        fetch.wait()
    parts = [
        turned_product(weight[at], normed_ref[...]) for at in range(3)
    ]
    store_by_core(core, head_blocks(*parts, sums_ref if piggy else None, pair), same_ref, cross_ref)


def near_kernel(piggy, normed_ref, sums_ref, weight_ref, *out_refs):
    width = weight_ref.shape[0] // 3
    wide = 2 * width // HEADS
    own, core = place_in_group()
    for step, move in enumerate((1, 2, 0)):
        pair = jnp.bitwise_xor(own, move)
        parts = []
        for at in range(3):
            here = pl.ds(pl.multiple_of(at * width + pair * wide, 16), wide)
            parts.append(
                turned_product(weight_ref[here, :], normed_ref[...])
            )
        blocks = head_blocks(*parts, sums_ref if piggy else None, pair)
        store_by_core(core, blocks, *out_refs[2 * step : 2 * step + 2])


def count_before(images, ids):
    image = lax.broadcasted_iota(jnp.int32, (rounded_up(images + 1, SPARE), ids.shape[1]), 0)
    before = jnp.sum((ids < image).astype(jnp.int32), axis=1, keepdims=True)
    return jnp.broadcast_to(before, (before.shape[0], LANES))


def write_marks(images, ids, marks):
    bits = max(1, (images - 1).bit_length())
    row = lax.broadcasted_iota(jnp.int32, (SPARE, ids.shape[1]), 0)
    bit = jnp.bitwise_and(lax.shift_right_logical(jnp.broadcast_to(ids, row.shape), row >> 1), 1)
    odd = jnp.bitwise_and(row, 1)
    used = row < 2 * bits
    outside = jnp.logical_or(ids < 0, ids >= images)
    key_side = jnp.where(odd == 1, bit, 1 - bit).astype(jnp.float32)
    key_side = jnp.where(outside, 1.0, key_side)
    marks[0] = jnp.where(used, key_side * HIDDEN, 0.0)
    marks[1] = jnp.where(used, jnp.where(odd == 1, 1 - bit, bit), 0).astype(jnp.float32)


def spare_sums(refs):
    parts = [ref[QUERY_AT : QUERY_AT + 16].astype(jnp.float32)[0:SPARE, 0 : 2 * LANES] for ref in refs]
    return sum(parts[1:], parts[0])


def image_at(images, starts, position):
    found = jnp.int32(0)
    for image in range(1, images):
        found += (starts[image] <= position).astype(jnp.int32)
    return found


def list_pairs(images, held, tile, last_begin, base, starts, table):
    tiles = held // tile
    shift = tile.bit_length() - 1
    low = image_at(images, starts, base)
    high = image_at(images, starts, base + held - 1)

    def bounds(image):
        first = jnp.maximum(starts[image] - base, 0) >> shift
        last = (jnp.minimum(starts[image + 1] - base, held) - 1) >> shift
        return jnp.minimum(first, tiles - 1), last

    pairs = jnp.int32(0)
    for image in range(images):
        first, last = bounds(image)
        wanted = jnp.logical_and(low <= image, image <= high)
        pairs += jnp.where(wanted, last - first + 1, 0)
    at, image = jnp.int32(0), low
    for step in range(tiles + images):
        table[0, step] = at
        table[1, step] = image
        table[2, step] = jnp.minimum(jnp.bitwise_and(starts[image], -LANES), last_begin)
        more = at < bounds(image)[1]
        later = jnp.minimum(image + 1, images - 1)
        at, image = jnp.where(more, at + 1, bounds(later)[0]), jnp.where(more, image, later)
    return pairs


def attend_images(pairs, table, ids_ref, keys, values, queries, attended, work, query_base):
    scores_a, scores_b, tops_a, tops_b = work
    window, tile = scores_a.shape
    size = attended.shape[0] - SPARE

    def window_of(state):
        return pl.ds(pl.multiple_of(table[2, state], LANES), window)

    def score(state, scores, tops):
        query = queries[:, pl.ds(pl.multiple_of(table[0, state] * tile, tile), tile)]
        found = jnp.dot(keys[window_of(state), :], query, preferred_element_type=jnp.float32)
        scores[...] = found
        tops[...] = jnp.max(found, axis=0, keepdims=True)

    def weigh(state, scores, tops):
        first = pl.multiple_of(table[0, state] * tile, tile)
        labels = ids_ref[:, pl.ds(pl.multiple_of(query_base + first, LANES), tile)]
        probs = jnp.exp2((scores[...] - tops[...]) * (size ** (-0.5) * math.log2(math.e)))
        share = 1.0 / jnp.sum(probs, axis=0, keepdims=True)
        weighted = jnp.dot(
            values[:, window_of(state)], probs.astype(jnp.bfloat16), preferred_element_type=jnp.float32
        )
        place = (slice(None), pl.ds(first, tile))
        attended[place] = jnp.where(labels == table[1, state], weighted * share, attended[place])

    def two_pairs(state):
        score(state + 1, scores_b, tops_b)
        weigh(state, scores_a, tops_a)
        score(state + 2, scores_a, tops_a)
        weigh(state + 1, scores_b, tops_b)

    def six_pairs(step, _):
        for place in range(0, 6, 2):
            two_pairs(6 * step + place)
        return 0

    def left_over(step, _):
        two_pairs(6 * whole + 2 * step)
        return 0

    score(0, scores_a, tops_a)
    whole = lax.div(pairs, 6)
    lax.fori_loop(0, whole, six_pairs, 0)
    lax.fori_loop(0, (pairs - 6 * whole) >> 1, left_over, 0)

    @pl.when(jnp.bitwise_and(pairs, 1) == 1)
    def _():
        weigh(pairs - 1, scores_a, tops_a)


def turned_keys(marked, block_ref):
    block = block_ref[KEY_AT : KEY_AT + PADDED].astype(jnp.float32)
    nothing = jnp.zeros((LANES - PADDED, block.shape[1]), jnp.float32)
    full = jnp.concatenate([marked, block[SPARE:], nothing], axis=0)
    return full.astype(jnp.bfloat16).T


def store_queries(marked, block_ref, queries, there):
    edge = block_ref[QUERY_AT : QUERY_AT + 16].astype(jnp.float32)
    edge = jnp.concatenate([marked, edge[SPARE:]], axis=0)
    queries[0:16, there] = edge.astype(jnp.bfloat16)
    queries[16:PADDED, there] = block_ref[QUERY_AT + 16 : QUERY_AT + PADDED]
    queries[PADDED:, there] = jnp.zeros((LANES - PADDED, block_ref.shape[1]), jnp.bfloat16)


def prepare_kernel(images, halo, ids_ref, out_weight_ref, *rest):
    got_refs, (keys, marks, before, weight, sems) = rest[: len(EARLY)], rest[len(EARLY) :]
    count = got_refs[0].shape[1]
    fetches = []
    for step, by in enumerate(ORDER):
        head = jnp.bitwise_xor(lax.rem(lax.axis_index("grp"), HEADS), by)
        first = lax.div(head, 2) * (2 * SIZE) + lax.rem(head, 2) * (SIZE - SPARE)
        fetches.append(
            pltpu.make_async_copy(
                out_weight_ref.at[pl.ds(pl.multiple_of(first, 16), PADDED)],
                weight.at[step * PADDED : (step + 1) * PADDED],
                sems.at[step],
            )
        )
        fetches[-1].start()
    before[...] = count_before(images, ids_ref[...])
    write_marks(images, ids_ref[...], marks)
    own = lax.rem(lax.axis_index("grp"), HEADS)
    for step, (by, ref) in enumerate(zip(EARLY, got_refs)):
        first = jnp.bitwise_xor(own, by) * count
        here = pl.ds(pl.multiple_of(halo + first, LANES), count)
        keys[step * count : (step + 1) * count, :] = turned_keys(marks[0, :, here], ref)
    for fetch in fetches:
        fetch.wait()


def attend_kernel(images, piggy, halo, ids_ref, before_ref, marks, early_keys, *rest):
    got_refs, rest = rest[:HEADS], rest[HEADS:]
    if piggy:
        text_ref, *rest = rest
    if halo:
        left_ref, right_ref, *rest = rest
    out_refs, rest = rest[:HEADS], rest[HEADS:]
    keys, values, queries, attended, *work, starts, table = rest
    count = got_refs[0].shape[1]
    padded = attended.shape[0]
    size = padded - SPARE
    total_rows = HEADS * count
    length = ids_ref.shape[1]
    ids = ids_ref[...]
    before = before_ref[...]
    for image in range(images + 1):
        starts[image] = before[image, 0]
    window, tile = work[0].shape
    pairs = list_pairs(images, total_rows, tile, length - window, halo, starts, table)

    own = lax.rem(lax.axis_index("grp"), HEADS)
    for step, (by, ref) in enumerate(zip(EARLY + LATE, got_refs)):
        first = jnp.bitwise_xor(own, by) * count
        here = pl.ds(pl.multiple_of(halo + first, LANES), count)
        there = pl.ds(pl.multiple_of(first, LANES), count)
        if by in EARLY:
            keys[here, :] = early_keys[step * count : (step + 1) * count, :]
        else:
            keys[here, :] = turned_keys(marks[0, :, here], ref)
        values[:, here] = ref[0:PADDED]
        store_queries(marks[1, :, here], ref, queries, there)
    if halo:
        for ref, here in ((left_ref, slice(0, halo)), (right_ref, slice(length - halo, length))):
            keys[here, :] = turned_keys(marks[0, :, here], ref)
            values[:, here] = ref[0:PADDED]
    attend_images(pairs, table, ids_ref, keys, values, queries, attended, work, halo)

    odd_head = lax.rem(own, 2) == 1
    mine = ids[:, halo : halo + total_rows]

    def placed(block, spare):
        even = jnp.concatenate([block[0:size], spare], axis=0)
        odd = jnp.concatenate([spare, block[0:size]], axis=0)
        return jnp.where(odd_head, odd, even)

    if piggy:
        nothing = jnp.zeros((SPARE, total_rows), jnp.float32)
        flat = placed(attended[...], nothing).astype(jnp.bfloat16)
        pooled = lax.dot_general(
            image_rows(mine, images), flat, (((1,), (1,)), ((), ())), preferred_element_type=jnp.float32
        )
        pooled = split_in_two(pooled, images)
        sums = spare_sums(got_refs)
        sums = split_in_two(sums + pltpu.roll(sums, images, axis=0), images)
        spare = jnp.concatenate(
            [pooled, jnp.zeros((SPARE, LANES - padded), jnp.float32), sums], axis=1
        )
        texts = text_ref[...].astype(jnp.float32)
        parts = [texts[:, at : at + count] for at in range(0, texts.shape[1], count)]
        unused = TEXT_ROWS - images * len(parts)
        below = jnp.concatenate(parts + [jnp.zeros((unused, count), jnp.float32)] * (unused > 0), axis=0)
        below = below.astype(jnp.bfloat16)
    else:
        spare = jnp.zeros((SPARE, count), jnp.float32)
    for by, out_ref in zip(ORDER, out_refs):
        there = pl.multiple_of(jnp.bitwise_xor(own, by) * count, LANES)
        out_ref[0:padded] = placed(attended[:, pl.ds(there, count)], spare).astype(jnp.bfloat16)
        if piggy:
            out_ref[padded:] = below


def joined_heads(got_refs, flat):
    own = lax.rem(lax.axis_index("grp"), HEADS)
    spares = []
    for step, (by, got_ref) in enumerate(zip(ORDER, got_refs)):
        odd = lax.rem(jnp.bitwise_xor(own, by), 2)
        at = step * PADDED
        top = got_ref[0:16].astype(jnp.float32)
        bottom = got_ref[PADDED - 16 : PADDED].astype(jnp.float32)
        spares.append(jnp.where(odd == 1, top[:SPARE], bottom[SPARE:]))
        top = jnp.concatenate([jnp.where(odd == 1, 0.0, top[:SPARE]), top[SPARE:]], axis=0)
        bottom = jnp.concatenate([bottom[:SPARE], jnp.where(odd == 1, bottom[SPARE:], 0.0)], axis=0)
        flat[at : at + 16] = top.astype(jnp.bfloat16)
        flat[at + 16 : at + PADDED - 16] = got_ref[16 : PADDED - 16]
        flat[at + PADDED - 16 : at + PADDED] = bottom.astype(jnp.bfloat16)
    return spares


def send_mixed_rows(rows_ref, weight_ref, flat, turned, mixed, mixed_ref, sems, meanwhile=None):
    turned[...] = flat[...].T
    pieces = sems.shape[0]
    step = rows_ref.shape[0] // pieces
    copies, value = [], None
    for piece in range(pieces):
        cut = slice(piece * step, (piece + 1) * step)
        if meanwhile is not None:
            value = meanwhile[piece](value)
        added = jnp.dot(turned[cut, :], weight_ref[...], preferred_element_type=jnp.float32)
        mixed[cut, :] = (rows_ref[cut, :].astype(jnp.float32) + added).astype(jnp.bfloat16)
        copies.append(pltpu.make_async_copy(mixed.at[cut], mixed_ref.at[cut], sems.at[piece]))
        copies[-1].start()
    return copies


def unit_rows(matrix):
    return matrix * lax.rsqrt(jnp.sum(matrix * matrix, axis=1, keepdims=True) + 1e-06)


def losses(cosine, labels):
    logits = -labels * (logit_scale * cosine + logit_bias)
    return jnp.maximum(logits, 0.0) + jnp.log1p(jnp.exp(-jnp.abs(logits)))


def finish_kernel(images, rows_ref, weight_ref, text_ref, *rest):
    got_refs, rest = rest[:HEADS], rest[HEADS:]
    mixed_ref, loss_ref, flat, turned, mixed, sems, pooled_heads, patch_sums, far_texts, loss, loss_sem = rest
    spares = joined_heads(got_refs, flat)
    own = lax.rem(lax.axis_index("grp"), HEADS)
    patch_sums[:, HEADS * LANES :] = spares[0][:, 2 * LANES :]
    for step, (by, spare) in enumerate(zip(ORDER, spares)):
        pooled_heads[:, step * PADDED : (step + 1) * PADDED] = spare[:, 0:PADDED]
        head = jnp.bitwise_xor(own, by)
        patch_sums[:, pl.ds(pl.multiple_of(head * LANES, LANES), LANES)] = spare[:, LANES : 2 * LANES]
        below = got_refs[step][PADDED:].astype(jnp.float32)
        count = below.shape[1]
        for part in range(patch_sums.shape[1] // count):
            here = slice(part * count, (part + 1) * count)
            far_texts[head, :, here] = below[part * images : (part + 1) * images]

    def find_images(_):
        pooled = jnp.dot(
            pooled_heads[...].astype(jnp.bfloat16), weight_ref[...], preferred_element_type=jnp.float32
        )
        pooled = pooled + patch_sums[...]
        others = [far_texts[place] for place in range(lax.axis_size("blk") - 1)]
        texts = jnp.concatenate([text_ref[...].astype(jnp.float32)] + others, axis=0)
        return pooled + pltpu.roll(pooled, images, axis=0), unit_rows(texts)

    def find_cosines(vectors):
        pooled, text_vecs = vectors
        return lax.dot_general(
            text_vecs,
            unit_rows(pooled),
            (((1,), (1,)), ((), ())),
            precision=lax.Precision.HIGHEST,
            preferred_element_type=jnp.float32,
        )

    def find_losses(cosine):
        text = lax.broadcasted_iota(jnp.int32, cosine.shape, 0)
        image = lax.broadcasted_iota(jnp.int32, cosine.shape, 1)
        terms = losses(cosine, jnp.where(text == image, 1.0, -1.0))
        loss[...] = jnp.sum(terms, axis=0, keepdims=True)[:, 0:images]
        loss_copy.start()

    loss_copy = pltpu.make_async_copy(loss, loss_ref, loss_sem)
    meanwhile = (find_images, find_cosines, find_losses)
    copies = send_mixed_rows(rows_ref, weight_ref, flat, turned, mixed, mixed_ref, sems, meanwhile)
    for copy in copies + [loss_copy]:
        copy.wait()


def mix_kernel(rows_ref, weight_ref, *rest):
    got_refs, rest = rest[:HEADS], rest[HEADS:]
    mixed_ref, flat, turned, mixed, sems = rest
    joined_heads(got_refs, flat)
    for copy in send_mixed_rows(rows_ref, weight_ref, flat, turned, mixed, mixed_ref, sems):
        copy.wait()


def in_vmem(count):
    return [pl.BlockSpec(memory_space=pltpu.VMEM)] * count


def in_hbm(value):
    return pltpu.with_memory_space_constraint(value, pltpu.HBM)


def call(kernel, out_shape, scratch, in_specs, flops, out_specs=None):
    if out_specs is None:
        out_specs = jax.tree.map(lambda _: pl.BlockSpec(memory_space=pltpu.VMEM), out_shape)
    return pl.pallas_call(
        kernel,
        out_shape=out_shape,
        in_specs=in_specs,
        out_specs=out_specs,
        scratch_shapes=scratch,
        compiler_params=pltpu.CompilerParams(vmem_limit_bytes=VMEM_LIMIT),
        cost_estimate=pl.CostEstimate(flops=flops, bytes_accessed=8 << 20, transcendentals=0),
    )


def moved(value, axis, pairs):
    return lax.ppermute(value, axis, pairs)


def partner(place, by, peers):
    return place ^ by if peers & (peers - 1) == 0 else (place + by) % peers


def all_texts(texts):
    peers = lax.axis_size("blk")
    steps = [[(partner(i, by, peers), i) for i in range(peers)] for by in range(1, peers)]
    return jnp.concatenate([texts] + [moved(texts, "blk", pairs) for pairs in steps], axis=0)


def one_text_block(texts):
    peers = lax.axis_size("blk")
    pairs = []
    for place in range(lax.axis_size("grp")):
        by = place % (peers - 1) + 1
        pairs += [(place * peers + partner(i, by, peers), place * peers + i) for i in range(peers)]
    return moved(texts, ("grp", "blk"), pairs)


def traded(blocks):
    peers = range(lax.axis_size("grp"))
    trades = {by: moved(blocks[by], "grp", [(i, i ^ by) for i in peers]) for by in ORDER if by}
    return {**trades, 0: blocks[0]}


def local(patches, segment_ids, qkv_weight, out_weight, text_embed):
    rows = patches[0]
    count, depth = rows.shape
    width = out_weight.shape[0]
    size = width // HEADS
    padded = size + SPARE
    images = text_embed.shape[0]
    group_size = lax.axis_size("grp")
    parts = group_size // HEADS
    piggy = (
        parts == 1
        and 2 * images == SPARE
        and count >= depth - (HEADS - 2) * LANES
        and depth % count == 0
        and images * (depth // count) <= TEXT_ROWS
        and 1 < lax.axis_size("blk") <= HEADS + 1
    )
    bf16, f32 = jnp.bfloat16, jnp.float32
    shape = jax.ShapeDtypeStruct

    block = shape((3 * size + SPARE, count), bf16)
    hbm = pl.BlockSpec(memory_space=pltpu.HBM)
    turned_weight = qkv_weight.T
    normed, sums, *sent = call(
        functools.partial(far_kernel, images, piggy),
        (shape((count, depth), bf16), shape((SPARE, depth), f32), block, block),
        [
            pltpu.VMEM((1, count), jnp.int32),
            pltpu.VMEM((count, depth), bf16),
            pltpu.VMEM((3, 2 * size, depth), bf16),
            pltpu.SemaphoreType.DMA,
            pltpu.SemaphoreType.DMA,
            pltpu.SemaphoreType.DMA((3,)),
        ],
        [hbm] * 3,
        2 * count * depth * 6 * size,
    )(in_hbm(segment_ids), in_hbm(rows), in_hbm(turned_weight))
    sent += call(
        functools.partial(near_kernel, piggy),
        (block,) * 6,
        [],
        in_vmem(3),
        2 * count * depth * 18 * size,
    )(normed, sums, turned_weight)
    sent = dict(zip((6, 7, 2, 3, 4, 5, 0, 1), sent))
    if piggy:
        late_texts, sent[0] = lax.optimization_barrier((text_embed, sent[0]))
        halos_and_texts = [one_text_block(late_texts)]
    else:
        halos_and_texts = []
    got = traded(sent)

    length = HEADS * count
    halo = 0
    near_ids = segment_ids
    if parts > 1:
        halo = rounded_up(MAXP - 1, LANES)
        part = lax.axis_index("grp") // HEADS
        whole_ids = jnp.concatenate(
            [
                jnp.full((1, halo), -1, jnp.int32),
                segment_ids,
                jnp.full((1, halo), images, jnp.int32),
            ],
            axis=1,
        )
        near_ids = lax.dynamic_slice_in_dim(whole_ids, part * length, length + 2 * halo, axis=1)
        order = jnp.bitwise_xor(lax.axis_index("grp") % HEADS, jnp.arange(HEADS))
        flat = jnp.stack([got[by] for by in range(HEADS)])[order][:, : 2 * size].transpose(1, 0, 2).reshape(2 * size, length)
        flat = jnp.concatenate([flat, jnp.zeros((16, length), bf16)], axis=0)
        ahead = [(i, i + HEADS) for i in range(group_size - HEADS)]
        back = [(i + HEADS, i) for i in range(group_size - HEADS)]
        left = moved(flat[:, length - halo :], "grp", ahead)
        right = moved(flat[:, :halo], "grp", back)
        halos_and_texts += [left, right]
    reach = length + 2 * halo
    window = min(rounded_up(MAXP + LANES - 1, LANES), reach)
    tile = 2 * LANES
    early_keys, marks, before, weight = call(
        functools.partial(prepare_kernel, images, halo),
        (
            shape((len(EARLY) * count, LANES), bf16),
            shape((2, SPARE, reach), f32),
            shape((rounded_up(images + 1, SPARE), LANES), jnp.int32),
            shape((HEADS * padded, depth), bf16),
        ),
        [pltpu.SemaphoreType.DMA((HEADS,))],
        in_vmem(1) + [hbm] + in_vmem(len(EARLY)),
        1 << 30,
    )(near_ids, in_hbm(out_weight), *[got[by] for by in EARLY])
    operands = [near_ids, before, marks, early_keys, *[got[by] for by in EARLY + LATE], *halos_and_texts]
    answers = call(
        functools.partial(attend_kernel, images, piggy, halo),
        (shape((padded + TEXT_ROWS * piggy, count), bf16),) * HEADS,
        [
            pltpu.VMEM((reach, LANES), bf16),
            pltpu.VMEM((padded, reach), bf16),
            pltpu.VMEM((LANES, length), bf16),
            pltpu.VMEM((padded, length), f32),
            pltpu.VMEM((window, tile), f32),
            pltpu.VMEM((window, tile), f32),
            pltpu.VMEM((1, tile), f32),
            pltpu.VMEM((1, tile), f32),
            pltpu.SMEM((images + 1,), jnp.int32),
            pltpu.SMEM((3, length // tile + images), jnp.int32),
        ],
        in_vmem(len(operands)),
        4 * size * length * MAXP,
    )(*operands)
    home = traded(dict(zip(ORDER, answers)))
    home = [home[by] for by in ORDER]

    joined = [
        pltpu.VMEM((HEADS * padded, count), bf16),
        pltpu.VMEM((count, HEADS * padded), bf16),
        pltpu.VMEM((count, depth), bf16),
        pltpu.SemaphoreType.DMA((3,)),
    ]
    flops = 2 * count * depth * width
    if piggy:
        mixed, row_loss = call(
            functools.partial(finish_kernel, images),
            (shape((count, depth), bf16), shape((1, images), f32)),
            joined
            + [
                pltpu.VMEM((SPARE, HEADS * padded), f32),
                pltpu.VMEM((SPARE, depth), f32),
                pltpu.VMEM((HEADS, images, depth), f32),
                pltpu.VMEM((1, images), f32),
                pltpu.SemaphoreType.DMA,
            ],
            in_vmem(3 + HEADS),
            flops,
            (hbm, hbm),
        )(rows, weight, text_embed, *home)
        return (mixed[None], row_loss[0])
    mixed = call(mix_kernel, shape((count, depth), bf16), joined, in_vmem(2 + HEADS), flops, hbm)(
        rows, weight, *home
    )
    own_ids = lax.dynamic_slice_in_dim(segment_ids[0], lax.axis_index("grp") * count, count)
    onehot = (own_ids[None, :] == jnp.arange(images, dtype=jnp.int32)[:, None]).astype(bf16)
    pooled = lax.psum(jnp.dot(onehot, mixed, preferred_element_type=f32), "grp")
    text_vecs = unit_rows(all_texts(text_embed).astype(f32))
    cosine = jnp.dot(unit_rows(pooled), text_vecs.T, precision=lax.Precision.HIGHEST)
    same = jnp.arange(images)[:, None] == jnp.arange(text_vecs.shape[0])[None, :]
    row_loss = jnp.sum(losses(cosine, jnp.where(same, 1.0, -1.0)), axis=1)
    return (mixed[None], row_loss)


def solution(mesh):
    placed = (P("blk", "grp", None), P("blk", None), P(), P(), P("blk", None))
    return jax.shard_map(
        local,
        mesh=mesh,
        in_specs=placed,
        out_specs=(P("blk", "grp", None), P("blk")),
        check_vma=False,
    )
```

```python
import functools
import math

import jax
import jax.numpy as jnp
from jax import lax
from jax.experimental import pallas as pl
from jax.experimental.pallas import tpu as pltpu
from jax.sharding import PartitionSpec as P

HEADS = 8
MAXP = 1024
LANES = 128
SPARE = 8
SIZE = 72
PADDED = SIZE + SPARE
KEY_AT = SIZE - SPARE
QUERY_AT = 2 * SIZE
TEXT_ROWS = 16
HIDDEN = -1e30
ORDER = (6, 7, 1, 2, 4, 3, 5, 0)
EARLY = (6, 7, 1, 0)
LATE = (2, 4, 3, 5)

logit_scale = 30.0
logit_bias = -5.0

VMEM_LIMIT = 32 * 1024 * 1024


def rounded_up(value, step):
    return (value + step - 1) // step * step


def split_in_two(total, images):
    row = lax.broadcasted_iota(jnp.int32, total.shape, 0)
    main = total.astype(jnp.bfloat16).astype(jnp.float32)
    return jnp.where(row < images, main, total - main)


def image_rows(ids, images):
    row = lax.broadcasted_iota(jnp.int32, (SPARE, ids.shape[1]), 0)
    return (lax.rem(row, images) == ids).astype(jnp.float32).astype(jnp.bfloat16)


def head_blocks(query, key, value, sums, pair):
    size = query.shape[0] // 2
    count = query.shape[1]
    for place in range(2):
        here = slice(place * size, (place + 1) * size)
        if sums is None:
            spare = jnp.zeros((SPARE, count), jnp.float32)
        else:
            first = pl.multiple_of((2 * pair + place) * LANES, LANES)
            parts = [sums[:, pl.ds(first, LANES)], sums[:, HEADS * LANES :]]
            held = sum(part.shape[1] for part in parts)
            spare = jnp.concatenate(parts + [jnp.zeros((SPARE, count - held), jnp.float32)], axis=1)
        yield jnp.concatenate([value[here], key[here], spare, query[here]], axis=0)


def store_by_core(core, blocks, same_ref, cross_ref):
    first, second = blocks
    same_ref[...] = jnp.where(core == 0, first, second).astype(jnp.bfloat16)
    cross_ref[...] = jnp.where(core == 0, second, first).astype(jnp.bfloat16)


def place_in_group():
    own = lax.rem(lax.axis_index("grp"), HEADS)
    return lax.div(own, 2), lax.rem(own, 2)


def far_kernel(images, piggy, ids_ref, rows_ref, weight_ref, normed_ref, sums_ref, same_ref, cross_ref, own_ids, rows_held, weight, id_sem, row_sem, sems):
    count, depth = rows_ref.shape
    width = weight_ref.shape[0] // 3
    wide = weight.shape[1]
    rows_fetch = pltpu.make_async_copy(rows_ref, rows_held, row_sem)
    rows_fetch.start()
    own = pl.multiple_of(lax.axis_index("grp") * count, LANES)
    ids_fetch = pltpu.make_async_copy(ids_ref.at[:, pl.ds(own, count)], own_ids, id_sem)
    ids_fetch.start()
    pair, core = place_in_group()
    pair = jnp.bitwise_xor(pair, 3)
    fetches = []
    for at in range(3):
        first = pl.multiple_of(at * width + pair * wide, 16)
        fetches.append(pltpu.make_async_copy(weight_ref.at[pl.ds(first, wide)], weight.at[at], sems.at[at]))
    for fetch in fetches:
        fetch.start()
    ids_fetch.wait()
    rows_fetch.wait()
    rows = rows_held[...]
    if piggy:
        sums = jnp.dot(image_rows(own_ids[...], images), rows, preferred_element_type=jnp.float32)
        sums_ref[...] = split_in_two(sums, images)
    values = rows.astype(jnp.float32)
    center = values - jnp.mean(values, axis=1, keepdims=True)
    spread = jnp.mean(center * center, axis=1, keepdims=True)
    normed = (center * lax.rsqrt(spread + 1e-06)).astype(jnp.bfloat16)
    normed_ref[...] = normed.T
    for fetch in fetches:
        fetch.wait()
    parts = [
        jnp.dot(weight[at], normed_ref[...], preferred_element_type=jnp.float32) for at in range(3)
    ]
    store_by_core(core, head_blocks(*parts, sums_ref if piggy else None, pair), same_ref, cross_ref)


def near_kernel(piggy, normed_ref, sums_ref, weight_ref, *out_refs):
    width = weight_ref.shape[0] // 3
    wide = 2 * width // HEADS
    own, core = place_in_group()
    for step, move in enumerate((1, 2, 0)):
        pair = jnp.bitwise_xor(own, move)
        parts = []
        for at in range(3):
            here = pl.ds(pl.multiple_of(at * width + pair * wide, 16), wide)
            parts.append(
                jnp.dot(weight_ref[here, :], normed_ref[...], preferred_element_type=jnp.float32)
            )
        blocks = head_blocks(*parts, sums_ref if piggy else None, pair)
        store_by_core(core, blocks, *out_refs[2 * step : 2 * step + 2])


def count_before(images, ids):
    image = lax.broadcasted_iota(jnp.int32, (rounded_up(images + 1, SPARE), ids.shape[1]), 0)
    before = jnp.sum((ids < image).astype(jnp.int32), axis=1, keepdims=True)
    return jnp.broadcast_to(before, (before.shape[0], LANES))


def write_marks(images, ids, marks):
    bits = max(1, (images - 1).bit_length())
    row = lax.broadcasted_iota(jnp.int32, (SPARE, ids.shape[1]), 0)
    bit = jnp.bitwise_and(lax.shift_right_logical(jnp.broadcast_to(ids, row.shape), row >> 1), 1)
    odd = jnp.bitwise_and(row, 1)
    used = row < 2 * bits
    outside = jnp.logical_or(ids < 0, ids >= images)
    key_side = jnp.where(odd == 1, bit, 1 - bit).astype(jnp.float32)
    key_side = jnp.where(outside, 1.0, key_side)
    marks[0] = jnp.where(used, key_side * HIDDEN, 0.0)
    marks[1] = jnp.where(used, jnp.where(odd == 1, 1 - bit, bit), 0).astype(jnp.float32)


def spare_sums(refs):
    parts = [ref[QUERY_AT : QUERY_AT + 16].astype(jnp.float32)[0:SPARE, 0 : 2 * LANES] for ref in refs]
    return sum(parts[1:], parts[0])


def image_at(images, starts, position):
    found = jnp.int32(0)
    for image in range(1, images):
        found += (starts[image] <= position).astype(jnp.int32)
    return found


def list_pairs(images, held, tile, last_begin, base, starts, table):
    tiles = held // tile
    shift = tile.bit_length() - 1
    low = image_at(images, starts, base)
    high = image_at(images, starts, base + held - 1)

    def bounds(image):
        first = jnp.maximum(starts[image] - base, 0) >> shift
        last = (jnp.minimum(starts[image + 1] - base, held) - 1) >> shift
        return jnp.minimum(first, tiles - 1), last

    pairs = jnp.int32(0)
    for image in range(images):
        first, last = bounds(image)
        wanted = jnp.logical_and(low <= image, image <= high)
        pairs += jnp.where(wanted, last - first + 1, 0)
    at, image = jnp.int32(0), low
    for step in range(tiles + images):
        table[0, step] = at
        table[1, step] = image
        table[2, step] = jnp.minimum(jnp.bitwise_and(starts[image], -LANES), last_begin)
        more = at < bounds(image)[1]
        later = jnp.minimum(image + 1, images - 1)
        at, image = jnp.where(more, at + 1, bounds(later)[0]), jnp.where(more, image, later)
    return pairs


def attend_images(pairs, table, ids_ref, keys, values, queries, attended, work, query_base):
    scores_a, scores_b, tops_a, tops_b = work
    window, tile = scores_a.shape
    size = attended.shape[0] - SPARE

    def window_of(state):
        return pl.ds(pl.multiple_of(table[2, state], LANES), window)

    def score(state, scores, tops):
        query = queries[:, pl.ds(pl.multiple_of(table[0, state] * tile, tile), tile)]
        found = jnp.dot(keys[window_of(state), :], query, preferred_element_type=jnp.float32)
        scores[...] = found
        tops[...] = jnp.max(found, axis=0, keepdims=True)

    def weigh(state, scores, tops):
        first = pl.multiple_of(table[0, state] * tile, tile)
        labels = ids_ref[:, pl.ds(pl.multiple_of(query_base + first, LANES), tile)]
        probs = jnp.exp2((scores[...] - tops[...]) * (size ** (-0.5) * math.log2(math.e)))
        share = 1.0 / jnp.sum(probs, axis=0, keepdims=True)
        weighted = jnp.dot(
            values[:, window_of(state)], probs.astype(jnp.bfloat16), preferred_element_type=jnp.float32
        )
        place = (slice(None), pl.ds(first, tile))
        attended[place] = jnp.where(labels == table[1, state], weighted * share, attended[place])

    def two_pairs(state):
        score(state + 1, scores_b, tops_b)
        weigh(state, scores_a, tops_a)
        score(state + 2, scores_a, tops_a)
        weigh(state + 1, scores_b, tops_b)

    def six_pairs(step, _):
        for place in range(0, 6, 2):
            two_pairs(6 * step + place)
        return 0

    def left_over(step, _):
        two_pairs(6 * whole + 2 * step)
        return 0

    score(0, scores_a, tops_a)
    whole = lax.div(pairs, 6)
    lax.fori_loop(0, whole, six_pairs, 0)
    lax.fori_loop(0, (pairs - 6 * whole) >> 1, left_over, 0)

    @pl.when(jnp.bitwise_and(pairs, 1) == 1)
    def _():
        weigh(pairs - 1, scores_a, tops_a)


def turned_keys(marked, block_ref):
    block = block_ref[KEY_AT : KEY_AT + PADDED].astype(jnp.float32)
    nothing = jnp.zeros((LANES - PADDED, block.shape[1]), jnp.float32)
    full = jnp.concatenate([marked, block[SPARE:], nothing], axis=0)
    return full.astype(jnp.bfloat16).T


def store_queries(marked, block_ref, queries, there):
    edge = block_ref[QUERY_AT : QUERY_AT + 16].astype(jnp.float32)
    edge = jnp.concatenate([marked, edge[SPARE:]], axis=0)
    queries[0:16, there] = edge.astype(jnp.bfloat16)
    queries[16:PADDED, there] = block_ref[QUERY_AT + 16 : QUERY_AT + PADDED]
    queries[PADDED:, there] = jnp.zeros((LANES - PADDED, block_ref.shape[1]), jnp.bfloat16)


def prepare_kernel(images, halo, ids_ref, out_weight_ref, *rest):
    got_refs, (keys, marks, before, weight, sems) = rest[: len(EARLY)], rest[len(EARLY) :]
    count = got_refs[0].shape[1]
    fetches = []
    for step, by in enumerate(ORDER):
        head = jnp.bitwise_xor(lax.rem(lax.axis_index("grp"), HEADS), by)
        first = lax.div(head, 2) * (2 * SIZE) + lax.rem(head, 2) * (SIZE - SPARE)
        fetches.append(
            pltpu.make_async_copy(
                out_weight_ref.at[pl.ds(pl.multiple_of(first, 16), PADDED)],
                weight.at[step * PADDED : (step + 1) * PADDED],
                sems.at[step],
            )
        )
        fetches[-1].start()
    before[...] = count_before(images, ids_ref[...])
    write_marks(images, ids_ref[...], marks)
    own = lax.rem(lax.axis_index("grp"), HEADS)
    for step, (by, ref) in enumerate(zip(EARLY, got_refs)):
        first = jnp.bitwise_xor(own, by) * count
        here = pl.ds(pl.multiple_of(halo + first, LANES), count)
        keys[step * count : (step + 1) * count, :] = turned_keys(marks[0, :, here], ref)
    for fetch in fetches:
        fetch.wait()


def attend_kernel(images, piggy, halo, ids_ref, before_ref, marks, early_keys, *rest):
    got_refs, rest = rest[:HEADS], rest[HEADS:]
    if piggy:
        text_ref, *rest = rest
    if halo:
        left_ref, right_ref, *rest = rest
    out_refs, rest = rest[:HEADS], rest[HEADS:]
    keys, values, queries, attended, *work, starts, table = rest
    count = got_refs[0].shape[1]
    padded = attended.shape[0]
    size = padded - SPARE
    total_rows = HEADS * count
    length = ids_ref.shape[1]
    ids = ids_ref[...]
    before = before_ref[...]
    for image in range(images + 1):
        starts[image] = before[image, 0]
    window, tile = work[0].shape
    pairs = list_pairs(images, total_rows, tile, length - window, halo, starts, table)

    own = lax.rem(lax.axis_index("grp"), HEADS)
    for step, (by, ref) in enumerate(zip(EARLY + LATE, got_refs)):
        first = jnp.bitwise_xor(own, by) * count
        here = pl.ds(pl.multiple_of(halo + first, LANES), count)
        there = pl.ds(pl.multiple_of(first, LANES), count)
        if by in EARLY:
            keys[here, :] = early_keys[step * count : (step + 1) * count, :]
        else:
            keys[here, :] = turned_keys(marks[0, :, here], ref)
        values[:, here] = ref[0:PADDED]
        store_queries(marks[1, :, here], ref, queries, there)
    if halo:
        for ref, here in ((left_ref, slice(0, halo)), (right_ref, slice(length - halo, length))):
            keys[here, :] = turned_keys(marks[0, :, here], ref)
            values[:, here] = ref[0:PADDED]
    attend_images(pairs, table, ids_ref, keys, values, queries, attended, work, halo)

    odd_head = lax.rem(own, 2) == 1
    mine = ids[:, halo : halo + total_rows]

    def placed(block, spare):
        even = jnp.concatenate([block[0:size], spare], axis=0)
        odd = jnp.concatenate([spare, block[0:size]], axis=0)
        return jnp.where(odd_head, odd, even)

    if piggy:
        nothing = jnp.zeros((SPARE, total_rows), jnp.float32)
        flat = placed(attended[...], nothing).astype(jnp.bfloat16)
        pooled = lax.dot_general(
            image_rows(mine, images), flat, (((1,), (1,)), ((), ())), preferred_element_type=jnp.float32
        )
        pooled = split_in_two(pooled, images)
        sums = spare_sums(got_refs)
        sums = split_in_two(sums + pltpu.roll(sums, images, axis=0), images)
        spare = jnp.concatenate(
            [pooled, jnp.zeros((SPARE, LANES - padded), jnp.float32), sums], axis=1
        )
        texts = text_ref[...].astype(jnp.float32)
        parts = [texts[:, at : at + count] for at in range(0, texts.shape[1], count)]
        unused = TEXT_ROWS - images * len(parts)
        below = jnp.concatenate(parts + [jnp.zeros((unused, count), jnp.float32)] * (unused > 0), axis=0)
        below = below.astype(jnp.bfloat16)
    else:
        spare = jnp.zeros((SPARE, count), jnp.float32)
    for by, out_ref in zip(ORDER, out_refs):
        there = pl.multiple_of(jnp.bitwise_xor(own, by) * count, LANES)
        out_ref[0:padded] = placed(attended[:, pl.ds(there, count)], spare).astype(jnp.bfloat16)
        if piggy:
            out_ref[padded:] = below


def joined_heads(got_refs, flat):
    own = lax.rem(lax.axis_index("grp"), HEADS)
    spares = []
    for step, (by, got_ref) in enumerate(zip(ORDER, got_refs)):
        odd = lax.rem(jnp.bitwise_xor(own, by), 2)
        at = step * PADDED
        top = got_ref[0:16].astype(jnp.float32)
        bottom = got_ref[PADDED - 16 : PADDED].astype(jnp.float32)
        spares.append(jnp.where(odd == 1, top[:SPARE], bottom[SPARE:]))
        top = jnp.concatenate([jnp.where(odd == 1, 0.0, top[:SPARE]), top[SPARE:]], axis=0)
        bottom = jnp.concatenate([bottom[:SPARE], jnp.where(odd == 1, bottom[SPARE:], 0.0)], axis=0)
        flat[at : at + 16] = top.astype(jnp.bfloat16)
        flat[at + 16 : at + PADDED - 16] = got_ref[16 : PADDED - 16]
        flat[at + PADDED - 16 : at + PADDED] = bottom.astype(jnp.bfloat16)
    return spares


def send_mixed_rows(rows_ref, weight_ref, flat, turned, mixed, mixed_ref, sems, meanwhile=None):
    turned[...] = flat[...].T
    pieces = sems.shape[0]
    step = rows_ref.shape[0] // pieces
    copies, value = [], None
    for piece in range(pieces):
        cut = slice(piece * step, (piece + 1) * step)
        if meanwhile is not None:
            value = meanwhile[piece](value)
        added = jnp.dot(turned[cut, :], weight_ref[...], preferred_element_type=jnp.float32)
        mixed[cut, :] = (rows_ref[cut, :].astype(jnp.float32) + added).astype(jnp.bfloat16)
        copies.append(pltpu.make_async_copy(mixed.at[cut], mixed_ref.at[cut], sems.at[piece]))
        copies[-1].start()
    return copies


def unit_rows(matrix):
    return matrix * lax.rsqrt(jnp.sum(matrix * matrix, axis=1, keepdims=True) + 1e-06)


def losses(cosine, labels):
    logits = -labels * (logit_scale * cosine + logit_bias)
    return jnp.maximum(logits, 0.0) + jnp.log1p(jnp.exp(-jnp.abs(logits)))


def finish_kernel(images, rows_ref, weight_ref, text_ref, *rest):
    got_refs, rest = rest[:HEADS], rest[HEADS:]
    mixed_ref, loss_ref, flat, turned, mixed, sems, pooled_heads, patch_sums, far_texts, loss, loss_sem = rest
    spares = joined_heads(got_refs, flat)
    own = lax.rem(lax.axis_index("grp"), HEADS)
    patch_sums[:, HEADS * LANES :] = spares[0][:, 2 * LANES :]
    for step, (by, spare) in enumerate(zip(ORDER, spares)):
        pooled_heads[:, step * PADDED : (step + 1) * PADDED] = spare[:, 0:PADDED]
        head = jnp.bitwise_xor(own, by)
        patch_sums[:, pl.ds(pl.multiple_of(head * LANES, LANES), LANES)] = spare[:, LANES : 2 * LANES]
        below = got_refs[step][PADDED:].astype(jnp.float32)
        count = below.shape[1]
        for part in range(patch_sums.shape[1] // count):
            here = slice(part * count, (part + 1) * count)
            far_texts[head, :, here] = below[part * images : (part + 1) * images]

    def find_images(_):
        pooled = jnp.dot(
            pooled_heads[...].astype(jnp.bfloat16), weight_ref[...], preferred_element_type=jnp.float32
        )
        pooled = pooled + patch_sums[...]
        others = [far_texts[place] for place in range(lax.axis_size("blk") - 1)]
        texts = jnp.concatenate([text_ref[...].astype(jnp.float32)] + others, axis=0)
        return pooled + pltpu.roll(pooled, images, axis=0), unit_rows(texts)

    def find_cosines(vectors):
        pooled, text_vecs = vectors
        return lax.dot_general(
            text_vecs,
            unit_rows(pooled),
            (((1,), (1,)), ((), ())),
            precision=lax.Precision.HIGHEST,
            preferred_element_type=jnp.float32,
        )

    def find_losses(cosine):
        text = lax.broadcasted_iota(jnp.int32, cosine.shape, 0)
        image = lax.broadcasted_iota(jnp.int32, cosine.shape, 1)
        terms = losses(cosine, jnp.where(text == image, 1.0, -1.0))
        loss[...] = jnp.sum(terms, axis=0, keepdims=True)[:, 0:images]
        loss_copy.start()

    loss_copy = pltpu.make_async_copy(loss, loss_ref, loss_sem)
    meanwhile = (find_images, find_cosines, find_losses)
    copies = send_mixed_rows(rows_ref, weight_ref, flat, turned, mixed, mixed_ref, sems, meanwhile)
    for copy in copies + [loss_copy]:
        copy.wait()


def mix_kernel(rows_ref, weight_ref, *rest):
    got_refs, rest = rest[:HEADS], rest[HEADS:]
    mixed_ref, flat, turned, mixed, sems = rest
    joined_heads(got_refs, flat)
    for copy in send_mixed_rows(rows_ref, weight_ref, flat, turned, mixed, mixed_ref, sems):
        copy.wait()


def in_vmem(count):
    return [pl.BlockSpec(memory_space=pltpu.VMEM)] * count


def in_hbm(value):
    return pltpu.with_memory_space_constraint(value, pltpu.HBM)


def call(kernel, out_shape, scratch, in_specs, flops, out_specs=None):
    if out_specs is None:
        out_specs = jax.tree.map(lambda _: pl.BlockSpec(memory_space=pltpu.VMEM), out_shape)
    return pl.pallas_call(
        kernel,
        out_shape=out_shape,
        in_specs=in_specs,
        out_specs=out_specs,
        scratch_shapes=scratch,
        compiler_params=pltpu.CompilerParams(vmem_limit_bytes=VMEM_LIMIT),
        cost_estimate=pl.CostEstimate(flops=flops, bytes_accessed=8 << 20, transcendentals=0),
    )


def moved(value, axis, pairs):
    return lax.ppermute(value, axis, pairs)


def partner(place, by, peers):
    return place ^ by if peers & (peers - 1) == 0 else (place + by) % peers


def all_texts(texts):
    peers = lax.axis_size("blk")
    steps = [[(partner(i, by, peers), i) for i in range(peers)] for by in range(1, peers)]
    return jnp.concatenate([texts] + [moved(texts, "blk", pairs) for pairs in steps], axis=0)


def one_text_block(texts):
    peers = lax.axis_size("blk")
    pairs = []
    for place in range(lax.axis_size("grp")):
        by = place % (peers - 1) + 1
        pairs += [(place * peers + partner(i, by, peers), place * peers + i) for i in range(peers)]
    return moved(texts, ("grp", "blk"), pairs)


def traded(blocks):
    peers = range(lax.axis_size("grp"))
    trades = {by: moved(blocks[by], "grp", [(i, i ^ by) for i in peers]) for by in ORDER if by}
    return {**trades, 0: blocks[0]}


def local(patches, segment_ids, qkv_weight, out_weight, text_embed):
    rows = patches[0]
    count, depth = rows.shape
    width = out_weight.shape[0]
    size = width // HEADS
    padded = size + SPARE
    images = text_embed.shape[0]
    group_size = lax.axis_size("grp")
    parts = group_size // HEADS
    piggy = (
        parts == 1
        and 2 * images == SPARE
        and count >= depth - (HEADS - 2) * LANES
        and depth % count == 0
        and images * (depth // count) <= TEXT_ROWS
        and 1 < lax.axis_size("blk") <= HEADS + 1
    )
    bf16, f32 = jnp.bfloat16, jnp.float32
    shape = jax.ShapeDtypeStruct

    block = shape((3 * size + SPARE, count), bf16)
    hbm = pl.BlockSpec(memory_space=pltpu.HBM)
    turned_weight = qkv_weight.T
    normed, sums, *sent = call(
        functools.partial(far_kernel, images, piggy),
        (shape((depth, count), bf16), shape((SPARE, depth), f32), block, block),
        [
            pltpu.VMEM((1, count), jnp.int32),
            pltpu.VMEM((count, depth), bf16),
            pltpu.VMEM((3, 2 * size, depth), bf16),
            pltpu.SemaphoreType.DMA,
            pltpu.SemaphoreType.DMA,
            pltpu.SemaphoreType.DMA((3,)),
        ],
        [hbm] * 3,
        2 * count * depth * 6 * size,
    )(in_hbm(segment_ids), in_hbm(rows), in_hbm(turned_weight))
    sent += call(
        functools.partial(near_kernel, piggy),
        (block,) * 6,
        [],
        in_vmem(3),
        2 * count * depth * 18 * size,
    )(normed, sums, turned_weight)
    sent = dict(zip((6, 7, 2, 3, 4, 5, 0, 1), sent))
    if piggy:
        late_texts, sent[0] = lax.optimization_barrier((text_embed, sent[0]))
        halos_and_texts = [one_text_block(late_texts)]
    else:
        halos_and_texts = []
    got = traded(sent)

    length = HEADS * count
    halo = 0
    near_ids = segment_ids
    if parts > 1:
        halo = rounded_up(MAXP - 1, LANES)
        part = lax.axis_index("grp") // HEADS
        whole_ids = jnp.concatenate(
            [
                jnp.full((1, halo), -1, jnp.int32),
                segment_ids,
                jnp.full((1, halo), images, jnp.int32),
            ],
            axis=1,
        )
        near_ids = lax.dynamic_slice_in_dim(whole_ids, part * length, length + 2 * halo, axis=1)
        order = jnp.bitwise_xor(lax.axis_index("grp") % HEADS, jnp.arange(HEADS))
        flat = jnp.stack([got[by] for by in range(HEADS)])[order][:, : 2 * size].transpose(1, 0, 2).reshape(2 * size, length)
        flat = jnp.concatenate([flat, jnp.zeros((16, length), bf16)], axis=0)
        ahead = [(i, i + HEADS) for i in range(group_size - HEADS)]
        back = [(i + HEADS, i) for i in range(group_size - HEADS)]
        left = moved(flat[:, length - halo :], "grp", ahead)
        right = moved(flat[:, :halo], "grp", back)
        halos_and_texts += [left, right]
    reach = length + 2 * halo
    window = min(rounded_up(MAXP + LANES - 1, LANES), reach)
    tile = 2 * LANES
    early_keys, marks, before, weight = call(
        functools.partial(prepare_kernel, images, halo),
        (
            shape((len(EARLY) * count, LANES), bf16),
            shape((2, SPARE, reach), f32),
            shape((rounded_up(images + 1, SPARE), LANES), jnp.int32),
            shape((HEADS * padded, depth), bf16),
        ),
        [pltpu.SemaphoreType.DMA((HEADS,))],
        in_vmem(1) + [hbm] + in_vmem(len(EARLY)),
        1 << 30,
    )(near_ids, in_hbm(out_weight), *[got[by] for by in EARLY])
    operands = [near_ids, before, marks, early_keys, *[got[by] for by in EARLY + LATE], *halos_and_texts]
    answers = call(
        functools.partial(attend_kernel, images, piggy, halo),
        (shape((padded + TEXT_ROWS * piggy, count), bf16),) * HEADS,
        [
            pltpu.VMEM((reach, LANES), bf16),
            pltpu.VMEM((padded, reach), bf16),
            pltpu.VMEM((LANES, length), bf16),
            pltpu.VMEM((padded, length), f32),
            pltpu.VMEM((window, tile), f32),
            pltpu.VMEM((window, tile), f32),
            pltpu.VMEM((1, tile), f32),
            pltpu.VMEM((1, tile), f32),
            pltpu.SMEM((images + 1,), jnp.int32),
            pltpu.SMEM((3, length // tile + images), jnp.int32),
        ],
        in_vmem(len(operands)),
        4 * size * length * MAXP,
    )(*operands)
    home = traded(dict(zip(ORDER, answers)))
    home = [home[by] for by in ORDER]

    joined = [
        pltpu.VMEM((HEADS * padded, count), bf16),
        pltpu.VMEM((count, HEADS * padded), bf16),
        pltpu.VMEM((count, depth), bf16),
        pltpu.SemaphoreType.DMA((3,)),
    ]
    flops = 2 * count * depth * width
    if piggy:
        mixed, row_loss = call(
            functools.partial(finish_kernel, images),
            (shape((count, depth), bf16), shape((1, images), f32)),
            joined
            + [
                pltpu.VMEM((SPARE, HEADS * padded), f32),
                pltpu.VMEM((SPARE, depth), f32),
                pltpu.VMEM((HEADS, images, depth), f32),
                pltpu.VMEM((1, images), f32),
                pltpu.SemaphoreType.DMA,
            ],
            in_vmem(3 + HEADS),
            flops,
            (hbm, hbm),
        )(rows, weight, text_embed, *home)
        return (mixed[None], row_loss[0])
    mixed = call(mix_kernel, shape((count, depth), bf16), joined, in_vmem(2 + HEADS), flops, hbm)(
        rows, weight, *home
    )
    own_ids = lax.dynamic_slice_in_dim(segment_ids[0], lax.axis_index("grp") * count, count)
    onehot = (own_ids[None, :] == jnp.arange(images, dtype=jnp.int32)[:, None]).astype(bf16)
    pooled = lax.psum(jnp.dot(onehot, mixed, preferred_element_type=f32), "grp")
    text_vecs = unit_rows(all_texts(text_embed).astype(f32))
    cosine = jnp.dot(unit_rows(pooled), text_vecs.T, precision=lax.Precision.HIGHEST)
    same = jnp.arange(images)[:, None] == jnp.arange(text_vecs.shape[0])[None, :]
    row_loss = jnp.sum(losses(cosine, jnp.where(same, 1.0, -1.0)), axis=1)
    return (mixed[None], row_loss)


def solution(mesh):
    placed = (P("blk", "grp", None), P("blk", None), P(), P(), P("blk", None))
    return jax.shard_map(
        local,
        mesh=mesh,
        in_specs=placed,
        out_specs=(P("blk", "grp", None), P("blk")),
        check_vma=False,
    )
```

```python
import functools
import math

import jax
import jax.numpy as jnp
from jax import lax
from jax.experimental import pallas as pl
from jax.experimental.pallas import tpu as pltpu
from jax.sharding import PartitionSpec as P

HEADS = 8
MAXP = 1024
LANES = 128
SPARE = 8
SIZE = 72
PADDED = SIZE + SPARE
KEY_AT = SIZE - SPARE
QUERY_AT = 2 * SIZE
TEXT_ROWS = 16
HIDDEN = -1e30
ORDER = (6, 7, 2, 4, 3, 5, 1, 0)
EARLY = (6, 7, 1, 0)
LATE = (2, 4, 3, 5)

logit_scale = 30.0
logit_bias = -5.0

VMEM_LIMIT = 32 * 1024 * 1024


def rounded_up(value, step):
    return (value + step - 1) // step * step


def split_in_two(total, images):
    row = lax.broadcasted_iota(jnp.int32, total.shape, 0)
    main = total.astype(jnp.bfloat16).astype(jnp.float32)
    return jnp.where(row < images, main, total - main)


def image_rows(ids, images):
    row = lax.broadcasted_iota(jnp.int32, (SPARE, ids.shape[1]), 0)
    return (lax.rem(row, images) == ids).astype(jnp.float32).astype(jnp.bfloat16)


def head_blocks(query, key, value, sums, pair):
    size = query.shape[0] // 2
    count = query.shape[1]
    for place in range(2):
        here = slice(place * size, (place + 1) * size)
        if sums is None:
            spare = jnp.zeros((SPARE, count), jnp.float32)
        else:
            first = pl.multiple_of((2 * pair + place) * LANES, LANES)
            parts = [sums[:, pl.ds(first, LANES)], sums[:, HEADS * LANES :]]
            held = sum(part.shape[1] for part in parts)
            spare = jnp.concatenate(parts + [jnp.zeros((SPARE, count - held), jnp.float32)], axis=1)
        yield jnp.concatenate([value[here], key[here], spare, query[here]], axis=0)


def store_by_core(core, blocks, same_ref, cross_ref):
    first, second = blocks
    same_ref[...] = jnp.where(core == 0, first, second).astype(jnp.bfloat16)
    cross_ref[...] = jnp.where(core == 0, second, first).astype(jnp.bfloat16)


def place_in_group():
    own = lax.rem(lax.axis_index("grp"), HEADS)
    return lax.div(own, 2), lax.rem(own, 2)


def far_kernel(images, piggy, ids_ref, rows_ref, weight_ref, normed_ref, sums_ref, same_ref, cross_ref, own_ids, rows_held, weight, id_sem, row_sem, sems):
    count, depth = rows_ref.shape
    width = weight_ref.shape[0] // 3
    wide = weight.shape[1]
    rows_fetch = pltpu.make_async_copy(rows_ref, rows_held, row_sem)
    rows_fetch.start()
    own = pl.multiple_of(lax.axis_index("grp") * count, LANES)
    ids_fetch = pltpu.make_async_copy(ids_ref.at[:, pl.ds(own, count)], own_ids, id_sem)
    ids_fetch.start()
    pair, core = place_in_group()
    pair = jnp.bitwise_xor(pair, 3)
    fetches = []
    for at in range(3):
        first = pl.multiple_of(at * width + pair * wide, 16)
        fetches.append(pltpu.make_async_copy(weight_ref.at[pl.ds(first, wide)], weight.at[at], sems.at[at]))
    for fetch in fetches:
        fetch.start()
    ids_fetch.wait()
    rows_fetch.wait()
    rows = rows_held[...]
    if piggy:
        sums = jnp.dot(image_rows(own_ids[...], images), rows, preferred_element_type=jnp.float32)
        sums_ref[...] = split_in_two(sums, images)
    values = rows.astype(jnp.float32)
    center = values - jnp.mean(values, axis=1, keepdims=True)
    spread = jnp.mean(center * center, axis=1, keepdims=True)
    normed = (center * lax.rsqrt(spread + 1e-06)).astype(jnp.bfloat16)
    normed_ref[...] = normed.T
    for fetch in fetches:
        fetch.wait()
    parts = [
        jnp.dot(weight[at], normed_ref[...], preferred_element_type=jnp.float32) for at in range(3)
    ]
    store_by_core(core, head_blocks(*parts, sums_ref if piggy else None, pair), same_ref, cross_ref)


def near_kernel(piggy, normed_ref, sums_ref, weight_ref, *out_refs):
    width = weight_ref.shape[0] // 3
    wide = 2 * width // HEADS
    own, core = place_in_group()
    for step, move in enumerate((1, 2, 0)):
        pair = jnp.bitwise_xor(own, move)
        parts = []
        for at in range(3):
            here = pl.ds(pl.multiple_of(at * width + pair * wide, 16), wide)
            parts.append(
                jnp.dot(weight_ref[here, :], normed_ref[...], preferred_element_type=jnp.float32)
            )
        blocks = head_blocks(*parts, sums_ref if piggy else None, pair)
        store_by_core(core, blocks, *out_refs[2 * step : 2 * step + 2])


def count_before(images, ids):
    image = lax.broadcasted_iota(jnp.int32, (rounded_up(images + 1, SPARE), ids.shape[1]), 0)
    before = jnp.sum((ids < image).astype(jnp.int32), axis=1, keepdims=True)
    return jnp.broadcast_to(before, (before.shape[0], LANES))


def write_marks(images, ids, marks):
    bits = max(1, (images - 1).bit_length())
    row = lax.broadcasted_iota(jnp.int32, (SPARE, ids.shape[1]), 0)
    bit = jnp.bitwise_and(lax.shift_right_logical(jnp.broadcast_to(ids, row.shape), row >> 1), 1)
    odd = jnp.bitwise_and(row, 1)
    used = row < 2 * bits
    outside = jnp.logical_or(ids < 0, ids >= images)
    key_side = jnp.where(odd == 1, bit, 1 - bit).astype(jnp.float32)
    key_side = jnp.where(outside, 1.0, key_side)
    marks[0] = jnp.where(used, key_side * HIDDEN, 0.0)
    marks[1] = jnp.where(used, jnp.where(odd == 1, 1 - bit, bit), 0).astype(jnp.float32)


def spare_sums(refs):
    parts = [ref[QUERY_AT : QUERY_AT + 16].astype(jnp.float32)[0:SPARE, 0 : 2 * LANES] for ref in refs]
    return sum(parts[1:], parts[0])


def image_at(images, starts, position):
    found = jnp.int32(0)
    for image in range(1, images):
        found += (starts[image] <= position).astype(jnp.int32)
    return found


def list_pairs(images, held, tile, last_begin, base, starts, table):
    tiles = held // tile
    shift = tile.bit_length() - 1
    low = image_at(images, starts, base)
    high = image_at(images, starts, base + held - 1)

    def bounds(image):
        first = jnp.maximum(starts[image] - base, 0) >> shift
        last = (jnp.minimum(starts[image + 1] - base, held) - 1) >> shift
        return jnp.minimum(first, tiles - 1), last

    pairs = jnp.int32(0)
    for image in range(images):
        first, last = bounds(image)
        wanted = jnp.logical_and(low <= image, image <= high)
        pairs += jnp.where(wanted, last - first + 1, 0)
    at, image = jnp.int32(0), low
    for step in range(tiles + images):
        table[0, step] = at
        table[1, step] = image
        table[2, step] = jnp.minimum(jnp.bitwise_and(starts[image], -LANES), last_begin)
        more = at < bounds(image)[1]
        later = jnp.minimum(image + 1, images - 1)
        at, image = jnp.where(more, at + 1, bounds(later)[0]), jnp.where(more, image, later)
    return pairs


def attend_images(pairs, table, ids_ref, keys, values, queries, attended, work, query_base):
    scores_a, scores_b, tops_a, tops_b = work
    window, tile = scores_a.shape
    size = attended.shape[0] - SPARE

    def window_of(state):
        return pl.ds(pl.multiple_of(table[2, state], LANES), window)

    def score(state, scores, tops):
        query = queries[:, pl.ds(pl.multiple_of(table[0, state] * tile, tile), tile)]
        found = jnp.dot(keys[window_of(state), :], query, preferred_element_type=jnp.float32)
        scores[...] = found
        tops[...] = jnp.max(found, axis=0, keepdims=True)

    def weigh(state, scores, tops):
        first = pl.multiple_of(table[0, state] * tile, tile)
        labels = ids_ref[:, pl.ds(pl.multiple_of(query_base + first, LANES), tile)]
        probs = jnp.exp2((scores[...] - tops[...]) * (size ** (-0.5) * math.log2(math.e)))
        share = 1.0 / jnp.sum(probs, axis=0, keepdims=True)
        weighted = jnp.dot(
            values[:, window_of(state)], probs.astype(jnp.bfloat16), preferred_element_type=jnp.float32
        )
        place = (slice(None), pl.ds(first, tile))
        attended[place] = jnp.where(labels == table[1, state], weighted * share, attended[place])

    def two_pairs(state):
        score(state + 1, scores_b, tops_b)
        weigh(state, scores_a, tops_a)
        score(state + 2, scores_a, tops_a)
        weigh(state + 1, scores_b, tops_b)

    def six_pairs(step, _):
        for place in range(0, 6, 2):
            two_pairs(6 * step + place)
        return 0

    def left_over(step, _):
        two_pairs(6 * whole + 2 * step)
        return 0

    score(0, scores_a, tops_a)
    whole = lax.div(pairs, 6)
    lax.fori_loop(0, whole, six_pairs, 0)
    lax.fori_loop(0, (pairs - 6 * whole) >> 1, left_over, 0)

    @pl.when(jnp.bitwise_and(pairs, 1) == 1)
    def _():
        weigh(pairs - 1, scores_a, tops_a)


def turned_keys(marked, block_ref):
    block = block_ref[KEY_AT : KEY_AT + PADDED].astype(jnp.float32)
    nothing = jnp.zeros((LANES - PADDED, block.shape[1]), jnp.float32)
    full = jnp.concatenate([marked, block[SPARE:], nothing], axis=0)
    return full.astype(jnp.bfloat16).T


def store_queries(marked, block_ref, queries, there):
    edge = block_ref[QUERY_AT : QUERY_AT + 16].astype(jnp.float32)
    edge = jnp.concatenate([marked, edge[SPARE:]], axis=0)
    queries[0:16, there] = edge.astype(jnp.bfloat16)
    queries[16:PADDED, there] = block_ref[QUERY_AT + 16 : QUERY_AT + PADDED]
    queries[PADDED:, there] = jnp.zeros((LANES - PADDED, block_ref.shape[1]), jnp.bfloat16)


def prepare_kernel(images, halo, ids_ref, out_weight_ref, *rest):
    got_refs, (keys, marks, before, weight, sems) = rest[: len(EARLY)], rest[len(EARLY) :]
    count = got_refs[0].shape[1]
    fetches = []
    for step, by in enumerate(ORDER):
        head = jnp.bitwise_xor(lax.rem(lax.axis_index("grp"), HEADS), by)
        first = lax.div(head, 2) * (2 * SIZE) + lax.rem(head, 2) * (SIZE - SPARE)
        fetches.append(
            pltpu.make_async_copy(
                out_weight_ref.at[pl.ds(pl.multiple_of(first, 16), PADDED)],
                weight.at[step * PADDED : (step + 1) * PADDED],
                sems.at[step],
            )
        )
        fetches[-1].start()
    before[...] = count_before(images, ids_ref[...])
    write_marks(images, ids_ref[...], marks)
    own = lax.rem(lax.axis_index("grp"), HEADS)
    for step, (by, ref) in enumerate(zip(EARLY, got_refs)):
        first = jnp.bitwise_xor(own, by) * count
        here = pl.ds(pl.multiple_of(halo + first, LANES), count)
        keys[step * count : (step + 1) * count, :] = turned_keys(marks[0, :, here], ref)
    for fetch in fetches:
        fetch.wait()


def attend_kernel(images, piggy, halo, ids_ref, before_ref, marks, early_keys, *rest):
    got_refs, rest = rest[:HEADS], rest[HEADS:]
    if piggy:
        text_ref, *rest = rest
    if halo:
        left_ref, right_ref, *rest = rest
    out_refs, rest = rest[:HEADS], rest[HEADS:]
    keys, values, queries, attended, *work, starts, table = rest
    count = got_refs[0].shape[1]
    padded = attended.shape[0]
    size = padded - SPARE
    total_rows = HEADS * count
    length = ids_ref.shape[1]
    ids = ids_ref[...]
    before = before_ref[...]
    for image in range(images + 1):
        starts[image] = before[image, 0]
    window, tile = work[0].shape
    pairs = list_pairs(images, total_rows, tile, length - window, halo, starts, table)

    own = lax.rem(lax.axis_index("grp"), HEADS)
    for step, (by, ref) in enumerate(zip(EARLY + LATE, got_refs)):
        first = jnp.bitwise_xor(own, by) * count
        here = pl.ds(pl.multiple_of(halo + first, LANES), count)
        there = pl.ds(pl.multiple_of(first, LANES), count)
        if by in EARLY:
            keys[here, :] = early_keys[step * count : (step + 1) * count, :]
        else:
            keys[here, :] = turned_keys(marks[0, :, here], ref)
        values[:, here] = ref[0:PADDED]
        store_queries(marks[1, :, here], ref, queries, there)
    if halo:
        for ref, here in ((left_ref, slice(0, halo)), (right_ref, slice(length - halo, length))):
            keys[here, :] = turned_keys(marks[0, :, here], ref)
            values[:, here] = ref[0:PADDED]
    attend_images(pairs, table, ids_ref, keys, values, queries, attended, work, halo)

    odd_head = lax.rem(own, 2) == 1
    mine = ids[:, halo : halo + total_rows]

    def placed(block, spare):
        even = jnp.concatenate([block[0:size], spare], axis=0)
        odd = jnp.concatenate([spare, block[0:size]], axis=0)
        return jnp.where(odd_head, odd, even)

    if piggy:
        nothing = jnp.zeros((SPARE, total_rows), jnp.float32)
        flat = placed(attended[...], nothing).astype(jnp.bfloat16)
        pooled = lax.dot_general(
            image_rows(mine, images), flat, (((1,), (1,)), ((), ())), preferred_element_type=jnp.float32
        )
        pooled = split_in_two(pooled, images)
        sums = spare_sums(got_refs)
        sums = split_in_two(sums + pltpu.roll(sums, images, axis=0), images)
        spare = jnp.concatenate(
            [pooled, jnp.zeros((SPARE, LANES - padded), jnp.float32), sums], axis=1
        )
        texts = text_ref[...].astype(jnp.float32)
        parts = [texts[:, at : at + count] for at in range(0, texts.shape[1], count)]
        unused = TEXT_ROWS - images * len(parts)
        below = jnp.concatenate(parts + [jnp.zeros((unused, count), jnp.float32)] * (unused > 0), axis=0)
        below = below.astype(jnp.bfloat16)
    else:
        spare = jnp.zeros((SPARE, count), jnp.float32)
    for by, out_ref in zip(ORDER, out_refs):
        there = pl.multiple_of(jnp.bitwise_xor(own, by) * count, LANES)
        out_ref[0:padded] = placed(attended[:, pl.ds(there, count)], spare).astype(jnp.bfloat16)
        if piggy:
            out_ref[padded:] = below


def joined_heads(got_refs, flat):
    own = lax.rem(lax.axis_index("grp"), HEADS)
    spares = []
    for step, (by, got_ref) in enumerate(zip(ORDER, got_refs)):
        odd = lax.rem(jnp.bitwise_xor(own, by), 2)
        at = step * PADDED
        top = got_ref[0:16].astype(jnp.float32)
        bottom = got_ref[PADDED - 16 : PADDED].astype(jnp.float32)
        spares.append(jnp.where(odd == 1, top[:SPARE], bottom[SPARE:]))
        top = jnp.concatenate([jnp.where(odd == 1, 0.0, top[:SPARE]), top[SPARE:]], axis=0)
        bottom = jnp.concatenate([bottom[:SPARE], jnp.where(odd == 1, bottom[SPARE:], 0.0)], axis=0)
        flat[at : at + 16] = top.astype(jnp.bfloat16)
        flat[at + 16 : at + PADDED - 16] = got_ref[16 : PADDED - 16]
        flat[at + PADDED - 16 : at + PADDED] = bottom.astype(jnp.bfloat16)
    return spares


def send_mixed_rows(rows_ref, weight_ref, flat, turned, mixed, mixed_ref, sems, meanwhile=None):
    turned[...] = flat[...].T
    pieces = sems.shape[0]
    step = rows_ref.shape[0] // pieces
    copies, value = [], None
    for piece in range(pieces):
        cut = slice(piece * step, (piece + 1) * step)
        if meanwhile is not None:
            value = meanwhile[piece](value)
        added = jnp.dot(turned[cut, :], weight_ref[...], preferred_element_type=jnp.float32)
        mixed[cut, :] = (rows_ref[cut, :].astype(jnp.float32) + added).astype(jnp.bfloat16)
        copies.append(pltpu.make_async_copy(mixed.at[cut], mixed_ref.at[cut], sems.at[piece]))
        copies[-1].start()
    return copies


def unit_rows(matrix):
    return matrix * lax.rsqrt(jnp.sum(matrix * matrix, axis=1, keepdims=True) + 1e-06)


def losses(cosine, labels):
    logits = -labels * (logit_scale * cosine + logit_bias)
    return jnp.maximum(logits, 0.0) + jnp.log1p(jnp.exp(-jnp.abs(logits)))


def finish_kernel(images, rows_ref, weight_ref, text_ref, *rest):
    got_refs, rest = rest[:HEADS], rest[HEADS:]
    mixed_ref, loss_ref, flat, turned, mixed, sems, pooled_heads, patch_sums, far_texts, loss, loss_sem = rest
    spares = joined_heads(got_refs, flat)
    own = lax.rem(lax.axis_index("grp"), HEADS)
    patch_sums[:, HEADS * LANES :] = spares[0][:, 2 * LANES :]
    for step, (by, spare) in enumerate(zip(ORDER, spares)):
        pooled_heads[:, step * PADDED : (step + 1) * PADDED] = spare[:, 0:PADDED]
        head = jnp.bitwise_xor(own, by)
        patch_sums[:, pl.ds(pl.multiple_of(head * LANES, LANES), LANES)] = spare[:, LANES : 2 * LANES]
        below = got_refs[step][PADDED:].astype(jnp.float32)
        count = below.shape[1]
        for part in range(patch_sums.shape[1] // count):
            here = slice(part * count, (part + 1) * count)
            far_texts[head, :, here] = below[part * images : (part + 1) * images]

    def find_images(_):
        pooled = jnp.dot(
            pooled_heads[...].astype(jnp.bfloat16), weight_ref[...], preferred_element_type=jnp.float32
        )
        pooled = pooled + patch_sums[...]
        others = [far_texts[place] for place in range(lax.axis_size("blk") - 1)]
        texts = jnp.concatenate([text_ref[...].astype(jnp.float32)] + others, axis=0)
        return pooled + pltpu.roll(pooled, images, axis=0), unit_rows(texts)

    def find_cosines(vectors):
        pooled, text_vecs = vectors
        return lax.dot_general(
            text_vecs,
            unit_rows(pooled),
            (((1,), (1,)), ((), ())),
            precision=lax.Precision.HIGHEST,
            preferred_element_type=jnp.float32,
        )

    def find_losses(cosine):
        text = lax.broadcasted_iota(jnp.int32, cosine.shape, 0)
        image = lax.broadcasted_iota(jnp.int32, cosine.shape, 1)
        terms = losses(cosine, jnp.where(text == image, 1.0, -1.0))
        loss[...] = jnp.sum(terms, axis=0, keepdims=True)[:, 0:images]
        loss_copy.start()

    loss_copy = pltpu.make_async_copy(loss, loss_ref, loss_sem)
    meanwhile = (find_images, find_cosines, find_losses)
    copies = send_mixed_rows(rows_ref, weight_ref, flat, turned, mixed, mixed_ref, sems, meanwhile)
    for copy in copies + [loss_copy]:
        copy.wait()


def mix_kernel(rows_ref, weight_ref, *rest):
    got_refs, rest = rest[:HEADS], rest[HEADS:]
    mixed_ref, flat, turned, mixed, sems = rest
    joined_heads(got_refs, flat)
    for copy in send_mixed_rows(rows_ref, weight_ref, flat, turned, mixed, mixed_ref, sems):
        copy.wait()


def in_vmem(count):
    return [pl.BlockSpec(memory_space=pltpu.VMEM)] * count


def in_hbm(value):
    return pltpu.with_memory_space_constraint(value, pltpu.HBM)


def call(kernel, out_shape, scratch, in_specs, flops, out_specs=None):
    if out_specs is None:
        out_specs = jax.tree.map(lambda _: pl.BlockSpec(memory_space=pltpu.VMEM), out_shape)
    return pl.pallas_call(
        kernel,
        out_shape=out_shape,
        in_specs=in_specs,
        out_specs=out_specs,
        scratch_shapes=scratch,
        compiler_params=pltpu.CompilerParams(vmem_limit_bytes=VMEM_LIMIT),
        cost_estimate=pl.CostEstimate(flops=flops, bytes_accessed=8 << 20, transcendentals=0),
    )


def moved(value, axis, pairs):
    return lax.ppermute(value, axis, pairs)


def partner(place, by, peers):
    return place ^ by if peers & (peers - 1) == 0 else (place + by) % peers


def all_texts(texts):
    peers = lax.axis_size("blk")
    steps = [[(partner(i, by, peers), i) for i in range(peers)] for by in range(1, peers)]
    return jnp.concatenate([texts] + [moved(texts, "blk", pairs) for pairs in steps], axis=0)


def one_text_block(texts):
    peers = lax.axis_size("blk")
    pairs = []
    for place in range(lax.axis_size("grp")):
        by = place % (peers - 1) + 1
        pairs += [(place * peers + partner(i, by, peers), place * peers + i) for i in range(peers)]
    return moved(texts, ("grp", "blk"), pairs)


def traded(blocks):
    peers = range(lax.axis_size("grp"))
    trades = {by: moved(blocks[by], "grp", [(i, i ^ by) for i in peers]) for by in ORDER if by}
    return {**trades, 0: blocks[0]}


def local(patches, segment_ids, qkv_weight, out_weight, text_embed):
    rows = patches[0]
    count, depth = rows.shape
    width = out_weight.shape[0]
    size = width // HEADS
    padded = size + SPARE
    images = text_embed.shape[0]
    group_size = lax.axis_size("grp")
    parts = group_size // HEADS
    piggy = (
        parts == 1
        and 2 * images == SPARE
        and count >= depth - (HEADS - 2) * LANES
        and depth % count == 0
        and images * (depth // count) <= TEXT_ROWS
        and 1 < lax.axis_size("blk") <= HEADS + 1
    )
    bf16, f32 = jnp.bfloat16, jnp.float32
    shape = jax.ShapeDtypeStruct

    block = shape((3 * size + SPARE, count), bf16)
    hbm = pl.BlockSpec(memory_space=pltpu.HBM)
    turned_weight = qkv_weight.T
    normed, sums, *sent = call(
        functools.partial(far_kernel, images, piggy),
        (shape((depth, count), bf16), shape((SPARE, depth), f32), block, block),
        [
            pltpu.VMEM((1, count), jnp.int32),
            pltpu.VMEM((count, depth), bf16),
            pltpu.VMEM((3, 2 * size, depth), bf16),
            pltpu.SemaphoreType.DMA,
            pltpu.SemaphoreType.DMA,
            pltpu.SemaphoreType.DMA((3,)),
        ],
        [hbm] * 3,
        2 * count * depth * 6 * size,
    )(in_hbm(segment_ids), in_hbm(rows), in_hbm(turned_weight))
    sent += call(
        functools.partial(near_kernel, piggy),
        (block,) * 6,
        [],
        in_vmem(3),
        2 * count * depth * 18 * size,
    )(normed, sums, turned_weight)
    sent = dict(zip((6, 7, 2, 3, 4, 5, 0, 1), sent))
    if piggy:
        late_texts, sent[0] = lax.optimization_barrier((text_embed, sent[0]))
        halos_and_texts = [one_text_block(late_texts)]
    else:
        halos_and_texts = []
    got = traded(sent)

    length = HEADS * count
    halo = 0
    near_ids = segment_ids
    if parts > 1:
        halo = rounded_up(MAXP - 1, LANES)
        part = lax.axis_index("grp") // HEADS
        whole_ids = jnp.concatenate(
            [
                jnp.full((1, halo), -1, jnp.int32),
                segment_ids,
                jnp.full((1, halo), images, jnp.int32),
            ],
            axis=1,
        )
        near_ids = lax.dynamic_slice_in_dim(whole_ids, part * length, length + 2 * halo, axis=1)
        order = jnp.bitwise_xor(lax.axis_index("grp") % HEADS, jnp.arange(HEADS))
        flat = jnp.stack([got[by] for by in range(HEADS)])[order][:, : 2 * size].transpose(1, 0, 2).reshape(2 * size, length)
        flat = jnp.concatenate([flat, jnp.zeros((16, length), bf16)], axis=0)
        ahead = [(i, i + HEADS) for i in range(group_size - HEADS)]
        back = [(i + HEADS, i) for i in range(group_size - HEADS)]
        left = moved(flat[:, length - halo :], "grp", ahead)
        right = moved(flat[:, :halo], "grp", back)
        halos_and_texts += [left, right]
    reach = length + 2 * halo
    window = min(rounded_up(MAXP + LANES - 1, LANES), reach)
    tile = 2 * LANES
    early_keys, marks, before, weight = call(
        functools.partial(prepare_kernel, images, halo),
        (
            shape((len(EARLY) * count, LANES), bf16),
            shape((2, SPARE, reach), f32),
            shape((rounded_up(images + 1, SPARE), LANES), jnp.int32),
            shape((HEADS * padded, depth), bf16),
        ),
        [pltpu.SemaphoreType.DMA((HEADS,))],
        in_vmem(1) + [hbm] + in_vmem(len(EARLY)),
        1 << 30,
    )(near_ids, in_hbm(out_weight), *[got[by] for by in EARLY])
    operands = [near_ids, before, marks, early_keys, *[got[by] for by in EARLY + LATE], *halos_and_texts]
    answers = call(
        functools.partial(attend_kernel, images, piggy, halo),
        (shape((padded + TEXT_ROWS * piggy, count), bf16),) * HEADS,
        [
            pltpu.VMEM((reach, LANES), bf16),
            pltpu.VMEM((padded, reach), bf16),
            pltpu.VMEM((LANES, length), bf16),
            pltpu.VMEM((padded, length), f32),
            pltpu.VMEM((window, tile), f32),
            pltpu.VMEM((window, tile), f32),
            pltpu.VMEM((1, tile), f32),
            pltpu.VMEM((1, tile), f32),
            pltpu.SMEM((images + 1,), jnp.int32),
            pltpu.SMEM((3, length // tile + images), jnp.int32),
        ],
        in_vmem(len(operands)),
        4 * size * length * MAXP,
    )(*operands)
    home = traded(dict(zip(ORDER, answers)))
    home = [home[by] for by in ORDER]

    joined = [
        pltpu.VMEM((HEADS * padded, count), bf16),
        pltpu.VMEM((count, HEADS * padded), bf16),
        pltpu.VMEM((count, depth), bf16),
        pltpu.SemaphoreType.DMA((3,)),
    ]
    flops = 2 * count * depth * width
    if piggy:
        mixed, row_loss = call(
            functools.partial(finish_kernel, images),
            (shape((count, depth), bf16), shape((1, images), f32)),
            joined
            + [
                pltpu.VMEM((SPARE, HEADS * padded), f32),
                pltpu.VMEM((SPARE, depth), f32),
                pltpu.VMEM((HEADS, images, depth), f32),
                pltpu.VMEM((1, images), f32),
                pltpu.SemaphoreType.DMA,
            ],
            in_vmem(3 + HEADS),
            flops,
            (hbm, hbm),
        )(rows, weight, text_embed, *home)
        return (mixed[None], row_loss[0])
    mixed = call(mix_kernel, shape((count, depth), bf16), joined, in_vmem(2 + HEADS), flops, hbm)(
        rows, weight, *home
    )
    own_ids = lax.dynamic_slice_in_dim(segment_ids[0], lax.axis_index("grp") * count, count)
    onehot = (own_ids[None, :] == jnp.arange(images, dtype=jnp.int32)[:, None]).astype(bf16)
    pooled = lax.psum(jnp.dot(onehot, mixed, preferred_element_type=f32), "grp")
    text_vecs = unit_rows(all_texts(text_embed).astype(f32))
    cosine = jnp.dot(unit_rows(pooled), text_vecs.T, precision=lax.Precision.HIGHEST)
    same = jnp.arange(images)[:, None] == jnp.arange(text_vecs.shape[0])[None, :]
    row_loss = jnp.sum(losses(cosine, jnp.where(same, 1.0, -1.0)), axis=1)
    return (mixed[None], row_loss)


def solution(mesh):
    placed = (P("blk", "grp", None), P("blk", None), P(), P(), P("blk", None))
    return jax.shard_map(
        local,
        mesh=mesh,
        in_specs=placed,
        out_specs=(P("blk", "grp", None), P("blk")),
        check_vma=False,
    )
```

```python
import functools
import math

import jax
import jax.numpy as jnp
from jax import lax
from jax.experimental import pallas as pl
from jax.experimental.pallas import tpu as pltpu
from jax.sharding import PartitionSpec as P

HEADS = 8
MAXP = 1024
LANES = 128
SPARE = 8
SIZE = 72
PADDED = SIZE + SPARE
KEY_AT = SIZE - SPARE
QUERY_AT = 2 * SIZE
TEXT_ROWS = 16
HIDDEN = -1e30
ORDER = (6, 7, 2, 4, 3, 5, 1, 0)
EARLY = (6, 7, 0)
LATE = (2, 4, 3, 5, 1)

logit_scale = 30.0
logit_bias = -5.0

VMEM_LIMIT = 32 * 1024 * 1024


def rounded_up(value, step):
    return (value + step - 1) // step * step


def split_in_two(total, images):
    row = lax.broadcasted_iota(jnp.int32, total.shape, 0)
    main = total.astype(jnp.bfloat16).astype(jnp.float32)
    return jnp.where(row < images, main, total - main)


def image_rows(ids, images):
    row = lax.broadcasted_iota(jnp.int32, (SPARE, ids.shape[1]), 0)
    return (lax.rem(row, images) == ids).astype(jnp.float32).astype(jnp.bfloat16)


def head_blocks(query, key, value, sums, pair):
    size = query.shape[0] // 2
    count = query.shape[1]
    for place in range(2):
        here = slice(place * size, (place + 1) * size)
        if sums is None:
            spare = jnp.zeros((SPARE, count), jnp.float32)
        else:
            first = pl.multiple_of((2 * pair + place) * LANES, LANES)
            parts = [sums[:, pl.ds(first, LANES)], sums[:, HEADS * LANES :]]
            held = sum(part.shape[1] for part in parts)
            spare = jnp.concatenate(parts + [jnp.zeros((SPARE, count - held), jnp.float32)], axis=1)
        yield jnp.concatenate([value[here], key[here], spare, query[here]], axis=0)


def store_by_core(core, blocks, same_ref, cross_ref):
    first, second = blocks
    same_ref[...] = jnp.where(core == 0, first, second).astype(jnp.bfloat16)
    cross_ref[...] = jnp.where(core == 0, second, first).astype(jnp.bfloat16)


def place_in_group():
    own = lax.rem(lax.axis_index("grp"), HEADS)
    return lax.div(own, 2), lax.rem(own, 2)


def far_kernel(images, piggy, ids_ref, rows_ref, weight_ref, normed_ref, sums_ref, same_ref, cross_ref, own_ids, rows_held, weight, id_sem, row_sem, sems):
    count, depth = rows_ref.shape
    width = weight_ref.shape[0] // 3
    wide = weight.shape[1]
    rows_fetch = pltpu.make_async_copy(rows_ref, rows_held, row_sem)
    rows_fetch.start()
    own = pl.multiple_of(lax.axis_index("grp") * count, LANES)
    ids_fetch = pltpu.make_async_copy(ids_ref.at[:, pl.ds(own, count)], own_ids, id_sem)
    ids_fetch.start()
    pair, core = place_in_group()
    pair = jnp.bitwise_xor(pair, 3)
    fetches = []
    for at in range(3):
        first = pl.multiple_of(at * width + pair * wide, 16)
        fetches.append(pltpu.make_async_copy(weight_ref.at[pl.ds(first, wide)], weight.at[at], sems.at[at]))
    for fetch in fetches:
        fetch.start()
    ids_fetch.wait()
    rows_fetch.wait()
    rows = rows_held[...]
    if piggy:
        sums = jnp.dot(image_rows(own_ids[...], images), rows, preferred_element_type=jnp.float32)
        sums_ref[...] = split_in_two(sums, images)
    values = rows.astype(jnp.float32)
    center = values - jnp.mean(values, axis=1, keepdims=True)
    spread = jnp.mean(center * center, axis=1, keepdims=True)
    normed = (center * lax.rsqrt(spread + 1e-06)).astype(jnp.bfloat16)
    normed_ref[...] = normed.T
    for fetch in fetches:
        fetch.wait()
    parts = [
        jnp.dot(weight[at], normed_ref[...], preferred_element_type=jnp.float32) for at in range(3)
    ]
    store_by_core(core, head_blocks(*parts, sums_ref if piggy else None, pair), same_ref, cross_ref)


def near_kernel(piggy, normed_ref, sums_ref, weight_ref, *out_refs):
    width = weight_ref.shape[0] // 3
    wide = 2 * width // HEADS
    own, core = place_in_group()
    for step, move in enumerate((1, 2, 0)):
        pair = jnp.bitwise_xor(own, move)
        parts = []
        for at in range(3):
            here = pl.ds(pl.multiple_of(at * width + pair * wide, 16), wide)
            parts.append(
                jnp.dot(weight_ref[here, :], normed_ref[...], preferred_element_type=jnp.float32)
            )
        blocks = head_blocks(*parts, sums_ref if piggy else None, pair)
        store_by_core(core, blocks, *out_refs[2 * step : 2 * step + 2])


def count_before(images, ids):
    image = lax.broadcasted_iota(jnp.int32, (rounded_up(images + 1, SPARE), ids.shape[1]), 0)
    before = jnp.sum((ids < image).astype(jnp.int32), axis=1, keepdims=True)
    return jnp.broadcast_to(before, (before.shape[0], LANES))


def write_marks(images, ids, marks):
    bits = max(1, (images - 1).bit_length())
    row = lax.broadcasted_iota(jnp.int32, (SPARE, ids.shape[1]), 0)
    bit = jnp.bitwise_and(lax.shift_right_logical(jnp.broadcast_to(ids, row.shape), row >> 1), 1)
    odd = jnp.bitwise_and(row, 1)
    used = row < 2 * bits
    outside = jnp.logical_or(ids < 0, ids >= images)
    key_side = jnp.where(odd == 1, bit, 1 - bit).astype(jnp.float32)
    key_side = jnp.where(outside, 1.0, key_side)
    marks[0] = jnp.where(used, key_side * HIDDEN, 0.0)
    marks[1] = jnp.where(used, jnp.where(odd == 1, 1 - bit, bit), 0).astype(jnp.float32)


def spare_sums(refs):
    parts = [ref[QUERY_AT : QUERY_AT + 16].astype(jnp.float32)[0:SPARE, 0 : 2 * LANES] for ref in refs]
    return sum(parts[1:], parts[0])


def image_at(images, starts, position):
    found = jnp.int32(0)
    for image in range(1, images):
        found += (starts[image] <= position).astype(jnp.int32)
    return found


def attend_images(images, ids_ref, keys, values, queries, attended, work, starts, halo):
    scores_a, scores_b, tops_a, tops_b = work
    query_base = halo
    window, tile = scores_a.shape
    size = attended.shape[0] - SPARE
    held = queries.shape[1]
    tiles = held // tile
    shift = tile.bit_length() - 1

    def bounds(image):
        first = jnp.maximum(starts[image] - query_base, 0) >> shift
        last = (jnp.minimum(starts[image + 1] - query_base, held) - 1) >> shift
        return jnp.minimum(first, tiles - 1), last

    def after(image):
        return jnp.minimum(image + 1, images - 1)

    def following(state):
        at, image = state
        more = at < bounds(image)[1]
        later = after(image)
        return jnp.where(more, at + 1, bounds(later)[0]), jnp.where(more, image, later)

    def window_of(image):
        begin = jnp.bitwise_and(starts[image], -LANES)
        return pl.ds(pl.multiple_of(jnp.minimum(begin, keys.shape[0] - window), LANES), window)

    def score(state, scores, tops):
        at, image = state
        query = queries[:, pl.ds(pl.multiple_of(at * tile, tile), tile)]
        found = jnp.dot(keys[window_of(image), :], query, preferred_element_type=jnp.float32)
        scores[...] = found
        tops[...] = jnp.max(found, axis=0, keepdims=True)

    def weigh(state, scores, tops):
        at, image = state
        first = pl.multiple_of(at * tile, tile)
        labels = ids_ref[:, pl.ds(pl.multiple_of(query_base + first, LANES), tile)]
        probs = jnp.exp2((scores[...] - tops[...]) * (size ** (-0.5) * math.log2(math.e)))
        share = 1.0 / jnp.sum(probs, axis=0, keepdims=True)
        weighted = jnp.dot(
            values[:, window_of(image)], probs.astype(jnp.bfloat16), preferred_element_type=jnp.float32
        )
        place = (slice(None), pl.ds(first, tile))
        attended[place] = jnp.where(labels == image, weighted * share, attended[place])

    low = image_at(images, starts, query_base)
    high = image_at(images, starts, query_base + held - 1)
    pairs = jnp.int32(0)
    for image in range(images):
        first, last = bounds(image)
        wanted = jnp.logical_and(low <= image, image <= high)
        pairs += jnp.where(wanted, last - first + 1, 0)

    def two_pairs(_, state):
        second = following(state)
        score(second, scores_b, tops_b)
        weigh(state, scores_a, tops_a)
        third = following(second)
        score(third, scores_a, tops_a)
        weigh(second, scores_b, tops_b)
        return third

    def four_pairs(step, state):
        return two_pairs(step, two_pairs(step, state))

    begun = (jnp.int32(0), low)
    score(begun, scores_a, tops_a)
    reached = lax.fori_loop(0, lax.div(pairs, 4), four_pairs, begun)
    reached = lax.fori_loop(0, lax.div(lax.rem(pairs, 4), 2), two_pairs, reached)

    @pl.when(lax.rem(pairs, 2) == 1)
    def _():
        weigh(reached, scores_a, tops_a)


def turned_keys(marked, block_ref):
    block = block_ref[KEY_AT : KEY_AT + PADDED].astype(jnp.float32)
    nothing = jnp.zeros((LANES - PADDED, block.shape[1]), jnp.float32)
    full = jnp.concatenate([marked, block[SPARE:], nothing], axis=0)
    return full.astype(jnp.bfloat16).T


def store_queries(marked, block_ref, queries, there):
    edge = block_ref[QUERY_AT : QUERY_AT + 16].astype(jnp.float32)
    edge = jnp.concatenate([marked, edge[SPARE:]], axis=0)
    queries[0:16, there] = edge.astype(jnp.bfloat16)
    queries[16:PADDED, there] = block_ref[QUERY_AT + 16 : QUERY_AT + PADDED]
    queries[PADDED:, there] = jnp.zeros((LANES - PADDED, block_ref.shape[1]), jnp.bfloat16)


def prepare_kernel(images, halo, ids_ref, out_weight_ref, *rest):
    got_refs, (keys, marks, before, weight, sems) = rest[: len(EARLY)], rest[len(EARLY) :]
    count = got_refs[0].shape[1]
    fetches = []
    for step, by in enumerate(ORDER):
        head = jnp.bitwise_xor(lax.rem(lax.axis_index("grp"), HEADS), by)
        first = lax.div(head, 2) * (2 * SIZE) + lax.rem(head, 2) * (SIZE - SPARE)
        fetches.append(
            pltpu.make_async_copy(
                out_weight_ref.at[pl.ds(pl.multiple_of(first, 16), PADDED)],
                weight.at[step * PADDED : (step + 1) * PADDED],
                sems.at[step],
            )
        )
        fetches[-1].start()
    before[...] = count_before(images, ids_ref[...])
    write_marks(images, ids_ref[...], marks)
    own = lax.rem(lax.axis_index("grp"), HEADS)
    for step, (by, ref) in enumerate(zip(EARLY, got_refs)):
        first = jnp.bitwise_xor(own, by) * count
        here = pl.ds(pl.multiple_of(halo + first, LANES), count)
        keys[step * count : (step + 1) * count, :] = turned_keys(marks[0, :, here], ref)
    for fetch in fetches:
        fetch.wait()


def attend_kernel(images, piggy, halo, ids_ref, before_ref, marks, early_keys, *rest):
    got_refs, rest = rest[:HEADS], rest[HEADS:]
    if piggy:
        text_ref, *rest = rest
    if halo:
        left_ref, right_ref, *rest = rest
    out_refs, rest = rest[:HEADS], rest[HEADS:]
    keys, values, queries, attended, *work, starts = rest
    count = got_refs[0].shape[1]
    padded = attended.shape[0]
    size = padded - SPARE
    total_rows = HEADS * count
    length = ids_ref.shape[1]
    ids = ids_ref[...]
    before = before_ref[...]
    for image in range(images + 1):
        starts[image] = before[image, 0]

    own = lax.rem(lax.axis_index("grp"), HEADS)
    for step, (by, ref) in enumerate(zip(EARLY + LATE, got_refs)):
        first = jnp.bitwise_xor(own, by) * count
        here = pl.ds(pl.multiple_of(halo + first, LANES), count)
        there = pl.ds(pl.multiple_of(first, LANES), count)
        if by in EARLY:
            keys[here, :] = early_keys[step * count : (step + 1) * count, :]
        else:
            keys[here, :] = turned_keys(marks[0, :, here], ref)
        values[:, here] = ref[0:PADDED]
        store_queries(marks[1, :, here], ref, queries, there)
    if halo:
        for ref, here in ((left_ref, slice(0, halo)), (right_ref, slice(length - halo, length))):
            keys[here, :] = turned_keys(marks[0, :, here], ref)
            values[:, here] = ref[0:PADDED]
    attend_images(images, ids_ref, keys, values, queries, attended, work, starts, halo)

    odd_head = lax.rem(own, 2) == 1
    mine = ids[:, halo : halo + total_rows]

    def placed(block, spare):
        even = jnp.concatenate([block[0:size], spare], axis=0)
        odd = jnp.concatenate([spare, block[0:size]], axis=0)
        return jnp.where(odd_head, odd, even)

    if piggy:
        nothing = jnp.zeros((SPARE, total_rows), jnp.float32)
        flat = placed(attended[...], nothing).astype(jnp.bfloat16)
        pooled = lax.dot_general(
            image_rows(mine, images), flat, (((1,), (1,)), ((), ())), preferred_element_type=jnp.float32
        )
        pooled = split_in_two(pooled, images)
        sums = spare_sums(got_refs)
        sums = split_in_two(sums + pltpu.roll(sums, images, axis=0), images)
        spare = jnp.concatenate(
            [pooled, jnp.zeros((SPARE, LANES - padded), jnp.float32), sums], axis=1
        )
        texts = text_ref[...].astype(jnp.float32)
        parts = [texts[:, at : at + count] for at in range(0, texts.shape[1], count)]
        unused = TEXT_ROWS - images * len(parts)
        below = jnp.concatenate(parts + [jnp.zeros((unused, count), jnp.float32)] * (unused > 0), axis=0)
        below = below.astype(jnp.bfloat16)
    else:
        spare = jnp.zeros((SPARE, count), jnp.float32)
    for by, out_ref in zip(ORDER, out_refs):
        there = pl.multiple_of(jnp.bitwise_xor(own, by) * count, LANES)
        out_ref[0:padded] = placed(attended[:, pl.ds(there, count)], spare).astype(jnp.bfloat16)
        if piggy:
            out_ref[padded:] = below


def joined_heads(got_refs, flat):
    own = lax.rem(lax.axis_index("grp"), HEADS)
    spares = []
    for step, (by, got_ref) in enumerate(zip(ORDER, got_refs)):
        odd = lax.rem(jnp.bitwise_xor(own, by), 2)
        at = step * PADDED
        top = got_ref[0:16].astype(jnp.float32)
        bottom = got_ref[PADDED - 16 : PADDED].astype(jnp.float32)
        spares.append(jnp.where(odd == 1, top[:SPARE], bottom[SPARE:]))
        top = jnp.concatenate([jnp.where(odd == 1, 0.0, top[:SPARE]), top[SPARE:]], axis=0)
        bottom = jnp.concatenate([bottom[:SPARE], jnp.where(odd == 1, bottom[SPARE:], 0.0)], axis=0)
        flat[at : at + 16] = top.astype(jnp.bfloat16)
        flat[at + 16 : at + PADDED - 16] = got_ref[16 : PADDED - 16]
        flat[at + PADDED - 16 : at + PADDED] = bottom.astype(jnp.bfloat16)
    return spares


def send_mixed_rows(rows_ref, weight_ref, flat, turned, mixed, mixed_ref, sems, meanwhile=None):
    turned[...] = flat[...].T
    pieces = sems.shape[0]
    step = rows_ref.shape[0] // pieces
    copies, value = [], None
    for piece in range(pieces):
        cut = slice(piece * step, (piece + 1) * step)
        if meanwhile is not None:
            value = meanwhile[piece](value)
        added = jnp.dot(turned[cut, :], weight_ref[...], preferred_element_type=jnp.float32)
        mixed[cut, :] = (rows_ref[cut, :].astype(jnp.float32) + added).astype(jnp.bfloat16)
        copies.append(pltpu.make_async_copy(mixed.at[cut], mixed_ref.at[cut], sems.at[piece]))
        copies[-1].start()
    return copies


def unit_rows(matrix):
    return matrix * lax.rsqrt(jnp.sum(matrix * matrix, axis=1, keepdims=True) + 1e-06)


def losses(cosine, labels):
    logits = -labels * (logit_scale * cosine + logit_bias)
    return jnp.maximum(logits, 0.0) + jnp.log1p(jnp.exp(-jnp.abs(logits)))


def finish_kernel(images, rows_ref, weight_ref, text_ref, *rest):
    got_refs, rest = rest[:HEADS], rest[HEADS:]
    mixed_ref, loss_ref, flat, turned, mixed, sems, pooled_heads, patch_sums, far_texts, loss, loss_sem = rest
    spares = joined_heads(got_refs, flat)
    own = lax.rem(lax.axis_index("grp"), HEADS)
    patch_sums[:, HEADS * LANES :] = spares[0][:, 2 * LANES :]
    for step, (by, spare) in enumerate(zip(ORDER, spares)):
        pooled_heads[:, step * PADDED : (step + 1) * PADDED] = spare[:, 0:PADDED]
        head = jnp.bitwise_xor(own, by)
        patch_sums[:, pl.ds(pl.multiple_of(head * LANES, LANES), LANES)] = spare[:, LANES : 2 * LANES]
        below = got_refs[step][PADDED:].astype(jnp.float32)
        count = below.shape[1]
        for part in range(patch_sums.shape[1] // count):
            here = slice(part * count, (part + 1) * count)
            far_texts[head, :, here] = below[part * images : (part + 1) * images]

    def find_images(_):
        pooled = jnp.dot(
            pooled_heads[...].astype(jnp.bfloat16), weight_ref[...], preferred_element_type=jnp.float32
        )
        pooled = pooled + patch_sums[...]
        others = [far_texts[place] for place in range(lax.axis_size("blk") - 1)]
        texts = jnp.concatenate([text_ref[...].astype(jnp.float32)] + others, axis=0)
        return pooled + pltpu.roll(pooled, images, axis=0), unit_rows(texts)

    def find_cosines(vectors):
        pooled, text_vecs = vectors
        return lax.dot_general(
            text_vecs,
            unit_rows(pooled),
            (((1,), (1,)), ((), ())),
            precision=lax.Precision.HIGHEST,
            preferred_element_type=jnp.float32,
        )

    def find_losses(cosine):
        text = lax.broadcasted_iota(jnp.int32, cosine.shape, 0)
        image = lax.broadcasted_iota(jnp.int32, cosine.shape, 1)
        terms = losses(cosine, jnp.where(text == image, 1.0, -1.0))
        loss[...] = jnp.sum(terms, axis=0, keepdims=True)[:, 0:images]
        loss_copy.start()

    loss_copy = pltpu.make_async_copy(loss, loss_ref, loss_sem)
    meanwhile = (find_images, find_cosines, find_losses)
    copies = send_mixed_rows(rows_ref, weight_ref, flat, turned, mixed, mixed_ref, sems, meanwhile)
    for copy in copies + [loss_copy]:
        copy.wait()


def mix_kernel(rows_ref, weight_ref, *rest):
    got_refs, rest = rest[:HEADS], rest[HEADS:]
    mixed_ref, flat, turned, mixed, sems = rest
    joined_heads(got_refs, flat)
    for copy in send_mixed_rows(rows_ref, weight_ref, flat, turned, mixed, mixed_ref, sems):
        copy.wait()


def in_vmem(count):
    return [pl.BlockSpec(memory_space=pltpu.VMEM)] * count


def in_hbm(value):
    return pltpu.with_memory_space_constraint(value, pltpu.HBM)


def call(kernel, out_shape, scratch, in_specs, flops, out_specs=None):
    if out_specs is None:
        out_specs = jax.tree.map(lambda _: pl.BlockSpec(memory_space=pltpu.VMEM), out_shape)
    return pl.pallas_call(
        kernel,
        out_shape=out_shape,
        in_specs=in_specs,
        out_specs=out_specs,
        scratch_shapes=scratch,
        compiler_params=pltpu.CompilerParams(vmem_limit_bytes=VMEM_LIMIT),
        cost_estimate=pl.CostEstimate(flops=flops, bytes_accessed=8 << 20, transcendentals=0),
    )


def moved(value, axis, pairs):
    return lax.ppermute(value, axis, pairs)


def partner(place, by, peers):
    return place ^ by if peers & (peers - 1) == 0 else (place + by) % peers


def all_texts(texts):
    peers = lax.axis_size("blk")
    steps = [[(partner(i, by, peers), i) for i in range(peers)] for by in range(1, peers)]
    return jnp.concatenate([texts] + [moved(texts, "blk", pairs) for pairs in steps], axis=0)


def one_text_block(texts):
    peers = lax.axis_size("blk")
    pairs = []
    for place in range(lax.axis_size("grp")):
        by = place % (peers - 1) + 1
        pairs += [(place * peers + partner(i, by, peers), place * peers + i) for i in range(peers)]
    return moved(texts, ("grp", "blk"), pairs)


def traded(blocks):
    peers = range(lax.axis_size("grp"))
    trades = {by: moved(blocks[by], "grp", [(i, i ^ by) for i in peers]) for by in ORDER if by}
    return {**trades, 0: blocks[0]}


def local(patches, segment_ids, qkv_weight, out_weight, text_embed):
    rows = patches[0]
    count, depth = rows.shape
    width = out_weight.shape[0]
    size = width // HEADS
    padded = size + SPARE
    images = text_embed.shape[0]
    group_size = lax.axis_size("grp")
    parts = group_size // HEADS
    piggy = (
        parts == 1
        and 2 * images == SPARE
        and count >= depth - (HEADS - 2) * LANES
        and depth % count == 0
        and images * (depth // count) <= TEXT_ROWS
        and 1 < lax.axis_size("blk") <= HEADS + 1
    )
    bf16, f32 = jnp.bfloat16, jnp.float32
    shape = jax.ShapeDtypeStruct

    block = shape((3 * size + SPARE, count), bf16)
    hbm = pl.BlockSpec(memory_space=pltpu.HBM)
    turned_weight = qkv_weight.T
    normed, sums, *sent = call(
        functools.partial(far_kernel, images, piggy),
        (shape((depth, count), bf16), shape((SPARE, depth), f32), block, block),
        [
            pltpu.VMEM((1, count), jnp.int32),
            pltpu.VMEM((count, depth), bf16),
            pltpu.VMEM((3, 2 * size, depth), bf16),
            pltpu.SemaphoreType.DMA,
            pltpu.SemaphoreType.DMA,
            pltpu.SemaphoreType.DMA((3,)),
        ],
        [hbm] * 3,
        2 * count * depth * 6 * size,
    )(in_hbm(segment_ids), in_hbm(rows), in_hbm(turned_weight))
    sent += call(
        functools.partial(near_kernel, piggy),
        (block,) * 6,
        [],
        in_vmem(3),
        2 * count * depth * 18 * size,
    )(normed, sums, turned_weight)
    sent = dict(zip((6, 7, 2, 3, 4, 5, 0, 1), sent))
    if piggy:
        late_texts, sent[0] = lax.optimization_barrier((text_embed, sent[0]))
        halos_and_texts = [one_text_block(late_texts)]
    else:
        halos_and_texts = []
    got = traded(sent)

    length = HEADS * count
    halo = 0
    near_ids = segment_ids
    if parts > 1:
        halo = rounded_up(MAXP - 1, LANES)
        part = lax.axis_index("grp") // HEADS
        whole_ids = jnp.concatenate(
            [
                jnp.full((1, halo), -1, jnp.int32),
                segment_ids,
                jnp.full((1, halo), images, jnp.int32),
            ],
            axis=1,
        )
        near_ids = lax.dynamic_slice_in_dim(whole_ids, part * length, length + 2 * halo, axis=1)
        order = jnp.bitwise_xor(lax.axis_index("grp") % HEADS, jnp.arange(HEADS))
        flat = jnp.stack([got[by] for by in range(HEADS)])[order][:, : 2 * size].transpose(1, 0, 2).reshape(2 * size, length)
        flat = jnp.concatenate([flat, jnp.zeros((16, length), bf16)], axis=0)
        ahead = [(i, i + HEADS) for i in range(group_size - HEADS)]
        back = [(i + HEADS, i) for i in range(group_size - HEADS)]
        left = moved(flat[:, length - halo :], "grp", ahead)
        right = moved(flat[:, :halo], "grp", back)
        halos_and_texts += [left, right]
    reach = length + 2 * halo
    window = min(rounded_up(MAXP + LANES - 1, LANES), reach)
    tile = 2 * LANES
    early_keys, marks, before, weight = call(
        functools.partial(prepare_kernel, images, halo),
        (
            shape((len(EARLY) * count, LANES), bf16),
            shape((2, SPARE, reach), f32),
            shape((rounded_up(images + 1, SPARE), LANES), jnp.int32),
            shape((HEADS * padded, depth), bf16),
        ),
        [pltpu.SemaphoreType.DMA((HEADS,))],
        in_vmem(1) + [hbm] + in_vmem(len(EARLY)),
        1 << 30,
    )(near_ids, in_hbm(out_weight), *[got[by] for by in EARLY])
    operands = [near_ids, before, marks, early_keys, *[got[by] for by in EARLY + LATE], *halos_and_texts]
    answers = call(
        functools.partial(attend_kernel, images, piggy, halo),
        (shape((padded + TEXT_ROWS * piggy, count), bf16),) * HEADS,
        [
            pltpu.VMEM((reach, LANES), bf16),
            pltpu.VMEM((padded, reach), bf16),
            pltpu.VMEM((LANES, length), bf16),
            pltpu.VMEM((padded, length), f32),
            pltpu.VMEM((window, tile), f32),
            pltpu.VMEM((window, tile), f32),
            pltpu.VMEM((1, tile), f32),
            pltpu.VMEM((1, tile), f32),
            pltpu.SMEM((images + 1,), jnp.int32),
        ],
        in_vmem(len(operands)),
        4 * size * length * MAXP,
    )(*operands)
    home = traded(dict(zip(ORDER, answers)))
    home = [home[by] for by in ORDER]

    joined = [
        pltpu.VMEM((HEADS * padded, count), bf16),
        pltpu.VMEM((count, HEADS * padded), bf16),
        pltpu.VMEM((count, depth), bf16),
        pltpu.SemaphoreType.DMA((3,)),
    ]
    flops = 2 * count * depth * width
    if piggy:
        mixed, row_loss = call(
            functools.partial(finish_kernel, images),
            (shape((count, depth), bf16), shape((1, images), f32)),
            joined
            + [
                pltpu.VMEM((SPARE, HEADS * padded), f32),
                pltpu.VMEM((SPARE, depth), f32),
                pltpu.VMEM((HEADS, images, depth), f32),
                pltpu.VMEM((1, images), f32),
                pltpu.SemaphoreType.DMA,
            ],
            in_vmem(3 + HEADS),
            flops,
            (hbm, hbm),
        )(rows, weight, text_embed, *home)
        return (mixed[None], row_loss[0])
    mixed = call(mix_kernel, shape((count, depth), bf16), joined, in_vmem(2 + HEADS), flops, hbm)(
        rows, weight, *home
    )
    own_ids = lax.dynamic_slice_in_dim(segment_ids[0], lax.axis_index("grp") * count, count)
    onehot = (own_ids[None, :] == jnp.arange(images, dtype=jnp.int32)[:, None]).astype(bf16)
    pooled = lax.psum(jnp.dot(onehot, mixed, preferred_element_type=f32), "grp")
    text_vecs = unit_rows(all_texts(text_embed).astype(f32))
    cosine = jnp.dot(unit_rows(pooled), text_vecs.T, precision=lax.Precision.HIGHEST)
    same = jnp.arange(images)[:, None] == jnp.arange(text_vecs.shape[0])[None, :]
    row_loss = jnp.sum(losses(cosine, jnp.where(same, 1.0, -1.0)), axis=1)
    return (mixed[None], row_loss)


def solution(mesh):
    placed = (P("blk", "grp", None), P("blk", None), P(), P(), P("blk", None))
    return jax.shard_map(
        local,
        mesh=mesh,
        in_specs=placed,
        out_specs=(P("blk", "grp", None), P("blk")),
        check_vma=False,
    )
```

```python
import functools
import math

import jax
import jax.numpy as jnp
from jax import lax
from jax.experimental import pallas as pl
from jax.experimental.pallas import tpu as pltpu
from jax.sharding import PartitionSpec as P

HEADS = 8
MAXP = 1024
LANES = 128
SPARE = 8
SIZE = 72
PADDED = SIZE + SPARE
KEY_AT = SIZE - SPARE
QUERY_AT = 2 * SIZE
TEXT_ROWS = 16
HIDDEN = -1e30
ORDER = (6, 7, 4, 2, 5, 3, 1, 0)
EARLY = (6, 7, 1, 0)
LATE = (4, 2, 5, 3)

logit_scale = 30.0
logit_bias = -5.0

VMEM_LIMIT = 32 * 1024 * 1024


def rounded_up(value, step):
    return (value + step - 1) // step * step


def split_in_two(total, images):
    row = lax.broadcasted_iota(jnp.int32, total.shape, 0)
    main = total.astype(jnp.bfloat16).astype(jnp.float32)
    return jnp.where(row < images, main, total - main)


def image_rows(ids, images):
    row = lax.broadcasted_iota(jnp.int32, (SPARE, ids.shape[1]), 0)
    return (lax.rem(row, images) == ids).astype(jnp.float32).astype(jnp.bfloat16)


def head_blocks(query, key, value, sums, pair):
    size = query.shape[0] // 2
    count = query.shape[1]
    for place in range(2):
        here = slice(place * size, (place + 1) * size)
        if sums is None:
            spare = jnp.zeros((SPARE, count), jnp.float32)
        else:
            first = pl.multiple_of((2 * pair + place) * LANES, LANES)
            parts = [sums[:, pl.ds(first, LANES)], sums[:, HEADS * LANES :]]
            held = sum(part.shape[1] for part in parts)
            spare = jnp.concatenate(parts + [jnp.zeros((SPARE, count - held), jnp.float32)], axis=1)
        yield jnp.concatenate([value[here], key[here], spare, query[here]], axis=0)


def store_by_core(core, blocks, same_ref, cross_ref):
    first, second = blocks
    same_ref[...] = jnp.where(core == 0, first, second).astype(jnp.bfloat16)
    cross_ref[...] = jnp.where(core == 0, second, first).astype(jnp.bfloat16)


def place_in_group():
    own = lax.rem(lax.axis_index("grp"), HEADS)
    return lax.div(own, 2), lax.rem(own, 2)


def far_kernel(images, piggy, ids_ref, rows_ref, weight_ref, normed_ref, sums_ref, same_ref, cross_ref, own_ids, rows_held, weight, id_sem, row_sem, sems):
    count, depth = rows_ref.shape
    width = weight_ref.shape[0] // 3
    wide = weight.shape[1]
    rows_fetch = pltpu.make_async_copy(rows_ref, rows_held, row_sem)
    rows_fetch.start()
    own = pl.multiple_of(lax.axis_index("grp") * count, LANES)
    ids_fetch = pltpu.make_async_copy(ids_ref.at[:, pl.ds(own, count)], own_ids, id_sem)
    ids_fetch.start()
    pair, core = place_in_group()
    pair = jnp.bitwise_xor(pair, 3)
    fetches = []
    for at in range(3):
        first = pl.multiple_of(at * width + pair * wide, 16)
        fetches.append(pltpu.make_async_copy(weight_ref.at[pl.ds(first, wide)], weight.at[at], sems.at[at]))
    for fetch in fetches:
        fetch.start()
    ids_fetch.wait()
    rows_fetch.wait()
    rows = rows_held[...]
    if piggy:
        sums = jnp.dot(image_rows(own_ids[...], images), rows, preferred_element_type=jnp.float32)
        sums_ref[...] = split_in_two(sums, images)
    values = rows.astype(jnp.float32)
    center = values - jnp.mean(values, axis=1, keepdims=True)
    spread = jnp.mean(center * center, axis=1, keepdims=True)
    normed = (center * lax.rsqrt(spread + 1e-06)).astype(jnp.bfloat16)
    normed_ref[...] = normed.T
    for fetch in fetches:
        fetch.wait()
    parts = [
        jnp.dot(weight[at], normed_ref[...], preferred_element_type=jnp.float32) for at in range(3)
    ]
    store_by_core(core, head_blocks(*parts, sums_ref if piggy else None, pair), same_ref, cross_ref)


def near_kernel(piggy, normed_ref, sums_ref, weight_ref, *out_refs):
    width = weight_ref.shape[0] // 3
    wide = 2 * width // HEADS
    own, core = place_in_group()
    for step, move in enumerate((1, 2, 0)):
        pair = jnp.bitwise_xor(own, move)
        parts = []
        for at in range(3):
            here = pl.ds(pl.multiple_of(at * width + pair * wide, 16), wide)
            parts.append(
                jnp.dot(weight_ref[here, :], normed_ref[...], preferred_element_type=jnp.float32)
            )
        blocks = head_blocks(*parts, sums_ref if piggy else None, pair)
        store_by_core(core, blocks, *out_refs[2 * step : 2 * step + 2])


def count_before(images, ids):
    image = lax.broadcasted_iota(jnp.int32, (rounded_up(images + 1, SPARE), ids.shape[1]), 0)
    before = jnp.sum((ids < image).astype(jnp.int32), axis=1, keepdims=True)
    return jnp.broadcast_to(before, (before.shape[0], LANES))


def write_marks(images, ids, marks):
    bits = max(1, (images - 1).bit_length())
    row = lax.broadcasted_iota(jnp.int32, (SPARE, ids.shape[1]), 0)
    bit = jnp.bitwise_and(lax.shift_right_logical(jnp.broadcast_to(ids, row.shape), row >> 1), 1)
    odd = jnp.bitwise_and(row, 1)
    used = row < 2 * bits
    outside = jnp.logical_or(ids < 0, ids >= images)
    key_side = jnp.where(odd == 1, bit, 1 - bit).astype(jnp.float32)
    key_side = jnp.where(outside, 1.0, key_side)
    marks[0] = jnp.where(used, key_side * HIDDEN, 0.0)
    marks[1] = jnp.where(used, jnp.where(odd == 1, 1 - bit, bit), 0).astype(jnp.float32)


def spare_sums(refs):
    parts = [ref[QUERY_AT : QUERY_AT + 16].astype(jnp.float32)[0:SPARE, 0 : 2 * LANES] for ref in refs]
    return sum(parts[1:], parts[0])


def image_at(images, starts, position):
    found = jnp.int32(0)
    for image in range(1, images):
        found += (starts[image] <= position).astype(jnp.int32)
    return found


def attend_images(images, ids_ref, keys, values, queries, attended, work, starts, halo):
    scores_a, scores_b, tops_a, tops_b = work
    query_base = halo
    window, tile = scores_a.shape
    size = attended.shape[0] - SPARE
    held = queries.shape[1]
    tiles = held // tile
    shift = tile.bit_length() - 1

    def bounds(image):
        first = jnp.maximum(starts[image] - query_base, 0) >> shift
        last = (jnp.minimum(starts[image + 1] - query_base, held) - 1) >> shift
        return jnp.minimum(first, tiles - 1), last

    def after(image):
        return jnp.minimum(image + 1, images - 1)

    def following(state):
        at, image = state
        more = at < bounds(image)[1]
        later = after(image)
        return jnp.where(more, at + 1, bounds(later)[0]), jnp.where(more, image, later)

    def window_of(image):
        begin = jnp.bitwise_and(starts[image], -LANES)
        return pl.ds(pl.multiple_of(jnp.minimum(begin, keys.shape[0] - window), LANES), window)

    def score(state, scores, tops):
        at, image = state
        query = queries[:, pl.ds(pl.multiple_of(at * tile, tile), tile)]
        found = jnp.dot(keys[window_of(image), :], query, preferred_element_type=jnp.float32)
        scores[...] = found
        tops[...] = jnp.max(found, axis=0, keepdims=True)

    def weigh(state, scores, tops):
        at, image = state
        first = pl.multiple_of(at * tile, tile)
        labels = ids_ref[:, pl.ds(pl.multiple_of(query_base + first, LANES), tile)]
        probs = jnp.exp2((scores[...] - tops[...]) * (size ** (-0.5) * math.log2(math.e)))
        share = 1.0 / jnp.sum(probs, axis=0, keepdims=True)
        weighted = jnp.dot(
            values[:, window_of(image)], probs.astype(jnp.bfloat16), preferred_element_type=jnp.float32
        )
        place = (slice(None), pl.ds(first, tile))
        attended[place] = jnp.where(labels == image, weighted * share, attended[place])

    low = image_at(images, starts, query_base)
    high = image_at(images, starts, query_base + held - 1)
    pairs = jnp.int32(0)
    for image in range(images):
        first, last = bounds(image)
        wanted = jnp.logical_and(low <= image, image <= high)
        pairs += jnp.where(wanted, last - first + 1, 0)

    def two_pairs(_, state):
        second = following(state)
        score(second, scores_b, tops_b)
        weigh(state, scores_a, tops_a)
        third = following(second)
        score(third, scores_a, tops_a)
        weigh(second, scores_b, tops_b)
        return third

    def four_pairs(step, state):
        return two_pairs(step, two_pairs(step, state))

    begun = (jnp.int32(0), low)
    score(begun, scores_a, tops_a)
    reached = lax.fori_loop(0, lax.div(pairs, 4), four_pairs, begun)
    reached = lax.fori_loop(0, lax.div(lax.rem(pairs, 4), 2), two_pairs, reached)

    @pl.when(lax.rem(pairs, 2) == 1)
    def _():
        weigh(reached, scores_a, tops_a)


def turned_keys(marked, block_ref):
    block = block_ref[KEY_AT : KEY_AT + PADDED].astype(jnp.float32)
    nothing = jnp.zeros((LANES - PADDED, block.shape[1]), jnp.float32)
    full = jnp.concatenate([marked, block[SPARE:], nothing], axis=0)
    return full.astype(jnp.bfloat16).T


def store_queries(marked, block_ref, queries, there):
    edge = block_ref[QUERY_AT : QUERY_AT + 16].astype(jnp.float32)
    edge = jnp.concatenate([marked, edge[SPARE:]], axis=0)
    queries[0:16, there] = edge.astype(jnp.bfloat16)
    queries[16:PADDED, there] = block_ref[QUERY_AT + 16 : QUERY_AT + PADDED]
    queries[PADDED:, there] = jnp.zeros((LANES - PADDED, block_ref.shape[1]), jnp.bfloat16)


def prepare_kernel(images, halo, ids_ref, out_weight_ref, *rest):
    got_refs, (keys, marks, before, weight, sems) = rest[: len(EARLY)], rest[len(EARLY) :]
    count = got_refs[0].shape[1]
    fetches = []
    for step, by in enumerate(ORDER):
        head = jnp.bitwise_xor(lax.rem(lax.axis_index("grp"), HEADS), by)
        first = lax.div(head, 2) * (2 * SIZE) + lax.rem(head, 2) * (SIZE - SPARE)
        fetches.append(
            pltpu.make_async_copy(
                out_weight_ref.at[pl.ds(pl.multiple_of(first, 16), PADDED)],
                weight.at[step * PADDED : (step + 1) * PADDED],
                sems.at[step],
            )
        )
        fetches[-1].start()
    before[...] = count_before(images, ids_ref[...])
    write_marks(images, ids_ref[...], marks)
    own = lax.rem(lax.axis_index("grp"), HEADS)
    for step, (by, ref) in enumerate(zip(EARLY, got_refs)):
        first = jnp.bitwise_xor(own, by) * count
        here = pl.ds(pl.multiple_of(halo + first, LANES), count)
        keys[step * count : (step + 1) * count, :] = turned_keys(marks[0, :, here], ref)
    for fetch in fetches:
        fetch.wait()


def attend_kernel(images, piggy, halo, ids_ref, before_ref, marks, early_keys, *rest):
    got_refs, rest = rest[:HEADS], rest[HEADS:]
    if piggy:
        text_ref, *rest = rest
    if halo:
        left_ref, right_ref, *rest = rest
    out_refs, rest = rest[:HEADS], rest[HEADS:]
    keys, values, queries, attended, *work, starts = rest
    count = got_refs[0].shape[1]
    padded = attended.shape[0]
    size = padded - SPARE
    total_rows = HEADS * count
    length = ids_ref.shape[1]
    ids = ids_ref[...]
    before = before_ref[...]
    for image in range(images + 1):
        starts[image] = before[image, 0]

    own = lax.rem(lax.axis_index("grp"), HEADS)
    for step, (by, ref) in enumerate(zip(EARLY + LATE, got_refs)):
        first = jnp.bitwise_xor(own, by) * count
        here = pl.ds(pl.multiple_of(halo + first, LANES), count)
        there = pl.ds(pl.multiple_of(first, LANES), count)
        if by in EARLY:
            keys[here, :] = early_keys[step * count : (step + 1) * count, :]
        else:
            keys[here, :] = turned_keys(marks[0, :, here], ref)
        values[:, here] = ref[0:PADDED]
        store_queries(marks[1, :, here], ref, queries, there)
    if halo:
        for ref, here in ((left_ref, slice(0, halo)), (right_ref, slice(length - halo, length))):
            keys[here, :] = turned_keys(marks[0, :, here], ref)
            values[:, here] = ref[0:PADDED]
    attend_images(images, ids_ref, keys, values, queries, attended, work, starts, halo)

    odd_head = lax.rem(own, 2) == 1
    mine = ids[:, halo : halo + total_rows]

    def placed(block, spare):
        even = jnp.concatenate([block[0:size], spare], axis=0)
        odd = jnp.concatenate([spare, block[0:size]], axis=0)
        return jnp.where(odd_head, odd, even)

    if piggy:
        nothing = jnp.zeros((SPARE, total_rows), jnp.float32)
        flat = placed(attended[...], nothing).astype(jnp.bfloat16)
        pooled = lax.dot_general(
            image_rows(mine, images), flat, (((1,), (1,)), ((), ())), preferred_element_type=jnp.float32
        )
        pooled = split_in_two(pooled, images)
        sums = spare_sums(got_refs)
        sums = split_in_two(sums + pltpu.roll(sums, images, axis=0), images)
        spare = jnp.concatenate(
            [pooled, jnp.zeros((SPARE, LANES - padded), jnp.float32), sums], axis=1
        )
        texts = text_ref[...].astype(jnp.float32)
        parts = [texts[:, at : at + count] for at in range(0, texts.shape[1], count)]
        unused = TEXT_ROWS - images * len(parts)
        below = jnp.concatenate(parts + [jnp.zeros((unused, count), jnp.float32)] * (unused > 0), axis=0)
        below = below.astype(jnp.bfloat16)
    else:
        spare = jnp.zeros((SPARE, count), jnp.float32)
    for by, out_ref in zip(ORDER, out_refs):
        there = pl.multiple_of(jnp.bitwise_xor(own, by) * count, LANES)
        out_ref[0:padded] = placed(attended[:, pl.ds(there, count)], spare).astype(jnp.bfloat16)
        if piggy:
            out_ref[padded:] = below


def joined_heads(got_refs, flat):
    own = lax.rem(lax.axis_index("grp"), HEADS)
    spares = []
    for step, (by, got_ref) in enumerate(zip(ORDER, got_refs)):
        odd = lax.rem(jnp.bitwise_xor(own, by), 2)
        at = step * PADDED
        top = got_ref[0:16].astype(jnp.float32)
        bottom = got_ref[PADDED - 16 : PADDED].astype(jnp.float32)
        spares.append(jnp.where(odd == 1, top[:SPARE], bottom[SPARE:]))
        top = jnp.concatenate([jnp.where(odd == 1, 0.0, top[:SPARE]), top[SPARE:]], axis=0)
        bottom = jnp.concatenate([bottom[:SPARE], jnp.where(odd == 1, bottom[SPARE:], 0.0)], axis=0)
        flat[at : at + 16] = top.astype(jnp.bfloat16)
        flat[at + 16 : at + PADDED - 16] = got_ref[16 : PADDED - 16]
        flat[at + PADDED - 16 : at + PADDED] = bottom.astype(jnp.bfloat16)
    return spares


def send_mixed_rows(rows_ref, weight_ref, flat, turned, mixed, mixed_ref, sems, meanwhile=None):
    turned[...] = flat[...].T
    pieces = sems.shape[0]
    step = rows_ref.shape[0] // pieces
    copies, value = [], None
    for piece in range(pieces):
        cut = slice(piece * step, (piece + 1) * step)
        if meanwhile is not None:
            value = meanwhile[piece](value)
        added = jnp.dot(turned[cut, :], weight_ref[...], preferred_element_type=jnp.float32)
        mixed[cut, :] = (rows_ref[cut, :].astype(jnp.float32) + added).astype(jnp.bfloat16)
        copies.append(pltpu.make_async_copy(mixed.at[cut], mixed_ref.at[cut], sems.at[piece]))
        copies[-1].start()
    return copies


def unit_rows(matrix):
    return matrix * lax.rsqrt(jnp.sum(matrix * matrix, axis=1, keepdims=True) + 1e-06)


def losses(cosine, labels):
    logits = -labels * (logit_scale * cosine + logit_bias)
    return jnp.maximum(logits, 0.0) + jnp.log1p(jnp.exp(-jnp.abs(logits)))


def finish_kernel(images, rows_ref, weight_ref, text_ref, *rest):
    got_refs, rest = rest[:HEADS], rest[HEADS:]
    mixed_ref, loss_ref, flat, turned, mixed, sems, pooled_heads, patch_sums, far_texts, loss, loss_sem = rest
    spares = joined_heads(got_refs, flat)
    own = lax.rem(lax.axis_index("grp"), HEADS)
    patch_sums[:, HEADS * LANES :] = spares[0][:, 2 * LANES :]
    for step, (by, spare) in enumerate(zip(ORDER, spares)):
        pooled_heads[:, step * PADDED : (step + 1) * PADDED] = spare[:, 0:PADDED]
        head = jnp.bitwise_xor(own, by)
        patch_sums[:, pl.ds(pl.multiple_of(head * LANES, LANES), LANES)] = spare[:, LANES : 2 * LANES]
        below = got_refs[step][PADDED:].astype(jnp.float32)
        count = below.shape[1]
        for part in range(patch_sums.shape[1] // count):
            here = slice(part * count, (part + 1) * count)
            far_texts[head, :, here] = below[part * images : (part + 1) * images]

    def find_images(_):
        pooled = jnp.dot(
            pooled_heads[...].astype(jnp.bfloat16), weight_ref[...], preferred_element_type=jnp.float32
        )
        pooled = pooled + patch_sums[...]
        others = [far_texts[place] for place in range(lax.axis_size("blk") - 1)]
        texts = jnp.concatenate([text_ref[...].astype(jnp.float32)] + others, axis=0)
        return pooled + pltpu.roll(pooled, images, axis=0), unit_rows(texts)

    def find_cosines(vectors):
        pooled, text_vecs = vectors
        return lax.dot_general(
            text_vecs,
            unit_rows(pooled),
            (((1,), (1,)), ((), ())),
            precision=lax.Precision.HIGHEST,
            preferred_element_type=jnp.float32,
        )

    def find_losses(cosine):
        text = lax.broadcasted_iota(jnp.int32, cosine.shape, 0)
        image = lax.broadcasted_iota(jnp.int32, cosine.shape, 1)
        terms = losses(cosine, jnp.where(text == image, 1.0, -1.0))
        loss[...] = jnp.sum(terms, axis=0, keepdims=True)[:, 0:images]
        loss_copy.start()

    loss_copy = pltpu.make_async_copy(loss, loss_ref, loss_sem)
    meanwhile = (find_images, find_cosines, find_losses)
    copies = send_mixed_rows(rows_ref, weight_ref, flat, turned, mixed, mixed_ref, sems, meanwhile)
    for copy in copies + [loss_copy]:
        copy.wait()


def mix_kernel(rows_ref, weight_ref, *rest):
    got_refs, rest = rest[:HEADS], rest[HEADS:]
    mixed_ref, flat, turned, mixed, sems = rest
    joined_heads(got_refs, flat)
    for copy in send_mixed_rows(rows_ref, weight_ref, flat, turned, mixed, mixed_ref, sems):
        copy.wait()


def in_vmem(count):
    return [pl.BlockSpec(memory_space=pltpu.VMEM)] * count


def in_hbm(value):
    return pltpu.with_memory_space_constraint(value, pltpu.HBM)


def call(kernel, out_shape, scratch, in_specs, flops, out_specs=None):
    if out_specs is None:
        out_specs = jax.tree.map(lambda _: pl.BlockSpec(memory_space=pltpu.VMEM), out_shape)
    return pl.pallas_call(
        kernel,
        out_shape=out_shape,
        in_specs=in_specs,
        out_specs=out_specs,
        scratch_shapes=scratch,
        compiler_params=pltpu.CompilerParams(vmem_limit_bytes=VMEM_LIMIT),
        cost_estimate=pl.CostEstimate(flops=flops, bytes_accessed=8 << 20, transcendentals=0),
    )


def moved(value, axis, pairs):
    return lax.ppermute(value, axis, pairs)


def partner(place, by, peers):
    return place ^ by if peers & (peers - 1) == 0 else (place + by) % peers


def all_texts(texts):
    peers = lax.axis_size("blk")
    steps = [[(partner(i, by, peers), i) for i in range(peers)] for by in range(1, peers)]
    return jnp.concatenate([texts] + [moved(texts, "blk", pairs) for pairs in steps], axis=0)


def one_text_block(texts):
    peers = lax.axis_size("blk")
    pairs = []
    for place in range(lax.axis_size("grp")):
        by = place % (peers - 1) + 1
        pairs += [(place * peers + partner(i, by, peers), place * peers + i) for i in range(peers)]
    return moved(texts, ("grp", "blk"), pairs)


def traded(blocks):
    peers = range(lax.axis_size("grp"))
    trades = {by: moved(blocks[by], "grp", [(i, i ^ by) for i in peers]) for by in ORDER if by}
    return {**trades, 0: blocks[0]}


def local(patches, segment_ids, qkv_weight, out_weight, text_embed):
    rows = patches[0]
    count, depth = rows.shape
    width = out_weight.shape[0]
    size = width // HEADS
    padded = size + SPARE
    images = text_embed.shape[0]
    group_size = lax.axis_size("grp")
    parts = group_size // HEADS
    piggy = (
        parts == 1
        and 2 * images == SPARE
        and count >= depth - (HEADS - 2) * LANES
        and depth % count == 0
        and images * (depth // count) <= TEXT_ROWS
        and 1 < lax.axis_size("blk") <= HEADS + 1
    )
    bf16, f32 = jnp.bfloat16, jnp.float32
    shape = jax.ShapeDtypeStruct

    block = shape((3 * size + SPARE, count), bf16)
    hbm = pl.BlockSpec(memory_space=pltpu.HBM)
    turned_weight = qkv_weight.T
    normed, sums, *sent = call(
        functools.partial(far_kernel, images, piggy),
        (shape((depth, count), bf16), shape((SPARE, depth), f32), block, block),
        [
            pltpu.VMEM((1, count), jnp.int32),
            pltpu.VMEM((count, depth), bf16),
            pltpu.VMEM((3, 2 * size, depth), bf16),
            pltpu.SemaphoreType.DMA,
            pltpu.SemaphoreType.DMA,
            pltpu.SemaphoreType.DMA((3,)),
        ],
        [hbm] * 3,
        2 * count * depth * 6 * size,
    )(in_hbm(segment_ids), in_hbm(rows), in_hbm(turned_weight))
    sent += call(
        functools.partial(near_kernel, piggy),
        (block,) * 6,
        [],
        in_vmem(3),
        2 * count * depth * 18 * size,
    )(normed, sums, turned_weight)
    sent = dict(zip((6, 7, 2, 3, 4, 5, 0, 1), sent))
    if piggy:
        late_texts, sent[0] = lax.optimization_barrier((text_embed, sent[0]))
        halos_and_texts = [one_text_block(late_texts)]
    else:
        halos_and_texts = []
    got = traded(sent)

    length = HEADS * count
    halo = 0
    near_ids = segment_ids
    if parts > 1:
        halo = rounded_up(MAXP - 1, LANES)
        part = lax.axis_index("grp") // HEADS
        whole_ids = jnp.concatenate(
            [
                jnp.full((1, halo), -1, jnp.int32),
                segment_ids,
                jnp.full((1, halo), images, jnp.int32),
            ],
            axis=1,
        )
        near_ids = lax.dynamic_slice_in_dim(whole_ids, part * length, length + 2 * halo, axis=1)
        order = jnp.bitwise_xor(lax.axis_index("grp") % HEADS, jnp.arange(HEADS))
        flat = jnp.stack([got[by] for by in range(HEADS)])[order][:, : 2 * size].transpose(1, 0, 2).reshape(2 * size, length)
        flat = jnp.concatenate([flat, jnp.zeros((16, length), bf16)], axis=0)
        ahead = [(i, i + HEADS) for i in range(group_size - HEADS)]
        back = [(i + HEADS, i) for i in range(group_size - HEADS)]
        left = moved(flat[:, length - halo :], "grp", ahead)
        right = moved(flat[:, :halo], "grp", back)
        halos_and_texts += [left, right]
    reach = length + 2 * halo
    window = min(rounded_up(MAXP + LANES - 1, LANES), reach)
    tile = 2 * LANES
    early_keys, marks, before, weight = call(
        functools.partial(prepare_kernel, images, halo),
        (
            shape((len(EARLY) * count, LANES), bf16),
            shape((2, SPARE, reach), f32),
            shape((rounded_up(images + 1, SPARE), LANES), jnp.int32),
            shape((HEADS * padded, depth), bf16),
        ),
        [pltpu.SemaphoreType.DMA((HEADS,))],
        in_vmem(1) + [hbm] + in_vmem(len(EARLY)),
        1 << 30,
    )(near_ids, in_hbm(out_weight), *[got[by] for by in EARLY])
    operands = [near_ids, before, marks, early_keys, *[got[by] for by in EARLY + LATE], *halos_and_texts]
    answers = call(
        functools.partial(attend_kernel, images, piggy, halo),
        (shape((padded + TEXT_ROWS * piggy, count), bf16),) * HEADS,
        [
            pltpu.VMEM((reach, LANES), bf16),
            pltpu.VMEM((padded, reach), bf16),
            pltpu.VMEM((LANES, length), bf16),
            pltpu.VMEM((padded, length), f32),
            pltpu.VMEM((window, tile), f32),
            pltpu.VMEM((window, tile), f32),
            pltpu.VMEM((1, tile), f32),
            pltpu.VMEM((1, tile), f32),
            pltpu.SMEM((images + 1,), jnp.int32),
        ],
        in_vmem(len(operands)),
        4 * size * length * MAXP,
    )(*operands)
    home = traded(dict(zip(ORDER, answers)))
    home = [home[by] for by in ORDER]

    joined = [
        pltpu.VMEM((HEADS * padded, count), bf16),
        pltpu.VMEM((count, HEADS * padded), bf16),
        pltpu.VMEM((count, depth), bf16),
        pltpu.SemaphoreType.DMA((3,)),
    ]
    flops = 2 * count * depth * width
    if piggy:
        mixed, row_loss = call(
            functools.partial(finish_kernel, images),
            (shape((count, depth), bf16), shape((1, images), f32)),
            joined
            + [
                pltpu.VMEM((SPARE, HEADS * padded), f32),
                pltpu.VMEM((SPARE, depth), f32),
                pltpu.VMEM((HEADS, images, depth), f32),
                pltpu.VMEM((1, images), f32),
                pltpu.SemaphoreType.DMA,
            ],
            in_vmem(3 + HEADS),
            flops,
            (hbm, hbm),
        )(rows, weight, text_embed, *home)
        return (mixed[None], row_loss[0])
    mixed = call(mix_kernel, shape((count, depth), bf16), joined, in_vmem(2 + HEADS), flops, hbm)(
        rows, weight, *home
    )
    own_ids = lax.dynamic_slice_in_dim(segment_ids[0], lax.axis_index("grp") * count, count)
    onehot = (own_ids[None, :] == jnp.arange(images, dtype=jnp.int32)[:, None]).astype(bf16)
    pooled = lax.psum(jnp.dot(onehot, mixed, preferred_element_type=f32), "grp")
    text_vecs = unit_rows(all_texts(text_embed).astype(f32))
    cosine = jnp.dot(unit_rows(pooled), text_vecs.T, precision=lax.Precision.HIGHEST)
    same = jnp.arange(images)[:, None] == jnp.arange(text_vecs.shape[0])[None, :]
    row_loss = jnp.sum(losses(cosine, jnp.where(same, 1.0, -1.0)), axis=1)
    return (mixed[None], row_loss)


def solution(mesh):
    placed = (P("blk", "grp", None), P("blk", None), P(), P(), P("blk", None))
    return jax.shard_map(
        local,
        mesh=mesh,
        in_specs=placed,
        out_specs=(P("blk", "grp", None), P("blk")),
        check_vma=False,
    )
```
